32 devices in a mesh: rep: 4 (over y, x), fsdp: 8 (over z, core).
Axes of the slice: x: 2, y: 2, z: 4, core: 2. Of those that a mesh axis runs over, the one named last changes fastest.
Arguments:
- tokens: bfloat16 [32768, 768], P(('rep', 'fsdp')), may hold values from -6 to 6
- exit_layer: int32 [256], P(('rep', 'fsdp')), may hold values from 1 to 12
- qkv_weight: bfloat16 [768, 2304], P('fsdp'), may hold values from -0.21875 to 0.21875
- query_bias: bfloat16 [768], P('fsdp'), may hold values from -3 to 3
- value_bias: bfloat16 [768], P('fsdp'), may hold values from -3 to 3
- out_weight: bfloat16 [768, 768], P('fsdp'), may hold values from -0.625 to 0.625
- out_bias: bfloat16 [768], P('fsdp'), may hold values from -3 to 3
- attn_gain: bfloat16 [768], P('fsdp'), may hold values from 0.099609375 to 1.8984375
- attn_shift: bfloat16 [768], P('fsdp'), may hold values from -3 to 3
- up_weight: bfloat16 [768, 3072], P('fsdp'), may hold values from -0.21875 to 0.21875
- up_bias: bfloat16 [3072], P('fsdp'), may hold values from -3 to 3
- down_weight: bfloat16 [3072, 768], P('fsdp'), may hold values from -0.109375 to 0.109375
- down_bias: bfloat16 [768], P('fsdp'), may hold values from -3 to 3
- block_gain: bfloat16 [768], P('fsdp'), may hold values from 0.099609375 to 1.8984375
- block_shift: bfloat16 [768], P('fsdp'), may hold values from -3 to 3
- pool_weight: bfloat16 [768, 768], P('fsdp'), may hold values from -0.21875 to 0.21875
- pool_bias: bfloat16 [768], P('fsdp'), may hold values from -3 to 3
- class_weight: bfloat16 [768, 3], P('fsdp'), may hold values from -0.875 to 0.875
- class_bias: bfloat16 [3], replicated, may hold values from -4 to 4
- output_grad: bfloat16 [32768, 768], P(('rep', 'fsdp')), may hold values from -6 to 6
- logit_grad: bfloat16 [256, 3], P(('rep', 'fsdp')), may hold values from -6 to 6
Outputs:
- output: bfloat16 [32768, 768], P(('rep', 'fsdp'))
- logits: float32 [256, 3], P(('rep', 'fsdp'))
- entropy_mean: float32 [], replicated
- input_grad: bfloat16 [32768, 768], P(('rep', 'fsdp'))
- qkv_weight_grad: float32 [768, 2304], P('fsdp')
- query_bias_grad: float32 [768], P('fsdp')
- value_bias_grad: float32 [768], P('fsdp')
- out_weight_grad: float32 [768, 768], P('fsdp')
- out_bias_grad: float32 [768], P('fsdp')
- attn_gain_grad: float32 [768], P('fsdp')
- attn_shift_grad: float32 [768], P('fsdp')
- up_weight_grad: float32 [768, 3072], P('fsdp')
- up_bias_grad: float32 [3072], P('fsdp')
- down_weight_grad: float32 [3072, 768], P('fsdp')
- down_bias_grad: float32 [768], P('fsdp')
- block_gain_grad: float32 [768], P('fsdp')
- block_shift_grad: float32 [768], P('fsdp')
- pool_weight_grad: float32 [768, 768], P('fsdp')
- pool_bias_grad: float32 [768], P('fsdp')
- class_weight_grad: float32 [768, 3], P('fsdp')
- class_bias_grad: float32 [3], replicated
The draws below stay inside these ranges and needn't reach their ends.
Inputs may be any that keep to these rules, and one draw needn't show every extreme that they name: `exit_layer`: the last layer that each sequence passes; this layer is number 6.
All inputs are finite; a program needn't handle non-finite values.
Results may differ from the reference program's by a relative error of at most 0.02.
Values may be sent and summed in bfloat16 or wider, within the bound.
No kernel may reach another device: no remote copies, remote signals or barrier semaphores. Data moves between devices by JAX's collectives and lax.ppermute only.
A program may use at most 192 MiB of HBM per device.

```python
import math
import jax
import jax.numpy as jnp
from jax import lax

D = 768
H = 12
HD = 64
FF = 3072
LAYERS = 12
LAYER = 6
CLASSES = 3
SEQ = 128
NSEQ = 256
TOKENS = 32768


def plant(entries, key, low, largest):
    place = [jax.random.randint(jax.random.fold_in(key, axis), (), 0, length) for axis, length in enumerate(entries.shape)]
    longest = entries.shape.index(max(entries.shape))
    beside = place[:longest] + [(place[longest] + 1) % entries.shape[longest]] + place[longest + 1:]
    return entries.at[tuple(place)].set(low).at[tuple(beside)].set(largest)


def block_levels(stream_key, dims, split, smallest, largest):
    level, own = 1.0, jax.random.fold_in(stream_key, 6)
    for axis_at, blocks in split:
        steps = jnp.exp(jax.random.uniform(jax.random.fold_in(own, axis_at), (blocks,), jnp.float32, smallest / len(split), largest / len(split)))
        level = level * jnp.repeat(steps, dims[axis_at] // blocks).reshape([-1 if axis == axis_at else 1 for axis in range(len(dims))])
    return level


def scatter_about(own_key, shape, width, limit, pieces=(), held_as=jnp.bfloat16):
    factor_of = block_levels(own_key, shape, pieces, -0.22, 0.18) if pieces else 1.0
    drawn = jax.random.normal(own_key, shape, jnp.float32) * width * factor_of
    return jnp.minimum(jnp.maximum(drawn, -limit), limit).astype(held_as)


def setup_inputs(seed: int = 0) -> dict:
    key_list = jax.random.split(jax.random.key(seed), 22)
    tokens = scatter_about(key_list[0], (TOKENS, D), 1.0, 6.0, ((0, 32),))
    exit_layer = plant(jax.random.randint(key_list[1], (NSEQ,), 1, LAYERS + 1), jax.random.fold_in(key_list[1], 1), 1, LAYERS).astype(jnp.int32)
    qkv_weight = scatter_about(key_list[2], (D, 3 * D), D ** -0.5, 0.21875, ((0, 8),))
    query_bias = scatter_about(key_list[3], (D,), 0.5, 3.0, ((0, 8),))
    value_bias = scatter_about(key_list[4], (D,), 0.5, 3.0, ((0, 8),))
    out_weight = scatter_about(key_list[5], (D, D), (D // 8) ** -0.5, 0.625, ((0, 8),))
    out_bias = scatter_about(key_list[6], (D,), 0.5, 3.0, ((0, 8),))
    attn_gain = jnp.clip(1.0 + 0.18 * jax.random.normal(key_list[7], (D,), jnp.float32), 0.099609375, 1.8984375).astype(jnp.bfloat16)
    attn_shift = scatter_about(key_list[8], (D,), 0.5, 3.0, ((0, 8),))
    up_weight = scatter_about(key_list[9], (D, FF), D ** -0.5, 0.21875, ((0, 8),))
    up_bias = scatter_about(key_list[10], (FF,), 0.5, 3.0, ((0, 8),))
    down_weight = scatter_about(key_list[11], (FF, D), FF ** -0.5, 0.109375, ((0, 8),))
    down_bias = scatter_about(key_list[12], (D,), 0.5, 3.0, ((0, 8),))
    block_gain = jnp.clip(1.0 + 0.18 * jax.random.normal(key_list[13], (D,), jnp.float32), 0.099609375, 1.8984375).astype(jnp.bfloat16)
    block_shift = scatter_about(key_list[14], (D,), 0.5, 3.0, ((0, 8),))
    pool_weight = scatter_about(key_list[15], (D, D), D ** -0.5, 0.21875, ((0, 8),))
    pool_bias = scatter_about(key_list[16], (D,), 0.5, 3.0, ((0, 8),))
    class_weight = scatter_about(key_list[17], (D, CLASSES), (D // 16) ** -0.5, 0.875, ((0, 8),))
    class_bias = scatter_about(key_list[18], (CLASSES,), 1.0, 4.0)
    output_grad = scatter_about(key_list[19], (TOKENS, D), 1.0, 6.0, ((0, 32),))
    logit_grad = scatter_about(key_list[20], (NSEQ, CLASSES), 1.0, 6.0, ((0, 32),))
    return {"tokens": tokens, "exit_layer": exit_layer, "qkv_weight": qkv_weight, "query_bias": query_bias, "value_bias": value_bias, "out_weight": out_weight, "out_bias": out_bias, "attn_gain": attn_gain, "attn_shift": attn_shift, "up_weight": up_weight, "up_bias": up_bias, "down_weight": down_weight, "down_bias": down_bias, "block_gain": block_gain, "block_shift": block_shift, "pool_weight": pool_weight, "pool_bias": pool_bias, "class_weight": class_weight, "class_bias": class_bias, "output_grad": output_grad, "logit_grad": logit_grad}


@jax.custom_vjp
def low(v):
    return lax.optimization_barrier(v.astype(jnp.bfloat16)).astype(jnp.float32)

@jax.custom_vjp
def low_back(v):
    return v

def low_keep(v):
    return (low(v), None)

def low_pass(kept, grad):
    return (grad,)

def back_keep(v):
    return (v, None)

def back_low(kept, grad):
    return (low(grad),)
low.defvjp(low_keep, low_pass)
low_back.defvjp(back_keep, back_low)

def matmul(left, right):
    return jnp.dot(left, right, precision=lax.Precision.HIGHEST, preferred_element_type=jnp.float32)

def norm_rows(values, gain, shift):
    center = values - lax.optimization_barrier(jnp.mean(values, axis=-1, keepdims=True))
    spread = lax.optimization_barrier(jnp.mean(center * center, axis=-1, keepdims=True))
    return center * lax.rsqrt(spread + 1e-06) * gain + shift

def forward(params, inputs, active):
    qkv_weight, query_bias, value_bias, out_weight, out_bias, attn_gain, attn_shift, up_weight, up_bias, down_weight, down_bias, block_gain, block_shift, pool_weight, pool_bias, class_weight, class_bias = params
    count = active.shape[0]
    zero_bias = jnp.zeros_like(query_bias)
    joined = low_back(low(matmul(inputs, qkv_weight) + jnp.concatenate([query_bias, zero_bias, value_bias])))
    joined = joined.reshape(count, SEQ, 3, H, HD)
    query_rows = joined[:, :, 0]
    key_rows = joined[:, :, 1]
    value_rows = joined[:, :, 2]
    scores = low_back(jnp.einsum('sqhd,skhd->shqk', query_rows, key_rows, precision=lax.Precision.HIGHEST) * 0.125)
    probs = low(jax.nn.softmax(scores, axis=-1))
    context = jnp.einsum('shqk,skhd->sqhd', probs, value_rows, precision=lax.Precision.HIGHEST)
    context = low_back(low(context)).reshape(count * SEQ, D)
    attended = low_back(matmul(context, out_weight) + out_bias)
    first = norm_rows(inputs + attended, attn_gain, attn_shift)
    hidden = low_back(matmul(low(first), up_weight) + up_bias)
    activated = low(jax.nn.gelu(hidden, approximate=False))
    branch = low_back(matmul(activated, down_weight) + down_bias)
    output = norm_rows(first + branch, block_gain, block_shift)
    output = output.reshape(count, SEQ, D) * active[:, None, None]
    leading = low(output[:, 0, :])
    pooled_pre = low_back(matmul(leading, pool_weight) + pool_bias)
    pooled = low(jnp.tanh(pooled_pre))
    raw = low_back(matmul(pooled, class_weight) + class_bias)
    logprob = jax.nn.log_softmax(raw, axis=-1)
    entropy = -lax.optimization_barrier(jnp.sum(jnp.exp(logprob) * logprob, axis=-1))
    return (output.reshape(count * SEQ, D), raw * active[:, None], jnp.sum(entropy * active))

def reference(tokens, exit_layer, qkv_weight, query_bias, value_bias, out_weight, out_bias, attn_gain, attn_shift, up_weight, up_bias, down_weight, down_bias, block_gain, block_shift, pool_weight, pool_bias, class_weight, class_bias, output_grad, logit_grad):
    params = tuple((weight.astype(jnp.float32) for weight in (qkv_weight, query_bias, value_bias, out_weight, out_bias, attn_gain, attn_shift, up_weight, up_bias, down_weight, down_bias, block_gain, block_shift, pool_weight, pool_bias, class_weight, class_bias)))
    seqs_total = exit_layer.shape[0]
    group = math.gcd(seqs_total, 32)
    rounds = seqs_total // group
    active = (exit_layer >= LAYER).astype(jnp.float32).reshape(rounds, group)
    inputs = tokens.astype(jnp.float32).reshape(rounds, group * SEQ, D)
    out_cot = output_grad.astype(jnp.float32).reshape(rounds, group * SEQ, D)
    log_cot = logit_grad.astype(jnp.float32).reshape(rounds, group, CLASSES)

    def one_group(carry, item):
        totals, entropy_total = carry
        block_in, block_active, block_out_cot, block_log_cot = item

        def local(weights, values):
            return forward(weights, values, block_active)
        results, backward = jax.vjp(local, params, block_in)
        weight_grads, in_grad = backward((block_out_cot, block_log_cot, jnp.zeros((), jnp.float32)))
        totals = jax.tree.map(jnp.add, totals, weight_grads)
        return ((totals, entropy_total + results[2]), (results[0].astype(jnp.bfloat16), results[1], in_grad.astype(jnp.bfloat16)))
    start = (jax.tree.map(jnp.zeros_like, params), jnp.zeros((), jnp.float32))
    (grads, entropy_total), (outputs, logits, in_grads) = lax.scan(one_group, start, (inputs, active, out_cot, log_cot))
    outputs = outputs.reshape(seqs_total * SEQ, D)
    logits = logits.reshape(seqs_total, CLASSES)
    in_grads = in_grads.reshape(seqs_total * SEQ, D)
    return (outputs, logits, entropy_total / seqs_total, in_grads, grads[0], grads[1], grads[2], grads[3], grads[4], grads[5], grads[6], grads[7], grads[8], grads[9], grads[10], grads[11], grads[12], grads[13], grads[14], grads[15], grads[16])
```

```python
import jax
import jax.numpy as jnp
from jax import lax
from jax.sharding import PartitionSpec as P

HD = 64
LAYER = 6


def plain_dot(left, right):
    return jnp.dot(left, right, preferred_element_type=jnp.float32)


def lead_dot(left, right):
    return lax.dot_general(
        left, right, (((0,), (0,)), ((), ())), preferred_element_type=jnp.float32
    )


def back_dot(left, right):
    return lax.dot_general(
        left, right, (((1,), (1,)), ((), ())), preferred_element_type=jnp.float32
    )


def norm_rows(values, gain, shift):
    center = values - jnp.mean(values, axis=-1, keepdims=True)
    spread = jnp.mean(center * center, axis=-1, keepdims=True)
    return center * lax.rsqrt(spread + 1e-06) * gain + shift


def gelu_exact(values):
    return jax.nn.gelu(values, approximate=False)


def column_sum(values):
    return jnp.sum(values.astype(jnp.float32), axis=0)


def run_forward(weights, tokens, active, class_bias):
    (
        qkv_weight,
        query_bias,
        value_bias,
        out_weight,
        out_bias,
        attn_gain,
        attn_shift,
        up_weight,
        up_bias,
        down_weight,
        down_bias,
        block_gain,
        block_shift,
        pool_weight,
        pool_bias,
        class_weight,
    ) = weights
    count = active.shape[0]
    rows = tokens.shape[0]
    length = rows // count
    width = out_weight.shape[0]
    heads = width // HD
    zero_bias = jnp.zeros(query_bias.shape, jnp.float32)
    bias_row = jnp.concatenate(
        [query_bias.astype(jnp.float32), zero_bias, value_bias.astype(jnp.float32)]
    )
    joined = (
        (plain_dot(tokens, qkv_weight) + bias_row)
        .astype(jnp.bfloat16)
        .reshape(count, length, 3, heads, HD)
    )
    query_rows = joined[:, :, 0]
    key_rows = joined[:, :, 1]
    value_rows = joined[:, :, 2]
    scores = (
        jnp.einsum("sqhd,skhd->shqk", query_rows, key_rows, preferred_element_type=jnp.float32)
        * 0.125
    )
    log_total = jax.nn.logsumexp(scores, axis=-1, keepdims=True)
    probs = jnp.exp(scores - log_total).astype(jnp.bfloat16)
    context = jnp.einsum("shqk,skhd->sqhd", probs, value_rows, preferred_element_type=jnp.float32)
    context = context.astype(jnp.bfloat16).reshape(rows, width)
    inner = tokens.astype(jnp.float32) + (
        plain_dot(context, out_weight) + out_bias.astype(jnp.float32)
    )
    first = norm_rows(inner, attn_gain.astype(jnp.float32), attn_shift.astype(jnp.float32))
    first_low = first.astype(jnp.bfloat16)
    hidden = plain_dot(first_low, up_weight) + up_bias.astype(jnp.float32)
    activated = gelu_exact(hidden).astype(jnp.bfloat16)
    outer = first + (plain_dot(activated, down_weight) + down_bias.astype(jnp.float32))
    output = norm_rows(outer, block_gain.astype(jnp.float32), block_shift.astype(jnp.float32))
    output = output.reshape(count, length, width) * active[:, None, None]
    leading = output[:, 0, :].astype(jnp.bfloat16)
    pooled = jnp.tanh(plain_dot(leading, pool_weight) + pool_bias.astype(jnp.float32))
    pooled_low = pooled.astype(jnp.bfloat16)
    raw = plain_dot(pooled_low, class_weight) + class_bias.astype(jnp.float32)
    logprob = jax.nn.log_softmax(raw, axis=-1)
    entropy = jnp.sum(-jnp.sum(jnp.exp(logprob) * logprob, axis=-1) * active)
    kept = (
        joined,
        log_total,
        context,
        inner,
        first_low,
        hidden,
        activated,
        outer,
        leading,
        pooled,
        pooled_low,
    )
    return (output.reshape(rows, width), raw * active[:, None], entropy, kept)


def run_backward(weights, kept, tokens, active, output_grad, logit_grad):
    (
        qkv_weight,
        query_bias,
        value_bias,
        out_weight,
        out_bias,
        attn_gain,
        attn_shift,
        up_weight,
        up_bias,
        down_weight,
        down_bias,
        block_gain,
        block_shift,
        pool_weight,
        pool_bias,
        class_weight,
    ) = weights
    (
        joined,
        log_total,
        context,
        inner,
        first_low,
        hidden,
        activated,
        outer,
        leading,
        pooled,
        pooled_low,
    ) = kept
    count = active.shape[0]
    rows = tokens.shape[0]
    length = rows // count
    width = out_weight.shape[0]
    heads = width // HD
    class_grad = (logit_grad.astype(jnp.float32) * active[:, None]).astype(jnp.bfloat16)
    class_bias_grad = column_sum(class_grad)
    class_weight_grad = lead_dot(pooled_low, class_grad)
    pooled_grad = back_dot(class_grad, class_weight)
    pre_grad = (pooled_grad * (1.0 - pooled * pooled)).astype(jnp.bfloat16)
    pool_bias_grad = column_sum(pre_grad)
    pool_weight_grad = lead_dot(leading, pre_grad)
    leading_grad = back_dot(pre_grad, pool_weight)
    top_grad = output_grad.astype(jnp.float32).reshape(count, length, width)
    top_grad = top_grad.at[:, 0, :].add(leading_grad) * active[:, None, None]
    top_grad = top_grad.reshape(rows, width)
    unused, block_back = jax.vjp(
        norm_rows, outer, block_gain.astype(jnp.float32), block_shift.astype(jnp.float32)
    )
    outer_grad, block_gain_grad, block_shift_grad = block_back(top_grad)
    branch_grad = outer_grad.astype(jnp.bfloat16)
    down_bias_grad = column_sum(branch_grad)
    down_weight_grad = lead_dot(activated, branch_grad)
    act_grad = back_dot(branch_grad, down_weight)
    unused, gelu_back = jax.vjp(gelu_exact, hidden)
    hidden_grad = gelu_back(act_grad)[0].astype(jnp.bfloat16)
    up_bias_grad = column_sum(hidden_grad)
    up_weight_grad = lead_dot(first_low, hidden_grad)
    first_grad = outer_grad + back_dot(hidden_grad, up_weight)
    unused, attn_back = jax.vjp(
        norm_rows, inner, attn_gain.astype(jnp.float32), attn_shift.astype(jnp.float32)
    )
    inner_grad, attn_gain_grad, attn_shift_grad = attn_back(first_grad)
    attended_grad = inner_grad.astype(jnp.bfloat16)
    out_bias_grad = column_sum(attended_grad)
    out_weight_grad = lead_dot(context, attended_grad)
    context_grad = (
        back_dot(attended_grad, out_weight).astype(jnp.bfloat16).reshape(count, length, heads, HD)
    )
    query_rows = joined[:, :, 0]
    key_rows = joined[:, :, 1]
    value_rows = joined[:, :, 2]
    scores = (
        jnp.einsum("sqhd,skhd->shqk", query_rows, key_rows, preferred_element_type=jnp.float32)
        * 0.125
    )
    probs = jnp.exp(scores - log_total)
    probs_low = probs.astype(jnp.bfloat16)
    value_grad = jnp.einsum(
        "shqk,sqhd->skhd", probs_low, context_grad, preferred_element_type=jnp.float32
    )
    prob_grad = jnp.einsum(
        "sqhd,skhd->shqk", context_grad, value_rows, preferred_element_type=jnp.float32
    )
    score_grad = probs * (prob_grad - jnp.sum(prob_grad * probs, axis=-1, keepdims=True))
    score_grad = score_grad.astype(jnp.bfloat16)
    query_grad = (
        jnp.einsum("shqk,skhd->sqhd", score_grad, key_rows, preferred_element_type=jnp.float32)
        * 0.125
    )
    key_grad = (
        jnp.einsum("shqk,sqhd->skhd", score_grad, query_rows, preferred_element_type=jnp.float32)
        * 0.125
    )
    joined_grad = (
        jnp.stack([query_grad, key_grad, value_grad], axis=2)
        .astype(jnp.bfloat16)
        .reshape(rows, 3 * width)
    )
    qkv_weight_grad = lead_dot(tokens, joined_grad)
    joined_total = column_sum(joined_grad)
    query_bias_grad = joined_total[:width]
    value_bias_grad = joined_total[2 * width :]
    input_grad = (inner_grad + back_dot(joined_grad, qkv_weight)).astype(jnp.bfloat16)
    grads = (
        qkv_weight_grad,
        query_bias_grad,
        value_bias_grad,
        out_weight_grad,
        out_bias_grad,
        attn_gain_grad,
        attn_shift_grad,
        up_weight_grad,
        up_bias_grad,
        down_weight_grad,
        down_bias_grad,
        block_gain_grad,
        block_shift_grad,
        pool_weight_grad,
        pool_bias_grad,
        class_weight_grad,
    )
    return (input_grad, grads, class_bias_grad)

LANES = 128


def share(rows, index, count):
    part = rows.shape[0] // count
    return lax.dynamic_slice_in_dim(rows, index * part, part, axis=0)


def gather_all(rows):
    return lax.all_gather(rows, ("fsdp", "rep"), axis=0, tiled=True)


def scatter_all(rows):
    return lax.psum_scatter(
        rows.astype(jnp.bfloat16), ("fsdp", "rep"), scatter_dimension=0, tiled=True
    )


def per_device(
    tokens,
    exit_layer,
    qkv_weight,
    query_bias,
    value_bias,
    out_weight,
    out_bias,
    attn_gain,
    attn_shift,
    up_weight,
    up_bias,
    down_weight,
    down_bias,
    block_gain,
    block_shift,
    pool_weight,
    pool_bias,
    class_weight,
    class_bias,
    output_grad,
    logit_grad,
):
    reps = lax.axis_size("rep")
    shards = lax.axis_size("fsdp")
    mine = lax.axis_index("rep")
    active = (exit_layer >= LAYER).astype(jnp.float32)
    shard_rows, qkv_width = qkv_weight.shape
    part = shard_rows // reps
    vectors = (
        query_bias,
        value_bias,
        out_bias,
        attn_gain,
        attn_shift,
        up_bias,
        down_bias,
        block_gain,
        block_shift,
        pool_bias,
        class_weight.reshape(-1),
    )
    sizes = [v.shape[0] for v in vectors]
    total = sum(sizes)
    extra = -(-(-(-total // reps)) // part)
    extra = -(-extra // LANES) * LANES
    padded = reps * part * extra
    small = jnp.pad(jnp.concatenate(vectors), (0, padded - total)).reshape(shard_rows, extra)
    first_piece = gather_all(share(jnp.concatenate([qkv_weight, small], axis=1), mine, reps))
    qkv_full = first_piece[:, :qkv_width]
    small_full = first_piece[:, qkv_width:].reshape(shards, padded)
    pieces = []
    at = 0
    for size in sizes:
        pieces.append(small_full[:, at : at + size].reshape(-1))
        at += size
    out_full = gather_all(share(out_weight, mine, reps))
    up_full = gather_all(share(up_weight, mine, reps))
    down_full = gather_all(share(down_weight, mine, reps))
    pool_full = gather_all(share(pool_weight, mine, reps))
    gathered = (
        qkv_full,
        pieces[0],
        pieces[1],
        out_full,
        pieces[2],
        pieces[3],
        pieces[4],
        up_full,
        pieces[5],
        down_full,
        pieces[6],
        pieces[7],
        pieces[8],
        pool_full,
        pieces[9],
        pieces[10].reshape(-1, class_weight.shape[1]),
    )
    output, logits, entropy, kept = run_forward(gathered, tokens, active, class_bias)
    input_grad, grads, class_bias_grad = run_backward(
        gathered, kept, tokens, active, output_grad, logit_grad
    )
    vector_grads = [
        grads[at].reshape(shards, -1) for at in (1, 2, 4, 5, 6, 8, 10, 11, 12, 14, 15)
    ]
    small_grads = jnp.pad(
        jnp.concatenate(vector_grads, axis=1), ((0, 0), (0, padded - total))
    ).reshape(shards * shard_rows, extra)

    def finish(grad):
        return lax.all_gather(scatter_all(grad), "rep", axis=0, tiled=True)

    down_sum = finish(grads[9]).astype(jnp.float32)
    up_sum = finish(grads[7]).astype(jnp.float32)
    pool_sum = finish(grads[13]).astype(jnp.float32)
    out_sum = finish(grads[3]).astype(jnp.float32)
    joint_sum = finish(jnp.concatenate([grads[0], small_grads], axis=1)).astype(jnp.float32)
    qkv_sum = joint_sum[:, :qkv_width]
    small_sum = joint_sum[:, qkv_width:].reshape(padded)
    sums = []
    at = 0
    for size in sizes:
        sums.append(small_sum[at : at + size])
        at += size
    entropy_total, bias_total = lax.psum((entropy, class_bias_grad), ("rep", "fsdp"))
    seqs_total = exit_layer.shape[0] * reps * shards
    entropy_mean = entropy_total / seqs_total
    return (
        output.astype(jnp.bfloat16),
        logits,
        entropy_mean,
        input_grad,
        qkv_sum,
        sums[0],
        sums[1],
        out_sum,
        sums[2],
        sums[3],
        sums[4],
        up_sum,
        sums[5],
        down_sum,
        sums[6],
        sums[7],
        sums[8],
        pool_sum,
        sums[9],
        sums[10].reshape(-1, class_weight.shape[1]),
        bias_total,
    )


def solution(mesh):
    return jax.shard_map(
        per_device,
        mesh=mesh,
        in_specs=(
            P(("rep", "fsdp"), None),
            P(("rep", "fsdp")),
            P("fsdp", None),
            P("fsdp"),
            P("fsdp"),
            P("fsdp", None),
            P("fsdp"),
            P("fsdp"),
            P("fsdp"),
            P("fsdp", None),
            P("fsdp"),
            P("fsdp", None),
            P("fsdp"),
            P("fsdp"),
            P("fsdp"),
            P("fsdp", None),
            P("fsdp"),
            P("fsdp", None),
            P(),
            P(("rep", "fsdp"), None),
            P(("rep", "fsdp"), None),
        ),
        out_specs=(
            P(("rep", "fsdp"), None),
            P(("rep", "fsdp"), None),
            P(),
            P(("rep", "fsdp"), None),
            P("fsdp", None),
            P("fsdp"),
            P("fsdp"),
            P("fsdp", None),
            P("fsdp"),
            P("fsdp"),
            P("fsdp"),
            P("fsdp", None),
            P("fsdp"),
            P("fsdp", None),
            P("fsdp"),
            P("fsdp"),
            P("fsdp"),
            P("fsdp", None),
            P("fsdp"),
            P("fsdp", None),
            P(),
        ),
        check_vma=False,
    )
```

```python
import functools

import jax
import jax.numpy as jnp
from jax import lax
from jax.experimental import pallas as pl
from jax.experimental.pallas import tpu as pltpu
from jax.sharding import PartitionSpec as P

HD = 64
LAYER = 6
PAIR = 2 * HD
VMEM_BYTES = 58 * 2**20
BF = jnp.bfloat16
F32 = jnp.float32

QUERY_BIAS, VALUE_BIAS, OUT_BIAS, ATTN_GAIN, ATTN_SHIFT = 0, 1, 2, 3, 4
DOWN_BIAS, BLOCK_GAIN, BLOCK_SHIFT, CLASS_ROWS, POOL_BIAS = 5, 6, 7, 8, 11
VECTOR_ROWS = 12


def nn(left, right):
    return jnp.dot(left, right, preferred_element_type=F32)


def tn(left, right):
    return lax.dot_general(left, right, (((0,), (0,)), ((), ())), preferred_element_type=F32)


def nt(left, right):
    return lax.dot_general(left, right, (((1,), (1,)), ((), ())), preferred_element_type=F32)


def full(shape):
    return pl.BlockSpec(shape, lambda *at: (0,) * len(shape))


def params():
    return pltpu.CompilerParams(
        dimension_semantics=("arbitrary",), vmem_limit_bytes=VMEM_BYTES
    )


def cost(flops, moved, trans=0):
    return pl.CostEstimate(flops=flops, bytes_accessed=moved, transcendentals=trans)


def split_heads(pair):
    lane = lax.broadcasted_iota(jnp.int32, pair.shape, 1)
    zero = jnp.zeros_like(pair)
    return jnp.concatenate(
        [jnp.where(lane < HD, pair, zero), jnp.where(lane < HD, zero, pair)], axis=0
    )


def norm_stats(values):
    center = values - jnp.mean(values, axis=-1, keepdims=True)
    spread = jnp.mean(center * center, axis=-1, keepdims=True)
    scale = lax.rsqrt(spread + 1e-06)
    return center * scale, scale


def norm_back(grad, unit, scale, gain):
    inner = grad * gain
    first = jnp.mean(inner, axis=-1, keepdims=True)
    second = jnp.mean(inner * unit, axis=-1, keepdims=True)
    return scale * (inner - first - unit * second)


def gelu_parts(values):
    size = jnp.abs(values)
    t = 1.0 / (1.0 + 0.23164189 * size)
    bell = jnp.exp(-0.5 * values * values)
    poly = t * (
        0.127414796
        + t * (-0.142248368 + t * (0.7107068705 + t * (-0.7265760135 + t * 0.5307027145)))
    )
    tail = poly * bell
    below = jnp.where(values >= 0.0, 1.0 - tail, tail)
    return values * below, below + values * (bell * 0.3989422804014327)


def attend_kernel(length, tok_ref, w_ref, bias_ref, joined_ref, probs_ref, ctx_ref):
    rows, width = ctx_ref.shape
    pairs = width // PAIR
    for part in range(3):
        cols = slice(part * width, (part + 1) * width)
        joined_ref[:, cols] = (nn(tok_ref[...], w_ref[:, cols]) + bias_ref[:, cols]).astype(BF)

    def one(seq, carry):
        at = pl.ds(pl.multiple_of(seq * length, length), length)
        for pair in range(pairs):
            cols = slice(pair * PAIR, (pair + 1) * PAIR)
            query = joined_ref[at, cols] * jnp.asarray(0.125, BF)
            keys = split_heads(joined_ref[at, width + pair * PAIR : width + (pair + 1) * PAIR])
            vals = split_heads(
                joined_ref[at, 2 * width + pair * PAIR : 2 * width + (pair + 1) * PAIR]
            )
            scores = nt(keys, query)
            halves = []
            for head in range(2):
                part = scores[head * length : (head + 1) * length]
                part = jnp.exp(part - jnp.max(part, axis=0, keepdims=True))
                part = part * (1.0 / jnp.sum(part, axis=0, keepdims=True))
                halves.append(part.astype(BF))
            probs = jnp.concatenate(halves, axis=0)
            probs_ref[seq, pair] = probs
            ctx_ref[at, cols] = tn(probs, vals).astype(BF)
        return carry

    lax.fori_loop(0, rows // length, one, 0)


def attend(tokens, qkv, bias_row, length):
    rows, width = tokens.shape
    count = rows // length
    steps = 2
    block = rows // steps
    pairs = width // PAIR
    return pl.pallas_call(
        functools.partial(attend_kernel, length),
        grid=(steps,),
        in_specs=[
            pl.BlockSpec((block, width), lambda i: (i, 0)),
            full(qkv.shape),
            full(bias_row.shape),
        ],
        out_specs=[
            pl.BlockSpec((block, 3 * width), lambda i: (i, 0)),
            pl.BlockSpec((count // steps, pairs, 2 * length, length), lambda i: (i, 0, 0, 0)),
            pl.BlockSpec((block, width), lambda i: (i, 0)),
        ],
        out_shape=[
            jax.ShapeDtypeStruct((rows, 3 * width), BF),
            jax.ShapeDtypeStruct((count, pairs, 2 * length, length), BF),
            jax.ShapeDtypeStruct((rows, width), BF),
        ],
        compiler_params=params(),
        cost_estimate=cost(8 * rows * width * width, 20 * rows * width, rows * width),
        name="attend",
    )(tokens, qkv, bias_row)


def feed_kernel(
    length,
    exit_ref,
    tok_ref,
    ctx_ref,
    out_w_ref,
    vec_ref,
    up_ref,
    up_b_ref,
    down_ref,
    low_ref,
    act_ref,
    slope_ref,
    unit1_ref,
    scale1_ref,
    unit2_ref,
    scale2_ref,
    output_ref,
    acc_ref,
):
    step = pl.program_id(0)
    rows = tok_ref.shape[0]
    sub = 256

    @pl.when(step == 0)
    def _():
        for m in range(rows // sub):
            at = slice(m * sub, (m + 1) * sub)
            inner = tok_ref[at].astype(F32) + (
                nn(ctx_ref[at], out_w_ref[...]) + vec_ref[OUT_BIAS : OUT_BIAS + 1]
            )
            unit, scale = norm_stats(inner)
            first = unit * vec_ref[ATTN_GAIN : ATTN_GAIN + 1] + vec_ref[ATTN_SHIFT : ATTN_SHIFT + 1]
            unit1_ref[at] = unit.astype(BF)
            scale1_ref[at] = scale
            low_ref[at] = first.astype(BF)
            acc_ref[at] = first + vec_ref[DOWN_BIAS : DOWN_BIAS + 1]

    for m in range(rows // sub):
        at = slice(m * sub, (m + 1) * sub)
        hidden = nn(low_ref[at], up_ref[...]) + up_b_ref[...]
        act, slope = gelu_parts(hidden)
        act = act.astype(BF)
        act_ref[at] = act
        slope_ref[at] = slope.astype(BF)
        acc_ref[at] += nn(act, down_ref[...])

    @pl.when(step == pl.num_programs(0) - 1)
    def _():
        for seq in range(rows // length):
            at = slice(seq * length, (seq + 1) * length)
            active = (exit_ref[seq] >= LAYER).astype(F32)
            unit, scale = norm_stats(acc_ref[at])
            unit2_ref[at] = unit.astype(BF)
            scale2_ref[at] = scale
            result = (
                unit * vec_ref[BLOCK_GAIN : BLOCK_GAIN + 1] + vec_ref[BLOCK_SHIFT : BLOCK_SHIFT + 1]
            ) * active
            output_ref[at] = result.astype(BF)


def feed(exit_layer, tokens, ctx, out_w, vec, up, up_bias, down, length):
    rows, width = tokens.shape
    hidden = up.shape[1]
    steps = hidden // width
    whole = full((rows, width))
    return pl.pallas_call(
        functools.partial(feed_kernel, length),
        grid=(steps,),
        in_specs=[
            pl.BlockSpec(memory_space=pltpu.SMEM),
            whole,
            whole,
            full(out_w.shape),
            full(vec.shape),
            pl.BlockSpec((width, width), lambda i: (0, i)),
            pl.BlockSpec((1, width), lambda i: (0, i)),
            pl.BlockSpec((width, width), lambda i: (i, 0)),
        ],
        out_specs=[
            whole,
            pl.BlockSpec((rows, width), lambda i: (0, i)),
            pl.BlockSpec((rows, width), lambda i: (0, i)),
            whole,
            full((rows, 1)),
            whole,
            full((rows, 1)),
            whole,
        ],
        out_shape=[
            jax.ShapeDtypeStruct((rows, width), BF),
            jax.ShapeDtypeStruct((rows, hidden), BF),
            jax.ShapeDtypeStruct((rows, hidden), BF),
            jax.ShapeDtypeStruct((rows, width), BF),
            jax.ShapeDtypeStruct((rows, 1), F32),
            jax.ShapeDtypeStruct((rows, width), BF),
            jax.ShapeDtypeStruct((rows, 1), F32),
            jax.ShapeDtypeStruct((rows, width), BF),
        ],
        scratch_shapes=[pltpu.VMEM((rows, width), F32)],
        compiler_params=params(),
        cost_estimate=cost(18 * rows * width * width, 40 * rows * width, 8 * rows * width),
        name="feed",
    )(exit_layer, tokens, ctx, out_w, vec, up, up_bias, down)


def leave_kernel(
    length,
    classes,
    exit_ref,
    output_ref,
    unit2_ref,
    scale2_ref,
    grad_ref,
    pool_ref,
    vec_ref,
    class_bias_ref,
    logit_grad_ref,
    act_ref,
    outer_ref,
    branch_ref,
    down_grad_ref,
    pool_grad_ref,
    sums_ref,
    class_grad_ref,
    logits_ref,
    stats_ref,
    lead_ref,
):
    step = pl.program_id(0)
    rows, width = output_ref.shape
    count = rows // length

    @pl.when(step == 0)
    def _():
        place = lax.broadcasted_iota(jnp.int32, (count, 1), 0)
        active = jnp.zeros((count, 1), F32)
        for seq in range(count):
            on = (exit_ref[seq] >= LAYER).astype(F32)
            active = jnp.where(place == seq, on, active)
        leading = jnp.concatenate(
            [output_ref[seq * length : seq * length + 1].astype(F32) for seq in range(count)],
            axis=0,
        ).astype(BF)
        pooled = jnp.tanh(nn(leading, pool_ref[...]) + vec_ref[POOL_BIAS : POOL_BIAS + 1])
        pooled_low = pooled.astype(BF)
        used = lax.broadcasted_iota(jnp.int32, (8, width), 0) < classes
        class_rows = jnp.where(used, vec_ref[CLASS_ROWS : CLASS_ROWS + 8], 0.0).astype(BF)
        raw = nt(pooled_low, class_rows) + class_bias_ref[...]
        lane = lax.broadcasted_iota(jnp.int32, raw.shape, 1) < classes
        top = jnp.max(jnp.where(lane, raw, -jnp.inf), axis=-1, keepdims=True)
        spread = jnp.where(lane, jnp.exp(raw - top), 0.0)
        logprob = raw - top - jnp.log(jnp.sum(spread, axis=-1, keepdims=True))
        entropy = -jnp.sum(
            jnp.where(lane, jnp.exp(logprob) * logprob, 0.0), axis=-1, keepdims=True
        )
        logits_ref[...] = raw * active
        class_grad = (logit_grad_ref[...].astype(F32) * active).astype(BF)
        stats_ref[0:1] = jnp.broadcast_to(jnp.sum(entropy * active, axis=0, keepdims=True), (1, 8))
        stats_ref[1:2] = jnp.sum(class_grad.astype(F32), axis=0, keepdims=True)
        class_grad_ref[...] = tn(class_grad, pooled_low)
        pooled_grad = nn(class_grad, class_rows)
        pre_grad = (pooled_grad * (1.0 - pooled * pooled)).astype(BF)
        sums_ref[3:4] = jnp.sum(pre_grad.astype(F32), axis=0, keepdims=True)
        pool_grad_ref[...] = tn(leading, pre_grad).astype(BF)
        lead_ref[...] = nt(pre_grad, pool_ref[...])
        head = lax.broadcasted_iota(jnp.int32, (length, 1), 0) == 0
        gain = vec_ref[BLOCK_GAIN : BLOCK_GAIN + 1]
        gain_sum = jnp.zeros((1, width), F32)
        shift_sum = jnp.zeros((1, width), F32)
        bias_sum = jnp.zeros((1, width), F32)
        for seq in range(count):
            at = slice(seq * length, (seq + 1) * length)
            on = (exit_ref[seq] >= LAYER).astype(F32)
            top_grad = (
                grad_ref[at].astype(F32) + jnp.where(head, lead_ref[seq : seq + 1], 0.0)
            ) * on
            unit = unit2_ref[at].astype(F32)
            outer = norm_back(top_grad, unit, scale2_ref[at], gain)
            branch = outer.astype(BF)
            outer_ref[at] = outer
            branch_ref[at] = branch
            gain_sum += jnp.sum(top_grad * unit, axis=0, keepdims=True)
            shift_sum += jnp.sum(top_grad, axis=0, keepdims=True)
            bias_sum += jnp.sum(branch.astype(F32), axis=0, keepdims=True)
        sums_ref[0:1] = gain_sum
        sums_ref[1:2] = shift_sum
        sums_ref[2:3] = bias_sum

    @pl.when(step > 0)
    def _():
        down_grad_ref[...] = tn(act_ref[...], branch_ref[...]).astype(BF)


def leave(
    exit_layer, output, unit2, scale2, output_grad, pool, vec, class_bias, logit_grad, act,
    length, classes,
):
    rows, width = output.shape
    count = rows // length
    hidden = act.shape[1]
    steps = hidden // width
    whole = full((rows, width))
    return pl.pallas_call(
        functools.partial(leave_kernel, length, classes),
        grid=(steps + 1,),
        in_specs=[
            pl.BlockSpec(memory_space=pltpu.SMEM),
            whole,
            whole,
            full((rows, 1)),
            whole,
            full(pool.shape),
            full(vec.shape),
            full(class_bias.shape),
            full(logit_grad.shape),
            pl.BlockSpec((rows, width), lambda i: (0, jnp.maximum(i - 1, 0))),
        ],
        out_specs=[
            whole,
            whole,
            pl.BlockSpec((width, width), lambda i: (jnp.maximum(i - 1, 0), 0)),
            full((width, width)),
            full((4, width)),
            full((8, width)),
            full((count, 8)),
            full((2, 8)),
        ],
        out_shape=[
            jax.ShapeDtypeStruct((rows, width), F32),
            jax.ShapeDtypeStruct((rows, width), BF),
            jax.ShapeDtypeStruct((hidden, width), BF),
            jax.ShapeDtypeStruct((width, width), BF),
            jax.ShapeDtypeStruct((4, width), F32),
            jax.ShapeDtypeStruct((8, width), F32),
            jax.ShapeDtypeStruct((count, 8), F32),
            jax.ShapeDtypeStruct((2, 8), F32),
        ],
        scratch_shapes=[pltpu.VMEM((count, width), F32)],
        compiler_params=params(),
        cost_estimate=cost(8 * rows * width * width, 30 * rows * width),
        name="leave",
    )(exit_layer, output, unit2, scale2, output_grad, pool, vec, class_bias, logit_grad, act)


def feed_back_kernel(
    branch_ref,
    slope_ref,
    low_ref,
    down_ref,
    up_ref,
    outer_ref,
    unit1_ref,
    scale1_ref,
    out_w_ref,
    vec_ref,
    up_grad_ref,
    up_sum_ref,
    inner_ref,
    attended_ref,
    ctx_grad_ref,
    sums_ref,
    acc_ref,
    hid_ref,
):
    step = pl.program_id(0)
    rows, width = branch_ref.shape
    sub = 256

    @pl.when(step == 0)
    def _():
        acc_ref[...] = outer_ref[...]

    total = jnp.zeros((1, width), F32)
    for m in range(rows // sub):
        at = slice(m * sub, (m + 1) * sub)
        hid = (nt(branch_ref[at], down_ref[...]) * slope_ref[at].astype(F32)).astype(BF)
        hid_ref[at] = hid
        total += jnp.sum(hid.astype(F32), axis=0, keepdims=True)
        acc_ref[at] += nt(hid, up_ref[...])
    up_sum_ref[...] = total
    up_grad_ref[...] = tn(low_ref[...], hid_ref[...]).astype(BF)

    @pl.when(step == pl.num_programs(0) - 1)
    def _():
        gain = vec_ref[ATTN_GAIN : ATTN_GAIN + 1]
        gain_sum = jnp.zeros((1, width), F32)
        shift_sum = jnp.zeros((1, width), F32)
        bias_sum = jnp.zeros((1, width), F32)
        for m in range(rows // sub):
            at = slice(m * sub, (m + 1) * sub)
            grad = acc_ref[at]
            unit = unit1_ref[at].astype(F32)
            inner = norm_back(grad, unit, scale1_ref[at], gain)
            attended = inner.astype(BF)
            inner_ref[at] = inner
            attended_ref[at] = attended
            ctx_grad_ref[at] = nt(attended, out_w_ref[...]).astype(BF)
            gain_sum += jnp.sum(grad * unit, axis=0, keepdims=True)
            shift_sum += jnp.sum(grad, axis=0, keepdims=True)
            bias_sum += jnp.sum(attended.astype(F32), axis=0, keepdims=True)
        sums_ref[0:1] = gain_sum
        sums_ref[1:2] = shift_sum
        sums_ref[2:3] = bias_sum


def feed_back(branch, slope, low, down, up, outer, unit1, scale1, out_w, vec):
    rows, width = branch.shape
    hidden = slope.shape[1]
    steps = hidden // width
    whole = full((rows, width))
    return pl.pallas_call(
        feed_back_kernel,
        grid=(steps,),
        in_specs=[
            whole,
            pl.BlockSpec((rows, width), lambda i: (0, i)),
            whole,
            pl.BlockSpec((width, width), lambda i: (i, 0)),
            pl.BlockSpec((width, width), lambda i: (0, i)),
            whole,
            whole,
            full((rows, 1)),
            full(out_w.shape),
            full(vec.shape),
        ],
        out_specs=[
            pl.BlockSpec((width, width), lambda i: (0, i)),
            pl.BlockSpec((1, width), lambda i: (0, i)),
            whole,
            whole,
            whole,
            full((3, width)),
        ],
        out_shape=[
            jax.ShapeDtypeStruct((width, hidden), BF),
            jax.ShapeDtypeStruct((1, hidden), F32),
            jax.ShapeDtypeStruct((rows, width), F32),
            jax.ShapeDtypeStruct((rows, width), BF),
            jax.ShapeDtypeStruct((rows, width), BF),
            jax.ShapeDtypeStruct((3, width), F32),
        ],
        scratch_shapes=[pltpu.VMEM((rows, width), F32), pltpu.VMEM((rows, width), BF)],
        compiler_params=params(),
        cost_estimate=cost(26 * rows * width * width, 40 * rows * width),
        name="feed_back",
    )(branch, slope, low, down, up, outer, unit1, scale1, out_w, vec)


def attend_back_kernel(length, joined_ref, probs_ref, ctx_grad_ref, grad_ref, sum_ref):
    rows, width = ctx_grad_ref.shape
    pairs = width // PAIR

    def one(seq, carry):
        at = pl.ds(pl.multiple_of(seq * length, length), length)
        for pair in range(pairs):
            at_q = slice(pair * PAIR, (pair + 1) * PAIR)
            at_k = slice(width + pair * PAIR, width + (pair + 1) * PAIR)
            at_v = slice(2 * width + pair * PAIR, 2 * width + (pair + 1) * PAIR)
            query = joined_ref[at, at_q] * jnp.asarray(0.125, BF)
            queries = split_heads(query)
            keys = split_heads(joined_ref[at, at_k])
            vals = split_heads(joined_ref[at, at_v])
            ctx_grad = ctx_grad_ref[at, at_q]
            ctx_grads = split_heads(ctx_grad)
            probs = probs_ref[seq, pair]
            prob_grad = nt(vals, ctx_grad)
            halves = []
            for head in range(2):
                cut = slice(head * length, (head + 1) * length)
                held = probs[cut].astype(F32)
                part = prob_grad[cut]
                base = jnp.sum(part * held, axis=0, keepdims=True)
                halves.append((held * (part - base)).astype(BF))
            stacked = jnp.concatenate(halves, axis=0)
            beside = jnp.concatenate(halves, axis=1)
            probs_beside = jnp.concatenate([probs[:length], probs[length:]], axis=1)
            grad_ref[at, at_q] = (tn(stacked, keys) * 0.125).astype(BF)
            grad_ref[at, at_k] = nn(beside, queries).astype(BF)
            grad_ref[at, at_v] = nn(probs_beside, ctx_grads).astype(BF)
        return carry

    lax.fori_loop(0, rows // length, one, 0)
    total = jnp.zeros(sum_ref.shape, F32)
    for m in range(rows // length):
        total += jnp.sum(
            grad_ref[m * length : (m + 1) * length].astype(F32), axis=0, keepdims=True
        )

    @pl.when(pl.program_id(0) == 0)
    def _():
        sum_ref[...] = total

    @pl.when(pl.program_id(0) > 0)
    def _():
        sum_ref[...] += total


def attend_back(joined, probs, ctx_grad, length):
    rows, width = ctx_grad.shape
    count = rows // length
    steps = 2
    block = rows // steps
    pairs = width // PAIR
    return pl.pallas_call(
        functools.partial(attend_back_kernel, length),
        grid=(steps,),
        in_specs=[
            pl.BlockSpec((block, 3 * width), lambda i: (i, 0)),
            pl.BlockSpec((count // steps, pairs, 2 * length, length), lambda i: (i, 0, 0, 0)),
            pl.BlockSpec((block, width), lambda i: (i, 0)),
        ],
        out_specs=[
            pl.BlockSpec((block, 3 * width), lambda i: (i, 0)),
            full((1, 3 * width)),
        ],
        out_shape=[
            jax.ShapeDtypeStruct((rows, 3 * width), BF),
            jax.ShapeDtypeStruct((1, 3 * width), F32),
        ],
        compiler_params=params(),
        cost_estimate=cost(8 * rows * width * width, 20 * rows * width),
        name="attend_back",
    )(joined, probs, ctx_grad)


def weight_grads_kernel(tok_ref, ctx_ref, joined_ref, attended_ref, out_ref):
    last = pl.num_programs(0) - 1

    @pl.when(pl.program_id(0) < last)
    def _():
        out_ref[...] = tn(tok_ref[...], joined_ref[...]).astype(BF)

    @pl.when(pl.program_id(0) == last)
    def _():
        out_ref[...] = tn(ctx_ref[...], attended_ref[...]).astype(BF)


def weight_grads(tokens, ctx, joined_grad, attended):
    rows, width = tokens.shape
    whole = full((rows, width))
    return pl.pallas_call(
        weight_grads_kernel,
        grid=(4,),
        in_specs=[
            whole,
            whole,
            pl.BlockSpec((rows, width), lambda i: (0, jnp.minimum(i, 2))),
            whole,
        ],
        out_specs=pl.BlockSpec((width, width), lambda i: (0, i)),
        out_shape=jax.ShapeDtypeStruct((width, 4 * width), BF),
        compiler_params=params(),
        cost_estimate=cost(8 * rows * width * width, 20 * rows * width),
        name="weight_grads",
    )(tokens, ctx, joined_grad, attended)


def input_kernel(inner_ref, joined_ref, w_ref, out_ref):
    out_ref[...] = (inner_ref[...] + nt(joined_ref[...], w_ref[...])).astype(BF)


def input_back(inner, joined_grad, qkv):
    rows, width = inner.shape
    steps = 4
    block = rows // steps
    return pl.pallas_call(
        input_kernel,
        grid=(steps,),
        in_specs=[
            pl.BlockSpec((block, width), lambda i: (i, 0)),
            pl.BlockSpec((block, 3 * width), lambda i: (i, 0)),
            full(qkv.shape),
        ],
        out_specs=pl.BlockSpec((block, width), lambda i: (i, 0)),
        out_shape=jax.ShapeDtypeStruct((rows, width), BF),
        compiler_params=params(),
        cost_estimate=cost(6 * rows * width * width, 12 * rows * width),
        name="input_back",
    )(inner, joined_grad, qkv)


def pack_vectors(rows, up_bias, class_weight):
    first = jnp.concatenate(rows[:8] + [class_weight.T.reshape(-1)] + rows[8:])
    return jnp.concatenate([first, up_bias])[None]


def per_device(
    tokens,
    exit_layer,
    qkv_weight,
    query_bias,
    value_bias,
    out_weight,
    out_bias,
    attn_gain,
    attn_shift,
    up_weight,
    up_bias,
    down_weight,
    down_bias,
    block_gain,
    block_shift,
    pool_weight,
    pool_bias,
    class_weight,
    class_bias,
    output_grad,
    logit_grad,
):
    reps = lax.axis_size("rep")
    shards = lax.axis_size("fsdp")
    mine = lax.axis_index("fsdp")
    rows, width = tokens.shape
    count = exit_layer.shape[0]
    length = rows // count
    classes = class_weight.shape[1]
    part = out_weight.shape[0]
    hidden = up_weight.shape[1]

    def gather(shard):
        return lax.all_gather(shard, "fsdp", axis=0, tiled=True)

    small = gather(
        pack_vectors(
            [
                query_bias,
                value_bias,
                out_bias,
                attn_gain,
                attn_shift,
                down_bias,
                block_gain,
                block_shift,
                pool_bias,
            ],
            up_bias,
            class_weight,
        )
    )
    vec = (
        small[:, : VECTOR_ROWS * part]
        .reshape(shards, VECTOR_ROWS, part)
        .transpose(1, 0, 2)
        .reshape(VECTOR_ROWS, width)
        .astype(F32)
    )
    vec = jnp.pad(vec, ((0, 16 - VECTOR_ROWS), (0, 0)))
    up_row = small[:, VECTOR_ROWS * part :].reshape(1, hidden).astype(F32)
    bias_row = jnp.concatenate(
        [vec[:1], jnp.zeros((1, width), F32), vec[1:2]], axis=1
    )
    qkv = gather(qkv_weight)
    out_w = gather(out_weight)
    up = gather(up_weight)
    down = gather(down_weight)
    pool = gather(pool_weight)

    joined, probs, ctx = attend(tokens, qkv, bias_row, length)
    low, act, slope, unit1, scale1, unit2, scale2, output = feed(
        exit_layer, tokens, ctx, out_w, vec, up, up_row, down, length
    )
    class_bias_row = jnp.pad(class_bias.astype(F32), (0, 8 - classes))[None]
    logit_grad_rows = jnp.pad(logit_grad, ((0, 0), (0, 8 - classes)))
    outer, branch, down_grad, pool_grad, exit_sums, class_grad, logits, stats = leave(
        exit_layer,
        output,
        unit2,
        scale2,
        output_grad,
        pool,
        vec,
        class_bias_row,
        logit_grad_rows,
        act,
        length,
        classes,
    )
    up_grad, up_sum, inner, attended, ctx_grad, feed_sums = feed_back(
        branch, slope, low, down, up, outer, unit1, scale1, out_w, vec
    )
    joined_grad, joined_sum = attend_back(joined, probs, ctx_grad, length)
    joint_grad = weight_grads(tokens, ctx, joined_grad, attended)
    input_grad = input_back(inner, joined_grad, qkv)

    def scatter(grad):
        return lax.psum_scatter(grad, "fsdp", scatter_dimension=0, tiled=True)

    down_part = scatter(down_grad)
    pool_part = scatter(pool_grad)
    up_part = scatter(up_grad)
    joint_part = scatter(joint_grad)
    down_part, pool_part, up_part, joint_part = lax.psum(
        (down_part, pool_part, up_part, joint_part), "rep"
    )
    joint_part = joint_part.astype(F32)

    stats_row = jnp.pad(stats.reshape(1, -1), ((0, 0), (0, width - stats.size)))
    small_sums = jnp.concatenate(
        [
            joined_sum.reshape(3, width),
            feed_sums,
            exit_sums,
            class_grad[:classes],
            up_sum.reshape(hidden // width, width),
            stats_row,
        ],
        axis=0,
    )
    small_sums = lax.psum(small_sums, ("rep", "fsdp"))
    own = lax.dynamic_slice_in_dim(small_sums, mine * part, part, axis=1)
    up_at = 10 + classes
    up_own = lax.dynamic_slice_in_dim(
        small_sums[up_at : up_at + hidden // width].reshape(-1), mine * (hidden // shards),
        hidden // shards,
    )
    stats_total = small_sums[-1]
    seqs_total = count * reps * shards
    return (
        output,
        logits[:, :classes],
        stats_total[0] / seqs_total,
        input_grad,
        joint_part[:, : 3 * width],
        own[0],
        own[2],
        joint_part[:, 3 * width :],
        own[5],
        own[3],
        own[4],
        up_part.astype(F32),
        up_own,
        down_part.astype(F32),
        own[8],
        own[6],
        own[7],
        pool_part.astype(F32),
        own[9],
        own[10 : 10 + classes].T,
        stats_total[8 : 8 + classes],
    )


def solution(mesh):
    return jax.shard_map(
        per_device,
        mesh=mesh,
        in_specs=(
            P(("rep", "fsdp"), None),
            P(("rep", "fsdp")),
            P("fsdp", None),
            P("fsdp"),
            P("fsdp"),
            P("fsdp", None),
            P("fsdp"),
            P("fsdp"),
            P("fsdp"),
            P("fsdp", None),
            P("fsdp"),
            P("fsdp", None),
            P("fsdp"),
            P("fsdp"),
            P("fsdp"),
            P("fsdp", None),
            P("fsdp"),
            P("fsdp", None),
            P(),
            P(("rep", "fsdp"), None),
            P(("rep", "fsdp"), None),
        ),
        out_specs=(
            P(("rep", "fsdp"), None),
            P(("rep", "fsdp"), None),
            P(),
            P(("rep", "fsdp"), None),
            P("fsdp", None),
            P("fsdp"),
            P("fsdp"),
            P("fsdp", None),
            P("fsdp"),
            P("fsdp"),
            P("fsdp"),
            P("fsdp", None),
            P("fsdp"),
            P("fsdp", None),
            P("fsdp"),
            P("fsdp"),
            P("fsdp"),
            P("fsdp", None),
            P("fsdp"),
            P("fsdp", None),
            P(),
        ),
        check_vma=False,
    )
```

```python
import functools

import jax
import jax.numpy as jnp
from jax import lax
from jax.experimental import pallas as pl
from jax.experimental.pallas import tpu as pltpu
from jax.sharding import PartitionSpec as P

HD = 64
LAYER = 6
PAIR = 2 * HD
VMEM_BYTES = 58 * 2**20
BF = jnp.bfloat16
F32 = jnp.float32

QUERY_BIAS, VALUE_BIAS, OUT_BIAS, ATTN_GAIN, ATTN_SHIFT = 0, 1, 2, 3, 4
DOWN_BIAS, BLOCK_GAIN, BLOCK_SHIFT, CLASS_ROWS, POOL_BIAS = 5, 6, 7, 8, 11
VECTOR_ROWS = 12


def nn(left, right):
    return jnp.dot(left, right, preferred_element_type=F32)


def tn(left, right):
    return lax.dot_general(left, right, (((0,), (0,)), ((), ())), preferred_element_type=F32)


def nt(left, right):
    return lax.dot_general(left, right, (((1,), (1,)), ((), ())), preferred_element_type=F32)


def full(shape):
    return pl.BlockSpec(shape, lambda *at: (0,) * len(shape))


def params():
    return pltpu.CompilerParams(
        dimension_semantics=("arbitrary",), vmem_limit_bytes=VMEM_BYTES
    )


def cost(flops, moved, trans=0):
    return pl.CostEstimate(flops=flops, bytes_accessed=moved, transcendentals=trans)


def split_heads(pair):
    lane = lax.broadcasted_iota(jnp.int32, pair.shape, 1)
    zero = jnp.zeros_like(pair)
    return jnp.concatenate(
        [jnp.where(lane < HD, pair, zero), jnp.where(lane < HD, zero, pair)], axis=0
    )


def norm_stats(values):
    center = values - jnp.mean(values, axis=-1, keepdims=True)
    spread = jnp.mean(center * center, axis=-1, keepdims=True)
    scale = lax.rsqrt(spread + 1e-06)
    return center * scale, scale


def norm_back(grad, unit, scale, gain):
    inner = grad * gain
    first = jnp.mean(inner, axis=-1, keepdims=True)
    second = jnp.mean(inner * unit, axis=-1, keepdims=True)
    return scale * (inner - first - unit * second)


def gelu_parts(values):
    size = jnp.abs(values)
    t = 1.0 / (1.0 + 0.23164189 * size)
    bell = jnp.exp(-0.5 * values * values)
    poly = t * (
        0.127414796
        + t * (-0.142248368 + t * (0.7107068705 + t * (-0.7265760135 + t * 0.5307027145)))
    )
    tail = poly * bell
    below = jnp.where(values >= 0.0, 1.0 - tail, tail)
    return values * below, below + values * (bell * 0.3989422804014327)


def attend_kernel(length, tok_ref, w_ref, bias_ref, joined_ref, probs_ref, ctx_ref):
    rows, width = ctx_ref.shape
    pairs = width // PAIR
    for part in range(3):
        cols = slice(part * width, (part + 1) * width)
        joined_ref[:, cols] = (nn(tok_ref[...], w_ref[part]) + bias_ref[:, cols]).astype(BF)

    def one(seq, carry):
        at = pl.ds(pl.multiple_of(seq * length, length), length)
        for pair in range(pairs):
            cols = slice(pair * PAIR, (pair + 1) * PAIR)
            query = joined_ref[at, cols] * jnp.asarray(0.125, BF)
            keys = split_heads(joined_ref[at, width + pair * PAIR : width + (pair + 1) * PAIR])
            vals = split_heads(
                joined_ref[at, 2 * width + pair * PAIR : 2 * width + (pair + 1) * PAIR]
            )
            scores = nt(keys, query)
            halves = []
            for head in range(2):
                part = scores[head * length : (head + 1) * length]
                part = jnp.exp(part - jnp.max(part, axis=0, keepdims=True))
                part = part * (1.0 / jnp.sum(part, axis=0, keepdims=True))
                halves.append(part.astype(BF))
            probs = jnp.concatenate(halves, axis=0)
            probs_ref[seq, pair] = probs
            ctx_ref[at, cols] = tn(probs, vals).astype(BF)
        return carry

    lax.fori_loop(0, rows // length, one, 0)


def attend(tokens, qkv, bias_row, length):
    rows, width = tokens.shape
    count = rows // length
    steps = 2
    block = rows // steps
    pairs = width // PAIR
    return pl.pallas_call(
        functools.partial(attend_kernel, length),
        grid=(steps,),
        in_specs=[
            pl.BlockSpec((block, width), lambda i: (i, 0)),
            full((3, width, width)),
            full(bias_row.shape),
        ],
        out_specs=[
            pl.BlockSpec((block, 3 * width), lambda i: (i, 0)),
            pl.BlockSpec((count // steps, pairs, 2 * length, length), lambda i: (i, 0, 0, 0)),
            pl.BlockSpec((block, width), lambda i: (i, 0)),
        ],
        out_shape=[
            jax.ShapeDtypeStruct((rows, 3 * width), BF),
            jax.ShapeDtypeStruct((count, pairs, 2 * length, length), BF),
            jax.ShapeDtypeStruct((rows, width), BF),
        ],
        compiler_params=params(),
        cost_estimate=cost(8 * rows * width * width, 20 * rows * width, rows * width),
        name="attend",
    )(tokens, qkv, bias_row)


def feed_kernel(
    length,
    exit_ref,
    tok_ref,
    ctx_ref,
    out_w_ref,
    vec_ref,
    up_ref,
    up_b_ref,
    down_ref,
    low_ref,
    act_ref,
    slope_ref,
    unit1_ref,
    scale1_ref,
    unit2_ref,
    scale2_ref,
    output_ref,
    acc_ref,
):
    step = pl.program_id(0)
    rows = tok_ref.shape[0]
    sub = 256

    @pl.when(step == 0)
    def _():
        for m in range(rows // sub):
            at = slice(m * sub, (m + 1) * sub)
            inner = tok_ref[at].astype(F32) + (
                nn(ctx_ref[at], out_w_ref[0]) + vec_ref[OUT_BIAS : OUT_BIAS + 1]
            )
            unit, scale = norm_stats(inner)
            first = unit * vec_ref[ATTN_GAIN : ATTN_GAIN + 1] + vec_ref[ATTN_SHIFT : ATTN_SHIFT + 1]
            unit1_ref[at] = unit.astype(BF)
            scale1_ref[at] = scale
            low_ref[at] = first.astype(BF)
            acc_ref[at] = first + vec_ref[DOWN_BIAS : DOWN_BIAS + 1]

    for m in range(rows // sub):
        at = slice(m * sub, (m + 1) * sub)
        hidden = nn(low_ref[at], up_ref[0]) + up_b_ref[...]
        act, slope = gelu_parts(hidden)
        act = act.astype(BF)
        act_ref[at] = act
        slope_ref[at] = slope.astype(BF)
        acc_ref[at] += nn(act, down_ref[...])

    @pl.when(step == pl.num_programs(0) - 1)
    def _():
        for seq in range(rows // length):
            at = slice(seq * length, (seq + 1) * length)
            active = (exit_ref[seq] >= LAYER).astype(F32)
            unit, scale = norm_stats(acc_ref[at])
            unit2_ref[at] = unit.astype(BF)
            scale2_ref[at] = scale
            result = (
                unit * vec_ref[BLOCK_GAIN : BLOCK_GAIN + 1] + vec_ref[BLOCK_SHIFT : BLOCK_SHIFT + 1]
            ) * active
            output_ref[at] = result.astype(BF)


def feed(exit_layer, tokens, ctx, out_w, vec, up, up_bias, down, length):
    rows, width = tokens.shape
    steps = up.shape[0]
    hidden = steps * width
    whole = full((rows, width))
    return pl.pallas_call(
        functools.partial(feed_kernel, length),
        grid=(steps,),
        in_specs=[
            pl.BlockSpec(memory_space=pltpu.SMEM),
            whole,
            whole,
            pl.BlockSpec((1, width, width), lambda i: (3, 0, 0)),
            full(vec.shape),
            pl.BlockSpec((1, width, width), lambda i: (i, 0, 0)),
            pl.BlockSpec((1, width), lambda i: (0, i)),
            pl.BlockSpec((width, width), lambda i: (i, 0)),
        ],
        out_specs=[
            whole,
            pl.BlockSpec((rows, width), lambda i: (0, i)),
            pl.BlockSpec((rows, width), lambda i: (0, i)),
            whole,
            full((rows, 1)),
            whole,
            full((rows, 1)),
            whole,
        ],
        out_shape=[
            jax.ShapeDtypeStruct((rows, width), BF),
            jax.ShapeDtypeStruct((rows, hidden), BF),
            jax.ShapeDtypeStruct((rows, hidden), BF),
            jax.ShapeDtypeStruct((rows, width), BF),
            jax.ShapeDtypeStruct((rows, 1), F32),
            jax.ShapeDtypeStruct((rows, width), BF),
            jax.ShapeDtypeStruct((rows, 1), F32),
            jax.ShapeDtypeStruct((rows, width), BF),
        ],
        scratch_shapes=[pltpu.VMEM((rows, width), F32)],
        compiler_params=params(),
        cost_estimate=cost(18 * rows * width * width, 40 * rows * width, 8 * rows * width),
        name="feed",
    )(exit_layer, tokens, ctx, out_w, vec, up, up_bias, down)


def leave_kernel(
    length,
    classes,
    exit_ref,
    output_ref,
    unit2_ref,
    scale2_ref,
    grad_ref,
    pool_ref,
    vec_ref,
    class_bias_ref,
    logit_grad_ref,
    act_ref,
    outer_ref,
    branch_ref,
    down_grad_ref,
    pool_grad_ref,
    sums_ref,
    class_grad_ref,
    logits_ref,
    stats_ref,
    lead_ref,
):
    step = pl.program_id(0)
    rows, width = output_ref.shape
    count = rows // length

    @pl.when(step == 0)
    def _():
        place = lax.broadcasted_iota(jnp.int32, (count, 1), 0)
        active = jnp.zeros((count, 1), F32)
        for seq in range(count):
            on = (exit_ref[seq] >= LAYER).astype(F32)
            active = jnp.where(place == seq, on, active)
        leading = jnp.concatenate(
            [output_ref[seq * length : seq * length + 1].astype(F32) for seq in range(count)],
            axis=0,
        ).astype(BF)
        pooled = jnp.tanh(nn(leading, pool_ref[...]) + vec_ref[POOL_BIAS : POOL_BIAS + 1])
        pooled_low = pooled.astype(BF)
        used = lax.broadcasted_iota(jnp.int32, (8, width), 0) < classes
        class_rows = jnp.where(used, vec_ref[CLASS_ROWS : CLASS_ROWS + 8], 0.0).astype(BF)
        raw = nt(pooled_low, class_rows) + class_bias_ref[...]
        lane = lax.broadcasted_iota(jnp.int32, raw.shape, 1) < classes
        top = jnp.max(jnp.where(lane, raw, -jnp.inf), axis=-1, keepdims=True)
        spread = jnp.where(lane, jnp.exp(raw - top), 0.0)
        logprob = raw - top - jnp.log(jnp.sum(spread, axis=-1, keepdims=True))
        entropy = -jnp.sum(
            jnp.where(lane, jnp.exp(logprob) * logprob, 0.0), axis=-1, keepdims=True
        )
        logits_ref[...] = raw * active
        class_grad = (logit_grad_ref[...].astype(F32) * active).astype(BF)
        stats_ref[0:1] = jnp.broadcast_to(jnp.sum(entropy * active, axis=0, keepdims=True), (1, 8))
        stats_ref[1:2] = jnp.sum(class_grad.astype(F32), axis=0, keepdims=True)
        class_grad_ref[...] = tn(class_grad, pooled_low)
        pooled_grad = nn(class_grad, class_rows)
        pre_grad = (pooled_grad * (1.0 - pooled * pooled)).astype(BF)
        sums_ref[3:4] = jnp.sum(pre_grad.astype(F32), axis=0, keepdims=True)
        pool_grad_ref[...] = tn(leading, pre_grad).astype(BF)
        lead_ref[...] = nt(pre_grad, pool_ref[...])
        head = lax.broadcasted_iota(jnp.int32, (length, 1), 0) == 0
        gain = vec_ref[BLOCK_GAIN : BLOCK_GAIN + 1]
        gain_sum = jnp.zeros((1, width), F32)
        shift_sum = jnp.zeros((1, width), F32)
        bias_sum = jnp.zeros((1, width), F32)
        for seq in range(count):
            at = slice(seq * length, (seq + 1) * length)
            on = (exit_ref[seq] >= LAYER).astype(F32)
            top_grad = (
                grad_ref[at].astype(F32) + jnp.where(head, lead_ref[seq : seq + 1], 0.0)
            ) * on
            unit = unit2_ref[at].astype(F32)
            outer = norm_back(top_grad, unit, scale2_ref[at], gain)
            branch = outer.astype(BF)
            outer_ref[at] = outer
            branch_ref[at] = branch
            gain_sum += jnp.sum(top_grad * unit, axis=0, keepdims=True)
            shift_sum += jnp.sum(top_grad, axis=0, keepdims=True)
            bias_sum += jnp.sum(branch.astype(F32), axis=0, keepdims=True)
        sums_ref[0:1] = gain_sum
        sums_ref[1:2] = shift_sum
        sums_ref[2:3] = bias_sum

    @pl.when(step > 0)
    def _():
        down_grad_ref[...] = tn(act_ref[...], branch_ref[...]).astype(BF)


def leave(
    exit_layer, output, unit2, scale2, output_grad, pool, vec, class_bias, logit_grad, act,
    length, classes,
):
    rows, width = output.shape
    count = rows // length
    hidden = act.shape[1]
    steps = hidden // width
    whole = full((rows, width))
    return pl.pallas_call(
        functools.partial(leave_kernel, length, classes),
        grid=(steps + 1,),
        in_specs=[
            pl.BlockSpec(memory_space=pltpu.SMEM),
            whole,
            whole,
            full((rows, 1)),
            whole,
            full(pool.shape),
            full(vec.shape),
            full(class_bias.shape),
            full(logit_grad.shape),
            pl.BlockSpec((rows, width), lambda i: (0, jnp.maximum(i - 1, 0))),
        ],
        out_specs=[
            whole,
            whole,
            pl.BlockSpec((width, width), lambda i: (jnp.maximum(i - 1, 0), 0)),
            full((width, width)),
            full((4, width)),
            full((8, width)),
            full((count, 8)),
            full((2, 8)),
        ],
        out_shape=[
            jax.ShapeDtypeStruct((rows, width), F32),
            jax.ShapeDtypeStruct((rows, width), BF),
            jax.ShapeDtypeStruct((hidden, width), BF),
            jax.ShapeDtypeStruct((width, width), BF),
            jax.ShapeDtypeStruct((4, width), F32),
            jax.ShapeDtypeStruct((8, width), F32),
            jax.ShapeDtypeStruct((count, 8), F32),
            jax.ShapeDtypeStruct((2, 8), F32),
        ],
        scratch_shapes=[pltpu.VMEM((count, width), F32)],
        compiler_params=params(),
        cost_estimate=cost(8 * rows * width * width, 30 * rows * width),
        name="leave",
    )(exit_layer, output, unit2, scale2, output_grad, pool, vec, class_bias, logit_grad, act)


def feed_back_kernel(
    branch_ref,
    slope_ref,
    low_ref,
    down_ref,
    up_ref,
    outer_ref,
    unit1_ref,
    scale1_ref,
    out_w_ref,
    vec_ref,
    up_grad_ref,
    up_sum_ref,
    inner_ref,
    attended_ref,
    ctx_grad_ref,
    sums_ref,
    acc_ref,
    hid_ref,
):
    step = pl.program_id(0)
    rows, width = branch_ref.shape
    sub = 256

    @pl.when(step == 0)
    def _():
        acc_ref[...] = outer_ref[...]

    total = jnp.zeros((1, width), F32)
    for m in range(rows // sub):
        at = slice(m * sub, (m + 1) * sub)
        hid = (nt(branch_ref[at], down_ref[...]) * slope_ref[at].astype(F32)).astype(BF)
        hid_ref[at] = hid
        total += jnp.sum(hid.astype(F32), axis=0, keepdims=True)
        acc_ref[at] += nt(hid, up_ref[0])
    up_sum_ref[...] = total
    up_grad_ref[...] = tn(low_ref[...], hid_ref[...]).astype(BF)

    @pl.when(step == pl.num_programs(0) - 1)
    def _():
        gain = vec_ref[ATTN_GAIN : ATTN_GAIN + 1]
        gain_sum = jnp.zeros((1, width), F32)
        shift_sum = jnp.zeros((1, width), F32)
        bias_sum = jnp.zeros((1, width), F32)
        for m in range(rows // sub):
            at = slice(m * sub, (m + 1) * sub)
            grad = acc_ref[at]
            unit = unit1_ref[at].astype(F32)
            inner = norm_back(grad, unit, scale1_ref[at], gain)
            attended = inner.astype(BF)
            inner_ref[at] = inner
            attended_ref[at] = attended
            ctx_grad_ref[at] = nt(attended, out_w_ref[0]).astype(BF)
            gain_sum += jnp.sum(grad * unit, axis=0, keepdims=True)
            shift_sum += jnp.sum(grad, axis=0, keepdims=True)
            bias_sum += jnp.sum(attended.astype(F32), axis=0, keepdims=True)
        sums_ref[0:1] = gain_sum
        sums_ref[1:2] = shift_sum
        sums_ref[2:3] = bias_sum


def feed_back(branch, slope, low, down, up, outer, unit1, scale1, out_w, vec):
    rows, width = branch.shape
    hidden = slope.shape[1]
    steps = hidden // width
    whole = full((rows, width))
    return pl.pallas_call(
        feed_back_kernel,
        grid=(steps,),
        in_specs=[
            whole,
            pl.BlockSpec((rows, width), lambda i: (0, i)),
            whole,
            pl.BlockSpec((width, width), lambda i: (i, 0)),
            pl.BlockSpec((1, width, width), lambda i: (i, 0, 0)),
            whole,
            whole,
            full((rows, 1)),
            pl.BlockSpec((1, width, width), lambda i: (3, 0, 0)),
            full(vec.shape),
        ],
        out_specs=[
            pl.BlockSpec((width, width), lambda i: (0, i)),
            pl.BlockSpec((1, width), lambda i: (0, i)),
            whole,
            whole,
            whole,
            full((3, width)),
        ],
        out_shape=[
            jax.ShapeDtypeStruct((width, hidden), BF),
            jax.ShapeDtypeStruct((1, hidden), F32),
            jax.ShapeDtypeStruct((rows, width), F32),
            jax.ShapeDtypeStruct((rows, width), BF),
            jax.ShapeDtypeStruct((rows, width), BF),
            jax.ShapeDtypeStruct((3, width), F32),
        ],
        scratch_shapes=[pltpu.VMEM((rows, width), F32), pltpu.VMEM((rows, width), BF)],
        compiler_params=params(),
        cost_estimate=cost(26 * rows * width * width, 40 * rows * width),
        name="feed_back",
    )(branch, slope, low, down, up, outer, unit1, scale1, out_w, vec)


def attend_back_kernel(length, joined_ref, probs_ref, ctx_grad_ref, grad_ref, sum_ref):
    rows, width = ctx_grad_ref.shape
    pairs = width // PAIR

    def one(seq, carry):
        at = pl.ds(pl.multiple_of(seq * length, length), length)
        for pair in range(pairs):
            at_q = slice(pair * PAIR, (pair + 1) * PAIR)
            at_k = slice(width + pair * PAIR, width + (pair + 1) * PAIR)
            at_v = slice(2 * width + pair * PAIR, 2 * width + (pair + 1) * PAIR)
            query = joined_ref[at, at_q] * jnp.asarray(0.125, BF)
            queries = split_heads(query)
            keys = split_heads(joined_ref[at, at_k])
            vals = split_heads(joined_ref[at, at_v])
            ctx_grad = ctx_grad_ref[at, at_q]
            ctx_grads = split_heads(ctx_grad)
            probs = probs_ref[seq, pair]
            prob_grad = nt(vals, ctx_grad)
            halves = []
            for head in range(2):
                cut = slice(head * length, (head + 1) * length)
                held = probs[cut].astype(F32)
                part = prob_grad[cut]
                base = jnp.sum(part * held, axis=0, keepdims=True)
                halves.append((held * (part - base)).astype(BF))
            stacked = jnp.concatenate(halves, axis=0)
            beside = jnp.concatenate(halves, axis=1)
            probs_beside = jnp.concatenate([probs[:length], probs[length:]], axis=1)
            grad_ref[at, at_q] = (tn(stacked, keys) * 0.125).astype(BF)
            grad_ref[at, at_k] = nn(beside, queries).astype(BF)
            grad_ref[at, at_v] = nn(probs_beside, ctx_grads).astype(BF)
        return carry

    lax.fori_loop(0, rows // length, one, 0)
    total = jnp.zeros(sum_ref.shape, F32)
    for m in range(rows // length):
        total += jnp.sum(
            grad_ref[m * length : (m + 1) * length].astype(F32), axis=0, keepdims=True
        )

    @pl.when(pl.program_id(0) == 0)
    def _():
        sum_ref[...] = total

    @pl.when(pl.program_id(0) > 0)
    def _():
        sum_ref[...] += total


def attend_back(joined, probs, ctx_grad, length):
    rows, width = ctx_grad.shape
    count = rows // length
    steps = 2
    block = rows // steps
    pairs = width // PAIR
    return pl.pallas_call(
        functools.partial(attend_back_kernel, length),
        grid=(steps,),
        in_specs=[
            pl.BlockSpec((block, 3 * width), lambda i: (i, 0)),
            pl.BlockSpec((count // steps, pairs, 2 * length, length), lambda i: (i, 0, 0, 0)),
            pl.BlockSpec((block, width), lambda i: (i, 0)),
        ],
        out_specs=[
            pl.BlockSpec((block, 3 * width), lambda i: (i, 0)),
            full((1, 3 * width)),
        ],
        out_shape=[
            jax.ShapeDtypeStruct((rows, 3 * width), BF),
            jax.ShapeDtypeStruct((1, 3 * width), F32),
        ],
        compiler_params=params(),
        cost_estimate=cost(8 * rows * width * width, 20 * rows * width),
        name="attend_back",
    )(joined, probs, ctx_grad)


def weight_grads_kernel(tok_ref, ctx_ref, joined_ref, attended_ref, out_ref):
    last = pl.num_programs(0) - 1

    @pl.when(pl.program_id(0) < last)
    def _():
        out_ref[...] = tn(tok_ref[...], joined_ref[...]).astype(BF)

    @pl.when(pl.program_id(0) == last)
    def _():
        out_ref[...] = tn(ctx_ref[...], attended_ref[...]).astype(BF)


def weight_grads(tokens, ctx, joined_grad, attended):
    rows, width = tokens.shape
    whole = full((rows, width))
    return pl.pallas_call(
        weight_grads_kernel,
        grid=(4,),
        in_specs=[
            whole,
            whole,
            pl.BlockSpec((rows, width), lambda i: (0, jnp.minimum(i, 2))),
            whole,
        ],
        out_specs=pl.BlockSpec((width, width), lambda i: (0, i)),
        out_shape=jax.ShapeDtypeStruct((width, 4 * width), BF),
        compiler_params=params(),
        cost_estimate=cost(8 * rows * width * width, 20 * rows * width),
        name="weight_grads",
    )(tokens, ctx, joined_grad, attended)


def input_kernel(inner_ref, joined_ref, w_ref, out_ref):
    width = inner_ref.shape[1]
    total = inner_ref[...]
    for part in range(3):
        total += nt(joined_ref[:, part * width : (part + 1) * width], w_ref[part])
    out_ref[...] = total.astype(BF)


def input_back(inner, joined_grad, qkv):
    rows, width = inner.shape
    steps = 4
    block = rows // steps
    return pl.pallas_call(
        input_kernel,
        grid=(steps,),
        in_specs=[
            pl.BlockSpec((block, width), lambda i: (i, 0)),
            pl.BlockSpec((block, 3 * width), lambda i: (i, 0)),
            full((3, width, width)),
        ],
        out_specs=pl.BlockSpec((block, width), lambda i: (i, 0)),
        out_shape=jax.ShapeDtypeStruct((rows, width), BF),
        compiler_params=params(),
        cost_estimate=cost(6 * rows * width * width, 12 * rows * width),
        name="input_back",
    )(inner, joined_grad, qkv)


def lay_kernel(chips, reps, place_ref, own_ref, twin_ref, *refs):
    far = chips - 1
    along = refs[:far]
    across = refs[far : far + reps - 1]
    swapped = refs[far + reps - 1 : far + 2 * reps - 1]
    out_ref, sems = refs[-2], refs[-1]
    rep, chip, core = place_ref[0], place_ref[1], place_ref[2]
    part, width = along[0].shape
    copies = []

    def put(source, block, at_chip, at_core):
        row = pl.multiple_of((at_chip * 2 + at_core) * part, part)
        copies.append(
            pltpu.make_async_copy(
                source, out_ref.at[block, pl.ds(row, part)], sems.at[len(copies)]
            )
        )
        copies[-1].start()

    for block in range(reps):
        cols = pl.ds(block * width, width)
        put(own_ref.at[:, cols], block, chip, core)
        put(twin_ref.at[:, cols], block, chip, 1 - core)
    for step in range(1, chips):
        source = lax.rem(chip + chips - step, chips)
        rows = pl.ds((step - 1) * part, part)
        put(along[step - 1], rep, source, core)
        put(swapped[0].at[rows], rep, source, 1 - core)
        for other in range(1, reps):
            put(across[other - 1].at[rows], rep ^ other, source, core)
            put(swapped[other].at[rows], rep ^ other, source, 1 - core)
    for copy in copies:
        copy.wait()


def lay(place, own, twin, along, across, swapped, chips, reps):
    part, width = along[0].shape
    anywhere = pl.BlockSpec(memory_space=pl.ANY)
    inputs = [own, twin, *along, *across, *swapped]
    return pl.pallas_call(
        functools.partial(lay_kernel, chips, reps),
        in_specs=[pl.BlockSpec(memory_space=pltpu.SMEM)] + [anywhere] * len(inputs),
        out_specs=anywhere,
        out_shape=jax.ShapeDtypeStruct((reps, chips * 2 * part, width), own.dtype),
        scratch_shapes=[pltpu.SemaphoreType.DMA((2 * chips * reps,))],
        cost_estimate=cost(0, 4 * reps * chips * 2 * part * width),
        name="lay",
    )(place, *inputs)


def pack_vectors(rows, up_bias, class_weight):
    first = jnp.concatenate(rows[:8] + [class_weight.T.reshape(-1)] + rows[8:])
    return jnp.concatenate([first, up_bias])[None]


def move(values, reps, chips, target):
    pairs = []
    for rep in range(reps):
        for chip in range(chips):
            for core in range(2):
                to_rep, to_chip, to_core = target(rep, chip, core)
                pairs.append(
                    (
                        (rep * chips + chip) * 2 + core,
                        (to_rep * chips + to_chip) * 2 + to_core,
                    )
                )
    return lax.ppermute(values, ("rep", "fsdp"), pairs)


def along_chips(step, chips):
    return lambda rep, chip, core: (rep, (chip + step) % chips, core)


def across_reps(other):
    return lambda rep, chip, core: (rep ^ other, chip, core)


def to_twin(rep, chip, core):
    return rep, chip, 1 - core


def gather_blocks(place, own, reps, chips, after):
    width = own.shape[1] // reps
    mine = lax.dynamic_slice_in_dim(own, place[0] * width, width, axis=1)
    if after is not None:
        mine, _ = lax.optimization_barrier((mine, after))
    along = [move(mine, reps, chips, along_chips(step, chips)) for step in range(1, chips)]
    twin = move(own, reps, chips, to_twin)
    stacked = jnp.concatenate(along, axis=0)
    across = [move(stacked, reps, chips, across_reps(other)) for other in range(1, reps)]
    swapped = [move(part, reps, chips, to_twin) for part in [stacked] + across]
    return lay(place, own, twin, along, across, swapped, chips, reps), along


def per_device(
    tokens,
    exit_layer,
    qkv_weight,
    query_bias,
    value_bias,
    out_weight,
    out_bias,
    attn_gain,
    attn_shift,
    up_weight,
    up_bias,
    down_weight,
    down_bias,
    block_gain,
    block_shift,
    pool_weight,
    pool_bias,
    class_weight,
    class_bias,
    output_grad,
    logit_grad,
):
    reps = lax.axis_size("rep")
    shards = lax.axis_size("fsdp")
    mine = lax.axis_index("fsdp")
    rows, width = tokens.shape
    count = exit_layer.shape[0]
    length = rows // count
    classes = class_weight.shape[1]
    part = out_weight.shape[0]
    hidden = up_weight.shape[1]

    def gather(shard):
        return lax.all_gather(shard, "fsdp", axis=0, tiled=True)

    small = gather(
        pack_vectors(
            [
                query_bias,
                value_bias,
                out_bias,
                attn_gain,
                attn_shift,
                down_bias,
                block_gain,
                block_shift,
                pool_bias,
            ],
            up_bias,
            class_weight,
        )
    )
    vec = (
        small[:, : VECTOR_ROWS * part]
        .reshape(shards, VECTOR_ROWS, part)
        .transpose(1, 0, 2)
        .reshape(VECTOR_ROWS, width)
        .astype(F32)
    )
    vec = jnp.pad(vec, ((0, 16 - VECTOR_ROWS), (0, 0)))
    up_row = small[:, VECTOR_ROWS * part :].reshape(1, hidden).astype(F32)
    bias_row = jnp.concatenate(
        [vec[:1], jnp.zeros((1, width), F32), vec[1:2]], axis=1
    )
    down = gather(down_weight)
    joint_own = jnp.concatenate([qkv_weight, out_weight], axis=1)
    if part % 16 == 0 and reps & (reps - 1) == 0 and reps * width == hidden:
        chips = shards // 2
        place = jnp.stack([lax.axis_index("rep"), mine // 2, mine % 2]).astype(jnp.int32)
        joint, sent = gather_blocks(place, joint_own, reps, chips, None)
        up, _ = gather_blocks(place, up_weight, reps, chips, sent)
    else:
        joint = jnp.stack(jnp.split(gather(joint_own), 4, axis=1))
        up = jnp.stack(jnp.split(gather(up_weight), hidden // width, axis=1))
    pool = gather(pool_weight)

    joined, probs, ctx = attend(tokens, joint, bias_row, length)
    low, act, slope, unit1, scale1, unit2, scale2, output = feed(
        exit_layer, tokens, ctx, joint, vec, up, up_row, down, length
    )
    class_bias_row = jnp.pad(class_bias.astype(F32), (0, 8 - classes))[None]
    logit_grad_rows = jnp.pad(logit_grad, ((0, 0), (0, 8 - classes)))
    outer, branch, down_grad, pool_grad, exit_sums, class_grad, logits, stats = leave(
        exit_layer,
        output,
        unit2,
        scale2,
        output_grad,
        pool,
        vec,
        class_bias_row,
        logit_grad_rows,
        act,
        length,
        classes,
    )
    up_grad, up_sum, inner, attended, ctx_grad, feed_sums = feed_back(
        branch, slope, low, down, up, outer, unit1, scale1, joint, vec
    )
    joined_grad, joined_sum = attend_back(joined, probs, ctx_grad, length)
    joint_grad = weight_grads(tokens, ctx, joined_grad, attended)
    input_grad = input_back(inner, joined_grad, joint)

    def scatter(grad):
        return lax.psum_scatter(grad, "fsdp", scatter_dimension=0, tiled=True)

    down_part = scatter(down_grad)
    pool_part = scatter(pool_grad)
    up_part = scatter(up_grad)
    joint_part = scatter(joint_grad)
    down_part, pool_part, up_part, joint_part = lax.psum(
        (down_part, pool_part, up_part, joint_part), "rep"
    )
    joint_part = joint_part.astype(F32)

    stats_row = jnp.pad(stats.reshape(1, -1), ((0, 0), (0, width - stats.size)))
    small_sums = jnp.concatenate(
        [
            joined_sum.reshape(3, width),
            feed_sums,
            exit_sums,
            class_grad[:classes],
            up_sum.reshape(hidden // width, width),
            stats_row,
        ],
        axis=0,
    )
    small_sums = lax.psum(small_sums, ("rep", "fsdp"))
    own = lax.dynamic_slice_in_dim(small_sums, mine * part, part, axis=1)
    up_at = 10 + classes
    up_own = lax.dynamic_slice_in_dim(
        small_sums[up_at : up_at + hidden // width].reshape(-1), mine * (hidden // shards),
        hidden // shards,
    )
    stats_total = small_sums[-1]
    seqs_total = count * reps * shards
    return (
        output,
        logits[:, :classes],
        stats_total[0] / seqs_total,
        input_grad,
        joint_part[:, : 3 * width],
        own[0],
        own[2],
        joint_part[:, 3 * width :],
        own[5],
        own[3],
        own[4],
        up_part.astype(F32),
        up_own,
        down_part.astype(F32),
        own[8],
        own[6],
        own[7],
        pool_part.astype(F32),
        own[9],
        own[10 : 10 + classes].T,
        stats_total[8 : 8 + classes],
    )


def solution(mesh):
    return jax.shard_map(
        per_device,
        mesh=mesh,
        in_specs=(
            P(("rep", "fsdp"), None),
            P(("rep", "fsdp")),
            P("fsdp", None),
            P("fsdp"),
            P("fsdp"),
            P("fsdp", None),
            P("fsdp"),
            P("fsdp"),
            P("fsdp"),
            P("fsdp", None),
            P("fsdp"),
            P("fsdp", None),
            P("fsdp"),
            P("fsdp"),
            P("fsdp"),
            P("fsdp", None),
            P("fsdp"),
            P("fsdp", None),
            P(),
            P(("rep", "fsdp"), None),
            P(("rep", "fsdp"), None),
        ),
        out_specs=(
            P(("rep", "fsdp"), None),
            P(("rep", "fsdp"), None),
            P(),
            P(("rep", "fsdp"), None),
            P("fsdp", None),
            P("fsdp"),
            P("fsdp"),
            P("fsdp", None),
            P("fsdp"),
            P("fsdp"),
            P("fsdp"),
            P("fsdp", None),
            P("fsdp"),
            P("fsdp", None),
            P("fsdp"),
            P("fsdp"),
            P("fsdp"),
            P("fsdp", None),
            P("fsdp"),
            P("fsdp", None),
            P(),
        ),
        check_vma=False,
    )
```

```python
import functools

import jax
import jax.numpy as jnp
from jax import lax
from jax.experimental import pallas as pl
from jax.experimental.pallas import tpu as pltpu
from jax.sharding import PartitionSpec as P

HD = 64
LAYER = 6
PAIR = 2 * HD
VMEM_BYTES = 58 * 2**20
BF = jnp.bfloat16
F32 = jnp.float32

QUERY_BIAS, VALUE_BIAS, OUT_BIAS, ATTN_GAIN, ATTN_SHIFT = 0, 1, 2, 3, 4
DOWN_BIAS, BLOCK_GAIN, BLOCK_SHIFT, CLASS_ROWS, POOL_BIAS = 5, 6, 7, 8, 11
VECTOR_ROWS = 12


def nn(left, right):
    return jnp.dot(left, right, preferred_element_type=F32)


def tn(left, right):
    return lax.dot_general(left, right, (((0,), (0,)), ((), ())), preferred_element_type=F32)


def nt(left, right):
    return lax.dot_general(left, right, (((1,), (1,)), ((), ())), preferred_element_type=F32)


def full(shape):
    return pl.BlockSpec(shape, lambda *at: (0,) * len(shape))


def params():
    return pltpu.CompilerParams(
        dimension_semantics=("arbitrary",), vmem_limit_bytes=VMEM_BYTES
    )


def cost(flops, moved, trans=0):
    return pl.CostEstimate(flops=flops, bytes_accessed=moved, transcendentals=trans)


def split_heads(pair):
    lane = lax.broadcasted_iota(jnp.int32, pair.shape, 1)
    zero = jnp.zeros_like(pair)
    return jnp.concatenate(
        [jnp.where(lane < HD, pair, zero), jnp.where(lane < HD, zero, pair)], axis=0
    )


def norm_stats(values):
    center = values - jnp.mean(values, axis=-1, keepdims=True)
    spread = jnp.mean(center * center, axis=-1, keepdims=True)
    scale = lax.rsqrt(spread + 1e-06)
    return center * scale, scale


def norm_back(grad, unit, scale, gain):
    inner = grad * gain
    first = jnp.mean(inner, axis=-1, keepdims=True)
    second = jnp.mean(inner * unit, axis=-1, keepdims=True)
    return scale * (inner - first - unit * second)


def gelu_parts(values):
    size = jnp.abs(values)
    t = 1.0 / (1.0 + 0.23164189 * size)
    bell = jnp.exp(-0.5 * values * values)
    poly = t * (
        0.127414796
        + t * (-0.142248368 + t * (0.7107068705 + t * (-0.7265760135 + t * 0.5307027145)))
    )
    tail = poly * bell
    below = jnp.where(values >= 0.0, 1.0 - tail, tail)
    return values * below, below + values * (bell * 0.3989422804014327)


def attend_kernel(length, tok_ref, w_ref, bias_ref, joined_ref, probs_ref, ctx_ref):
    rows, width = ctx_ref.shape
    pairs = width // PAIR
    for part in range(3):
        cols = slice(part * width, (part + 1) * width)
        joined_ref[:, cols] = (nn(tok_ref[...], w_ref[part]) + bias_ref[:, cols]).astype(BF)

    def one(seq, carry):
        at = pl.ds(pl.multiple_of(seq * length, length), length)
        for pair in range(pairs):
            cols = slice(pair * PAIR, (pair + 1) * PAIR)
            query = joined_ref[at, cols] * jnp.asarray(0.125, BF)
            keys = split_heads(joined_ref[at, width + pair * PAIR : width + (pair + 1) * PAIR])
            vals = split_heads(
                joined_ref[at, 2 * width + pair * PAIR : 2 * width + (pair + 1) * PAIR]
            )
            scores = nt(keys, query)
            halves = []
            for head in range(2):
                part = scores[head * length : (head + 1) * length]
                part = jnp.exp(part - jnp.max(part, axis=0, keepdims=True))
                part = part * (1.0 / jnp.sum(part, axis=0, keepdims=True))
                halves.append(part.astype(BF))
            probs = jnp.concatenate(halves, axis=0)
            probs_ref[seq, pair] = probs
            ctx_ref[at, cols] = tn(probs, vals).astype(BF)
        return carry

    lax.fori_loop(0, rows // length, one, 0)


def attend(tokens, qkv, bias_row, length):
    rows, width = tokens.shape
    count = rows // length
    steps = 2
    block = rows // steps
    pairs = width // PAIR
    return pl.pallas_call(
        functools.partial(attend_kernel, length),
        grid=(steps,),
        in_specs=[
            pl.BlockSpec((block, width), lambda i: (i, 0)),
            full((3, width, width)),
            full(bias_row.shape),
        ],
        out_specs=[
            pl.BlockSpec((block, 3 * width), lambda i: (i, 0)),
            pl.BlockSpec((count // steps, pairs, 2 * length, length), lambda i: (i, 0, 0, 0)),
            pl.BlockSpec((block, width), lambda i: (i, 0)),
        ],
        out_shape=[
            jax.ShapeDtypeStruct((rows, 3 * width), BF),
            jax.ShapeDtypeStruct((count, pairs, 2 * length, length), BF),
            jax.ShapeDtypeStruct((rows, width), BF),
        ],
        compiler_params=params(),
        cost_estimate=cost(8 * rows * width * width, 20 * rows * width, rows * width),
        name="attend",
    )(tokens, qkv, bias_row)


def feed_kernel(
    length,
    exit_ref,
    tok_ref,
    ctx_ref,
    out_w_ref,
    vec_ref,
    up_ref,
    up_b_ref,
    down_ref,
    low_ref,
    act_ref,
    slope_ref,
    unit1_ref,
    scale1_ref,
    unit2_ref,
    scale2_ref,
    output_ref,
    acc_ref,
):
    step = pl.program_id(0)
    rows = tok_ref.shape[0]
    sub = 256

    @pl.when(step == 0)
    def _():
        for m in range(rows // sub):
            at = slice(m * sub, (m + 1) * sub)
            inner = tok_ref[at].astype(F32) + (
                nn(ctx_ref[at], out_w_ref[0]) + vec_ref[OUT_BIAS : OUT_BIAS + 1]
            )
            unit, scale = norm_stats(inner)
            first = unit * vec_ref[ATTN_GAIN : ATTN_GAIN + 1] + vec_ref[ATTN_SHIFT : ATTN_SHIFT + 1]
            unit1_ref[at] = unit.astype(BF)
            scale1_ref[at] = scale
            low_ref[at] = first.astype(BF)
            acc_ref[at] = first + vec_ref[DOWN_BIAS : DOWN_BIAS + 1]

    down = down_ref[...].reshape(up_ref.shape[1:])
    for m in range(rows // sub):
        at = slice(m * sub, (m + 1) * sub)
        hidden = nn(low_ref[at], up_ref[0]) + up_b_ref[...]
        act, slope = gelu_parts(hidden)
        act = act.astype(BF)
        act_ref[at] = act
        slope_ref[at] = slope.astype(BF)
        acc_ref[at] += nn(act, down)

    @pl.when(step == pl.num_programs(0) - 1)
    def _():
        for seq in range(rows // length):
            at = slice(seq * length, (seq + 1) * length)
            active = (exit_ref[seq] >= LAYER).astype(F32)
            unit, scale = norm_stats(acc_ref[at])
            unit2_ref[at] = unit.astype(BF)
            scale2_ref[at] = scale
            result = (
                unit * vec_ref[BLOCK_GAIN : BLOCK_GAIN + 1] + vec_ref[BLOCK_SHIFT : BLOCK_SHIFT + 1]
            ) * active
            output_ref[at] = result.astype(BF)


def feed(exit_layer, tokens, ctx, out_w, vec, up, up_bias, down, down_block, length):
    rows, width = tokens.shape
    steps = up.shape[0]
    hidden = steps * width
    whole = full((rows, width))
    return pl.pallas_call(
        functools.partial(feed_kernel, length),
        grid=(steps,),
        in_specs=[
            pl.BlockSpec(memory_space=pltpu.SMEM),
            whole,
            whole,
            pl.BlockSpec((1, width, width), lambda i: (3, 0, 0)),
            full(vec.shape),
            pl.BlockSpec((1, width, width), lambda i: (i, 0, 0)),
            pl.BlockSpec((1, width), lambda i: (0, i)),
            pl.BlockSpec(down_block, lambda i: (i, 0, 0)),
        ],
        out_specs=[
            whole,
            pl.BlockSpec((rows, width), lambda i: (0, i)),
            pl.BlockSpec((rows, width), lambda i: (0, i)),
            whole,
            full((rows, 1)),
            whole,
            full((rows, 1)),
            whole,
        ],
        out_shape=[
            jax.ShapeDtypeStruct((rows, width), BF),
            jax.ShapeDtypeStruct((rows, hidden), BF),
            jax.ShapeDtypeStruct((rows, hidden), BF),
            jax.ShapeDtypeStruct((rows, width), BF),
            jax.ShapeDtypeStruct((rows, 1), F32),
            jax.ShapeDtypeStruct((rows, width), BF),
            jax.ShapeDtypeStruct((rows, 1), F32),
            jax.ShapeDtypeStruct((rows, width), BF),
        ],
        scratch_shapes=[pltpu.VMEM((rows, width), F32)],
        compiler_params=params(),
        cost_estimate=cost(18 * rows * width * width, 40 * rows * width, 8 * rows * width),
        name="feed",
    )(exit_layer, tokens, ctx, out_w, vec, up, up_bias, down)


def leave_kernel(
    length,
    classes,
    exit_ref,
    output_ref,
    unit2_ref,
    scale2_ref,
    grad_ref,
    pool_ref,
    vec_ref,
    class_bias_ref,
    logit_grad_ref,
    act_ref,
    outer_ref,
    branch_ref,
    joint_grad_ref,
    sums_ref,
    class_grad_ref,
    logits_ref,
    stats_ref,
    lead_ref,
    pool_grad_ref,
):
    step = pl.program_id(0)
    rows, width = output_ref.shape
    pool = pool_ref[...].reshape(width, width)
    count = rows // length

    @pl.when(step == 0)
    def _():
        place = lax.broadcasted_iota(jnp.int32, (count, 1), 0)
        active = jnp.zeros((count, 1), F32)
        for seq in range(count):
            on = (exit_ref[seq] >= LAYER).astype(F32)
            active = jnp.where(place == seq, on, active)
        leading = jnp.concatenate(
            [output_ref[seq * length : seq * length + 1].astype(F32) for seq in range(count)],
            axis=0,
        ).astype(BF)
        pooled = jnp.tanh(nn(leading, pool) + vec_ref[POOL_BIAS : POOL_BIAS + 1])
        pooled_low = pooled.astype(BF)
        used = lax.broadcasted_iota(jnp.int32, (8, width), 0) < classes
        class_rows = jnp.where(used, vec_ref[CLASS_ROWS : CLASS_ROWS + 8], 0.0).astype(BF)
        raw = nt(pooled_low, class_rows) + class_bias_ref[...]
        lane = lax.broadcasted_iota(jnp.int32, raw.shape, 1) < classes
        top = jnp.max(jnp.where(lane, raw, -jnp.inf), axis=-1, keepdims=True)
        spread = jnp.where(lane, jnp.exp(raw - top), 0.0)
        logprob = raw - top - jnp.log(jnp.sum(spread, axis=-1, keepdims=True))
        entropy = -jnp.sum(
            jnp.where(lane, jnp.exp(logprob) * logprob, 0.0), axis=-1, keepdims=True
        )
        logits_ref[...] = raw * active
        class_grad = (logit_grad_ref[...].astype(F32) * active).astype(BF)
        stats_ref[0:1] = jnp.broadcast_to(jnp.sum(entropy * active, axis=0, keepdims=True), (1, 8))
        stats_ref[1:2] = jnp.sum(class_grad.astype(F32), axis=0, keepdims=True)
        class_grad_ref[...] = tn(class_grad, pooled_low)
        pooled_grad = nn(class_grad, class_rows)
        pre_grad = (pooled_grad * (1.0 - pooled * pooled)).astype(BF)
        sums_ref[3:4] = jnp.sum(pre_grad.astype(F32), axis=0, keepdims=True)
        pool_grad_ref[...] = tn(leading, pre_grad).reshape(pool_grad_ref.shape).astype(BF)
        lead_ref[...] = nt(pre_grad, pool)
        head = lax.broadcasted_iota(jnp.int32, (length, 1), 0) == 0
        gain = vec_ref[BLOCK_GAIN : BLOCK_GAIN + 1]
        gain_sum = jnp.zeros((1, width), F32)
        shift_sum = jnp.zeros((1, width), F32)
        bias_sum = jnp.zeros((1, width), F32)
        for seq in range(count):
            at = slice(seq * length, (seq + 1) * length)
            on = (exit_ref[seq] >= LAYER).astype(F32)
            top_grad = (
                grad_ref[at].astype(F32) + jnp.where(head, lead_ref[seq : seq + 1], 0.0)
            ) * on
            unit = unit2_ref[at].astype(F32)
            outer = norm_back(top_grad, unit, scale2_ref[at], gain)
            branch = outer.astype(BF)
            outer_ref[at] = outer
            branch_ref[at] = branch
            gain_sum += jnp.sum(top_grad * unit, axis=0, keepdims=True)
            shift_sum += jnp.sum(top_grad, axis=0, keepdims=True)
            bias_sum += jnp.sum(branch.astype(F32), axis=0, keepdims=True)
        sums_ref[0:1] = gain_sum
        sums_ref[1:2] = shift_sum
        sums_ref[2:3] = bias_sum

    @pl.when(step > 0)
    def _():
        few, both, _ = joint_grad_ref.shape
        deep = width // few
        value = tn(act_ref[...], branch_ref[...])
        for at in range(few):
            joint_grad_ref[at, 0:deep] = value[at * deep : (at + 1) * deep].astype(BF)
            joint_grad_ref[at, deep:both] = pool_grad_ref[(step - 1) * few + at]


def leave(
    exit_layer, output, unit2, scale2, output_grad, pool, vec, class_bias, logit_grad, act,
    pool_spec, shards, length, classes,
):
    rows, width = output.shape
    count = rows // length
    hidden = act.shape[1]
    steps = hidden // width
    few = shards // steps
    both = (hidden + width) // shards
    whole = full((rows, width))
    return pl.pallas_call(
        functools.partial(leave_kernel, length, classes),
        grid=(steps + 1,),
        in_specs=[
            pl.BlockSpec(memory_space=pltpu.SMEM),
            whole,
            whole,
            full((rows, 1)),
            whole,
            pool_spec,
            full(vec.shape),
            full(class_bias.shape),
            full(logit_grad.shape),
            pl.BlockSpec((rows, width), lambda i: (0, jnp.maximum(i - 1, 0))),
        ],
        out_specs=[
            whole,
            whole,
            pl.BlockSpec((few, both, width), lambda i: (jnp.maximum(i - 1, 0), 0, 0)),
            full((4, width)),
            full((8, width)),
            full((count, 8)),
            full((2, 8)),
        ],
        out_shape=[
            jax.ShapeDtypeStruct((rows, width), F32),
            jax.ShapeDtypeStruct((rows, width), BF),
            jax.ShapeDtypeStruct((shards, both, width), BF),
            jax.ShapeDtypeStruct((4, width), F32),
            jax.ShapeDtypeStruct((8, width), F32),
            jax.ShapeDtypeStruct((count, 8), F32),
            jax.ShapeDtypeStruct((2, 8), F32),
        ],
        scratch_shapes=[
            pltpu.VMEM((count, width), F32),
            pltpu.VMEM((shards, width // shards, width), BF),
        ],
        compiler_params=params(),
        cost_estimate=cost(8 * rows * width * width, 30 * rows * width),
        name="leave",
    )(exit_layer, output, unit2, scale2, output_grad, pool, vec, class_bias, logit_grad, act)


def feed_back_kernel(
    branch_ref,
    slope_ref,
    low_ref,
    down_ref,
    up_ref,
    outer_ref,
    unit1_ref,
    scale1_ref,
    out_w_ref,
    vec_ref,
    up_grad_ref,
    up_sum_ref,
    inner_ref,
    attended_ref,
    ctx_grad_ref,
    sums_ref,
    acc_ref,
    hid_ref,
):
    step = pl.program_id(0)
    rows, width = branch_ref.shape
    sub = 256

    @pl.when(step == 0)
    def _():
        acc_ref[...] = outer_ref[...]

    total = jnp.zeros((1, width), F32)
    down = down_ref[...].reshape(up_ref.shape[1:])
    for m in range(rows // sub):
        at = slice(m * sub, (m + 1) * sub)
        hid = (nt(branch_ref[at], down) * slope_ref[at].astype(F32)).astype(BF)
        hid_ref[at] = hid
        total += jnp.sum(hid.astype(F32), axis=0, keepdims=True)
        acc_ref[at] += nt(hid, up_ref[0])
    up_sum_ref[...] = total
    up_grad_ref[...] = tn(low_ref[...], hid_ref[...]).astype(BF)

    @pl.when(step == pl.num_programs(0) - 1)
    def _():
        gain = vec_ref[ATTN_GAIN : ATTN_GAIN + 1]
        gain_sum = jnp.zeros((1, width), F32)
        shift_sum = jnp.zeros((1, width), F32)
        bias_sum = jnp.zeros((1, width), F32)
        for m in range(rows // sub):
            at = slice(m * sub, (m + 1) * sub)
            grad = acc_ref[at]
            unit = unit1_ref[at].astype(F32)
            inner = norm_back(grad, unit, scale1_ref[at], gain)
            attended = inner.astype(BF)
            inner_ref[at] = inner
            attended_ref[at] = attended
            ctx_grad_ref[at] = nt(attended, out_w_ref[0]).astype(BF)
            gain_sum += jnp.sum(grad * unit, axis=0, keepdims=True)
            shift_sum += jnp.sum(grad, axis=0, keepdims=True)
            bias_sum += jnp.sum(attended.astype(F32), axis=0, keepdims=True)
        sums_ref[0:1] = gain_sum
        sums_ref[1:2] = shift_sum
        sums_ref[2:3] = bias_sum


def feed_back(branch, slope, low, down, down_block, up, outer, unit1, scale1, out_w, vec):
    rows, width = branch.shape
    hidden = slope.shape[1]
    steps = hidden // width
    whole = full((rows, width))
    return pl.pallas_call(
        feed_back_kernel,
        grid=(steps,),
        in_specs=[
            whole,
            pl.BlockSpec((rows, width), lambda i: (0, i)),
            whole,
            pl.BlockSpec(down_block, lambda i: (i, 0, 0)),
            pl.BlockSpec((1, width, width), lambda i: (i, 0, 0)),
            whole,
            whole,
            full((rows, 1)),
            pl.BlockSpec((1, width, width), lambda i: (3, 0, 0)),
            full(vec.shape),
        ],
        out_specs=[
            pl.BlockSpec((width, width), lambda i: (0, i)),
            pl.BlockSpec((1, width), lambda i: (0, i)),
            whole,
            whole,
            whole,
            full((3, width)),
        ],
        out_shape=[
            jax.ShapeDtypeStruct((width, hidden), BF),
            jax.ShapeDtypeStruct((1, hidden), F32),
            jax.ShapeDtypeStruct((rows, width), F32),
            jax.ShapeDtypeStruct((rows, width), BF),
            jax.ShapeDtypeStruct((rows, width), BF),
            jax.ShapeDtypeStruct((3, width), F32),
        ],
        scratch_shapes=[pltpu.VMEM((rows, width), F32), pltpu.VMEM((rows, width), BF)],
        compiler_params=params(),
        cost_estimate=cost(26 * rows * width * width, 40 * rows * width),
        name="feed_back",
    )(branch, slope, low, down, up, outer, unit1, scale1, out_w, vec)


def attend_back_kernel(length, joined_ref, probs_ref, ctx_grad_ref, grad_ref, sum_ref):
    rows, width = ctx_grad_ref.shape
    pairs = width // PAIR

    def one(seq, carry):
        at = pl.ds(pl.multiple_of(seq * length, length), length)
        for pair in range(pairs):
            at_q = slice(pair * PAIR, (pair + 1) * PAIR)
            at_k = slice(width + pair * PAIR, width + (pair + 1) * PAIR)
            at_v = slice(2 * width + pair * PAIR, 2 * width + (pair + 1) * PAIR)
            query = joined_ref[at, at_q] * jnp.asarray(0.125, BF)
            queries = split_heads(query)
            keys = split_heads(joined_ref[at, at_k])
            vals = split_heads(joined_ref[at, at_v])
            ctx_grad = ctx_grad_ref[at, at_q]
            ctx_grads = split_heads(ctx_grad)
            probs = probs_ref[seq, pair]
            prob_grad = nt(vals, ctx_grad)
            halves = []
            for head in range(2):
                cut = slice(head * length, (head + 1) * length)
                held = probs[cut].astype(F32)
                part = prob_grad[cut]
                base = jnp.sum(part * held, axis=0, keepdims=True)
                halves.append((held * (part - base)).astype(BF))
            stacked = jnp.concatenate(halves, axis=0)
            beside = jnp.concatenate(halves, axis=1)
            probs_beside = jnp.concatenate([probs[:length], probs[length:]], axis=1)
            grad_ref[at, at_q] = (tn(stacked, keys) * 0.125).astype(BF)
            grad_ref[at, at_k] = nn(beside, queries).astype(BF)
            grad_ref[at, at_v] = nn(probs_beside, ctx_grads).astype(BF)
        return carry

    lax.fori_loop(0, rows // length, one, 0)
    total = jnp.zeros(sum_ref.shape, F32)
    for m in range(rows // length):
        total += jnp.sum(
            grad_ref[m * length : (m + 1) * length].astype(F32), axis=0, keepdims=True
        )

    @pl.when(pl.program_id(0) == 0)
    def _():
        sum_ref[...] = total

    @pl.when(pl.program_id(0) > 0)
    def _():
        sum_ref[...] += total


def attend_back(joined, probs, ctx_grad, length):
    rows, width = ctx_grad.shape
    count = rows // length
    steps = 2
    block = rows // steps
    pairs = width // PAIR
    return pl.pallas_call(
        functools.partial(attend_back_kernel, length),
        grid=(steps,),
        in_specs=[
            pl.BlockSpec((block, 3 * width), lambda i: (i, 0)),
            pl.BlockSpec((count // steps, pairs, 2 * length, length), lambda i: (i, 0, 0, 0)),
            pl.BlockSpec((block, width), lambda i: (i, 0)),
        ],
        out_specs=[
            pl.BlockSpec((block, 3 * width), lambda i: (i, 0)),
            full((1, 3 * width)),
        ],
        out_shape=[
            jax.ShapeDtypeStruct((rows, 3 * width), BF),
            jax.ShapeDtypeStruct((1, 3 * width), F32),
        ],
        compiler_params=params(),
        cost_estimate=cost(8 * rows * width * width, 20 * rows * width),
        name="attend_back",
    )(joined, probs, ctx_grad)


def weight_grads_kernel(
    place_ref, tok_ref, ctx_ref, joined_ref, attended_ref, row_ref, keep_ref, send_ref, value_ref
):
    last = pl.num_programs(0) - 1
    chips, depth, width = keep_ref.shape[1:]
    part = tok_ref.shape[1] // (2 * chips)
    first = place_ref[2] == 0

    @pl.when(pl.program_id(0) < last)
    def _():
        value_ref[...] = tn(tok_ref[...], joined_ref[...])

    @pl.when(pl.program_id(0) == last)
    def _():
        value_ref[...] = tn(ctx_ref[...], attended_ref[...])

    for chip in range(chips):
        even = value_ref[2 * chip * part : (2 * chip + 1) * part]
        odd = value_ref[(2 * chip + 1) * part : (2 * chip + 2) * part]
        keep_ref[0, chip, 0:part] = jnp.where(first, even, odd).astype(BF)
        send_ref[0, chip, 0:part] = jnp.where(first, odd, even).astype(BF)
        if depth > part:
            top = lax.broadcasted_iota(jnp.int32, (depth - part, width), 0) == 0
            even = row_ref[0, 2 * chip : 2 * chip + 1]
            odd = row_ref[0, 2 * chip + 1 : 2 * chip + 2]
            keep_ref[0, chip, part:depth] = jnp.where(
                top, jnp.where(first, even, odd), 0.0
            ).astype(BF)
            send_ref[0, chip, part:depth] = jnp.where(
                top, jnp.where(first, odd, even), 0.0
            ).astype(BF)


def weight_grads(place, tokens, ctx, joined_grad, attended, small, chips, extra):
    rows, width = tokens.shape
    depth = width // (2 * chips) + extra
    whole = full((rows, width))
    spec = pl.BlockSpec((1, chips, depth, width), lambda i: (i, 0, 0, 0))
    shape = jax.ShapeDtypeStruct((4, chips, depth, width), BF)
    return pl.pallas_call(
        weight_grads_kernel,
        grid=(4,),
        in_specs=[
            pl.BlockSpec(memory_space=pltpu.SMEM),
            whole,
            whole,
            pl.BlockSpec((rows, width), lambda i: (0, jnp.minimum(i, 2))),
            whole,
            pl.BlockSpec((1, 2 * chips, width), lambda i: (i, 0, 0)),
        ],
        out_specs=[spec, spec],
        out_shape=[shape, shape],
        scratch_shapes=[pltpu.VMEM((width, width), F32)],
        compiler_params=params(),
        cost_estimate=cost(8 * rows * width * width, 20 * rows * width),
        name="weight_grads",
    )(place, tokens, ctx, joined_grad, attended, small)


def input_kernel(inner_ref, joined_ref, w_ref, out_ref):
    width = inner_ref.shape[1]
    total = inner_ref[...]
    for part in range(3):
        total += nt(joined_ref[:, part * width : (part + 1) * width], w_ref[part])
    out_ref[...] = total.astype(BF)


def input_back(inner, joined_grad, qkv):
    rows, width = inner.shape
    steps = 4
    block = rows // steps
    return pl.pallas_call(
        input_kernel,
        grid=(steps,),
        in_specs=[
            pl.BlockSpec((block, width), lambda i: (i, 0)),
            pl.BlockSpec((block, 3 * width), lambda i: (i, 0)),
            full((3, width, width)),
        ],
        out_specs=pl.BlockSpec((block, width), lambda i: (i, 0)),
        out_shape=jax.ShapeDtypeStruct((rows, width), BF),
        compiler_params=params(),
        cost_estimate=cost(6 * rows * width * width, 12 * rows * width),
        name="input_back",
    )(inner, joined_grad, qkv)


def lay_kernel(chips, reps, place_ref, own_ref, twin_ref, *refs):
    far = chips - 1
    along = refs[:far]
    across = refs[far : far + reps - 1]
    swapped = refs[far + reps - 1 : far + 2 * reps - 1]
    extra = refs[far + 2 * reps - 1] if len(refs) > far + 2 * reps + 1 else None
    if extra is None:
        out_ref, sems = refs[-2], refs[-1]
    else:
        out_ref, more_ref, sems = refs[-3], refs[-2], refs[-1]
    rep, chip, core = place_ref[0], place_ref[1], place_ref[2]
    width = out_ref.shape[2]
    part = out_ref.shape[1] // (2 * chips)
    copies = []

    def start(source, target):
        copies.append(pltpu.make_async_copy(source, target, sems.at[len(copies)]))
        copies[-1].start()

    def put(source, block, at_chip, at_core):
        row = pl.multiple_of((at_chip * 2 + at_core) * part, part)
        start(source, out_ref.at[block, pl.ds(row, part)])

    own_rows = pl.ds(0, part)
    for block in range(reps):
        cols = pl.ds(block * width, width)
        put(own_ref.at[own_rows, cols], block, chip, core)
        put(twin_ref.at[own_rows, cols], block, chip, 1 - core)
    for step in range(1, chips):
        source = lax.rem(chip + chips - step, chips)
        rows = pl.ds((step - 1) * part, part)
        put(along[step - 1].at[own_rows], rep, source, core)
        put(swapped[0].at[rows], rep, source, 1 - core)
        for other in range(1, reps):
            put(across[other - 1].at[rows], rep ^ other, source, core)
            put(swapped[other].at[rows], rep ^ other, source, 1 - core)
    if extra is not None:
        tail = pl.ds(part, 16)
        cols = pl.ds(0, width)
        start(own_ref.at[tail, cols], more_ref.at[chip * 2 + core])
        start(twin_ref.at[tail, cols], more_ref.at[chip * 2 + 1 - core])
        for step in range(1, chips):
            source = lax.rem(chip + chips - step, chips)
            start(along[step - 1].at[tail], more_ref.at[source * 2 + core])
            start(extra.at[pl.ds((step - 1) * 16, 16)], more_ref.at[source * 2 + 1 - core])
    for copy in copies:
        copy.wait()


def lay(place, own, twin, along, across, swapped, extra, part, chips, reps):
    width = along[0].shape[1]
    anywhere = pl.BlockSpec(memory_space=pl.ANY)
    inputs = [own, twin, *along, *across, *swapped]
    shapes = [jax.ShapeDtypeStruct((reps, chips * 2 * part, width), own.dtype)]
    if extra is not None:
        inputs.append(extra)
        shapes.append(jax.ShapeDtypeStruct((2 * chips, 16, width), own.dtype))
    return pl.pallas_call(
        functools.partial(lay_kernel, chips, reps),
        in_specs=[pl.BlockSpec(memory_space=pltpu.SMEM)] + [anywhere] * len(inputs),
        out_specs=[pl.BlockSpec(memory_space=pltpu.VMEM)] * len(shapes),
        out_shape=shapes,
        scratch_shapes=[pltpu.SemaphoreType.DMA((2 * chips * (reps + 1),))],
        compiler_params=pltpu.CompilerParams(vmem_limit_bytes=VMEM_BYTES),
        cost_estimate=cost(0, 4 * reps * chips * 2 * part * width),
        name="lay",
    )(place, *inputs)


def pack_vectors(rows, up_bias, class_weight):
    first = jnp.concatenate(rows[:8] + [class_weight.T.reshape(-1)] + rows[8:])
    return jnp.concatenate([first, up_bias])[None]


def move(values, reps, chips, target):
    pairs = []
    for rep in range(reps):
        for chip in range(chips):
            for core in range(2):
                to_rep, to_chip, to_core = target(rep, chip, core)
                pairs.append(
                    (
                        (rep * chips + chip) * 2 + core,
                        (to_rep * chips + to_chip) * 2 + to_core,
                    )
                )
    return lax.ppermute(values, ("rep", "fsdp"), pairs)


def along_chips(step, chips):
    return lambda rep, chip, core: (rep, (chip + step) % chips, core)


def across_reps(other):
    return lambda rep, chip, core: (rep ^ other, chip, core)


def to_twin(rep, chip, core):
    return rep, chip, 1 - core


def gather_blocks(place, own, part, reps, chips, after):
    width = own.shape[1] // reps
    mine = lax.dynamic_slice_in_dim(own, place[0] * width, width, axis=1)
    if after is not None:
        mine, _ = lax.optimization_barrier((mine, after))
    along = [move(mine, reps, chips, along_chips(step, chips)) for step in range(1, chips)]
    twin = move(own, reps, chips, to_twin)
    stacked = jnp.concatenate([rows[:part] for rows in along], axis=0)
    across = [move(stacked, reps, chips, across_reps(other)) for other in range(1, reps)]
    swapped = [move(rows, reps, chips, to_twin) for rows in [stacked] + across]
    extra = None
    if own.shape[0] > part:
        extra = move(
            jnp.concatenate([rows[part:] for rows in along], axis=0), reps, chips, to_twin
        )
    return lay(place, own, twin, along, across, swapped, extra, part, chips, reps), along


def pick(parts, at):
    return lax.dynamic_index_in_dim(parts, at, axis=0, keepdims=False)


def in_order(rep, reps, own, others, axis):
    blocks = jnp.stack([own] + others)
    return jnp.concatenate([pick(blocks, rep ^ at) for at in range(reps)], axis=axis)


def sum_blocks(place, keep, send, reps, chips):
    rep, chip = place[0], place[1]
    got = move(send, reps, chips, to_twin)

    def both(at):
        return pick(keep, at).astype(F32) + pick(got, at).astype(F32)

    arrived = [
        move(both(rep ^ other).astype(BF), reps, chips, across_reps(other))
        for other in range(1, reps)
    ]

    def over_reps(at):
        total = pick(pick(keep, rep), at).astype(F32) + pick(pick(got, rep), at).astype(F32)
        for block in arrived:
            total = total + pick(block, at).astype(F32)
        return total

    total = over_reps(chip)
    for step in range(1, chips):
        there = over_reps(lax.rem(chip + step, chips)).astype(BF)
        total = total + move(there, reps, chips, along_chips(step, chips)).astype(F32)
    total = total.astype(BF)
    others = [move(total, reps, chips, across_reps(other)) for other in range(1, reps)]
    return in_order(rep, reps, total, others, 1)


def sum_over_reps(place, rows, reps, chips):
    rep = place[0]
    parts = rows.reshape(reps, -1, rows.shape[1])
    total = pick(parts, rep).astype(F32)
    for other in range(1, reps):
        there = pick(parts, rep ^ other)
        total = total + move(there, reps, chips, across_reps(other)).astype(F32)
    total = total.astype(BF)
    others = [move(total, reps, chips, across_reps(other)) for other in range(1, reps)]
    return in_order(rep, reps, total, others, 0)


def per_device(
    tokens,
    exit_layer,
    qkv_weight,
    query_bias,
    value_bias,
    out_weight,
    out_bias,
    attn_gain,
    attn_shift,
    up_weight,
    up_bias,
    down_weight,
    down_bias,
    block_gain,
    block_shift,
    pool_weight,
    pool_bias,
    class_weight,
    class_bias,
    output_grad,
    logit_grad,
):
    reps = lax.axis_size("rep")
    shards = lax.axis_size("fsdp")
    mine = lax.axis_index("fsdp")
    rows, width = tokens.shape
    count = exit_layer.shape[0]
    length = rows // count
    classes = class_weight.shape[1]
    part = out_weight.shape[0]
    hidden = up_weight.shape[1]

    def gather(shard):
        return lax.all_gather(shard, "fsdp", axis=0, tiled=True)

    packed = pack_vectors(
        [
            query_bias,
            value_bias,
            out_bias,
            attn_gain,
            attn_shift,
            down_bias,
            block_gain,
            block_shift,
            pool_bias,
        ],
        up_bias,
        class_weight,
    )
    joint_own = jnp.concatenate([qkv_weight, out_weight], axis=1)
    low_own = jnp.concatenate([down_weight, pool_weight], axis=0)
    deep = down_weight.shape[0]
    low_all = gather(low_own).reshape(shards, deep + part, width)
    chips = shards // 2
    place = jnp.stack([lax.axis_index("rep"), mine // 2, mine % 2]).astype(jnp.int32)
    direct = (
        part % 16 == 0
        and reps & (reps - 1) == 0
        and reps * width == hidden
        and packed.shape[1] % width == 0
        and packed.shape[1] <= 16 * width
    )
    if direct:
        lines = packed.shape[1] // width
        held = jnp.pad(packed.reshape(lines, width), ((0, 16 - lines), (0, 0)))
        own = jnp.concatenate([joint_own, jnp.tile(held, (1, reps))], axis=0)
        (joint, small), sent = gather_blocks(place, own, part, reps, chips, None)
        small = small[:, :lines].reshape(shards, -1)
        (up,), _ = gather_blocks(place, up_weight, part, reps, chips, sent)
        down = low_all
        down_block = (width // deep, deep, width)
        pool = low_all
        pool_spec = pl.BlockSpec((shards, part, width), lambda i: (0, deep // part, 0))
    else:
        small = gather(packed)
        joint = jnp.stack(jnp.split(gather(joint_own), 4, axis=1))
        up = jnp.stack(jnp.split(gather(up_weight), hidden // width, axis=1))
        down = low_all[:, :deep].reshape(-1, width, width)
        down_block = (1, width, width)
        pool = low_all[:, deep:].reshape(width, width)
        pool_spec = full((width, width))
    vec = (
        small[:, : VECTOR_ROWS * part]
        .reshape(shards, VECTOR_ROWS, part)
        .transpose(1, 0, 2)
        .reshape(VECTOR_ROWS, width)
        .astype(F32)
    )
    vec = jnp.pad(vec, ((0, 16 - VECTOR_ROWS), (0, 0)))
    up_row = small[:, VECTOR_ROWS * part :].reshape(1, hidden).astype(F32)
    bias_row = jnp.concatenate([vec[:1], jnp.zeros((1, width), F32), vec[1:2]], axis=1)

    joined, probs, ctx = attend(tokens, joint, bias_row, length)
    low, act, slope, unit1, scale1, unit2, scale2, output = feed(
        exit_layer, tokens, ctx, joint, vec, up, up_row, down, down_block, length
    )
    class_bias_row = jnp.pad(class_bias.astype(F32), (0, 8 - classes))[None]
    logit_grad_rows = jnp.pad(logit_grad, ((0, 0), (0, 8 - classes)))
    outer, branch, low_grad, exit_sums, class_grad, logits, stats = leave(
        exit_layer,
        output,
        unit2,
        scale2,
        output_grad,
        pool,
        vec,
        class_bias_row,
        logit_grad_rows,
        act,
        pool_spec,
        shards,
        length,
        classes,
    )
    up_grad, up_sum, inner, attended, ctx_grad, feed_sums = feed_back(
        branch, slope, low, down, down_block, up, outer, unit1, scale1, joint, vec
    )
    joined_grad, joined_sum = attend_back(joined, probs, ctx_grad, length)
    sums = jnp.concatenate(
        [
            joined_sum.reshape(3, width)[::2],
            feed_sums,
            exit_sums,
            class_grad[:classes],
        ],
        axis=0,
    )
    lines = sums.shape[0]
    own_sums = sums.reshape(lines, shards, part).transpose(1, 0, 2).reshape(shards, lines * part)
    own_sums = jnp.concatenate([own_sums, up_sum.reshape(shards, deep)], axis=1)
    used = own_sums.shape[1]
    seqs_total = count * reps * shards
    figures = jnp.concatenate([stats[0, :1], stats[1, :classes]])
    slots = reps * shards * figures.shape[0] * 3
    direct = direct and used + slots <= 4 * width
    if direct:
        high = figures.astype(BF).astype(F32)
        middle = (figures - high).astype(BF).astype(F32)
        lowest = figures - high - middle
        split = jnp.concatenate([high, middle, lowest])
        slot = lax.axis_index("rep") * shards + mine
        lone = jnp.where(
            jnp.arange(reps * shards)[:, None] == slot, split[None], 0.0
        ).reshape(1, slots)
        row = jnp.concatenate([own_sums, jnp.broadcast_to(lone, (shards, slots))], axis=1)
        row = jnp.pad(row, ((0, 0), (0, 4 * width - row.shape[1])))
        row = row.reshape(shards, 4, width).transpose(1, 0, 2)
    else:
        row = jnp.zeros((4, shards, width), F32)
    keep, send = weight_grads(
        place, tokens, ctx, joined_grad, attended, row, chips, 16 if direct else 0
    )
    input_grad = input_back(inner, joined_grad, joint)

    def scatter(grad):
        return lax.psum_scatter(grad, "fsdp", scatter_dimension=0, tiled=True)

    low_part = scatter(low_grad.reshape(shards * (deep + part), width))
    up_grad, low_part = lax.optimization_barrier((up_grad, low_part))
    up_part = scatter(up_grad)
    if direct:
        joint_sum = sum_blocks(place, keep, send, reps, chips).astype(F32)
        low_sum = sum_over_reps(place, low_part, reps, chips).astype(F32)
        up_sum = sum_over_reps(place, up_part, reps, chips).astype(F32)
        small_sum = joint_sum[part]
        joint_sum = joint_sum[:part]
        total = small_sum[used : used + slots].reshape(-1, figures.shape[0]).sum(axis=0)
    else:
        first = mine % 2 == 0
        pair = jnp.stack([jnp.where(first, keep, send), jnp.where(first, send, keep)], axis=2)
        joint_grad = pair.reshape(4, width, width).transpose(1, 0, 2).reshape(width, 4 * width)
        joint_sum, low_sum, up_sum = lax.psum((scatter(joint_grad), low_part, up_part), "rep")
        joint_sum, low_sum, up_sum = (
            joint_sum.astype(F32),
            low_sum.astype(F32),
            up_sum.astype(F32),
        )
        own_sums, total = lax.psum((own_sums, figures), ("rep", "fsdp"))
        small_sum = pick(own_sums, mine)
    own = small_sum[: lines * part].reshape(lines, part)
    return (
        output,
        logits[:, :classes],
        total[0] / seqs_total,
        input_grad,
        joint_sum[:, : 3 * width],
        own[0],
        own[1],
        joint_sum[:, 3 * width :],
        own[4],
        own[2],
        own[3],
        up_sum,
        small_sum[lines * part : used],
        low_sum[:deep],
        own[7],
        own[5],
        own[6],
        low_sum[deep:],
        own[8],
        own[9 : 9 + classes].T,
        total[1:],
    )


def solution(mesh):
    return jax.shard_map(
        per_device,
        mesh=mesh,
        in_specs=(
            P(("rep", "fsdp"), None),
            P(("rep", "fsdp")),
            P("fsdp", None),
            P("fsdp"),
            P("fsdp"),
            P("fsdp", None),
            P("fsdp"),
            P("fsdp"),
            P("fsdp"),
            P("fsdp", None),
            P("fsdp"),
            P("fsdp", None),
            P("fsdp"),
            P("fsdp"),
            P("fsdp"),
            P("fsdp", None),
            P("fsdp"),
            P("fsdp", None),
            P(),
            P(("rep", "fsdp"), None),
            P(("rep", "fsdp"), None),
        ),
        out_specs=(
            P(("rep", "fsdp"), None),
            P(("rep", "fsdp"), None),
            P(),
            P(("rep", "fsdp"), None),
            P("fsdp", None),
            P("fsdp"),
            P("fsdp"),
            P("fsdp", None),
            P("fsdp"),
            P("fsdp"),
            P("fsdp"),
            P("fsdp", None),
            P("fsdp"),
            P("fsdp", None),
            P("fsdp"),
            P("fsdp"),
            P("fsdp"),
            P("fsdp", None),
            P("fsdp"),
            P("fsdp", None),
            P(),
        ),
        check_vma=False,
    )
```

```python
import functools
import math

import jax
import jax.numpy as jnp
from jax import lax
from jax.experimental import pallas as pl
from jax.experimental.pallas import tpu as pltpu
from jax.sharding import PartitionSpec as P

HD = 64
LAYER = 6
PAIR = 2 * HD
VMEM_BYTES = 58 * 2**20
BF = jnp.bfloat16
F32 = jnp.float32

QUERY_BIAS, VALUE_BIAS, OUT_BIAS, ATTN_GAIN, ATTN_SHIFT = 0, 1, 2, 3, 4
DOWN_BIAS, BLOCK_GAIN, BLOCK_SHIFT, CLASS_ROWS, POOL_BIAS = 5, 6, 7, 8, 11
VECTOR_ROWS = 12


def nn(left, right):
    return jnp.dot(left, right, preferred_element_type=F32)


def tn(left, right):
    return lax.dot_general(left, right, (((0,), (0,)), ((), ())), preferred_element_type=F32)


def nt(left, right):
    return lax.dot_general(left, right, (((1,), (1,)), ((), ())), preferred_element_type=F32)


def full(shape):
    return pl.BlockSpec(shape, lambda *at: (0,) * len(shape))


def params():
    return pltpu.CompilerParams(
        dimension_semantics=("arbitrary",), vmem_limit_bytes=VMEM_BYTES
    )


def cost(flops, moved, trans=0):
    return pl.CostEstimate(flops=flops, bytes_accessed=moved, transcendentals=trans)


def split_heads(pair):
    lane = lax.broadcasted_iota(jnp.int32, pair.shape, 1)
    zero = jnp.zeros_like(pair)
    return jnp.concatenate(
        [jnp.where(lane < HD, pair, zero), jnp.where(lane < HD, zero, pair)], axis=0
    )


def norm_stats(values):
    center = values - jnp.mean(values, axis=-1, keepdims=True)
    spread = jnp.mean(center * center, axis=-1, keepdims=True)
    scale = lax.rsqrt(spread + 1e-06)
    return center * scale, scale


def norm_back(grad, unit, scale, gain):
    inner = grad * gain
    first = jnp.mean(inner, axis=-1, keepdims=True)
    second = jnp.mean(inner * unit, axis=-1, keepdims=True)
    return scale * (inner - first - unit * second)


def gelu_parts(values):
    size = jnp.abs(values)
    t = 1.0 / (1.0 + 0.23164189 * size)
    bell = jnp.exp(-0.5 * values * values)
    poly = t * (
        0.127414796
        + t * (-0.142248368 + t * (0.7107068705 + t * (-0.7265760135 + t * 0.5307027145)))
    )
    tail = poly * bell
    below = jnp.where(values >= 0.0, 1.0 - tail, tail)
    return values * below, below + values * (bell * 0.3989422804014327)


def attend_kernel(length, tok_ref, w_ref, bias_ref, joined_ref, probs_ref, ctx_ref):
    rows, width = ctx_ref.shape
    pairs = width // PAIR
    for part in range(3):
        cols = slice(part * width, (part + 1) * width)
        joined_ref[:, cols] = (nn(tok_ref[...], w_ref[part]) + bias_ref[:, cols]).astype(BF)

    def one(seq, carry):
        at = pl.ds(pl.multiple_of(seq * length, length), length)
        for pair in range(pairs):
            cols = slice(pair * PAIR, (pair + 1) * PAIR)
            query = joined_ref[at, cols] * jnp.asarray(0.125, BF)
            keys = split_heads(joined_ref[at, width + pair * PAIR : width + (pair + 1) * PAIR])
            vals = split_heads(
                joined_ref[at, 2 * width + pair * PAIR : 2 * width + (pair + 1) * PAIR]
            )
            scores = nt(keys, query)
            halves = []
            for head in range(2):
                part = scores[head * length : (head + 1) * length]
                part = jnp.exp(part - jnp.max(part, axis=0, keepdims=True))
                part = part * (1.0 / jnp.sum(part, axis=0, keepdims=True))
                halves.append(part.astype(BF))
            probs = jnp.concatenate(halves, axis=0)
            probs_ref[seq, pair] = probs
            ctx_ref[at, cols] = tn(probs, vals).astype(BF)
        return carry

    lax.fori_loop(0, rows // length, one, 0)


def attend(tokens, qkv, bias_row, length):
    rows, width = tokens.shape
    count = rows // length
    steps = 2
    block = rows // steps
    pairs = width // PAIR
    return pl.pallas_call(
        functools.partial(attend_kernel, length),
        grid=(steps,),
        in_specs=[
            pl.BlockSpec((block, width), lambda i: (i, 0)),
            full((3, width, width)),
            full(bias_row.shape),
        ],
        out_specs=[
            pl.BlockSpec((block, 3 * width), lambda i: (i, 0)),
            pl.BlockSpec((count // steps, pairs, 2 * length, length), lambda i: (i, 0, 0, 0)),
            pl.BlockSpec((block, width), lambda i: (i, 0)),
        ],
        out_shape=[
            jax.ShapeDtypeStruct((rows, 3 * width), BF),
            jax.ShapeDtypeStruct((count, pairs, 2 * length, length), BF),
            jax.ShapeDtypeStruct((rows, width), BF),
        ],
        compiler_params=params(),
        cost_estimate=cost(8 * rows * width * width, 20 * rows * width, rows * width),
        name="attend",
    )(tokens, qkv, bias_row)


def feed_kernel(
    length,
    exit_ref,
    tok_ref,
    ctx_ref,
    out_w_ref,
    vec_ref,
    up_ref,
    up_b_ref,
    down_ref,
    low_ref,
    act_ref,
    slope_ref,
    unit1_ref,
    scale1_ref,
    unit2_ref,
    scale2_ref,
    output_ref,
    acc_ref,
):
    step = pl.program_id(0)
    rows = tok_ref.shape[0]
    sub = 256

    @pl.when(step == 0)
    def _():
        for m in range(rows // sub):
            at = slice(m * sub, (m + 1) * sub)
            inner = tok_ref[at].astype(F32) + (
                nn(ctx_ref[at], out_w_ref[0]) + vec_ref[OUT_BIAS : OUT_BIAS + 1]
            )
            unit, scale = norm_stats(inner)
            first = unit * vec_ref[ATTN_GAIN : ATTN_GAIN + 1] + vec_ref[ATTN_SHIFT : ATTN_SHIFT + 1]
            unit1_ref[at] = unit.astype(BF)
            scale1_ref[at] = scale
            low_ref[at] = first.astype(BF)
            acc_ref[at] = first + vec_ref[DOWN_BIAS : DOWN_BIAS + 1]

    down = down_ref[...].reshape(up_ref.shape[1:])
    for m in range(rows // sub):
        at = slice(m * sub, (m + 1) * sub)
        hidden = nn(low_ref[at], up_ref[0]) + up_b_ref[...]
        act, slope = gelu_parts(hidden)
        act = act.astype(BF)
        act_ref[at] = act
        slope_ref[at] = slope.astype(BF)
        acc_ref[at] += nn(act, down)

    @pl.when(step == pl.num_programs(0) - 1)
    def _():
        for seq in range(rows // length):
            at = slice(seq * length, (seq + 1) * length)
            active = (exit_ref[seq] >= LAYER).astype(F32)
            unit, scale = norm_stats(acc_ref[at])
            unit2_ref[at] = unit.astype(BF)
            scale2_ref[at] = scale
            result = (
                unit * vec_ref[BLOCK_GAIN : BLOCK_GAIN + 1] + vec_ref[BLOCK_SHIFT : BLOCK_SHIFT + 1]
            ) * active
            output_ref[at] = result.astype(BF)


def feed(exit_layer, tokens, ctx, out_w, vec, up, up_bias, down, down_block, length):
    rows, width = tokens.shape
    steps = up.shape[0]
    hidden = steps * width
    whole = full((rows, width))
    return pl.pallas_call(
        functools.partial(feed_kernel, length),
        grid=(steps,),
        in_specs=[
            pl.BlockSpec(memory_space=pltpu.SMEM),
            whole,
            whole,
            pl.BlockSpec((1, width, width), lambda i: (3, 0, 0)),
            full(vec.shape),
            pl.BlockSpec((1, width, width), lambda i: (i, 0, 0)),
            pl.BlockSpec((1, width), lambda i: (0, i)),
            pl.BlockSpec(down_block, lambda i: (i, 0, 0)),
        ],
        out_specs=[
            whole,
            pl.BlockSpec((rows, width), lambda i: (0, i)),
            pl.BlockSpec((rows, width), lambda i: (0, i)),
            whole,
            full((rows, 1)),
            whole,
            full((rows, 1)),
            whole,
        ],
        out_shape=[
            jax.ShapeDtypeStruct((rows, width), BF),
            jax.ShapeDtypeStruct((rows, hidden), BF),
            jax.ShapeDtypeStruct((rows, hidden), BF),
            jax.ShapeDtypeStruct((rows, width), BF),
            jax.ShapeDtypeStruct((rows, 1), F32),
            jax.ShapeDtypeStruct((rows, width), BF),
            jax.ShapeDtypeStruct((rows, 1), F32),
            jax.ShapeDtypeStruct((rows, width), BF),
        ],
        scratch_shapes=[pltpu.VMEM((rows, width), F32)],
        compiler_params=params(),
        cost_estimate=cost(18 * rows * width * width, 40 * rows * width, 8 * rows * width),
        name="feed",
    )(exit_layer, tokens, ctx, out_w, vec, up, up_bias, down)


def leave_kernel(
    length,
    classes,
    exit_ref,
    output_ref,
    unit2_ref,
    scale2_ref,
    grad_ref,
    pool_ref,
    vec_ref,
    class_bias_ref,
    logit_grad_ref,
    act_ref,
    outer_ref,
    branch_ref,
    joint_grad_ref,
    sums_ref,
    class_grad_ref,
    logits_ref,
    stats_ref,
    lead_ref,
    pool_grad_ref,
):
    step = pl.program_id(0)
    rows, width = output_ref.shape
    pool = pool_ref[...].reshape(width, width)
    count = rows // length

    @pl.when(step == 0)
    def _():
        place = lax.broadcasted_iota(jnp.int32, (count, 1), 0)
        active = jnp.zeros((count, 1), F32)
        for seq in range(count):
            on = (exit_ref[seq] >= LAYER).astype(F32)
            active = jnp.where(place == seq, on, active)
        leading = jnp.concatenate(
            [output_ref[seq * length : seq * length + 1].astype(F32) for seq in range(count)],
            axis=0,
        ).astype(BF)
        pooled = jnp.tanh(nn(leading, pool) + vec_ref[POOL_BIAS : POOL_BIAS + 1])
        pooled_low = pooled.astype(BF)
        used = lax.broadcasted_iota(jnp.int32, (8, width), 0) < classes
        class_rows = jnp.where(used, vec_ref[CLASS_ROWS : CLASS_ROWS + 8], 0.0).astype(BF)
        raw = nt(pooled_low, class_rows) + class_bias_ref[...]
        lane = lax.broadcasted_iota(jnp.int32, raw.shape, 1) < classes
        top = jnp.max(jnp.where(lane, raw, -jnp.inf), axis=-1, keepdims=True)
        spread = jnp.where(lane, jnp.exp(raw - top), 0.0)
        logprob = raw - top - jnp.log(jnp.sum(spread, axis=-1, keepdims=True))
        entropy = -jnp.sum(
            jnp.where(lane, jnp.exp(logprob) * logprob, 0.0), axis=-1, keepdims=True
        )
        logits_ref[...] = raw * active
        class_grad = (logit_grad_ref[...].astype(F32) * active).astype(BF)
        stats_ref[0:1] = jnp.broadcast_to(jnp.sum(entropy * active, axis=0, keepdims=True), (1, 8))
        stats_ref[1:2] = jnp.sum(class_grad.astype(F32), axis=0, keepdims=True)
        class_grad_ref[...] = tn(class_grad, pooled_low)
        pooled_grad = nn(class_grad, class_rows)
        pre_grad = (pooled_grad * (1.0 - pooled * pooled)).astype(BF)
        sums_ref[3:4] = jnp.sum(pre_grad.astype(F32), axis=0, keepdims=True)
        pool_grad_ref[...] = tn(leading, pre_grad).reshape(pool_grad_ref.shape).astype(BF)
        lead_ref[...] = nt(pre_grad, pool)
        head = lax.broadcasted_iota(jnp.int32, (length, 1), 0) == 0
        gain = vec_ref[BLOCK_GAIN : BLOCK_GAIN + 1]
        gain_sum = jnp.zeros((1, width), F32)
        shift_sum = jnp.zeros((1, width), F32)
        bias_sum = jnp.zeros((1, width), F32)
        for seq in range(count):
            at = slice(seq * length, (seq + 1) * length)
            on = (exit_ref[seq] >= LAYER).astype(F32)
            top_grad = (
                grad_ref[at].astype(F32) + jnp.where(head, lead_ref[seq : seq + 1], 0.0)
            ) * on
            unit = unit2_ref[at].astype(F32)
            outer = norm_back(top_grad, unit, scale2_ref[at], gain)
            branch = outer.astype(BF)
            outer_ref[at] = outer
            branch_ref[at] = branch
            gain_sum += jnp.sum(top_grad * unit, axis=0, keepdims=True)
            shift_sum += jnp.sum(top_grad, axis=0, keepdims=True)
            bias_sum += jnp.sum(branch.astype(F32), axis=0, keepdims=True)
        sums_ref[0:1] = gain_sum
        sums_ref[1:2] = shift_sum
        sums_ref[2:3] = bias_sum

    @pl.when(step > 0)
    def _():
        few, both, _ = joint_grad_ref.shape
        deep = width // few
        value = tn(act_ref[...], branch_ref[...])
        for at in range(few):
            joint_grad_ref[at, 0:deep] = value[at * deep : (at + 1) * deep].astype(BF)
            joint_grad_ref[at, deep:both] = pool_grad_ref[(step - 1) * few + at]


def leave(
    exit_layer, output, unit2, scale2, output_grad, pool, vec, class_bias, logit_grad, act,
    pool_spec, shards, length, classes,
):
    rows, width = output.shape
    count = rows // length
    hidden = act.shape[1]
    steps = hidden // width
    few = shards // steps
    both = (hidden + width) // shards
    whole = full((rows, width))
    return pl.pallas_call(
        functools.partial(leave_kernel, length, classes),
        grid=(steps + 1,),
        in_specs=[
            pl.BlockSpec(memory_space=pltpu.SMEM),
            whole,
            whole,
            full((rows, 1)),
            whole,
            pool_spec,
            full(vec.shape),
            full(class_bias.shape),
            full(logit_grad.shape),
            pl.BlockSpec((rows, width), lambda i: (0, jnp.maximum(i - 1, 0))),
        ],
        out_specs=[
            whole,
            whole,
            pl.BlockSpec((few, both, width), lambda i: (jnp.maximum(i - 1, 0), 0, 0)),
            full((4, width)),
            full((8, width)),
            full((count, 8)),
            full((2, 8)),
        ],
        out_shape=[
            jax.ShapeDtypeStruct((rows, width), F32),
            jax.ShapeDtypeStruct((rows, width), BF),
            jax.ShapeDtypeStruct((shards, both, width), BF),
            jax.ShapeDtypeStruct((4, width), F32),
            jax.ShapeDtypeStruct((8, width), F32),
            jax.ShapeDtypeStruct((count, 8), F32),
            jax.ShapeDtypeStruct((2, 8), F32),
        ],
        scratch_shapes=[
            pltpu.VMEM((count, width), F32),
            pltpu.VMEM((shards, width // shards, width), BF),
        ],
        compiler_params=params(),
        cost_estimate=cost(8 * rows * width * width, 30 * rows * width),
        name="leave",
    )(exit_layer, output, unit2, scale2, output_grad, pool, vec, class_bias, logit_grad, act)


def feed_back_kernel(
    branch_ref,
    slope_ref,
    low_ref,
    down_ref,
    up_ref,
    outer_ref,
    unit1_ref,
    scale1_ref,
    out_w_ref,
    vec_ref,
    up_grad_ref,
    up_sum_ref,
    inner_ref,
    attended_ref,
    ctx_grad_ref,
    sums_ref,
    acc_ref,
    hid_ref,
):
    step = pl.program_id(0)
    rows, width = branch_ref.shape
    sub = 256

    @pl.when(step == 0)
    def _():
        acc_ref[...] = outer_ref[...]

    total = jnp.zeros((1, width), F32)
    down = down_ref[...].reshape(up_ref.shape[1:])
    for m in range(rows // sub):
        at = slice(m * sub, (m + 1) * sub)
        hid = (nt(branch_ref[at], down) * slope_ref[at].astype(F32)).astype(BF)
        hid_ref[at] = hid
        total += jnp.sum(hid.astype(F32), axis=0, keepdims=True)
        acc_ref[at] += nt(hid, up_ref[0])
    up_sum_ref[...] = total
    up_grad_ref[...] = tn(low_ref[...], hid_ref[...]).astype(BF)

    @pl.when(step == pl.num_programs(0) - 1)
    def _():
        gain = vec_ref[ATTN_GAIN : ATTN_GAIN + 1]
        gain_sum = jnp.zeros((1, width), F32)
        shift_sum = jnp.zeros((1, width), F32)
        bias_sum = jnp.zeros((1, width), F32)
        for m in range(rows // sub):
            at = slice(m * sub, (m + 1) * sub)
            grad = acc_ref[at]
            unit = unit1_ref[at].astype(F32)
            inner = norm_back(grad, unit, scale1_ref[at], gain)
            attended = inner.astype(BF)
            inner_ref[at] = inner
            attended_ref[at] = attended
            ctx_grad_ref[at] = nt(attended, out_w_ref[0]).astype(BF)
            gain_sum += jnp.sum(grad * unit, axis=0, keepdims=True)
            shift_sum += jnp.sum(grad, axis=0, keepdims=True)
            bias_sum += jnp.sum(attended.astype(F32), axis=0, keepdims=True)
        sums_ref[0:1] = gain_sum
        sums_ref[1:2] = shift_sum
        sums_ref[2:3] = bias_sum


def feed_back(branch, slope, low, down, down_block, up, outer, unit1, scale1, out_w, vec):
    rows, width = branch.shape
    hidden = slope.shape[1]
    steps = hidden // width
    whole = full((rows, width))
    return pl.pallas_call(
        feed_back_kernel,
        grid=(steps,),
        in_specs=[
            whole,
            pl.BlockSpec((rows, width), lambda i: (0, i)),
            whole,
            pl.BlockSpec(down_block, lambda i: (i, 0, 0)),
            pl.BlockSpec((1, width, width), lambda i: (i, 0, 0)),
            whole,
            whole,
            full((rows, 1)),
            pl.BlockSpec((1, width, width), lambda i: (3, 0, 0)),
            full(vec.shape),
        ],
        out_specs=[
            pl.BlockSpec((width, width), lambda i: (0, i)),
            pl.BlockSpec((1, width), lambda i: (0, i)),
            whole,
            whole,
            whole,
            full((3, width)),
        ],
        out_shape=[
            jax.ShapeDtypeStruct((width, hidden), BF),
            jax.ShapeDtypeStruct((1, hidden), F32),
            jax.ShapeDtypeStruct((rows, width), F32),
            jax.ShapeDtypeStruct((rows, width), BF),
            jax.ShapeDtypeStruct((rows, width), BF),
            jax.ShapeDtypeStruct((3, width), F32),
        ],
        scratch_shapes=[pltpu.VMEM((rows, width), F32), pltpu.VMEM((rows, width), BF)],
        compiler_params=params(),
        cost_estimate=cost(26 * rows * width * width, 40 * rows * width),
        name="feed_back",
    )(branch, slope, low, down, up, outer, unit1, scale1, out_w, vec)


def attend_back_kernel(length, joined_ref, probs_ref, ctx_grad_ref, grad_ref, sum_ref):
    rows, width = ctx_grad_ref.shape
    pairs = width // PAIR

    def one(seq, carry):
        at = pl.ds(pl.multiple_of(seq * length, length), length)
        for pair in range(pairs):
            at_q = slice(pair * PAIR, (pair + 1) * PAIR)
            at_k = slice(width + pair * PAIR, width + (pair + 1) * PAIR)
            at_v = slice(2 * width + pair * PAIR, 2 * width + (pair + 1) * PAIR)
            query = joined_ref[at, at_q] * jnp.asarray(0.125, BF)
            queries = split_heads(query)
            keys = split_heads(joined_ref[at, at_k])
            vals = split_heads(joined_ref[at, at_v])
            ctx_grad = ctx_grad_ref[at, at_q]
            ctx_grads = split_heads(ctx_grad)
            probs = probs_ref[seq, pair]
            prob_grad = nt(vals, ctx_grad)
            halves = []
            for head in range(2):
                cut = slice(head * length, (head + 1) * length)
                held = probs[cut].astype(F32)
                part = prob_grad[cut]
                base = jnp.sum(part * held, axis=0, keepdims=True)
                halves.append((held * (part - base)).astype(BF))
            stacked = jnp.concatenate(halves, axis=0)
            beside = jnp.concatenate(halves, axis=1)
            probs_beside = jnp.concatenate([probs[:length], probs[length:]], axis=1)
            grad_ref[at, at_q] = (tn(stacked, keys) * 0.125).astype(BF)
            grad_ref[at, at_k] = nn(beside, queries).astype(BF)
            grad_ref[at, at_v] = nn(probs_beside, ctx_grads).astype(BF)
        return carry

    lax.fori_loop(0, rows // length, one, 0)
    total = jnp.zeros(sum_ref.shape, F32)
    for m in range(rows // length):
        total += jnp.sum(
            grad_ref[m * length : (m + 1) * length].astype(F32), axis=0, keepdims=True
        )

    @pl.when(pl.program_id(0) == 0)
    def _():
        sum_ref[...] = total

    @pl.when(pl.program_id(0) > 0)
    def _():
        sum_ref[...] += total


def attend_back(joined, probs, ctx_grad, length):
    rows, width = ctx_grad.shape
    count = rows // length
    steps = 2
    block = rows // steps
    pairs = width // PAIR
    return pl.pallas_call(
        functools.partial(attend_back_kernel, length),
        grid=(steps,),
        in_specs=[
            pl.BlockSpec((block, 3 * width), lambda i: (i, 0)),
            pl.BlockSpec((count // steps, pairs, 2 * length, length), lambda i: (i, 0, 0, 0)),
            pl.BlockSpec((block, width), lambda i: (i, 0)),
        ],
        out_specs=[
            pl.BlockSpec((block, 3 * width), lambda i: (i, 0)),
            full((1, 3 * width)),
        ],
        out_shape=[
            jax.ShapeDtypeStruct((rows, 3 * width), BF),
            jax.ShapeDtypeStruct((1, 3 * width), F32),
        ],
        compiler_params=params(),
        cost_estimate=cost(8 * rows * width * width, 20 * rows * width),
        name="attend_back",
    )(joined, probs, ctx_grad)


def weight_grads_kernel(
    place_ref, tok_ref, ctx_ref, joined_ref, attended_ref, row_ref, keep_ref, send_ref, value_ref
):
    last = pl.num_programs(0) - 1
    chips, depth, width = keep_ref.shape[1:]
    part = tok_ref.shape[1] // (2 * chips)
    first = place_ref[2] == 0

    @pl.when(pl.program_id(0) < last)
    def _():
        value_ref[...] = tn(tok_ref[...], joined_ref[...])

    @pl.when(pl.program_id(0) == last)
    def _():
        value_ref[...] = tn(ctx_ref[...], attended_ref[...])

    for chip in range(chips):
        even = value_ref[2 * chip * part : (2 * chip + 1) * part]
        odd = value_ref[(2 * chip + 1) * part : (2 * chip + 2) * part]
        keep_ref[0, chip, 0:part] = jnp.where(first, even, odd).astype(BF)
        send_ref[0, chip, 0:part] = jnp.where(first, odd, even).astype(BF)
        if depth > part:
            top = lax.broadcasted_iota(jnp.int32, (depth - part, width), 0) == 0
            even = row_ref[0, 2 * chip : 2 * chip + 1]
            odd = row_ref[0, 2 * chip + 1 : 2 * chip + 2]
            keep_ref[0, chip, part:depth] = jnp.where(
                top, jnp.where(first, even, odd), 0.0
            ).astype(BF)
            send_ref[0, chip, part:depth] = jnp.where(
                top, jnp.where(first, odd, even), 0.0
            ).astype(BF)


def weight_grads(place, tokens, ctx, joined_grad, attended, small, chips, extra):
    rows, width = tokens.shape
    depth = width // (2 * chips) + extra
    whole = full((rows, width))
    spec = pl.BlockSpec((1, chips, depth, width), lambda i: (i, 0, 0, 0))
    shape = jax.ShapeDtypeStruct((4, chips, depth, width), BF)
    return pl.pallas_call(
        weight_grads_kernel,
        grid=(4,),
        in_specs=[
            pl.BlockSpec(memory_space=pltpu.SMEM),
            whole,
            whole,
            pl.BlockSpec((rows, width), lambda i: (0, jnp.minimum(i, 2))),
            whole,
            pl.BlockSpec((1, 2 * chips, width), lambda i: (i, 0, 0)),
        ],
        out_specs=[spec, spec],
        out_shape=[shape, shape],
        scratch_shapes=[pltpu.VMEM((width, width), F32)],
        compiler_params=params(),
        cost_estimate=cost(8 * rows * width * width, 20 * rows * width),
        name="weight_grads",
    )(place, tokens, ctx, joined_grad, attended, small)


def input_kernel(inner_ref, joined_ref, w_ref, out_ref):
    width = inner_ref.shape[1]
    total = inner_ref[...]
    for part in range(3):
        total += nt(joined_ref[:, part * width : (part + 1) * width], w_ref[part])
    out_ref[...] = total.astype(BF)


def input_back(inner, joined_grad, qkv):
    rows, width = inner.shape
    steps = 4
    block = rows // steps
    return pl.pallas_call(
        input_kernel,
        grid=(steps,),
        in_specs=[
            pl.BlockSpec((block, width), lambda i: (i, 0)),
            pl.BlockSpec((block, 3 * width), lambda i: (i, 0)),
            full((3, width, width)),
        ],
        out_specs=pl.BlockSpec((block, width), lambda i: (i, 0)),
        out_shape=jax.ShapeDtypeStruct((rows, width), BF),
        compiler_params=params(),
        cost_estimate=cost(6 * rows * width * width, 12 * rows * width),
        name="input_back",
    )(inner, joined_grad, qkv)


def lay_kernel(plan, chips, reps, part, counts, place_ref, *refs):
    at = 0
    groups = []
    for number in counts:
        groups.append(refs[at : at + number])
        at += number
    sems = refs[-1]
    rep, chip, core = place_ref[0], place_ref[1], place_ref[2]
    copies = []

    def start(source, target):
        copies.append(pltpu.make_async_copy(source, target, sems.at[len(copies)]))
        copies[-1].start()

    plan(start, groups, refs[at:-1], rep, chip, core, chips, reps, part)
    for copy in copies:
        copy.wait()


def blocks_plan(put, own, twin, along, across, swapped, depth, first, rep, chip, core, chips, reps, part):
    for block in range(reps):
        put(own(block), block, chip, core)
        put(twin(block), block, chip, 1 - core)
    for step in range(1, chips):
        source = lax.rem(chip + chips - step, chips)
        rows = pl.ds((step - 1) * depth + first, part)
        put(along[step - 1].at[pl.ds(first, part)], rep, source, core)
        put(swapped[0].at[rows], rep, source, 1 - core)
        for other in range(1, reps):
            put(across[other - 1].at[rows], rep ^ other, source, core)
            put(swapped[other].at[rows], rep ^ other, source, 1 - core)


def wide_put(start, out_ref, part):
    def put(source, block, at_chip, at_core):
        row = pl.multiple_of((at_chip * 2 + at_core) * part, part)
        start(source, out_ref.at[block, pl.ds(row, part)])

    return put


def wide_block(ref, width, part):
    return lambda block: ref.at[pl.ds(0, part), pl.ds(block * width, width)]


def first_plan(start, groups, outs, rep, chip, core, chips, reps, part):
    owns, along, across, swapped, extra = groups
    own, twin = owns
    out_ref, more_ref = outs
    width = out_ref.shape[2]
    blocks_plan(
        wide_put(start, out_ref, part),
        wide_block(own, width, part),
        wide_block(twin, width, part),
        along,
        across,
        swapped,
        part,
        0,
        rep,
        chip,
        core,
        chips,
        reps,
        part,
    )
    tail = pl.ds(part, 16)
    cols = pl.ds(0, width)
    start(own.at[tail, cols], more_ref.at[chip * 2 + core])
    start(twin.at[tail, cols], more_ref.at[chip * 2 + 1 - core])
    for step in range(1, chips):
        source = lax.rem(chip + chips - step, chips)
        start(along[step - 1].at[tail], more_ref.at[source * 2 + core])
        start(extra[0].at[pl.ds((step - 1) * 16, 16)], more_ref.at[source * 2 + 1 - core])


def second_plan(start, groups, outs, rep, chip, core, chips, reps, part):
    owns, along, across, swapped = groups
    up, up_twin, down, down_twin = owns
    up_ref, down_ref = outs
    width = up_ref.shape[2]
    where = (rep, chip, core, chips, reps, part)
    blocks_plan(
        wide_put(start, up_ref, part),
        wide_block(up, width, part),
        wide_block(up_twin, width, part),
        along,
        across,
        swapped,
        2 * part,
        0,
        *where,
    )

    def put(source, block, at_chip, at_core):
        row = pl.multiple_of(block * part, part)
        start(source, down_ref.at[at_chip * 2 + at_core, pl.ds(row, part)])

    def tall(ref):
        return lambda block: ref.at[pl.ds(block * part, part)]

    blocks_plan(
        put, tall(down), tall(down_twin), along, across, swapped, 2 * part, part, *where
    )


def lay(plan, place, groups, shapes, copies, part, chips, reps):
    anywhere = pl.BlockSpec(memory_space=pl.ANY)
    inputs = [ref for group in groups for ref in group]
    return pl.pallas_call(
        functools.partial(
            lay_kernel, plan, chips, reps, part, [len(group) for group in groups]
        ),
        in_specs=[pl.BlockSpec(memory_space=pltpu.SMEM)] + [anywhere] * len(inputs),
        out_specs=[pl.BlockSpec(memory_space=pltpu.VMEM)] * len(shapes),
        out_shape=[jax.ShapeDtypeStruct(shape, BF) for shape in shapes],
        scratch_shapes=[pltpu.SemaphoreType.DMA((copies,))],
        compiler_params=pltpu.CompilerParams(vmem_limit_bytes=VMEM_BYTES),
        cost_estimate=cost(0, 4 * sum(math.prod(shape) for shape in shapes)),
        name="lay",
    )(place, *inputs)


def pack_vectors(rows, up_bias, class_weight):
    first = jnp.concatenate(rows[:8] + [class_weight.T.reshape(-1)] + rows[8:])
    return jnp.concatenate([first, up_bias])[None]


def move(values, reps, chips, target):
    pairs = []
    for rep in range(reps):
        for chip in range(chips):
            for core in range(2):
                to_rep, to_chip, to_core = target(rep, chip, core)
                pairs.append(
                    (
                        (rep * chips + chip) * 2 + core,
                        (to_rep * chips + to_chip) * 2 + to_core,
                    )
                )
    return lax.ppermute(values, ("rep", "fsdp"), pairs)


def along_chips(step, chips):
    return lambda rep, chip, core: (rep, (chip + step) % chips, core)


def across_reps(other):
    return lambda rep, chip, core: (rep ^ other, chip, core)


def to_twin(rep, chip, core):
    return rep, chip, 1 - core


def after(values, *gates):
    return lax.optimization_barrier((values, *gates))[0]


def along_z(mine, reps, chips):
    return [move(mine, reps, chips, along_chips(step, chips)) for step in range(1, chips)]


def over_reps(stacked, reps, chips):
    return [move(stacked, reps, chips, across_reps(other)) for other in range(1, reps)]


def pick(parts, at):
    return lax.dynamic_index_in_dim(parts, at, axis=0, keepdims=False)


def in_order(rep, reps, own, others, axis):
    blocks = jnp.stack([own] + others)
    return jnp.concatenate([pick(blocks, rep ^ at) for at in range(reps)], axis=axis)


def sum_blocks(place, keep, send, reps, chips):
    rep, chip = place[0], place[1]
    got = move(send, reps, chips, to_twin)

    def both(at):
        return pick(keep, at).astype(F32) + pick(got, at).astype(F32)

    arrived = [
        move(both(rep ^ other).astype(BF), reps, chips, across_reps(other))
        for other in range(1, reps)
    ]

    def over_reps(at):
        total = pick(pick(keep, rep), at).astype(F32) + pick(pick(got, rep), at).astype(F32)
        for block in arrived:
            total = total + pick(block, at).astype(F32)
        return total

    total = over_reps(chip)
    for step in range(1, chips):
        there = over_reps(lax.rem(chip + step, chips)).astype(BF)
        total = total + move(there, reps, chips, along_chips(step, chips)).astype(F32)
    total = total.astype(BF)
    others = [move(total, reps, chips, across_reps(other)) for other in range(1, reps)]
    return in_order(rep, reps, total, others, 1)


def sum_over_reps(place, rows, reps, chips):
    rep = place[0]
    parts = rows.reshape(reps, -1, rows.shape[1])
    total = pick(parts, rep).astype(F32)
    for other in range(1, reps):
        there = pick(parts, rep ^ other)
        total = total + move(there, reps, chips, across_reps(other)).astype(F32)
    total = total.astype(BF)
    others = [move(total, reps, chips, across_reps(other)) for other in range(1, reps)]
    return in_order(rep, reps, total, others, 0)


def per_device(
    tokens,
    exit_layer,
    qkv_weight,
    query_bias,
    value_bias,
    out_weight,
    out_bias,
    attn_gain,
    attn_shift,
    up_weight,
    up_bias,
    down_weight,
    down_bias,
    block_gain,
    block_shift,
    pool_weight,
    pool_bias,
    class_weight,
    class_bias,
    output_grad,
    logit_grad,
):
    reps = lax.axis_size("rep")
    shards = lax.axis_size("fsdp")
    mine = lax.axis_index("fsdp")
    rows, width = tokens.shape
    count = exit_layer.shape[0]
    length = rows // count
    classes = class_weight.shape[1]
    part = out_weight.shape[0]
    hidden = up_weight.shape[1]

    def gather(shard):
        return lax.all_gather(shard, "fsdp", axis=0, tiled=True)

    packed = pack_vectors(
        [
            query_bias,
            value_bias,
            out_bias,
            attn_gain,
            attn_shift,
            down_bias,
            block_gain,
            block_shift,
            pool_bias,
        ],
        up_bias,
        class_weight,
    )
    joint_own = jnp.concatenate([qkv_weight, out_weight], axis=1)
    deep = down_weight.shape[0]
    pool = gather(pool_weight)
    chips = shards // 2
    place = jnp.stack([lax.axis_index("rep"), mine // 2, mine % 2]).astype(jnp.int32)
    direct = (
        part % 16 == 0
        and reps & (reps - 1) == 0
        and reps * width == hidden
        and packed.shape[1] % width == 0
        and packed.shape[1] <= 16 * width
    )
    if direct:
        lines = packed.shape[1] // width
        held = jnp.pad(packed.reshape(lines, width), ((0, 16 - lines), (0, 0)))
        own = jnp.concatenate([joint_own, jnp.tile(held, (1, reps))], axis=0)
        rep = place[0]
        along = along_z(
            lax.dynamic_slice_in_dim(own, rep * width, width, axis=1), reps, chips
        )
        twin = move(own, reps, chips, to_twin)
        stacked = jnp.concatenate([rows_[:part] for rows_ in along], axis=0)
        across = over_reps(stacked, reps, chips)
        swapped = [move(rows_, reps, chips, to_twin) for rows_ in [stacked] + across]
        extra = move(
            jnp.concatenate([rows_[part:] for rows_ in along], axis=0), reps, chips, to_twin
        )
        second = jnp.concatenate(
            [
                lax.dynamic_slice_in_dim(up_weight, rep * width, width, axis=1),
                lax.dynamic_slice_in_dim(down_weight, rep * part, part, axis=0),
            ],
            axis=0,
        )
        second_along = along_z(after(second, *along), reps, chips)
        up_twin = move(up_weight, reps, chips, to_twin)
        down_twin = move(down_weight, reps, chips, to_twin)
        second_stacked = jnp.concatenate(second_along, axis=0)
        second_across = over_reps(after(second_stacked, *across), reps, chips)
        joint, small = lay(
            first_plan,
            place,
            [[own, twin], along, across, swapped, [extra]],
            [(reps, width, width), (shards, 16, width)],
            2 * chips * (reps + 1),
            part,
            chips,
            reps,
        )
        small = small[:, :lines].reshape(shards, -1)
        down_block = (width // deep, deep, width)
    else:
        small = gather(packed)
        joint = jnp.stack(jnp.split(gather(joint_own), 4, axis=1))
        up = jnp.stack(jnp.split(gather(up_weight), hidden // width, axis=1))
        down = gather(down_weight).reshape(-1, width, width)
        down_block = (1, width, width)
    vec = (
        small[:, : VECTOR_ROWS * part]
        .reshape(shards, VECTOR_ROWS, part)
        .transpose(1, 0, 2)
        .reshape(VECTOR_ROWS, width)
        .astype(F32)
    )
    vec = jnp.pad(vec, ((0, 16 - VECTOR_ROWS), (0, 0)))
    up_row = small[:, VECTOR_ROWS * part :].reshape(1, hidden).astype(F32)
    bias_row = jnp.concatenate([vec[:1], jnp.zeros((1, width), F32), vec[1:2]], axis=1)

    joined, probs, ctx = attend(tokens, joint, bias_row, length)
    if direct:
        second_swapped = [
            move(after(rows_, ctx), reps, chips, to_twin)
            for rows_ in [second_stacked] + second_across
        ]
        up, down = lay(
            second_plan,
            place,
            [
                [up_weight, up_twin, down_weight, down_twin],
                second_along,
                second_across,
                second_swapped,
            ],
            [(reps, width, width), (shards, deep, width)],
            4 * chips * reps,
            part,
            chips,
            reps,
        )
    low, act, slope, unit1, scale1, unit2, scale2, output = feed(
        exit_layer, tokens, ctx, joint, vec, up, up_row, down, down_block, length
    )
    class_bias_row = jnp.pad(class_bias.astype(F32), (0, 8 - classes))[None]
    logit_grad_rows = jnp.pad(logit_grad, ((0, 0), (0, 8 - classes)))
    outer, branch, low_grad, exit_sums, class_grad, logits, stats = leave(
        exit_layer,
        output,
        unit2,
        scale2,
        output_grad,
        pool,
        vec,
        class_bias_row,
        logit_grad_rows,
        act,
        full((width, width)),
        shards,
        length,
        classes,
    )
    up_grad, up_sum, inner, attended, ctx_grad, feed_sums = feed_back(
        branch, slope, low, down, down_block, up, outer, unit1, scale1, joint, vec
    )
    joined_grad, joined_sum = attend_back(joined, probs, ctx_grad, length)
    sums = jnp.concatenate(
        [
            joined_sum.reshape(3, width)[::2],
            feed_sums,
            exit_sums,
            class_grad[:classes],
        ],
        axis=0,
    )
    lines = sums.shape[0]
    own_sums = sums.reshape(lines, shards, part).transpose(1, 0, 2).reshape(shards, lines * part)
    own_sums = jnp.concatenate([own_sums, up_sum.reshape(shards, deep)], axis=1)
    used = own_sums.shape[1]
    seqs_total = count * reps * shards
    figures = jnp.concatenate([stats[0, :1], stats[1, :classes]])
    slots = reps * shards * figures.shape[0] * 3
    direct = direct and used + slots <= 4 * width
    if direct:
        high = figures.astype(BF).astype(F32)
        middle = (figures - high).astype(BF).astype(F32)
        lowest = figures - high - middle
        split = jnp.concatenate([high, middle, lowest])
        slot = lax.axis_index("rep") * shards + mine
        lone = jnp.where(
            jnp.arange(reps * shards)[:, None] == slot, split[None], 0.0
        ).reshape(1, slots)
        row = jnp.concatenate([own_sums, jnp.broadcast_to(lone, (shards, slots))], axis=1)
        row = jnp.pad(row, ((0, 0), (0, 4 * width - row.shape[1])))
        row = row.reshape(shards, 4, width).transpose(1, 0, 2)
    else:
        row = jnp.zeros((4, shards, width), F32)
    keep, send = weight_grads(
        place, tokens, ctx, joined_grad, attended, row, chips, 16 if direct else 0
    )
    input_grad = input_back(inner, joined_grad, joint)

    def scatter(grad):
        return lax.psum_scatter(grad, "fsdp", scatter_dimension=0, tiled=True)

    low_part = scatter(low_grad.reshape(shards * (deep + part), width))
    up_grad = after(up_grad, low_part, keep)
    up_part = scatter(up_grad)
    if direct:
        joint_sum = sum_blocks(place, keep, send, reps, chips).astype(F32)
        low_sum = sum_over_reps(place, low_part, reps, chips).astype(F32)
        up_sum = sum_over_reps(place, up_part, reps, chips).astype(F32)
        small_sum = joint_sum[part]
        joint_sum = joint_sum[:part]
        total = small_sum[used : used + slots].reshape(-1, figures.shape[0]).sum(axis=0)
    else:
        first = mine % 2 == 0
        pair = jnp.stack([jnp.where(first, keep, send), jnp.where(first, send, keep)], axis=2)
        joint_grad = pair.reshape(4, width, width).transpose(1, 0, 2).reshape(width, 4 * width)
        joint_sum, low_sum, up_sum = lax.psum((scatter(joint_grad), low_part, up_part), "rep")
        joint_sum, low_sum, up_sum = (
            joint_sum.astype(F32),
            low_sum.astype(F32),
            up_sum.astype(F32),
        )
        own_sums, total = lax.psum((own_sums, figures), ("rep", "fsdp"))
        small_sum = pick(own_sums, mine)
    own = small_sum[: lines * part].reshape(lines, part)
    return (
        output,
        logits[:, :classes],
        total[0] / seqs_total,
        input_grad,
        joint_sum[:, : 3 * width],
        own[0],
        own[1],
        joint_sum[:, 3 * width :],
        own[4],
        own[2],
        own[3],
        up_sum,
        small_sum[lines * part : used],
        low_sum[:deep],
        own[7],
        own[5],
        own[6],
        low_sum[deep:],
        own[8],
        own[9 : 9 + classes].T,
        total[1:],
    )


def solution(mesh):
    return jax.shard_map(
        per_device,
        mesh=mesh,
        in_specs=(
            P(("rep", "fsdp"), None),
            P(("rep", "fsdp")),
            P("fsdp", None),
            P("fsdp"),
            P("fsdp"),
            P("fsdp", None),
            P("fsdp"),
            P("fsdp"),
            P("fsdp"),
            P("fsdp", None),
            P("fsdp"),
            P("fsdp", None),
            P("fsdp"),
            P("fsdp"),
            P("fsdp"),
            P("fsdp", None),
            P("fsdp"),
            P("fsdp", None),
            P(),
            P(("rep", "fsdp"), None),
            P(("rep", "fsdp"), None),
        ),
        out_specs=(
            P(("rep", "fsdp"), None),
            P(("rep", "fsdp"), None),
            P(),
            P(("rep", "fsdp"), None),
            P("fsdp", None),
            P("fsdp"),
            P("fsdp"),
            P("fsdp", None),
            P("fsdp"),
            P("fsdp"),
            P("fsdp"),
            P("fsdp", None),
            P("fsdp"),
            P("fsdp", None),
            P("fsdp"),
            P("fsdp"),
            P("fsdp"),
            P("fsdp", None),
            P("fsdp"),
            P("fsdp", None),
            P(),
        ),
        check_vma=False,
    )
```

```python
import functools
import math

import jax
import jax.numpy as jnp
from jax import lax
from jax.experimental import pallas as pl
from jax.experimental.pallas import tpu as pltpu
from jax.sharding import PartitionSpec as P

HD = 64
LAYER = 6
PAIR = 2 * HD
VMEM_BYTES = 58 * 2**20
BF = jnp.bfloat16
F32 = jnp.float32

QUERY_BIAS, VALUE_BIAS, OUT_BIAS, ATTN_GAIN, ATTN_SHIFT = 0, 1, 2, 3, 4
DOWN_BIAS, BLOCK_GAIN, BLOCK_SHIFT, CLASS_ROWS, POOL_BIAS = 5, 6, 7, 8, 11
VECTOR_ROWS = 12


def nn(left, right):
    return jnp.dot(left, right, preferred_element_type=F32)


def tn(left, right):
    return lax.dot_general(left, right, (((0,), (0,)), ((), ())), preferred_element_type=F32)


def nt(left, right):
    return lax.dot_general(left, right, (((1,), (1,)), ((), ())), preferred_element_type=F32)


def full(shape):
    return pl.BlockSpec(shape, lambda *at: (0,) * len(shape))


def params():
    return pltpu.CompilerParams(
        dimension_semantics=("arbitrary",), vmem_limit_bytes=VMEM_BYTES
    )


def cost(flops, moved, trans=0):
    return pl.CostEstimate(flops=flops, bytes_accessed=moved, transcendentals=trans)


def split_heads(pair):
    lane = lax.broadcasted_iota(jnp.int32, pair.shape, 1)
    zero = jnp.zeros_like(pair)
    return jnp.concatenate(
        [jnp.where(lane < HD, pair, zero), jnp.where(lane < HD, zero, pair)], axis=0
    )


def norm_stats(values):
    center = values - jnp.mean(values, axis=-1, keepdims=True)
    spread = jnp.mean(center * center, axis=-1, keepdims=True)
    scale = lax.rsqrt(spread + 1e-06)
    return center * scale, scale


def norm_back(grad, unit, scale, gain):
    inner = grad * gain
    first = jnp.mean(inner, axis=-1, keepdims=True)
    second = jnp.mean(inner * unit, axis=-1, keepdims=True)
    return scale * (inner - first - unit * second)


def gelu_parts(values):
    size = jnp.abs(values)
    t = 1.0 / (1.0 + 0.23164189 * size)
    bell = jnp.exp(-0.5 * values * values)
    poly = t * (
        0.127414796
        + t * (-0.142248368 + t * (0.7107068705 + t * (-0.7265760135 + t * 0.5307027145)))
    )
    tail = poly * bell
    below = jnp.where(values >= 0.0, 1.0 - tail, tail)
    return values * below, below + values * (bell * 0.3989422804014327)


def attend_kernel(length, tok_ref, w_ref, bias_ref, joined_ref, probs_ref, ctx_ref):
    rows, width = ctx_ref.shape
    pairs = width // PAIR
    for part in range(3):
        cols = slice(part * width, (part + 1) * width)
        joined_ref[:, cols] = (nn(tok_ref[...], w_ref[part]) + bias_ref[:, cols]).astype(BF)

    def one(seq, carry):
        at = pl.ds(pl.multiple_of(seq * length, length), length)
        for pair in range(pairs):
            cols = slice(pair * PAIR, (pair + 1) * PAIR)
            query = joined_ref[at, cols] * jnp.asarray(0.125, BF)
            keys = split_heads(joined_ref[at, width + pair * PAIR : width + (pair + 1) * PAIR])
            vals = split_heads(
                joined_ref[at, 2 * width + pair * PAIR : 2 * width + (pair + 1) * PAIR]
            )
            scores = nt(keys, query)
            halves = []
            for head in range(2):
                part = scores[head * length : (head + 1) * length]
                part = jnp.exp(part - jnp.max(part, axis=0, keepdims=True))
                part = part * (1.0 / jnp.sum(part, axis=0, keepdims=True))
                halves.append(part.astype(BF))
            probs = jnp.concatenate(halves, axis=0)
            probs_ref[seq, pair] = probs
            ctx_ref[at, cols] = tn(probs, vals).astype(BF)
        return carry

    lax.fori_loop(0, rows // length, one, 0)


def attend(tokens, qkv, bias_row, length):
    rows, width = tokens.shape
    count = rows // length
    steps = 2
    block = rows // steps
    pairs = width // PAIR
    return pl.pallas_call(
        functools.partial(attend_kernel, length),
        grid=(steps,),
        in_specs=[
            pl.BlockSpec((block, width), lambda i: (i, 0)),
            full((3, width, width)),
            full(bias_row.shape),
        ],
        out_specs=[
            pl.BlockSpec((block, 3 * width), lambda i: (i, 0)),
            pl.BlockSpec((count // steps, pairs, 2 * length, length), lambda i: (i, 0, 0, 0)),
            pl.BlockSpec((block, width), lambda i: (i, 0)),
        ],
        out_shape=[
            jax.ShapeDtypeStruct((rows, 3 * width), BF),
            jax.ShapeDtypeStruct((count, pairs, 2 * length, length), BF),
            jax.ShapeDtypeStruct((rows, width), BF),
        ],
        compiler_params=params(),
        cost_estimate=cost(8 * rows * width * width, 20 * rows * width, rows * width),
        name="attend",
    )(tokens, qkv, bias_row)


def feed_kernel(
    length,
    exit_ref,
    tok_ref,
    ctx_ref,
    out_w_ref,
    vec_ref,
    up_ref,
    up_b_ref,
    down_ref,
    low_ref,
    act_ref,
    slope_ref,
    unit1_ref,
    scale1_ref,
    unit2_ref,
    scale2_ref,
    output_ref,
    acc_ref,
):
    step = pl.program_id(0)
    rows = tok_ref.shape[0]
    sub = 256

    @pl.when(step == 0)
    def _():
        for m in range(rows // sub):
            at = slice(m * sub, (m + 1) * sub)
            inner = tok_ref[at].astype(F32) + (
                nn(ctx_ref[at], out_w_ref[0]) + vec_ref[OUT_BIAS : OUT_BIAS + 1]
            )
            unit, scale = norm_stats(inner)
            first = unit * vec_ref[ATTN_GAIN : ATTN_GAIN + 1] + vec_ref[ATTN_SHIFT : ATTN_SHIFT + 1]
            unit1_ref[at] = unit.astype(BF)
            scale1_ref[at] = scale
            low_ref[at] = first.astype(BF)
            acc_ref[at] = first + vec_ref[DOWN_BIAS : DOWN_BIAS + 1]

    down = down_ref[...].reshape(up_ref.shape[1:])
    for m in range(rows // sub):
        at = slice(m * sub, (m + 1) * sub)
        hidden = nn(low_ref[at], up_ref[0]) + up_b_ref[...]
        act, slope = gelu_parts(hidden)
        act = act.astype(BF)
        act_ref[at] = act
        slope_ref[at] = slope.astype(BF)
        acc_ref[at] += nn(act, down)

    @pl.when(step == pl.num_programs(0) - 1)
    def _():
        for seq in range(rows // length):
            at = slice(seq * length, (seq + 1) * length)
            active = (exit_ref[seq] >= LAYER).astype(F32)
            unit, scale = norm_stats(acc_ref[at])
            unit2_ref[at] = unit.astype(BF)
            scale2_ref[at] = scale
            result = (
                unit * vec_ref[BLOCK_GAIN : BLOCK_GAIN + 1] + vec_ref[BLOCK_SHIFT : BLOCK_SHIFT + 1]
            ) * active
            output_ref[at] = result.astype(BF)


def feed(exit_layer, tokens, ctx, out_w, vec, up, up_bias, down, down_block, length):
    rows, width = tokens.shape
    steps = up.shape[0]
    hidden = steps * width
    whole = full((rows, width))
    return pl.pallas_call(
        functools.partial(feed_kernel, length),
        grid=(steps,),
        in_specs=[
            pl.BlockSpec(memory_space=pltpu.SMEM),
            whole,
            whole,
            pl.BlockSpec((1, width, width), lambda i: (3, 0, 0)),
            full(vec.shape),
            pl.BlockSpec((1, width, width), lambda i: (i, 0, 0)),
            pl.BlockSpec((1, width), lambda i: (0, i)),
            pl.BlockSpec(down_block, lambda i: (i, 0, 0)),
        ],
        out_specs=[
            whole,
            pl.BlockSpec((rows, width), lambda i: (0, i)),
            pl.BlockSpec((rows, width), lambda i: (0, i)),
            whole,
            full((rows, 1)),
            whole,
            full((rows, 1)),
            whole,
        ],
        out_shape=[
            jax.ShapeDtypeStruct((rows, width), BF),
            jax.ShapeDtypeStruct((rows, hidden), BF),
            jax.ShapeDtypeStruct((rows, hidden), BF),
            jax.ShapeDtypeStruct((rows, width), BF),
            jax.ShapeDtypeStruct((rows, 1), F32),
            jax.ShapeDtypeStruct((rows, width), BF),
            jax.ShapeDtypeStruct((rows, 1), F32),
            jax.ShapeDtypeStruct((rows, width), BF),
        ],
        scratch_shapes=[pltpu.VMEM((rows, width), F32)],
        compiler_params=params(),
        cost_estimate=cost(18 * rows * width * width, 40 * rows * width, 8 * rows * width),
        name="feed",
    )(exit_layer, tokens, ctx, out_w, vec, up, up_bias, down)


def leave_kernel(
    length,
    classes,
    place_ref,
    exit_ref,
    output_ref,
    unit2_ref,
    scale2_ref,
    grad_ref,
    pool_ref,
    vec_ref,
    class_bias_ref,
    logit_grad_ref,
    act_ref,
    outer_ref,
    branch_ref,
    keep_ref,
    send_ref,
    sums_ref,
    class_grad_ref,
    logits_ref,
    stats_ref,
    lead_ref,
    pool_grad_ref,
):
    step = pl.program_id(0)
    rows, width = output_ref.shape
    pool = pool_ref[...].reshape(width, width)
    count = rows // length

    @pl.when(step == 0)
    def _():
        place = lax.broadcasted_iota(jnp.int32, (count, 1), 0)
        active = jnp.zeros((count, 1), F32)
        for seq in range(count):
            on = (exit_ref[seq] >= LAYER).astype(F32)
            active = jnp.where(place == seq, on, active)
        leading = jnp.concatenate(
            [output_ref[seq * length : seq * length + 1].astype(F32) for seq in range(count)],
            axis=0,
        ).astype(BF)
        pooled = jnp.tanh(nn(leading, pool) + vec_ref[POOL_BIAS : POOL_BIAS + 1])
        pooled_low = pooled.astype(BF)
        used = lax.broadcasted_iota(jnp.int32, (8, width), 0) < classes
        class_rows = jnp.where(used, vec_ref[CLASS_ROWS : CLASS_ROWS + 8], 0.0).astype(BF)
        raw = nt(pooled_low, class_rows) + class_bias_ref[...]
        lane = lax.broadcasted_iota(jnp.int32, raw.shape, 1) < classes
        top = jnp.max(jnp.where(lane, raw, -jnp.inf), axis=-1, keepdims=True)
        spread = jnp.where(lane, jnp.exp(raw - top), 0.0)
        logprob = raw - top - jnp.log(jnp.sum(spread, axis=-1, keepdims=True))
        entropy = -jnp.sum(
            jnp.where(lane, jnp.exp(logprob) * logprob, 0.0), axis=-1, keepdims=True
        )
        logits_ref[...] = raw * active
        class_grad = (logit_grad_ref[...].astype(F32) * active).astype(BF)
        stats_ref[0:1] = jnp.broadcast_to(jnp.sum(entropy * active, axis=0, keepdims=True), (1, 8))
        stats_ref[1:2] = jnp.sum(class_grad.astype(F32), axis=0, keepdims=True)
        class_grad_ref[...] = tn(class_grad, pooled_low)
        pooled_grad = nn(class_grad, class_rows)
        pre_grad = (pooled_grad * (1.0 - pooled * pooled)).astype(BF)
        sums_ref[3:4] = jnp.sum(pre_grad.astype(F32), axis=0, keepdims=True)
        pool_grad_ref[...] = tn(leading, pre_grad).reshape(pool_grad_ref.shape).astype(BF)
        lead_ref[...] = nt(pre_grad, pool)
        head = lax.broadcasted_iota(jnp.int32, (length, 1), 0) == 0
        gain = vec_ref[BLOCK_GAIN : BLOCK_GAIN + 1]
        gain_sum = jnp.zeros((1, width), F32)
        shift_sum = jnp.zeros((1, width), F32)
        bias_sum = jnp.zeros((1, width), F32)
        for seq in range(count):
            at = slice(seq * length, (seq + 1) * length)
            on = (exit_ref[seq] >= LAYER).astype(F32)
            top_grad = (
                grad_ref[at].astype(F32) + jnp.where(head, lead_ref[seq : seq + 1], 0.0)
            ) * on
            unit = unit2_ref[at].astype(F32)
            outer = norm_back(top_grad, unit, scale2_ref[at], gain)
            branch = outer.astype(BF)
            outer_ref[at] = outer
            branch_ref[at] = branch
            gain_sum += jnp.sum(top_grad * unit, axis=0, keepdims=True)
            shift_sum += jnp.sum(top_grad, axis=0, keepdims=True)
            bias_sum += jnp.sum(branch.astype(F32), axis=0, keepdims=True)
        sums_ref[0:1] = gain_sum
        sums_ref[1:2] = shift_sum
        sums_ref[2:3] = bias_sum

    @pl.when(step > 0)
    def _():
        few, both, _ = keep_ref.shape
        deep = width // (2 * few)
        value = tn(act_ref[...], branch_ref[...])
        first = place_ref[2] == 0
        for chip in range(few):
            shard = 2 * ((step - 1) * few + chip)
            even = value[2 * chip * deep : (2 * chip + 1) * deep]
            odd = value[(2 * chip + 1) * deep : (2 * chip + 2) * deep]
            keep_ref[chip, 0:deep] = jnp.where(first, even, odd).astype(BF)
            send_ref[chip, 0:deep] = jnp.where(first, odd, even).astype(BF)
            keep_ref[chip, deep:both] = pool_grad_ref[shard + place_ref[2]]
            send_ref[chip, deep:both] = pool_grad_ref[shard + 1 - place_ref[2]]


def leave(
    place, exit_layer, output, unit2, scale2, output_grad, pool, vec, class_bias, logit_grad, act,
    pool_spec, shards, length, classes,
):
    rows, width = output.shape
    count = rows // length
    hidden = act.shape[1]
    steps = hidden // width
    few = shards // steps // 2
    both = (hidden + width) // shards
    whole = full((rows, width))
    return pl.pallas_call(
        functools.partial(leave_kernel, length, classes),
        grid=(steps + 1,),
        in_specs=[
            pl.BlockSpec(memory_space=pltpu.SMEM),
            pl.BlockSpec(memory_space=pltpu.SMEM),
            whole,
            whole,
            full((rows, 1)),
            whole,
            pool_spec,
            full(vec.shape),
            full(class_bias.shape),
            full(logit_grad.shape),
            pl.BlockSpec((rows, width), lambda i: (0, jnp.maximum(i - 1, 0))),
        ],
        out_specs=[
            whole,
            whole,
            pl.BlockSpec((few, both, width), lambda i: (jnp.maximum(i - 1, 0), 0, 0)),
            pl.BlockSpec((few, both, width), lambda i: (jnp.maximum(i - 1, 0), 0, 0)),
            full((4, width)),
            full((8, width)),
            full((count, 8)),
            full((2, 8)),
        ],
        out_shape=[
            jax.ShapeDtypeStruct((rows, width), F32),
            jax.ShapeDtypeStruct((rows, width), BF),
            jax.ShapeDtypeStruct((shards // 2, both, width), BF),
            jax.ShapeDtypeStruct((shards // 2, both, width), BF),
            jax.ShapeDtypeStruct((4, width), F32),
            jax.ShapeDtypeStruct((8, width), F32),
            jax.ShapeDtypeStruct((count, 8), F32),
            jax.ShapeDtypeStruct((2, 8), F32),
        ],
        scratch_shapes=[
            pltpu.VMEM((count, width), F32),
            pltpu.VMEM((shards, width // shards, width), BF),
        ],
        compiler_params=params(),
        cost_estimate=cost(8 * rows * width * width, 30 * rows * width),
        name="leave",
    )(
        place, exit_layer, output, unit2, scale2, output_grad, pool, vec, class_bias, logit_grad, act
    )


def feed_back_kernel(
    branch_ref,
    slope_ref,
    low_ref,
    down_ref,
    up_ref,
    outer_ref,
    unit1_ref,
    scale1_ref,
    out_w_ref,
    vec_ref,
    ctx_ref,
    grad_ref,
    up_sum_ref,
    inner_ref,
    attended_ref,
    ctx_grad_ref,
    sums_ref,
    acc_ref,
    hid_ref,
):
    step = pl.program_id(0)
    rows, width = branch_ref.shape
    sub = 256

    @pl.when(step == 0)
    def _():
        acc_ref[...] = outer_ref[...]

    last = pl.num_programs(0) - 1

    @pl.when(step < last)
    def _():
        total = jnp.zeros((1, width), F32)
        down = down_ref[...].reshape(up_ref.shape[1:])
        for m in range(rows // sub):
            at = slice(m * sub, (m + 1) * sub)
            hid = (nt(branch_ref[at], down) * slope_ref[at].astype(F32)).astype(BF)
            hid_ref[at] = hid
            total += jnp.sum(hid.astype(F32), axis=0, keepdims=True)
            acc_ref[at] += nt(hid, up_ref[0])
        up_sum_ref[...] = total
        grad_ref[...] = tn(low_ref[...], hid_ref[...]).astype(BF)

    @pl.when(step == last)
    def _():
        gain = vec_ref[ATTN_GAIN : ATTN_GAIN + 1]
        gain_sum = jnp.zeros((1, width), F32)
        shift_sum = jnp.zeros((1, width), F32)
        bias_sum = jnp.zeros((1, width), F32)
        for m in range(rows // sub):
            at = slice(m * sub, (m + 1) * sub)
            grad = acc_ref[at]
            unit = unit1_ref[at].astype(F32)
            inner = norm_back(grad, unit, scale1_ref[at], gain)
            attended = inner.astype(BF)
            inner_ref[at] = inner
            attended_ref[at] = attended
            ctx_grad_ref[at] = nt(attended, out_w_ref[0]).astype(BF)
            gain_sum += jnp.sum(grad * unit, axis=0, keepdims=True)
            shift_sum += jnp.sum(grad, axis=0, keepdims=True)
            bias_sum += jnp.sum(attended.astype(F32), axis=0, keepdims=True)
        sums_ref[0:1] = gain_sum
        sums_ref[1:2] = shift_sum
        sums_ref[2:3] = bias_sum
        grad_ref[...] = tn(ctx_ref[...], attended_ref[...]).astype(BF)


def feed_back(branch, slope, low, down, down_block, up, outer, unit1, scale1, out_w, vec, ctx):
    rows, width = branch.shape
    hidden = slope.shape[1]
    steps = hidden // width
    whole = full((rows, width))
    end = steps - 1
    return pl.pallas_call(
        feed_back_kernel,
        grid=(steps + 1,),
        in_specs=[
            whole,
            pl.BlockSpec((rows, width), lambda i: (0, jnp.minimum(i, end))),
            whole,
            pl.BlockSpec(down_block, lambda i: (jnp.minimum(i, end), 0, 0)),
            pl.BlockSpec((1, width, width), lambda i: (jnp.minimum(i, end), 0, 0)),
            whole,
            whole,
            full((rows, 1)),
            pl.BlockSpec((1, width, width), lambda i: (3, 0, 0)),
            full(vec.shape),
            whole,
        ],
        out_specs=[
            pl.BlockSpec((width, width), lambda i: (0, i)),
            pl.BlockSpec((1, width), lambda i: (0, jnp.minimum(i, end))),
            whole,
            whole,
            whole,
            full((3, width)),
        ],
        out_shape=[
            jax.ShapeDtypeStruct((width, hidden + width), BF),
            jax.ShapeDtypeStruct((1, hidden), F32),
            jax.ShapeDtypeStruct((rows, width), F32),
            jax.ShapeDtypeStruct((rows, width), BF),
            jax.ShapeDtypeStruct((rows, width), BF),
            jax.ShapeDtypeStruct((3, width), F32),
        ],
        scratch_shapes=[pltpu.VMEM((rows, width), F32), pltpu.VMEM((rows, width), BF)],
        compiler_params=params(),
        cost_estimate=cost(28 * rows * width * width, 40 * rows * width),
        name="feed_back",
    )(branch, slope, low, down, up, outer, unit1, scale1, out_w, vec, ctx)


def attend_back_kernel(length, joined_ref, probs_ref, ctx_grad_ref, grad_ref, sum_ref):
    rows, width = ctx_grad_ref.shape
    pairs = width // PAIR

    def one(seq, carry):
        at = pl.ds(pl.multiple_of(seq * length, length), length)
        for pair in range(pairs):
            at_q = slice(pair * PAIR, (pair + 1) * PAIR)
            at_k = slice(width + pair * PAIR, width + (pair + 1) * PAIR)
            at_v = slice(2 * width + pair * PAIR, 2 * width + (pair + 1) * PAIR)
            query = joined_ref[at, at_q] * jnp.asarray(0.125, BF)
            queries = split_heads(query)
            keys = split_heads(joined_ref[at, at_k])
            vals = split_heads(joined_ref[at, at_v])
            ctx_grad = ctx_grad_ref[at, at_q]
            ctx_grads = split_heads(ctx_grad)
            probs = probs_ref[seq, pair]
            prob_grad = nt(vals, ctx_grad)
            halves = []
            for head in range(2):
                cut = slice(head * length, (head + 1) * length)
                held = probs[cut].astype(F32)
                part = prob_grad[cut]
                base = jnp.sum(part * held, axis=0, keepdims=True)
                halves.append((held * (part - base)).astype(BF))
            stacked = jnp.concatenate(halves, axis=0)
            beside = jnp.concatenate(halves, axis=1)
            probs_beside = jnp.concatenate([probs[:length], probs[length:]], axis=1)
            grad_ref[at, at_q] = (tn(stacked, keys) * 0.125).astype(BF)
            grad_ref[at, at_k] = nn(beside, queries).astype(BF)
            grad_ref[at, at_v] = nn(probs_beside, ctx_grads).astype(BF)
        return carry

    lax.fori_loop(0, rows // length, one, 0)
    total = jnp.zeros(sum_ref.shape, F32)
    for m in range(rows // length):
        total += jnp.sum(
            grad_ref[m * length : (m + 1) * length].astype(F32), axis=0, keepdims=True
        )

    @pl.when(pl.program_id(0) == 0)
    def _():
        sum_ref[...] = total

    @pl.when(pl.program_id(0) > 0)
    def _():
        sum_ref[...] += total


def attend_back(joined, probs, ctx_grad, length):
    rows, width = ctx_grad.shape
    count = rows // length
    steps = 2
    block = rows // steps
    pairs = width // PAIR
    return pl.pallas_call(
        functools.partial(attend_back_kernel, length),
        grid=(steps,),
        in_specs=[
            pl.BlockSpec((block, 3 * width), lambda i: (i, 0)),
            pl.BlockSpec((count // steps, pairs, 2 * length, length), lambda i: (i, 0, 0, 0)),
            pl.BlockSpec((block, width), lambda i: (i, 0)),
        ],
        out_specs=[
            pl.BlockSpec((block, 3 * width), lambda i: (i, 0)),
            full((1, 3 * width)),
        ],
        out_shape=[
            jax.ShapeDtypeStruct((rows, 3 * width), BF),
            jax.ShapeDtypeStruct((1, 3 * width), F32),
        ],
        compiler_params=params(),
        cost_estimate=cost(8 * rows * width * width, 20 * rows * width),
        name="attend_back",
    )(joined, probs, ctx_grad)


def weight_grads_kernel(place_ref, tok_ref, joined_ref, small_ref, keep_ref, send_ref):
    chips, part, _ = keep_ref.shape
    step = pl.program_id(0)
    width = tok_ref.shape[1]
    first = place_ref[2] == 0
    value = tn(tok_ref[...], joined_ref[...])
    cols = pl.ds(pl.multiple_of(step * width, width), width)
    for chip in range(chips):
        even = value[2 * chip * part : (2 * chip + 1) * part]
        odd = value[(2 * chip + 1) * part : (2 * chip + 2) * part]
        keep_ref[chip, :, cols] = jnp.where(first, even, odd).astype(BF)
        send_ref[chip, :, cols] = jnp.where(first, odd, even).astype(BF)

    lines = small_ref.shape[1]
    if keep_ref.shape[2] > 3 * width:

        @pl.when(step == 0)
        def _():
            tail = slice(3 * width, keep_ref.shape[2])
            keep_ref[:, :, tail] = jnp.zeros((chips, part, keep_ref.shape[2] - 3 * width), BF)
            send_ref[:, :, tail] = jnp.zeros((chips, part, keep_ref.shape[2] - 3 * width), BF)
            for chip in range(chips):
                even, odd = small_ref[2 * chip], small_ref[2 * chip + 1]
                keep_ref[chip, 0:lines, tail] = jnp.where(first, even, odd).astype(BF)
                send_ref[chip, 0:lines, tail] = jnp.where(first, odd, even).astype(BF)


def weight_grads(place, tokens, joined_grad, small, chips, extra):
    rows, width = tokens.shape
    shape = (chips, width // (2 * chips), 3 * width + extra)
    return pl.pallas_call(
        weight_grads_kernel,
        grid=(3,),
        in_specs=[
            pl.BlockSpec(memory_space=pltpu.SMEM),
            full((rows, width)),
            pl.BlockSpec((rows, width), lambda i: (0, i)),
            full(small.shape),
        ],
        out_specs=[full(shape), full(shape)],
        out_shape=[jax.ShapeDtypeStruct(shape, BF)] * 2,
        compiler_params=params(),
        cost_estimate=cost(6 * rows * width * width, 20 * rows * width),
        name="weight_grads",
    )(place, tokens, joined_grad, small)


def input_kernel(inner_ref, joined_ref, w_ref, out_ref):
    width = inner_ref.shape[1]
    total = inner_ref[...]
    for part in range(3):
        total += nt(joined_ref[:, part * width : (part + 1) * width], w_ref[part])
    out_ref[...] = total.astype(BF)


def input_back(inner, joined_grad, qkv):
    rows, width = inner.shape
    steps = 4
    block = rows // steps
    return pl.pallas_call(
        input_kernel,
        grid=(steps,),
        in_specs=[
            pl.BlockSpec((block, width), lambda i: (i, 0)),
            pl.BlockSpec((block, 3 * width), lambda i: (i, 0)),
            full((3, width, width)),
        ],
        out_specs=pl.BlockSpec((block, width), lambda i: (i, 0)),
        out_shape=jax.ShapeDtypeStruct((rows, width), BF),
        compiler_params=params(),
        cost_estimate=cost(6 * rows * width * width, 12 * rows * width),
        name="input_back",
    )(inner, joined_grad, qkv)


def lay_kernel(plan, chips, reps, part, counts, place_ref, *refs):
    at = 0
    groups = []
    for number in counts:
        groups.append(refs[at : at + number])
        at += number
    sems = refs[-1]
    rep, chip, core = place_ref[0], place_ref[1], place_ref[2]
    copies = []

    def start(source, target):
        copies.append(pltpu.make_async_copy(source, target, sems.at[len(copies)]))
        copies[-1].start()

    plan(start, groups, refs[at:-1], rep, chip, core, chips, reps, part)
    for copy in copies:
        copy.wait()


def blocks_plan(put, own, twin, along, across, swapped, depth, first, rep, chip, core, chips, reps, part):
    for block in range(reps):
        put(own(block), block, chip, core)
        put(twin(block), block, chip, 1 - core)
    for step in range(1, chips):
        source = lax.rem(chip + chips - step, chips)
        rows = pl.ds((step - 1) * depth + first, part)
        put(along[step - 1].at[pl.ds(first, part)], rep, source, core)
        put(swapped[0].at[rows], rep, source, 1 - core)
        for other in range(1, reps):
            put(across[other - 1].at[rows], rep ^ other, source, core)
            put(swapped[other].at[rows], rep ^ other, source, 1 - core)


def wide_put(start, out_ref, part):
    def put(source, block, at_chip, at_core):
        row = pl.multiple_of((at_chip * 2 + at_core) * part, part)
        start(source, out_ref.at[block, pl.ds(row, part)])

    return put


def wide_block(ref, width, part):
    return lambda block: ref.at[pl.ds(0, part), pl.ds(block * width, width)]


def first_plan(start, groups, outs, rep, chip, core, chips, reps, part):
    owns, along, across, swapped, extra = groups
    own, twin = owns
    out_ref, more_ref = outs
    width = out_ref.shape[2]
    blocks_plan(
        wide_put(start, out_ref, part),
        wide_block(own, width, part),
        wide_block(twin, width, part),
        along,
        across,
        swapped,
        part,
        0,
        rep,
        chip,
        core,
        chips,
        reps,
        part,
    )
    tail = pl.ds(part, 16)
    cols = pl.ds(0, width)
    start(own.at[tail, cols], more_ref.at[chip * 2 + core])
    start(twin.at[tail, cols], more_ref.at[chip * 2 + 1 - core])
    for step in range(1, chips):
        source = lax.rem(chip + chips - step, chips)
        start(along[step - 1].at[tail], more_ref.at[source * 2 + core])
        start(extra[0].at[pl.ds((step - 1) * 16, 16)], more_ref.at[source * 2 + 1 - core])


def second_plan(start, groups, outs, rep, chip, core, chips, reps, part):
    owns, along, across, swapped = groups
    up, up_twin, down, down_twin = owns
    up_ref, down_ref = outs
    width = up_ref.shape[2]
    where = (rep, chip, core, chips, reps, part)
    blocks_plan(
        wide_put(start, up_ref, part),
        wide_block(up, width, part),
        wide_block(up_twin, width, part),
        along,
        across,
        swapped,
        2 * part,
        0,
        *where,
    )

    def put(source, block, at_chip, at_core):
        row = pl.multiple_of(block * part, part)
        start(source, down_ref.at[at_chip * 2 + at_core, pl.ds(row, part)])

    def tall(ref):
        return lambda block: ref.at[pl.ds(block * part, part)]

    blocks_plan(
        put, tall(down), tall(down_twin), along, across, swapped, 2 * part, part, *where
    )


def lay(plan, place, groups, shapes, copies, part, chips, reps):
    anywhere = pl.BlockSpec(memory_space=pl.ANY)
    inputs = [ref for group in groups for ref in group]
    return pl.pallas_call(
        functools.partial(
            lay_kernel, plan, chips, reps, part, [len(group) for group in groups]
        ),
        in_specs=[pl.BlockSpec(memory_space=pltpu.SMEM)] + [anywhere] * len(inputs),
        out_specs=[pl.BlockSpec(memory_space=pltpu.VMEM)] * len(shapes),
        out_shape=[jax.ShapeDtypeStruct(shape, BF) for shape in shapes],
        scratch_shapes=[pltpu.SemaphoreType.DMA((copies,))],
        compiler_params=pltpu.CompilerParams(vmem_limit_bytes=VMEM_BYTES),
        cost_estimate=cost(0, 4 * sum(math.prod(shape) for shape in shapes)),
        name="lay",
    )(place, *inputs)


LANES = 128


def pack_vectors(rows, up_bias, class_weight):
    part = rows[0].shape[0]
    lines = [row[None] for row in rows[:8]] + [class_weight.T] + [row[None] for row in rows[8:]]
    pieces = up_bias.shape[0] // part
    lines += [up_bias[None, at * part : (at + 1) * part] for at in range(pieces)]
    return jnp.concatenate(lines, axis=0)


def move(values, reps, chips, target):
    pairs = []
    for rep in range(reps):
        for chip in range(chips):
            for core in range(2):
                to_rep, to_chip, to_core = target(rep, chip, core)
                pairs.append(
                    (
                        (rep * chips + chip) * 2 + core,
                        (to_rep * chips + to_chip) * 2 + to_core,
                    )
                )
    return lax.ppermute(values, ("rep", "fsdp"), pairs)


def along_chips(step, chips):
    return lambda rep, chip, core: (rep, (chip + step) % chips, core)


def across_reps(other):
    return lambda rep, chip, core: (rep ^ other, chip, core)


def to_twin(rep, chip, core):
    return rep, chip, 1 - core


def after(values, *gates):
    return lax.optimization_barrier((values, *gates))[0]


def along_z(mine, reps, chips):
    return [move(mine, reps, chips, along_chips(step, chips)) for step in range(1, chips)]


def over_reps(stacked, reps, chips):
    return [move(stacked, reps, chips, across_reps(other)) for other in range(1, reps)]


def pick(parts, at):
    return lax.dynamic_index_in_dim(parts, at, axis=0, keepdims=False)


def in_order(rep, reps, own, others, axis):
    blocks = jnp.stack([own] + others)
    return jnp.concatenate([pick(blocks, rep ^ at) for at in range(reps)], axis=axis)


class Reduction:
    def __init__(self, place, keep, send, reps, chips):
        self.rep, self.chip = place[0], place[1]
        self.reps, self.chips = reps, chips
        self.shape = (chips, reps, keep.shape[1] // reps, keep.shape[2])
        self.keep = keep.reshape(self.shape)
        self.got = move(send, reps, chips, to_twin)

    def at_rep(self, at):
        kept = lax.dynamic_index_in_dim(self.keep, at, axis=1, keepdims=False)
        came = lax.dynamic_index_in_dim(
            self.got.reshape(self.shape), at, axis=1, keepdims=False
        )
        return kept.astype(F32) + came.astype(F32)

    def over_reps(self, *gates):
        if gates:
            self.got = after(self.got, *gates)
        self.arrived = [
            move(
                self.at_rep(self.rep ^ other).astype(BF),
                self.reps,
                self.chips,
                across_reps(other),
            )
            for other in range(1, self.reps)
        ]

    def over_chips(self, *gates):
        if gates:
            self.arrived = [after(block, *gates) for block in self.arrived]
        mine = self.at_rep(self.rep)

        def both_at(at):
            total = pick(mine, at)
            for block in self.arrived:
                total = total + pick(block, at).astype(F32)
            return total

        self.total = both_at(self.chip)
        self.passed = [
            move(
                both_at(lax.rem(self.chip + step, self.chips)).astype(BF),
                self.reps,
                self.chips,
                along_chips(step, self.chips),
            )
            for step in range(1, self.chips)
        ]

    def share(self, *gates):
        if gates:
            self.passed = [after(block, *gates) for block in self.passed]
        total = self.total
        for block in self.passed:
            total = total + block.astype(F32)
        self.total = total.astype(BF)
        self.others = [
            move(self.total, self.reps, self.chips, across_reps(other))
            for other in range(1, self.reps)
        ]

    def result(self):
        return in_order(self.rep, self.reps, self.total, self.others, 0).astype(F32)


def sum_over_reps(place, rows, reps, chips):
    rep = place[0]
    parts = rows.reshape(reps, -1, rows.shape[1])
    total = pick(parts, rep).astype(F32)
    for other in range(1, reps):
        there = pick(parts, rep ^ other)
        total = total + move(there, reps, chips, across_reps(other)).astype(F32)
    total = total.astype(BF)
    others = [move(total, reps, chips, across_reps(other)) for other in range(1, reps)]
    return in_order(rep, reps, total, others, 0)


def per_device(
    tokens,
    exit_layer,
    qkv_weight,
    query_bias,
    value_bias,
    out_weight,
    out_bias,
    attn_gain,
    attn_shift,
    up_weight,
    up_bias,
    down_weight,
    down_bias,
    block_gain,
    block_shift,
    pool_weight,
    pool_bias,
    class_weight,
    class_bias,
    output_grad,
    logit_grad,
):
    reps = lax.axis_size("rep")
    shards = lax.axis_size("fsdp")
    mine = lax.axis_index("fsdp")
    rows, width = tokens.shape
    count = exit_layer.shape[0]
    length = rows // count
    classes = class_weight.shape[1]
    part = out_weight.shape[0]
    hidden = up_weight.shape[1]

    def gather(shard):
        return lax.all_gather(shard, "fsdp", axis=0, tiled=True)

    packed = pack_vectors(
        [
            query_bias,
            value_bias,
            out_bias,
            attn_gain,
            attn_shift,
            down_bias,
            block_gain,
            block_shift,
            pool_bias,
        ],
        up_bias,
        class_weight,
    )
    joint_own = jnp.concatenate([qkv_weight, out_weight], axis=1)
    deep = down_weight.shape[0]
    pool = gather(pool_weight)
    chips = shards // 2
    place = jnp.stack([lax.axis_index("rep"), mine // 2, mine % 2]).astype(jnp.int32)
    direct = (
        part % 16 == 0
        and reps & (reps - 1) == 0
        and reps * width == hidden
        and packed.shape[0] <= 16
    )
    if direct:
        lines = packed.shape[0]
        held = jnp.pad(packed, ((0, 16 - lines), (0, width - part)))
        own = jnp.concatenate([joint_own, jnp.tile(held, (1, reps))], axis=0)
        rep = place[0]
        along = along_z(
            lax.dynamic_slice_in_dim(own, rep * width, width, axis=1), reps, chips
        )
        twin = move(own, reps, chips, to_twin)
        stacked = jnp.concatenate([rows_[:part] for rows_ in along], axis=0)
        across = over_reps(stacked, reps, chips)
        swapped = [move(rows_, reps, chips, to_twin) for rows_ in [stacked] + across]
        extra = move(
            jnp.concatenate([rows_[part:] for rows_ in along], axis=0), reps, chips, to_twin
        )
        second = jnp.concatenate(
            [
                lax.dynamic_slice_in_dim(up_weight, rep * width, width, axis=1),
                lax.dynamic_slice_in_dim(down_weight, rep * part, part, axis=0),
            ],
            axis=0,
        )
        second_along = along_z(after(second, *along), reps, chips)
        up_twin = move(up_weight, reps, chips, to_twin)
        down_twin = move(down_weight, reps, chips, to_twin)
        second_stacked = jnp.concatenate(second_along, axis=0)
        second_across = over_reps(after(second_stacked, *across), reps, chips)
        joint, small = lay(
            first_plan,
            place,
            [[own, twin], along, across, swapped, [extra]],
            [(reps, width, width), (shards, 16, width)],
            2 * chips * (reps + 1),
            part,
            chips,
            reps,
        )
        small = small[:, :lines, :part]
        down_block = (width // deep, deep, width)
    else:
        small = gather(packed[None])
        joint = jnp.stack(jnp.split(gather(joint_own), 4, axis=1))
        up = jnp.stack(jnp.split(gather(up_weight), hidden // width, axis=1))
        down = gather(down_weight).reshape(-1, width, width)
        down_block = (1, width, width)
    vec = small[:, :VECTOR_ROWS].transpose(1, 0, 2).reshape(VECTOR_ROWS, width).astype(F32)
    vec = jnp.pad(vec, ((0, 16 - VECTOR_ROWS), (0, 0)))
    up_row = small[:, VECTOR_ROWS:].reshape(1, hidden).astype(F32)
    bias_row = jnp.concatenate([vec[:1], jnp.zeros((1, width), F32), vec[1:2]], axis=1)

    joined, probs, ctx = attend(tokens, joint, bias_row, length)
    if direct:
        second_swapped = [
            move(after(rows_, ctx), reps, chips, to_twin)
            for rows_ in [second_stacked] + second_across
        ]
        up, down = lay(
            second_plan,
            place,
            [
                [up_weight, up_twin, down_weight, down_twin],
                second_along,
                second_across,
                second_swapped,
            ],
            [(reps, width, width), (shards, deep, width)],
            4 * chips * reps,
            part,
            chips,
            reps,
        )
    low, act, slope, unit1, scale1, unit2, scale2, output = feed(
        exit_layer, tokens, ctx, joint, vec, up, up_row, down, down_block, length
    )
    class_bias_row = jnp.pad(class_bias.astype(F32), (0, 8 - classes))[None]
    logit_grad_rows = jnp.pad(logit_grad, ((0, 0), (0, 8 - classes)))
    outer, branch, low_keep, low_send, exit_sums, class_grad, logits, stats = leave(
        place,
        exit_layer,
        output,
        unit2,
        scale2,
        output_grad,
        pool,
        vec,
        class_bias_row,
        logit_grad_rows,
        act,
        full((width, width)),
        shards,
        length,
        classes,
    )
    if direct:
        low_red = Reduction(place, low_keep, low_send, reps, chips)
    up_grad, up_sum, inner, attended, ctx_grad, feed_sums = feed_back(
        branch, slope, low, down, down_block, up, outer, unit1, scale1, joint, vec, ctx
    )
    if direct:
        low_red.over_reps(attended)
        ctx_grad = after(ctx_grad, low_red.got)
    joined_grad, joined_sum = attend_back(joined, probs, ctx_grad, length)
    joined_seen = joined_grad
    if direct:
        low_red.over_chips(joined_grad)
        joined_seen = after(joined_grad, *low_red.arrived)
    sums = jnp.concatenate(
        [
            joined_sum.reshape(3, width)[::2],
            feed_sums,
            exit_sums,
            class_grad[:classes],
        ],
        axis=0,
    )
    lines = sums.shape[0]
    own_sums = sums.reshape(lines, shards, part).transpose(1, 0, 2).reshape(shards, lines * part)
    own_sums = jnp.concatenate([own_sums, up_sum.reshape(shards, deep)], axis=1)
    used = own_sums.shape[1]
    seqs_total = count * reps * shards
    figures = jnp.concatenate([stats[0, :1], stats[1, :classes]])
    slots = reps * shards * figures.shape[0] * 3
    direct = direct and used + slots <= part * LANES
    small_lines = 16
    if direct:
        high = figures.astype(BF).astype(F32)
        middle = (figures - high).astype(BF).astype(F32)
        lowest = figures - high - middle
        split = jnp.concatenate([high, middle, lowest])
        slot = lax.axis_index("rep") * shards + mine
        lone = jnp.where(
            jnp.arange(reps * shards)[:, None] == slot, split[None], 0.0
        ).reshape(1, slots)
        row = jnp.concatenate([own_sums, jnp.broadcast_to(lone, (shards, slots))], axis=1)
        small_lines = -(-row.shape[1] // (LANES * 16)) * 16
        row = jnp.pad(row, ((0, 0), (0, small_lines * LANES - row.shape[1])))
        row = row.reshape(shards, small_lines, LANES)
    else:
        row = jnp.zeros((shards, small_lines, LANES), F32)
    keep, send = weight_grads(
        place, tokens, joined_seen, row, chips, LANES if direct else 0
    )
    input_grad = input_back(inner, joined_grad, joint)

    def scatter(grad):
        return lax.psum_scatter(grad, "fsdp", scatter_dimension=0, tiled=True)

    up_part = scatter(up_grad)
    if direct:
        low_red.share(keep)
        joint_red = Reduction(place, keep, send, reps, chips)
        joint_red.over_reps(*low_red.passed)
        joint_red.over_chips(*low_red.others)
        joint_red.share(up_part)
        up_sum = sum_over_reps(place, up_part, reps, chips).astype(F32)
        low_sum = low_red.result()
        joint_sum = joint_red.result()
        small_sum = joint_sum[:small_lines, 3 * width :].reshape(-1)
        total = small_sum[used : used + slots].reshape(-1, figures.shape[0]).sum(axis=0)
    else:
        first = mine % 2 == 0

        def whole_of(kept, sent):
            pair = jnp.stack([jnp.where(first, kept, sent), jnp.where(first, sent, kept)], axis=1)
            return pair.reshape(-1, kept.shape[2])

        joint_sum, low_sum, up_sum = lax.psum(
            (
                scatter(whole_of(keep, send)),
                scatter(whole_of(low_keep, low_send)),
                up_part,
            ),
            "rep",
        )
        joint_sum, low_sum, up_sum = (
            joint_sum.astype(F32),
            low_sum.astype(F32),
            up_sum.astype(F32),
        )
        own_sums, total = lax.psum((own_sums, figures), ("rep", "fsdp"))
        small_sum = pick(own_sums, mine)
    own = small_sum[: lines * part].reshape(lines, part)
    return (
        output,
        logits[:, :classes],
        total[0] / seqs_total,
        input_grad,
        joint_sum[:, : 3 * width],
        own[0],
        own[1],
        up_sum[:, hidden:],
        own[4],
        own[2],
        own[3],
        up_sum[:, :hidden],
        small_sum[lines * part : used],
        low_sum[:deep],
        own[7],
        own[5],
        own[6],
        low_sum[deep:],
        own[8],
        own[9 : 9 + classes].T,
        total[1:],
    )


def solution(mesh):
    return jax.shard_map(
        per_device,
        mesh=mesh,
        in_specs=(
            P(("rep", "fsdp"), None),
            P(("rep", "fsdp")),
            P("fsdp", None),
            P("fsdp"),
            P("fsdp"),
            P("fsdp", None),
            P("fsdp"),
            P("fsdp"),
            P("fsdp"),
            P("fsdp", None),
            P("fsdp"),
            P("fsdp", None),
            P("fsdp"),
            P("fsdp"),
            P("fsdp"),
            P("fsdp", None),
            P("fsdp"),
            P("fsdp", None),
            P(),
            P(("rep", "fsdp"), None),
            P(("rep", "fsdp"), None),
        ),
        out_specs=(
            P(("rep", "fsdp"), None),
            P(("rep", "fsdp"), None),
            P(),
            P(("rep", "fsdp"), None),
            P("fsdp", None),
            P("fsdp"),
            P("fsdp"),
            P("fsdp", None),
            P("fsdp"),
            P("fsdp"),
            P("fsdp"),
            P("fsdp", None),
            P("fsdp"),
            P("fsdp", None),
            P("fsdp"),
            P("fsdp"),
            P("fsdp"),
            P("fsdp", None),
            P("fsdp"),
            P("fsdp", None),
            P(),
        ),
        check_vma=False,
    )
```

```python
import functools
import math

import jax
import jax.numpy as jnp
from jax import lax
from jax.experimental import pallas as pl
from jax.experimental.pallas import tpu as pltpu
from jax.sharding import PartitionSpec as P

HD = 64
LAYER = 6
PAIR = 2 * HD
NEAR = (1, 2)
FAR = 3
VMEM_BYTES = 58 * 2**20
BF = jnp.bfloat16
F32 = jnp.float32

QUERY_BIAS, VALUE_BIAS, OUT_BIAS, ATTN_GAIN, ATTN_SHIFT = 0, 1, 2, 3, 4
DOWN_BIAS, BLOCK_GAIN, BLOCK_SHIFT, CLASS_ROWS, POOL_BIAS = 5, 6, 7, 8, 11
VECTOR_ROWS = 12


def nn(left, right):
    return jnp.dot(left, right, preferred_element_type=F32)


def tn(left, right):
    return lax.dot_general(left, right, (((0,), (0,)), ((), ())), preferred_element_type=F32)


def nt(left, right):
    return lax.dot_general(left, right, (((1,), (1,)), ((), ())), preferred_element_type=F32)


def full(shape):
    return pl.BlockSpec(shape, lambda *at: (0,) * len(shape))


def params():
    return pltpu.CompilerParams(
        dimension_semantics=("arbitrary",), vmem_limit_bytes=VMEM_BYTES
    )


def cost(flops, moved, trans=0):
    return pl.CostEstimate(flops=flops, bytes_accessed=moved, transcendentals=trans)


def split_heads(pair):
    lane = lax.broadcasted_iota(jnp.int32, pair.shape, 1)
    zero = jnp.zeros_like(pair)
    return jnp.concatenate(
        [jnp.where(lane < HD, pair, zero), jnp.where(lane < HD, zero, pair)], axis=0
    )


def norm_stats(values):
    center = values - jnp.mean(values, axis=-1, keepdims=True)
    spread = jnp.mean(center * center, axis=-1, keepdims=True)
    scale = lax.rsqrt(spread + 1e-06)
    return center * scale, scale


def norm_back(grad, unit, scale, gain):
    inner = grad * gain
    first = jnp.mean(inner, axis=-1, keepdims=True)
    second = jnp.mean(inner * unit, axis=-1, keepdims=True)
    return scale * (inner - first - unit * second)


def gelu_parts(values):
    size = jnp.abs(values)
    t = 1.0 / (1.0 + 0.23164189 * size)
    bell = jnp.exp(-0.5 * values * values)
    poly = t * (
        0.127414796
        + t * (-0.142248368 + t * (0.7107068705 + t * (-0.7265760135 + t * 0.5307027145)))
    )
    tail = poly * bell
    below = jnp.where(values >= 0.0, 1.0 - tail, tail)
    return values * below, below + values * (bell * 0.3989422804014327)


def attend_kernel(length, tok_ref, w_ref, bias_ref, joined_ref, probs_ref, ctx_ref):
    rows, width = ctx_ref.shape
    pairs = width // PAIR
    for part in range(3):
        cols = slice(part * width, (part + 1) * width)
        joined_ref[:, cols] = (nn(tok_ref[...], w_ref[part]) + bias_ref[:, cols]).astype(BF)

    def one(seq, carry):
        at = pl.ds(pl.multiple_of(seq * length, length), length)
        for pair in range(pairs):
            cols = slice(pair * PAIR, (pair + 1) * PAIR)
            query = joined_ref[at, cols] * jnp.asarray(0.125, BF)
            keys = split_heads(joined_ref[at, width + pair * PAIR : width + (pair + 1) * PAIR])
            vals = split_heads(
                joined_ref[at, 2 * width + pair * PAIR : 2 * width + (pair + 1) * PAIR]
            )
            scores = nt(keys, query)
            halves = []
            for head in range(2):
                part = scores[head * length : (head + 1) * length]
                part = jnp.exp(part - jnp.max(part, axis=0, keepdims=True))
                part = part * (1.0 / jnp.sum(part, axis=0, keepdims=True))
                halves.append(part.astype(BF))
            probs = jnp.concatenate(halves, axis=0)
            probs_ref[seq, pair] = probs
            ctx_ref[at, cols] = tn(probs, vals).astype(BF)
        return carry

    lax.fori_loop(0, rows // length, one, 0)


def attend(tokens, qkv, bias_row, length):
    rows, width = tokens.shape
    count = rows // length
    steps = 2
    block = rows // steps
    pairs = width // PAIR
    return pl.pallas_call(
        functools.partial(attend_kernel, length),
        grid=(steps,),
        in_specs=[
            pl.BlockSpec((block, width), lambda i: (i, 0)),
            full((3, width, width)),
            full(bias_row.shape),
        ],
        out_specs=[
            pl.BlockSpec((block, 3 * width), lambda i: (i, 0)),
            pl.BlockSpec((count // steps, pairs, 2 * length, length), lambda i: (i, 0, 0, 0)),
            pl.BlockSpec((block, width), lambda i: (i, 0)),
        ],
        out_shape=[
            jax.ShapeDtypeStruct((rows, 3 * width), BF),
            jax.ShapeDtypeStruct((count, pairs, 2 * length, length), BF),
            jax.ShapeDtypeStruct((rows, width), BF),
        ],
        compiler_params=params(),
        cost_estimate=cost(8 * rows * width * width, 20 * rows * width, rows * width),
        name="attend",
    )(tokens, qkv, bias_row)


def feed_kernel(
    length,
    exit_ref,
    tok_ref,
    ctx_ref,
    out_w_ref,
    vec_ref,
    up_ref,
    up_b_ref,
    down_ref,
    low_ref,
    act_ref,
    slope_ref,
    unit1_ref,
    scale1_ref,
    unit2_ref,
    scale2_ref,
    output_ref,
    acc_ref,
):
    step = pl.program_id(0)
    rows = tok_ref.shape[0]
    sub = 256

    @pl.when(step == 0)
    def _():
        for m in range(rows // sub):
            at = slice(m * sub, (m + 1) * sub)
            inner = tok_ref[at].astype(F32) + (
                nn(ctx_ref[at], out_w_ref[0]) + vec_ref[OUT_BIAS : OUT_BIAS + 1]
            )
            unit, scale = norm_stats(inner)
            first = unit * vec_ref[ATTN_GAIN : ATTN_GAIN + 1] + vec_ref[ATTN_SHIFT : ATTN_SHIFT + 1]
            unit1_ref[at] = unit.astype(BF)
            scale1_ref[at] = scale
            low_ref[at] = first.astype(BF)
            acc_ref[at] = first + vec_ref[DOWN_BIAS : DOWN_BIAS + 1]

    down = down_ref[...].reshape(up_ref.shape[1:])
    for m in range(rows // sub):
        at = slice(m * sub, (m + 1) * sub)
        hidden = nn(low_ref[at], up_ref[0]) + up_b_ref[...]
        act, slope = gelu_parts(hidden)
        act = act.astype(BF)
        act_ref[at] = act
        slope_ref[at] = slope.astype(BF)
        acc_ref[at] += nn(act, down)

    @pl.when(step == pl.num_programs(0) - 1)
    def _():
        for seq in range(rows // length):
            at = slice(seq * length, (seq + 1) * length)
            active = (exit_ref[seq] >= LAYER).astype(F32)
            unit, scale = norm_stats(acc_ref[at])
            unit2_ref[at] = unit.astype(BF)
            scale2_ref[at] = scale
            result = (
                unit * vec_ref[BLOCK_GAIN : BLOCK_GAIN + 1] + vec_ref[BLOCK_SHIFT : BLOCK_SHIFT + 1]
            ) * active
            output_ref[at] = result.astype(BF)


def feed(exit_layer, tokens, ctx, out_w, vec, up, up_bias, down, down_block, length):
    rows, width = tokens.shape
    steps = up.shape[0]
    hidden = steps * width
    whole = full((rows, width))
    return pl.pallas_call(
        functools.partial(feed_kernel, length),
        grid=(steps,),
        in_specs=[
            pl.BlockSpec(memory_space=pltpu.SMEM),
            whole,
            whole,
            pl.BlockSpec((1, width, width), lambda i: (3, 0, 0)),
            full(vec.shape),
            pl.BlockSpec((1, width, width), lambda i: (i, 0, 0)),
            pl.BlockSpec((1, width), lambda i: (0, i)),
            pl.BlockSpec(down_block, lambda i: (i, 0, 0)),
        ],
        out_specs=[
            whole,
            pl.BlockSpec((rows, width), lambda i: (0, i)),
            pl.BlockSpec((rows, width), lambda i: (0, i)),
            whole,
            full((rows, 1)),
            whole,
            full((rows, 1)),
            whole,
        ],
        out_shape=[
            jax.ShapeDtypeStruct((rows, width), BF),
            jax.ShapeDtypeStruct((rows, hidden), BF),
            jax.ShapeDtypeStruct((rows, hidden), BF),
            jax.ShapeDtypeStruct((rows, width), BF),
            jax.ShapeDtypeStruct((rows, 1), F32),
            jax.ShapeDtypeStruct((rows, width), BF),
            jax.ShapeDtypeStruct((rows, 1), F32),
            jax.ShapeDtypeStruct((rows, width), BF),
        ],
        scratch_shapes=[pltpu.VMEM((rows, width), F32)],
        compiler_params=params(),
        cost_estimate=cost(18 * rows * width * width, 40 * rows * width, 8 * rows * width),
        name="feed",
    )(exit_layer, tokens, ctx, out_w, vec, up, up_bias, down)


def leave_kernel(
    length,
    classes,
    place_ref,
    exit_ref,
    output_ref,
    unit2_ref,
    scale2_ref,
    grad_ref,
    pool_ref,
    vec_ref,
    class_bias_ref,
    logit_grad_ref,
    act_ref,
    outer_ref,
    branch_ref,
    keep_ref,
    send_ref,
    sums_ref,
    class_grad_ref,
    logits_ref,
    stats_ref,
    lead_ref,
    pool_grad_ref,
):
    step = pl.program_id(0)
    rows, width = output_ref.shape
    pool = pool_ref[...].reshape(width, width)
    count = rows // length

    @pl.when(step == 0)
    def _():
        place = lax.broadcasted_iota(jnp.int32, (count, 1), 0)
        active = jnp.zeros((count, 1), F32)
        for seq in range(count):
            on = (exit_ref[seq] >= LAYER).astype(F32)
            active = jnp.where(place == seq, on, active)
        leading = jnp.concatenate(
            [output_ref[seq * length : seq * length + 1].astype(F32) for seq in range(count)],
            axis=0,
        ).astype(BF)
        pooled = jnp.tanh(nn(leading, pool) + vec_ref[POOL_BIAS : POOL_BIAS + 1])
        pooled_low = pooled.astype(BF)
        used = lax.broadcasted_iota(jnp.int32, (8, width), 0) < classes
        class_rows = jnp.where(used, vec_ref[CLASS_ROWS : CLASS_ROWS + 8], 0.0).astype(BF)
        raw = nt(pooled_low, class_rows) + class_bias_ref[...]
        lane = lax.broadcasted_iota(jnp.int32, raw.shape, 1) < classes
        top = jnp.max(jnp.where(lane, raw, -jnp.inf), axis=-1, keepdims=True)
        spread = jnp.where(lane, jnp.exp(raw - top), 0.0)
        logprob = raw - top - jnp.log(jnp.sum(spread, axis=-1, keepdims=True))
        entropy = -jnp.sum(
            jnp.where(lane, jnp.exp(logprob) * logprob, 0.0), axis=-1, keepdims=True
        )
        logits_ref[...] = raw * active
        class_grad = (logit_grad_ref[...].astype(F32) * active).astype(BF)
        stats_ref[0:1] = jnp.broadcast_to(jnp.sum(entropy * active, axis=0, keepdims=True), (1, 8))
        stats_ref[1:2] = jnp.sum(class_grad.astype(F32), axis=0, keepdims=True)
        class_grad_ref[...] = tn(class_grad, pooled_low)
        pooled_grad = nn(class_grad, class_rows)
        pre_grad = (pooled_grad * (1.0 - pooled * pooled)).astype(BF)
        sums_ref[3:4] = jnp.sum(pre_grad.astype(F32), axis=0, keepdims=True)
        pool_grad_ref[...] = tn(leading, pre_grad).reshape(pool_grad_ref.shape).astype(BF)
        lead_ref[...] = nt(pre_grad, pool)
        head = lax.broadcasted_iota(jnp.int32, (length, 1), 0) == 0
        gain = vec_ref[BLOCK_GAIN : BLOCK_GAIN + 1]
        gain_sum = jnp.zeros((1, width), F32)
        shift_sum = jnp.zeros((1, width), F32)
        bias_sum = jnp.zeros((1, width), F32)
        for seq in range(count):
            at = slice(seq * length, (seq + 1) * length)
            on = (exit_ref[seq] >= LAYER).astype(F32)
            top_grad = (
                grad_ref[at].astype(F32) + jnp.where(head, lead_ref[seq : seq + 1], 0.0)
            ) * on
            unit = unit2_ref[at].astype(F32)
            outer = norm_back(top_grad, unit, scale2_ref[at], gain)
            branch = outer.astype(BF)
            outer_ref[at] = outer
            branch_ref[at] = branch
            gain_sum += jnp.sum(top_grad * unit, axis=0, keepdims=True)
            shift_sum += jnp.sum(top_grad, axis=0, keepdims=True)
            bias_sum += jnp.sum(branch.astype(F32), axis=0, keepdims=True)
        sums_ref[0:1] = gain_sum
        sums_ref[1:2] = shift_sum
        sums_ref[2:3] = bias_sum

    @pl.when(step > 0)
    def _():
        few, both, _ = keep_ref.shape
        deep = width // (2 * few)
        value = tn(act_ref[...], branch_ref[...])
        first = place_ref[2] == 0
        for chip in range(few):
            shard = 2 * ((step - 1) * few + chip)
            even = value[2 * chip * deep : (2 * chip + 1) * deep]
            odd = value[(2 * chip + 1) * deep : (2 * chip + 2) * deep]
            keep_ref[chip, 0:deep] = jnp.where(first, even, odd).astype(BF)
            send_ref[chip, 0:deep] = jnp.where(first, odd, even).astype(BF)
            keep_ref[chip, deep:both] = pool_grad_ref[shard + place_ref[2]]
            send_ref[chip, deep:both] = pool_grad_ref[shard + 1 - place_ref[2]]


def leave(
    place, exit_layer, output, unit2, scale2, output_grad, pool, vec, class_bias, logit_grad, act,
    pool_spec, shards, length, classes,
):
    rows, width = output.shape
    count = rows // length
    hidden = act.shape[1]
    steps = hidden // width
    few = shards // steps // 2
    both = (hidden + width) // shards
    whole = full((rows, width))
    return pl.pallas_call(
        functools.partial(leave_kernel, length, classes),
        grid=(steps + 1,),
        in_specs=[
            pl.BlockSpec(memory_space=pltpu.SMEM),
            pl.BlockSpec(memory_space=pltpu.SMEM),
            whole,
            whole,
            full((rows, 1)),
            whole,
            pool_spec,
            full(vec.shape),
            full(class_bias.shape),
            full(logit_grad.shape),
            pl.BlockSpec((rows, width), lambda i: (0, jnp.maximum(i - 1, 0))),
        ],
        out_specs=[
            whole,
            whole,
            pl.BlockSpec((few, both, width), lambda i: (jnp.maximum(i - 1, 0), 0, 0)),
            pl.BlockSpec((few, both, width), lambda i: (jnp.maximum(i - 1, 0), 0, 0)),
            full((4, width)),
            full((8, width)),
            full((count, 8)),
            full((2, 8)),
        ],
        out_shape=[
            jax.ShapeDtypeStruct((rows, width), F32),
            jax.ShapeDtypeStruct((rows, width), BF),
            jax.ShapeDtypeStruct((shards // 2, both, width), BF),
            jax.ShapeDtypeStruct((shards // 2, both, width), BF),
            jax.ShapeDtypeStruct((4, width), F32),
            jax.ShapeDtypeStruct((8, width), F32),
            jax.ShapeDtypeStruct((count, 8), F32),
            jax.ShapeDtypeStruct((2, 8), F32),
        ],
        scratch_shapes=[
            pltpu.VMEM((count, width), F32),
            pltpu.VMEM((shards, width // shards, width), BF),
        ],
        compiler_params=params(),
        cost_estimate=cost(8 * rows * width * width, 30 * rows * width),
        name="leave",
    )(
        place, exit_layer, output, unit2, scale2, output_grad, pool, vec, class_bias, logit_grad, act
    )


def feed_back_kernel(
    branch_ref,
    slope_ref,
    low_ref,
    down_ref,
    up_ref,
    outer_ref,
    unit1_ref,
    scale1_ref,
    out_w_ref,
    vec_ref,
    ctx_ref,
    grad_ref,
    up_sum_ref,
    inner_ref,
    attended_ref,
    ctx_grad_ref,
    sums_ref,
    acc_ref,
    hid_ref,
):
    step = pl.program_id(0)
    rows, width = branch_ref.shape
    sub = 256

    @pl.when(step == 0)
    def _():
        acc_ref[...] = outer_ref[...]

    last = pl.num_programs(0) - 1

    @pl.when(step < last)
    def _():
        total = jnp.zeros((1, width), F32)
        down = down_ref[...].reshape(up_ref.shape[1:])
        for m in range(rows // sub):
            at = slice(m * sub, (m + 1) * sub)
            hid = (nt(branch_ref[at], down) * slope_ref[at].astype(F32)).astype(BF)
            hid_ref[at] = hid
            total += jnp.sum(hid.astype(F32), axis=0, keepdims=True)
            acc_ref[at] += nt(hid, up_ref[0])
        up_sum_ref[...] = total
        grad_ref[...] = tn(low_ref[...], hid_ref[...]).astype(BF)

    @pl.when(step == last)
    def _():
        gain = vec_ref[ATTN_GAIN : ATTN_GAIN + 1]
        gain_sum = jnp.zeros((1, width), F32)
        shift_sum = jnp.zeros((1, width), F32)
        bias_sum = jnp.zeros((1, width), F32)
        for m in range(rows // sub):
            at = slice(m * sub, (m + 1) * sub)
            grad = acc_ref[at]
            unit = unit1_ref[at].astype(F32)
            inner = norm_back(grad, unit, scale1_ref[at], gain)
            attended = inner.astype(BF)
            inner_ref[at] = inner
            attended_ref[at] = attended
            ctx_grad_ref[at] = nt(attended, out_w_ref[0]).astype(BF)
            gain_sum += jnp.sum(grad * unit, axis=0, keepdims=True)
            shift_sum += jnp.sum(grad, axis=0, keepdims=True)
            bias_sum += jnp.sum(attended.astype(F32), axis=0, keepdims=True)
        sums_ref[0:1] = gain_sum
        sums_ref[1:2] = shift_sum
        sums_ref[2:3] = bias_sum
        grad_ref[...] = tn(ctx_ref[...], attended_ref[...]).astype(BF)


def feed_back(branch, slope, low, down, down_block, up, outer, unit1, scale1, out_w, vec, ctx):
    rows, width = branch.shape
    hidden = slope.shape[1]
    steps = hidden // width
    whole = full((rows, width))
    end = steps - 1
    return pl.pallas_call(
        feed_back_kernel,
        grid=(steps + 1,),
        in_specs=[
            whole,
            pl.BlockSpec((rows, width), lambda i: (0, jnp.minimum(i, end))),
            whole,
            pl.BlockSpec(down_block, lambda i: (jnp.minimum(i, end), 0, 0)),
            pl.BlockSpec((1, width, width), lambda i: (jnp.minimum(i, end), 0, 0)),
            whole,
            whole,
            full((rows, 1)),
            pl.BlockSpec((1, width, width), lambda i: (3, 0, 0)),
            full(vec.shape),
            whole,
        ],
        out_specs=[
            pl.BlockSpec((width, width), lambda i: (0, i)),
            pl.BlockSpec((1, width), lambda i: (0, jnp.minimum(i, end))),
            whole,
            whole,
            whole,
            full((3, width)),
        ],
        out_shape=[
            jax.ShapeDtypeStruct((width, hidden + width), BF),
            jax.ShapeDtypeStruct((1, hidden), F32),
            jax.ShapeDtypeStruct((rows, width), F32),
            jax.ShapeDtypeStruct((rows, width), BF),
            jax.ShapeDtypeStruct((rows, width), BF),
            jax.ShapeDtypeStruct((3, width), F32),
        ],
        scratch_shapes=[pltpu.VMEM((rows, width), F32), pltpu.VMEM((rows, width), BF)],
        compiler_params=params(),
        cost_estimate=cost(28 * rows * width * width, 40 * rows * width),
        name="feed_back",
    )(branch, slope, low, down, up, outer, unit1, scale1, out_w, vec, ctx)


def attend_back_kernel(length, joined_ref, probs_ref, ctx_grad_ref, grad_ref, sum_ref):
    rows, width = ctx_grad_ref.shape
    pairs = width // PAIR

    def one(seq, carry):
        at = pl.ds(pl.multiple_of(seq * length, length), length)
        for pair in range(pairs):
            at_q = slice(pair * PAIR, (pair + 1) * PAIR)
            at_k = slice(width + pair * PAIR, width + (pair + 1) * PAIR)
            at_v = slice(2 * width + pair * PAIR, 2 * width + (pair + 1) * PAIR)
            query = joined_ref[at, at_q] * jnp.asarray(0.125, BF)
            queries = split_heads(query)
            keys = split_heads(joined_ref[at, at_k])
            vals = split_heads(joined_ref[at, at_v])
            ctx_grad = ctx_grad_ref[at, at_q]
            ctx_grads = split_heads(ctx_grad)
            probs = probs_ref[seq, pair]
            prob_grad = nt(vals, ctx_grad)
            halves = []
            for head in range(2):
                cut = slice(head * length, (head + 1) * length)
                held = probs[cut].astype(F32)
                part = prob_grad[cut]
                base = jnp.sum(part * held, axis=0, keepdims=True)
                halves.append((held * (part - base)).astype(BF))
            stacked = jnp.concatenate(halves, axis=0)
            beside = jnp.concatenate(halves, axis=1)
            probs_beside = jnp.concatenate([probs[:length], probs[length:]], axis=1)
            grad_ref[at, at_q] = (tn(stacked, keys) * 0.125).astype(BF)
            grad_ref[at, at_k] = nn(beside, queries).astype(BF)
            grad_ref[at, at_v] = nn(probs_beside, ctx_grads).astype(BF)
        return carry

    lax.fori_loop(0, rows // length, one, 0)
    total = jnp.zeros(sum_ref.shape, F32)
    for m in range(rows // length):
        total += jnp.sum(
            grad_ref[m * length : (m + 1) * length].astype(F32), axis=0, keepdims=True
        )

    @pl.when(pl.program_id(0) == 0)
    def _():
        sum_ref[...] = total

    @pl.when(pl.program_id(0) > 0)
    def _():
        sum_ref[...] += total


def attend_back(joined, probs, ctx_grad, length):
    rows, width = ctx_grad.shape
    count = rows // length
    steps = 2
    block = rows // steps
    pairs = width // PAIR
    return pl.pallas_call(
        functools.partial(attend_back_kernel, length),
        grid=(steps,),
        in_specs=[
            pl.BlockSpec((block, 3 * width), lambda i: (i, 0)),
            pl.BlockSpec((count // steps, pairs, 2 * length, length), lambda i: (i, 0, 0, 0)),
            pl.BlockSpec((block, width), lambda i: (i, 0)),
        ],
        out_specs=[
            pl.BlockSpec((block, 3 * width), lambda i: (i, 0)),
            full((1, 3 * width)),
        ],
        out_shape=[
            jax.ShapeDtypeStruct((rows, 3 * width), BF),
            jax.ShapeDtypeStruct((1, 3 * width), F32),
        ],
        compiler_params=params(),
        cost_estimate=cost(8 * rows * width * width, 20 * rows * width),
        name="attend_back",
    )(joined, probs, ctx_grad)


def weight_grads_kernel(place_ref, tok_ref, joined_ref, small_ref, keep_ref, send_ref):
    chips, part, _ = keep_ref.shape
    step = pl.program_id(0)
    width = tok_ref.shape[1]
    first = place_ref[2] == 0
    value = tn(tok_ref[...], joined_ref[...])
    cols = pl.ds(pl.multiple_of(step * width, width), width)
    for chip in range(chips):
        even = value[2 * chip * part : (2 * chip + 1) * part]
        odd = value[(2 * chip + 1) * part : (2 * chip + 2) * part]
        keep_ref[chip, :, cols] = jnp.where(first, even, odd).astype(BF)
        send_ref[chip, :, cols] = jnp.where(first, odd, even).astype(BF)

    lines = small_ref.shape[1]
    if keep_ref.shape[2] > 3 * width:

        @pl.when(step == 0)
        def _():
            tail = slice(3 * width, keep_ref.shape[2])
            keep_ref[:, :, tail] = jnp.zeros((chips, part, keep_ref.shape[2] - 3 * width), BF)
            send_ref[:, :, tail] = jnp.zeros((chips, part, keep_ref.shape[2] - 3 * width), BF)
            for chip in range(chips):
                even, odd = small_ref[2 * chip], small_ref[2 * chip + 1]
                keep_ref[chip, 0:lines, tail] = jnp.where(first, even, odd).astype(BF)
                send_ref[chip, 0:lines, tail] = jnp.where(first, odd, even).astype(BF)


def weight_grads(place, tokens, joined_grad, small, chips, extra):
    rows, width = tokens.shape
    shape = (chips, width // (2 * chips), 3 * width + extra)
    return pl.pallas_call(
        weight_grads_kernel,
        grid=(3,),
        in_specs=[
            pl.BlockSpec(memory_space=pltpu.SMEM),
            full((rows, width)),
            pl.BlockSpec((rows, width), lambda i: (0, i)),
            full(small.shape),
        ],
        out_specs=[full(shape), full(shape)],
        out_shape=[jax.ShapeDtypeStruct(shape, BF)] * 2,
        compiler_params=params(),
        cost_estimate=cost(6 * rows * width * width, 20 * rows * width),
        name="weight_grads",
    )(place, tokens, joined_grad, small)


def input_kernel(inner_ref, joined_ref, w_ref, out_ref):
    width = inner_ref.shape[1]
    total = inner_ref[...]
    for part in range(3):
        total += nt(joined_ref[:, part * width : (part + 1) * width], w_ref[part])
    out_ref[...] = total.astype(BF)


def input_back(inner, joined_grad, qkv):
    rows, width = inner.shape
    steps = 4
    block = rows // steps
    return pl.pallas_call(
        input_kernel,
        grid=(steps,),
        in_specs=[
            pl.BlockSpec((block, width), lambda i: (i, 0)),
            pl.BlockSpec((block, 3 * width), lambda i: (i, 0)),
            full((3, width, width)),
        ],
        out_specs=pl.BlockSpec((block, width), lambda i: (i, 0)),
        out_shape=jax.ShapeDtypeStruct((rows, width), BF),
        compiler_params=params(),
        cost_estimate=cost(6 * rows * width * width, 12 * rows * width),
        name="input_back",
    )(inner, joined_grad, qkv)


def lay_kernel(plan, chips, reps, part, counts, place_ref, *refs):
    at = 0
    groups = []
    for number in counts:
        groups.append(refs[at : at + number])
        at += number
    sems = refs[-1]
    rep, chip, core = place_ref[0], place_ref[1], place_ref[2]
    copies = []

    def start(source, target):
        copies.append(pltpu.make_async_copy(source, target, sems.at[len(copies)]))
        copies[-1].start()

    plan(start, groups, refs[at:-1], rep, chip, core, chips, reps, part)
    for copy in copies:
        copy.wait()


def blocks_plan(
    put, own, twin, along, across, swapped, far, depth, first, rep, chip, core, chips, reps, part
):
    for block in range(reps):
        put(own(block), block, chip, core)
        put(twin(block), block, chip, 1 - core)
    for step in range(1, chips):
        source = lax.rem(chip + chips - step, chips)
        rows = pl.ds((step - 1) * depth + first, part)
        put(along[step - 1].at[pl.ds(first, part)], rep, source, core)
        put(swapped[0].at[rows], rep, source, 1 - core)
        for at, other in enumerate(NEAR):
            put(across[at].at[rows], rep ^ other, source, core)
            put(swapped[1 + at].at[rows], rep ^ other, source, 1 - core)
        for side in range(2):
            put(far.at[source * 2 + side, pl.ds(first, part)], rep ^ FAR, source, side)


def wide_put(start, out_ref, part):
    def put(source, block, at_chip, at_core):
        row = pl.multiple_of((at_chip * 2 + at_core) * part, part)
        start(source, out_ref.at[block, pl.ds(row, part)])

    return put


def wide_block(ref, width, part):
    return lambda block: ref.at[pl.ds(0, part), pl.ds(block * width, width)]


def first_plan(start, groups, outs, rep, chip, core, chips, reps, part):
    owns, along, across, swapped, (far,), extra = groups
    own, twin = owns
    out_ref, more_ref = outs
    width = out_ref.shape[2]
    blocks_plan(
        wide_put(start, out_ref, part),
        wide_block(own, width, part),
        wide_block(twin, width, part),
        along,
        across,
        swapped,
        far,
        part,
        0,
        rep,
        chip,
        core,
        chips,
        reps,
        part,
    )
    tail = pl.ds(part, 16)
    cols = pl.ds(0, width)
    start(own.at[tail, cols], more_ref.at[chip * 2 + core])
    start(twin.at[tail, cols], more_ref.at[chip * 2 + 1 - core])
    for step in range(1, chips):
        source = lax.rem(chip + chips - step, chips)
        start(along[step - 1].at[tail], more_ref.at[source * 2 + core])
        start(extra[0].at[pl.ds((step - 1) * 16, 16)], more_ref.at[source * 2 + 1 - core])


def second_plan(start, groups, outs, rep, chip, core, chips, reps, part):
    owns, along, across, swapped, (far,) = groups
    up, up_twin, down, down_twin = owns
    up_ref, down_ref = outs
    width = up_ref.shape[2]
    where = (rep, chip, core, chips, reps, part)
    blocks_plan(
        wide_put(start, up_ref, part),
        wide_block(up, width, part),
        wide_block(up_twin, width, part),
        along,
        across,
        swapped,
        far,
        2 * part,
        0,
        *where,
    )

    def put(source, block, at_chip, at_core):
        row = pl.multiple_of(block * part, part)
        start(source, down_ref.at[at_chip * 2 + at_core, pl.ds(row, part)])

    def tall(ref):
        return lambda block: ref.at[pl.ds(block * part, part)]

    blocks_plan(
        put, tall(down), tall(down_twin), along, across, swapped, far, 2 * part, part, *where
    )


def lay(plan, place, groups, shapes, copies, part, chips, reps):
    anywhere = pl.BlockSpec(memory_space=pl.ANY)
    inputs = [ref for group in groups for ref in group]
    return pl.pallas_call(
        functools.partial(
            lay_kernel, plan, chips, reps, part, [len(group) for group in groups]
        ),
        in_specs=[pl.BlockSpec(memory_space=pltpu.SMEM)] + [anywhere] * len(inputs),
        out_specs=[pl.BlockSpec(memory_space=pltpu.VMEM)] * len(shapes),
        out_shape=[jax.ShapeDtypeStruct(shape, BF) for shape in shapes],
        scratch_shapes=[pltpu.SemaphoreType.DMA((copies,))],
        compiler_params=pltpu.CompilerParams(vmem_limit_bytes=VMEM_BYTES),
        cost_estimate=cost(0, 4 * sum(math.prod(shape) for shape in shapes)),
        name="lay",
    )(place, *inputs)


LANES = 128


def pack_vectors(rows, up_bias, class_weight):
    part = rows[0].shape[0]
    lines = [row[None] for row in rows[:8]] + [class_weight.T] + [row[None] for row in rows[8:]]
    pieces = up_bias.shape[0] // part
    lines += [up_bias[None, at * part : (at + 1) * part] for at in range(pieces)]
    return jnp.concatenate(lines, axis=0)


def move(values, reps, chips, target):
    pairs = []
    for rep in range(reps):
        for chip in range(chips):
            for core in range(2):
                to_rep, to_chip, to_core = target(rep, chip, core)
                pairs.append(
                    (
                        (rep * chips + chip) * 2 + core,
                        (to_rep * chips + to_chip) * 2 + to_core,
                    )
                )
    return lax.ppermute(values, ("rep", "fsdp"), pairs)


def along_chips(step, chips):
    return lambda rep, chip, core: (rep, (chip + step) % chips, core)


def across_reps(other):
    return lambda rep, chip, core: (rep ^ other, chip, core)


def to_twin(rep, chip, core):
    return rep, chip, 1 - core


def after(values, *gates):
    return lax.optimization_barrier((values, *gates))[0]


def along_z(mine, reps, chips):
    return [move(mine, reps, chips, along_chips(step, chips)) for step in range(1, chips)]


def over_near(stacked, reps, chips):
    return [move(stacked, reps, chips, across_reps(other)) for other in NEAR]


def pick(parts, at):
    return lax.dynamic_index_in_dim(parts, at, axis=0, keepdims=False)


def in_order(rep, reps, own, others, axis):
    blocks = jnp.stack([own] + others)
    return jnp.concatenate([pick(blocks, rep ^ at) for at in range(reps)], axis=axis)


class Reduction:
    def __init__(self, place, keep, send, reps, chips, by_chain=False):
        self.rep, self.chip = place[0], place[1]
        self.reps, self.chips = reps, chips
        self.shape = (chips, reps, keep.shape[1] // reps, keep.shape[2])
        self.keep = keep.reshape(self.shape)
        self.others_of = range(1, reps)
        self.far = None
        if by_chain:
            self.others_of = NEAR
            first = place[2] == 0
            kept = lax.dynamic_index_in_dim(self.keep, self.rep ^ FAR, axis=1, keepdims=False)
            sent = lax.dynamic_index_in_dim(
                send.reshape(self.shape), self.rep ^ FAR, axis=1, keepdims=False
            )
            pair = jnp.stack(
                [jnp.where(first, kept, sent), jnp.where(first, sent, kept)], axis=1
            )
            self.far = lax.psum_scatter(
                pair.reshape(-1, keep.shape[2]), "fsdp", scatter_dimension=0, tiled=True
            )
        self.got = move(send, reps, chips, to_twin)

    def at_rep(self, at):
        kept = lax.dynamic_index_in_dim(self.keep, at, axis=1, keepdims=False)
        came = lax.dynamic_index_in_dim(
            self.got.reshape(self.shape), at, axis=1, keepdims=False
        )
        return kept.astype(F32) + came.astype(F32)

    def over_reps(self, *gates):
        if gates:
            self.got = after(self.got, *gates)
        self.arrived = [
            move(
                self.at_rep(self.rep ^ other).astype(BF),
                self.reps,
                self.chips,
                across_reps(other),
            )
            for other in self.others_of
        ]

    def over_chips(self, *gates):
        if gates:
            self.arrived = [after(block, *gates) for block in self.arrived]
        mine = self.at_rep(self.rep)

        def both_at(at):
            total = pick(mine, at)
            for block in self.arrived:
                total = total + pick(block, at).astype(F32)
            return total

        self.total = both_at(self.chip)
        if self.far is not None:
            came = move(self.far, self.reps, self.chips, across_reps(FAR))
            self.total = self.total + came.astype(F32)
        self.passed = [
            move(
                both_at(lax.rem(self.chip + step, self.chips)).astype(BF),
                self.reps,
                self.chips,
                along_chips(step, self.chips),
            )
            for step in range(1, self.chips)
        ]

    def share(self, *gates):
        if gates:
            self.passed = [after(block, *gates) for block in self.passed]
        total = self.total
        for block in self.passed:
            total = total + block.astype(F32)
        self.total = total.astype(BF)
        self.others = [
            move(self.total, self.reps, self.chips, across_reps(other))
            for other in range(1, self.reps)
        ]

    def result(self):
        return in_order(self.rep, self.reps, self.total, self.others, 0).astype(F32)


def sum_over_reps(place, rows, reps, chips):
    rep = place[0]
    parts = rows.reshape(reps, -1, rows.shape[1])
    total = pick(parts, rep).astype(F32)
    for other in range(1, reps):
        there = pick(parts, rep ^ other)
        total = total + move(there, reps, chips, across_reps(other)).astype(F32)
    total = total.astype(BF)
    others = [move(total, reps, chips, across_reps(other)) for other in range(1, reps)]
    return in_order(rep, reps, total, others, 0)


def per_device(
    tokens,
    exit_layer,
    qkv_weight,
    query_bias,
    value_bias,
    out_weight,
    out_bias,
    attn_gain,
    attn_shift,
    up_weight,
    up_bias,
    down_weight,
    down_bias,
    block_gain,
    block_shift,
    pool_weight,
    pool_bias,
    class_weight,
    class_bias,
    output_grad,
    logit_grad,
):
    reps = lax.axis_size("rep")
    shards = lax.axis_size("fsdp")
    mine = lax.axis_index("fsdp")
    rows, width = tokens.shape
    count = exit_layer.shape[0]
    length = rows // count
    classes = class_weight.shape[1]
    part = out_weight.shape[0]
    hidden = up_weight.shape[1]

    def gather(shard):
        return lax.all_gather(shard, "fsdp", axis=0, tiled=True)

    packed = pack_vectors(
        [
            query_bias,
            value_bias,
            out_bias,
            attn_gain,
            attn_shift,
            down_bias,
            block_gain,
            block_shift,
            pool_bias,
        ],
        up_bias,
        class_weight,
    )
    joint_own = jnp.concatenate([qkv_weight, out_weight], axis=1)
    deep = down_weight.shape[0]
    chips = shards // 2
    place = jnp.stack([lax.axis_index("rep"), mine // 2, mine % 2]).astype(jnp.int32)
    direct = (
        part % 16 == 0
        and reps & (reps - 1) == 0
        and reps * width == hidden
        and reps == 4
        and packed.shape[0] <= 16
    )
    if direct:
        lines = packed.shape[0]
        held = jnp.pad(packed, ((0, 16 - lines), (0, width - part)))
        own = jnp.concatenate([joint_own, jnp.tile(held, (1, reps))], axis=0)
        rep = place[0]

        def block_of(weights, at):
            return lax.dynamic_slice_in_dim(weights, at * width, width, axis=1)

        far = gather(block_of(joint_own, rep ^ FAR))
        along = along_z(block_of(own, rep), reps, chips)
        twin = move(own, reps, chips, to_twin)
        stacked = jnp.concatenate([rows_[:part] for rows_ in along], axis=0)
        across = over_near(stacked, reps, chips)
        swapped = [move(rows_, reps, chips, to_twin) for rows_ in [stacked] + across]
        extra = move(
            jnp.concatenate([rows_[part:] for rows_ in along], axis=0), reps, chips, to_twin
        )

        def second_of(at):
            return jnp.concatenate(
                [
                    block_of(up_weight, at),
                    lax.dynamic_slice_in_dim(down_weight, at * part, part, axis=0),
                ],
                axis=0,
            )

        second_far = gather(after(second_of(rep ^ FAR), *along))
        second_along = along_z(after(second_of(rep), stacked), reps, chips)
        pool = gather(after(pool_weight, *second_along))
        up_twin = move(up_weight, reps, chips, to_twin)
        down_twin = move(down_weight, reps, chips, to_twin)
        second_stacked = jnp.concatenate(second_along, axis=0)
        second_across = over_near(after(second_stacked, *across), reps, chips)
        joint, small = lay(
            first_plan,
            place,
            [
                [own, twin],
                along,
                across,
                swapped,
                [far.reshape(shards, part, width)],
                [extra],
            ],
            [(reps, width, width), (shards, 16, width)],
            2 * chips * (reps + 1),
            part,
            chips,
            reps,
        )
        small = small[:, :lines, :part]
        down_block = (width // deep, deep, width)
    else:
        small = gather(packed[None])
        pool = gather(pool_weight)
        joint = jnp.stack(jnp.split(gather(joint_own), 4, axis=1))
        up = jnp.stack(jnp.split(gather(up_weight), hidden // width, axis=1))
        down = gather(down_weight).reshape(-1, width, width)
        down_block = (1, width, width)
    vec = small[:, :VECTOR_ROWS].transpose(1, 0, 2).reshape(VECTOR_ROWS, width).astype(F32)
    vec = jnp.pad(vec, ((0, 16 - VECTOR_ROWS), (0, 0)))
    up_row = small[:, VECTOR_ROWS:].reshape(1, hidden).astype(F32)
    bias_row = jnp.concatenate([vec[:1], jnp.zeros((1, width), F32), vec[1:2]], axis=1)

    joined, probs, ctx = attend(tokens, joint, bias_row, length)
    if direct:
        second_swapped = [
            move(after(rows_, ctx), reps, chips, to_twin)
            for rows_ in [second_stacked] + second_across
        ]
        up, down = lay(
            second_plan,
            place,
            [
                [up_weight, up_twin, down_weight, down_twin],
                second_along,
                second_across,
                second_swapped,
                [second_far.reshape(shards, 2 * part, width)],
            ],
            [(reps, width, width), (shards, deep, width)],
            4 * chips * reps,
            part,
            chips,
            reps,
        )
    low, act, slope, unit1, scale1, unit2, scale2, output = feed(
        exit_layer, tokens, ctx, joint, vec, up, up_row, down, down_block, length
    )
    class_bias_row = jnp.pad(class_bias.astype(F32), (0, 8 - classes))[None]
    logit_grad_rows = jnp.pad(logit_grad, ((0, 0), (0, 8 - classes)))
    outer, branch, low_keep, low_send, exit_sums, class_grad, logits, stats = leave(
        place,
        exit_layer,
        output,
        unit2,
        scale2,
        output_grad,
        pool,
        vec,
        class_bias_row,
        logit_grad_rows,
        act,
        full((width, width)),
        shards,
        length,
        classes,
    )
    if direct:
        low_red = Reduction(place, low_keep, low_send, reps, chips, True)
    up_grad, up_sum, inner, attended, ctx_grad, feed_sums = feed_back(
        branch, slope, low, down, down_block, up, outer, unit1, scale1, joint, vec, ctx
    )
    if direct:
        low_red.over_reps(attended)
        ctx_grad = after(ctx_grad, low_red.got, low_red.far)
    joined_grad, joined_sum = attend_back(joined, probs, ctx_grad, length)
    joined_seen = joined_grad
    if direct:
        low_red.over_chips(joined_grad)
        joined_seen = after(joined_grad, *low_red.arrived)
    sums = jnp.concatenate(
        [
            joined_sum.reshape(3, width)[::2],
            feed_sums,
            exit_sums,
            class_grad[:classes],
        ],
        axis=0,
    )
    lines = sums.shape[0]
    own_sums = sums.reshape(lines, shards, part).transpose(1, 0, 2).reshape(shards, lines * part)
    own_sums = jnp.concatenate([own_sums, up_sum.reshape(shards, deep)], axis=1)
    used = own_sums.shape[1]
    seqs_total = count * reps * shards
    figures = jnp.concatenate([stats[0, :1], stats[1, :classes]])
    slots = reps * shards * figures.shape[0] * 3
    direct = direct and used + slots <= part * LANES
    small_lines = 16
    if direct:
        high = figures.astype(BF).astype(F32)
        middle = (figures - high).astype(BF).astype(F32)
        lowest = figures - high - middle
        split = jnp.concatenate([high, middle, lowest])
        slot = lax.axis_index("rep") * shards + mine
        lone = jnp.where(
            jnp.arange(reps * shards)[:, None] == slot, split[None], 0.0
        ).reshape(1, slots)
        row = jnp.concatenate([own_sums, jnp.broadcast_to(lone, (shards, slots))], axis=1)
        small_lines = -(-row.shape[1] // (LANES * 16)) * 16
        row = jnp.pad(row, ((0, 0), (0, small_lines * LANES - row.shape[1])))
        row = row.reshape(shards, small_lines, LANES)
    else:
        row = jnp.zeros((shards, small_lines, LANES), F32)
    keep, send = weight_grads(
        place, tokens, joined_seen, row, chips, LANES if direct else 0
    )
    input_grad = input_back(inner, joined_grad, joint)

    def scatter(grad):
        return lax.psum_scatter(grad, "fsdp", scatter_dimension=0, tiled=True)

    up_part = scatter(up_grad)
    if direct:
        joint_red = Reduction(place, keep, send, reps, chips)
        joint_red.over_reps(*low_red.passed)
        low_red.share()
        joint_red.over_chips(*low_red.others)
        joint_red.share(up_part)
        up_sum = sum_over_reps(place, up_part, reps, chips).astype(F32)
        low_sum = low_red.result()
        joint_sum = joint_red.result()
        small_sum = joint_sum[:small_lines, 3 * width :].reshape(-1)
        total = small_sum[used : used + slots].reshape(-1, figures.shape[0]).sum(axis=0)
    else:
        first = mine % 2 == 0

        def whole_of(kept, sent):
            pair = jnp.stack([jnp.where(first, kept, sent), jnp.where(first, sent, kept)], axis=1)
            return pair.reshape(-1, kept.shape[2])

        joint_sum, low_sum, up_sum = lax.psum(
            (
                scatter(whole_of(keep, send)),
                scatter(whole_of(low_keep, low_send)),
                up_part,
            ),
            "rep",
        )
        joint_sum, low_sum, up_sum = (
            joint_sum.astype(F32),
            low_sum.astype(F32),
            up_sum.astype(F32),
        )
        own_sums, total = lax.psum((own_sums, figures), ("rep", "fsdp"))
        small_sum = pick(own_sums, mine)
    own = small_sum[: lines * part].reshape(lines, part)
    return (
        output,
        logits[:, :classes],
        total[0] / seqs_total,
        input_grad,
        joint_sum[:, : 3 * width],
        own[0],
        own[1],
        up_sum[:, hidden:],
        own[4],
        own[2],
        own[3],
        up_sum[:, :hidden],
        small_sum[lines * part : used],
        low_sum[:deep],
        own[7],
        own[5],
        own[6],
        low_sum[deep:],
        own[8],
        own[9 : 9 + classes].T,
        total[1:],
    )


def solution(mesh):
    return jax.shard_map(
        per_device,
        mesh=mesh,
        in_specs=(
            P(("rep", "fsdp"), None),
            P(("rep", "fsdp")),
            P("fsdp", None),
            P("fsdp"),
            P("fsdp"),
            P("fsdp", None),
            P("fsdp"),
            P("fsdp"),
            P("fsdp"),
            P("fsdp", None),
            P("fsdp"),
            P("fsdp", None),
            P("fsdp"),
            P("fsdp"),
            P("fsdp"),
            P("fsdp", None),
            P("fsdp"),
            P("fsdp", None),
            P(),
            P(("rep", "fsdp"), None),
            P(("rep", "fsdp"), None),
        ),
        out_specs=(
            P(("rep", "fsdp"), None),
            P(("rep", "fsdp"), None),
            P(),
            P(("rep", "fsdp"), None),
            P("fsdp", None),
            P("fsdp"),
            P("fsdp"),
            P("fsdp", None),
            P("fsdp"),
            P("fsdp"),
            P("fsdp"),
            P("fsdp", None),
            P("fsdp"),
            P("fsdp", None),
            P("fsdp"),
            P("fsdp"),
            P("fsdp"),
            P("fsdp", None),
            P("fsdp"),
            P("fsdp", None),
            P(),
        ),
        check_vma=False,
    )
```

```python
import functools
import math

import jax
import jax.numpy as jnp
from jax import lax
from jax.experimental import pallas as pl
from jax.experimental.pallas import tpu as pltpu
from jax.sharding import PartitionSpec as P

HD = 64
LAYER = 6
PAIR = 2 * HD
NEAR = (1, 2)
FAR = 3
VMEM_BYTES = 58 * 2**20
BF = jnp.bfloat16
F32 = jnp.float32

QUERY_BIAS, VALUE_BIAS, OUT_BIAS, ATTN_GAIN, ATTN_SHIFT = 0, 1, 2, 3, 4
DOWN_BIAS, BLOCK_GAIN, BLOCK_SHIFT, CLASS_ROWS, POOL_BIAS = 5, 6, 7, 8, 11
VECTOR_ROWS = 12


def nn(left, right):
    return jnp.dot(left, right, preferred_element_type=F32)


def tn(left, right):
    return lax.dot_general(left, right, (((0,), (0,)), ((), ())), preferred_element_type=F32)


def nt(left, right):
    return lax.dot_general(left, right, (((1,), (1,)), ((), ())), preferred_element_type=F32)


def full(shape):
    return pl.BlockSpec(shape, lambda *at: (0,) * len(shape))


def params():
    return pltpu.CompilerParams(
        dimension_semantics=("arbitrary",), vmem_limit_bytes=VMEM_BYTES
    )


def cost(flops, moved, trans=0):
    return pl.CostEstimate(flops=flops, bytes_accessed=moved, transcendentals=trans)


def split_heads(pair):
    lane = lax.broadcasted_iota(jnp.int32, pair.shape, 1)
    zero = jnp.zeros_like(pair)
    return jnp.concatenate(
        [jnp.where(lane < HD, pair, zero), jnp.where(lane < HD, zero, pair)], axis=0
    )


def norm_stats(values):
    center = values - jnp.mean(values, axis=-1, keepdims=True)
    spread = jnp.mean(center * center, axis=-1, keepdims=True)
    scale = lax.rsqrt(spread + 1e-06)
    return center * scale, scale


def norm_back(grad, unit, scale, gain):
    inner = grad * gain
    first = jnp.mean(inner, axis=-1, keepdims=True)
    second = jnp.mean(inner * unit, axis=-1, keepdims=True)
    return scale * (inner - first - unit * second)


def gelu_parts(values):
    size = jnp.abs(values)
    t = 1.0 / (1.0 + 0.23164189 * size)
    bell = jnp.exp(-0.5 * values * values)
    poly = t * (
        0.127414796
        + t * (-0.142248368 + t * (0.7107068705 + t * (-0.7265760135 + t * 0.5307027145)))
    )
    tail = poly * bell
    below = jnp.where(values >= 0.0, 1.0 - tail, tail)
    return values * below, below + values * (bell * 0.3989422804014327)


def attend_kernel(length, tok_ref, w_ref, bias_ref, joined_ref, probs_ref, ctx_ref):
    rows, width = ctx_ref.shape
    pairs = width // PAIR
    for part in range(3):
        cols = slice(part * width, (part + 1) * width)
        joined_ref[:, cols] = (nn(tok_ref[...], w_ref[part]) + bias_ref[:, cols]).astype(BF)

    def one(seq, carry):
        at = pl.ds(pl.multiple_of(seq * length, length), length)
        for pair in range(pairs):
            cols = slice(pair * PAIR, (pair + 1) * PAIR)
            query = joined_ref[at, cols] * jnp.asarray(0.125, BF)
            keys = split_heads(joined_ref[at, width + pair * PAIR : width + (pair + 1) * PAIR])
            vals = split_heads(
                joined_ref[at, 2 * width + pair * PAIR : 2 * width + (pair + 1) * PAIR]
            )
            scores = nt(keys, query)
            halves = []
            for head in range(2):
                part = scores[head * length : (head + 1) * length]
                part = jnp.exp(part - jnp.max(part, axis=0, keepdims=True))
                part = part * (1.0 / jnp.sum(part, axis=0, keepdims=True))
                halves.append(part.astype(BF))
            probs = jnp.concatenate(halves, axis=0)
            probs_ref[seq, pair] = probs
            ctx_ref[at, cols] = tn(probs, vals).astype(BF)
        return carry

    lax.fori_loop(0, rows // length, one, 0)


def attend(tokens, qkv, bias_row, length):
    rows, width = tokens.shape
    count = rows // length
    steps = 2
    block = rows // steps
    pairs = width // PAIR
    return pl.pallas_call(
        functools.partial(attend_kernel, length),
        grid=(steps,),
        in_specs=[
            pl.BlockSpec((block, width), lambda i: (i, 0)),
            full((3, width, width)),
            full(bias_row.shape),
        ],
        out_specs=[
            pl.BlockSpec((block, 3 * width), lambda i: (i, 0)),
            pl.BlockSpec((count // steps, pairs, 2 * length, length), lambda i: (i, 0, 0, 0)),
            pl.BlockSpec((block, width), lambda i: (i, 0)),
        ],
        out_shape=[
            jax.ShapeDtypeStruct((rows, 3 * width), BF),
            jax.ShapeDtypeStruct((count, pairs, 2 * length, length), BF),
            jax.ShapeDtypeStruct((rows, width), BF),
        ],
        compiler_params=params(),
        cost_estimate=cost(8 * rows * width * width, 20 * rows * width, rows * width),
        name="attend",
    )(tokens, qkv, bias_row)


def feed_kernel(
    length,
    exit_ref,
    tok_ref,
    ctx_ref,
    out_w_ref,
    vec_ref,
    up_ref,
    up_b_ref,
    down_ref,
    low_ref,
    act_ref,
    slope_ref,
    unit1_ref,
    scale1_ref,
    unit2_ref,
    scale2_ref,
    output_ref,
    acc_ref,
):
    step = pl.program_id(0)
    rows = tok_ref.shape[0]
    sub = 256

    @pl.when(step == 0)
    def _():
        for m in range(rows // sub):
            at = slice(m * sub, (m + 1) * sub)
            inner = tok_ref[at].astype(F32) + (
                nn(ctx_ref[at], out_w_ref[0]) + vec_ref[OUT_BIAS : OUT_BIAS + 1]
            )
            unit, scale = norm_stats(inner)
            first = unit * vec_ref[ATTN_GAIN : ATTN_GAIN + 1] + vec_ref[ATTN_SHIFT : ATTN_SHIFT + 1]
            unit1_ref[at] = unit.astype(BF)
            scale1_ref[at] = scale
            low_ref[at] = first.astype(BF)
            acc_ref[at] = first + vec_ref[DOWN_BIAS : DOWN_BIAS + 1]

    down = down_ref[...].reshape(up_ref.shape[1:])
    for m in range(rows // sub):
        at = slice(m * sub, (m + 1) * sub)
        hidden = nn(low_ref[at], up_ref[0]) + up_b_ref[...]
        act, slope = gelu_parts(hidden)
        act = act.astype(BF)
        act_ref[at] = act
        slope_ref[at] = slope.astype(BF)
        acc_ref[at] += nn(act, down)

    @pl.when(step == pl.num_programs(0) - 1)
    def _():
        for seq in range(rows // length):
            at = slice(seq * length, (seq + 1) * length)
            active = (exit_ref[seq] >= LAYER).astype(F32)
            unit, scale = norm_stats(acc_ref[at])
            unit2_ref[at] = unit.astype(BF)
            scale2_ref[at] = scale
            result = (
                unit * vec_ref[BLOCK_GAIN : BLOCK_GAIN + 1] + vec_ref[BLOCK_SHIFT : BLOCK_SHIFT + 1]
            ) * active
            output_ref[at] = result.astype(BF)


def feed(exit_layer, tokens, ctx, out_w, vec, up, up_bias, down, down_block, length):
    rows, width = tokens.shape
    steps = up.shape[0]
    hidden = steps * width
    whole = full((rows, width))
    return pl.pallas_call(
        functools.partial(feed_kernel, length),
        grid=(steps,),
        in_specs=[
            pl.BlockSpec(memory_space=pltpu.SMEM),
            whole,
            whole,
            pl.BlockSpec((1, width, width), lambda i: (3, 0, 0)),
            full(vec.shape),
            pl.BlockSpec((1, width, width), lambda i: (i, 0, 0)),
            pl.BlockSpec((1, width), lambda i: (0, i)),
            pl.BlockSpec(down_block, lambda i: (i, 0, 0)),
        ],
        out_specs=[
            whole,
            pl.BlockSpec((rows, width), lambda i: (0, i)),
            pl.BlockSpec((rows, width), lambda i: (0, i)),
            whole,
            full((rows, 1)),
            whole,
            full((rows, 1)),
            whole,
        ],
        out_shape=[
            jax.ShapeDtypeStruct((rows, width), BF),
            jax.ShapeDtypeStruct((rows, hidden), BF),
            jax.ShapeDtypeStruct((rows, hidden), BF),
            jax.ShapeDtypeStruct((rows, width), BF),
            jax.ShapeDtypeStruct((rows, 1), F32),
            jax.ShapeDtypeStruct((rows, width), BF),
            jax.ShapeDtypeStruct((rows, 1), F32),
            jax.ShapeDtypeStruct((rows, width), BF),
        ],
        scratch_shapes=[pltpu.VMEM((rows, width), F32)],
        compiler_params=params(),
        cost_estimate=cost(18 * rows * width * width, 40 * rows * width, 8 * rows * width),
        name="feed",
    )(exit_layer, tokens, ctx, out_w, vec, up, up_bias, down)


def leave_kernel(
    length,
    classes,
    exit_ref,
    output_ref,
    unit2_ref,
    scale2_ref,
    grad_ref,
    pool_ref,
    vec_ref,
    class_bias_ref,
    logit_grad_ref,
    act_ref,
    outer_ref,
    branch_ref,
    joint_grad_ref,
    sums_ref,
    class_grad_ref,
    logits_ref,
    stats_ref,
    lead_ref,
    pool_grad_ref,
):
    step = pl.program_id(0)
    rows, width = output_ref.shape
    pool = pool_ref[...].reshape(width, width)
    count = rows // length

    @pl.when(step == 0)
    def _():
        place = lax.broadcasted_iota(jnp.int32, (count, 1), 0)
        active = jnp.zeros((count, 1), F32)
        for seq in range(count):
            on = (exit_ref[seq] >= LAYER).astype(F32)
            active = jnp.where(place == seq, on, active)
        leading = jnp.concatenate(
            [output_ref[seq * length : seq * length + 1].astype(F32) for seq in range(count)],
            axis=0,
        ).astype(BF)
        pooled = jnp.tanh(nn(leading, pool) + vec_ref[POOL_BIAS : POOL_BIAS + 1])
        pooled_low = pooled.astype(BF)
        used = lax.broadcasted_iota(jnp.int32, (8, width), 0) < classes
        class_rows = jnp.where(used, vec_ref[CLASS_ROWS : CLASS_ROWS + 8], 0.0).astype(BF)
        raw = nt(pooled_low, class_rows) + class_bias_ref[...]
        lane = lax.broadcasted_iota(jnp.int32, raw.shape, 1) < classes
        top = jnp.max(jnp.where(lane, raw, -jnp.inf), axis=-1, keepdims=True)
        spread = jnp.where(lane, jnp.exp(raw - top), 0.0)
        logprob = raw - top - jnp.log(jnp.sum(spread, axis=-1, keepdims=True))
        entropy = -jnp.sum(
            jnp.where(lane, jnp.exp(logprob) * logprob, 0.0), axis=-1, keepdims=True
        )
        logits_ref[...] = raw * active
        class_grad = (logit_grad_ref[...].astype(F32) * active).astype(BF)
        stats_ref[0:1] = jnp.broadcast_to(jnp.sum(entropy * active, axis=0, keepdims=True), (1, 8))
        stats_ref[1:2] = jnp.sum(class_grad.astype(F32), axis=0, keepdims=True)
        class_grad_ref[...] = tn(class_grad, pooled_low)
        pooled_grad = nn(class_grad, class_rows)
        pre_grad = (pooled_grad * (1.0 - pooled * pooled)).astype(BF)
        sums_ref[3:4] = jnp.sum(pre_grad.astype(F32), axis=0, keepdims=True)
        pool_grad_ref[...] = tn(leading, pre_grad).reshape(pool_grad_ref.shape).astype(BF)
        lead_ref[...] = nt(pre_grad, pool)
        head = lax.broadcasted_iota(jnp.int32, (length, 1), 0) == 0
        gain = vec_ref[BLOCK_GAIN : BLOCK_GAIN + 1]
        gain_sum = jnp.zeros((1, width), F32)
        shift_sum = jnp.zeros((1, width), F32)
        bias_sum = jnp.zeros((1, width), F32)
        for seq in range(count):
            at = slice(seq * length, (seq + 1) * length)
            on = (exit_ref[seq] >= LAYER).astype(F32)
            top_grad = (
                grad_ref[at].astype(F32) + jnp.where(head, lead_ref[seq : seq + 1], 0.0)
            ) * on
            unit = unit2_ref[at].astype(F32)
            outer = norm_back(top_grad, unit, scale2_ref[at], gain)
            branch = outer.astype(BF)
            outer_ref[at] = outer
            branch_ref[at] = branch
            gain_sum += jnp.sum(top_grad * unit, axis=0, keepdims=True)
            shift_sum += jnp.sum(top_grad, axis=0, keepdims=True)
            bias_sum += jnp.sum(branch.astype(F32), axis=0, keepdims=True)
        sums_ref[0:1] = gain_sum
        sums_ref[1:2] = shift_sum
        sums_ref[2:3] = bias_sum

    @pl.when(step > 0)
    def _():
        few, both, _ = joint_grad_ref.shape
        deep = width // few
        value = tn(act_ref[...], branch_ref[...])
        for at in range(few):
            joint_grad_ref[at, 0:deep] = value[at * deep : (at + 1) * deep].astype(BF)
            joint_grad_ref[at, deep:both] = pool_grad_ref[(step - 1) * few + at]


def leave(
    exit_layer, output, unit2, scale2, output_grad, pool, vec, class_bias, logit_grad, act,
    pool_spec, shards, length, classes,
):
    rows, width = output.shape
    count = rows // length
    hidden = act.shape[1]
    steps = hidden // width
    few = shards // steps
    both = (hidden + width) // shards
    whole = full((rows, width))
    return pl.pallas_call(
        functools.partial(leave_kernel, length, classes),
        grid=(steps + 1,),
        in_specs=[
            pl.BlockSpec(memory_space=pltpu.SMEM),
            whole,
            whole,
            full((rows, 1)),
            whole,
            pool_spec,
            full(vec.shape),
            full(class_bias.shape),
            full(logit_grad.shape),
            pl.BlockSpec((rows, width), lambda i: (0, jnp.maximum(i - 1, 0))),
        ],
        out_specs=[
            whole,
            whole,
            pl.BlockSpec((few, both, width), lambda i: (jnp.maximum(i - 1, 0), 0, 0)),
            full((4, width)),
            full((8, width)),
            full((count, 8)),
            full((2, 8)),
        ],
        out_shape=[
            jax.ShapeDtypeStruct((rows, width), F32),
            jax.ShapeDtypeStruct((rows, width), BF),
            jax.ShapeDtypeStruct((shards, both, width), BF),
            jax.ShapeDtypeStruct((4, width), F32),
            jax.ShapeDtypeStruct((8, width), F32),
            jax.ShapeDtypeStruct((count, 8), F32),
            jax.ShapeDtypeStruct((2, 8), F32),
        ],
        scratch_shapes=[
            pltpu.VMEM((count, width), F32),
            pltpu.VMEM((shards, width // shards, width), BF),
        ],
        compiler_params=params(),
        cost_estimate=cost(8 * rows * width * width, 30 * rows * width),
        name="leave",
    )(
        exit_layer, output, unit2, scale2, output_grad, pool, vec, class_bias, logit_grad, act
    )


def split_cores(value, place_ref, keep_ref, send_ref):
    chips, part, _ = keep_ref.shape
    first = place_ref[2] == 0
    for chip in range(chips):
        even = value[2 * chip * part : (2 * chip + 1) * part]
        odd = value[(2 * chip + 1) * part : (2 * chip + 2) * part]
        keep_ref[chip] = jnp.where(first, even, odd).astype(BF)
        send_ref[chip] = jnp.where(first, odd, even).astype(BF)


def feed_back_kernel(
    place_ref,
    branch_ref,
    slope_ref,
    low_ref,
    down_ref,
    up_ref,
    outer_ref,
    unit1_ref,
    scale1_ref,
    out_w_ref,
    vec_ref,
    ctx_ref,
    keep_ref,
    send_ref,
    up_sum_ref,
    inner_ref,
    attended_ref,
    ctx_grad_ref,
    sums_ref,
    acc_ref,
    hid_ref,
):
    step = pl.program_id(0)
    rows, width = branch_ref.shape
    sub = 256

    @pl.when(step == 0)
    def _():
        acc_ref[...] = outer_ref[...]

    last = pl.num_programs(0) - 1

    @pl.when(step < last)
    def _():
        total = jnp.zeros((1, width), F32)
        down = down_ref[...].reshape(up_ref.shape[1:])
        for m in range(rows // sub):
            at = slice(m * sub, (m + 1) * sub)
            hid = (nt(branch_ref[at], down) * slope_ref[at].astype(F32)).astype(BF)
            hid_ref[at] = hid
            total += jnp.sum(hid.astype(F32), axis=0, keepdims=True)
            acc_ref[at] += nt(hid, up_ref[0])
        up_sum_ref[...] = total
        split_cores(tn(low_ref[...], hid_ref[...]), place_ref, keep_ref, send_ref)

    @pl.when(step == last)
    def _():
        gain = vec_ref[ATTN_GAIN : ATTN_GAIN + 1]
        gain_sum = jnp.zeros((1, width), F32)
        shift_sum = jnp.zeros((1, width), F32)
        bias_sum = jnp.zeros((1, width), F32)
        for m in range(rows // sub):
            at = slice(m * sub, (m + 1) * sub)
            grad = acc_ref[at]
            unit = unit1_ref[at].astype(F32)
            inner = norm_back(grad, unit, scale1_ref[at], gain)
            attended = inner.astype(BF)
            inner_ref[at] = inner
            attended_ref[at] = attended
            ctx_grad_ref[at] = nt(attended, out_w_ref[0]).astype(BF)
            gain_sum += jnp.sum(grad * unit, axis=0, keepdims=True)
            shift_sum += jnp.sum(grad, axis=0, keepdims=True)
            bias_sum += jnp.sum(attended.astype(F32), axis=0, keepdims=True)
        sums_ref[0:1] = gain_sum
        sums_ref[1:2] = shift_sum
        sums_ref[2:3] = bias_sum
        split_cores(tn(ctx_ref[...], attended_ref[...]), place_ref, keep_ref, send_ref)


def feed_back(place, chips, branch, slope, low, down, down_block, up, outer, unit1, scale1, out_w, vec, ctx):
    rows, width = branch.shape
    hidden = slope.shape[1]
    steps = hidden // width
    whole = full((rows, width))
    end = steps - 1
    part = width // (2 * chips)
    return pl.pallas_call(
        feed_back_kernel,
        grid=(steps + 1,),
        in_specs=[
            pl.BlockSpec(memory_space=pltpu.SMEM),
            whole,
            pl.BlockSpec((rows, width), lambda i: (0, jnp.minimum(i, end))),
            whole,
            pl.BlockSpec(down_block, lambda i: (jnp.minimum(i, end), 0, 0)),
            pl.BlockSpec((1, width, width), lambda i: (jnp.minimum(i, end), 0, 0)),
            whole,
            whole,
            full((rows, 1)),
            pl.BlockSpec((1, width, width), lambda i: (3, 0, 0)),
            full(vec.shape),
            whole,
        ],
        out_specs=[
            pl.BlockSpec((chips, part, width), lambda i: (0, 0, i)),
            pl.BlockSpec((chips, part, width), lambda i: (0, 0, i)),
            pl.BlockSpec((1, width), lambda i: (0, jnp.minimum(i, end))),
            whole,
            whole,
            whole,
            full((3, width)),
        ],
        out_shape=[
            jax.ShapeDtypeStruct((chips, part, hidden + width), BF),
            jax.ShapeDtypeStruct((chips, part, hidden + width), BF),
            jax.ShapeDtypeStruct((1, hidden), F32),
            jax.ShapeDtypeStruct((rows, width), F32),
            jax.ShapeDtypeStruct((rows, width), BF),
            jax.ShapeDtypeStruct((rows, width), BF),
            jax.ShapeDtypeStruct((3, width), F32),
        ],
        scratch_shapes=[pltpu.VMEM((rows, width), F32), pltpu.VMEM((rows, width), BF)],
        compiler_params=params(),
        cost_estimate=cost(28 * rows * width * width, 40 * rows * width),
        name="feed_back",
    )(place, branch, slope, low, down, up, outer, unit1, scale1, out_w, vec, ctx)


def attend_back_kernel(length, joined_ref, probs_ref, ctx_grad_ref, grad_ref, sum_ref):
    rows, width = ctx_grad_ref.shape
    pairs = width // PAIR

    def one(seq, carry):
        at = pl.ds(pl.multiple_of(seq * length, length), length)
        for pair in range(pairs):
            at_q = slice(pair * PAIR, (pair + 1) * PAIR)
            at_k = slice(width + pair * PAIR, width + (pair + 1) * PAIR)
            at_v = slice(2 * width + pair * PAIR, 2 * width + (pair + 1) * PAIR)
            query = joined_ref[at, at_q] * jnp.asarray(0.125, BF)
            queries = split_heads(query)
            keys = split_heads(joined_ref[at, at_k])
            vals = split_heads(joined_ref[at, at_v])
            ctx_grad = ctx_grad_ref[at, at_q]
            ctx_grads = split_heads(ctx_grad)
            probs = probs_ref[seq, pair]
            prob_grad = nt(vals, ctx_grad)
            halves = []
            for head in range(2):
                cut = slice(head * length, (head + 1) * length)
                held = probs[cut].astype(F32)
                part = prob_grad[cut]
                base = jnp.sum(part * held, axis=0, keepdims=True)
                halves.append((held * (part - base)).astype(BF))
            stacked = jnp.concatenate(halves, axis=0)
            beside = jnp.concatenate(halves, axis=1)
            probs_beside = jnp.concatenate([probs[:length], probs[length:]], axis=1)
            grad_ref[at, at_q] = (tn(stacked, keys) * 0.125).astype(BF)
            grad_ref[at, at_k] = nn(beside, queries).astype(BF)
            grad_ref[at, at_v] = nn(probs_beside, ctx_grads).astype(BF)
        return carry

    lax.fori_loop(0, rows // length, one, 0)
    total = jnp.zeros(sum_ref.shape, F32)
    for m in range(rows // length):
        total += jnp.sum(
            grad_ref[m * length : (m + 1) * length].astype(F32), axis=0, keepdims=True
        )

    @pl.when(pl.program_id(0) == 0)
    def _():
        sum_ref[...] = total

    @pl.when(pl.program_id(0) > 0)
    def _():
        sum_ref[...] += total


def attend_back(joined, probs, ctx_grad, length):
    rows, width = ctx_grad.shape
    count = rows // length
    steps = 2
    block = rows // steps
    pairs = width // PAIR
    return pl.pallas_call(
        functools.partial(attend_back_kernel, length),
        grid=(steps,),
        in_specs=[
            pl.BlockSpec((block, 3 * width), lambda i: (i, 0)),
            pl.BlockSpec((count // steps, pairs, 2 * length, length), lambda i: (i, 0, 0, 0)),
            pl.BlockSpec((block, width), lambda i: (i, 0)),
        ],
        out_specs=[
            pl.BlockSpec((block, 3 * width), lambda i: (i, 0)),
            full((1, 3 * width)),
        ],
        out_shape=[
            jax.ShapeDtypeStruct((rows, 3 * width), BF),
            jax.ShapeDtypeStruct((1, 3 * width), F32),
        ],
        compiler_params=params(),
        cost_estimate=cost(8 * rows * width * width, 20 * rows * width),
        name="attend_back",
    )(joined, probs, ctx_grad)


def weight_grads_kernel(tok_ref, joined_ref, small_ref, out_ref):
    step = pl.program_id(0)
    last = pl.num_programs(0) - 1
    shards, part, width = out_ref.shape
    value = tn(tok_ref[...], joined_ref[...])
    cols = pl.ds(pl.multiple_of(step * joined_ref.shape[1], joined_ref.shape[1]), joined_ref.shape[1])
    out_ref[:, :, cols] = value.reshape(shards, part, joined_ref.shape[1]).astype(BF)
    tail = 3 * joined_ref.shape[1]
    if width > tail:

        @pl.when(step == last)
        def _():
            lines = small_ref.shape[1]
            out_ref[:, lines:part, tail:width] = jnp.zeros(
                (shards, part - lines, width - tail), BF
            )
            out_ref[:, 0:lines, tail:width] = small_ref[...].astype(BF)


def weight_grads(tokens, joined_grad, small, shards, extra):
    rows, width = tokens.shape
    shape = (shards, width // shards, 3 * width + extra)
    return pl.pallas_call(
        weight_grads_kernel,
        grid=(3,),
        in_specs=[
            full((rows, width)),
            pl.BlockSpec((rows, width), lambda i: (0, i)),
            full(small.shape),
        ],
        out_specs=full(shape),
        out_shape=jax.ShapeDtypeStruct(shape, BF),
        compiler_params=params(),
        cost_estimate=cost(6 * rows * width * width, 20 * rows * width),
        name="weight_grads",
    )(tokens, joined_grad, small)


def input_kernel(inner_ref, joined_ref, w_ref, out_ref):
    width = inner_ref.shape[1]
    total = inner_ref[...]
    for part in range(3):
        total += nt(joined_ref[:, part * width : (part + 1) * width], w_ref[part])
    out_ref[...] = total.astype(BF)


def input_back(inner, joined_grad, qkv):
    rows, width = inner.shape
    steps = 4
    block = rows // steps
    return pl.pallas_call(
        input_kernel,
        grid=(steps,),
        in_specs=[
            pl.BlockSpec((block, width), lambda i: (i, 0)),
            pl.BlockSpec((block, 3 * width), lambda i: (i, 0)),
            full((3, width, width)),
        ],
        out_specs=pl.BlockSpec((block, width), lambda i: (i, 0)),
        out_shape=jax.ShapeDtypeStruct((rows, width), BF),
        compiler_params=params(),
        cost_estimate=cost(6 * rows * width * width, 12 * rows * width),
        name="input_back",
    )(inner, joined_grad, qkv)


def lay_kernel(plan, chips, reps, part, counts, place_ref, *refs):
    at = 0
    groups = []
    for number in counts:
        groups.append(refs[at : at + number])
        at += number
    sems = refs[-1]
    rep, chip, core = place_ref[0], place_ref[1], place_ref[2]
    copies = []

    def start(source, target):
        copies.append(pltpu.make_async_copy(source, target, sems.at[len(copies)]))
        copies[-1].start()

    plan(start, groups, refs[at:-1], rep, chip, core, chips, reps, part)
    for copy in copies:
        copy.wait()


def blocks_plan(
    put, own, twin, along, across, swapped, depth, first, rep, chip, core, chips, reps, part
):
    for block in range(reps):
        put(own(block), block, chip, core)
        put(twin(block), block, chip, 1 - core)
    for step in range(1, chips):
        source = lax.rem(chip + chips - step, chips)
        rows = pl.ds((step - 1) * depth + first, part)
        for other, block in along.items():
            put(block(step, source, 0), rep ^ other, source, core)
            put(block(step, source, 1), rep ^ other, source, 1 - core)
        for other in across:
            put(across[other].at[rows], rep ^ other, source, core)
            put(swapped[other].at[rows], rep ^ other, source, 1 - core)


def wide_put(start, out_ref, part):
    def put(source, block, at_chip, at_core):
        row = pl.multiple_of((at_chip * 2 + at_core) * part, part)
        start(source, out_ref.at[block, pl.ds(row, part)])

    return put


def wide_block(ref, width, part):
    return lambda block: ref.at[pl.ds(0, part), pl.ds(block * width, width)]


def first_plan(start, groups, outs, rep, chip, core, chips, reps, part):
    (own, twin), along, across, swapped, (extra,) = groups
    out_ref, more_ref = outs
    width = out_ref.shape[2]

    def near(step, source, side):
        if side == 0:
            return along[step - 1].at[pl.ds(0, part)]
        return swapped[0].at[pl.ds((step - 1) * part, part)]

    blocks_plan(
        wide_put(start, out_ref, part),
        wide_block(own, width, part),
        wide_block(twin, width, part),
        {0: near},
        {at + 1: ref for at, ref in enumerate(across)},
        {at + 1: ref for at, ref in enumerate(swapped[1:])},
        part,
        0,
        rep,
        chip,
        core,
        chips,
        reps,
        part,
    )
    tail = pl.ds(part, 16)
    cols = pl.ds(0, width)
    start(own.at[tail, cols], more_ref.at[chip * 2 + core])
    start(twin.at[tail, cols], more_ref.at[chip * 2 + 1 - core])
    for step in range(1, chips):
        source = lax.rem(chip + chips - step, chips)
        start(along[step - 1].at[tail], more_ref.at[source * 2 + core])
        start(extra.at[pl.ds((step - 1) * 16, 16)], more_ref.at[source * 2 + 1 - core])


def second_plan(start, groups, outs, rep, chip, core, chips, reps, part):
    (up, up_twin, down, down_twin), (chain,), across, swapped = groups
    up_ref, down_ref = outs
    width = up_ref.shape[2]
    where = (rep, chip, core, chips, reps, part)

    def chained(first):
        def block(step, source, side):
            shard = source * 2 + (core if side == 0 else 1 - core)
            return chain.at[shard, pl.ds(first, part)]

        return block

    across = dict(zip(NEAR, across))
    swapped = dict(zip(NEAR, swapped))
    blocks_plan(
        wide_put(start, up_ref, part),
        wide_block(up, width, part),
        wide_block(up_twin, width, part),
        {0: chained(0), FAR: chained(2 * part)},
        across,
        swapped,
        2 * part,
        0,
        *where,
    )

    def put(source, block, at_chip, at_core):
        row = pl.multiple_of(block * part, part)
        start(source, down_ref.at[at_chip * 2 + at_core, pl.ds(row, part)])

    def tall(ref):
        return lambda block: ref.at[pl.ds(block * part, part)]

    blocks_plan(
        put,
        tall(down),
        tall(down_twin),
        {0: chained(part), FAR: chained(3 * part)},
        across,
        swapped,
        2 * part,
        part,
        *where,
    )


def lay(plan, place, groups, shapes, copies, part, chips, reps):
    anywhere = pl.BlockSpec(memory_space=pl.ANY)
    inputs = [ref for group in groups for ref in group]
    return pl.pallas_call(
        functools.partial(
            lay_kernel, plan, chips, reps, part, [len(group) for group in groups]
        ),
        in_specs=[pl.BlockSpec(memory_space=pltpu.SMEM)] + [anywhere] * len(inputs),
        out_specs=[pl.BlockSpec(memory_space=pltpu.VMEM)] * len(shapes),
        out_shape=[jax.ShapeDtypeStruct(shape, BF) for shape in shapes],
        scratch_shapes=[pltpu.SemaphoreType.DMA((copies,))],
        compiler_params=pltpu.CompilerParams(vmem_limit_bytes=VMEM_BYTES),
        cost_estimate=cost(0, 4 * sum(math.prod(shape) for shape in shapes)),
        name="lay",
    )(place, *inputs)


LANES = 128


def pack_vectors(rows, up_bias, class_weight):
    part = rows[0].shape[0]
    lines = [row[None] for row in rows[:8]] + [class_weight.T] + [row[None] for row in rows[8:]]
    pieces = up_bias.shape[0] // part
    lines += [up_bias[None, at * part : (at + 1) * part] for at in range(pieces)]
    return jnp.concatenate(lines, axis=0)


def move(values, reps, chips, target):
    pairs = []
    for rep in range(reps):
        for chip in range(chips):
            for core in range(2):
                to_rep, to_chip, to_core = target(rep, chip, core)
                pairs.append(
                    (
                        (rep * chips + chip) * 2 + core,
                        (to_rep * chips + to_chip) * 2 + to_core,
                    )
                )
    return lax.ppermute(values, ("rep", "fsdp"), pairs)


def along_chips(step, chips):
    return lambda rep, chip, core: (rep, (chip + step) % chips, core)


def across_reps(other):
    return lambda rep, chip, core: (rep ^ other, chip, core)


def to_twin(rep, chip, core):
    return rep, chip, 1 - core


def after(values, *gates):
    return lax.optimization_barrier((values, *gates))[0]


def along_z(mine, reps, chips):
    return [move(mine, reps, chips, along_chips(step, chips)) for step in range(1, chips)]


def over_reps(stacked, reps, chips, others):
    return [move(stacked, reps, chips, across_reps(other)) for other in others]


def pick(parts, at):
    return lax.dynamic_index_in_dim(parts, at, axis=0, keepdims=False)


def in_order(rep, reps, own, others, axis):
    blocks = jnp.stack([own] + others)
    return jnp.concatenate([pick(blocks, rep ^ at) for at in range(reps)], axis=axis)


class Reduction:
    def __init__(self, place, keep, send, reps, chips, by_chain=False):
        self.rep, self.chip = place[0], place[1]
        self.reps, self.chips = reps, chips
        self.shape = (chips, reps, keep.shape[1] // reps, keep.shape[2])
        self.keep = keep.reshape(self.shape)
        self.others_of = range(1, reps)
        self.far = None
        if by_chain:
            self.others_of = NEAR
            first = place[2] == 0
            kept = lax.dynamic_index_in_dim(self.keep, self.rep ^ FAR, axis=1, keepdims=False)
            sent = lax.dynamic_index_in_dim(
                send.reshape(self.shape), self.rep ^ FAR, axis=1, keepdims=False
            )
            pair = jnp.stack(
                [jnp.where(first, kept, sent), jnp.where(first, sent, kept)], axis=1
            )
            self.far = lax.psum_scatter(
                pair.reshape(-1, keep.shape[2]), "fsdp", scatter_dimension=0, tiled=True
            )
        self.got = move(send, reps, chips, to_twin)

    def at_rep(self, at):
        kept = lax.dynamic_index_in_dim(self.keep, at, axis=1, keepdims=False)
        came = lax.dynamic_index_in_dim(
            self.got.reshape(self.shape), at, axis=1, keepdims=False
        )
        return kept.astype(F32) + came.astype(F32)

    def over_reps(self, *gates):
        if gates:
            self.got = after(self.got, *gates)
        self.arrived = [
            move(
                self.at_rep(self.rep ^ other).astype(BF),
                self.reps,
                self.chips,
                across_reps(other),
            )
            for other in self.others_of
        ]

    def over_chips(self, *gates):
        if gates:
            self.arrived = [after(block, *gates) for block in self.arrived]
        mine = self.at_rep(self.rep)

        def both_at(at):
            total = pick(mine, at)
            for block in self.arrived:
                total = total + pick(block, at).astype(F32)
            return total

        self.total = both_at(self.chip)
        if self.far is not None:
            came = move(self.far, self.reps, self.chips, across_reps(FAR))
            self.total = self.total + came.astype(F32)
        self.passed = [
            move(
                both_at(lax.rem(self.chip + step, self.chips)).astype(BF),
                self.reps,
                self.chips,
                along_chips(step, self.chips),
            )
            for step in range(1, self.chips)
        ]

    def share(self, *gates):
        if gates:
            self.passed = [after(block, *gates) for block in self.passed]
        total = self.total
        for block in self.passed:
            total = total + block.astype(F32)
        self.total = total.astype(BF)
        self.others = [
            move(self.total, self.reps, self.chips, across_reps(other))
            for other in range(1, self.reps)
        ]

    def result(self):
        return in_order(self.rep, self.reps, self.total, self.others, 0).astype(F32)


def sum_over_reps(place, rows, reps, chips):
    rep = place[0]
    parts = rows.reshape(reps, -1, rows.shape[1])
    total = pick(parts, rep).astype(F32)
    for other in range(1, reps):
        there = pick(parts, rep ^ other)
        total = total + move(there, reps, chips, across_reps(other)).astype(F32)
    total = total.astype(BF)
    others = [move(total, reps, chips, across_reps(other)) for other in range(1, reps)]
    return in_order(rep, reps, total, others, 0)


def per_device(
    tokens,
    exit_layer,
    qkv_weight,
    query_bias,
    value_bias,
    out_weight,
    out_bias,
    attn_gain,
    attn_shift,
    up_weight,
    up_bias,
    down_weight,
    down_bias,
    block_gain,
    block_shift,
    pool_weight,
    pool_bias,
    class_weight,
    class_bias,
    output_grad,
    logit_grad,
):
    reps = lax.axis_size("rep")
    shards = lax.axis_size("fsdp")
    mine = lax.axis_index("fsdp")
    rows, width = tokens.shape
    count = exit_layer.shape[0]
    length = rows // count
    classes = class_weight.shape[1]
    part = out_weight.shape[0]
    hidden = up_weight.shape[1]

    def gather(shard):
        return lax.all_gather(shard, "fsdp", axis=0, tiled=True)

    packed = pack_vectors(
        [
            query_bias,
            value_bias,
            out_bias,
            attn_gain,
            attn_shift,
            down_bias,
            block_gain,
            block_shift,
            pool_bias,
        ],
        up_bias,
        class_weight,
    )
    joint_own = jnp.concatenate([qkv_weight, out_weight], axis=1)
    deep = down_weight.shape[0]
    chips = shards // 2
    place = jnp.stack([lax.axis_index("rep"), mine // 2, mine % 2]).astype(jnp.int32)
    direct = (
        part % 16 == 0
        and reps & (reps - 1) == 0
        and reps * width == hidden
        and reps == 4
        and packed.shape[0] <= 16
    )
    if direct:
        lines = packed.shape[0]
        held = jnp.pad(packed, ((0, 16 - lines), (0, width - part)))
        own = jnp.concatenate([joint_own, jnp.tile(held, (1, reps))], axis=0)
        rep = place[0]

        def block_of(weights, at):
            return lax.dynamic_slice_in_dim(weights, at * width, width, axis=1)

        def second_of(at):
            return [
                block_of(up_weight, at),
                lax.dynamic_slice_in_dim(down_weight, at * part, part, axis=0),
            ]

        along = along_z(block_of(own, rep), reps, chips)
        chain = gather(jnp.concatenate(second_of(rep) + second_of(rep ^ FAR), axis=0))
        chain = chain.reshape(chips, 2, 4 * part, width)
        twin = move(own, reps, chips, to_twin)
        stacked = jnp.concatenate([rows_[:part] for rows_ in along], axis=0)
        across = over_reps(stacked, reps, chips, range(1, reps))
        swapped = [move(rows_, reps, chips, to_twin) for rows_ in [stacked] + across]
        extra = move(
            jnp.concatenate([rows_[part:] for rows_ in along], axis=0), reps, chips, to_twin
        )
        up_twin = move(up_weight, reps, chips, to_twin)
        down_twin = move(down_weight, reps, chips, to_twin)
        pool = gather(after(pool_weight, chain))
        mine_chain = lax.dynamic_index_in_dim(chain, place[2], axis=1, keepdims=False)
        second_stacked = jnp.concatenate(
            [
                pick(mine_chain, lax.rem(place[1] + chips - step, chips))[: 2 * part]
                for step in range(1, chips)
            ],
            axis=0,
        )
        second_across = over_reps(after(second_stacked, *across), reps, chips, NEAR)
        joint, small = lay(
            first_plan,
            place,
            [
                [own, twin],
                along,
                across,
                swapped,
                [extra],
            ],
            [(reps, width, width), (shards, 16, width)],
            2 * chips * (reps + 1),
            part,
            chips,
            reps,
        )
        small = small[:, :lines, :part]
        down_block = (width // deep, deep, width)
    else:
        small = gather(packed[None])
        pool = gather(pool_weight)
        joint = jnp.stack(jnp.split(gather(joint_own), 4, axis=1))
        up = jnp.stack(jnp.split(gather(up_weight), hidden // width, axis=1))
        down = gather(down_weight).reshape(-1, width, width)
        down_block = (1, width, width)
    vec = small[:, :VECTOR_ROWS].transpose(1, 0, 2).reshape(VECTOR_ROWS, width).astype(F32)
    vec = jnp.pad(vec, ((0, 16 - VECTOR_ROWS), (0, 0)))
    up_row = small[:, VECTOR_ROWS:].reshape(1, hidden).astype(F32)
    bias_row = jnp.concatenate([vec[:1], jnp.zeros((1, width), F32), vec[1:2]], axis=1)

    joined, probs, ctx = attend(tokens, joint, bias_row, length)
    if direct:
        second_swapped = [
            move(after(rows_, ctx), reps, chips, to_twin) for rows_ in second_across
        ]
        up, down = lay(
            second_plan,
            place,
            [
                [up_weight, up_twin, down_weight, down_twin],
                [chain.reshape(shards, 4 * part, width)],
                second_across,
                second_swapped,
            ],
            [(reps, width, width), (shards, deep, width)],
            4 * chips * reps,
            part,
            chips,
            reps,
        )
    low, act, slope, unit1, scale1, unit2, scale2, output = feed(
        exit_layer, tokens, ctx, joint, vec, up, up_row, down, down_block, length
    )
    class_bias_row = jnp.pad(class_bias.astype(F32), (0, 8 - classes))[None]
    logit_grad_rows = jnp.pad(logit_grad, ((0, 0), (0, 8 - classes)))
    outer, branch, low_grad, exit_sums, class_grad, logits, stats = leave(
        exit_layer,
        output,
        unit2,
        scale2,
        output_grad,
        pool,
        vec,
        class_bias_row,
        logit_grad_rows,
        act,
        full((width, width)),
        shards,
        length,
        classes,
    )
    up_keep, up_send, up_sum, inner, attended, ctx_grad, feed_sums = feed_back(
        place, chips, branch, slope, low, down, down_block, up, outer, unit1, scale1, joint, vec, ctx
    )
    if direct:
        up_red = Reduction(place, up_keep, up_send, reps, chips)
    joined_grad, joined_sum = attend_back(joined, probs, ctx_grad, length)
    joined_seen = joined_grad
    if direct:
        up_red.over_reps(joined_grad)
        joined_seen = after(joined_grad, up_red.got)
    sums = jnp.concatenate(
        [
            joined_sum.reshape(3, width)[::2],
            feed_sums,
            exit_sums,
            class_grad[:classes],
        ],
        axis=0,
    )
    lines = sums.shape[0]
    own_sums = sums.reshape(lines, shards, part).transpose(1, 0, 2).reshape(shards, lines * part)
    own_sums = jnp.concatenate([own_sums, up_sum.reshape(shards, deep)], axis=1)
    used = own_sums.shape[1]
    seqs_total = count * reps * shards
    figures = jnp.concatenate([stats[0, :1], stats[1, :classes]])
    slots = reps * shards * figures.shape[0] * 3
    direct = direct and used + slots <= part * LANES
    small_lines = 16
    if direct:
        high = figures.astype(BF).astype(F32)
        middle = (figures - high).astype(BF).astype(F32)
        lowest = figures - high - middle
        split = jnp.concatenate([high, middle, lowest])
        slot = lax.axis_index("rep") * shards + mine
        lone = jnp.where(
            jnp.arange(reps * shards)[:, None] == slot, split[None], 0.0
        ).reshape(1, slots)
        row = jnp.concatenate([own_sums, jnp.broadcast_to(lone, (shards, slots))], axis=1)
        small_lines = -(-row.shape[1] // (LANES * 16)) * 16
        row = jnp.pad(row, ((0, 0), (0, small_lines * LANES - row.shape[1])))
        row = row.reshape(shards, small_lines, LANES)
    else:
        row = jnp.zeros((shards, small_lines, LANES), F32)
    joint_grad = weight_grads(tokens, joined_seen, row, shards, LANES if direct else 0)
    input_grad = input_back(inner, joined_grad, joint)

    def scatter(grad):
        return lax.psum_scatter(grad, "fsdp", scatter_dimension=0, tiled=True)

    low_part = scatter(low_grad.reshape(-1, width))
    if direct:
        joint_grad = after(joint_grad, low_part)
    joint_part = scatter(joint_grad.reshape(width, -1))
    if direct:
        up_red.over_chips(input_grad)
        low_sum = sum_over_reps(place, after(low_part, *up_red.arrived), reps, chips)
        up_red.share()
        joint_sum = sum_over_reps(place, after(joint_part, *up_red.passed), reps, chips)
        low_sum = low_sum.astype(F32)
        joint_sum = joint_sum.astype(F32)
        up_sum = up_red.result()
        small_sum = joint_sum[:small_lines, 3 * width :].reshape(-1)
        total = small_sum[used : used + slots].reshape(-1, figures.shape[0]).sum(axis=0)
    else:
        first = mine % 2 == 0

        def whole_of(kept, sent):
            pair = jnp.stack([jnp.where(first, kept, sent), jnp.where(first, sent, kept)], axis=1)
            return pair.reshape(-1, kept.shape[2])

        joint_sum, low_sum, up_sum = lax.psum(
            (joint_part, low_part, scatter(whole_of(up_keep, up_send))), "rep"
        )
        joint_sum, low_sum, up_sum = (
            joint_sum.astype(F32),
            low_sum.astype(F32),
            up_sum.astype(F32),
        )
        own_sums, total = lax.psum((own_sums, figures), ("rep", "fsdp"))
        small_sum = pick(own_sums, mine)
    own = small_sum[: lines * part].reshape(lines, part)
    return (
        output,
        logits[:, :classes],
        total[0] / seqs_total,
        input_grad,
        joint_sum[:, : 3 * width],
        own[0],
        own[1],
        up_sum[:, hidden:],
        own[4],
        own[2],
        own[3],
        up_sum[:, :hidden],
        small_sum[lines * part : used],
        low_sum[:deep],
        own[7],
        own[5],
        own[6],
        low_sum[deep:],
        own[8],
        own[9 : 9 + classes].T,
        total[1:],
    )


def solution(mesh):
    return jax.shard_map(
        per_device,
        mesh=mesh,
        in_specs=(
            P(("rep", "fsdp"), None),
            P(("rep", "fsdp")),
            P("fsdp", None),
            P("fsdp"),
            P("fsdp"),
            P("fsdp", None),
            P("fsdp"),
            P("fsdp"),
            P("fsdp"),
            P("fsdp", None),
            P("fsdp"),
            P("fsdp", None),
            P("fsdp"),
            P("fsdp"),
            P("fsdp"),
            P("fsdp", None),
            P("fsdp"),
            P("fsdp", None),
            P(),
            P(("rep", "fsdp"), None),
            P(("rep", "fsdp"), None),
        ),
        out_specs=(
            P(("rep", "fsdp"), None),
            P(("rep", "fsdp"), None),
            P(),
            P(("rep", "fsdp"), None),
            P("fsdp", None),
            P("fsdp"),
            P("fsdp"),
            P("fsdp", None),
            P("fsdp"),
            P("fsdp"),
            P("fsdp"),
            P("fsdp", None),
            P("fsdp"),
            P("fsdp", None),
            P("fsdp"),
            P("fsdp"),
            P("fsdp"),
            P("fsdp", None),
            P("fsdp"),
            P("fsdp", None),
            P(),
        ),
        check_vma=False,
    )
```

```python
import functools
import math

import jax
import jax.numpy as jnp
from jax import lax
from jax.experimental import pallas as pl
from jax.experimental.pallas import tpu as pltpu
from jax.sharding import PartitionSpec as P

HD = 64
LAYER = 6
PAIR = 2 * HD
NEAR = (1, 2)
FAR = 3
LANES = 128
VMEM_BYTES = 58 * 2**20
BF = jnp.bfloat16
F32 = jnp.float32

QUERY_BIAS, VALUE_BIAS, OUT_BIAS, ATTN_GAIN, ATTN_SHIFT = 0, 1, 2, 3, 4
DOWN_BIAS, BLOCK_GAIN, BLOCK_SHIFT, CLASS_ROWS, POOL_BIAS = 5, 6, 7, 8, 11
VECTOR_ROWS = 12


def nn(left, right):
    return jnp.dot(left, right, preferred_element_type=F32)


def tn(left, right):
    return lax.dot_general(left, right, (((0,), (0,)), ((), ())), preferred_element_type=F32)


def nt(left, right):
    return lax.dot_general(left, right, (((1,), (1,)), ((), ())), preferred_element_type=F32)


def full(shape):
    return pl.BlockSpec(shape, lambda *at: (0,) * len(shape))


def params():
    return pltpu.CompilerParams(
        dimension_semantics=("arbitrary",), vmem_limit_bytes=VMEM_BYTES
    )


def cost(flops, moved, trans=0):
    return pl.CostEstimate(flops=flops, bytes_accessed=moved, transcendentals=trans)


def split_heads(pair):
    lane = lax.broadcasted_iota(jnp.int32, pair.shape, 1)
    zero = jnp.zeros_like(pair)
    return jnp.concatenate(
        [jnp.where(lane < HD, pair, zero), jnp.where(lane < HD, zero, pair)], axis=0
    )


def norm_stats(values):
    center = values - jnp.mean(values, axis=-1, keepdims=True)
    spread = jnp.mean(center * center, axis=-1, keepdims=True)
    scale = lax.rsqrt(spread + 1e-06)
    return center * scale, scale


def norm_back(grad, unit, scale, gain):
    inner = grad * gain
    first = jnp.mean(inner, axis=-1, keepdims=True)
    second = jnp.mean(inner * unit, axis=-1, keepdims=True)
    return scale * (inner - first - unit * second)


def gelu_parts(values):
    size = jnp.abs(values)
    t = 1.0 / (1.0 + 0.23164189 * size)
    bell = jnp.exp(-0.5 * values * values)
    poly = t * (
        0.127414796
        + t * (-0.142248368 + t * (0.7107068705 + t * (-0.7265760135 + t * 0.5307027145)))
    )
    tail = poly * bell
    below = jnp.where(values >= 0.0, 1.0 - tail, tail)
    return values * below, below + values * (bell * 0.3989422804014327)


def attend_kernel(length, tok_ref, w_ref, vec_ref, joined_ref, probs_ref, ctx_ref):
    rows, width = ctx_ref.shape
    pairs = width // PAIR
    for part in range(3):
        cols = slice(part * width, (part + 1) * width)
        value = nn(tok_ref[...], w_ref[part])
        if part == 0:
            value += vec_ref[QUERY_BIAS : QUERY_BIAS + 1]
        elif part == 2:
            value += vec_ref[VALUE_BIAS : VALUE_BIAS + 1]
        joined_ref[:, cols] = value.astype(BF)

    def one(seq, carry):
        at = pl.ds(pl.multiple_of(seq * length, length), length)
        for pair in range(pairs):
            cols = slice(pair * PAIR, (pair + 1) * PAIR)
            query = joined_ref[at, cols] * jnp.asarray(0.125, BF)
            keys = split_heads(joined_ref[at, width + pair * PAIR : width + (pair + 1) * PAIR])
            vals = split_heads(
                joined_ref[at, 2 * width + pair * PAIR : 2 * width + (pair + 1) * PAIR]
            )
            scores = nt(keys, query)
            halves = []
            for head in range(2):
                part = scores[head * length : (head + 1) * length]
                part = jnp.exp(part - jnp.max(part, axis=0, keepdims=True))
                part = part * (1.0 / jnp.sum(part, axis=0, keepdims=True))
                halves.append(part.astype(BF))
            probs = jnp.concatenate(halves, axis=0)
            probs_ref[seq, pair] = probs
            ctx_ref[at, cols] = tn(probs, vals).astype(BF)
        return carry

    lax.fori_loop(0, rows // length, one, 0)


def attend(tokens, qkv, vec, length):
    rows, width = tokens.shape
    count = rows // length
    steps = 2
    block = rows // steps
    pairs = width // PAIR
    return pl.pallas_call(
        functools.partial(attend_kernel, length),
        grid=(steps,),
        in_specs=[
            pl.BlockSpec((block, width), lambda i: (i, 0)),
            full((3, width, width)),
            full(vec.shape),
        ],
        out_specs=[
            pl.BlockSpec((block, 3 * width), lambda i: (i, 0)),
            pl.BlockSpec((count // steps, pairs, 2 * length, length), lambda i: (i, 0, 0, 0)),
            pl.BlockSpec((block, width), lambda i: (i, 0)),
        ],
        out_shape=[
            jax.ShapeDtypeStruct((rows, 3 * width), BF),
            jax.ShapeDtypeStruct((count, pairs, 2 * length, length), BF),
            jax.ShapeDtypeStruct((rows, width), BF),
        ],
        compiler_params=params(),
        cost_estimate=cost(8 * rows * width * width, 20 * rows * width, rows * width),
        name="attend",
    )(tokens, qkv, vec)


def feed_kernel(
    length,
    exit_ref,
    tok_ref,
    ctx_ref,
    out_w_ref,
    vec_ref,
    up_ref,
    up_b_ref,
    down_ref,
    low_ref,
    act_ref,
    slope_ref,
    unit1_ref,
    scale1_ref,
    unit2_ref,
    scale2_ref,
    output_ref,
    acc_ref,
):
    step = pl.program_id(0)
    rows = tok_ref.shape[0]
    sub = 256

    @pl.when(step == 0)
    def _():
        for m in range(rows // sub):
            at = slice(m * sub, (m + 1) * sub)
            inner = tok_ref[at].astype(F32) + (
                nn(ctx_ref[at], out_w_ref[0]) + vec_ref[OUT_BIAS : OUT_BIAS + 1]
            )
            unit, scale = norm_stats(inner)
            first = unit * vec_ref[ATTN_GAIN : ATTN_GAIN + 1] + vec_ref[ATTN_SHIFT : ATTN_SHIFT + 1]
            unit1_ref[at] = unit.astype(BF)
            scale1_ref[at] = scale
            low_ref[at] = first.astype(BF)
            acc_ref[at] = first + vec_ref[DOWN_BIAS : DOWN_BIAS + 1]

    down = down_ref[...].reshape(up_ref.shape[1:])
    for m in range(rows // sub):
        at = slice(m * sub, (m + 1) * sub)
        hidden = nn(low_ref[at], up_ref[0]) + up_b_ref[...]
        act, slope = gelu_parts(hidden)
        act = act.astype(BF)
        act_ref[at] = act
        slope_ref[at] = slope.astype(BF)
        acc_ref[at] += nn(act, down)

    @pl.when(step == pl.num_programs(0) - 1)
    def _():
        for seq in range(rows // length):
            at = slice(seq * length, (seq + 1) * length)
            active = (exit_ref[seq] >= LAYER).astype(F32)
            unit, scale = norm_stats(acc_ref[at])
            unit2_ref[at] = unit.astype(BF)
            scale2_ref[at] = scale
            result = (
                unit * vec_ref[BLOCK_GAIN : BLOCK_GAIN + 1] + vec_ref[BLOCK_SHIFT : BLOCK_SHIFT + 1]
            ) * active
            output_ref[at] = result.astype(BF)


def feed(exit_layer, tokens, ctx, out_w, vec, up, up_bias, down, down_block, length):
    rows, width = tokens.shape
    steps = up.shape[0]
    hidden = steps * width
    whole = full((rows, width))
    return pl.pallas_call(
        functools.partial(feed_kernel, length),
        grid=(steps,),
        in_specs=[
            pl.BlockSpec(memory_space=pltpu.SMEM),
            whole,
            whole,
            pl.BlockSpec((1, width, width), lambda i: (3, 0, 0)),
            full(vec.shape),
            pl.BlockSpec((1, width, width), lambda i: (i, 0, 0)),
            pl.BlockSpec((1, width), lambda i: (0, i)),
            pl.BlockSpec(down_block, lambda i: (i, 0, 0)),
        ],
        out_specs=[
            whole,
            pl.BlockSpec((rows, width), lambda i: (0, i)),
            pl.BlockSpec((rows, width), lambda i: (0, i)),
            whole,
            full((rows, 1)),
            whole,
            full((rows, 1)),
            whole,
        ],
        out_shape=[
            jax.ShapeDtypeStruct((rows, width), BF),
            jax.ShapeDtypeStruct((rows, hidden), BF),
            jax.ShapeDtypeStruct((rows, hidden), BF),
            jax.ShapeDtypeStruct((rows, width), BF),
            jax.ShapeDtypeStruct((rows, 1), F32),
            jax.ShapeDtypeStruct((rows, width), BF),
            jax.ShapeDtypeStruct((rows, 1), F32),
            jax.ShapeDtypeStruct((rows, width), BF),
        ],
        scratch_shapes=[pltpu.VMEM((rows, width), F32)],
        compiler_params=params(),
        cost_estimate=cost(18 * rows * width * width, 40 * rows * width, 8 * rows * width),
        name="feed",
    )(exit_layer, tokens, ctx, out_w, vec, up, up_bias, down)


def leave_kernel(
    length,
    classes,
    exit_ref,
    output_ref,
    unit2_ref,
    scale2_ref,
    grad_ref,
    pool_ref,
    vec_ref,
    class_bias_ref,
    logit_grad_ref,
    act_ref,
    outer_ref,
    branch_ref,
    joint_grad_ref,
    sums_ref,
    class_grad_ref,
    logits_ref,
    stats_ref,
    lead_ref,
    pool_grad_ref,
):
    step = pl.program_id(0)
    rows, width = output_ref.shape
    pool = pool_ref[...].reshape(width, width)
    count = rows // length

    @pl.when(step == 0)
    def _():
        place = lax.broadcasted_iota(jnp.int32, (count, 1), 0)
        active = jnp.zeros((count, 1), F32)
        for seq in range(count):
            on = (exit_ref[seq] >= LAYER).astype(F32)
            active = jnp.where(place == seq, on, active)
        leading = jnp.concatenate(
            [output_ref[seq * length : seq * length + 1].astype(F32) for seq in range(count)],
            axis=0,
        ).astype(BF)
        pooled = jnp.tanh(nn(leading, pool) + vec_ref[POOL_BIAS : POOL_BIAS + 1])
        pooled_low = pooled.astype(BF)
        used = lax.broadcasted_iota(jnp.int32, (8, width), 0) < classes
        class_rows = jnp.where(used, vec_ref[CLASS_ROWS : CLASS_ROWS + 8], 0.0).astype(BF)
        raw = nt(pooled_low, class_rows) + class_bias_ref[...]
        lane = lax.broadcasted_iota(jnp.int32, raw.shape, 1) < classes
        top = jnp.max(jnp.where(lane, raw, -jnp.inf), axis=-1, keepdims=True)
        spread = jnp.where(lane, jnp.exp(raw - top), 0.0)
        logprob = raw - top - jnp.log(jnp.sum(spread, axis=-1, keepdims=True))
        entropy = -jnp.sum(
            jnp.where(lane, jnp.exp(logprob) * logprob, 0.0), axis=-1, keepdims=True
        )
        logits_ref[...] = raw * active
        class_grad = (logit_grad_ref[...].astype(F32) * active).astype(BF)
        stats_ref[0:1] = jnp.broadcast_to(jnp.sum(entropy * active, axis=0, keepdims=True), (1, 8))
        stats_ref[1:2] = jnp.sum(class_grad.astype(F32), axis=0, keepdims=True)
        class_grad_ref[...] = tn(class_grad, pooled_low)
        pooled_grad = nn(class_grad, class_rows)
        pre_grad = (pooled_grad * (1.0 - pooled * pooled)).astype(BF)
        sums_ref[3:4] = jnp.sum(pre_grad.astype(F32), axis=0, keepdims=True)
        pool_grad_ref[...] = tn(leading, pre_grad).reshape(pool_grad_ref.shape).astype(BF)
        lead_ref[...] = nt(pre_grad, pool)
        head = lax.broadcasted_iota(jnp.int32, (length, 1), 0) == 0
        gain = vec_ref[BLOCK_GAIN : BLOCK_GAIN + 1]
        gain_sum = jnp.zeros((1, width), F32)
        shift_sum = jnp.zeros((1, width), F32)
        bias_sum = jnp.zeros((1, width), F32)
        for seq in range(count):
            at = slice(seq * length, (seq + 1) * length)
            on = (exit_ref[seq] >= LAYER).astype(F32)
            top_grad = (
                grad_ref[at].astype(F32) + jnp.where(head, lead_ref[seq : seq + 1], 0.0)
            ) * on
            unit = unit2_ref[at].astype(F32)
            outer = norm_back(top_grad, unit, scale2_ref[at], gain)
            branch = outer.astype(BF)
            outer_ref[at] = outer
            branch_ref[at] = branch
            gain_sum += jnp.sum(top_grad * unit, axis=0, keepdims=True)
            shift_sum += jnp.sum(top_grad, axis=0, keepdims=True)
            bias_sum += jnp.sum(branch.astype(F32), axis=0, keepdims=True)
        sums_ref[0:1] = gain_sum
        sums_ref[1:2] = shift_sum
        sums_ref[2:3] = bias_sum

    @pl.when(step > 0)
    def _():
        few, both, _ = joint_grad_ref.shape
        deep = width // few
        value = tn(act_ref[...], branch_ref[...])
        for at in range(few):
            joint_grad_ref[at, 0:deep] = value[at * deep : (at + 1) * deep].astype(BF)
            joint_grad_ref[at, deep:both] = pool_grad_ref[(step - 1) * few + at]


def leave(
    exit_layer, output, unit2, scale2, output_grad, pool, vec, class_bias, logit_grad, act,
    pool_spec, shards, length, classes,
):
    rows, width = output.shape
    count = rows // length
    hidden = act.shape[1]
    steps = hidden // width
    few = shards // steps
    both = (hidden + width) // shards
    whole = full((rows, width))
    return pl.pallas_call(
        functools.partial(leave_kernel, length, classes),
        grid=(steps + 1,),
        in_specs=[
            pl.BlockSpec(memory_space=pltpu.SMEM),
            whole,
            whole,
            full((rows, 1)),
            whole,
            pool_spec,
            full(vec.shape),
            full(class_bias.shape),
            full(logit_grad.shape),
            pl.BlockSpec((rows, width), lambda i: (0, jnp.maximum(i - 1, 0))),
        ],
        out_specs=[
            whole,
            whole,
            pl.BlockSpec((few, both, width), lambda i: (jnp.maximum(i - 1, 0), 0, 0)),
            full((4, width)),
            full((8, width)),
            full((count, 8)),
            full((2, 8)),
        ],
        out_shape=[
            jax.ShapeDtypeStruct((rows, width), F32),
            jax.ShapeDtypeStruct((rows, width), BF),
            jax.ShapeDtypeStruct((shards, both, width), BF),
            jax.ShapeDtypeStruct((4, width), F32),
            jax.ShapeDtypeStruct((8, width), F32),
            jax.ShapeDtypeStruct((count, 8), F32),
            jax.ShapeDtypeStruct((2, 8), F32),
        ],
        scratch_shapes=[
            pltpu.VMEM((count, width), F32),
            pltpu.VMEM((shards, width // shards, width), BF),
        ],
        compiler_params=params(),
        cost_estimate=cost(8 * rows * width * width, 30 * rows * width),
        name="leave",
    )(
        exit_layer, output, unit2, scale2, output_grad, pool, vec, class_bias, logit_grad, act
    )


def split_cores(value, place_ref, keep_ref, send_ref):
    chips, part, _ = keep_ref.shape
    first = place_ref[2] == 0
    for chip in range(chips):
        even = value[2 * chip * part : (2 * chip + 1) * part]
        odd = value[(2 * chip + 1) * part : (2 * chip + 2) * part]
        keep_ref[chip] = jnp.where(first, even, odd).astype(BF)
        send_ref[chip] = jnp.where(first, odd, even).astype(BF)


def feed_back_kernel(
    place_ref,
    branch_ref,
    slope_ref,
    low_ref,
    down_ref,
    up_ref,
    outer_ref,
    unit1_ref,
    scale1_ref,
    out_w_ref,
    vec_ref,
    ctx_ref,
    keep_ref,
    send_ref,
    up_sum_ref,
    inner_ref,
    attended_ref,
    ctx_grad_ref,
    sums_ref,
    acc_ref,
    hid_ref,
):
    step = pl.program_id(0)
    rows, width = branch_ref.shape
    sub = 256

    @pl.when(step == 0)
    def _():
        acc_ref[...] = outer_ref[...]

    last = pl.num_programs(0) - 1

    @pl.when(step < last)
    def _():
        total = jnp.zeros((1, width), F32)
        down = down_ref[...].reshape(up_ref.shape[1:])
        for m in range(rows // sub):
            at = slice(m * sub, (m + 1) * sub)
            hid = (nt(branch_ref[at], down) * slope_ref[at].astype(F32)).astype(BF)
            hid_ref[at] = hid
            total += jnp.sum(hid.astype(F32), axis=0, keepdims=True)
            acc_ref[at] += nt(hid, up_ref[0])
        up_sum_ref[...] = total
        split_cores(tn(low_ref[...], hid_ref[...]), place_ref, keep_ref, send_ref)

    @pl.when(step == last)
    def _():
        gain = vec_ref[ATTN_GAIN : ATTN_GAIN + 1]
        gain_sum = jnp.zeros((1, width), F32)
        shift_sum = jnp.zeros((1, width), F32)
        bias_sum = jnp.zeros((1, width), F32)
        for m in range(rows // sub):
            at = slice(m * sub, (m + 1) * sub)
            grad = acc_ref[at]
            unit = unit1_ref[at].astype(F32)
            inner = norm_back(grad, unit, scale1_ref[at], gain)
            attended = inner.astype(BF)
            inner_ref[at] = inner
            attended_ref[at] = attended
            ctx_grad_ref[at] = nt(attended, out_w_ref[0]).astype(BF)
            gain_sum += jnp.sum(grad * unit, axis=0, keepdims=True)
            shift_sum += jnp.sum(grad, axis=0, keepdims=True)
            bias_sum += jnp.sum(attended.astype(F32), axis=0, keepdims=True)
        sums_ref[0:1] = gain_sum
        sums_ref[1:2] = shift_sum
        sums_ref[2:3] = bias_sum
        split_cores(tn(ctx_ref[...], attended_ref[...]), place_ref, keep_ref, send_ref)


def feed_back(place, chips, branch, slope, low, down, down_block, up, outer, unit1, scale1, out_w, vec, ctx):
    rows, width = branch.shape
    hidden = slope.shape[1]
    steps = hidden // width
    whole = full((rows, width))
    end = steps - 1
    part = width // (2 * chips)
    return pl.pallas_call(
        feed_back_kernel,
        grid=(steps + 1,),
        in_specs=[
            pl.BlockSpec(memory_space=pltpu.SMEM),
            whole,
            pl.BlockSpec((rows, width), lambda i: (0, jnp.minimum(i, end))),
            whole,
            pl.BlockSpec(down_block, lambda i: (jnp.minimum(i, end), 0, 0)),
            pl.BlockSpec((1, width, width), lambda i: (jnp.minimum(i, end), 0, 0)),
            whole,
            whole,
            full((rows, 1)),
            pl.BlockSpec((1, width, width), lambda i: (3, 0, 0)),
            full(vec.shape),
            whole,
        ],
        out_specs=[
            pl.BlockSpec((chips, part, width), lambda i: (0, 0, i)),
            pl.BlockSpec((chips, part, width), lambda i: (0, 0, i)),
            pl.BlockSpec((1, width), lambda i: (0, jnp.minimum(i, end))),
            whole,
            whole,
            whole,
            full((3, width)),
        ],
        out_shape=[
            jax.ShapeDtypeStruct((chips, part, hidden + width), BF),
            jax.ShapeDtypeStruct((chips, part, hidden + width), BF),
            jax.ShapeDtypeStruct((1, hidden), F32),
            jax.ShapeDtypeStruct((rows, width), F32),
            jax.ShapeDtypeStruct((rows, width), BF),
            jax.ShapeDtypeStruct((rows, width), BF),
            jax.ShapeDtypeStruct((3, width), F32),
        ],
        scratch_shapes=[pltpu.VMEM((rows, width), F32), pltpu.VMEM((rows, width), BF)],
        compiler_params=params(),
        cost_estimate=cost(28 * rows * width * width, 40 * rows * width),
        name="feed_back",
    )(place, branch, slope, low, down, up, outer, unit1, scale1, out_w, vec, ctx)


def attend_back_kernel(length, joined_ref, probs_ref, ctx_grad_ref, grad_ref, sum_ref):
    rows, width = ctx_grad_ref.shape
    pairs = width // PAIR

    def one(seq, carry):
        at = pl.ds(pl.multiple_of(seq * length, length), length)
        for pair in range(pairs):
            at_q = slice(pair * PAIR, (pair + 1) * PAIR)
            at_k = slice(width + pair * PAIR, width + (pair + 1) * PAIR)
            at_v = slice(2 * width + pair * PAIR, 2 * width + (pair + 1) * PAIR)
            query = joined_ref[at, at_q] * jnp.asarray(0.125, BF)
            queries = split_heads(query)
            keys = split_heads(joined_ref[at, at_k])
            vals = split_heads(joined_ref[at, at_v])
            ctx_grad = ctx_grad_ref[at, at_q]
            ctx_grads = split_heads(ctx_grad)
            probs = probs_ref[seq, pair]
            prob_grad = nt(vals, ctx_grad)
            halves = []
            for head in range(2):
                cut = slice(head * length, (head + 1) * length)
                held = probs[cut].astype(F32)
                part = prob_grad[cut]
                base = jnp.sum(part * held, axis=0, keepdims=True)
                halves.append((held * (part - base)).astype(BF))
            stacked = jnp.concatenate(halves, axis=0)
            beside = jnp.concatenate(halves, axis=1)
            probs_beside = jnp.concatenate([probs[:length], probs[length:]], axis=1)
            grad_ref[at, at_q] = (tn(stacked, keys) * 0.125).astype(BF)
            grad_ref[at, at_k] = nn(beside, queries).astype(BF)
            grad_ref[at, at_v] = nn(probs_beside, ctx_grads).astype(BF)
        return carry

    lax.fori_loop(0, rows // length, one, 0)
    total = jnp.zeros(sum_ref.shape, F32)
    for m in range(rows // length):
        total += jnp.sum(
            grad_ref[m * length : (m + 1) * length].astype(F32), axis=0, keepdims=True
        )

    @pl.when(pl.program_id(0) == 0)
    def _():
        sum_ref[...] = total

    @pl.when(pl.program_id(0) > 0)
    def _():
        sum_ref[...] += total


def attend_back(joined, probs, ctx_grad, length):
    rows, width = ctx_grad.shape
    count = rows // length
    steps = 2
    block = rows // steps
    pairs = width // PAIR
    return pl.pallas_call(
        functools.partial(attend_back_kernel, length),
        grid=(steps,),
        in_specs=[
            pl.BlockSpec((block, 3 * width), lambda i: (i, 0)),
            pl.BlockSpec((count // steps, pairs, 2 * length, length), lambda i: (i, 0, 0, 0)),
            pl.BlockSpec((block, width), lambda i: (i, 0)),
        ],
        out_specs=[
            pl.BlockSpec((block, 3 * width), lambda i: (i, 0)),
            full((1, 3 * width)),
        ],
        out_shape=[
            jax.ShapeDtypeStruct((rows, 3 * width), BF),
            jax.ShapeDtypeStruct((1, 3 * width), F32),
        ],
        compiler_params=params(),
        cost_estimate=cost(8 * rows * width * width, 20 * rows * width),
        name="attend_back",
    )(joined, probs, ctx_grad)


def weight_grads_kernel(tok_ref, joined_ref, small_ref, out_ref):
    step = pl.program_id(0)
    last = pl.num_programs(0) - 1
    shards, part, width = out_ref.shape
    value = tn(tok_ref[...], joined_ref[...])
    cols = pl.ds(pl.multiple_of(step * joined_ref.shape[1], joined_ref.shape[1]), joined_ref.shape[1])
    out_ref[:, :, cols] = value.reshape(shards, part, joined_ref.shape[1]).astype(BF)
    tail = 3 * joined_ref.shape[1]
    if width > tail:

        @pl.when(step == last)
        def _():
            lines = small_ref.shape[1]
            out_ref[:, lines:part, tail:width] = jnp.zeros(
                (shards, part - lines, width - tail), BF
            )
            out_ref[:, 0:lines, tail:width] = small_ref[...].astype(BF)


def weight_grads(tokens, joined_grad, small, shards, extra):
    rows, width = tokens.shape
    shape = (shards, width // shards, 3 * width + extra)
    return pl.pallas_call(
        weight_grads_kernel,
        grid=(3,),
        in_specs=[
            full((rows, width)),
            pl.BlockSpec((rows, width), lambda i: (0, i)),
            full(small.shape),
        ],
        out_specs=full(shape),
        out_shape=jax.ShapeDtypeStruct(shape, BF),
        compiler_params=params(),
        cost_estimate=cost(6 * rows * width * width, 20 * rows * width),
        name="weight_grads",
    )(tokens, joined_grad, small)


def input_kernel(inner_ref, joined_ref, w_ref, out_ref):
    width = inner_ref.shape[1]
    total = inner_ref[...]
    for part in range(3):
        total += nt(joined_ref[:, part * width : (part + 1) * width], w_ref[part])
    out_ref[...] = total.astype(BF)


def input_back(inner, joined_grad, qkv):
    rows, width = inner.shape
    steps = 4
    block = rows // steps
    return pl.pallas_call(
        input_kernel,
        grid=(steps,),
        in_specs=[
            pl.BlockSpec((block, width), lambda i: (i, 0)),
            pl.BlockSpec((block, 3 * width), lambda i: (i, 0)),
            full((3, width, width)),
        ],
        out_specs=pl.BlockSpec((block, width), lambda i: (i, 0)),
        out_shape=jax.ShapeDtypeStruct((rows, width), BF),
        compiler_params=params(),
        cost_estimate=cost(6 * rows * width * width, 12 * rows * width),
        name="input_back",
    )(inner, joined_grad, qkv)


def lay_kernel(plan, chips, reps, part, counts, place_ref, *refs):
    at = 0
    groups = []
    for number in counts:
        groups.append(refs[at : at + number])
        at += number
    sems = refs[-1]
    rep, chip, core = place_ref[0], place_ref[1], place_ref[2]
    copies = []

    def start(source, target):
        copies.append(pltpu.make_async_copy(source, target, sems.at[len(copies)]))
        copies[-1].start()

    finish = plan(start, groups, refs[at:-1], rep, chip, core, chips, reps, part)
    for copy in copies:
        copy.wait()
    if finish is not None:
        finish()


def blocks_plan(
    put, own, twin, along, across, swapped, depth, first, rep, chip, core, chips, reps, part
):
    for block in range(reps):
        put(own(block), block, chip, core)
        put(twin(block), block, chip, 1 - core)
    for step in range(1, chips):
        source = lax.rem(chip + chips - step, chips)
        rows = pl.ds((step - 1) * depth + first, part)
        for other, block in along.items():
            put(block(step, source, 0), rep ^ other, source, core)
            put(block(step, source, 1), rep ^ other, source, 1 - core)
        for other in across:
            put(across[other].at[rows], rep ^ other, source, core)
            put(swapped[other].at[rows], rep ^ other, source, 1 - core)


def wide_put(start, out_ref, part):
    def put(source, block, at_chip, at_core):
        row = pl.multiple_of((at_chip * 2 + at_core) * part, part)
        start(source, out_ref.at[block, pl.ds(row, part)])

    return put


def wide_block(ref, width, part):
    return lambda block: ref.at[pl.ds(0, part), pl.ds(block * width, width)]


def first_plan(start, groups, outs, rep, chip, core, chips, reps, part):
    (own, twin), along, across, swapped, (extra,) = groups
    out_ref, vec_ref, more_ref = outs
    width = out_ref.shape[2]

    def near(step, source, side):
        if side == 0:
            return along[step - 1].at[pl.ds(0, part)]
        return swapped[0].at[pl.ds((step - 1) * part, part)]

    blocks_plan(
        wide_put(start, out_ref, part),
        wide_block(own, width, part),
        wide_block(twin, width, part),
        {0: near},
        {at + 1: ref for at, ref in enumerate(across)},
        {at + 1: ref for at, ref in enumerate(swapped[1:])},
        part,
        0,
        rep,
        chip,
        core,
        chips,
        reps,
        part,
    )
    tail = pl.ds(part, 16)
    cols = pl.ds(0, width)
    start(own.at[tail, cols], more_ref.at[chip * 2 + core])
    start(twin.at[tail, cols], more_ref.at[chip * 2 + 1 - core])
    for step in range(1, chips):
        source = lax.rem(chip + chips - step, chips)
        start(along[step - 1].at[tail], more_ref.at[source * 2 + core])
        start(extra.at[pl.ds((step - 1) * 16, 16)], more_ref.at[source * 2 + 1 - core])

    def finish():
        lane = lax.broadcasted_iota(jnp.int32, (LANES, width), 0)
        place = lax.broadcasted_iota(jnp.int32, (LANES, width), 1)
        total = jnp.zeros((16, width), F32)
        for shard in range(2 * chips):
            there = (place - shard * part == lane) & (lane < part)
            total += nn(more_ref[shard, :, 0:LANES], there.astype(F32).astype(BF))
        vec_ref[...] = total

    return finish


def second_plan(start, groups, outs, rep, chip, core, chips, reps, part):
    (up, up_twin, down, down_twin), (close, far), across, swapped = groups
    up_ref, down_ref = outs
    width = up_ref.shape[2]
    where = (rep, chip, core, chips, reps, part)

    def chained(chain, first):
        def block(step, source, side):
            shard = source * 2 + (core if side == 0 else 1 - core)
            return chain.at[shard, pl.ds(first, part)]

        return block

    across = dict(zip(NEAR, across))
    swapped = dict(zip(NEAR, swapped))
    blocks_plan(
        wide_put(start, up_ref, part),
        wide_block(up, width, part),
        wide_block(up_twin, width, part),
        {0: chained(close, 0), FAR: chained(far, 0)},
        across,
        swapped,
        2 * part,
        0,
        *where,
    )

    def put(source, block, at_chip, at_core):
        row = pl.multiple_of(block * part, part)
        start(source, down_ref.at[at_chip * 2 + at_core, pl.ds(row, part)])

    def tall(ref):
        return lambda block: ref.at[pl.ds(block * part, part)]

    blocks_plan(
        put,
        tall(down),
        tall(down_twin),
        {0: chained(close, part), FAR: chained(far, part)},
        across,
        swapped,
        2 * part,
        part,
        *where,
    )


def lay(plan, place, groups, shapes, scratch, copies, part, chips, reps):
    anywhere = pl.BlockSpec(memory_space=pl.ANY)
    inputs = [ref for group in groups for ref in group]
    return pl.pallas_call(
        functools.partial(
            lay_kernel, plan, chips, reps, part, [len(group) for group in groups]
        ),
        in_specs=[pl.BlockSpec(memory_space=pltpu.SMEM)] + [anywhere] * len(inputs),
        out_specs=[pl.BlockSpec(memory_space=pltpu.VMEM)] * len(shapes),
        out_shape=[jax.ShapeDtypeStruct(shape, kind) for shape, kind in shapes],
        scratch_shapes=[pltpu.VMEM(shape, BF) for shape in scratch]
        + [pltpu.SemaphoreType.DMA((copies,))],
        compiler_params=pltpu.CompilerParams(vmem_limit_bytes=VMEM_BYTES),
        cost_estimate=cost(0, 4 * sum(math.prod(shape) for shape, kind in shapes)),
        name="lay",
    )(place, *inputs)


def pack_vectors(rows, up_bias, class_weight):
    part = rows[0].shape[0]
    lines = [row[None] for row in rows[:8]] + [class_weight.T] + [row[None] for row in rows[8:]]
    pieces = up_bias.shape[0] // part
    lines += [up_bias[None, at * part : (at + 1) * part] for at in range(pieces)]
    return jnp.concatenate(lines, axis=0)


def move(values, reps, chips, target):
    pairs = []
    for rep in range(reps):
        for chip in range(chips):
            for core in range(2):
                to_rep, to_chip, to_core = target(rep, chip, core)
                pairs.append(
                    (
                        (rep * chips + chip) * 2 + core,
                        (to_rep * chips + to_chip) * 2 + to_core,
                    )
                )
    return lax.ppermute(values, ("rep", "fsdp"), pairs)


def along_chips(step, chips):
    return lambda rep, chip, core: (rep, (chip + step) % chips, core)


def across_reps(other):
    return lambda rep, chip, core: (rep ^ other, chip, core)


def to_twin(rep, chip, core):
    return rep, chip, 1 - core


def after(values, *gates):
    return lax.optimization_barrier((values, *gates))[0]


def along_z(mine, reps, chips):
    return [move(mine, reps, chips, along_chips(step, chips)) for step in range(1, chips)]


def over_reps(stacked, reps, chips, others):
    return [move(stacked, reps, chips, across_reps(other)) for other in others]


def pick(parts, at):
    return lax.dynamic_index_in_dim(parts, at, axis=0, keepdims=False)


def in_order(rep, reps, own, others, axis):
    blocks = jnp.stack([own] + others)
    return jnp.concatenate([pick(blocks, rep ^ at) for at in range(reps)], axis=axis)


class Reduction:
    def __init__(self, place, keep, send, reps, chips, by_chain=False):
        self.rep, self.chip = place[0], place[1]
        self.reps, self.chips = reps, chips
        self.shape = (chips, reps, keep.shape[1] // reps, keep.shape[2])
        self.keep = keep.reshape(self.shape)
        self.others_of = range(1, reps)
        self.far = None
        if by_chain:
            self.others_of = NEAR
            first = place[2] == 0
            kept = lax.dynamic_index_in_dim(self.keep, self.rep ^ FAR, axis=1, keepdims=False)
            sent = lax.dynamic_index_in_dim(
                send.reshape(self.shape), self.rep ^ FAR, axis=1, keepdims=False
            )
            pair = jnp.stack(
                [jnp.where(first, kept, sent), jnp.where(first, sent, kept)], axis=1
            )
            self.far = lax.psum_scatter(
                pair.reshape(-1, keep.shape[2]), "fsdp", scatter_dimension=0, tiled=True
            )
        self.got = move(send, reps, chips, to_twin)

    def at_rep(self, at):
        kept = lax.dynamic_index_in_dim(self.keep, at, axis=1, keepdims=False)
        came = lax.dynamic_index_in_dim(
            self.got.reshape(self.shape), at, axis=1, keepdims=False
        )
        return kept.astype(F32) + came.astype(F32)

    def over_reps(self, *gates):
        if gates:
            self.got = after(self.got, *gates)
        self.arrived = [
            move(
                self.at_rep(self.rep ^ other).astype(BF),
                self.reps,
                self.chips,
                across_reps(other),
            )
            for other in self.others_of
        ]

    def over_chips(self, *gates):
        if gates:
            self.arrived = [after(block, *gates) for block in self.arrived]
        mine = self.at_rep(self.rep)

        def both_at(at):
            total = pick(mine, at)
            for block in self.arrived:
                total = total + pick(block, at).astype(F32)
            return total

        self.total = both_at(self.chip)
        if self.far is not None:
            came = move(self.far, self.reps, self.chips, across_reps(FAR))
            self.total = self.total + came.astype(F32)
        self.passed = [
            move(
                both_at(lax.rem(self.chip + step, self.chips)).astype(BF),
                self.reps,
                self.chips,
                along_chips(step, self.chips),
            )
            for step in range(1, self.chips)
        ]

    def share(self, *gates):
        if gates:
            self.passed = [after(block, *gates) for block in self.passed]
        total = self.total
        for block in self.passed:
            total = total + block.astype(F32)
        self.total = total.astype(BF)
        self.others = [
            move(self.total, self.reps, self.chips, across_reps(other))
            for other in range(1, self.reps)
        ]

    def result(self):
        return in_order(self.rep, self.reps, self.total, self.others, 0).astype(F32)


def exchange_reps(place, rows, reps, chips):
    rep = place[0]
    parts = rows.reshape(reps, -1, rows.shape[1])
    total = pick(parts, rep).astype(F32)
    arrived = [
        move(pick(parts, rep ^ other), reps, chips, across_reps(other))
        for other in range(1, reps)
    ]
    for block in arrived:
        total = total + block.astype(F32)
    return total.astype(BF), arrived


def per_device(
    tokens,
    exit_layer,
    qkv_weight,
    query_bias,
    value_bias,
    out_weight,
    out_bias,
    attn_gain,
    attn_shift,
    up_weight,
    up_bias,
    down_weight,
    down_bias,
    block_gain,
    block_shift,
    pool_weight,
    pool_bias,
    class_weight,
    class_bias,
    output_grad,
    logit_grad,
):
    reps = lax.axis_size("rep")
    shards = lax.axis_size("fsdp")
    mine = lax.axis_index("fsdp")
    rows, width = tokens.shape
    count = exit_layer.shape[0]
    length = rows // count
    classes = class_weight.shape[1]
    part = out_weight.shape[0]
    hidden = up_weight.shape[1]

    def gather(shard):
        return lax.all_gather(shard, "fsdp", axis=0, tiled=True)

    packed = pack_vectors(
        [
            query_bias,
            value_bias,
            out_bias,
            attn_gain,
            attn_shift,
            down_bias,
            block_gain,
            block_shift,
            pool_bias,
        ],
        up_bias,
        class_weight,
    )
    joint_own = jnp.concatenate([qkv_weight, out_weight], axis=1)
    deep = down_weight.shape[0]
    chips = shards // 2
    place = jnp.stack([lax.axis_index("rep"), mine // 2, mine % 2]).astype(jnp.int32)
    direct = (
        part % 16 == 0
        and reps & (reps - 1) == 0
        and reps * width == hidden
        and reps == 4
        and packed.shape[0] <= 16
    )
    if direct:
        lines = packed.shape[0]
        held = jnp.pad(packed, ((0, 16 - lines), (0, width - part)))
        own = jnp.concatenate([joint_own, jnp.tile(held, (1, reps))], axis=0)
        rep = place[0]

        def block_of(weights, at):
            return lax.dynamic_slice_in_dim(weights, at * width, width, axis=1)

        def second_of(at):
            return [
                block_of(up_weight, at),
                lax.dynamic_slice_in_dim(down_weight, at * part, part, axis=0),
            ]

        along = along_z(block_of(own, rep), reps, chips)
        chain = gather(after(jnp.concatenate(second_of(rep), axis=0), *along))
        chain = chain.reshape(chips, 2, 2 * part, width)
        twin = move(own, reps, chips, to_twin)
        stacked = jnp.concatenate([rows_[:part] for rows_ in along], axis=0)
        across = over_reps(stacked, reps, chips, range(1, reps))
        far_chain = gather(after(jnp.concatenate(second_of(rep ^ FAR), axis=0), *across))
        swapped = [move(rows_, reps, chips, to_twin) for rows_ in [stacked] + across]
        extra = move(
            jnp.concatenate([rows_[part:] for rows_ in along], axis=0), reps, chips, to_twin
        )
        up_twin = move(up_weight, reps, chips, to_twin)
        down_twin = move(down_weight, reps, chips, to_twin)
        pool = gather(after(pool_weight, far_chain))
        mine_chain = lax.dynamic_index_in_dim(chain, place[2], axis=1, keepdims=False)
        second_stacked = jnp.concatenate(
            [
                pick(mine_chain, lax.rem(place[1] + chips - step, chips))
                for step in range(1, chips)
            ],
            axis=0,
        )
        second_across = over_reps(after(second_stacked, *across), reps, chips, NEAR)
        joint, vec = lay(
            first_plan,
            place,
            [
                [own, twin],
                along,
                across,
                swapped,
                [extra],
            ],
            [((reps, width, width), BF), ((16, width), F32)],
            [(shards, 16, width)],
            2 * chips * (reps + 1),
            part,
            chips,
            reps,
        )
        up_row = (
            vec[VECTOR_ROWS:lines].reshape(-1, shards, part).transpose(1, 0, 2).reshape(1, hidden)
        )
        down_block = (width // deep, deep, width)
    else:
        small = gather(packed[None])
        vec = small[:, :VECTOR_ROWS].transpose(1, 0, 2).reshape(VECTOR_ROWS, width).astype(F32)
        vec = jnp.pad(vec, ((0, 16 - VECTOR_ROWS), (0, 0)))
        up_row = small[:, VECTOR_ROWS:].transpose(0, 1, 2).reshape(1, hidden).astype(F32)
        pool = gather(pool_weight)
        joint = jnp.stack(jnp.split(gather(joint_own), 4, axis=1))
        up = jnp.stack(jnp.split(gather(up_weight), hidden // width, axis=1))
        down = gather(down_weight).reshape(-1, width, width)
        down_block = (1, width, width)
    joined, probs, ctx = attend(tokens, joint, vec, length)
    if direct:
        second_swapped = [
            move(after(rows_, ctx), reps, chips, to_twin) for rows_ in second_across
        ]
        up, down = lay(
            second_plan,
            place,
            [
                [up_weight, up_twin, down_weight, down_twin],
                [
                    chain.reshape(shards, 2 * part, width),
                    far_chain.reshape(shards, 2 * part, width),
                ],
                second_across,
                second_swapped,
            ],
            [((reps, width, width), BF), ((shards, deep, width), BF)],
            [],
            4 * chips * reps,
            part,
            chips,
            reps,
        )
    low, act, slope, unit1, scale1, unit2, scale2, output = feed(
        exit_layer, tokens, ctx, joint, vec, up, up_row, down, down_block, length
    )
    class_bias_row = jnp.pad(class_bias.astype(F32), (0, 8 - classes))[None]
    logit_grad_rows = jnp.pad(logit_grad, ((0, 0), (0, 8 - classes)))
    outer, branch, low_grad, exit_sums, class_grad, logits, stats = leave(
        exit_layer,
        output,
        unit2,
        scale2,
        output_grad,
        pool,
        vec,
        class_bias_row,
        logit_grad_rows,
        act,
        full((width, width)),
        shards,
        length,
        classes,
    )
    up_keep, up_send, up_sum, inner, attended, ctx_grad, feed_sums = feed_back(
        place, chips, branch, slope, low, down, down_block, up, outer, unit1, scale1, joint, vec, ctx
    )
    if direct:
        up_red = Reduction(place, up_keep, up_send, reps, chips)
    joined_grad, joined_sum = attend_back(joined, probs, ctx_grad, length)
    joined_seen = joined_grad
    if direct:
        up_red.over_reps(joined_grad)
        joined_seen = after(joined_grad, up_red.got)
    sums = jnp.concatenate(
        [
            joined_sum.reshape(3, width)[::2],
            feed_sums,
            exit_sums,
            class_grad[:classes],
        ],
        axis=0,
    )
    lines = sums.shape[0]
    own_sums = sums.reshape(lines, shards, part).transpose(1, 0, 2).reshape(shards, lines * part)
    own_sums = jnp.concatenate([own_sums, up_sum.reshape(shards, deep)], axis=1)
    used = own_sums.shape[1]
    seqs_total = count * reps * shards
    figures = jnp.concatenate([stats[0, :1], stats[1, :classes]])
    slots = reps * shards * figures.shape[0] * 3
    direct = direct and used + slots <= part * LANES
    small_lines = 16
    if direct:
        high = figures.astype(BF).astype(F32)
        middle = (figures - high).astype(BF).astype(F32)
        lowest = figures - high - middle
        split = jnp.concatenate([high, middle, lowest])
        slot = lax.axis_index("rep") * shards + mine
        lone = jnp.where(
            jnp.arange(reps * shards)[:, None] == slot, split[None], 0.0
        ).reshape(1, slots)
        row = jnp.concatenate([own_sums, jnp.broadcast_to(lone, (shards, slots))], axis=1)
        small_lines = -(-row.shape[1] // (LANES * 16)) * 16
        row = jnp.pad(row, ((0, 0), (0, small_lines * LANES - row.shape[1])))
        row = row.reshape(shards, small_lines, LANES)
    else:
        row = jnp.zeros((shards, small_lines, LANES), F32)
    joint_grad = weight_grads(tokens, joined_seen, row, shards, LANES if direct else 0)
    if direct:
        inner = after(inner, *up_red.arrived)
    input_grad = input_back(inner, joined_grad, joint)

    def scatter(grad):
        return lax.psum_scatter(grad, "fsdp", scatter_dimension=0, tiled=True)

    low_part = scatter(low_grad.reshape(-1, width))
    if direct:
        joint_grad = after(joint_grad, low_part)
    joint_part = scatter(joint_grad.reshape(width, -1))
    if direct:
        up_red.over_chips()
        low_total, low_arrived = exchange_reps(
            place, after(low_part, *up_red.passed), reps, chips
        )
        up_red.share()
        joint_total, _ = exchange_reps(
            place, after(joint_part, *low_arrived, *up_red.others), reps, chips
        )
        wide = low_total.shape[0] * width // joint_total.shape[0]
        both = jnp.concatenate(
            [joint_total, low_total.reshape(joint_total.shape[0], wide)], axis=1
        )
        others = [move(both, reps, chips, across_reps(other)) for other in range(1, reps)]
        both = in_order(place[0], reps, both, others, 0).astype(F32)
        low_sum = both[:, joint_total.shape[1] :].reshape(deep + part, width)
        joint_sum = both[:, : joint_total.shape[1]]
        up_sum = up_red.result()
        small_sum = joint_sum[:small_lines, 3 * width :].reshape(-1)
        total = small_sum[used : used + slots].reshape(-1, figures.shape[0]).sum(axis=0)
    else:
        first = mine % 2 == 0

        def whole_of(kept, sent):
            pair = jnp.stack([jnp.where(first, kept, sent), jnp.where(first, sent, kept)], axis=1)
            return pair.reshape(-1, kept.shape[2])

        joint_sum, low_sum, up_sum = lax.psum(
            (joint_part, low_part, scatter(whole_of(up_keep, up_send))), "rep"
        )
        joint_sum, low_sum, up_sum = (
            joint_sum.astype(F32),
            low_sum.astype(F32),
            up_sum.astype(F32),
        )
        own_sums, total = lax.psum((own_sums, figures), ("rep", "fsdp"))
        small_sum = pick(own_sums, mine)
    own = small_sum[: lines * part].reshape(lines, part)
    return (
        output,
        logits[:, :classes],
        total[0] / seqs_total,
        input_grad,
        joint_sum[:, : 3 * width],
        own[0],
        own[1],
        up_sum[:, hidden:],
        own[4],
        own[2],
        own[3],
        up_sum[:, :hidden],
        small_sum[lines * part : used],
        low_sum[:deep],
        own[7],
        own[5],
        own[6],
        low_sum[deep:],
        own[8],
        own[9 : 9 + classes].T,
        total[1:],
    )


def solution(mesh):
    return jax.shard_map(
        per_device,
        mesh=mesh,
        in_specs=(
            P(("rep", "fsdp"), None),
            P(("rep", "fsdp")),
            P("fsdp", None),
            P("fsdp"),
            P("fsdp"),
            P("fsdp", None),
            P("fsdp"),
            P("fsdp"),
            P("fsdp"),
            P("fsdp", None),
            P("fsdp"),
            P("fsdp", None),
            P("fsdp"),
            P("fsdp"),
            P("fsdp"),
            P("fsdp", None),
            P("fsdp"),
            P("fsdp", None),
            P(),
            P(("rep", "fsdp"), None),
            P(("rep", "fsdp"), None),
        ),
        out_specs=(
            P(("rep", "fsdp"), None),
            P(("rep", "fsdp"), None),
            P(),
            P(("rep", "fsdp"), None),
            P("fsdp", None),
            P("fsdp"),
            P("fsdp"),
            P("fsdp", None),
            P("fsdp"),
            P("fsdp"),
            P("fsdp"),
            P("fsdp", None),
            P("fsdp"),
            P("fsdp", None),
            P("fsdp"),
            P("fsdp"),
            P("fsdp"),
            P("fsdp", None),
            P("fsdp"),
            P("fsdp", None),
            P(),
        ),
        check_vma=False,
    )
```

```python
import functools
import math

import jax
import jax.numpy as jnp
from jax import lax
from jax.experimental import pallas as pl
from jax.experimental.pallas import tpu as pltpu
from jax.sharding import PartitionSpec as P

HD = 64
LAYER = 6
PAIR = 2 * HD
NEAR = (1, 2)
FAR = 3
LANES = 128
VMEM_BYTES = 58 * 2**20
BF = jnp.bfloat16
F32 = jnp.float32

QUERY_BIAS, VALUE_BIAS, OUT_BIAS, ATTN_GAIN, ATTN_SHIFT = 0, 1, 2, 3, 4
DOWN_BIAS, BLOCK_GAIN, BLOCK_SHIFT, CLASS_ROWS, POOL_BIAS = 5, 6, 7, 8, 11
VECTOR_ROWS = 12


def nn(left, right):
    return jnp.dot(left, right, preferred_element_type=F32)


def tn(left, right):
    return lax.dot_general(left, right, (((0,), (0,)), ((), ())), preferred_element_type=F32)


def nt(left, right):
    return lax.dot_general(left, right, (((1,), (1,)), ((), ())), preferred_element_type=F32)


def full(shape):
    return pl.BlockSpec(shape, lambda *at: (0,) * len(shape))


def params():
    return pltpu.CompilerParams(
        dimension_semantics=("arbitrary",), vmem_limit_bytes=VMEM_BYTES
    )


def cost(flops, moved, trans=0):
    return pl.CostEstimate(flops=flops, bytes_accessed=moved, transcendentals=trans)


def split_heads(pair):
    lane = lax.broadcasted_iota(jnp.int32, pair.shape, 1)
    zero = jnp.zeros_like(pair)
    return jnp.concatenate(
        [jnp.where(lane < HD, pair, zero), jnp.where(lane < HD, zero, pair)], axis=0
    )


def norm_stats(values):
    center = values - jnp.mean(values, axis=-1, keepdims=True)
    spread = jnp.mean(center * center, axis=-1, keepdims=True)
    scale = lax.rsqrt(spread + 1e-06)
    return center * scale, scale


def norm_back(grad, unit, scale, gain):
    inner = grad * gain
    first = jnp.mean(inner, axis=-1, keepdims=True)
    second = jnp.mean(inner * unit, axis=-1, keepdims=True)
    return scale * (inner - first - unit * second)


def gelu_parts(values):
    base = 1.0 + 0.23164189 * jnp.abs(values)
    t = pl.reciprocal(base, approx=True)
    t = t * (2.0 - base * t)
    bell = jnp.exp2((values * values) * -0.7213475204444817)
    poly = t * (
        0.127414796
        + t * (-0.142248368 + t * (0.7107068705 + t * (-0.7265760135 + t * 0.5307027145)))
    )
    tail = poly * bell
    below = jnp.where(values >= 0.0, 1.0 - tail, tail)
    return values * below, below + values * (bell * 0.3989422804014327)


def attend_kernel(length, tok_ref, w_ref, vec_ref, joined_ref, probs_ref, ctx_ref):
    rows, width = ctx_ref.shape
    pairs = width // PAIR
    for part in range(3):
        cols = slice(part * width, (part + 1) * width)
        value = nn(tok_ref[...], w_ref[part])
        if part == 0:
            value += vec_ref[QUERY_BIAS : QUERY_BIAS + 1]
        elif part == 2:
            value += vec_ref[VALUE_BIAS : VALUE_BIAS + 1]
        joined_ref[:, cols] = value.astype(BF)

    def one(seq, carry):
        at = pl.ds(pl.multiple_of(seq * length, length), length)
        scores = []
        for pair in range(pairs):
            query = joined_ref[at, pair * PAIR : (pair + 1) * PAIR] * jnp.asarray(0.125, BF)
            keys = split_heads(joined_ref[at, width + pair * PAIR : width + (pair + 1) * PAIR])
            scores.append(nt(keys, query))
        all_probs = []
        for pair in range(pairs):
            halves = []
            for head in range(2):
                part = scores[pair][head * length : (head + 1) * length]
                part = jnp.exp(part - jnp.max(part, axis=0, keepdims=True))
                part = part * (1.0 / jnp.sum(part, axis=0, keepdims=True))
                halves.append(part.astype(BF))
            probs = jnp.concatenate(halves, axis=0)
            probs_ref[seq, pair] = probs
            all_probs.append(probs)
        for pair in range(pairs):
            vals = split_heads(
                joined_ref[at, 2 * width + pair * PAIR : 2 * width + (pair + 1) * PAIR]
            )
            ctx_ref[at, pair * PAIR : (pair + 1) * PAIR] = tn(all_probs[pair], vals).astype(BF)
        return carry

    lax.fori_loop(0, rows // length, one, 0)


def attend(tokens, qkv, vec, length):
    rows, width = tokens.shape
    count = rows // length
    steps = 2
    block = rows // steps
    pairs = width // PAIR
    return pl.pallas_call(
        functools.partial(attend_kernel, length),
        grid=(steps,),
        in_specs=[
            pl.BlockSpec((block, width), lambda i: (i, 0)),
            full((3, width, width)),
            full(vec.shape),
        ],
        out_specs=[
            pl.BlockSpec((block, 3 * width), lambda i: (i, 0)),
            pl.BlockSpec((count // steps, pairs, 2 * length, length), lambda i: (i, 0, 0, 0)),
            pl.BlockSpec((block, width), lambda i: (i, 0)),
        ],
        out_shape=[
            jax.ShapeDtypeStruct((rows, 3 * width), BF),
            jax.ShapeDtypeStruct((count, pairs, 2 * length, length), BF),
            jax.ShapeDtypeStruct((rows, width), BF),
        ],
        compiler_params=params(),
        cost_estimate=cost(8 * rows * width * width, 20 * rows * width, rows * width),
        name="attend",
    )(tokens, qkv, vec)


def feed_kernel(
    length,
    exit_ref,
    tok_ref,
    ctx_ref,
    out_w_ref,
    vec_ref,
    up_ref,
    up_b_ref,
    down_ref,
    turned_ref,
    act_ref,
    slope_ref,
    unit1_ref,
    scale1_ref,
    unit2_ref,
    scale2_ref,
    output_ref,
    acc_ref,
    low_ref,
):
    step = pl.program_id(0)
    rows = tok_ref.shape[0]
    sub = 256

    @pl.when(step == 0)
    def _():
        for m in range(rows // sub):
            at = slice(m * sub, (m + 1) * sub)
            inner = tok_ref[at].astype(F32) + (
                nn(ctx_ref[at], out_w_ref[0]) + vec_ref[OUT_BIAS : OUT_BIAS + 1]
            )
            unit, scale = norm_stats(inner)
            first = unit * vec_ref[ATTN_GAIN : ATTN_GAIN + 1] + vec_ref[ATTN_SHIFT : ATTN_SHIFT + 1]
            unit1_ref[at] = unit.astype(BF)
            scale1_ref[at] = scale
            low = first.astype(BF)
            low_ref[at] = low
            turned_ref[:, at] = low.T
            acc_ref[at] = first + vec_ref[DOWN_BIAS : DOWN_BIAS + 1]

    down = down_ref[...].reshape(up_ref.shape[1:])
    ahead = nn(low_ref[0:sub], up_ref[0])
    for m in range(rows // sub):
        at = slice(m * sub, (m + 1) * sub)
        hidden = ahead + up_b_ref[...]
        if (m + 1) * sub < rows:
            ahead = nn(low_ref[(m + 1) * sub : (m + 2) * sub], up_ref[0])
        act, slope = gelu_parts(hidden)
        act = act.astype(BF)
        act_ref[:, at] = act.T
        slope_ref[at] = slope.astype(BF)
        acc_ref[at] += nn(act, down)

    @pl.when(step == pl.num_programs(0) - 1)
    def _():
        for seq in range(rows // length):
            at = slice(seq * length, (seq + 1) * length)
            active = (exit_ref[seq] >= LAYER).astype(F32)
            unit, scale = norm_stats(acc_ref[at])
            unit2_ref[at] = unit.astype(BF)
            scale2_ref[at] = scale
            result = (
                unit * vec_ref[BLOCK_GAIN : BLOCK_GAIN + 1] + vec_ref[BLOCK_SHIFT : BLOCK_SHIFT + 1]
            ) * active
            output_ref[at] = result.astype(BF)


def feed(exit_layer, tokens, ctx, out_w, vec, up, up_bias, down, down_block, length):
    rows, width = tokens.shape
    steps = up.shape[0]
    hidden = steps * width
    whole = full((rows, width))
    return pl.pallas_call(
        functools.partial(feed_kernel, length),
        grid=(steps,),
        in_specs=[
            pl.BlockSpec(memory_space=pltpu.SMEM),
            whole,
            whole,
            pl.BlockSpec((1, width, width), lambda i: (3, 0, 0)),
            full(vec.shape),
            pl.BlockSpec((1, width, width), lambda i: (i, 0, 0)),
            pl.BlockSpec((1, width), lambda i: (0, i)),
            pl.BlockSpec(down_block, lambda i: (i, 0, 0)),
        ],
        out_specs=[
            full((width, rows)),
            pl.BlockSpec((width, rows), lambda i: (i, 0)),
            pl.BlockSpec((rows, width), lambda i: (0, i)),
            whole,
            full((rows, 1)),
            whole,
            full((rows, 1)),
            whole,
        ],
        out_shape=[
            jax.ShapeDtypeStruct((width, rows), BF),
            jax.ShapeDtypeStruct((hidden, rows), BF),
            jax.ShapeDtypeStruct((rows, hidden), BF),
            jax.ShapeDtypeStruct((rows, width), BF),
            jax.ShapeDtypeStruct((rows, 1), F32),
            jax.ShapeDtypeStruct((rows, width), BF),
            jax.ShapeDtypeStruct((rows, 1), F32),
            jax.ShapeDtypeStruct((rows, width), BF),
        ],
        scratch_shapes=[pltpu.VMEM((rows, width), F32), pltpu.VMEM((rows, width), BF)],
        compiler_params=params(),
        cost_estimate=cost(18 * rows * width * width, 40 * rows * width, 8 * rows * width),
        name="feed",
    )(exit_layer, tokens, ctx, out_w, vec, up, up_bias, down)


def leave_kernel(
    length,
    classes,
    exit_ref,
    output_ref,
    unit2_ref,
    scale2_ref,
    grad_ref,
    pool_ref,
    vec_ref,
    class_bias_ref,
    logit_grad_ref,
    act_ref,
    outer_ref,
    branch_ref,
    joint_grad_ref,
    sums_ref,
    class_grad_ref,
    logits_ref,
    stats_ref,
    lead_ref,
    pool_grad_ref,
):
    step = pl.program_id(0)
    rows, width = output_ref.shape
    pool = pool_ref[...].reshape(width, width)
    count = rows // length

    @pl.when(step == 0)
    def _():
        place = lax.broadcasted_iota(jnp.int32, (count, 1), 0)
        active = jnp.zeros((count, 1), F32)
        for seq in range(count):
            on = (exit_ref[seq] >= LAYER).astype(F32)
            active = jnp.where(place == seq, on, active)
        leading = jnp.concatenate(
            [output_ref[seq * length : seq * length + 1].astype(F32) for seq in range(count)],
            axis=0,
        ).astype(BF)
        pooled = jnp.tanh(nn(leading, pool) + vec_ref[POOL_BIAS : POOL_BIAS + 1])
        pooled_low = pooled.astype(BF)
        used = lax.broadcasted_iota(jnp.int32, (8, width), 0) < classes
        class_rows = jnp.where(used, vec_ref[CLASS_ROWS : CLASS_ROWS + 8], 0.0).astype(BF)
        raw = nt(pooled_low, class_rows) + class_bias_ref[...]
        lane = lax.broadcasted_iota(jnp.int32, raw.shape, 1) < classes
        top = jnp.max(jnp.where(lane, raw, -jnp.inf), axis=-1, keepdims=True)
        spread = jnp.where(lane, jnp.exp(raw - top), 0.0)
        logprob = raw - top - jnp.log(jnp.sum(spread, axis=-1, keepdims=True))
        entropy = -jnp.sum(
            jnp.where(lane, jnp.exp(logprob) * logprob, 0.0), axis=-1, keepdims=True
        )
        logits_ref[...] = raw * active
        class_grad = (logit_grad_ref[...].astype(F32) * active).astype(BF)
        stats_ref[0:1] = jnp.broadcast_to(jnp.sum(entropy * active, axis=0, keepdims=True), (1, 8))
        stats_ref[1:2] = jnp.sum(class_grad.astype(F32), axis=0, keepdims=True)
        class_grad_ref[...] = tn(class_grad, pooled_low)
        pooled_grad = nn(class_grad, class_rows)
        pre_grad = (pooled_grad * (1.0 - pooled * pooled)).astype(BF)
        sums_ref[3:4] = jnp.sum(pre_grad.astype(F32), axis=0, keepdims=True)
        pool_grad_ref[...] = tn(leading, pre_grad).reshape(pool_grad_ref.shape).astype(BF)
        lead_ref[...] = nt(pre_grad, pool)
        head = lax.broadcasted_iota(jnp.int32, (length, 1), 0) == 0
        gain = vec_ref[BLOCK_GAIN : BLOCK_GAIN + 1]
        gain_sum = jnp.zeros((1, width), F32)
        shift_sum = jnp.zeros((1, width), F32)
        bias_sum = jnp.zeros((1, width), F32)
        for seq in range(count):
            at = slice(seq * length, (seq + 1) * length)
            on = (exit_ref[seq] >= LAYER).astype(F32)
            top_grad = (
                grad_ref[at].astype(F32) + jnp.where(head, lead_ref[seq : seq + 1], 0.0)
            ) * on
            unit = unit2_ref[at].astype(F32)
            outer = norm_back(top_grad, unit, scale2_ref[at], gain)
            branch = outer.astype(BF)
            outer_ref[at] = outer
            branch_ref[at] = branch
            gain_sum += jnp.sum(top_grad * unit, axis=0, keepdims=True)
            shift_sum += jnp.sum(top_grad, axis=0, keepdims=True)
            bias_sum += jnp.sum(branch.astype(F32), axis=0, keepdims=True)
        sums_ref[0:1] = gain_sum
        sums_ref[1:2] = shift_sum
        sums_ref[2:3] = bias_sum

    @pl.when(step > 0)
    def _():
        few, both, _ = joint_grad_ref.shape
        deep = width // few
        value = nn(act_ref[...], branch_ref[...])
        for at in range(few):
            joint_grad_ref[at, 0:deep] = value[at * deep : (at + 1) * deep].astype(BF)
            joint_grad_ref[at, deep:both] = pool_grad_ref[(step - 1) * few + at]


def leave(
    exit_layer, output, unit2, scale2, output_grad, pool, vec, class_bias, logit_grad, act,
    pool_spec, shards, length, classes,
):
    rows, width = output.shape
    count = rows // length
    hidden = act.shape[0]
    steps = hidden // width
    few = shards // steps
    both = (hidden + width) // shards
    whole = full((rows, width))
    return pl.pallas_call(
        functools.partial(leave_kernel, length, classes),
        grid=(steps + 1,),
        in_specs=[
            pl.BlockSpec(memory_space=pltpu.SMEM),
            whole,
            whole,
            full((rows, 1)),
            whole,
            pool_spec,
            full(vec.shape),
            full(class_bias.shape),
            full(logit_grad.shape),
            pl.BlockSpec((width, rows), lambda i: (jnp.maximum(i - 1, 0), 0)),
        ],
        out_specs=[
            whole,
            whole,
            pl.BlockSpec((few, both, width), lambda i: (jnp.maximum(i - 1, 0), 0, 0)),
            full((4, width)),
            full((8, width)),
            full((count, 8)),
            full((2, 8)),
        ],
        out_shape=[
            jax.ShapeDtypeStruct((rows, width), F32),
            jax.ShapeDtypeStruct((rows, width), BF),
            jax.ShapeDtypeStruct((shards, both, width), BF),
            jax.ShapeDtypeStruct((4, width), F32),
            jax.ShapeDtypeStruct((8, width), F32),
            jax.ShapeDtypeStruct((count, 8), F32),
            jax.ShapeDtypeStruct((2, 8), F32),
        ],
        scratch_shapes=[
            pltpu.VMEM((count, width), F32),
            pltpu.VMEM((shards, width // shards, width), BF),
        ],
        compiler_params=params(),
        cost_estimate=cost(8 * rows * width * width, 30 * rows * width),
        name="leave",
    )(
        exit_layer, output, unit2, scale2, output_grad, pool, vec, class_bias, logit_grad, act
    )


def split_cores(value, place_ref, keep_ref, send_ref):
    chips, part, _ = keep_ref.shape
    first = place_ref[2] == 0
    for chip in range(chips):
        even = value[2 * chip * part : (2 * chip + 1) * part]
        odd = value[(2 * chip + 1) * part : (2 * chip + 2) * part]
        keep_ref[chip] = jnp.where(first, even, odd).astype(BF)
        send_ref[chip] = jnp.where(first, odd, even).astype(BF)


def feed_back_kernel(
    place_ref,
    branch_ref,
    slope_ref,
    turned_ref,
    down_ref,
    up_ref,
    outer_ref,
    unit1_ref,
    scale1_ref,
    out_w_ref,
    vec_ref,
    ctx_ref,
    keep_ref,
    send_ref,
    up_sum_ref,
    inner_ref,
    attended_ref,
    ctx_grad_ref,
    sums_ref,
    acc_ref,
    hid_ref,
):
    step = pl.program_id(0)
    rows, width = branch_ref.shape
    sub = 256

    @pl.when(step == 0)
    def _():
        acc_ref[...] = outer_ref[...]

    last = pl.num_programs(0) - 1

    @pl.when(step < last)
    def _():
        total = jnp.zeros((1, width), F32)
        down = down_ref[...].reshape(up_ref.shape[1:])
        ahead = nt(branch_ref[0:sub], down)
        for m in range(rows // sub):
            at = slice(m * sub, (m + 1) * sub)
            hid = (ahead * slope_ref[at].astype(F32)).astype(BF)
            if (m + 1) * sub < rows:
                ahead = nt(branch_ref[(m + 1) * sub : (m + 2) * sub], down)
            hid_ref[at] = hid
            total += jnp.sum(hid.astype(F32), axis=0, keepdims=True)
            acc_ref[at] += nt(hid, up_ref[0])
        up_sum_ref[...] = total
        split_cores(nn(turned_ref[...], hid_ref[...]), place_ref, keep_ref, send_ref)

    @pl.when(step == last)
    def _():
        gain = vec_ref[ATTN_GAIN : ATTN_GAIN + 1]
        gain_sum = jnp.zeros((1, width), F32)
        shift_sum = jnp.zeros((1, width), F32)
        bias_sum = jnp.zeros((1, width), F32)
        for m in range(rows // sub):
            at = slice(m * sub, (m + 1) * sub)
            grad = acc_ref[at]
            unit = unit1_ref[at].astype(F32)
            inner = norm_back(grad, unit, scale1_ref[at], gain)
            attended = inner.astype(BF)
            inner_ref[at] = inner
            attended_ref[at] = attended
            ctx_grad_ref[at] = nt(attended, out_w_ref[0]).astype(BF)
            gain_sum += jnp.sum(grad * unit, axis=0, keepdims=True)
            shift_sum += jnp.sum(grad, axis=0, keepdims=True)
            bias_sum += jnp.sum(attended.astype(F32), axis=0, keepdims=True)
        sums_ref[0:1] = gain_sum
        sums_ref[1:2] = shift_sum
        sums_ref[2:3] = bias_sum
        split_cores(tn(ctx_ref[...], attended_ref[...]), place_ref, keep_ref, send_ref)


def feed_back(place, chips, branch, slope, low, down, down_block, up, outer, unit1, scale1, out_w, vec, ctx):
    rows, width = branch.shape
    hidden = slope.shape[1]
    steps = hidden // width
    whole = full((rows, width))
    end = steps - 1
    part = width // (2 * chips)
    return pl.pallas_call(
        feed_back_kernel,
        grid=(steps + 1,),
        in_specs=[
            pl.BlockSpec(memory_space=pltpu.SMEM),
            whole,
            pl.BlockSpec((rows, width), lambda i: (0, jnp.minimum(i, end))),
            full((width, rows)),
            pl.BlockSpec(down_block, lambda i: (jnp.minimum(i, end), 0, 0)),
            pl.BlockSpec((1, width, width), lambda i: (jnp.minimum(i, end), 0, 0)),
            whole,
            whole,
            full((rows, 1)),
            pl.BlockSpec((1, width, width), lambda i: (3, 0, 0)),
            full(vec.shape),
            whole,
        ],
        out_specs=[
            pl.BlockSpec((chips, part, width), lambda i: (0, 0, i)),
            pl.BlockSpec((chips, part, width), lambda i: (0, 0, i)),
            pl.BlockSpec((1, width), lambda i: (0, jnp.minimum(i, end))),
            whole,
            whole,
            whole,
            full((3, width)),
        ],
        out_shape=[
            jax.ShapeDtypeStruct((chips, part, hidden + width), BF),
            jax.ShapeDtypeStruct((chips, part, hidden + width), BF),
            jax.ShapeDtypeStruct((1, hidden), F32),
            jax.ShapeDtypeStruct((rows, width), F32),
            jax.ShapeDtypeStruct((rows, width), BF),
            jax.ShapeDtypeStruct((rows, width), BF),
            jax.ShapeDtypeStruct((3, width), F32),
        ],
        scratch_shapes=[pltpu.VMEM((rows, width), F32), pltpu.VMEM((rows, width), BF)],
        compiler_params=params(),
        cost_estimate=cost(28 * rows * width * width, 40 * rows * width),
        name="feed_back",
    )(place, branch, slope, low, down, up, outer, unit1, scale1, out_w, vec, ctx)


def attend_back_kernel(length, joined_ref, probs_ref, ctx_grad_ref, grad_ref, sum_ref):
    rows, width = ctx_grad_ref.shape
    pairs = width // PAIR

    def one(seq, carry):
        at = pl.ds(pl.multiple_of(seq * length, length), length)

        def columns(part, pair):
            return slice(part * width + pair * PAIR, part * width + (pair + 1) * PAIR)

        prob_grads = []
        for pair in range(pairs):
            vals = split_heads(joined_ref[at, columns(2, pair)])
            prob_grads.append(nt(vals, ctx_grad_ref[at, columns(0, pair)]))
        score_grads = []
        for pair in range(pairs):
            probs = probs_ref[seq, pair]
            halves = []
            for head in range(2):
                cut = slice(head * length, (head + 1) * length)
                held = probs[cut].astype(F32)
                part = prob_grads[pair][cut]
                base = jnp.sum(part * held, axis=0, keepdims=True)
                halves.append((held * (part - base)).astype(BF))
            score_grads.append(halves)
        for pair in range(pairs):
            probs = probs_ref[seq, pair]
            beside = jnp.concatenate([probs[:length], probs[length:]], axis=1)
            ctx_grads = split_heads(ctx_grad_ref[at, columns(0, pair)])
            grad_ref[at, columns(2, pair)] = nn(beside, ctx_grads).astype(BF)
        for pair in range(pairs):
            queries = split_heads(joined_ref[at, columns(0, pair)] * jnp.asarray(0.125, BF))
            beside = jnp.concatenate(score_grads[pair], axis=1)
            grad_ref[at, columns(1, pair)] = nn(beside, queries).astype(BF)
        for pair in range(pairs):
            keys = split_heads(joined_ref[at, columns(1, pair)])
            stacked = jnp.concatenate(score_grads[pair], axis=0)
            grad_ref[at, columns(0, pair)] = (tn(stacked, keys) * 0.125).astype(BF)
        return carry

    lax.fori_loop(0, rows // length, one, 0)
    total = jnp.zeros(sum_ref.shape, F32)
    for m in range(rows // length):
        total += jnp.sum(
            grad_ref[m * length : (m + 1) * length].astype(F32), axis=0, keepdims=True
        )

    @pl.when(pl.program_id(0) == 0)
    def _():
        sum_ref[...] = total

    @pl.when(pl.program_id(0) > 0)
    def _():
        sum_ref[...] += total


def attend_back(joined, probs, ctx_grad, length):
    rows, width = ctx_grad.shape
    count = rows // length
    steps = 2
    block = rows // steps
    pairs = width // PAIR
    return pl.pallas_call(
        functools.partial(attend_back_kernel, length),
        grid=(steps,),
        in_specs=[
            pl.BlockSpec((block, 3 * width), lambda i: (i, 0)),
            pl.BlockSpec((count // steps, pairs, 2 * length, length), lambda i: (i, 0, 0, 0)),
            pl.BlockSpec((block, width), lambda i: (i, 0)),
        ],
        out_specs=[
            pl.BlockSpec((block, 3 * width), lambda i: (i, 0)),
            full((1, 3 * width)),
        ],
        out_shape=[
            jax.ShapeDtypeStruct((rows, 3 * width), BF),
            jax.ShapeDtypeStruct((1, 3 * width), F32),
        ],
        compiler_params=params(),
        cost_estimate=cost(8 * rows * width * width, 20 * rows * width),
        name="attend_back",
    )(joined, probs, ctx_grad)


def weight_grads_kernel(tok_ref, joined_ref, small_ref, out_ref, turned_ref):
    step = pl.program_id(0)
    last = pl.num_programs(0) - 1
    shards, part, width = out_ref.shape

    @pl.when(step == 0)
    def _():
        turned_ref[...] = tok_ref[...].T

    value = nn(turned_ref[...], joined_ref[...])
    cols = pl.ds(pl.multiple_of(step * joined_ref.shape[1], joined_ref.shape[1]), joined_ref.shape[1])
    out_ref[:, :, cols] = value.reshape(shards, part, joined_ref.shape[1]).astype(BF)
    tail = 3 * joined_ref.shape[1]
    if width > tail:

        @pl.when(step == last)
        def _():
            lines = small_ref.shape[1]
            out_ref[:, lines:part, tail:width] = jnp.zeros(
                (shards, part - lines, width - tail), BF
            )
            out_ref[:, 0:lines, tail:width] = small_ref[...].astype(BF)


def weight_grads(tokens, joined_grad, small, shards, extra):
    rows, width = tokens.shape
    shape = (shards, width // shards, 3 * width + extra)
    return pl.pallas_call(
        weight_grads_kernel,
        grid=(3,),
        in_specs=[
            full((rows, width)),
            pl.BlockSpec((rows, width), lambda i: (0, i)),
            full(small.shape),
        ],
        out_specs=full(shape),
        out_shape=jax.ShapeDtypeStruct(shape, BF),
        scratch_shapes=[pltpu.VMEM((width, rows), BF)],
        compiler_params=params(),
        cost_estimate=cost(6 * rows * width * width, 20 * rows * width),
        name="weight_grads",
    )(tokens, joined_grad, small)


def input_kernel(inner_ref, joined_ref, w_ref, out_ref):
    width = inner_ref.shape[1]
    total = inner_ref[...]
    for part in range(3):
        total += nt(joined_ref[:, part * width : (part + 1) * width], w_ref[part])
    out_ref[...] = total.astype(BF)


def input_back(inner, joined_grad, qkv):
    rows, width = inner.shape
    steps = 4
    block = rows // steps
    return pl.pallas_call(
        input_kernel,
        grid=(steps,),
        in_specs=[
            pl.BlockSpec((block, width), lambda i: (i, 0)),
            pl.BlockSpec((block, 3 * width), lambda i: (i, 0)),
            full((3, width, width)),
        ],
        out_specs=pl.BlockSpec((block, width), lambda i: (i, 0)),
        out_shape=jax.ShapeDtypeStruct((rows, width), BF),
        compiler_params=params(),
        cost_estimate=cost(6 * rows * width * width, 12 * rows * width),
        name="input_back",
    )(inner, joined_grad, qkv)


def lay_kernel(plan, chips, reps, part, counts, place_ref, *refs):
    at = 0
    groups = []
    for number in counts:
        groups.append(refs[at : at + number])
        at += number
    sems = refs[-1]
    rep, chip, core = place_ref[0], place_ref[1], place_ref[2]
    copies = []

    def start(source, target):
        copies.append(pltpu.make_async_copy(source, target, sems.at[len(copies)]))
        copies[-1].start()

    finish = plan(start, groups, refs[at:-1], rep, chip, core, chips, reps, part)
    for copy in copies:
        copy.wait()
    if finish is not None:
        finish()


def blocks_plan(
    put, own, twin, along, across, swapped, depth, first, rep, chip, core, chips, reps, part
):
    for block in range(reps):
        put(own(block), block, chip, core)
        put(twin(block), block, chip, 1 - core)
    for step in range(1, chips):
        source = lax.rem(chip + chips - step, chips)
        rows = pl.ds((step - 1) * depth + first, part)
        for other, block in along.items():
            put(block(step, source, 0), rep ^ other, source, core)
            put(block(step, source, 1), rep ^ other, source, 1 - core)
        for other in across:
            put(across[other].at[rows], rep ^ other, source, core)
            put(swapped[other].at[rows], rep ^ other, source, 1 - core)


def wide_put(start, out_ref, part):
    def put(source, block, at_chip, at_core):
        row = pl.multiple_of((at_chip * 2 + at_core) * part, part)
        start(source, out_ref.at[block, pl.ds(row, part)])

    return put


def wide_block(ref, width, part):
    return lambda block: ref.at[pl.ds(0, part), pl.ds(block * width, width)]


def first_plan(start, groups, outs, rep, chip, core, chips, reps, part):
    (own, twin), along, across, swapped, (extra,) = groups
    out_ref, vec_ref, more_ref = outs
    width = out_ref.shape[2]

    def near(step, source, side):
        if side == 0:
            return along[step - 1].at[pl.ds(0, part)]
        return swapped[0].at[pl.ds((step - 1) * part, part)]

    blocks_plan(
        wide_put(start, out_ref, part),
        wide_block(own, width, part),
        wide_block(twin, width, part),
        {0: near},
        {at + 1: ref for at, ref in enumerate(across)},
        {at + 1: ref for at, ref in enumerate(swapped[1:])},
        part,
        0,
        rep,
        chip,
        core,
        chips,
        reps,
        part,
    )
    tail = pl.ds(part, 16)
    cols = pl.ds(0, width)
    start(own.at[tail, cols], more_ref.at[chip * 2 + core])
    start(twin.at[tail, cols], more_ref.at[chip * 2 + 1 - core])
    for step in range(1, chips):
        source = lax.rem(chip + chips - step, chips)
        start(along[step - 1].at[tail], more_ref.at[source * 2 + core])
        start(extra.at[pl.ds((step - 1) * 16, 16)], more_ref.at[source * 2 + 1 - core])

    def finish():
        lane = lax.broadcasted_iota(jnp.int32, (LANES, width), 0)
        place = lax.broadcasted_iota(jnp.int32, (LANES, width), 1)
        total = jnp.zeros((16, width), F32)
        for shard in range(2 * chips):
            there = (place - shard * part == lane) & (lane < part)
            total += nn(more_ref[shard, :, 0:LANES], there.astype(F32).astype(BF))
        vec_ref[...] = total

    return finish


def second_plan(start, groups, outs, rep, chip, core, chips, reps, part):
    (up, up_twin, down, down_twin), (close, far), across, swapped = groups
    up_ref, down_ref = outs
    width = up_ref.shape[2]
    where = (rep, chip, core, chips, reps, part)

    def chained(chain, first):
        def block(step, source, side):
            shard = source * 2 + (core if side == 0 else 1 - core)
            return chain.at[shard, pl.ds(first, part)]

        return block

    across = dict(zip(NEAR, across))
    swapped = dict(zip(NEAR, swapped))
    blocks_plan(
        wide_put(start, up_ref, part),
        wide_block(up, width, part),
        wide_block(up_twin, width, part),
        {0: chained(close, 0), FAR: chained(far, 0)},
        across,
        swapped,
        2 * part,
        0,
        *where,
    )

    def put(source, block, at_chip, at_core):
        row = pl.multiple_of(block * part, part)
        start(source, down_ref.at[at_chip * 2 + at_core, pl.ds(row, part)])

    def tall(ref):
        return lambda block: ref.at[pl.ds(block * part, part)]

    blocks_plan(
        put,
        tall(down),
        tall(down_twin),
        {0: chained(close, part), FAR: chained(far, part)},
        across,
        swapped,
        2 * part,
        part,
        *where,
    )


def lay(plan, place, groups, shapes, scratch, copies, part, chips, reps):
    anywhere = pl.BlockSpec(memory_space=pl.ANY)
    inputs = [ref for group in groups for ref in group]
    return pl.pallas_call(
        functools.partial(
            lay_kernel, plan, chips, reps, part, [len(group) for group in groups]
        ),
        in_specs=[pl.BlockSpec(memory_space=pltpu.SMEM)] + [anywhere] * len(inputs),
        out_specs=[pl.BlockSpec(memory_space=pltpu.VMEM)] * len(shapes),
        out_shape=[jax.ShapeDtypeStruct(shape, kind) for shape, kind in shapes],
        scratch_shapes=[pltpu.VMEM(shape, BF) for shape in scratch]
        + [pltpu.SemaphoreType.DMA((copies,))],
        compiler_params=pltpu.CompilerParams(vmem_limit_bytes=VMEM_BYTES),
        cost_estimate=cost(0, 4 * sum(math.prod(shape) for shape, kind in shapes)),
        name="lay",
    )(place, *inputs)


def pack_vectors(rows, up_bias, class_weight):
    part = rows[0].shape[0]
    lines = [row[None] for row in rows[:8]] + [class_weight.T] + [row[None] for row in rows[8:]]
    pieces = up_bias.shape[0] // part
    lines += [up_bias[None, at * part : (at + 1) * part] for at in range(pieces)]
    return jnp.concatenate(lines, axis=0)


def move(values, reps, chips, target):
    pairs = []
    for rep in range(reps):
        for chip in range(chips):
            for core in range(2):
                to_rep, to_chip, to_core = target(rep, chip, core)
                pairs.append(
                    (
                        (rep * chips + chip) * 2 + core,
                        (to_rep * chips + to_chip) * 2 + to_core,
                    )
                )
    return lax.ppermute(values, ("rep", "fsdp"), pairs)


def along_chips(step, chips):
    return lambda rep, chip, core: (rep, (chip + step) % chips, core)


def across_reps(other):
    return lambda rep, chip, core: (rep ^ other, chip, core)


def to_twin(rep, chip, core):
    return rep, chip, 1 - core


def after(values, *gates):
    return lax.optimization_barrier((values, *gates))[0]


def along_z(mine, reps, chips):
    return [move(mine, reps, chips, along_chips(step, chips)) for step in range(1, chips)]


def over_reps(stacked, reps, chips, others):
    return [move(stacked, reps, chips, across_reps(other)) for other in others]


def pick(parts, at):
    return lax.dynamic_index_in_dim(parts, at, axis=0, keepdims=False)


def in_order(rep, reps, own, others, axis):
    blocks = jnp.stack([own] + others)
    return jnp.concatenate([pick(blocks, rep ^ at) for at in range(reps)], axis=axis)


class Reduction:
    def __init__(self, place, keep, send, reps, chips, by_chain=False):
        self.rep, self.chip = place[0], place[1]
        self.reps, self.chips = reps, chips
        self.shape = (chips, reps, keep.shape[1] // reps, keep.shape[2])
        self.keep = keep.reshape(self.shape)
        self.others_of = range(1, reps)
        self.far = None
        if by_chain:
            self.others_of = NEAR
            first = place[2] == 0
            kept = lax.dynamic_index_in_dim(self.keep, self.rep ^ FAR, axis=1, keepdims=False)
            sent = lax.dynamic_index_in_dim(
                send.reshape(self.shape), self.rep ^ FAR, axis=1, keepdims=False
            )
            pair = jnp.stack(
                [jnp.where(first, kept, sent), jnp.where(first, sent, kept)], axis=1
            )
            self.far = lax.psum_scatter(
                pair.reshape(-1, keep.shape[2]), "fsdp", scatter_dimension=0, tiled=True
            )
        self.got = move(send, reps, chips, to_twin)

    def at_rep(self, at):
        kept = lax.dynamic_index_in_dim(self.keep, at, axis=1, keepdims=False)
        came = lax.dynamic_index_in_dim(
            self.got.reshape(self.shape), at, axis=1, keepdims=False
        )
        return kept.astype(F32) + came.astype(F32)

    def over_reps(self, *gates):
        if gates:
            self.got = after(self.got, *gates)
        self.arrived = [
            move(
                self.at_rep(self.rep ^ other).astype(BF),
                self.reps,
                self.chips,
                across_reps(other),
            )
            for other in self.others_of
        ]

    def over_chips(self, *gates):
        if gates:
            self.arrived = [after(block, *gates) for block in self.arrived]
        mine = self.at_rep(self.rep)

        def both_at(at):
            total = pick(mine, at)
            for block in self.arrived:
                total = total + pick(block, at).astype(F32)
            return total

        self.total = both_at(self.chip)
        if self.far is not None:
            came = move(self.far, self.reps, self.chips, across_reps(FAR))
            self.total = self.total + came.astype(F32)
        self.passed = [
            move(
                both_at(lax.rem(self.chip + step, self.chips)).astype(BF),
                self.reps,
                self.chips,
                along_chips(step, self.chips),
            )
            for step in range(1, self.chips)
        ]

    def share(self, *gates):
        if gates:
            self.passed = [after(block, *gates) for block in self.passed]
        total = self.total
        for block in self.passed:
            total = total + block.astype(F32)
        self.total = total.astype(BF)
        self.others = [
            move(self.total, self.reps, self.chips, across_reps(other))
            for other in range(1, self.reps)
        ]

    def result(self):
        return in_order(self.rep, self.reps, self.total, self.others, 0).astype(F32)


def exchange_reps(place, rows, reps, chips):
    rep = place[0]
    parts = rows.reshape(reps, -1, rows.shape[1])
    total = pick(parts, rep).astype(F32)
    arrived = [
        move(pick(parts, rep ^ other), reps, chips, across_reps(other))
        for other in range(1, reps)
    ]
    for block in arrived:
        total = total + block.astype(F32)
    return total.astype(BF), arrived


def per_device(
    tokens,
    exit_layer,
    qkv_weight,
    query_bias,
    value_bias,
    out_weight,
    out_bias,
    attn_gain,
    attn_shift,
    up_weight,
    up_bias,
    down_weight,
    down_bias,
    block_gain,
    block_shift,
    pool_weight,
    pool_bias,
    class_weight,
    class_bias,
    output_grad,
    logit_grad,
):
    reps = lax.axis_size("rep")
    shards = lax.axis_size("fsdp")
    mine = lax.axis_index("fsdp")
    rows, width = tokens.shape
    count = exit_layer.shape[0]
    length = rows // count
    classes = class_weight.shape[1]
    part = out_weight.shape[0]
    hidden = up_weight.shape[1]

    def gather(shard):
        return lax.all_gather(shard, "fsdp", axis=0, tiled=True)

    packed = pack_vectors(
        [
            query_bias,
            value_bias,
            out_bias,
            attn_gain,
            attn_shift,
            down_bias,
            block_gain,
            block_shift,
            pool_bias,
        ],
        up_bias,
        class_weight,
    )
    joint_own = jnp.concatenate([qkv_weight, out_weight], axis=1)
    deep = down_weight.shape[0]
    chips = shards // 2
    place = jnp.stack([lax.axis_index("rep"), mine // 2, mine % 2]).astype(jnp.int32)
    direct = (
        part % 16 == 0
        and reps & (reps - 1) == 0
        and reps * width == hidden
        and reps == 4
        and packed.shape[0] <= 16
    )
    if direct:
        lines = packed.shape[0]
        held = jnp.pad(packed, ((0, 16 - lines), (0, width - part)))
        own = jnp.concatenate([joint_own, jnp.tile(held, (1, reps))], axis=0)
        rep = place[0]

        def block_of(weights, at):
            return lax.dynamic_slice_in_dim(weights, at * width, width, axis=1)

        def second_of(at):
            return [
                block_of(up_weight, at),
                lax.dynamic_slice_in_dim(down_weight, at * part, part, axis=0),
            ]

        along = along_z(block_of(own, rep), reps, chips)
        chain = gather(after(jnp.concatenate(second_of(rep), axis=0), *along))
        chain = chain.reshape(chips, 2, 2 * part, width)
        twin = move(own, reps, chips, to_twin)
        stacked = jnp.concatenate([rows_[:part] for rows_ in along], axis=0)
        across = over_reps(stacked, reps, chips, range(1, reps))
        far_chain = gather(after(jnp.concatenate(second_of(rep ^ FAR), axis=0), *across))
        swapped = [move(rows_, reps, chips, to_twin) for rows_ in [stacked] + across]
        extra = move(
            jnp.concatenate([rows_[part:] for rows_ in along], axis=0), reps, chips, to_twin
        )
        up_twin = move(up_weight, reps, chips, to_twin)
        down_twin = move(down_weight, reps, chips, to_twin)
        joint, vec = lay(
            first_plan,
            place,
            [
                [own, twin],
                along,
                across,
                swapped,
                [extra],
            ],
            [((reps, width, width), BF), ((16, width), F32)],
            [(shards, 16, width)],
            2 * chips * (reps + 1),
            part,
            chips,
            reps,
        )
        mine_chain = lax.dynamic_index_in_dim(
            after(chain, joint), place[2], axis=1, keepdims=False
        )
        second_stacked = jnp.concatenate(
            [
                pick(mine_chain, lax.rem(place[1] + chips - step, chips))
                for step in range(1, chips)
            ],
            axis=0,
        )
        second_across = over_reps(after(second_stacked, *across), reps, chips, NEAR)
        up_row = (
            vec[VECTOR_ROWS:lines].reshape(-1, shards, part).transpose(1, 0, 2).reshape(1, hidden)
        )
        down_block = (width // deep, deep, width)
    else:
        small = gather(packed[None])
        vec = small[:, :VECTOR_ROWS].transpose(1, 0, 2).reshape(VECTOR_ROWS, width).astype(F32)
        vec = jnp.pad(vec, ((0, 16 - VECTOR_ROWS), (0, 0)))
        up_row = small[:, VECTOR_ROWS:].transpose(0, 1, 2).reshape(1, hidden).astype(F32)
        pool = gather(pool_weight)
        joint = jnp.stack(jnp.split(gather(joint_own), 4, axis=1))
        up = jnp.stack(jnp.split(gather(up_weight), hidden // width, axis=1))
        down = gather(down_weight).reshape(-1, width, width)
        down_block = (1, width, width)
    joined, probs, ctx = attend(tokens, joint, vec, length)
    if direct:
        pool = gather(after(pool_weight, ctx))
        far_chain = after(far_chain, ctx)
        second_swapped = [
            move(after(rows_, ctx), reps, chips, to_twin) for rows_ in second_across
        ]
        up, down = lay(
            second_plan,
            place,
            [
                [up_weight, up_twin, down_weight, down_twin],
                [
                    chain.reshape(shards, 2 * part, width),
                    far_chain.reshape(shards, 2 * part, width),
                ],
                second_across,
                second_swapped,
            ],
            [((reps, width, width), BF), ((shards, deep, width), BF)],
            [],
            4 * chips * reps,
            part,
            chips,
            reps,
        )
    turned, act, slope, unit1, scale1, unit2, scale2, output = feed(
        exit_layer, tokens, ctx, joint, vec, up, up_row, down, down_block, length
    )
    class_bias_row = jnp.pad(class_bias.astype(F32), (0, 8 - classes))[None]
    logit_grad_rows = jnp.pad(logit_grad, ((0, 0), (0, 8 - classes)))
    outer, branch, low_grad, exit_sums, class_grad, logits, stats = leave(
        exit_layer,
        output,
        unit2,
        scale2,
        output_grad,
        pool,
        vec,
        class_bias_row,
        logit_grad_rows,
        act,
        full((width, width)),
        shards,
        length,
        classes,
    )
    up_keep, up_send, up_sum, inner, attended, ctx_grad, feed_sums = feed_back(
        place, chips, branch, slope, turned, down, down_block, up, outer, unit1, scale1, joint, vec, ctx
    )
    if direct:
        up_red = Reduction(place, up_keep, up_send, reps, chips)
    joined_grad, joined_sum = attend_back(joined, probs, ctx_grad, length)
    joined_seen = joined_grad
    if direct:
        up_red.over_reps(joined_grad)
        joined_seen = after(joined_grad, up_red.got)
    sums = jnp.concatenate(
        [
            joined_sum.reshape(3, width)[::2],
            feed_sums,
            exit_sums,
            class_grad[:classes],
        ],
        axis=0,
    )
    lines = sums.shape[0]
    own_sums = sums.reshape(lines, shards, part).transpose(1, 0, 2).reshape(shards, lines * part)
    own_sums = jnp.concatenate([own_sums, up_sum.reshape(shards, deep)], axis=1)
    used = own_sums.shape[1]
    seqs_total = count * reps * shards
    figures = jnp.concatenate([stats[0, :1], stats[1, :classes]])
    slots = reps * shards * figures.shape[0] * 3
    direct = direct and used + slots <= part * LANES
    small_lines = 16
    if direct:
        high = figures.astype(BF).astype(F32)
        middle = (figures - high).astype(BF).astype(F32)
        lowest = figures - high - middle
        split = jnp.concatenate([high, middle, lowest])
        slot = lax.axis_index("rep") * shards + mine
        lone = jnp.where(
            jnp.arange(reps * shards)[:, None] == slot, split[None], 0.0
        ).reshape(1, slots)
        row = jnp.concatenate([own_sums, jnp.broadcast_to(lone, (shards, slots))], axis=1)
        small_lines = -(-row.shape[1] // (LANES * 16)) * 16
        row = jnp.pad(row, ((0, 0), (0, small_lines * LANES - row.shape[1])))
        row = row.reshape(shards, small_lines, LANES)
    else:
        row = jnp.zeros((shards, small_lines, LANES), F32)
    joint_grad = weight_grads(tokens, joined_seen, row, shards, LANES if direct else 0)
    input_grad = input_back(inner, joined_grad, joint)

    def scatter(grad):
        return lax.psum_scatter(grad, "fsdp", scatter_dimension=0, tiled=True)

    low_part = scatter(low_grad.reshape(-1, width))
    if direct:
        joint_grad = after(joint_grad, low_part, up_red.arrived[0])
    joint_part = scatter(joint_grad.reshape(width, -1))
    if direct:
        up_red.over_chips()
        up_red.share()
        wide = (deep + part) * width // part
        both = jnp.concatenate(
            [
                after(joint_part, *up_red.others).reshape(reps, part // reps, -1),
                low_part.reshape(reps, part // reps, wide),
            ],
            axis=2,
        )
        columns = both.shape[2] - wide
        both, _ = exchange_reps(place, both.reshape(part, -1), reps, chips)
        others = [move(both, reps, chips, across_reps(other)) for other in range(1, reps)]
        both = in_order(place[0], reps, both, others, 0).astype(F32)
        low_sum = both[:, columns:].reshape(deep + part, width)
        joint_sum = both[:, :columns]
        up_sum = up_red.result()
        small_sum = joint_sum[:small_lines, 3 * width :].reshape(-1)
        total = small_sum[used : used + slots].reshape(-1, figures.shape[0]).sum(axis=0)
    else:
        first = mine % 2 == 0

        def whole_of(kept, sent):
            pair = jnp.stack([jnp.where(first, kept, sent), jnp.where(first, sent, kept)], axis=1)
            return pair.reshape(-1, kept.shape[2])

        joint_sum, low_sum, up_sum = lax.psum(
            (joint_part, low_part, scatter(whole_of(up_keep, up_send))), "rep"
        )
        joint_sum, low_sum, up_sum = (
            joint_sum.astype(F32),
            low_sum.astype(F32),
            up_sum.astype(F32),
        )
        own_sums, total = lax.psum((own_sums, figures), ("rep", "fsdp"))
        small_sum = pick(own_sums, mine)
    own = small_sum[: lines * part].reshape(lines, part)
    return (
        output,
        logits[:, :classes],
        total[0] / seqs_total,
        input_grad,
        joint_sum[:, : 3 * width],
        own[0],
        own[1],
        up_sum[:, hidden:],
        own[4],
        own[2],
        own[3],
        up_sum[:, :hidden],
        small_sum[lines * part : used],
        low_sum[:deep],
        own[7],
        own[5],
        own[6],
        low_sum[deep:],
        own[8],
        own[9 : 9 + classes].T,
        total[1:],
    )


def solution(mesh):
    return jax.shard_map(
        per_device,
        mesh=mesh,
        in_specs=(
            P(("rep", "fsdp"), None),
            P(("rep", "fsdp")),
            P("fsdp", None),
            P("fsdp"),
            P("fsdp"),
            P("fsdp", None),
            P("fsdp"),
            P("fsdp"),
            P("fsdp"),
            P("fsdp", None),
            P("fsdp"),
            P("fsdp", None),
            P("fsdp"),
            P("fsdp"),
            P("fsdp"),
            P("fsdp", None),
            P("fsdp"),
            P("fsdp", None),
            P(),
            P(("rep", "fsdp"), None),
            P(("rep", "fsdp"), None),
        ),
        out_specs=(
            P(("rep", "fsdp"), None),
            P(("rep", "fsdp"), None),
            P(),
            P(("rep", "fsdp"), None),
            P("fsdp", None),
            P("fsdp"),
            P("fsdp"),
            P("fsdp", None),
            P("fsdp"),
            P("fsdp"),
            P("fsdp"),
            P("fsdp", None),
            P("fsdp"),
            P("fsdp", None),
            P("fsdp"),
            P("fsdp"),
            P("fsdp"),
            P("fsdp", None),
            P("fsdp"),
            P("fsdp", None),
            P(),
        ),
        check_vma=False,
    )
```

```python
import functools
import math

import jax
import jax.numpy as jnp
from jax import lax
from jax.experimental import pallas as pl
from jax.experimental.pallas import tpu as pltpu
from jax.sharding import PartitionSpec as P

HD = 64
LAYER = 6
PAIR = 2 * HD
NEAR = (1, 2)
FAR = 3
LANES = 128
VMEM_BYTES = 58 * 2**20
BF = jnp.bfloat16
F32 = jnp.float32

QUERY_BIAS, VALUE_BIAS, OUT_BIAS, ATTN_GAIN, ATTN_SHIFT = 0, 1, 2, 3, 4
DOWN_BIAS, BLOCK_GAIN, BLOCK_SHIFT, CLASS_ROWS, POOL_BIAS = 5, 6, 7, 8, 11
VECTOR_ROWS = 12


def nn(left, right):
    return jnp.dot(left, right, preferred_element_type=F32)


def tn(left, right):
    return lax.dot_general(left, right, (((0,), (0,)), ((), ())), preferred_element_type=F32)


def nt(left, right):
    return lax.dot_general(left, right, (((1,), (1,)), ((), ())), preferred_element_type=F32)


def full(shape):
    return pl.BlockSpec(shape, lambda *at: (0,) * len(shape))


def params():
    return pltpu.CompilerParams(
        dimension_semantics=("arbitrary",), vmem_limit_bytes=VMEM_BYTES
    )


def cost(flops, moved, trans=0):
    return pl.CostEstimate(flops=flops, bytes_accessed=moved, transcendentals=trans)


def split_heads(pair):
    lane = lax.broadcasted_iota(jnp.int32, pair.shape, 1)
    zero = jnp.zeros_like(pair)
    return jnp.concatenate(
        [jnp.where(lane < HD, pair, zero), jnp.where(lane < HD, zero, pair)], axis=0
    )


def norm_stats(values):
    center = values - jnp.mean(values, axis=-1, keepdims=True)
    spread = jnp.mean(center * center, axis=-1, keepdims=True)
    scale = lax.rsqrt(spread + 1e-06)
    return center * scale, scale


def norm_back(grad, unit, scale, gain):
    inner = grad * gain
    first = jnp.mean(inner, axis=-1, keepdims=True)
    second = jnp.mean(inner * unit, axis=-1, keepdims=True)
    return scale * (inner - first - unit * second)


def gelu_parts(values):
    base = 1.0 + 0.23164189 * jnp.abs(values)
    t = pl.reciprocal(base, approx=True)
    t = t * (2.0 - base * t)
    bell = jnp.exp2((values * values) * -0.7213475204444817)
    poly = t * (
        0.127414796
        + t * (-0.142248368 + t * (0.7107068705 + t * (-0.7265760135 + t * 0.5307027145)))
    )
    tail = poly * bell
    below = jnp.where(values >= 0.0, 1.0 - tail, tail)
    return values * below, below + values * (bell * 0.3989422804014327)


def attend_kernel(length, tok_ref, w_ref, vec_ref, joined_ref, probs_ref, ctx_ref):
    rows, width = ctx_ref.shape
    pairs = width // PAIR
    for part in range(3):
        cols = slice(part * width, (part + 1) * width)
        value = nn(tok_ref[...], w_ref[part])
        if part == 0:
            value += vec_ref[QUERY_BIAS : QUERY_BIAS + 1]
        elif part == 2:
            value += vec_ref[VALUE_BIAS : VALUE_BIAS + 1]
        joined_ref[:, cols] = value.astype(BF)

    def one(seq, carry):
        at = pl.ds(pl.multiple_of(seq * length, length), length)
        scores = []
        for pair in range(pairs):
            query = joined_ref[at, pair * PAIR : (pair + 1) * PAIR] * jnp.asarray(0.125, BF)
            keys = split_heads(joined_ref[at, width + pair * PAIR : width + (pair + 1) * PAIR])
            scores.append(nt(keys, query))
        all_probs = []
        for pair in range(pairs):
            halves = []
            for head in range(2):
                part = scores[pair][head * length : (head + 1) * length]
                part = jnp.exp(part - jnp.max(part, axis=0, keepdims=True))
                part = part * (1.0 / jnp.sum(part, axis=0, keepdims=True))
                halves.append(part.astype(BF))
            probs = jnp.concatenate(halves, axis=0)
            probs_ref[seq, pair] = probs
            all_probs.append(probs)
        for pair in range(pairs):
            vals = split_heads(
                joined_ref[at, 2 * width + pair * PAIR : 2 * width + (pair + 1) * PAIR]
            )
            ctx_ref[at, pair * PAIR : (pair + 1) * PAIR] = tn(all_probs[pair], vals).astype(BF)
        return carry

    lax.fori_loop(0, rows // length, one, 0)


def attend(tokens, qkv, vec, length):
    rows, width = tokens.shape
    count = rows // length
    steps = 2
    block = rows // steps
    pairs = width // PAIR
    return pl.pallas_call(
        functools.partial(attend_kernel, length),
        grid=(steps,),
        in_specs=[
            pl.BlockSpec((block, width), lambda i: (i, 0)),
            full((3, width, width)),
            full(vec.shape),
        ],
        out_specs=[
            pl.BlockSpec((block, 3 * width), lambda i: (i, 0)),
            pl.BlockSpec((count // steps, pairs, 2 * length, length), lambda i: (i, 0, 0, 0)),
            pl.BlockSpec((block, width), lambda i: (i, 0)),
        ],
        out_shape=[
            jax.ShapeDtypeStruct((rows, 3 * width), BF),
            jax.ShapeDtypeStruct((count, pairs, 2 * length, length), BF),
            jax.ShapeDtypeStruct((rows, width), BF),
        ],
        compiler_params=params(),
        cost_estimate=cost(8 * rows * width * width, 20 * rows * width, rows * width),
        name="attend",
    )(tokens, qkv, vec)


def feed_kernel(
    length,
    exit_ref,
    tok_ref,
    ctx_ref,
    out_w_ref,
    vec_ref,
    up_ref,
    up_b_ref,
    down_ref,
    turned_ref,
    act_ref,
    slope_ref,
    unit1_ref,
    scale1_ref,
    unit2_ref,
    scale2_ref,
    output_ref,
    acc_ref,
    low_ref,
):
    step = pl.program_id(0)
    rows = tok_ref.shape[0]
    sub = 512

    @pl.when(step == 0)
    def _():
        for m in range(rows // sub):
            at = slice(m * sub, (m + 1) * sub)
            inner = tok_ref[at].astype(F32) + (
                nn(ctx_ref[at], out_w_ref[0]) + vec_ref[OUT_BIAS : OUT_BIAS + 1]
            )
            unit, scale = norm_stats(inner)
            first = unit * vec_ref[ATTN_GAIN : ATTN_GAIN + 1] + vec_ref[ATTN_SHIFT : ATTN_SHIFT + 1]
            unit1_ref[at] = unit.astype(BF)
            scale1_ref[at] = scale
            low = first.astype(BF)
            low_ref[at] = low
            turned_ref[:, at] = low.T
            acc_ref[at] = first + vec_ref[DOWN_BIAS : DOWN_BIAS + 1]

    down = down_ref[...].reshape(up_ref.shape[1:])
    ahead = nn(low_ref[0:sub], up_ref[0])
    for m in range(rows // sub):
        at = slice(m * sub, (m + 1) * sub)
        hidden = ahead + up_b_ref[...]
        if (m + 1) * sub < rows:
            ahead = nn(low_ref[(m + 1) * sub : (m + 2) * sub], up_ref[0])
        act, slope = gelu_parts(hidden)
        act = act.astype(BF)
        act_ref[:, at] = act.T
        slope_ref[at] = slope.astype(BF)
        acc_ref[at] += nn(act, down)

    @pl.when(step == pl.num_programs(0) - 1)
    def _():
        for seq in range(rows // length):
            at = slice(seq * length, (seq + 1) * length)
            active = (exit_ref[seq] >= LAYER).astype(F32)
            unit, scale = norm_stats(acc_ref[at])
            unit2_ref[at] = unit.astype(BF)
            scale2_ref[at] = scale
            result = (
                unit * vec_ref[BLOCK_GAIN : BLOCK_GAIN + 1] + vec_ref[BLOCK_SHIFT : BLOCK_SHIFT + 1]
            ) * active
            output_ref[at] = result.astype(BF)


def feed(exit_layer, tokens, ctx, out_w, vec, up, up_bias, down, down_block, length):
    rows, width = tokens.shape
    steps = up.shape[0]
    hidden = steps * width
    whole = full((rows, width))
    return pl.pallas_call(
        functools.partial(feed_kernel, length),
        grid=(steps,),
        in_specs=[
            pl.BlockSpec(memory_space=pltpu.SMEM),
            whole,
            whole,
            pl.BlockSpec((1, width, width), lambda i: (3, 0, 0)),
            full(vec.shape),
            pl.BlockSpec((1, width, width), lambda i: (i, 0, 0)),
            pl.BlockSpec((1, width), lambda i: (0, i)),
            pl.BlockSpec(down_block, lambda i: (i, 0, 0)),
        ],
        out_specs=[
            full((width, rows)),
            pl.BlockSpec((width, rows), lambda i: (i, 0)),
            pl.BlockSpec((rows, width), lambda i: (0, i)),
            whole,
            full((rows, 1)),
            whole,
            full((rows, 1)),
            whole,
        ],
        out_shape=[
            jax.ShapeDtypeStruct((width, rows), BF),
            jax.ShapeDtypeStruct((hidden, rows), BF),
            jax.ShapeDtypeStruct((rows, hidden), BF),
            jax.ShapeDtypeStruct((rows, width), BF),
            jax.ShapeDtypeStruct((rows, 1), F32),
            jax.ShapeDtypeStruct((rows, width), BF),
            jax.ShapeDtypeStruct((rows, 1), F32),
            jax.ShapeDtypeStruct((rows, width), BF),
        ],
        scratch_shapes=[pltpu.VMEM((rows, width), F32), pltpu.VMEM((rows, width), BF)],
        compiler_params=params(),
        cost_estimate=cost(18 * rows * width * width, 40 * rows * width, 8 * rows * width),
        name="feed",
    )(exit_layer, tokens, ctx, out_w, vec, up, up_bias, down)


def leave_kernel(
    length,
    classes,
    exit_ref,
    output_ref,
    unit2_ref,
    scale2_ref,
    grad_ref,
    pool_ref,
    vec_ref,
    class_bias_ref,
    logit_grad_ref,
    act_ref,
    outer_ref,
    branch_ref,
    joint_grad_ref,
    sums_ref,
    class_grad_ref,
    logits_ref,
    stats_ref,
    lead_ref,
    pool_grad_ref,
):
    step = pl.program_id(0)
    rows, width = output_ref.shape
    pool = pool_ref[...].reshape(width, width)
    count = rows // length

    @pl.when(step == 0)
    def _():
        place = lax.broadcasted_iota(jnp.int32, (count, 1), 0)
        active = jnp.zeros((count, 1), F32)
        for seq in range(count):
            on = (exit_ref[seq] >= LAYER).astype(F32)
            active = jnp.where(place == seq, on, active)
        leading = jnp.concatenate(
            [output_ref[seq * length : seq * length + 1].astype(F32) for seq in range(count)],
            axis=0,
        ).astype(BF)
        pooled = jnp.tanh(nn(leading, pool) + vec_ref[POOL_BIAS : POOL_BIAS + 1])
        pooled_low = pooled.astype(BF)
        used = lax.broadcasted_iota(jnp.int32, (8, width), 0) < classes
        class_rows = jnp.where(used, vec_ref[CLASS_ROWS : CLASS_ROWS + 8], 0.0).astype(BF)
        raw = nt(pooled_low, class_rows) + class_bias_ref[...]
        lane = lax.broadcasted_iota(jnp.int32, raw.shape, 1) < classes
        top = jnp.max(jnp.where(lane, raw, -jnp.inf), axis=-1, keepdims=True)
        spread = jnp.where(lane, jnp.exp(raw - top), 0.0)
        logprob = raw - top - jnp.log(jnp.sum(spread, axis=-1, keepdims=True))
        entropy = -jnp.sum(
            jnp.where(lane, jnp.exp(logprob) * logprob, 0.0), axis=-1, keepdims=True
        )
        logits_ref[...] = raw * active
        class_grad = (logit_grad_ref[...].astype(F32) * active).astype(BF)
        stats_ref[0:1] = jnp.broadcast_to(jnp.sum(entropy * active, axis=0, keepdims=True), (1, 8))
        stats_ref[1:2] = jnp.sum(class_grad.astype(F32), axis=0, keepdims=True)
        class_grad_ref[...] = tn(class_grad, pooled_low)
        pooled_grad = nn(class_grad, class_rows)
        pre_grad = (pooled_grad * (1.0 - pooled * pooled)).astype(BF)
        sums_ref[3:4] = jnp.sum(pre_grad.astype(F32), axis=0, keepdims=True)
        pool_grad_ref[...] = tn(leading, pre_grad).reshape(pool_grad_ref.shape).astype(BF)
        lead_ref[...] = nt(pre_grad, pool)
        head = lax.broadcasted_iota(jnp.int32, (length, 1), 0) == 0
        gain = vec_ref[BLOCK_GAIN : BLOCK_GAIN + 1]
        gain_sum = jnp.zeros((1, width), F32)
        shift_sum = jnp.zeros((1, width), F32)
        bias_sum = jnp.zeros((1, width), F32)
        for seq in range(count):
            at = slice(seq * length, (seq + 1) * length)
            on = (exit_ref[seq] >= LAYER).astype(F32)
            top_grad = (
                grad_ref[at].astype(F32) + jnp.where(head, lead_ref[seq : seq + 1], 0.0)
            ) * on
            unit = unit2_ref[at].astype(F32)
            outer = norm_back(top_grad, unit, scale2_ref[at], gain)
            branch = outer.astype(BF)
            outer_ref[at] = outer
            branch_ref[at] = branch
            gain_sum += jnp.sum(top_grad * unit, axis=0, keepdims=True)
            shift_sum += jnp.sum(top_grad, axis=0, keepdims=True)
            bias_sum += jnp.sum(branch.astype(F32), axis=0, keepdims=True)
        sums_ref[0:1] = gain_sum
        sums_ref[1:2] = shift_sum
        sums_ref[2:3] = bias_sum

    @pl.when(step > 0)
    def _():
        few, both, _ = joint_grad_ref.shape
        deep = width // few
        value = nn(act_ref[...], branch_ref[...])
        for at in range(few):
            joint_grad_ref[at, 0:deep] = value[at * deep : (at + 1) * deep].astype(BF)
            joint_grad_ref[at, deep:both] = pool_grad_ref[(step - 1) * few + at]


def leave(
    exit_layer, output, unit2, scale2, output_grad, pool, vec, class_bias, logit_grad, act,
    pool_spec, shards, length, classes,
):
    rows, width = output.shape
    count = rows // length
    hidden = act.shape[0]
    steps = hidden // width
    few = shards // steps
    both = (hidden + width) // shards
    whole = full((rows, width))
    return pl.pallas_call(
        functools.partial(leave_kernel, length, classes),
        grid=(steps + 1,),
        in_specs=[
            pl.BlockSpec(memory_space=pltpu.SMEM),
            whole,
            whole,
            full((rows, 1)),
            whole,
            pool_spec,
            full(vec.shape),
            full(class_bias.shape),
            full(logit_grad.shape),
            pl.BlockSpec((width, rows), lambda i: (jnp.maximum(i - 1, 0), 0)),
        ],
        out_specs=[
            whole,
            whole,
            pl.BlockSpec((few, both, width), lambda i: (jnp.maximum(i - 1, 0), 0, 0)),
            full((4, width)),
            full((8, width)),
            full((count, 8)),
            full((2, 8)),
        ],
        out_shape=[
            jax.ShapeDtypeStruct((rows, width), F32),
            jax.ShapeDtypeStruct((rows, width), BF),
            jax.ShapeDtypeStruct((shards, both, width), BF),
            jax.ShapeDtypeStruct((4, width), F32),
            jax.ShapeDtypeStruct((8, width), F32),
            jax.ShapeDtypeStruct((count, 8), F32),
            jax.ShapeDtypeStruct((2, 8), F32),
        ],
        scratch_shapes=[
            pltpu.VMEM((count, width), F32),
            pltpu.VMEM((shards, width // shards, width), BF),
        ],
        compiler_params=params(),
        cost_estimate=cost(8 * rows * width * width, 30 * rows * width),
        name="leave",
    )(
        exit_layer, output, unit2, scale2, output_grad, pool, vec, class_bias, logit_grad, act
    )


def split_cores(value, place_ref, keep_ref, send_ref):
    chips, part, _ = keep_ref.shape
    first = place_ref[2] == 0
    for chip in range(chips):
        even = value[2 * chip * part : (2 * chip + 1) * part]
        odd = value[(2 * chip + 1) * part : (2 * chip + 2) * part]
        keep_ref[chip] = jnp.where(first, even, odd).astype(BF)
        send_ref[chip] = jnp.where(first, odd, even).astype(BF)


def feed_back_kernel(
    place_ref,
    branch_ref,
    slope_ref,
    turned_ref,
    down_ref,
    up_ref,
    outer_ref,
    unit1_ref,
    scale1_ref,
    out_w_ref,
    vec_ref,
    ctx_ref,
    keep_ref,
    send_ref,
    up_sum_ref,
    inner_ref,
    attended_ref,
    ctx_grad_ref,
    sums_ref,
    acc_ref,
    hid_ref,
):
    step = pl.program_id(0)
    rows, width = branch_ref.shape
    sub = 512

    @pl.when(step == 0)
    def _():
        acc_ref[...] = outer_ref[...]

    last = pl.num_programs(0) - 1

    @pl.when(step < last)
    def _():
        total = jnp.zeros((1, width), F32)
        down = down_ref[...].reshape(up_ref.shape[1:])
        ahead = nt(branch_ref[0:sub], down)
        for m in range(rows // sub):
            at = slice(m * sub, (m + 1) * sub)
            hid = (ahead * slope_ref[at].astype(F32)).astype(BF)
            if (m + 1) * sub < rows:
                ahead = nt(branch_ref[(m + 1) * sub : (m + 2) * sub], down)
            hid_ref[at] = hid
            total += jnp.sum(hid.astype(F32), axis=0, keepdims=True)
            acc_ref[at] += nt(hid, up_ref[0])
        up_sum_ref[...] = total
        split_cores(nn(turned_ref[...], hid_ref[...]), place_ref, keep_ref, send_ref)

    @pl.when(step == last)
    def _():
        gain = vec_ref[ATTN_GAIN : ATTN_GAIN + 1]
        gain_sum = jnp.zeros((1, width), F32)
        shift_sum = jnp.zeros((1, width), F32)
        bias_sum = jnp.zeros((1, width), F32)
        for m in range(rows // sub):
            at = slice(m * sub, (m + 1) * sub)
            grad = acc_ref[at]
            unit = unit1_ref[at].astype(F32)
            inner = norm_back(grad, unit, scale1_ref[at], gain)
            attended = inner.astype(BF)
            inner_ref[at] = inner
            attended_ref[at] = attended
            ctx_grad_ref[at] = nt(attended, out_w_ref[0]).astype(BF)
            gain_sum += jnp.sum(grad * unit, axis=0, keepdims=True)
            shift_sum += jnp.sum(grad, axis=0, keepdims=True)
            bias_sum += jnp.sum(attended.astype(F32), axis=0, keepdims=True)
        sums_ref[0:1] = gain_sum
        sums_ref[1:2] = shift_sum
        sums_ref[2:3] = bias_sum
        split_cores(tn(ctx_ref[...], attended_ref[...]), place_ref, keep_ref, send_ref)


def feed_back(place, chips, branch, slope, low, down, down_block, up, outer, unit1, scale1, out_w, vec, ctx):
    rows, width = branch.shape
    hidden = slope.shape[1]
    steps = hidden // width
    whole = full((rows, width))
    end = steps - 1
    part = width // (2 * chips)
    return pl.pallas_call(
        feed_back_kernel,
        grid=(steps + 1,),
        in_specs=[
            pl.BlockSpec(memory_space=pltpu.SMEM),
            whole,
            pl.BlockSpec((rows, width), lambda i: (0, jnp.minimum(i, end))),
            full((width, rows)),
            pl.BlockSpec(down_block, lambda i: (jnp.minimum(i, end), 0, 0)),
            pl.BlockSpec((1, width, width), lambda i: (jnp.minimum(i, end), 0, 0)),
            whole,
            whole,
            full((rows, 1)),
            pl.BlockSpec((1, width, width), lambda i: (3, 0, 0)),
            full(vec.shape),
            whole,
        ],
        out_specs=[
            pl.BlockSpec((chips, part, width), lambda i: (0, 0, i)),
            pl.BlockSpec((chips, part, width), lambda i: (0, 0, i)),
            pl.BlockSpec((1, width), lambda i: (0, jnp.minimum(i, end))),
            whole,
            whole,
            whole,
            full((3, width)),
        ],
        out_shape=[
            jax.ShapeDtypeStruct((chips, part, hidden + width), BF),
            jax.ShapeDtypeStruct((chips, part, hidden + width), BF),
            jax.ShapeDtypeStruct((1, hidden), F32),
            jax.ShapeDtypeStruct((rows, width), F32),
            jax.ShapeDtypeStruct((rows, width), BF),
            jax.ShapeDtypeStruct((rows, width), BF),
            jax.ShapeDtypeStruct((3, width), F32),
        ],
        scratch_shapes=[pltpu.VMEM((rows, width), F32), pltpu.VMEM((rows, width), BF)],
        compiler_params=params(),
        cost_estimate=cost(28 * rows * width * width, 40 * rows * width),
        name="feed_back",
    )(place, branch, slope, low, down, up, outer, unit1, scale1, out_w, vec, ctx)


def attend_back_kernel(length, joined_ref, probs_ref, ctx_grad_ref, grad_ref, sum_ref):
    rows, width = ctx_grad_ref.shape
    pairs = width // PAIR

    def one(seq, carry):
        at = pl.ds(pl.multiple_of(seq * length, length), length)

        def columns(part, pair):
            return slice(part * width + pair * PAIR, part * width + (pair + 1) * PAIR)

        prob_grads = []
        for pair in range(pairs):
            vals = split_heads(joined_ref[at, columns(2, pair)])
            prob_grads.append(nt(vals, ctx_grad_ref[at, columns(0, pair)]))
        score_grads = []
        for pair in range(pairs):
            probs = probs_ref[seq, pair]
            halves = []
            for head in range(2):
                cut = slice(head * length, (head + 1) * length)
                held = probs[cut].astype(F32)
                part = prob_grads[pair][cut]
                base = jnp.sum(part * held, axis=0, keepdims=True)
                halves.append((held * (part - base)).astype(BF))
            score_grads.append(halves)
        for pair in range(pairs):
            probs = probs_ref[seq, pair]
            beside = jnp.concatenate([probs[:length], probs[length:]], axis=1)
            ctx_grads = split_heads(ctx_grad_ref[at, columns(0, pair)])
            grad_ref[at, columns(2, pair)] = nn(beside, ctx_grads).astype(BF)
        for pair in range(pairs):
            queries = split_heads(joined_ref[at, columns(0, pair)] * jnp.asarray(0.125, BF))
            beside = jnp.concatenate(score_grads[pair], axis=1)
            grad_ref[at, columns(1, pair)] = nn(beside, queries).astype(BF)
        for pair in range(pairs):
            keys = split_heads(joined_ref[at, columns(1, pair)])
            stacked = jnp.concatenate(score_grads[pair], axis=0)
            grad_ref[at, columns(0, pair)] = (tn(stacked, keys) * 0.125).astype(BF)
        return carry

    lax.fori_loop(0, rows // length, one, 0)
    total = jnp.zeros(sum_ref.shape, F32)
    for m in range(rows // length):
        total += jnp.sum(
            grad_ref[m * length : (m + 1) * length].astype(F32), axis=0, keepdims=True
        )

    @pl.when(pl.program_id(0) == 0)
    def _():
        sum_ref[...] = total

    @pl.when(pl.program_id(0) > 0)
    def _():
        sum_ref[...] += total


def attend_back(joined, probs, ctx_grad, length):
    rows, width = ctx_grad.shape
    count = rows // length
    steps = 2
    block = rows // steps
    pairs = width // PAIR
    return pl.pallas_call(
        functools.partial(attend_back_kernel, length),
        grid=(steps,),
        in_specs=[
            pl.BlockSpec((block, 3 * width), lambda i: (i, 0)),
            pl.BlockSpec((count // steps, pairs, 2 * length, length), lambda i: (i, 0, 0, 0)),
            pl.BlockSpec((block, width), lambda i: (i, 0)),
        ],
        out_specs=[
            pl.BlockSpec((block, 3 * width), lambda i: (i, 0)),
            full((1, 3 * width)),
        ],
        out_shape=[
            jax.ShapeDtypeStruct((rows, 3 * width), BF),
            jax.ShapeDtypeStruct((1, 3 * width), F32),
        ],
        compiler_params=params(),
        cost_estimate=cost(8 * rows * width * width, 20 * rows * width),
        name="attend_back",
    )(joined, probs, ctx_grad)


def weight_grads_kernel(tok_ref, joined_ref, small_ref, out_ref, turned_ref):
    step = pl.program_id(0)
    last = pl.num_programs(0) - 1
    shards, part, width = out_ref.shape

    @pl.when(step == 0)
    def _():
        turned_ref[...] = tok_ref[...].T

    value = nn(turned_ref[...], joined_ref[...])
    cols = pl.ds(pl.multiple_of(step * joined_ref.shape[1], joined_ref.shape[1]), joined_ref.shape[1])
    out_ref[:, :, cols] = value.reshape(shards, part, joined_ref.shape[1]).astype(BF)
    tail = 3 * joined_ref.shape[1]
    if width > tail:

        @pl.when(step == last)
        def _():
            lines = small_ref.shape[1]
            out_ref[:, lines:part, tail:width] = jnp.zeros(
                (shards, part - lines, width - tail), BF
            )
            out_ref[:, 0:lines, tail:width] = small_ref[...].astype(BF)


def weight_grads(tokens, joined_grad, small, shards, extra):
    rows, width = tokens.shape
    shape = (shards, width // shards, 3 * width + extra)
    return pl.pallas_call(
        weight_grads_kernel,
        grid=(3,),
        in_specs=[
            full((rows, width)),
            pl.BlockSpec((rows, width), lambda i: (0, i)),
            full(small.shape),
        ],
        out_specs=full(shape),
        out_shape=jax.ShapeDtypeStruct(shape, BF),
        scratch_shapes=[pltpu.VMEM((width, rows), BF)],
        compiler_params=params(),
        cost_estimate=cost(6 * rows * width * width, 20 * rows * width),
        name="weight_grads",
    )(tokens, joined_grad, small)


def input_kernel(inner_ref, joined_ref, w_ref, out_ref):
    width = inner_ref.shape[1]
    total = inner_ref[...]
    for part in range(3):
        total += nt(joined_ref[:, part * width : (part + 1) * width], w_ref[part])
    out_ref[...] = total.astype(BF)


def input_back(inner, joined_grad, qkv):
    rows, width = inner.shape
    steps = 4
    block = rows // steps
    return pl.pallas_call(
        input_kernel,
        grid=(steps,),
        in_specs=[
            pl.BlockSpec((block, width), lambda i: (i, 0)),
            pl.BlockSpec((block, 3 * width), lambda i: (i, 0)),
            full((3, width, width)),
        ],
        out_specs=pl.BlockSpec((block, width), lambda i: (i, 0)),
        out_shape=jax.ShapeDtypeStruct((rows, width), BF),
        compiler_params=params(),
        cost_estimate=cost(6 * rows * width * width, 12 * rows * width),
        name="input_back",
    )(inner, joined_grad, qkv)


def lay_kernel(plan, chips, reps, part, counts, place_ref, *refs):
    at = 0
    groups = []
    for number in counts:
        groups.append(refs[at : at + number])
        at += number
    sems = refs[-1]
    rep, chip, core = place_ref[0], place_ref[1], place_ref[2]
    copies = []

    def start(source, target):
        copies.append(pltpu.make_async_copy(source, target, sems.at[len(copies)]))
        copies[-1].start()

    finish = plan(start, groups, refs[at:-1], rep, chip, core, chips, reps, part)
    for copy in copies:
        copy.wait()
    if finish is not None:
        finish()


def blocks_plan(
    put, own, twin, along, across, swapped, depth, first, rep, chip, core, chips, reps, part
):
    for block in range(reps):
        put(own(block), block, chip, core)
        put(twin(block), block, chip, 1 - core)
    for step in range(1, chips):
        source = lax.rem(chip + chips - step, chips)
        rows = pl.ds((step - 1) * depth + first, part)
        for other, block in along.items():
            put(block(step, source, 0), rep ^ other, source, core)
            put(block(step, source, 1), rep ^ other, source, 1 - core)
        for other in across:
            put(across[other].at[rows], rep ^ other, source, core)
            put(swapped[other].at[rows], rep ^ other, source, 1 - core)


def wide_put(start, out_ref, part):
    def put(source, block, at_chip, at_core):
        row = pl.multiple_of((at_chip * 2 + at_core) * part, part)
        start(source, out_ref.at[block, pl.ds(row, part)])

    return put


def wide_block(ref, width, part):
    return lambda block: ref.at[pl.ds(0, part), pl.ds(block * width, width)]


def first_plan(start, groups, outs, rep, chip, core, chips, reps, part):
    (own, twin), along, across, swapped, (extra,) = groups
    out_ref, vec_ref, more_ref = outs
    width = out_ref.shape[2]

    def near(step, source, side):
        if side == 0:
            return along[step - 1].at[pl.ds(0, part)]
        return swapped[0].at[pl.ds((step - 1) * part, part)]

    blocks_plan(
        wide_put(start, out_ref, part),
        wide_block(own, width, part),
        wide_block(twin, width, part),
        {0: near},
        {at + 1: ref for at, ref in enumerate(across)},
        {at + 1: ref for at, ref in enumerate(swapped[1:])},
        part,
        0,
        rep,
        chip,
        core,
        chips,
        reps,
        part,
    )
    tail = pl.ds(part, 16)
    cols = pl.ds(0, width)
    start(own.at[tail, cols], more_ref.at[chip * 2 + core])
    start(twin.at[tail, cols], more_ref.at[chip * 2 + 1 - core])
    for step in range(1, chips):
        source = lax.rem(chip + chips - step, chips)
        start(along[step - 1].at[tail], more_ref.at[source * 2 + core])
        start(extra.at[pl.ds((step - 1) * 16, 16)], more_ref.at[source * 2 + 1 - core])

    def finish():
        lane = lax.broadcasted_iota(jnp.int32, (LANES, width), 0)
        place = lax.broadcasted_iota(jnp.int32, (LANES, width), 1)
        total = jnp.zeros((16, width), F32)
        for shard in range(2 * chips):
            there = (place - shard * part == lane) & (lane < part)
            total += nn(more_ref[shard, :, 0:LANES], there.astype(F32).astype(BF))
        vec_ref[...] = total

    return finish


def second_plan(start, groups, outs, rep, chip, core, chips, reps, part):
    (up, up_twin, down, down_twin), (close, far), across, swapped = groups
    up_ref, down_ref = outs
    width = up_ref.shape[2]
    where = (rep, chip, core, chips, reps, part)

    def chained(chain, first):
        def block(step, source, side):
            shard = source * 2 + (core if side == 0 else 1 - core)
            return chain.at[shard, pl.ds(first, part)]

        return block

    across = dict(zip(NEAR, across))
    swapped = dict(zip(NEAR, swapped))
    blocks_plan(
        wide_put(start, up_ref, part),
        wide_block(up, width, part),
        wide_block(up_twin, width, part),
        {0: chained(close, 0), FAR: chained(far, 0)},
        across,
        swapped,
        2 * part,
        0,
        *where,
    )

    def put(source, block, at_chip, at_core):
        row = pl.multiple_of(block * part, part)
        start(source, down_ref.at[at_chip * 2 + at_core, pl.ds(row, part)])

    def tall(ref):
        return lambda block: ref.at[pl.ds(block * part, part)]

    blocks_plan(
        put,
        tall(down),
        tall(down_twin),
        {0: chained(close, part), FAR: chained(far, part)},
        across,
        swapped,
        2 * part,
        part,
        *where,
    )


def lay(plan, place, groups, shapes, scratch, copies, part, chips, reps):
    anywhere = pl.BlockSpec(memory_space=pl.ANY)
    inputs = [ref for group in groups for ref in group]
    return pl.pallas_call(
        functools.partial(
            lay_kernel, plan, chips, reps, part, [len(group) for group in groups]
        ),
        in_specs=[pl.BlockSpec(memory_space=pltpu.SMEM)] + [anywhere] * len(inputs),
        out_specs=[pl.BlockSpec(memory_space=pltpu.VMEM)] * len(shapes),
        out_shape=[jax.ShapeDtypeStruct(shape, kind) for shape, kind in shapes],
        scratch_shapes=[pltpu.VMEM(shape, BF) for shape in scratch]
        + [pltpu.SemaphoreType.DMA((copies,))],
        compiler_params=pltpu.CompilerParams(vmem_limit_bytes=VMEM_BYTES),
        cost_estimate=cost(0, 4 * sum(math.prod(shape) for shape, kind in shapes)),
        name="lay",
    )(place, *inputs)


def pack_vectors(rows, up_bias, class_weight):
    part = rows[0].shape[0]
    lines = [row[None] for row in rows[:8]] + [class_weight.T] + [row[None] for row in rows[8:]]
    pieces = up_bias.shape[0] // part
    lines += [up_bias[None, at * part : (at + 1) * part] for at in range(pieces)]
    return jnp.concatenate(lines, axis=0)


def move(values, reps, chips, target):
    pairs = []
    for rep in range(reps):
        for chip in range(chips):
            for core in range(2):
                to_rep, to_chip, to_core = target(rep, chip, core)
                pairs.append(
                    (
                        (rep * chips + chip) * 2 + core,
                        (to_rep * chips + to_chip) * 2 + to_core,
                    )
                )
    return lax.ppermute(values, ("rep", "fsdp"), pairs)


def along_chips(step, chips):
    return lambda rep, chip, core: (rep, (chip + step) % chips, core)


def across_reps(other):
    return lambda rep, chip, core: (rep ^ other, chip, core)


def to_twin(rep, chip, core):
    return rep, chip, 1 - core


def after(values, *gates):
    return lax.optimization_barrier((values, *gates))[0]


def along_z(mine, reps, chips):
    return [move(mine, reps, chips, along_chips(step, chips)) for step in range(1, chips)]


def over_reps(stacked, reps, chips, others):
    return [move(stacked, reps, chips, across_reps(other)) for other in others]


def pick(parts, at):
    return lax.dynamic_index_in_dim(parts, at, axis=0, keepdims=False)


def in_order(rep, reps, own, others, axis):
    blocks = jnp.stack([own] + others)
    return jnp.concatenate([pick(blocks, rep ^ at) for at in range(reps)], axis=axis)


class Reduction:
    def __init__(self, place, keep, send, reps, chips, by_chain=False):
        self.rep, self.chip = place[0], place[1]
        self.reps, self.chips = reps, chips
        self.shape = (chips, reps, keep.shape[1] // reps, keep.shape[2])
        self.keep = keep.reshape(self.shape)
        self.others_of = range(1, reps)
        self.far = None
        if by_chain:
            self.others_of = NEAR
            first = place[2] == 0
            kept = lax.dynamic_index_in_dim(self.keep, self.rep ^ FAR, axis=1, keepdims=False)
            sent = lax.dynamic_index_in_dim(
                send.reshape(self.shape), self.rep ^ FAR, axis=1, keepdims=False
            )
            pair = jnp.stack(
                [jnp.where(first, kept, sent), jnp.where(first, sent, kept)], axis=1
            )
            self.far = lax.psum_scatter(
                pair.reshape(-1, keep.shape[2]), "fsdp", scatter_dimension=0, tiled=True
            )
        self.got = move(send, reps, chips, to_twin)

    def at_rep(self, at):
        kept = lax.dynamic_index_in_dim(self.keep, at, axis=1, keepdims=False)
        came = lax.dynamic_index_in_dim(
            self.got.reshape(self.shape), at, axis=1, keepdims=False
        )
        return kept.astype(F32) + came.astype(F32)

    def over_reps(self, *gates):
        if gates:
            self.got = after(self.got, *gates)
        self.arrived = [
            move(
                self.at_rep(self.rep ^ other).astype(BF),
                self.reps,
                self.chips,
                across_reps(other),
            )
            for other in self.others_of
        ]

    def over_chips(self, *gates):
        if gates:
            self.arrived = [after(block, *gates) for block in self.arrived]
        mine = self.at_rep(self.rep)

        def both_at(at):
            total = pick(mine, at)
            for block in self.arrived:
                total = total + pick(block, at).astype(F32)
            return total

        self.total = both_at(self.chip)
        if self.far is not None:
            came = move(self.far, self.reps, self.chips, across_reps(FAR))
            self.total = self.total + came.astype(F32)
        self.passed = [
            move(
                both_at(lax.rem(self.chip + step, self.chips)).astype(BF),
                self.reps,
                self.chips,
                along_chips(step, self.chips),
            )
            for step in range(1, self.chips)
        ]

    def chip_sum(self):
        total = self.total
        for block in self.passed:
            total = total + block.astype(F32)
        return total.astype(BF)


def share_reps(place, total, reps, chips):
    others = [move(total, reps, chips, across_reps(other)) for other in range(1, reps)]
    return in_order(place[0], reps, total, others, 0).astype(F32), others


def exchange_reps(place, rows, reps, chips):
    rep = place[0]
    parts = rows.reshape(reps, -1, rows.shape[1])
    total = pick(parts, rep).astype(F32)
    arrived = [
        move(pick(parts, rep ^ other), reps, chips, across_reps(other))
        for other in range(1, reps)
    ]
    for block in arrived:
        total = total + block.astype(F32)
    return total.astype(BF), arrived


def per_device(
    tokens,
    exit_layer,
    qkv_weight,
    query_bias,
    value_bias,
    out_weight,
    out_bias,
    attn_gain,
    attn_shift,
    up_weight,
    up_bias,
    down_weight,
    down_bias,
    block_gain,
    block_shift,
    pool_weight,
    pool_bias,
    class_weight,
    class_bias,
    output_grad,
    logit_grad,
):
    reps = lax.axis_size("rep")
    shards = lax.axis_size("fsdp")
    mine = lax.axis_index("fsdp")
    rows, width = tokens.shape
    count = exit_layer.shape[0]
    length = rows // count
    classes = class_weight.shape[1]
    part = out_weight.shape[0]
    hidden = up_weight.shape[1]

    def gather(shard):
        return lax.all_gather(shard, "fsdp", axis=0, tiled=True)

    packed = pack_vectors(
        [
            query_bias,
            value_bias,
            out_bias,
            attn_gain,
            attn_shift,
            down_bias,
            block_gain,
            block_shift,
            pool_bias,
        ],
        up_bias,
        class_weight,
    )
    joint_own = jnp.concatenate([qkv_weight, out_weight], axis=1)
    deep = down_weight.shape[0]
    chips = shards // 2
    place = jnp.stack([lax.axis_index("rep"), mine // 2, mine % 2]).astype(jnp.int32)
    direct = (
        part % 16 == 0
        and reps & (reps - 1) == 0
        and reps * width == hidden
        and reps == 4
        and packed.shape[0] <= 16
    )
    if direct:
        lines = packed.shape[0]
        held = jnp.pad(packed, ((0, 16 - lines), (0, width - part)))
        own = jnp.concatenate([joint_own, jnp.tile(held, (1, reps))], axis=0)
        rep = place[0]

        def block_of(weights, at):
            return lax.dynamic_slice_in_dim(weights, at * width, width, axis=1)

        def second_of(at):
            return [
                block_of(up_weight, at),
                lax.dynamic_slice_in_dim(down_weight, at * part, part, axis=0),
            ]

        along = along_z(block_of(own, rep), reps, chips)
        chain = gather(after(jnp.concatenate(second_of(rep), axis=0), *along))
        chain = chain.reshape(chips, 2, 2 * part, width)
        twin = move(own, reps, chips, to_twin)
        stacked = jnp.concatenate([rows_[:part] for rows_ in along], axis=0)
        across = over_reps(stacked, reps, chips, range(1, reps))
        far_chain = gather(after(jnp.concatenate(second_of(rep ^ FAR), axis=0), *across))
        swapped = [move(rows_, reps, chips, to_twin) for rows_ in [stacked] + across]
        extra = move(
            jnp.concatenate([rows_[part:] for rows_ in along], axis=0), reps, chips, to_twin
        )
        up_twin = move(up_weight, reps, chips, to_twin)
        down_twin = move(down_weight, reps, chips, to_twin)
        joint, vec = lay(
            first_plan,
            place,
            [
                [own, twin],
                along,
                across,
                swapped,
                [extra],
            ],
            [((reps, width, width), BF), ((16, width), F32)],
            [(shards, 16, width)],
            2 * chips * (reps + 1),
            part,
            chips,
            reps,
        )
        mine_chain = lax.dynamic_index_in_dim(
            after(chain, joint), place[2], axis=1, keepdims=False
        )
        second_stacked = jnp.concatenate(
            [
                pick(mine_chain, lax.rem(place[1] + chips - step, chips))
                for step in range(1, chips)
            ],
            axis=0,
        )
        second_across = over_reps(after(second_stacked, *across), reps, chips, NEAR)
        up_row = (
            vec[VECTOR_ROWS:lines].reshape(-1, shards, part).transpose(1, 0, 2).reshape(1, hidden)
        )
        down_block = (width // deep, deep, width)
    else:
        small = gather(packed[None])
        vec = small[:, :VECTOR_ROWS].transpose(1, 0, 2).reshape(VECTOR_ROWS, width).astype(F32)
        vec = jnp.pad(vec, ((0, 16 - VECTOR_ROWS), (0, 0)))
        up_row = small[:, VECTOR_ROWS:].transpose(0, 1, 2).reshape(1, hidden).astype(F32)
        pool = gather(pool_weight)
        joint = jnp.stack(jnp.split(gather(joint_own), 4, axis=1))
        up = jnp.stack(jnp.split(gather(up_weight), hidden // width, axis=1))
        down = gather(down_weight).reshape(-1, width, width)
        down_block = (1, width, width)
    joined, probs, ctx = attend(tokens, joint, vec, length)
    if direct:
        pool = gather(after(pool_weight, ctx))
        far_chain = after(far_chain, ctx)
        second_swapped = [
            move(after(rows_, ctx), reps, chips, to_twin) for rows_ in second_across
        ]
        up, down = lay(
            second_plan,
            place,
            [
                [up_weight, up_twin, down_weight, down_twin],
                [
                    chain.reshape(shards, 2 * part, width),
                    far_chain.reshape(shards, 2 * part, width),
                ],
                second_across,
                second_swapped,
            ],
            [((reps, width, width), BF), ((shards, deep, width), BF)],
            [],
            4 * chips * reps,
            part,
            chips,
            reps,
        )
    turned, act, slope, unit1, scale1, unit2, scale2, output = feed(
        exit_layer, tokens, ctx, joint, vec, up, up_row, down, down_block, length
    )
    class_bias_row = jnp.pad(class_bias.astype(F32), (0, 8 - classes))[None]
    logit_grad_rows = jnp.pad(logit_grad, ((0, 0), (0, 8 - classes)))
    outer, branch, low_grad, exit_sums, class_grad, logits, stats = leave(
        exit_layer,
        output,
        unit2,
        scale2,
        output_grad,
        pool,
        vec,
        class_bias_row,
        logit_grad_rows,
        act,
        full((width, width)),
        shards,
        length,
        classes,
    )
    up_keep, up_send, up_sum, inner, attended, ctx_grad, feed_sums = feed_back(
        place, chips, branch, slope, turned, down, down_block, up, outer, unit1, scale1, joint, vec, ctx
    )
    if direct:
        up_red = Reduction(place, up_keep, up_send, reps, chips)
        ctx_grad = after(ctx_grad, up_red.got)
    joined_grad, joined_sum = attend_back(joined, probs, ctx_grad, length)
    joined_seen = joined_grad
    if direct:
        up_red.over_reps()
        joined_seen = after(joined_grad, up_red.arrived[0])
    sums = jnp.concatenate(
        [
            joined_sum.reshape(3, width)[::2],
            feed_sums,
            exit_sums,
            class_grad[:classes],
        ],
        axis=0,
    )
    lines = sums.shape[0]
    own_sums = sums.reshape(lines, shards, part).transpose(1, 0, 2).reshape(shards, lines * part)
    own_sums = jnp.concatenate([own_sums, up_sum.reshape(shards, deep)], axis=1)
    used = own_sums.shape[1]
    seqs_total = count * reps * shards
    figures = jnp.concatenate([stats[0, :1], stats[1, :classes]])
    slots = reps * shards * figures.shape[0] * 3
    direct = direct and used + slots <= part * LANES
    small_lines = 16
    if direct:
        high = figures.astype(BF).astype(F32)
        middle = (figures - high).astype(BF).astype(F32)
        lowest = figures - high - middle
        split = jnp.concatenate([high, middle, lowest])
        slot = lax.axis_index("rep") * shards + mine
        lone = jnp.where(
            jnp.arange(reps * shards)[:, None] == slot, split[None], 0.0
        ).reshape(1, slots)
        row = jnp.concatenate([own_sums, jnp.broadcast_to(lone, (shards, slots))], axis=1)
        small_lines = -(-row.shape[1] // (LANES * 16)) * 16
        row = jnp.pad(row, ((0, 0), (0, small_lines * LANES - row.shape[1])))
        row = row.reshape(shards, small_lines, LANES)
    else:
        row = jnp.zeros((shards, small_lines, LANES), F32)
    joint_grad = weight_grads(tokens, joined_seen, row, shards, LANES if direct else 0)
    input_grad = input_back(inner, joined_grad, joint)

    def scatter(grad):
        return lax.psum_scatter(grad, "fsdp", scatter_dimension=0, tiled=True)

    low_part = scatter(low_grad.reshape(-1, width))
    if direct:
        joint_grad = after(joint_grad, low_part, *up_red.arrived)
    joint_part = scatter(joint_grad.reshape(width, -1))
    if direct:
        up_red.over_chips(joint_grad)
        low_total, low_arrived = exchange_reps(
            place, after(low_part, *up_red.passed), reps, chips
        )
        wide = (deep + part) * width // part
        up_total = up_red.chip_sum()
        columns = up_total.shape[1]
        pair, pair_others = share_reps(
            place,
            jnp.concatenate([up_total, low_total.reshape(-1, wide)], axis=1),
            reps,
            chips,
        )
        up_sum = pair[:, :columns]
        low_sum = pair[:, columns:].reshape(deep + part, width)
        joint_total, _ = exchange_reps(
            place, after(joint_part, *pair_others), reps, chips
        )
        joint_sum, _ = share_reps(place, joint_total, reps, chips)
        small_sum = joint_sum[:small_lines, 3 * width :].reshape(-1)
        total = small_sum[used : used + slots].reshape(-1, figures.shape[0]).sum(axis=0)
    else:
        first = mine % 2 == 0

        def whole_of(kept, sent):
            pair = jnp.stack([jnp.where(first, kept, sent), jnp.where(first, sent, kept)], axis=1)
            return pair.reshape(-1, kept.shape[2])

        joint_sum, low_sum, up_sum = lax.psum(
            (joint_part, low_part, scatter(whole_of(up_keep, up_send))), "rep"
        )
        joint_sum, low_sum, up_sum = (
            joint_sum.astype(F32),
            low_sum.astype(F32),
            up_sum.astype(F32),
        )
        own_sums, total = lax.psum((own_sums, figures), ("rep", "fsdp"))
        small_sum = pick(own_sums, mine)
    own = small_sum[: lines * part].reshape(lines, part)
    return (
        output,
        logits[:, :classes],
        total[0] / seqs_total,
        input_grad,
        joint_sum[:, : 3 * width],
        own[0],
        own[1],
        up_sum[:, hidden:],
        own[4],
        own[2],
        own[3],
        up_sum[:, :hidden],
        small_sum[lines * part : used],
        low_sum[:deep],
        own[7],
        own[5],
        own[6],
        low_sum[deep:],
        own[8],
        own[9 : 9 + classes].T,
        total[1:],
    )


def solution(mesh):
    return jax.shard_map(
        per_device,
        mesh=mesh,
        in_specs=(
            P(("rep", "fsdp"), None),
            P(("rep", "fsdp")),
            P("fsdp", None),
            P("fsdp"),
            P("fsdp"),
            P("fsdp", None),
            P("fsdp"),
            P("fsdp"),
            P("fsdp"),
            P("fsdp", None),
            P("fsdp"),
            P("fsdp", None),
            P("fsdp"),
            P("fsdp"),
            P("fsdp"),
            P("fsdp", None),
            P("fsdp"),
            P("fsdp", None),
            P(),
            P(("rep", "fsdp"), None),
            P(("rep", "fsdp"), None),
        ),
        out_specs=(
            P(("rep", "fsdp"), None),
            P(("rep", "fsdp"), None),
            P(),
            P(("rep", "fsdp"), None),
            P("fsdp", None),
            P("fsdp"),
            P("fsdp"),
            P("fsdp", None),
            P("fsdp"),
            P("fsdp"),
            P("fsdp"),
            P("fsdp", None),
            P("fsdp"),
            P("fsdp", None),
            P("fsdp"),
            P("fsdp"),
            P("fsdp"),
            P("fsdp", None),
            P("fsdp"),
            P("fsdp", None),
            P(),
        ),
        check_vma=False,
    )
```

```python
import functools
import math

import jax
import jax.numpy as jnp
from jax import lax
from jax.experimental import pallas as pl
from jax.experimental.pallas import tpu as pltpu
from jax.sharding import PartitionSpec as P

HD = 64
LAYER = 6
PAIR = 2 * HD
NEAR = (1, 2)
FAR = 3
LANES = 128
VMEM_BYTES = 58 * 2**20
BF = jnp.bfloat16
F32 = jnp.float32

QUERY_BIAS, VALUE_BIAS, OUT_BIAS, ATTN_GAIN, ATTN_SHIFT = 0, 1, 2, 3, 4
DOWN_BIAS, BLOCK_GAIN, BLOCK_SHIFT, CLASS_ROWS, POOL_BIAS = 5, 6, 7, 8, 11
VECTOR_ROWS = 12


def nn(left, right):
    return jnp.dot(left, right, preferred_element_type=F32)


def tn(left, right):
    return lax.dot_general(left, right, (((0,), (0,)), ((), ())), preferred_element_type=F32)


def nt(left, right):
    return lax.dot_general(left, right, (((1,), (1,)), ((), ())), preferred_element_type=F32)


def full(shape):
    return pl.BlockSpec(shape, lambda *at: (0,) * len(shape))


def params():
    return pltpu.CompilerParams(
        dimension_semantics=("arbitrary",), vmem_limit_bytes=VMEM_BYTES
    )


def cost(flops, moved, trans=0):
    return pl.CostEstimate(flops=flops, bytes_accessed=moved, transcendentals=trans)


def split_heads(pair):
    lane = lax.broadcasted_iota(jnp.int32, pair.shape, 1)
    zero = jnp.zeros_like(pair)
    return jnp.concatenate(
        [jnp.where(lane < HD, pair, zero), jnp.where(lane < HD, zero, pair)], axis=0
    )


def norm_stats(values):
    center = values - jnp.mean(values, axis=-1, keepdims=True)
    spread = jnp.mean(center * center, axis=-1, keepdims=True)
    scale = lax.rsqrt(spread + 1e-06)
    return center * scale, scale


def norm_back(grad, unit, scale, gain):
    inner = grad * gain
    first = jnp.mean(inner, axis=-1, keepdims=True)
    second = jnp.mean(inner * unit, axis=-1, keepdims=True)
    return scale * (inner - first - unit * second)


def gelu_parts(values):
    base = 1.0 + 0.23164189 * jnp.abs(values)
    t = pl.reciprocal(base, approx=True)
    t = t * (2.0 - base * t)
    bell = jnp.exp2((values * values) * -0.7213475204444817)
    poly = t * (
        0.127414796
        + t * (-0.142248368 + t * (0.7107068705 + t * (-0.7265760135 + t * 0.5307027145)))
    )
    tail = poly * bell
    below = jnp.where(values >= 0.0, 1.0 - tail, tail)
    return values * below, below + values * (bell * 0.3989422804014327)


def attend_kernel(length, tok_ref, w_ref, vec_ref, joined_ref, probs_ref, ctx_ref):
    rows, width = ctx_ref.shape
    pairs = width // PAIR
    for part in range(3):
        cols = slice(part * width, (part + 1) * width)
        value = nn(tok_ref[...], w_ref[part])
        if part == 0:
            value += vec_ref[QUERY_BIAS : QUERY_BIAS + 1]
        elif part == 2:
            value += vec_ref[VALUE_BIAS : VALUE_BIAS + 1]
        joined_ref[:, cols] = value.astype(BF)

    def one(seq, carry):
        at = pl.ds(pl.multiple_of(seq * length, length), length)
        scores = []
        for pair in range(pairs):
            query = joined_ref[at, pair * PAIR : (pair + 1) * PAIR] * jnp.asarray(0.125, BF)
            keys = split_heads(joined_ref[at, width + pair * PAIR : width + (pair + 1) * PAIR])
            scores.append(nt(keys, query))
        all_probs = []
        for pair in range(pairs):
            halves = []
            for head in range(2):
                part = scores[pair][head * length : (head + 1) * length]
                part = jnp.exp(part - jnp.max(part, axis=0, keepdims=True))
                part = part * (1.0 / jnp.sum(part, axis=0, keepdims=True))
                halves.append(part.astype(BF))
            probs = jnp.concatenate(halves, axis=0)
            probs_ref[seq, pair] = probs
            all_probs.append(probs)
        for pair in range(pairs):
            vals = split_heads(
                joined_ref[at, 2 * width + pair * PAIR : 2 * width + (pair + 1) * PAIR]
            )
            ctx_ref[at, pair * PAIR : (pair + 1) * PAIR] = tn(all_probs[pair], vals).astype(BF)
        return carry

    lax.fori_loop(0, rows // length, one, 0)


def attend(tokens, qkv, vec, length):
    rows, width = tokens.shape
    count = rows // length
    steps = 2
    block = rows // steps
    pairs = width // PAIR
    return pl.pallas_call(
        functools.partial(attend_kernel, length),
        grid=(steps,),
        in_specs=[
            pl.BlockSpec((block, width), lambda i: (i, 0)),
            full((3, width, width)),
            full(vec.shape),
        ],
        out_specs=[
            pl.BlockSpec((block, 3 * width), lambda i: (i, 0)),
            pl.BlockSpec((count // steps, pairs, 2 * length, length), lambda i: (i, 0, 0, 0)),
            pl.BlockSpec((block, width), lambda i: (i, 0)),
        ],
        out_shape=[
            jax.ShapeDtypeStruct((rows, 3 * width), BF),
            jax.ShapeDtypeStruct((count, pairs, 2 * length, length), BF),
            jax.ShapeDtypeStruct((rows, width), BF),
        ],
        compiler_params=params(),
        cost_estimate=cost(8 * rows * width * width, 20 * rows * width, rows * width),
        name="attend",
    )(tokens, qkv, vec)


def feed_kernel(
    length,
    load,
    inputs,
    place_ref,
    exit_ref,
    tok_ref,
    ctx_ref,
    out_w_ref,
    vec_ref,
    up_b_ref,
    *refs,
):
    weights, refs = refs[:inputs], refs[inputs:]
    (
        turned_ref,
        act_ref,
        slope_ref,
        unit1_ref,
        scale1_ref,
        unit2_ref,
        scale2_ref,
        output_ref,
        *more,
        acc_ref,
        low_ref,
        line_ref,
    ) = refs[: 11 + (2 if load else 0)]
    step = pl.program_id(0)
    last = pl.num_programs(0) - 1
    rows, width = tok_ref.shape
    sub = 256
    if load:
        up_all, down_all, sems, out_sems = refs[13:]
        each = down_all.shape[0] // up_all.shape[0]
        stores = [
            pltpu.make_async_copy(up_all, more[0], out_sems.at[0]),
            pltpu.make_async_copy(down_all, more[1], out_sems.at[1]),
        ]

        def up_part(cols):
            return up_all[step, :, cols]

        def down_part(cols):
            return down_all[pl.ds(step * each, each), :, cols].reshape(width, sub)

    else:

        def up_part(cols):
            return weights[0][0, :, cols]

        def down_part(cols):
            return weights[1][:, :, cols].reshape(width, sub)

    @pl.when(step == 0)
    def _():
        if load:
            copies = load(weights, up_all, down_all, place_ref, sems)
        for m in range(rows // sub):
            at = slice(m * sub, (m + 1) * sub)
            inner = tok_ref[at].astype(F32) + (
                nn(ctx_ref[at], out_w_ref[0]) + vec_ref[OUT_BIAS : OUT_BIAS + 1]
            )
            unit, scale = norm_stats(inner)
            first = unit * vec_ref[ATTN_GAIN : ATTN_GAIN + 1] + vec_ref[ATTN_SHIFT : ATTN_SHIFT + 1]
            unit1_ref[at] = unit.astype(BF)
            scale1_ref[at] = scale
            low = first.astype(BF)
            low_ref[at] = low
            turned_ref[:, at] = low.T
            acc_ref[at] = first + vec_ref[DOWN_BIAS : DOWN_BIAS + 1]
        if load:
            for copy in copies:
                copy.wait()
            for store in stores:
                store.start()

    tiles = [(m, n) for m in range(rows // sub) for n in range(width // sub)]

    def rows_of(m):
        return slice(m * sub, (m + 1) * sub)

    def first_product(tile):
        return nn(low_ref[rows_of(tile[0])], up_part(rows_of(tile[1])))

    def second_product(m, n):
        at, cols = rows_of(m), rows_of(n)
        acc_ref[at, cols] += nn(line_ref[m % 2], down_part(cols))

    ahead = first_product(tiles[0])
    for index, (m, n) in enumerate(tiles):
        at, cols = rows_of(m), rows_of(n)
        hidden = ahead + up_b_ref[:, cols]
        if index + 1 < len(tiles):
            ahead = first_product(tiles[index + 1])
        if m > 0:
            second_product(m - 1, n)
        act, slope = gelu_parts(hidden)
        act = act.astype(BF)
        line_ref[m % 2, :, cols] = act
        act_ref[cols, at] = act.T
        slope_ref[at, cols] = slope.astype(BF)
    for n in range(width // sub):
        second_product(rows // sub - 1, n)

    @pl.when(step == last)
    def _():
        for seq in range(rows // length):
            at = slice(seq * length, (seq + 1) * length)
            active = (exit_ref[seq] >= LAYER).astype(F32)
            unit, scale = norm_stats(acc_ref[at])
            unit2_ref[at] = unit.astype(BF)
            scale2_ref[at] = scale
            result = (
                unit * vec_ref[BLOCK_GAIN : BLOCK_GAIN + 1] + vec_ref[BLOCK_SHIFT : BLOCK_SHIFT + 1]
            ) * active
            output_ref[at] = result.astype(BF)
        if load:
            for store in stores:
                store.wait()


def feed(place, exit_layer, tokens, ctx, out_w, vec, up_bias, weights, load, shapes, length):
    rows, width = tokens.shape
    hidden = up_bias.shape[1]
    steps = hidden // width
    whole = full((rows, width))
    if load:
        weight_specs = [pl.BlockSpec(memory_space=pl.ANY)] * len(weights)
        more_specs = [pl.BlockSpec(memory_space=pl.ANY)] * 2
        more = [jax.ShapeDtypeStruct(shape, BF) for shape in shapes]
        copies = 2 * shapes[1][0] * shapes[0][0]
        scratch = [pltpu.VMEM(shape, BF) for shape in shapes] + [
            pltpu.SemaphoreType.DMA((copies,)),
            pltpu.SemaphoreType.DMA((2,)),
        ]
    else:
        weight_specs = [
            pl.BlockSpec((1, width, width), lambda i: (i, 0, 0)),
            pl.BlockSpec((1, width, width), lambda i: (i, 0, 0)),
        ]
        more_specs, more, scratch = [], [], []
    return pl.pallas_call(
        functools.partial(feed_kernel, length, load, len(weights)),
        grid=(steps,),
        in_specs=[
            pl.BlockSpec(memory_space=pltpu.SMEM),
            pl.BlockSpec(memory_space=pltpu.SMEM),
            whole,
            whole,
            pl.BlockSpec((1, width, width), lambda i: (3, 0, 0)),
            full(vec.shape),
            pl.BlockSpec((1, width), lambda i: (0, i)),
        ]
        + weight_specs,
        out_specs=[
            full((width, rows)),
            pl.BlockSpec((width, rows), lambda i: (i, 0)),
            pl.BlockSpec((rows, width), lambda i: (0, i)),
            whole,
            full((rows, 1)),
            whole,
            full((rows, 1)),
            whole,
        ]
        + more_specs,
        out_shape=[
            jax.ShapeDtypeStruct((width, rows), BF),
            jax.ShapeDtypeStruct((hidden, rows), BF),
            jax.ShapeDtypeStruct((rows, hidden), BF),
            jax.ShapeDtypeStruct((rows, width), BF),
            jax.ShapeDtypeStruct((rows, 1), F32),
            jax.ShapeDtypeStruct((rows, width), BF),
            jax.ShapeDtypeStruct((rows, 1), F32),
            jax.ShapeDtypeStruct((rows, width), BF),
        ]
        + more,
        scratch_shapes=[
            pltpu.VMEM((rows, width), F32),
            pltpu.VMEM((rows, width), BF),
            pltpu.VMEM((2, 256, width), BF),
        ]
        + scratch,
        compiler_params=params(),
        cost_estimate=cost(18 * rows * width * width, 40 * rows * width, 8 * rows * width),
        name="feed",
    )(place, exit_layer, tokens, ctx, out_w, vec, up_bias, *weights)


def load_second(counts, chips, reps, part, weights, up_all, down_all, place_ref, sems):
    at = 0
    groups = []
    for number in counts:
        groups.append(weights[at : at + number])
        at += number
    copies = []

    def start(source, target):
        copies.append(pltpu.make_async_copy(source, target, sems.at[len(copies)]))
        copies[-1].start()

    second_plan(
        start,
        groups,
        (up_all, down_all),
        place_ref[0],
        place_ref[1],
        place_ref[2],
        chips,
        reps,
        part,
    )
    return copies


def leave_kernel(
    length,
    classes,
    exit_ref,
    output_ref,
    unit2_ref,
    scale2_ref,
    grad_ref,
    pool_ref,
    vec_ref,
    class_bias_ref,
    logit_grad_ref,
    act_ref,
    outer_ref,
    branch_ref,
    joint_grad_ref,
    sums_ref,
    class_grad_ref,
    logits_ref,
    stats_ref,
    lead_ref,
    pool_grad_ref,
):
    step = pl.program_id(0)
    rows, width = output_ref.shape
    pool = pool_ref[...].reshape(width, width)
    count = rows // length

    @pl.when(step == 0)
    def _():
        place = lax.broadcasted_iota(jnp.int32, (count, 1), 0)
        active = jnp.zeros((count, 1), F32)
        for seq in range(count):
            on = (exit_ref[seq] >= LAYER).astype(F32)
            active = jnp.where(place == seq, on, active)
        leading = jnp.concatenate(
            [output_ref[seq * length : seq * length + 1].astype(F32) for seq in range(count)],
            axis=0,
        ).astype(BF)
        pooled = jnp.tanh(nn(leading, pool) + vec_ref[POOL_BIAS : POOL_BIAS + 1])
        pooled_low = pooled.astype(BF)
        used = lax.broadcasted_iota(jnp.int32, (8, width), 0) < classes
        class_rows = jnp.where(used, vec_ref[CLASS_ROWS : CLASS_ROWS + 8], 0.0).astype(BF)
        raw = nt(pooled_low, class_rows) + class_bias_ref[...]
        lane = lax.broadcasted_iota(jnp.int32, raw.shape, 1) < classes
        top = jnp.max(jnp.where(lane, raw, -jnp.inf), axis=-1, keepdims=True)
        spread = jnp.where(lane, jnp.exp(raw - top), 0.0)
        logprob = raw - top - jnp.log(jnp.sum(spread, axis=-1, keepdims=True))
        entropy = -jnp.sum(
            jnp.where(lane, jnp.exp(logprob) * logprob, 0.0), axis=-1, keepdims=True
        )
        logits_ref[...] = raw * active
        class_grad = (logit_grad_ref[...].astype(F32) * active).astype(BF)
        stats_ref[0:1] = jnp.broadcast_to(jnp.sum(entropy * active, axis=0, keepdims=True), (1, 8))
        stats_ref[1:2] = jnp.sum(class_grad.astype(F32), axis=0, keepdims=True)
        class_grad_ref[...] = tn(class_grad, pooled_low)
        pooled_grad = nn(class_grad, class_rows)
        pre_grad = (pooled_grad * (1.0 - pooled * pooled)).astype(BF)
        sums_ref[3:4] = jnp.sum(pre_grad.astype(F32), axis=0, keepdims=True)
        pool_grad_ref[...] = tn(leading, pre_grad).reshape(pool_grad_ref.shape).astype(BF)
        lead_ref[...] = nt(pre_grad, pool)
        head = lax.broadcasted_iota(jnp.int32, (length, 1), 0) == 0
        gain = vec_ref[BLOCK_GAIN : BLOCK_GAIN + 1]
        gain_sum = jnp.zeros((1, width), F32)
        shift_sum = jnp.zeros((1, width), F32)
        bias_sum = jnp.zeros((1, width), F32)
        for seq in range(count):
            at = slice(seq * length, (seq + 1) * length)
            on = (exit_ref[seq] >= LAYER).astype(F32)
            top_grad = (
                grad_ref[at].astype(F32) + jnp.where(head, lead_ref[seq : seq + 1], 0.0)
            ) * on
            unit = unit2_ref[at].astype(F32)
            outer = norm_back(top_grad, unit, scale2_ref[at], gain)
            branch = outer.astype(BF)
            outer_ref[at] = outer
            branch_ref[at] = branch
            gain_sum += jnp.sum(top_grad * unit, axis=0, keepdims=True)
            shift_sum += jnp.sum(top_grad, axis=0, keepdims=True)
            bias_sum += jnp.sum(branch.astype(F32), axis=0, keepdims=True)
        sums_ref[0:1] = gain_sum
        sums_ref[1:2] = shift_sum
        sums_ref[2:3] = bias_sum

    @pl.when(step > 0)
    def _():
        few, both, _ = joint_grad_ref.shape
        deep = width // few
        value = nn(act_ref[...], branch_ref[...])
        for at in range(few):
            joint_grad_ref[at, 0:deep] = value[at * deep : (at + 1) * deep].astype(BF)
            joint_grad_ref[at, deep:both] = pool_grad_ref[(step - 1) * few + at]


def leave(
    exit_layer, output, unit2, scale2, output_grad, pool, vec, class_bias, logit_grad, act,
    pool_spec, shards, length, classes,
):
    rows, width = output.shape
    count = rows // length
    hidden = act.shape[0]
    steps = hidden // width
    few = shards // steps
    both = (hidden + width) // shards
    whole = full((rows, width))
    return pl.pallas_call(
        functools.partial(leave_kernel, length, classes),
        grid=(steps + 1,),
        in_specs=[
            pl.BlockSpec(memory_space=pltpu.SMEM),
            whole,
            whole,
            full((rows, 1)),
            whole,
            pool_spec,
            full(vec.shape),
            full(class_bias.shape),
            full(logit_grad.shape),
            pl.BlockSpec((width, rows), lambda i: (jnp.maximum(i - 1, 0), 0)),
        ],
        out_specs=[
            whole,
            whole,
            pl.BlockSpec((few, both, width), lambda i: (jnp.maximum(i - 1, 0), 0, 0)),
            full((4, width)),
            full((8, width)),
            full((count, 8)),
            full((2, 8)),
        ],
        out_shape=[
            jax.ShapeDtypeStruct((rows, width), F32),
            jax.ShapeDtypeStruct((rows, width), BF),
            jax.ShapeDtypeStruct((shards, both, width), BF),
            jax.ShapeDtypeStruct((4, width), F32),
            jax.ShapeDtypeStruct((8, width), F32),
            jax.ShapeDtypeStruct((count, 8), F32),
            jax.ShapeDtypeStruct((2, 8), F32),
        ],
        scratch_shapes=[
            pltpu.VMEM((count, width), F32),
            pltpu.VMEM((shards, width // shards, width), BF),
        ],
        compiler_params=params(),
        cost_estimate=cost(8 * rows * width * width, 30 * rows * width),
        name="leave",
    )(
        exit_layer, output, unit2, scale2, output_grad, pool, vec, class_bias, logit_grad, act
    )


def split_cores(value, place_ref, keep_ref, send_ref):
    chips, part, _ = keep_ref.shape
    first = place_ref[2] == 0
    for chip in range(chips):
        even = value[2 * chip * part : (2 * chip + 1) * part]
        odd = value[(2 * chip + 1) * part : (2 * chip + 2) * part]
        keep_ref[chip] = jnp.where(first, even, odd).astype(BF)
        send_ref[chip] = jnp.where(first, odd, even).astype(BF)


def feed_back_kernel(
    place_ref,
    branch_ref,
    slope_ref,
    turned_ref,
    down_ref,
    up_ref,
    outer_ref,
    unit1_ref,
    scale1_ref,
    out_w_ref,
    vec_ref,
    ctx_ref,
    keep_ref,
    send_ref,
    up_sum_ref,
    inner_ref,
    attended_ref,
    ctx_grad_ref,
    sums_ref,
    acc_ref,
    hid_ref,
):
    step = pl.program_id(0)
    rows, width = branch_ref.shape
    sub = 512

    @pl.when(step == 0)
    def _():
        acc_ref[...] = outer_ref[...]

    last = pl.num_programs(0) - 1

    @pl.when(step < last)
    def _():
        total = jnp.zeros((1, width), F32)
        down = down_ref[...].reshape(up_ref.shape[1:])
        ahead = nt(branch_ref[0:sub], down)
        for m in range(rows // sub):
            at = slice(m * sub, (m + 1) * sub)
            hid = (ahead * slope_ref[at].astype(F32)).astype(BF)
            if (m + 1) * sub < rows:
                ahead = nt(branch_ref[(m + 1) * sub : (m + 2) * sub], down)
            hid_ref[at] = hid
            total += jnp.sum(hid.astype(F32), axis=0, keepdims=True)
            acc_ref[at] += nt(hid, up_ref[0])
        up_sum_ref[...] = total
        split_cores(nn(turned_ref[...], hid_ref[...]), place_ref, keep_ref, send_ref)

    @pl.when(step == last)
    def _():
        gain = vec_ref[ATTN_GAIN : ATTN_GAIN + 1]
        gain_sum = jnp.zeros((1, width), F32)
        shift_sum = jnp.zeros((1, width), F32)
        bias_sum = jnp.zeros((1, width), F32)
        for m in range(rows // sub):
            at = slice(m * sub, (m + 1) * sub)
            grad = acc_ref[at]
            unit = unit1_ref[at].astype(F32)
            inner = norm_back(grad, unit, scale1_ref[at], gain)
            attended = inner.astype(BF)
            inner_ref[at] = inner
            attended_ref[at] = attended
            ctx_grad_ref[at] = nt(attended, out_w_ref[0]).astype(BF)
            gain_sum += jnp.sum(grad * unit, axis=0, keepdims=True)
            shift_sum += jnp.sum(grad, axis=0, keepdims=True)
            bias_sum += jnp.sum(attended.astype(F32), axis=0, keepdims=True)
        sums_ref[0:1] = gain_sum
        sums_ref[1:2] = shift_sum
        sums_ref[2:3] = bias_sum
        split_cores(tn(ctx_ref[...], attended_ref[...]), place_ref, keep_ref, send_ref)


def feed_back(place, chips, branch, slope, low, down, down_block, up, outer, unit1, scale1, out_w, vec, ctx):
    rows, width = branch.shape
    hidden = slope.shape[1]
    steps = hidden // width
    whole = full((rows, width))
    end = steps - 1
    part = width // (2 * chips)
    return pl.pallas_call(
        feed_back_kernel,
        grid=(steps + 1,),
        in_specs=[
            pl.BlockSpec(memory_space=pltpu.SMEM),
            whole,
            pl.BlockSpec((rows, width), lambda i: (0, jnp.minimum(i, end))),
            full((width, rows)),
            pl.BlockSpec(down_block, lambda i: (jnp.minimum(i, end), 0, 0)),
            pl.BlockSpec((1, width, width), lambda i: (jnp.minimum(i, end), 0, 0)),
            whole,
            whole,
            full((rows, 1)),
            pl.BlockSpec((1, width, width), lambda i: (3, 0, 0)),
            full(vec.shape),
            whole,
        ],
        out_specs=[
            pl.BlockSpec((chips, part, width), lambda i: (0, 0, i)),
            pl.BlockSpec((chips, part, width), lambda i: (0, 0, i)),
            pl.BlockSpec((1, width), lambda i: (0, jnp.minimum(i, end))),
            whole,
            whole,
            whole,
            full((3, width)),
        ],
        out_shape=[
            jax.ShapeDtypeStruct((chips, part, hidden + width), BF),
            jax.ShapeDtypeStruct((chips, part, hidden + width), BF),
            jax.ShapeDtypeStruct((1, hidden), F32),
            jax.ShapeDtypeStruct((rows, width), F32),
            jax.ShapeDtypeStruct((rows, width), BF),
            jax.ShapeDtypeStruct((rows, width), BF),
            jax.ShapeDtypeStruct((3, width), F32),
        ],
        scratch_shapes=[pltpu.VMEM((rows, width), F32), pltpu.VMEM((rows, width), BF)],
        compiler_params=params(),
        cost_estimate=cost(28 * rows * width * width, 40 * rows * width),
        name="feed_back",
    )(place, branch, slope, low, down, up, outer, unit1, scale1, out_w, vec, ctx)


def attend_back_kernel(length, joined_ref, probs_ref, ctx_grad_ref, grad_ref, sum_ref):
    rows, width = ctx_grad_ref.shape
    pairs = width // PAIR

    def one(seq, carry):
        at = pl.ds(pl.multiple_of(seq * length, length), length)

        def columns(part, pair):
            return slice(part * width + pair * PAIR, part * width + (pair + 1) * PAIR)

        prob_grads = []
        for pair in range(pairs):
            vals = split_heads(joined_ref[at, columns(2, pair)])
            prob_grads.append(nt(vals, ctx_grad_ref[at, columns(0, pair)]))
        score_grads = []
        for pair in range(pairs):
            probs = probs_ref[seq, pair]
            halves = []
            for head in range(2):
                cut = slice(head * length, (head + 1) * length)
                held = probs[cut].astype(F32)
                part = prob_grads[pair][cut]
                base = jnp.sum(part * held, axis=0, keepdims=True)
                halves.append((held * (part - base)).astype(BF))
            score_grads.append(halves)
        for pair in range(pairs):
            probs = probs_ref[seq, pair]
            beside = jnp.concatenate([probs[:length], probs[length:]], axis=1)
            ctx_grads = split_heads(ctx_grad_ref[at, columns(0, pair)])
            grad_ref[at, columns(2, pair)] = nn(beside, ctx_grads).astype(BF)
        for pair in range(pairs):
            queries = split_heads(joined_ref[at, columns(0, pair)] * jnp.asarray(0.125, BF))
            beside = jnp.concatenate(score_grads[pair], axis=1)
            grad_ref[at, columns(1, pair)] = nn(beside, queries).astype(BF)
        for pair in range(pairs):
            keys = split_heads(joined_ref[at, columns(1, pair)])
            stacked = jnp.concatenate(score_grads[pair], axis=0)
            grad_ref[at, columns(0, pair)] = (tn(stacked, keys) * 0.125).astype(BF)
        return carry

    lax.fori_loop(0, rows // length, one, 0)
    total = jnp.zeros(sum_ref.shape, F32)
    for m in range(rows // length):
        total += jnp.sum(
            grad_ref[m * length : (m + 1) * length].astype(F32), axis=0, keepdims=True
        )

    @pl.when(pl.program_id(0) == 0)
    def _():
        sum_ref[...] = total

    @pl.when(pl.program_id(0) > 0)
    def _():
        sum_ref[...] += total


def attend_back(joined, probs, ctx_grad, length):
    rows, width = ctx_grad.shape
    count = rows // length
    steps = 2
    block = rows // steps
    pairs = width // PAIR
    return pl.pallas_call(
        functools.partial(attend_back_kernel, length),
        grid=(steps,),
        in_specs=[
            pl.BlockSpec((block, 3 * width), lambda i: (i, 0)),
            pl.BlockSpec((count // steps, pairs, 2 * length, length), lambda i: (i, 0, 0, 0)),
            pl.BlockSpec((block, width), lambda i: (i, 0)),
        ],
        out_specs=[
            pl.BlockSpec((block, 3 * width), lambda i: (i, 0)),
            full((1, 3 * width)),
        ],
        out_shape=[
            jax.ShapeDtypeStruct((rows, 3 * width), BF),
            jax.ShapeDtypeStruct((1, 3 * width), F32),
        ],
        compiler_params=params(),
        cost_estimate=cost(8 * rows * width * width, 20 * rows * width),
        name="attend_back",
    )(joined, probs, ctx_grad)


def weight_grads_kernel(tok_ref, joined_ref, small_ref, out_ref, turned_ref):
    step = pl.program_id(0)
    last = pl.num_programs(0) - 1
    shards, part, width = out_ref.shape

    @pl.when(step == 0)
    def _():
        turned_ref[...] = tok_ref[...].T

    value = nn(turned_ref[...], joined_ref[...])
    cols = pl.ds(pl.multiple_of(step * joined_ref.shape[1], joined_ref.shape[1]), joined_ref.shape[1])
    out_ref[:, :, cols] = value.reshape(shards, part, joined_ref.shape[1]).astype(BF)
    tail = 3 * joined_ref.shape[1]
    if width > tail:

        @pl.when(step == last)
        def _():
            lines = small_ref.shape[1]
            out_ref[:, lines:part, tail:width] = jnp.zeros(
                (shards, part - lines, width - tail), BF
            )
            out_ref[:, 0:lines, tail:width] = small_ref[...].astype(BF)


def weight_grads(tokens, joined_grad, small, shards, extra):
    rows, width = tokens.shape
    shape = (shards, width // shards, 3 * width + extra)
    return pl.pallas_call(
        weight_grads_kernel,
        grid=(3,),
        in_specs=[
            full((rows, width)),
            pl.BlockSpec((rows, width), lambda i: (0, i)),
            full(small.shape),
        ],
        out_specs=full(shape),
        out_shape=jax.ShapeDtypeStruct(shape, BF),
        scratch_shapes=[pltpu.VMEM((width, rows), BF)],
        compiler_params=params(),
        cost_estimate=cost(6 * rows * width * width, 20 * rows * width),
        name="weight_grads",
    )(tokens, joined_grad, small)


def input_kernel(inner_ref, joined_ref, w_ref, out_ref):
    width = inner_ref.shape[1]
    total = inner_ref[...]
    for part in range(3):
        total += nt(joined_ref[:, part * width : (part + 1) * width], w_ref[part])
    out_ref[...] = total.astype(BF)


def input_back(inner, joined_grad, qkv):
    rows, width = inner.shape
    steps = 4
    block = rows // steps
    return pl.pallas_call(
        input_kernel,
        grid=(steps,),
        in_specs=[
            pl.BlockSpec((block, width), lambda i: (i, 0)),
            pl.BlockSpec((block, 3 * width), lambda i: (i, 0)),
            full((3, width, width)),
        ],
        out_specs=pl.BlockSpec((block, width), lambda i: (i, 0)),
        out_shape=jax.ShapeDtypeStruct((rows, width), BF),
        compiler_params=params(),
        cost_estimate=cost(6 * rows * width * width, 12 * rows * width),
        name="input_back",
    )(inner, joined_grad, qkv)


def lay_kernel(plan, chips, reps, part, counts, place_ref, *refs):
    at = 0
    groups = []
    for number in counts:
        groups.append(refs[at : at + number])
        at += number
    sems = refs[-1]
    rep, chip, core = place_ref[0], place_ref[1], place_ref[2]
    copies = []

    def start(source, target):
        copies.append(pltpu.make_async_copy(source, target, sems.at[len(copies)]))
        copies[-1].start()

    finish = plan(start, groups, refs[at:-1], rep, chip, core, chips, reps, part)
    for copy in copies:
        copy.wait()
    if finish is not None:
        finish()


def blocks_plan(
    put, own, twin, along, across, swapped, depth, first, rep, chip, core, chips, reps, part
):
    for block in range(reps):
        put(own(block), block, chip, core)
        put(twin(block), block, chip, 1 - core)
    for step in range(1, chips):
        source = lax.rem(chip + chips - step, chips)
        rows = pl.ds((step - 1) * depth + first, part)
        for other, block in along.items():
            put(block(step, source, 0), rep ^ other, source, core)
            put(block(step, source, 1), rep ^ other, source, 1 - core)
        for other in across:
            put(across[other].at[rows], rep ^ other, source, core)
            put(swapped[other].at[rows], rep ^ other, source, 1 - core)


def wide_put(start, out_ref, part):
    def put(source, block, at_chip, at_core):
        row = pl.multiple_of((at_chip * 2 + at_core) * part, part)
        start(source, out_ref.at[block, pl.ds(row, part)])

    return put


def wide_block(ref, width, part):
    return lambda block: ref.at[pl.ds(0, part), pl.ds(block * width, width)]


def first_plan(start, groups, outs, rep, chip, core, chips, reps, part):
    (own, twin), along, across, swapped, (extra,) = groups
    out_ref, vec_ref, more_ref = outs
    width = out_ref.shape[2]

    def near(step, source, side):
        if side == 0:
            return along[step - 1].at[pl.ds(0, part)]
        return swapped[0].at[pl.ds((step - 1) * part, part)]

    blocks_plan(
        wide_put(start, out_ref, part),
        wide_block(own, width, part),
        wide_block(twin, width, part),
        {0: near},
        {at + 1: ref for at, ref in enumerate(across)},
        {at + 1: ref for at, ref in enumerate(swapped[1:])},
        part,
        0,
        rep,
        chip,
        core,
        chips,
        reps,
        part,
    )
    tail = pl.ds(part, 16)
    cols = pl.ds(0, width)
    start(own.at[tail, cols], more_ref.at[chip * 2 + core])
    start(twin.at[tail, cols], more_ref.at[chip * 2 + 1 - core])
    for step in range(1, chips):
        source = lax.rem(chip + chips - step, chips)
        start(along[step - 1].at[tail], more_ref.at[source * 2 + core])
        start(extra.at[pl.ds((step - 1) * 16, 16)], more_ref.at[source * 2 + 1 - core])

    def finish():
        lane = lax.broadcasted_iota(jnp.int32, (LANES, width), 0)
        place = lax.broadcasted_iota(jnp.int32, (LANES, width), 1)
        total = jnp.zeros((16, width), F32)
        for shard in range(2 * chips):
            there = (place - shard * part == lane) & (lane < part)
            total += nn(more_ref[shard, :, 0:LANES], there.astype(F32).astype(BF))
        vec_ref[...] = total

    return finish


def second_plan(start, groups, outs, rep, chip, core, chips, reps, part):
    (up, up_twin, down, down_twin), (close, far), across, swapped = groups
    up_ref, down_ref = outs
    width = up_ref.shape[2]
    where = (rep, chip, core, chips, reps, part)

    def chained(chain, first):
        def block(step, source, side):
            shard = source * 2 + (core if side == 0 else 1 - core)
            return chain.at[shard, pl.ds(first, part)]

        return block

    across = dict(zip(NEAR, across))
    swapped = dict(zip(NEAR, swapped))
    blocks_plan(
        wide_put(start, up_ref, part),
        wide_block(up, width, part),
        wide_block(up_twin, width, part),
        {0: chained(close, 0), FAR: chained(far, 0)},
        across,
        swapped,
        2 * part,
        0,
        *where,
    )

    def put(source, block, at_chip, at_core):
        row = pl.multiple_of(block * part, part)
        start(source, down_ref.at[at_chip * 2 + at_core, pl.ds(row, part)])

    def tall(ref):
        return lambda block: ref.at[pl.ds(block * part, part)]

    blocks_plan(
        put,
        tall(down),
        tall(down_twin),
        {0: chained(close, part), FAR: chained(far, part)},
        across,
        swapped,
        2 * part,
        part,
        *where,
    )


def lay(plan, place, groups, shapes, scratch, copies, part, chips, reps):
    anywhere = pl.BlockSpec(memory_space=pl.ANY)
    inputs = [ref for group in groups for ref in group]
    return pl.pallas_call(
        functools.partial(
            lay_kernel, plan, chips, reps, part, [len(group) for group in groups]
        ),
        in_specs=[pl.BlockSpec(memory_space=pltpu.SMEM)] + [anywhere] * len(inputs),
        out_specs=[pl.BlockSpec(memory_space=pltpu.VMEM)] * len(shapes),
        out_shape=[jax.ShapeDtypeStruct(shape, kind) for shape, kind in shapes],
        scratch_shapes=[pltpu.VMEM(shape, BF) for shape in scratch]
        + [pltpu.SemaphoreType.DMA((copies,))],
        compiler_params=pltpu.CompilerParams(vmem_limit_bytes=VMEM_BYTES),
        cost_estimate=cost(0, 4 * sum(math.prod(shape) for shape, kind in shapes)),
        name="lay",
    )(place, *inputs)


def pack_vectors(rows, up_bias, class_weight):
    part = rows[0].shape[0]
    lines = [row[None] for row in rows[:8]] + [class_weight.T] + [row[None] for row in rows[8:]]
    pieces = up_bias.shape[0] // part
    lines += [up_bias[None, at * part : (at + 1) * part] for at in range(pieces)]
    return jnp.concatenate(lines, axis=0)


def move(values, reps, chips, target):
    pairs = []
    for rep in range(reps):
        for chip in range(chips):
            for core in range(2):
                to_rep, to_chip, to_core = target(rep, chip, core)
                pairs.append(
                    (
                        (rep * chips + chip) * 2 + core,
                        (to_rep * chips + to_chip) * 2 + to_core,
                    )
                )
    return lax.ppermute(values, ("rep", "fsdp"), pairs)


def along_chips(step, chips):
    return lambda rep, chip, core: (rep, (chip + step) % chips, core)


def across_reps(other):
    return lambda rep, chip, core: (rep ^ other, chip, core)


def to_twin(rep, chip, core):
    return rep, chip, 1 - core


def after(values, *gates):
    return lax.optimization_barrier((values, *gates))[0]


def along_z(mine, reps, chips):
    return [move(mine, reps, chips, along_chips(step, chips)) for step in range(1, chips)]


def over_reps(stacked, reps, chips, others):
    return [move(stacked, reps, chips, across_reps(other)) for other in others]


def pick(parts, at):
    return lax.dynamic_index_in_dim(parts, at, axis=0, keepdims=False)


def in_order(rep, reps, own, others, axis):
    blocks = jnp.stack([own] + others)
    return jnp.concatenate([pick(blocks, rep ^ at) for at in range(reps)], axis=axis)


class Reduction:
    def __init__(self, place, keep, send, reps, chips, by_chain=False):
        self.rep, self.chip = place[0], place[1]
        self.reps, self.chips = reps, chips
        self.shape = (chips, reps, keep.shape[1] // reps, keep.shape[2])
        self.keep = keep.reshape(self.shape)
        self.others_of = range(1, reps)
        self.far = None
        if by_chain:
            self.others_of = NEAR
            first = place[2] == 0
            kept = lax.dynamic_index_in_dim(self.keep, self.rep ^ FAR, axis=1, keepdims=False)
            sent = lax.dynamic_index_in_dim(
                send.reshape(self.shape), self.rep ^ FAR, axis=1, keepdims=False
            )
            pair = jnp.stack(
                [jnp.where(first, kept, sent), jnp.where(first, sent, kept)], axis=1
            )
            self.far = lax.psum_scatter(
                pair.reshape(-1, keep.shape[2]), "fsdp", scatter_dimension=0, tiled=True
            )
        self.got = move(send, reps, chips, to_twin)

    def at_rep(self, at):
        kept = lax.dynamic_index_in_dim(self.keep, at, axis=1, keepdims=False)
        came = lax.dynamic_index_in_dim(
            self.got.reshape(self.shape), at, axis=1, keepdims=False
        )
        return kept.astype(F32) + came.astype(F32)

    def over_reps(self, *gates):
        if gates:
            self.got = after(self.got, *gates)
        self.arrived = [
            move(
                self.at_rep(self.rep ^ other).astype(BF),
                self.reps,
                self.chips,
                across_reps(other),
            )
            for other in self.others_of
        ]

    def over_chips(self, *gates):
        if gates:
            self.arrived = [after(block, *gates) for block in self.arrived]
        mine = self.at_rep(self.rep)

        def both_at(at):
            total = pick(mine, at)
            for block in self.arrived:
                total = total + pick(block, at).astype(F32)
            return total

        self.total = both_at(self.chip)
        if self.far is not None:
            came = move(self.far, self.reps, self.chips, across_reps(FAR))
            self.total = self.total + came.astype(F32)
        self.passed = [
            move(
                both_at(lax.rem(self.chip + step, self.chips)).astype(BF),
                self.reps,
                self.chips,
                along_chips(step, self.chips),
            )
            for step in range(1, self.chips)
        ]

    def chip_sum(self):
        total = self.total
        for block in self.passed:
            total = total + block.astype(F32)
        return total.astype(BF)


def share_reps(place, total, reps, chips):
    others = [move(total, reps, chips, across_reps(other)) for other in range(1, reps)]
    return in_order(place[0], reps, total, others, 0).astype(F32), others


def exchange_reps(place, rows, reps, chips):
    rep = place[0]
    parts = rows.reshape(reps, -1, rows.shape[1])
    total = pick(parts, rep).astype(F32)
    arrived = [
        move(pick(parts, rep ^ other), reps, chips, across_reps(other))
        for other in range(1, reps)
    ]
    for block in arrived:
        total = total + block.astype(F32)
    return total.astype(BF), arrived


def per_device(
    tokens,
    exit_layer,
    qkv_weight,
    query_bias,
    value_bias,
    out_weight,
    out_bias,
    attn_gain,
    attn_shift,
    up_weight,
    up_bias,
    down_weight,
    down_bias,
    block_gain,
    block_shift,
    pool_weight,
    pool_bias,
    class_weight,
    class_bias,
    output_grad,
    logit_grad,
):
    reps = lax.axis_size("rep")
    shards = lax.axis_size("fsdp")
    mine = lax.axis_index("fsdp")
    rows, width = tokens.shape
    count = exit_layer.shape[0]
    length = rows // count
    classes = class_weight.shape[1]
    part = out_weight.shape[0]
    hidden = up_weight.shape[1]

    def gather(shard):
        return lax.all_gather(shard, "fsdp", axis=0, tiled=True)

    packed = pack_vectors(
        [
            query_bias,
            value_bias,
            out_bias,
            attn_gain,
            attn_shift,
            down_bias,
            block_gain,
            block_shift,
            pool_bias,
        ],
        up_bias,
        class_weight,
    )
    joint_own = jnp.concatenate([qkv_weight, out_weight], axis=1)
    deep = down_weight.shape[0]
    chips = shards // 2
    place = jnp.stack([lax.axis_index("rep"), mine // 2, mine % 2]).astype(jnp.int32)
    direct = (
        part % 16 == 0
        and reps & (reps - 1) == 0
        and reps * width == hidden
        and reps == 4
        and packed.shape[0] <= 16
    )
    if direct:
        lines = packed.shape[0]
        held = jnp.pad(packed, ((0, 16 - lines), (0, width - part)))
        own = jnp.concatenate([joint_own, jnp.tile(held, (1, reps))], axis=0)
        rep = place[0]

        def block_of(weights, at):
            return lax.dynamic_slice_in_dim(weights, at * width, width, axis=1)

        def second_of(at):
            return [
                block_of(up_weight, at),
                lax.dynamic_slice_in_dim(down_weight, at * part, part, axis=0),
            ]

        along = along_z(block_of(own, rep), reps, chips)
        chain = gather(after(jnp.concatenate(second_of(rep), axis=0), *along))
        chain = chain.reshape(chips, 2, 2 * part, width)
        twin = move(own, reps, chips, to_twin)
        stacked = jnp.concatenate([rows_[:part] for rows_ in along], axis=0)
        across = over_reps(stacked, reps, chips, range(1, reps))
        far_chain = gather(after(jnp.concatenate(second_of(rep ^ FAR), axis=0), *across))
        swapped = [move(rows_, reps, chips, to_twin) for rows_ in [stacked] + across]
        extra = move(
            jnp.concatenate([rows_[part:] for rows_ in along], axis=0), reps, chips, to_twin
        )
        up_twin = move(up_weight, reps, chips, to_twin)
        down_twin = move(down_weight, reps, chips, to_twin)
        joint, vec = lay(
            first_plan,
            place,
            [
                [own, twin],
                along,
                across,
                swapped,
                [extra],
            ],
            [((reps, width, width), BF), ((16, width), F32)],
            [(shards, 16, width)],
            2 * chips * (reps + 1),
            part,
            chips,
            reps,
        )
        mine_chain = lax.dynamic_index_in_dim(
            after(chain, joint), place[2], axis=1, keepdims=False
        )
        second_stacked = jnp.concatenate(
            [
                pick(mine_chain, lax.rem(place[1] + chips - step, chips))
                for step in range(1, chips)
            ],
            axis=0,
        )
        second_across = over_reps(after(second_stacked, *across), reps, chips, NEAR)
        up_row = (
            vec[VECTOR_ROWS:lines].reshape(-1, shards, part).transpose(1, 0, 2).reshape(1, hidden)
        )
        down_block = (width // deep, deep, width)
    else:
        small = gather(packed[None])
        vec = small[:, :VECTOR_ROWS].transpose(1, 0, 2).reshape(VECTOR_ROWS, width).astype(F32)
        vec = jnp.pad(vec, ((0, 16 - VECTOR_ROWS), (0, 0)))
        up_row = small[:, VECTOR_ROWS:].transpose(0, 1, 2).reshape(1, hidden).astype(F32)
        pool = gather(pool_weight)
        joint = jnp.stack(jnp.split(gather(joint_own), 4, axis=1))
        up = jnp.stack(jnp.split(gather(up_weight), hidden // width, axis=1))
        down = gather(down_weight).reshape(-1, width, width)
        down_block = (1, width, width)
    joined, probs, ctx = attend(tokens, joint, vec, length)
    if direct:
        pool = gather(after(pool_weight, ctx))
        far_chain = after(far_chain, ctx)
        second_swapped = [
            move(after(rows_, ctx), reps, chips, to_twin) for rows_ in second_across
        ]
        groups = [
            [up_weight, up_twin, down_weight, down_twin],
            [
                chain.reshape(shards, 2 * part, width),
                far_chain.reshape(shards, 2 * part, width),
            ],
            second_across,
            second_swapped,
        ]
        weights = [ref for group in groups for ref in group]
        load = functools.partial(load_second, [len(group) for group in groups], chips, reps, part)
        shapes = [(reps, width, width), (shards, deep, width)]
    else:
        weights, load, shapes = [up, down], None, None
    turned, act, slope, unit1, scale1, unit2, scale2, output, *laid = feed(
        place, exit_layer, tokens, ctx, joint, vec, up_row, weights, load, shapes, length
    )
    if direct:
        up, down = laid
    class_bias_row = jnp.pad(class_bias.astype(F32), (0, 8 - classes))[None]
    logit_grad_rows = jnp.pad(logit_grad, ((0, 0), (0, 8 - classes)))
    outer, branch, low_grad, exit_sums, class_grad, logits, stats = leave(
        exit_layer,
        output,
        unit2,
        scale2,
        output_grad,
        pool,
        vec,
        class_bias_row,
        logit_grad_rows,
        act,
        full((width, width)),
        shards,
        length,
        classes,
    )
    up_keep, up_send, up_sum, inner, attended, ctx_grad, feed_sums = feed_back(
        place, chips, branch, slope, turned, down, down_block, up, outer, unit1, scale1, joint, vec, ctx
    )
    if direct:
        up_red = Reduction(place, up_keep, up_send, reps, chips)
        ctx_grad = after(ctx_grad, up_red.got)
    joined_grad, joined_sum = attend_back(joined, probs, ctx_grad, length)
    joined_seen = joined_grad
    if direct:
        up_red.over_reps()
        joined_seen = after(joined_grad, up_red.arrived[0])
    sums = jnp.concatenate(
        [
            joined_sum.reshape(3, width)[::2],
            feed_sums,
            exit_sums,
            class_grad[:classes],
        ],
        axis=0,
    )
    lines = sums.shape[0]
    own_sums = sums.reshape(lines, shards, part).transpose(1, 0, 2).reshape(shards, lines * part)
    own_sums = jnp.concatenate([own_sums, up_sum.reshape(shards, deep)], axis=1)
    used = own_sums.shape[1]
    seqs_total = count * reps * shards
    figures = jnp.concatenate([stats[0, :1], stats[1, :classes]])
    slots = reps * shards * figures.shape[0] * 3
    direct = direct and used + slots <= part * LANES
    small_lines = 16
    if direct:
        high = figures.astype(BF).astype(F32)
        middle = (figures - high).astype(BF).astype(F32)
        lowest = figures - high - middle
        split = jnp.concatenate([high, middle, lowest])
        slot = lax.axis_index("rep") * shards + mine
        lone = jnp.where(
            jnp.arange(reps * shards)[:, None] == slot, split[None], 0.0
        ).reshape(1, slots)
        row = jnp.concatenate([own_sums, jnp.broadcast_to(lone, (shards, slots))], axis=1)
        small_lines = -(-row.shape[1] // (LANES * 16)) * 16
        row = jnp.pad(row, ((0, 0), (0, small_lines * LANES - row.shape[1])))
        row = row.reshape(shards, small_lines, LANES)
    else:
        row = jnp.zeros((shards, small_lines, LANES), F32)
    joint_grad = weight_grads(tokens, joined_seen, row, shards, LANES if direct else 0)
    input_grad = input_back(inner, joined_grad, joint)

    def scatter(grad):
        return lax.psum_scatter(grad, "fsdp", scatter_dimension=0, tiled=True)

    low_part = scatter(low_grad.reshape(-1, width))
    if direct:
        joint_grad = after(joint_grad, low_part, up_red.arrived[1])
    joint_part = scatter(joint_grad.reshape(width, -1))
    if direct:
        low_total, low_arrived = exchange_reps(place, after(low_part, joint_grad), reps, chips)
        up_red.over_chips(*low_arrived)
        wide = (deep + part) * width // part
        up_total = up_red.chip_sum()
        columns = up_total.shape[1]
        pair, pair_others = share_reps(
            place,
            jnp.concatenate([up_total, low_total.reshape(-1, wide)], axis=1),
            reps,
            chips,
        )
        up_sum = pair[:, :columns]
        low_sum = pair[:, columns:].reshape(deep + part, width)
        joint_total, _ = exchange_reps(
            place, after(joint_part, *pair_others), reps, chips
        )
        joint_sum, _ = share_reps(place, joint_total, reps, chips)
        small_sum = joint_sum[:small_lines, 3 * width :].reshape(-1)
        total = small_sum[used : used + slots].reshape(-1, figures.shape[0]).sum(axis=0)
    else:
        first = mine % 2 == 0

        def whole_of(kept, sent):
            pair = jnp.stack([jnp.where(first, kept, sent), jnp.where(first, sent, kept)], axis=1)
            return pair.reshape(-1, kept.shape[2])

        joint_sum, low_sum, up_sum = lax.psum(
            (joint_part, low_part, scatter(whole_of(up_keep, up_send))), "rep"
        )
        joint_sum, low_sum, up_sum = (
            joint_sum.astype(F32),
            low_sum.astype(F32),
            up_sum.astype(F32),
        )
        own_sums, total = lax.psum((own_sums, figures), ("rep", "fsdp"))
        small_sum = pick(own_sums, mine)
    own = small_sum[: lines * part].reshape(lines, part)
    return (
        output,
        logits[:, :classes],
        total[0] / seqs_total,
        input_grad,
        joint_sum[:, : 3 * width],
        own[0],
        own[1],
        up_sum[:, hidden:],
        own[4],
        own[2],
        own[3],
        up_sum[:, :hidden],
        small_sum[lines * part : used],
        low_sum[:deep],
        own[7],
        own[5],
        own[6],
        low_sum[deep:],
        own[8],
        own[9 : 9 + classes].T,
        total[1:],
    )


def solution(mesh):
    return jax.shard_map(
        per_device,
        mesh=mesh,
        in_specs=(
            P(("rep", "fsdp"), None),
            P(("rep", "fsdp")),
            P("fsdp", None),
            P("fsdp"),
            P("fsdp"),
            P("fsdp", None),
            P("fsdp"),
            P("fsdp"),
            P("fsdp"),
            P("fsdp", None),
            P("fsdp"),
            P("fsdp", None),
            P("fsdp"),
            P("fsdp"),
            P("fsdp"),
            P("fsdp", None),
            P("fsdp"),
            P("fsdp", None),
            P(),
            P(("rep", "fsdp"), None),
            P(("rep", "fsdp"), None),
        ),
        out_specs=(
            P(("rep", "fsdp"), None),
            P(("rep", "fsdp"), None),
            P(),
            P(("rep", "fsdp"), None),
            P("fsdp", None),
            P("fsdp"),
            P("fsdp"),
            P("fsdp", None),
            P("fsdp"),
            P("fsdp"),
            P("fsdp"),
            P("fsdp", None),
            P("fsdp"),
            P("fsdp", None),
            P("fsdp"),
            P("fsdp"),
            P("fsdp"),
            P("fsdp", None),
            P("fsdp"),
            P("fsdp", None),
            P(),
        ),
        check_vma=False,
    )
```

```python
import functools
import math

import jax
import jax.numpy as jnp
from jax import lax
from jax.experimental import pallas as pl
from jax.experimental.pallas import tpu as pltpu
from jax.sharding import PartitionSpec as P

HD = 64
LAYER = 6
PAIR = 2 * HD
NEAR = (1, 2)
FAR = 3
LANES = 128
VMEM_BYTES = 58 * 2**20
BF = jnp.bfloat16
F32 = jnp.float32

QUERY_BIAS, VALUE_BIAS, OUT_BIAS, ATTN_GAIN, ATTN_SHIFT = 0, 1, 2, 3, 4
DOWN_BIAS, BLOCK_GAIN, BLOCK_SHIFT, CLASS_ROWS, POOL_BIAS = 5, 6, 7, 8, 11
VECTOR_ROWS = 12


def nn(left, right):
    return jnp.dot(left, right, preferred_element_type=F32)


def tn(left, right):
    return lax.dot_general(left, right, (((0,), (0,)), ((), ())), preferred_element_type=F32)


def nt(left, right):
    return lax.dot_general(left, right, (((1,), (1,)), ((), ())), preferred_element_type=F32)


def full(shape):
    return pl.BlockSpec(shape, lambda *at: (0,) * len(shape))


def params():
    return pltpu.CompilerParams(
        dimension_semantics=("arbitrary",), vmem_limit_bytes=VMEM_BYTES
    )


def cost(flops, moved, trans=0):
    return pl.CostEstimate(flops=flops, bytes_accessed=moved, transcendentals=trans)


def split_heads(pair):
    lane = lax.broadcasted_iota(jnp.int32, pair.shape, 1)
    zero = jnp.zeros_like(pair)
    return jnp.concatenate(
        [jnp.where(lane < HD, pair, zero), jnp.where(lane < HD, zero, pair)], axis=0
    )


def norm_stats(values):
    center = values - jnp.mean(values, axis=-1, keepdims=True)
    spread = jnp.mean(center * center, axis=-1, keepdims=True)
    scale = lax.rsqrt(spread + 1e-06)
    return center * scale, scale


def norm_back(grad, unit, scale, gain):
    inner = grad * gain
    first = jnp.mean(inner, axis=-1, keepdims=True)
    second = jnp.mean(inner * unit, axis=-1, keepdims=True)
    return scale * (inner - first - unit * second)


def gelu_parts(values):
    base = 1.0 + 0.23164189 * jnp.abs(values)
    t = pl.reciprocal(base, approx=True)
    t = t * (2.0 - base * t)
    bell = jnp.exp2((values * values) * -0.7213475204444817)
    poly = t * (
        0.127414796
        + t * (-0.142248368 + t * (0.7107068705 + t * (-0.7265760135 + t * 0.5307027145)))
    )
    tail = poly * bell
    below = jnp.where(values >= 0.0, 1.0 - tail, tail)
    return values * below, below + values * (bell * 0.3989422804014327)


def attend_kernel(length, tok_ref, w_ref, vec_ref, joined_ref, probs_ref, ctx_ref):
    rows, width = ctx_ref.shape
    pairs = width // PAIR
    for part in range(3):
        cols = slice(part * width, (part + 1) * width)
        value = nn(tok_ref[...], w_ref[part])
        if part == 0:
            value += vec_ref[QUERY_BIAS : QUERY_BIAS + 1]
        elif part == 2:
            value += vec_ref[VALUE_BIAS : VALUE_BIAS + 1]
        joined_ref[:, cols] = value.astype(BF)

    def one(seq, carry):
        at = pl.ds(pl.multiple_of(seq * length, length), length)
        scores = []
        for pair in range(pairs):
            query = joined_ref[at, pair * PAIR : (pair + 1) * PAIR] * jnp.asarray(0.125, BF)
            keys = split_heads(joined_ref[at, width + pair * PAIR : width + (pair + 1) * PAIR])
            scores.append(nt(keys, query))
        all_probs = []
        for pair in range(pairs):
            halves = []
            for head in range(2):
                part = scores[pair][head * length : (head + 1) * length]
                part = jnp.exp(part - jnp.max(part, axis=0, keepdims=True))
                part = part * (1.0 / jnp.sum(part, axis=0, keepdims=True))
                halves.append(part.astype(BF))
            probs = jnp.concatenate(halves, axis=0)
            probs_ref[seq, pair] = probs
            all_probs.append(probs)
        for pair in range(pairs):
            vals = split_heads(
                joined_ref[at, 2 * width + pair * PAIR : 2 * width + (pair + 1) * PAIR]
            )
            ctx_ref[at, pair * PAIR : (pair + 1) * PAIR] = tn(all_probs[pair], vals).astype(BF)
        return carry

    lax.fori_loop(0, rows // length, one, 0)


def attend(tokens, qkv, vec, length):
    rows, width = tokens.shape
    count = rows // length
    steps = 2
    block = rows // steps
    pairs = width // PAIR
    return pl.pallas_call(
        functools.partial(attend_kernel, length),
        grid=(steps,),
        in_specs=[
            pl.BlockSpec((block, width), lambda i: (i, 0)),
            full((3, width, width)),
            full(vec.shape),
        ],
        out_specs=[
            pl.BlockSpec((block, 3 * width), lambda i: (i, 0)),
            pl.BlockSpec((count // steps, pairs, 2 * length, length), lambda i: (i, 0, 0, 0)),
            pl.BlockSpec((block, width), lambda i: (i, 0)),
        ],
        out_shape=[
            jax.ShapeDtypeStruct((rows, 3 * width), BF),
            jax.ShapeDtypeStruct((count, pairs, 2 * length, length), BF),
            jax.ShapeDtypeStruct((rows, width), BF),
        ],
        compiler_params=params(),
        cost_estimate=cost(8 * rows * width * width, 20 * rows * width, rows * width),
        name="attend",
    )(tokens, qkv, vec)


def feed_kernel(
    length,
    load,
    inputs,
    place_ref,
    exit_ref,
    tok_ref,
    ctx_ref,
    out_w_ref,
    vec_ref,
    up_b_ref,
    *refs,
):
    weights, refs = refs[:inputs], refs[inputs:]
    (
        turned_ref,
        act_ref,
        slope_ref,
        unit1_ref,
        scale1_ref,
        unit2_ref,
        scale2_ref,
        output_ref,
        *more,
        acc_ref,
        low_ref,
        line_ref,
    ) = refs[: 11 + (2 if load else 0)]
    step = pl.program_id(0)
    last = pl.num_programs(0) - 1
    rows, width = tok_ref.shape
    sub = 256
    if load:
        up_all, down_all, sems, out_sems = refs[13:]
        each = down_all.shape[0] // up_all.shape[0]
        stores = [
            pltpu.make_async_copy(up_all, more[0], out_sems.at[0]),
            pltpu.make_async_copy(down_all, more[1], out_sems.at[1]),
        ]

        def up_part(cols):
            return up_all[step, :, cols]

        def down_part(cols):
            return down_all[pl.ds(step * each, each), :, cols].reshape(width, sub)

    else:

        def up_part(cols):
            return weights[0][0, :, cols]

        def down_part(cols):
            return weights[1][:, :, cols].reshape(width, sub)

    @pl.when(step == 0)
    def _():
        if load:
            copies = load(weights, up_all, down_all, place_ref, sems)
        for m in range(rows // sub):
            at = slice(m * sub, (m + 1) * sub)
            inner = tok_ref[at].astype(F32) + (
                nn(ctx_ref[at], out_w_ref[0]) + vec_ref[OUT_BIAS : OUT_BIAS + 1]
            )
            unit, scale = norm_stats(inner)
            first = unit * vec_ref[ATTN_GAIN : ATTN_GAIN + 1] + vec_ref[ATTN_SHIFT : ATTN_SHIFT + 1]
            unit1_ref[at] = unit.astype(BF)
            scale1_ref[at] = scale
            low = first.astype(BF)
            low_ref[at] = low
            turned_ref[:, at] = low.T
            acc_ref[at] = first + vec_ref[DOWN_BIAS : DOWN_BIAS + 1]
        if load:
            for copy in copies:
                copy.wait()
            for store in stores:
                store.start()

    tiles = [(m, n) for m in range(rows // sub) for n in range(width // sub)]

    def rows_of(m):
        return slice(m * sub, (m + 1) * sub)

    def first_product(tile):
        return nn(low_ref[rows_of(tile[0])], up_part(rows_of(tile[1])))

    def second_product(m, n):
        at, cols = rows_of(m), rows_of(n)
        acc_ref[at, cols] += nn(line_ref[m % 2], down_part(cols))

    ahead = first_product(tiles[0])
    for index, (m, n) in enumerate(tiles):
        at, cols = rows_of(m), rows_of(n)
        hidden = ahead + up_b_ref[:, cols]
        if index + 1 < len(tiles):
            ahead = first_product(tiles[index + 1])
        if m > 0:
            second_product(m - 1, n)
        act, slope = gelu_parts(hidden)
        act = act.astype(BF)
        line_ref[m % 2, :, cols] = act
        act_ref[cols, at] = act.T
        slope_ref[at, cols] = slope.astype(BF)
    for n in range(width // sub):
        second_product(rows // sub - 1, n)

    @pl.when(step == last)
    def _():
        for seq in range(rows // length):
            at = slice(seq * length, (seq + 1) * length)
            active = (exit_ref[seq] >= LAYER).astype(F32)
            unit, scale = norm_stats(acc_ref[at])
            unit2_ref[at] = unit.astype(BF)
            scale2_ref[at] = scale
            result = (
                unit * vec_ref[BLOCK_GAIN : BLOCK_GAIN + 1] + vec_ref[BLOCK_SHIFT : BLOCK_SHIFT + 1]
            ) * active
            output_ref[at] = result.astype(BF)
        if load:
            for store in stores:
                store.wait()


def feed(place, exit_layer, tokens, ctx, out_w, vec, up_bias, weights, load, shapes, length):
    rows, width = tokens.shape
    hidden = up_bias.shape[1]
    steps = hidden // width
    whole = full((rows, width))
    if load:
        weight_specs = [pl.BlockSpec(memory_space=pl.ANY)] * len(weights)
        more_specs = [pl.BlockSpec(memory_space=pl.ANY)] * 2
        more = [jax.ShapeDtypeStruct(shape, BF) for shape in shapes]
        copies = 2 * shapes[1][0] * shapes[0][0]
        scratch = [pltpu.VMEM(shape, BF) for shape in shapes] + [
            pltpu.SemaphoreType.DMA((copies,)),
            pltpu.SemaphoreType.DMA((2,)),
        ]
    else:
        weight_specs = [
            pl.BlockSpec((1, width, width), lambda i: (i, 0, 0)),
            pl.BlockSpec((1, width, width), lambda i: (i, 0, 0)),
        ]
        more_specs, more, scratch = [], [], []
    return pl.pallas_call(
        functools.partial(feed_kernel, length, load, len(weights)),
        grid=(steps,),
        in_specs=[
            pl.BlockSpec(memory_space=pltpu.SMEM),
            pl.BlockSpec(memory_space=pltpu.SMEM),
            whole,
            whole,
            pl.BlockSpec((1, width, width), lambda i: (3, 0, 0)),
            full(vec.shape),
            pl.BlockSpec((1, width), lambda i: (0, i)),
        ]
        + weight_specs,
        out_specs=[
            full((width, rows)),
            pl.BlockSpec((width, rows), lambda i: (i, 0)),
            pl.BlockSpec((rows, width), lambda i: (0, i)),
            whole,
            full((rows, 1)),
            whole,
            full((rows, 1)),
            whole,
        ]
        + more_specs,
        out_shape=[
            jax.ShapeDtypeStruct((width, rows), BF),
            jax.ShapeDtypeStruct((hidden, rows), BF),
            jax.ShapeDtypeStruct((rows, hidden), BF),
            jax.ShapeDtypeStruct((rows, width), BF),
            jax.ShapeDtypeStruct((rows, 1), F32),
            jax.ShapeDtypeStruct((rows, width), BF),
            jax.ShapeDtypeStruct((rows, 1), F32),
            jax.ShapeDtypeStruct((rows, width), BF),
        ]
        + more,
        scratch_shapes=[
            pltpu.VMEM((rows, width), F32),
            pltpu.VMEM((rows, width), BF),
            pltpu.VMEM((2, 256, width), BF),
        ]
        + scratch,
        compiler_params=params(),
        cost_estimate=cost(18 * rows * width * width, 40 * rows * width, 8 * rows * width),
        name="feed",
    )(place, exit_layer, tokens, ctx, out_w, vec, up_bias, *weights)


def load_second(counts, chips, reps, part, weights, up_all, down_all, place_ref, sems):
    at = 0
    groups = []
    for number in counts:
        groups.append(weights[at : at + number])
        at += number
    copies = []

    def start(source, target):
        copies.append(pltpu.make_async_copy(source, target, sems.at[len(copies)]))
        copies[-1].start()

    second_plan(
        start,
        groups,
        (up_all, down_all),
        place_ref[0],
        place_ref[1],
        place_ref[2],
        chips,
        reps,
        part,
    )
    return copies


def leave_kernel(
    length,
    classes,
    exit_ref,
    output_ref,
    unit2_ref,
    scale2_ref,
    grad_ref,
    pool_ref,
    vec_ref,
    class_bias_ref,
    logit_grad_ref,
    act_ref,
    outer_ref,
    branch_ref,
    early_grad_ref,
    late_grad_ref,
    sums_ref,
    class_grad_ref,
    logits_ref,
    stats_ref,
    lead_ref,
    pool_grad_ref,
):
    step = pl.program_id(0)
    rows, width = output_ref.shape
    pool = pool_ref[...].reshape(width, width)
    count = rows // length

    @pl.when(step == 0)
    def _():
        place = lax.broadcasted_iota(jnp.int32, (count, 1), 0)
        active = jnp.zeros((count, 1), F32)
        for seq in range(count):
            on = (exit_ref[seq] >= LAYER).astype(F32)
            active = jnp.where(place == seq, on, active)
        leading = jnp.concatenate(
            [output_ref[seq * length : seq * length + 1].astype(F32) for seq in range(count)],
            axis=0,
        ).astype(BF)
        pooled = jnp.tanh(nn(leading, pool) + vec_ref[POOL_BIAS : POOL_BIAS + 1])
        pooled_low = pooled.astype(BF)
        used = lax.broadcasted_iota(jnp.int32, (8, width), 0) < classes
        class_rows = jnp.where(used, vec_ref[CLASS_ROWS : CLASS_ROWS + 8], 0.0).astype(BF)
        raw = nt(pooled_low, class_rows) + class_bias_ref[...]
        lane = lax.broadcasted_iota(jnp.int32, raw.shape, 1) < classes
        top = jnp.max(jnp.where(lane, raw, -jnp.inf), axis=-1, keepdims=True)
        spread = jnp.where(lane, jnp.exp(raw - top), 0.0)
        logprob = raw - top - jnp.log(jnp.sum(spread, axis=-1, keepdims=True))
        entropy = -jnp.sum(
            jnp.where(lane, jnp.exp(logprob) * logprob, 0.0), axis=-1, keepdims=True
        )
        logits_ref[...] = raw * active
        class_grad = (logit_grad_ref[...].astype(F32) * active).astype(BF)
        stats_ref[0:1] = jnp.broadcast_to(jnp.sum(entropy * active, axis=0, keepdims=True), (1, 8))
        stats_ref[1:2] = jnp.sum(class_grad.astype(F32), axis=0, keepdims=True)
        class_grad_ref[...] = tn(class_grad, pooled_low)
        pooled_grad = nn(class_grad, class_rows)
        pre_grad = (pooled_grad * (1.0 - pooled * pooled)).astype(BF)
        sums_ref[3:4] = jnp.sum(pre_grad.astype(F32), axis=0, keepdims=True)
        pool_grad_ref[...] = tn(leading, pre_grad).reshape(pool_grad_ref.shape).astype(BF)
        lead_ref[...] = nt(pre_grad, pool)
        head = lax.broadcasted_iota(jnp.int32, (length, 1), 0) == 0
        gain = vec_ref[BLOCK_GAIN : BLOCK_GAIN + 1]
        gain_sum = jnp.zeros((1, width), F32)
        shift_sum = jnp.zeros((1, width), F32)
        bias_sum = jnp.zeros((1, width), F32)
        for seq in range(count):
            at = slice(seq * length, (seq + 1) * length)
            on = (exit_ref[seq] >= LAYER).astype(F32)
            top_grad = (
                grad_ref[at].astype(F32) + jnp.where(head, lead_ref[seq : seq + 1], 0.0)
            ) * on
            unit = unit2_ref[at].astype(F32)
            outer = norm_back(top_grad, unit, scale2_ref[at], gain)
            branch = outer.astype(BF)
            outer_ref[at] = outer
            branch_ref[at] = branch
            gain_sum += jnp.sum(top_grad * unit, axis=0, keepdims=True)
            shift_sum += jnp.sum(top_grad, axis=0, keepdims=True)
            bias_sum += jnp.sum(branch.astype(F32), axis=0, keepdims=True)
        sums_ref[0:1] = gain_sum
        sums_ref[1:2] = shift_sum
        sums_ref[2:3] = bias_sum

    @pl.when(step > 0)
    def _():
        few, early, _ = early_grad_ref.shape
        late = late_grad_ref.shape[1]
        deep = width // few
        value = nn(act_ref[...], branch_ref[...])
        for at in range(few):
            row = at * deep
            early_grad_ref[at] = value[row : row + early].astype(BF)
            late_grad_ref[at, 0 : deep - early] = value[row + early : row + deep].astype(BF)
            late_grad_ref[at, deep - early : late] = pool_grad_ref[(step - 1) * few + at]


def leave(
    exit_layer, output, unit2, scale2, output_grad, pool, vec, class_bias, logit_grad, act,
    pool_spec, shards, length, classes,
):
    rows, width = output.shape
    count = rows // length
    hidden = act.shape[0]
    steps = hidden // width
    few = shards // steps
    deep, part = hidden // shards, width // shards
    early = deep // 2
    late = deep - early + part
    whole = full((rows, width))
    return pl.pallas_call(
        functools.partial(leave_kernel, length, classes),
        grid=(steps + 1,),
        in_specs=[
            pl.BlockSpec(memory_space=pltpu.SMEM),
            whole,
            whole,
            full((rows, 1)),
            whole,
            pool_spec,
            full(vec.shape),
            full(class_bias.shape),
            full(logit_grad.shape),
            pl.BlockSpec((width, rows), lambda i: (jnp.maximum(i - 1, 0), 0)),
        ],
        out_specs=[
            whole,
            whole,
            pl.BlockSpec((few, early, width), lambda i: (jnp.maximum(i - 1, 0), 0, 0)),
            pl.BlockSpec((few, late, width), lambda i: (jnp.maximum(i - 1, 0), 0, 0)),
            full((4, width)),
            full((8, width)),
            full((count, 8)),
            full((2, 8)),
        ],
        out_shape=[
            jax.ShapeDtypeStruct((rows, width), F32),
            jax.ShapeDtypeStruct((rows, width), BF),
            jax.ShapeDtypeStruct((shards, early, width), BF),
            jax.ShapeDtypeStruct((shards, late, width), BF),
            jax.ShapeDtypeStruct((4, width), F32),
            jax.ShapeDtypeStruct((8, width), F32),
            jax.ShapeDtypeStruct((count, 8), F32),
            jax.ShapeDtypeStruct((2, 8), F32),
        ],
        scratch_shapes=[
            pltpu.VMEM((count, width), F32),
            pltpu.VMEM((shards, width // shards, width), BF),
        ],
        compiler_params=params(),
        cost_estimate=cost(8 * rows * width * width, 30 * rows * width),
        name="leave",
    )(
        exit_layer, output, unit2, scale2, output_grad, pool, vec, class_bias, logit_grad, act
    )


def split_cores(value, place_ref, keep_ref, send_ref):
    chips, part, _ = keep_ref.shape
    first = place_ref[2] == 0
    for chip in range(chips):
        even = value[2 * chip * part : (2 * chip + 1) * part]
        odd = value[(2 * chip + 1) * part : (2 * chip + 2) * part]
        keep_ref[chip] = jnp.where(first, even, odd).astype(BF)
        send_ref[chip] = jnp.where(first, odd, even).astype(BF)


def feed_back_kernel(
    place_ref,
    branch_ref,
    slope_ref,
    turned_ref,
    down_ref,
    up_ref,
    outer_ref,
    unit1_ref,
    scale1_ref,
    out_w_ref,
    vec_ref,
    ctx_ref,
    keep_ref,
    send_ref,
    up_sum_ref,
    inner_ref,
    attended_ref,
    ctx_grad_ref,
    sums_ref,
    acc_ref,
    hid_ref,
):
    step = pl.program_id(0)
    rows, width = branch_ref.shape
    sub = 512

    @pl.when(step == 0)
    def _():
        acc_ref[...] = outer_ref[...]

    last = pl.num_programs(0) - 1

    @pl.when(step < last)
    def _():
        total = jnp.zeros((1, width), F32)
        down = down_ref[...].reshape(up_ref.shape[1:])
        ahead = nt(branch_ref[0:sub], down)
        for m in range(rows // sub):
            at = slice(m * sub, (m + 1) * sub)
            hid = (ahead * slope_ref[at].astype(F32)).astype(BF)
            if (m + 1) * sub < rows:
                ahead = nt(branch_ref[(m + 1) * sub : (m + 2) * sub], down)
            hid_ref[at] = hid
            total += jnp.sum(hid.astype(F32), axis=0, keepdims=True)
            acc_ref[at] += nt(hid, up_ref[0])
        up_sum_ref[...] = total
        split_cores(nn(turned_ref[...], hid_ref[...]), place_ref, keep_ref, send_ref)

    @pl.when(step == last)
    def _():
        gain = vec_ref[ATTN_GAIN : ATTN_GAIN + 1]
        gain_sum = jnp.zeros((1, width), F32)
        shift_sum = jnp.zeros((1, width), F32)
        bias_sum = jnp.zeros((1, width), F32)
        for m in range(rows // sub):
            at = slice(m * sub, (m + 1) * sub)
            grad = acc_ref[at]
            unit = unit1_ref[at].astype(F32)
            inner = norm_back(grad, unit, scale1_ref[at], gain)
            attended = inner.astype(BF)
            inner_ref[at] = inner
            attended_ref[at] = attended
            ctx_grad_ref[at] = nt(attended, out_w_ref[0]).astype(BF)
            gain_sum += jnp.sum(grad * unit, axis=0, keepdims=True)
            shift_sum += jnp.sum(grad, axis=0, keepdims=True)
            bias_sum += jnp.sum(attended.astype(F32), axis=0, keepdims=True)
        sums_ref[0:1] = gain_sum
        sums_ref[1:2] = shift_sum
        sums_ref[2:3] = bias_sum
        split_cores(tn(ctx_ref[...], attended_ref[...]), place_ref, keep_ref, send_ref)


def feed_back(place, chips, branch, slope, low, down, down_block, up, outer, unit1, scale1, out_w, vec, ctx):
    rows, width = branch.shape
    hidden = slope.shape[1]
    steps = hidden // width
    whole = full((rows, width))
    end = steps - 1
    part = width // (2 * chips)
    return pl.pallas_call(
        feed_back_kernel,
        grid=(steps + 1,),
        in_specs=[
            pl.BlockSpec(memory_space=pltpu.SMEM),
            whole,
            pl.BlockSpec((rows, width), lambda i: (0, jnp.minimum(i, end))),
            full((width, rows)),
            pl.BlockSpec(down_block, lambda i: (jnp.minimum(i, end), 0, 0)),
            pl.BlockSpec((1, width, width), lambda i: (jnp.minimum(i, end), 0, 0)),
            whole,
            whole,
            full((rows, 1)),
            pl.BlockSpec((1, width, width), lambda i: (3, 0, 0)),
            full(vec.shape),
            whole,
        ],
        out_specs=[
            pl.BlockSpec((chips, part, width), lambda i: (0, 0, i)),
            pl.BlockSpec((chips, part, width), lambda i: (0, 0, i)),
            pl.BlockSpec((1, width), lambda i: (0, jnp.minimum(i, end))),
            whole,
            whole,
            whole,
            full((3, width)),
        ],
        out_shape=[
            jax.ShapeDtypeStruct((chips, part, hidden + width), BF),
            jax.ShapeDtypeStruct((chips, part, hidden + width), BF),
            jax.ShapeDtypeStruct((1, hidden), F32),
            jax.ShapeDtypeStruct((rows, width), F32),
            jax.ShapeDtypeStruct((rows, width), BF),
            jax.ShapeDtypeStruct((rows, width), BF),
            jax.ShapeDtypeStruct((3, width), F32),
        ],
        scratch_shapes=[pltpu.VMEM((rows, width), F32), pltpu.VMEM((rows, width), BF)],
        compiler_params=params(),
        cost_estimate=cost(28 * rows * width * width, 40 * rows * width),
        name="feed_back",
    )(place, branch, slope, low, down, up, outer, unit1, scale1, out_w, vec, ctx)


def attend_back_kernel(length, joined_ref, probs_ref, ctx_grad_ref, grad_ref, sum_ref):
    rows, width = ctx_grad_ref.shape
    pairs = width // PAIR

    def one(seq, carry):
        at = pl.ds(pl.multiple_of(seq * length, length), length)

        def columns(part, pair):
            return slice(part * width + pair * PAIR, part * width + (pair + 1) * PAIR)

        prob_grads = []
        for pair in range(pairs):
            vals = split_heads(joined_ref[at, columns(2, pair)])
            prob_grads.append(nt(vals, ctx_grad_ref[at, columns(0, pair)]))
        score_grads = []
        for pair in range(pairs):
            probs = probs_ref[seq, pair]
            halves = []
            for head in range(2):
                cut = slice(head * length, (head + 1) * length)
                held = probs[cut].astype(F32)
                part = prob_grads[pair][cut]
                base = jnp.sum(part * held, axis=0, keepdims=True)
                halves.append((held * (part - base)).astype(BF))
            score_grads.append(halves)
        for pair in range(pairs):
            probs = probs_ref[seq, pair]
            beside = jnp.concatenate([probs[:length], probs[length:]], axis=1)
            ctx_grads = split_heads(ctx_grad_ref[at, columns(0, pair)])
            grad_ref[at, columns(2, pair)] = nn(beside, ctx_grads).astype(BF)
        for pair in range(pairs):
            queries = split_heads(joined_ref[at, columns(0, pair)] * jnp.asarray(0.125, BF))
            beside = jnp.concatenate(score_grads[pair], axis=1)
            grad_ref[at, columns(1, pair)] = nn(beside, queries).astype(BF)
        for pair in range(pairs):
            keys = split_heads(joined_ref[at, columns(1, pair)])
            stacked = jnp.concatenate(score_grads[pair], axis=0)
            grad_ref[at, columns(0, pair)] = (tn(stacked, keys) * 0.125).astype(BF)
        return carry

    lax.fori_loop(0, rows // length, one, 0)
    total = jnp.zeros(sum_ref.shape, F32)
    for m in range(rows // length):
        total += jnp.sum(
            grad_ref[m * length : (m + 1) * length].astype(F32), axis=0, keepdims=True
        )

    @pl.when(pl.program_id(0) == 0)
    def _():
        sum_ref[...] = total

    @pl.when(pl.program_id(0) > 0)
    def _():
        sum_ref[...] += total


def attend_back(joined, probs, ctx_grad, length):
    rows, width = ctx_grad.shape
    count = rows // length
    steps = 2
    block = rows // steps
    pairs = width // PAIR
    return pl.pallas_call(
        functools.partial(attend_back_kernel, length),
        grid=(steps,),
        in_specs=[
            pl.BlockSpec((block, 3 * width), lambda i: (i, 0)),
            pl.BlockSpec((count // steps, pairs, 2 * length, length), lambda i: (i, 0, 0, 0)),
            pl.BlockSpec((block, width), lambda i: (i, 0)),
        ],
        out_specs=[
            pl.BlockSpec((block, 3 * width), lambda i: (i, 0)),
            full((1, 3 * width)),
        ],
        out_shape=[
            jax.ShapeDtypeStruct((rows, 3 * width), BF),
            jax.ShapeDtypeStruct((1, 3 * width), F32),
        ],
        compiler_params=params(),
        cost_estimate=cost(8 * rows * width * width, 20 * rows * width),
        name="attend_back",
    )(joined, probs, ctx_grad)


def weight_grads_kernel(tok_ref, joined_ref, small_ref, out_ref, turned_ref):
    step = pl.program_id(0)
    last = pl.num_programs(0) - 1
    shards, part, width = out_ref.shape

    @pl.when(step == 0)
    def _():
        turned_ref[...] = tok_ref[...].T

    value = nn(turned_ref[...], joined_ref[...])
    cols = pl.ds(pl.multiple_of(step * joined_ref.shape[1], joined_ref.shape[1]), joined_ref.shape[1])
    out_ref[:, :, cols] = value.reshape(shards, part, joined_ref.shape[1]).astype(BF)
    tail = 3 * joined_ref.shape[1]
    if width > tail:

        @pl.when(step == last)
        def _():
            lines = small_ref.shape[1]
            out_ref[:, lines:part, tail:width] = jnp.zeros(
                (shards, part - lines, width - tail), BF
            )
            out_ref[:, 0:lines, tail:width] = small_ref[...].astype(BF)


def weight_grads(tokens, joined_grad, small, shards, extra):
    rows, width = tokens.shape
    shape = (shards, width // shards, 3 * width + extra)
    return pl.pallas_call(
        weight_grads_kernel,
        grid=(3,),
        in_specs=[
            full((rows, width)),
            pl.BlockSpec((rows, width), lambda i: (0, i)),
            full(small.shape),
        ],
        out_specs=full(shape),
        out_shape=jax.ShapeDtypeStruct(shape, BF),
        scratch_shapes=[pltpu.VMEM((width, rows), BF)],
        compiler_params=params(),
        cost_estimate=cost(6 * rows * width * width, 20 * rows * width),
        name="weight_grads",
    )(tokens, joined_grad, small)


def input_kernel(inner_ref, joined_ref, w_ref, out_ref):
    width = inner_ref.shape[1]
    total = inner_ref[...]
    for part in range(3):
        total += nt(joined_ref[:, part * width : (part + 1) * width], w_ref[part])
    out_ref[...] = total.astype(BF)


def input_back(inner, joined_grad, qkv):
    rows, width = inner.shape
    steps = 4
    block = rows // steps
    return pl.pallas_call(
        input_kernel,
        grid=(steps,),
        in_specs=[
            pl.BlockSpec((block, width), lambda i: (i, 0)),
            pl.BlockSpec((block, 3 * width), lambda i: (i, 0)),
            full((3, width, width)),
        ],
        out_specs=pl.BlockSpec((block, width), lambda i: (i, 0)),
        out_shape=jax.ShapeDtypeStruct((rows, width), BF),
        compiler_params=params(),
        cost_estimate=cost(6 * rows * width * width, 12 * rows * width),
        name="input_back",
    )(inner, joined_grad, qkv)


def lay_kernel(plan, chips, reps, part, counts, place_ref, *refs):
    at = 0
    groups = []
    for number in counts:
        groups.append(refs[at : at + number])
        at += number
    sems = refs[-1]
    rep, chip, core = place_ref[0], place_ref[1], place_ref[2]
    copies = []

    def start(source, target):
        copies.append(pltpu.make_async_copy(source, target, sems.at[len(copies)]))
        copies[-1].start()

    finish = plan(start, groups, refs[at:-1], rep, chip, core, chips, reps, part)
    for copy in copies:
        copy.wait()
    if finish is not None:
        finish()


def blocks_plan(
    put, own, twin, along, across, swapped, depth, first, rep, chip, core, chips, reps, part
):
    for block in range(reps):
        put(own(block), block, chip, core)
        put(twin(block), block, chip, 1 - core)
    for step in range(1, chips):
        source = lax.rem(chip + chips - step, chips)
        rows = pl.ds((step - 1) * depth + first, part)
        for other, block in along.items():
            put(block(step, source, 0), rep ^ other, source, core)
            put(block(step, source, 1), rep ^ other, source, 1 - core)
        for other in across:
            put(across[other].at[rows], rep ^ other, source, core)
            put(swapped[other].at[rows], rep ^ other, source, 1 - core)


def wide_put(start, out_ref, part):
    def put(source, block, at_chip, at_core):
        row = pl.multiple_of((at_chip * 2 + at_core) * part, part)
        start(source, out_ref.at[block, pl.ds(row, part)])

    return put


def wide_block(ref, width, part):
    return lambda block: ref.at[pl.ds(0, part), pl.ds(block * width, width)]


def first_plan(start, groups, outs, rep, chip, core, chips, reps, part):
    (own, twin), along, across, swapped, (extra,) = groups
    out_ref, vec_ref, more_ref = outs
    width = out_ref.shape[2]

    def near(step, source, side):
        if side == 0:
            return along[step - 1].at[pl.ds(0, part)]
        return swapped[0].at[pl.ds((step - 1) * part, part)]

    blocks_plan(
        wide_put(start, out_ref, part),
        wide_block(own, width, part),
        wide_block(twin, width, part),
        {0: near},
        {at + 1: ref for at, ref in enumerate(across)},
        {at + 1: ref for at, ref in enumerate(swapped[1:])},
        part,
        0,
        rep,
        chip,
        core,
        chips,
        reps,
        part,
    )
    tail = pl.ds(part, 16)
    cols = pl.ds(0, width)
    start(own.at[tail, cols], more_ref.at[chip * 2 + core])
    start(twin.at[tail, cols], more_ref.at[chip * 2 + 1 - core])
    for step in range(1, chips):
        source = lax.rem(chip + chips - step, chips)
        start(along[step - 1].at[tail], more_ref.at[source * 2 + core])
        start(extra.at[pl.ds((step - 1) * 16, 16)], more_ref.at[source * 2 + 1 - core])

    def finish():
        lane = lax.broadcasted_iota(jnp.int32, (LANES, width), 0)
        place = lax.broadcasted_iota(jnp.int32, (LANES, width), 1)
        total = jnp.zeros((16, width), F32)
        for shard in range(2 * chips):
            there = (place - shard * part == lane) & (lane < part)
            total += nn(more_ref[shard, :, 0:LANES], there.astype(F32).astype(BF))
        vec_ref[...] = total

    return finish


def second_plan(start, groups, outs, rep, chip, core, chips, reps, part):
    (up, up_twin, down, down_twin), (close, far), across, swapped = groups
    up_ref, down_ref = outs
    width = up_ref.shape[2]
    where = (rep, chip, core, chips, reps, part)

    def chained(chain, first):
        def block(step, source, side):
            shard = source * 2 + (core if side == 0 else 1 - core)
            return chain.at[shard, pl.ds(first, part)]

        return block

    across = dict(zip(NEAR, across))
    swapped = dict(zip(NEAR, swapped))
    blocks_plan(
        wide_put(start, up_ref, part),
        wide_block(up, width, part),
        wide_block(up_twin, width, part),
        {0: chained(close, 0), FAR: chained(far, 0)},
        across,
        swapped,
        2 * part,
        0,
        *where,
    )

    def put(source, block, at_chip, at_core):
        row = pl.multiple_of(block * part, part)
        start(source, down_ref.at[at_chip * 2 + at_core, pl.ds(row, part)])

    def tall(ref):
        return lambda block: ref.at[pl.ds(block * part, part)]

    blocks_plan(
        put,
        tall(down),
        tall(down_twin),
        {0: chained(close, part), FAR: chained(far, part)},
        across,
        swapped,
        2 * part,
        part,
        *where,
    )


def lay(plan, place, groups, shapes, scratch, copies, part, chips, reps):
    anywhere = pl.BlockSpec(memory_space=pl.ANY)
    inputs = [ref for group in groups for ref in group]
    return pl.pallas_call(
        functools.partial(
            lay_kernel, plan, chips, reps, part, [len(group) for group in groups]
        ),
        in_specs=[pl.BlockSpec(memory_space=pltpu.SMEM)] + [anywhere] * len(inputs),
        out_specs=[pl.BlockSpec(memory_space=pltpu.VMEM)] * len(shapes),
        out_shape=[jax.ShapeDtypeStruct(shape, kind) for shape, kind in shapes],
        scratch_shapes=[pltpu.VMEM(shape, BF) for shape in scratch]
        + [pltpu.SemaphoreType.DMA((copies,))],
        compiler_params=pltpu.CompilerParams(vmem_limit_bytes=VMEM_BYTES),
        cost_estimate=cost(0, 4 * sum(math.prod(shape) for shape, kind in shapes)),
        name="lay",
    )(place, *inputs)


def pack_vectors(rows, up_bias, class_weight):
    part = rows[0].shape[0]
    lines = [row[None] for row in rows[:8]] + [class_weight.T] + [row[None] for row in rows[8:]]
    pieces = up_bias.shape[0] // part
    lines += [up_bias[None, at * part : (at + 1) * part] for at in range(pieces)]
    return jnp.concatenate(lines, axis=0)


def move(values, reps, chips, target):
    pairs = []
    for rep in range(reps):
        for chip in range(chips):
            for core in range(2):
                to_rep, to_chip, to_core = target(rep, chip, core)
                pairs.append(
                    (
                        (rep * chips + chip) * 2 + core,
                        (to_rep * chips + to_chip) * 2 + to_core,
                    )
                )
    return lax.ppermute(values, ("rep", "fsdp"), pairs)


def along_chips(step, chips):
    return lambda rep, chip, core: (rep, (chip + step) % chips, core)


def across_reps(other):
    return lambda rep, chip, core: (rep ^ other, chip, core)


def to_twin(rep, chip, core):
    return rep, chip, 1 - core


def after(values, *gates):
    return lax.optimization_barrier((values, *gates))[0]


def along_z(mine, reps, chips):
    return [move(mine, reps, chips, along_chips(step, chips)) for step in range(1, chips)]


def over_reps(stacked, reps, chips, others):
    return [move(stacked, reps, chips, across_reps(other)) for other in others]


def pick(parts, at):
    return lax.dynamic_index_in_dim(parts, at, axis=0, keepdims=False)


def in_order(rep, reps, own, others, axis):
    blocks = jnp.stack([own] + others)
    return jnp.concatenate([pick(blocks, rep ^ at) for at in range(reps)], axis=axis)


class Reduction:
    def __init__(self, place, keep, send, reps, chips):
        self.rep, self.chip = place[0], place[1]
        self.reps, self.chips = reps, chips
        self.keep = keep
        self.got = move(send, reps, chips, to_twin)

    def at_rep(self, at):
        return lax.dynamic_index_in_dim(self.both, at, axis=1, keepdims=False)

    def over_reps(self):
        chips, rows, width = self.keep.shape
        both = (self.keep.astype(F32) + self.got.astype(F32)).astype(BF)
        self.both = lax.optimization_barrier(both).reshape(
            chips, self.reps, rows // self.reps, width
        )
        self.arrived = [
            move(self.at_rep(self.rep ^ other), self.reps, self.chips, across_reps(other))
            for other in range(1, self.reps)
        ]

    def over_chips(self, *gates):
        if gates:
            self.arrived = [after(block, *gates) for block in self.arrived]
        total = self.at_rep(self.rep).astype(F32)
        for block in self.arrived:
            total = total + block.astype(F32)
        self.total = pick(total, self.chip)
        self.passed = [
            move(
                pick(total, lax.rem(self.chip + step, self.chips)).astype(BF),
                self.reps,
                self.chips,
                along_chips(step, self.chips),
            )
            for step in range(1, self.chips)
        ]

    def chip_sum(self):
        total = self.total
        for block in self.passed:
            total = total + block.astype(F32)
        return total.astype(BF)


def share_reps(place, total, reps, chips):
    others = [move(total, reps, chips, across_reps(other)) for other in range(1, reps)]
    return in_order(place[0], reps, total, others, 0).astype(F32), others


def exchange_reps(place, rows, reps, chips):
    rep = place[0]
    parts = rows.reshape(reps, -1, rows.shape[1])
    total = pick(parts, rep).astype(F32)
    arrived = [
        move(pick(parts, rep ^ other), reps, chips, across_reps(other))
        for other in range(1, reps)
    ]
    for block in arrived:
        total = total + block.astype(F32)
    return total.astype(BF), arrived


def per_device(
    tokens,
    exit_layer,
    qkv_weight,
    query_bias,
    value_bias,
    out_weight,
    out_bias,
    attn_gain,
    attn_shift,
    up_weight,
    up_bias,
    down_weight,
    down_bias,
    block_gain,
    block_shift,
    pool_weight,
    pool_bias,
    class_weight,
    class_bias,
    output_grad,
    logit_grad,
):
    reps = lax.axis_size("rep")
    shards = lax.axis_size("fsdp")
    mine = lax.axis_index("fsdp")
    rows, width = tokens.shape
    count = exit_layer.shape[0]
    length = rows // count
    classes = class_weight.shape[1]
    part = out_weight.shape[0]
    hidden = up_weight.shape[1]

    def gather(shard):
        return lax.all_gather(shard, "fsdp", axis=0, tiled=True)

    packed = pack_vectors(
        [
            query_bias,
            value_bias,
            out_bias,
            attn_gain,
            attn_shift,
            down_bias,
            block_gain,
            block_shift,
            pool_bias,
        ],
        up_bias,
        class_weight,
    )
    joint_own = jnp.concatenate([qkv_weight, out_weight], axis=1)
    deep = down_weight.shape[0]
    chips = shards // 2
    place = jnp.stack([lax.axis_index("rep"), mine // 2, mine % 2]).astype(jnp.int32)
    direct = (
        part % 16 == 0
        and reps & (reps - 1) == 0
        and reps * width == hidden
        and reps == 4
        and packed.shape[0] <= 16
    )
    if direct:
        lines = packed.shape[0]
        held = jnp.pad(packed, ((0, 16 - lines), (0, width - part)))
        own = jnp.concatenate([joint_own, jnp.tile(held, (1, reps))], axis=0)
        rep = place[0]

        def block_of(weights, at):
            return lax.dynamic_slice_in_dim(weights, at * width, width, axis=1)

        def second_of(at):
            return [
                block_of(up_weight, at),
                lax.dynamic_slice_in_dim(down_weight, at * part, part, axis=0),
            ]

        along = along_z(block_of(own, rep), reps, chips)
        chain = gather(after(jnp.concatenate(second_of(rep), axis=0), *along))
        chain = chain.reshape(chips, 2, 2 * part, width)
        twin = move(own, reps, chips, to_twin)
        stacked = jnp.concatenate([rows_[:part] for rows_ in along], axis=0)
        across = over_reps(stacked, reps, chips, range(1, reps))
        far_chain = gather(after(jnp.concatenate(second_of(rep ^ FAR), axis=0), *across))
        swapped = [move(rows_, reps, chips, to_twin) for rows_ in [stacked] + across]
        extra = move(
            jnp.concatenate([rows_[part:] for rows_ in along], axis=0), reps, chips, to_twin
        )
        up_twin = move(up_weight, reps, chips, to_twin)
        down_twin = move(down_weight, reps, chips, to_twin)
        joint, vec = lay(
            first_plan,
            place,
            [
                [own, twin],
                along,
                across,
                swapped,
                [extra],
            ],
            [((reps, width, width), BF), ((16, width), F32)],
            [(shards, 16, width)],
            2 * chips * (reps + 1),
            part,
            chips,
            reps,
        )
        mine_chain = lax.dynamic_index_in_dim(
            after(chain, joint), place[2], axis=1, keepdims=False
        )
        second_stacked = jnp.concatenate(
            [
                pick(mine_chain, lax.rem(place[1] + chips - step, chips))
                for step in range(1, chips)
            ],
            axis=0,
        )
        second_across = over_reps(after(second_stacked, *across), reps, chips, NEAR)
        up_row = (
            vec[VECTOR_ROWS:lines].reshape(-1, shards, part).transpose(1, 0, 2).reshape(1, hidden)
        )
        down_block = (width // deep, deep, width)
    else:
        small = gather(packed[None])
        vec = small[:, :VECTOR_ROWS].transpose(1, 0, 2).reshape(VECTOR_ROWS, width).astype(F32)
        vec = jnp.pad(vec, ((0, 16 - VECTOR_ROWS), (0, 0)))
        up_row = small[:, VECTOR_ROWS:].transpose(0, 1, 2).reshape(1, hidden).astype(F32)
        pool = gather(pool_weight)
        joint = jnp.stack(jnp.split(gather(joint_own), 4, axis=1))
        up = jnp.stack(jnp.split(gather(up_weight), hidden // width, axis=1))
        down = gather(down_weight).reshape(-1, width, width)
        down_block = (1, width, width)
    joined, probs, ctx = attend(tokens, joint, vec, length)
    if direct:
        pool = gather(after(pool_weight, ctx))
        far_chain = after(far_chain, ctx)
        second_swapped = [
            move(after(rows_, ctx), reps, chips, to_twin) for rows_ in second_across
        ]
        groups = [
            [up_weight, up_twin, down_weight, down_twin],
            [
                chain.reshape(shards, 2 * part, width),
                far_chain.reshape(shards, 2 * part, width),
            ],
            second_across,
            second_swapped,
        ]
        weights = [ref for group in groups for ref in group]
        load = functools.partial(load_second, [len(group) for group in groups], chips, reps, part)
        shapes = [(reps, width, width), (shards, deep, width)]
    else:
        weights, load, shapes = [up, down], None, None
    turned, act, slope, unit1, scale1, unit2, scale2, output, *laid = feed(
        place, exit_layer, tokens, ctx, joint, vec, up_row, weights, load, shapes, length
    )
    if direct:
        up, down = laid
    class_bias_row = jnp.pad(class_bias.astype(F32), (0, 8 - classes))[None]
    logit_grad_rows = jnp.pad(logit_grad, ((0, 0), (0, 8 - classes)))
    outer, branch, early_grad, late_grad, exit_sums, class_grad, logits, stats = leave(
        exit_layer,
        output,
        unit2,
        scale2,
        output_grad,
        pool,
        vec,
        class_bias_row,
        logit_grad_rows,
        act,
        full((width, width)),
        shards,
        length,
        classes,
    )
    def scatter(grad):
        return lax.psum_scatter(grad, "fsdp", scatter_dimension=0, tiled=True)

    early_part = scatter(early_grad.reshape(-1, width))
    up_keep, up_send, up_sum, inner, attended, ctx_grad, feed_sums = feed_back(
        place, chips, branch, slope, turned, down, down_block, up, outer, unit1, scale1, joint, vec, ctx
    )
    if direct:
        up_red = Reduction(place, up_keep, up_send, reps, chips)
        up_red.over_reps()
        ctx_grad = after(ctx_grad, up_red.both, early_part)
    joined_grad, joined_sum = attend_back(joined, probs, ctx_grad, length)
    joined_seen = joined_grad
    if direct:
        joined_seen = after(joined_grad, *up_red.arrived[:2])
    sums = jnp.concatenate(
        [
            joined_sum.reshape(3, width)[::2],
            feed_sums,
            exit_sums,
            class_grad[:classes],
        ],
        axis=0,
    )
    lines = sums.shape[0]
    own_sums = sums.reshape(lines, shards, part).transpose(1, 0, 2).reshape(shards, lines * part)
    own_sums = jnp.concatenate([own_sums, up_sum.reshape(shards, deep)], axis=1)
    used = own_sums.shape[1]
    seqs_total = count * reps * shards
    figures = jnp.concatenate([stats[0, :1], stats[1, :classes]])
    slots = reps * shards * figures.shape[0] * 3
    direct = direct and used + slots <= part * LANES
    small_lines = 16
    if direct:
        high = figures.astype(BF).astype(F32)
        middle = (figures - high).astype(BF).astype(F32)
        lowest = figures - high - middle
        split = jnp.concatenate([high, middle, lowest])
        slot = lax.axis_index("rep") * shards + mine
        lone = jnp.where(
            jnp.arange(reps * shards)[:, None] == slot, split[None], 0.0
        ).reshape(1, slots)
        row = jnp.concatenate([own_sums, jnp.broadcast_to(lone, (shards, slots))], axis=1)
        small_lines = -(-row.shape[1] // (LANES * 16)) * 16
        row = jnp.pad(row, ((0, 0), (0, small_lines * LANES - row.shape[1])))
        row = row.reshape(shards, small_lines, LANES)
    else:
        row = jnp.zeros((shards, small_lines, LANES), F32)
    joint_grad = weight_grads(tokens, joined_seen, row, shards, LANES if direct else 0)
    input_grad = input_back(inner, joined_grad, joint)

    late_part = scatter(late_grad.reshape(-1, width))
    if direct:
        joint_grad = after(joint_grad, *up_red.arrived)
        early_part, late_part = after(early_part, joint_grad), after(late_part, joint_grad)
    low_part = jnp.concatenate([early_part, late_part], axis=0)
    joint_part = scatter(joint_grad.reshape(width, -1))
    if direct:
        low_total, low_arrived = exchange_reps(place, low_part, reps, chips)
        up_red.over_chips(*low_arrived)
        wide = (deep + part) * width // part
        up_total = up_red.chip_sum()
        columns = up_total.shape[1]
        pair, pair_others = share_reps(
            place,
            jnp.concatenate([up_total, low_total.reshape(-1, wide)], axis=1),
            reps,
            chips,
        )
        up_sum = pair[:, :columns]
        low_sum = pair[:, columns:].reshape(deep + part, width)
        joint_total, _ = exchange_reps(
            place, after(joint_part, *pair_others), reps, chips
        )
        joint_sum, _ = share_reps(place, joint_total, reps, chips)
        small_sum = joint_sum[:small_lines, 3 * width :].reshape(-1)
        total = small_sum[used : used + slots].reshape(-1, figures.shape[0]).sum(axis=0)
    else:
        first = mine % 2 == 0

        def whole_of(kept, sent):
            pair = jnp.stack([jnp.where(first, kept, sent), jnp.where(first, sent, kept)], axis=1)
            return pair.reshape(-1, kept.shape[2])

        joint_sum, low_sum, up_sum = lax.psum(
            (joint_part, low_part, scatter(whole_of(up_keep, up_send))), "rep"
        )
        joint_sum, low_sum, up_sum = (
            joint_sum.astype(F32),
            low_sum.astype(F32),
            up_sum.astype(F32),
        )
        own_sums, total = lax.psum((own_sums, figures), ("rep", "fsdp"))
        small_sum = pick(own_sums, mine)
    own = small_sum[: lines * part].reshape(lines, part)
    return (
        output,
        logits[:, :classes],
        total[0] / seqs_total,
        input_grad,
        joint_sum[:, : 3 * width],
        own[0],
        own[1],
        up_sum[:, hidden:],
        own[4],
        own[2],
        own[3],
        up_sum[:, :hidden],
        small_sum[lines * part : used],
        low_sum[:deep],
        own[7],
        own[5],
        own[6],
        low_sum[deep:],
        own[8],
        own[9 : 9 + classes].T,
        total[1:],
    )


def solution(mesh):
    return jax.shard_map(
        per_device,
        mesh=mesh,
        in_specs=(
            P(("rep", "fsdp"), None),
            P(("rep", "fsdp")),
            P("fsdp", None),
            P("fsdp"),
            P("fsdp"),
            P("fsdp", None),
            P("fsdp"),
            P("fsdp"),
            P("fsdp"),
            P("fsdp", None),
            P("fsdp"),
            P("fsdp", None),
            P("fsdp"),
            P("fsdp"),
            P("fsdp"),
            P("fsdp", None),
            P("fsdp"),
            P("fsdp", None),
            P(),
            P(("rep", "fsdp"), None),
            P(("rep", "fsdp"), None),
        ),
        out_specs=(
            P(("rep", "fsdp"), None),
            P(("rep", "fsdp"), None),
            P(),
            P(("rep", "fsdp"), None),
            P("fsdp", None),
            P("fsdp"),
            P("fsdp"),
            P("fsdp", None),
            P("fsdp"),
            P("fsdp"),
            P("fsdp"),
            P("fsdp", None),
            P("fsdp"),
            P("fsdp", None),
            P("fsdp"),
            P("fsdp"),
            P("fsdp"),
            P("fsdp", None),
            P("fsdp"),
            P("fsdp", None),
            P(),
        ),
        check_vma=False,
    )
```

```python
import functools
import math

import jax
import jax.numpy as jnp
from jax import lax
from jax.experimental import pallas as pl
from jax.experimental.pallas import tpu as pltpu
from jax.sharding import PartitionSpec as P

HD = 64
LAYER = 6
PAIR = 2 * HD
NEAR = (1, 2)
FAR = 3
LANES = 128
VMEM_BYTES = 58 * 2**20
BF = jnp.bfloat16
F32 = jnp.float32

QUERY_BIAS, VALUE_BIAS, OUT_BIAS, ATTN_GAIN, ATTN_SHIFT = 0, 1, 2, 3, 4
DOWN_BIAS, BLOCK_GAIN, BLOCK_SHIFT, CLASS_ROWS, POOL_BIAS = 5, 6, 7, 8, 11
VECTOR_ROWS = 12


def nn(left, right):
    return jnp.dot(left, right, preferred_element_type=F32)


def tn(left, right):
    return lax.dot_general(left, right, (((0,), (0,)), ((), ())), preferred_element_type=F32)


def nt(left, right):
    return lax.dot_general(left, right, (((1,), (1,)), ((), ())), preferred_element_type=F32)


def full(shape):
    return pl.BlockSpec(shape, lambda *at: (0,) * len(shape))


def params():
    return pltpu.CompilerParams(
        dimension_semantics=("arbitrary",), vmem_limit_bytes=VMEM_BYTES
    )


def cost(flops, moved, trans=0):
    return pl.CostEstimate(flops=flops, bytes_accessed=moved, transcendentals=trans)


def split_heads(pair):
    lane = lax.broadcasted_iota(jnp.int32, pair.shape, 1)
    zero = jnp.zeros_like(pair)
    return jnp.concatenate(
        [jnp.where(lane < HD, pair, zero), jnp.where(lane < HD, zero, pair)], axis=0
    )


def norm_stats(values):
    center = values - jnp.mean(values, axis=-1, keepdims=True)
    spread = jnp.mean(center * center, axis=-1, keepdims=True)
    scale = lax.rsqrt(spread + 1e-06)
    return center * scale, scale


def norm_back(grad, unit, scale, gain):
    inner = grad * gain
    first = jnp.mean(inner, axis=-1, keepdims=True)
    second = jnp.mean(inner * unit, axis=-1, keepdims=True)
    return scale * (inner - first - unit * second)


def gelu_parts(values):
    base = 1.0 + 0.23164189 * jnp.abs(values)
    t = pl.reciprocal(base, approx=True)
    t = t * (2.0 - base * t)
    bell = jnp.exp2((values * values) * -0.7213475204444817)
    poly = t * (
        0.127414796
        + t * (-0.142248368 + t * (0.7107068705 + t * (-0.7265760135 + t * 0.5307027145)))
    )
    tail = poly * bell
    below = jnp.where(values >= 0.0, 1.0 - tail, tail)
    return values * below, below + values * (bell * 0.3989422804014327)


def attend_kernel(length, tok_ref, w_ref, vec_ref, joined_ref, probs_ref, ctx_ref):
    rows, width = ctx_ref.shape
    pairs = width // PAIR
    for part in range(3):
        cols = slice(part * width, (part + 1) * width)
        value = nn(tok_ref[...], w_ref[part])
        if part == 0:
            value += vec_ref[QUERY_BIAS : QUERY_BIAS + 1]
        elif part == 2:
            value += vec_ref[VALUE_BIAS : VALUE_BIAS + 1]
        joined_ref[:, cols] = value.astype(BF)

    def one(seq, carry):
        at = pl.ds(pl.multiple_of(seq * length, length), length)
        scores = []
        for pair in range(pairs):
            query = joined_ref[at, pair * PAIR : (pair + 1) * PAIR] * jnp.asarray(0.125, BF)
            keys = split_heads(joined_ref[at, width + pair * PAIR : width + (pair + 1) * PAIR])
            scores.append(nt(keys, query))
        all_probs = []
        for pair in range(pairs):
            halves = []
            for head in range(2):
                part = scores[pair][head * length : (head + 1) * length]
                part = jnp.exp(part - jnp.max(part, axis=0, keepdims=True))
                part = part * (1.0 / jnp.sum(part, axis=0, keepdims=True))
                halves.append(part.astype(BF))
            probs = jnp.concatenate(halves, axis=0)
            probs_ref[seq, pair] = probs
            all_probs.append(probs)
        for pair in range(pairs):
            vals = split_heads(
                joined_ref[at, 2 * width + pair * PAIR : 2 * width + (pair + 1) * PAIR]
            )
            ctx_ref[at, pair * PAIR : (pair + 1) * PAIR] = tn(all_probs[pair], vals).astype(BF)
        return carry

    lax.fori_loop(0, rows // length, one, 0)


def attend(tokens, qkv, vec, length):
    rows, width = tokens.shape
    count = rows // length
    steps = 2
    block = rows // steps
    pairs = width // PAIR
    return pl.pallas_call(
        functools.partial(attend_kernel, length),
        grid=(steps,),
        in_specs=[
            pl.BlockSpec((block, width), lambda i: (i, 0)),
            full((3, width, width)),
            full(vec.shape),
        ],
        out_specs=[
            pl.BlockSpec((block, 3 * width), lambda i: (i, 0)),
            pl.BlockSpec((count // steps, pairs, 2 * length, length), lambda i: (i, 0, 0, 0)),
            pl.BlockSpec((block, width), lambda i: (i, 0)),
        ],
        out_shape=[
            jax.ShapeDtypeStruct((rows, 3 * width), BF),
            jax.ShapeDtypeStruct((count, pairs, 2 * length, length), BF),
            jax.ShapeDtypeStruct((rows, width), BF),
        ],
        compiler_params=params(),
        cost_estimate=cost(8 * rows * width * width, 20 * rows * width, rows * width),
        name="attend",
    )(tokens, qkv, vec)


def feed_kernel(
    length,
    load,
    inputs,
    place_ref,
    exit_ref,
    tok_ref,
    ctx_ref,
    out_w_ref,
    vec_ref,
    up_b_ref,
    *refs,
):
    weights, refs = refs[:inputs], refs[inputs:]
    (
        turned_ref,
        act_ref,
        slope_ref,
        unit1_ref,
        scale1_ref,
        unit2_ref,
        scale2_ref,
        output_ref,
        *more,
        acc_ref,
        low_ref,
        line_ref,
    ) = refs[: 11 + (2 if load else 0)]
    step = pl.program_id(0)
    last = pl.num_programs(0) - 1
    rows, width = tok_ref.shape
    sub = 256
    if load:
        up_all, down_all, sems, out_sems = refs[13:]
        each = down_all.shape[0] // up_all.shape[0]
        stores = [
            pltpu.make_async_copy(up_all, more[0], out_sems.at[0]),
            pltpu.make_async_copy(down_all, more[1], out_sems.at[1]),
        ]

        def up_part(cols):
            return up_all[step, :, cols]

        def down_part(cols):
            return down_all[pl.ds(step * each, each), :, cols].reshape(width, sub)

    else:

        def up_part(cols):
            return weights[0][0, :, cols]

        def down_part(cols):
            return weights[1][:, :, cols].reshape(width, sub)

    @pl.when(step == 0)
    def _():
        if load:
            copies = load(weights, up_all, down_all, place_ref, sems)
        for m in range(rows // sub):
            at = slice(m * sub, (m + 1) * sub)
            inner = tok_ref[at].astype(F32) + (
                nn(ctx_ref[at], out_w_ref[0]) + vec_ref[OUT_BIAS : OUT_BIAS + 1]
            )
            unit, scale = norm_stats(inner)
            first = unit * vec_ref[ATTN_GAIN : ATTN_GAIN + 1] + vec_ref[ATTN_SHIFT : ATTN_SHIFT + 1]
            unit1_ref[at] = unit.astype(BF)
            scale1_ref[at] = scale
            low = first.astype(BF)
            low_ref[at] = low
            turned_ref[:, at] = low.T
            acc_ref[at] = first + vec_ref[DOWN_BIAS : DOWN_BIAS + 1]
        if load:
            for copy in copies:
                copy.wait()
            for store in stores:
                store.start()

    tiles = [(m, n) for m in range(rows // sub) for n in range(width // sub)]

    def rows_of(m):
        return slice(m * sub, (m + 1) * sub)

    def first_product(tile):
        return nn(low_ref[rows_of(tile[0])], up_part(rows_of(tile[1])))

    def second_product(m, n):
        at, cols = rows_of(m), rows_of(n)
        acc_ref[at, cols] += nn(line_ref[m % 2], down_part(cols))

    ahead = first_product(tiles[0])
    for index, (m, n) in enumerate(tiles):
        at, cols = rows_of(m), rows_of(n)
        hidden = ahead + up_b_ref[:, cols]
        if index + 1 < len(tiles):
            ahead = first_product(tiles[index + 1])
        if m > 0:
            second_product(m - 1, n)
        act, slope = gelu_parts(hidden)
        act = act.astype(BF)
        line_ref[m % 2, :, cols] = act
        act_ref[cols, at] = act.T
        slope_ref[at, cols] = slope.astype(BF)
    for n in range(width // sub):
        second_product(rows // sub - 1, n)

    @pl.when(step == last)
    def _():
        for seq in range(rows // length):
            at = slice(seq * length, (seq + 1) * length)
            active = (exit_ref[seq] >= LAYER).astype(F32)
            unit, scale = norm_stats(acc_ref[at])
            unit2_ref[at] = unit.astype(BF)
            scale2_ref[at] = scale
            result = (
                unit * vec_ref[BLOCK_GAIN : BLOCK_GAIN + 1] + vec_ref[BLOCK_SHIFT : BLOCK_SHIFT + 1]
            ) * active
            output_ref[at] = result.astype(BF)
        if load:
            for store in stores:
                store.wait()


def feed(place, exit_layer, tokens, ctx, out_w, vec, up_bias, weights, load, shapes, length):
    rows, width = tokens.shape
    hidden = up_bias.shape[1]
    steps = hidden // width
    whole = full((rows, width))
    if load:
        weight_specs = [pl.BlockSpec(memory_space=pl.ANY)] * len(weights)
        more_specs = [pl.BlockSpec(memory_space=pl.ANY)] * 2
        more = [jax.ShapeDtypeStruct(shape, BF) for shape in shapes]
        copies = 2 * shapes[1][0] * shapes[0][0]
        scratch = [pltpu.VMEM(shape, BF) for shape in shapes] + [
            pltpu.SemaphoreType.DMA((copies,)),
            pltpu.SemaphoreType.DMA((2,)),
        ]
    else:
        weight_specs = [
            pl.BlockSpec((1, width, width), lambda i: (i, 0, 0)),
            pl.BlockSpec((1, width, width), lambda i: (i, 0, 0)),
        ]
        more_specs, more, scratch = [], [], []
    return pl.pallas_call(
        functools.partial(feed_kernel, length, load, len(weights)),
        grid=(steps,),
        in_specs=[
            pl.BlockSpec(memory_space=pltpu.SMEM),
            pl.BlockSpec(memory_space=pltpu.SMEM),
            whole,
            whole,
            pl.BlockSpec((1, width, width), lambda i: (3, 0, 0)),
            full(vec.shape),
            pl.BlockSpec((1, width), lambda i: (0, i)),
        ]
        + weight_specs,
        out_specs=[
            full((width, rows)),
            pl.BlockSpec((width, rows), lambda i: (i, 0)),
            pl.BlockSpec((rows, width), lambda i: (0, i)),
            whole,
            full((rows, 1)),
            whole,
            full((rows, 1)),
            whole,
        ]
        + more_specs,
        out_shape=[
            jax.ShapeDtypeStruct((width, rows), BF),
            jax.ShapeDtypeStruct((hidden, rows), BF),
            jax.ShapeDtypeStruct((rows, hidden), BF),
            jax.ShapeDtypeStruct((rows, width), BF),
            jax.ShapeDtypeStruct((rows, 1), F32),
            jax.ShapeDtypeStruct((rows, width), BF),
            jax.ShapeDtypeStruct((rows, 1), F32),
            jax.ShapeDtypeStruct((rows, width), BF),
        ]
        + more,
        scratch_shapes=[
            pltpu.VMEM((rows, width), F32),
            pltpu.VMEM((rows, width), BF),
            pltpu.VMEM((2, 256, width), BF),
        ]
        + scratch,
        compiler_params=params(),
        cost_estimate=cost(18 * rows * width * width, 40 * rows * width, 8 * rows * width),
        name="feed",
    )(place, exit_layer, tokens, ctx, out_w, vec, up_bias, *weights)


def load_second(counts, chips, reps, part, weights, up_all, down_all, place_ref, sems):
    at = 0
    groups = []
    for number in counts:
        groups.append(weights[at : at + number])
        at += number
    copies = []

    def start(source, target):
        copies.append(pltpu.make_async_copy(source, target, sems.at[len(copies)]))
        copies[-1].start()

    second_plan(
        start,
        groups,
        (up_all, down_all),
        place_ref[0],
        place_ref[1],
        place_ref[2],
        chips,
        reps,
        part,
    )
    return copies


def leave_kernel(
    length,
    classes,
    exit_ref,
    output_ref,
    unit2_ref,
    scale2_ref,
    grad_ref,
    pool_ref,
    vec_ref,
    class_bias_ref,
    logit_grad_ref,
    act_ref,
    outer_ref,
    branch_ref,
    joint_grad_ref,
    sums_ref,
    class_grad_ref,
    logits_ref,
    stats_ref,
    lead_ref,
    pool_grad_ref,
):
    step = pl.program_id(0)
    rows, width = output_ref.shape
    pool = pool_ref[...].reshape(width, width)
    count = rows // length

    @pl.when(step == 0)
    def _():
        place = lax.broadcasted_iota(jnp.int32, (count, 1), 0)
        active = jnp.zeros((count, 1), F32)
        for seq in range(count):
            on = (exit_ref[seq] >= LAYER).astype(F32)
            active = jnp.where(place == seq, on, active)
        leading = jnp.concatenate(
            [output_ref[seq * length : seq * length + 1].astype(F32) for seq in range(count)],
            axis=0,
        ).astype(BF)
        pooled = jnp.tanh(nn(leading, pool) + vec_ref[POOL_BIAS : POOL_BIAS + 1])
        pooled_low = pooled.astype(BF)
        used = lax.broadcasted_iota(jnp.int32, (8, width), 0) < classes
        class_rows = jnp.where(used, vec_ref[CLASS_ROWS : CLASS_ROWS + 8], 0.0).astype(BF)
        raw = nt(pooled_low, class_rows) + class_bias_ref[...]
        lane = lax.broadcasted_iota(jnp.int32, raw.shape, 1) < classes
        top = jnp.max(jnp.where(lane, raw, -jnp.inf), axis=-1, keepdims=True)
        spread = jnp.where(lane, jnp.exp(raw - top), 0.0)
        logprob = raw - top - jnp.log(jnp.sum(spread, axis=-1, keepdims=True))
        entropy = -jnp.sum(
            jnp.where(lane, jnp.exp(logprob) * logprob, 0.0), axis=-1, keepdims=True
        )
        logits_ref[...] = raw * active
        class_grad = (logit_grad_ref[...].astype(F32) * active).astype(BF)
        stats_ref[0:1] = jnp.broadcast_to(jnp.sum(entropy * active, axis=0, keepdims=True), (1, 8))
        stats_ref[1:2] = jnp.sum(class_grad.astype(F32), axis=0, keepdims=True)
        class_grad_ref[...] = tn(class_grad, pooled_low)
        pooled_grad = nn(class_grad, class_rows)
        pre_grad = (pooled_grad * (1.0 - pooled * pooled)).astype(BF)
        sums_ref[3:4] = jnp.sum(pre_grad.astype(F32), axis=0, keepdims=True)
        pool_grad_ref[...] = tn(leading, pre_grad).reshape(pool_grad_ref.shape).astype(BF)
        lead_ref[...] = nt(pre_grad, pool)
        head = lax.broadcasted_iota(jnp.int32, (length, 1), 0) == 0
        gain = vec_ref[BLOCK_GAIN : BLOCK_GAIN + 1]
        gain_sum = jnp.zeros((1, width), F32)
        shift_sum = jnp.zeros((1, width), F32)
        bias_sum = jnp.zeros((1, width), F32)
        for seq in range(count):
            at = slice(seq * length, (seq + 1) * length)
            on = (exit_ref[seq] >= LAYER).astype(F32)
            top_grad = (
                grad_ref[at].astype(F32) + jnp.where(head, lead_ref[seq : seq + 1], 0.0)
            ) * on
            unit = unit2_ref[at].astype(F32)
            outer = norm_back(top_grad, unit, scale2_ref[at], gain)
            branch = outer.astype(BF)
            outer_ref[at] = outer
            branch_ref[at] = branch
            gain_sum += jnp.sum(top_grad * unit, axis=0, keepdims=True)
            shift_sum += jnp.sum(top_grad, axis=0, keepdims=True)
            bias_sum += jnp.sum(branch.astype(F32), axis=0, keepdims=True)
        sums_ref[0:1] = gain_sum
        sums_ref[1:2] = shift_sum
        sums_ref[2:3] = bias_sum

    @pl.when(step > 0)
    def _():
        few, both, _ = joint_grad_ref.shape
        deep = width // few
        value = nn(act_ref[...], branch_ref[...])
        for at in range(few):
            joint_grad_ref[at, 0:deep] = value[at * deep : (at + 1) * deep].astype(BF)
            joint_grad_ref[at, deep:both] = pool_grad_ref[(step - 1) * few + at]


def leave(
    exit_layer, output, unit2, scale2, output_grad, pool, vec, class_bias, logit_grad, act,
    pool_spec, shards, length, classes,
):
    rows, width = output.shape
    count = rows // length
    hidden = act.shape[0]
    steps = hidden // width
    few = shards // steps
    both = (hidden + width) // shards
    whole = full((rows, width))
    return pl.pallas_call(
        functools.partial(leave_kernel, length, classes),
        grid=(steps + 1,),
        in_specs=[
            pl.BlockSpec(memory_space=pltpu.SMEM),
            whole,
            whole,
            full((rows, 1)),
            whole,
            pool_spec,
            full(vec.shape),
            full(class_bias.shape),
            full(logit_grad.shape),
            pl.BlockSpec((width, rows), lambda i: (jnp.maximum(i - 1, 0), 0)),
        ],
        out_specs=[
            whole,
            whole,
            pl.BlockSpec((few, both, width), lambda i: (jnp.maximum(i - 1, 0), 0, 0)),
            full((4, width)),
            full((8, width)),
            full((count, 8)),
            full((2, 8)),
        ],
        out_shape=[
            jax.ShapeDtypeStruct((rows, width), F32),
            jax.ShapeDtypeStruct((rows, width), BF),
            jax.ShapeDtypeStruct((shards, both, width), BF),
            jax.ShapeDtypeStruct((4, width), F32),
            jax.ShapeDtypeStruct((8, width), F32),
            jax.ShapeDtypeStruct((count, 8), F32),
            jax.ShapeDtypeStruct((2, 8), F32),
        ],
        scratch_shapes=[
            pltpu.VMEM((count, width), F32),
            pltpu.VMEM((shards, width // shards, width), BF),
        ],
        compiler_params=params(),
        cost_estimate=cost(8 * rows * width * width, 30 * rows * width),
        name="leave",
    )(
        exit_layer, output, unit2, scale2, output_grad, pool, vec, class_bias, logit_grad, act
    )


def split_cores(value, place_ref, keep_ref, send_ref):
    chips, part, _ = keep_ref.shape
    first = place_ref[2] == 0
    for chip in range(chips):
        even = value[2 * chip * part : (2 * chip + 1) * part]
        odd = value[(2 * chip + 1) * part : (2 * chip + 2) * part]
        keep_ref[chip] = jnp.where(first, even, odd).astype(BF)
        send_ref[chip] = jnp.where(first, odd, even).astype(BF)


def feed_back_kernel(
    place_ref,
    branch_ref,
    slope_ref,
    turned_ref,
    down_ref,
    up_ref,
    outer_ref,
    unit1_ref,
    scale1_ref,
    out_w_ref,
    vec_ref,
    ctx_ref,
    keep_ref,
    send_ref,
    up_sum_ref,
    inner_ref,
    attended_ref,
    ctx_grad_ref,
    sums_ref,
    acc_ref,
    hid_ref,
):
    step = pl.program_id(0)
    rows, width = branch_ref.shape
    sub = 512

    @pl.when(step == 0)
    def _():
        acc_ref[...] = outer_ref[...]

    last = pl.num_programs(0) - 1

    @pl.when(step < last)
    def _():
        total = jnp.zeros((1, width), F32)
        down = down_ref[...].reshape(up_ref.shape[1:])
        ahead = nt(branch_ref[0:sub], down)
        for m in range(rows // sub):
            at = slice(m * sub, (m + 1) * sub)
            hid = (ahead * slope_ref[at].astype(F32)).astype(BF)
            if (m + 1) * sub < rows:
                ahead = nt(branch_ref[(m + 1) * sub : (m + 2) * sub], down)
            hid_ref[at] = hid
            total += jnp.sum(hid.astype(F32), axis=0, keepdims=True)
            acc_ref[at] += nt(hid, up_ref[0])
        up_sum_ref[...] = total
        split_cores(nn(turned_ref[...], hid_ref[...]), place_ref, keep_ref, send_ref)

    @pl.when(step == last)
    def _():
        gain = vec_ref[ATTN_GAIN : ATTN_GAIN + 1]
        gain_sum = jnp.zeros((1, width), F32)
        shift_sum = jnp.zeros((1, width), F32)
        bias_sum = jnp.zeros((1, width), F32)
        for m in range(rows // sub):
            at = slice(m * sub, (m + 1) * sub)
            grad = acc_ref[at]
            unit = unit1_ref[at].astype(F32)
            inner = norm_back(grad, unit, scale1_ref[at], gain)
            attended = inner.astype(BF)
            inner_ref[at] = inner
            attended_ref[at] = attended
            ctx_grad_ref[at] = nt(attended, out_w_ref[0]).astype(BF)
            gain_sum += jnp.sum(grad * unit, axis=0, keepdims=True)
            shift_sum += jnp.sum(grad, axis=0, keepdims=True)
            bias_sum += jnp.sum(attended.astype(F32), axis=0, keepdims=True)
        sums_ref[0:1] = gain_sum
        sums_ref[1:2] = shift_sum
        sums_ref[2:3] = bias_sum
        split_cores(tn(ctx_ref[...], attended_ref[...]), place_ref, keep_ref, send_ref)


def feed_back(place, chips, branch, slope, low, down, down_block, up, outer, unit1, scale1, out_w, vec, ctx):
    rows, width = branch.shape
    hidden = slope.shape[1]
    steps = hidden // width
    whole = full((rows, width))
    end = steps - 1
    part = width // (2 * chips)
    return pl.pallas_call(
        feed_back_kernel,
        grid=(steps + 1,),
        in_specs=[
            pl.BlockSpec(memory_space=pltpu.SMEM),
            whole,
            pl.BlockSpec((rows, width), lambda i: (0, jnp.minimum(i, end))),
            full((width, rows)),
            pl.BlockSpec(down_block, lambda i: (jnp.minimum(i, end), 0, 0)),
            pl.BlockSpec((1, width, width), lambda i: (jnp.minimum(i, end), 0, 0)),
            whole,
            whole,
            full((rows, 1)),
            pl.BlockSpec((1, width, width), lambda i: (3, 0, 0)),
            full(vec.shape),
            whole,
        ],
        out_specs=[
            pl.BlockSpec((chips, part, width), lambda i: (0, 0, i)),
            pl.BlockSpec((chips, part, width), lambda i: (0, 0, i)),
            pl.BlockSpec((1, width), lambda i: (0, jnp.minimum(i, end))),
            whole,
            whole,
            whole,
            full((3, width)),
        ],
        out_shape=[
            jax.ShapeDtypeStruct((chips, part, hidden + width), BF),
            jax.ShapeDtypeStruct((chips, part, hidden + width), BF),
            jax.ShapeDtypeStruct((1, hidden), F32),
            jax.ShapeDtypeStruct((rows, width), F32),
            jax.ShapeDtypeStruct((rows, width), BF),
            jax.ShapeDtypeStruct((rows, width), BF),
            jax.ShapeDtypeStruct((3, width), F32),
        ],
        scratch_shapes=[pltpu.VMEM((rows, width), F32), pltpu.VMEM((rows, width), BF)],
        compiler_params=params(),
        cost_estimate=cost(28 * rows * width * width, 40 * rows * width),
        name="feed_back",
    )(place, branch, slope, low, down, up, outer, unit1, scale1, out_w, vec, ctx)


def attend_back_kernel(length, joined_ref, probs_ref, ctx_grad_ref, grad_ref, sum_ref):
    rows, width = ctx_grad_ref.shape
    pairs = width // PAIR

    def one(seq, carry):
        at = pl.ds(pl.multiple_of(seq * length, length), length)

        def columns(part, pair):
            return slice(part * width + pair * PAIR, part * width + (pair + 1) * PAIR)

        prob_grads = []
        for pair in range(pairs):
            vals = split_heads(joined_ref[at, columns(2, pair)])
            prob_grads.append(nt(vals, ctx_grad_ref[at, columns(0, pair)]))
        score_grads = []
        for pair in range(pairs):
            probs = probs_ref[seq, pair]
            halves = []
            for head in range(2):
                cut = slice(head * length, (head + 1) * length)
                held = probs[cut].astype(F32)
                part = prob_grads[pair][cut]
                base = jnp.sum(part * held, axis=0, keepdims=True)
                halves.append((held * (part - base)).astype(BF))
            score_grads.append(halves)
        for pair in range(pairs):
            probs = probs_ref[seq, pair]
            beside = jnp.concatenate([probs[:length], probs[length:]], axis=1)
            ctx_grads = split_heads(ctx_grad_ref[at, columns(0, pair)])
            grad_ref[at, columns(2, pair)] = nn(beside, ctx_grads).astype(BF)
        for pair in range(pairs):
            queries = split_heads(joined_ref[at, columns(0, pair)] * jnp.asarray(0.125, BF))
            beside = jnp.concatenate(score_grads[pair], axis=1)
            grad_ref[at, columns(1, pair)] = nn(beside, queries).astype(BF)
        for pair in range(pairs):
            keys = split_heads(joined_ref[at, columns(1, pair)])
            stacked = jnp.concatenate(score_grads[pair], axis=0)
            grad_ref[at, columns(0, pair)] = (tn(stacked, keys) * 0.125).astype(BF)
        return carry

    lax.fori_loop(0, rows // length, one, 0)
    total = jnp.zeros(sum_ref.shape, F32)
    for m in range(rows // length):
        total += jnp.sum(
            grad_ref[m * length : (m + 1) * length].astype(F32), axis=0, keepdims=True
        )

    @pl.when(pl.program_id(0) == 0)
    def _():
        sum_ref[...] = total

    @pl.when(pl.program_id(0) > 0)
    def _():
        sum_ref[...] += total


def attend_back(joined, probs, ctx_grad, length):
    rows, width = ctx_grad.shape
    count = rows // length
    steps = 2
    block = rows // steps
    pairs = width // PAIR
    return pl.pallas_call(
        functools.partial(attend_back_kernel, length),
        grid=(steps,),
        in_specs=[
            pl.BlockSpec((block, 3 * width), lambda i: (i, 0)),
            pl.BlockSpec((count // steps, pairs, 2 * length, length), lambda i: (i, 0, 0, 0)),
            pl.BlockSpec((block, width), lambda i: (i, 0)),
        ],
        out_specs=[
            pl.BlockSpec((block, 3 * width), lambda i: (i, 0)),
            full((1, 3 * width)),
        ],
        out_shape=[
            jax.ShapeDtypeStruct((rows, 3 * width), BF),
            jax.ShapeDtypeStruct((1, 3 * width), F32),
        ],
        compiler_params=params(),
        cost_estimate=cost(rows * width, rows * width),
        name="attend_back",
    )(joined, probs, ctx_grad)


def weight_grads_kernel(tok_ref, joined_ref, small_ref, out_ref, turned_ref):
    step = pl.program_id(0)
    last = pl.num_programs(0) - 1
    shards, part, width = out_ref.shape

    @pl.when(step == 0)
    def _():
        turned_ref[...] = tok_ref[...].T

    value = nn(turned_ref[...], joined_ref[...])
    cols = pl.ds(pl.multiple_of(step * joined_ref.shape[1], joined_ref.shape[1]), joined_ref.shape[1])
    out_ref[:, :, cols] = value.reshape(shards, part, joined_ref.shape[1]).astype(BF)
    tail = 3 * joined_ref.shape[1]
    if width > tail:

        @pl.when(step == last)
        def _():
            lines = small_ref.shape[1]
            out_ref[:, lines:part, tail:width] = jnp.zeros(
                (shards, part - lines, width - tail), BF
            )
            out_ref[:, 0:lines, tail:width] = small_ref[...].astype(BF)


def weight_grads(tokens, joined_grad, small, shards, extra):
    rows, width = tokens.shape
    shape = (shards, width // shards, 3 * width + extra)
    return pl.pallas_call(
        weight_grads_kernel,
        grid=(3,),
        in_specs=[
            full((rows, width)),
            pl.BlockSpec((rows, width), lambda i: (0, i)),
            full(small.shape),
        ],
        out_specs=full(shape),
        out_shape=jax.ShapeDtypeStruct(shape, BF),
        scratch_shapes=[pltpu.VMEM((width, rows), BF)],
        compiler_params=params(),
        cost_estimate=cost(rows * width, rows * width),
        name="weight_grads",
    )(tokens, joined_grad, small)


def input_kernel(inner_ref, joined_ref, w_ref, out_ref):
    width = inner_ref.shape[1]
    total = inner_ref[...]
    for part in range(3):
        total += nt(joined_ref[:, part * width : (part + 1) * width], w_ref[part])
    out_ref[...] = total.astype(BF)


def input_back(inner, joined_grad, qkv):
    rows, width = inner.shape
    steps = 4
    block = rows // steps
    return pl.pallas_call(
        input_kernel,
        grid=(steps,),
        in_specs=[
            pl.BlockSpec((block, width), lambda i: (i, 0)),
            pl.BlockSpec((block, 3 * width), lambda i: (i, 0)),
            full((3, width, width)),
        ],
        out_specs=pl.BlockSpec((block, width), lambda i: (i, 0)),
        out_shape=jax.ShapeDtypeStruct((rows, width), BF),
        compiler_params=params(),
        cost_estimate=cost(rows * width, rows * width),
        name="input_back",
    )(inner, joined_grad, qkv)


def lay_kernel(plan, chips, reps, part, counts, place_ref, *refs):
    at = 0
    groups = []
    for number in counts:
        groups.append(refs[at : at + number])
        at += number
    sems = refs[-1]
    rep, chip, core = place_ref[0], place_ref[1], place_ref[2]
    copies = []

    def start(source, target):
        copies.append(pltpu.make_async_copy(source, target, sems.at[len(copies)]))
        copies[-1].start()

    finish = plan(start, groups, refs[at:-1], rep, chip, core, chips, reps, part)
    for copy in copies:
        copy.wait()
    if finish is not None:
        finish()


def blocks_plan(
    put, own, twin, along, across, swapped, depth, first, rep, chip, core, chips, reps, part
):
    for block in range(reps):
        put(own(block), block, chip, core)
        put(twin(block), block, chip, 1 - core)
    for step in range(1, chips):
        source = lax.rem(chip + chips - step, chips)
        rows = pl.ds((step - 1) * depth + first, part)
        for other, block in along.items():
            put(block(step, source, 0), rep ^ other, source, core)
            put(block(step, source, 1), rep ^ other, source, 1 - core)
        for other in across:
            put(across[other].at[rows], rep ^ other, source, core)
            put(swapped[other].at[rows], rep ^ other, source, 1 - core)


def wide_put(start, out_ref, part):
    def put(source, block, at_chip, at_core):
        row = pl.multiple_of((at_chip * 2 + at_core) * part, part)
        start(source, out_ref.at[block, pl.ds(row, part)])

    return put


def wide_block(ref, width, part):
    return lambda block: ref.at[pl.ds(0, part), pl.ds(block * width, width)]


def first_plan(start, groups, outs, rep, chip, core, chips, reps, part):
    (own, twin), along, across, swapped, (extra,) = groups
    out_ref, vec_ref, more_ref = outs
    width = out_ref.shape[2]

    def near(step, source, side):
        if side == 0:
            return along[step - 1].at[pl.ds(0, part)]
        return swapped[0].at[pl.ds((step - 1) * part, part)]

    blocks_plan(
        wide_put(start, out_ref, part),
        wide_block(own, width, part),
        wide_block(twin, width, part),
        {0: near},
        {at + 1: ref for at, ref in enumerate(across)},
        {at + 1: ref for at, ref in enumerate(swapped[1:])},
        part,
        0,
        rep,
        chip,
        core,
        chips,
        reps,
        part,
    )
    tail = pl.ds(part, 16)
    cols = pl.ds(0, width)
    start(own.at[tail, cols], more_ref.at[chip * 2 + core])
    start(twin.at[tail, cols], more_ref.at[chip * 2 + 1 - core])
    for step in range(1, chips):
        source = lax.rem(chip + chips - step, chips)
        start(along[step - 1].at[tail], more_ref.at[source * 2 + core])
        start(extra.at[pl.ds((step - 1) * 16, 16)], more_ref.at[source * 2 + 1 - core])

    def finish():
        lane = lax.broadcasted_iota(jnp.int32, (LANES, width), 0)
        place = lax.broadcasted_iota(jnp.int32, (LANES, width), 1)
        total = jnp.zeros((16, width), F32)
        for shard in range(2 * chips):
            there = (place - shard * part == lane) & (lane < part)
            total += nn(more_ref[shard, :, 0:LANES], there.astype(F32).astype(BF))
        vec_ref[...] = total

    return finish


def second_plan(start, groups, outs, rep, chip, core, chips, reps, part):
    (up, up_twin, down, down_twin), (close, far), across, swapped = groups
    up_ref, down_ref = outs
    width = up_ref.shape[2]
    where = (rep, chip, core, chips, reps, part)

    def chained(chain, first):
        def block(step, source, side):
            shard = source * 2 + (core if side == 0 else 1 - core)
            return chain.at[shard, pl.ds(first, part)]

        return block

    across = dict(zip(NEAR, across))
    swapped = dict(zip(NEAR, swapped))
    blocks_plan(
        wide_put(start, up_ref, part),
        wide_block(up, width, part),
        wide_block(up_twin, width, part),
        {0: chained(close, 0), FAR: chained(far, 0)},
        across,
        swapped,
        2 * part,
        0,
        *where,
    )

    def put(source, block, at_chip, at_core):
        row = pl.multiple_of(block * part, part)
        start(source, down_ref.at[at_chip * 2 + at_core, pl.ds(row, part)])

    def tall(ref):
        return lambda block: ref.at[pl.ds(block * part, part)]

    blocks_plan(
        put,
        tall(down),
        tall(down_twin),
        {0: chained(close, part), FAR: chained(far, part)},
        across,
        swapped,
        2 * part,
        part,
        *where,
    )


def lay(plan, place, groups, shapes, scratch, copies, part, chips, reps):
    anywhere = pl.BlockSpec(memory_space=pl.ANY)
    inputs = [ref for group in groups for ref in group]
    return pl.pallas_call(
        functools.partial(
            lay_kernel, plan, chips, reps, part, [len(group) for group in groups]
        ),
        in_specs=[pl.BlockSpec(memory_space=pltpu.SMEM)] + [anywhere] * len(inputs),
        out_specs=[pl.BlockSpec(memory_space=pltpu.VMEM)] * len(shapes),
        out_shape=[jax.ShapeDtypeStruct(shape, kind) for shape, kind in shapes],
        scratch_shapes=[pltpu.VMEM(shape, BF) for shape in scratch]
        + [pltpu.SemaphoreType.DMA((copies,))],
        compiler_params=pltpu.CompilerParams(vmem_limit_bytes=VMEM_BYTES),
        cost_estimate=cost(0, 4 * sum(math.prod(shape) for shape, kind in shapes)),
        name="lay",
    )(place, *inputs)


def pack_vectors(rows, up_bias, class_weight):
    part = rows[0].shape[0]
    lines = [row[None] for row in rows[:8]] + [class_weight.T] + [row[None] for row in rows[8:]]
    pieces = up_bias.shape[0] // part
    lines += [up_bias[None, at * part : (at + 1) * part] for at in range(pieces)]
    return jnp.concatenate(lines, axis=0)


def move(values, reps, chips, target):
    pairs = []
    for rep in range(reps):
        for chip in range(chips):
            for core in range(2):
                to_rep, to_chip, to_core = target(rep, chip, core)
                pairs.append(
                    (
                        (rep * chips + chip) * 2 + core,
                        (to_rep * chips + to_chip) * 2 + to_core,
                    )
                )
    return lax.ppermute(values, ("rep", "fsdp"), pairs)


def along_chips(step, chips):
    return lambda rep, chip, core: (rep, (chip + step) % chips, core)


def across_reps(other):
    return lambda rep, chip, core: (rep ^ other, chip, core)


def to_twin(rep, chip, core):
    return rep, chip, 1 - core


def after(values, *gates):
    return lax.optimization_barrier((values, *gates))[0]


def along_z(mine, reps, chips):
    return [move(mine, reps, chips, along_chips(step, chips)) for step in range(1, chips)]


def over_reps(stacked, reps, chips, others):
    return [move(stacked, reps, chips, across_reps(other)) for other in others]


def pick(parts, at):
    return lax.dynamic_index_in_dim(parts, at, axis=0, keepdims=False)


def in_order(rep, reps, own, others, axis):
    blocks = jnp.stack([own] + others)
    return jnp.concatenate([pick(blocks, rep ^ at) for at in range(reps)], axis=axis)


class Reduction:
    def __init__(self, place, keep, send, reps, chips):
        self.rep, self.chip = place[0], place[1]
        self.reps, self.chips = reps, chips
        self.keep = keep
        self.got = move(send, reps, chips, to_twin)

    def at_rep(self, at):
        return lax.dynamic_index_in_dim(self.both, at, axis=1, keepdims=False)

    def over_reps(self):
        chips, rows, width = self.keep.shape
        both = (self.keep.astype(F32) + self.got.astype(F32)).astype(BF)
        self.both = lax.optimization_barrier(both).reshape(
            chips, self.reps, rows // self.reps, width
        )
        self.arrived = [
            move(self.at_rep(self.rep ^ other), self.reps, self.chips, across_reps(other))
            for other in range(1, self.reps)
        ]

    def over_chips(self, *gates):
        if gates:
            self.arrived = [after(block, *gates) for block in self.arrived]
        total = self.at_rep(self.rep).astype(F32)
        for block in self.arrived:
            total = total + block.astype(F32)
        self.total = pick(total, self.chip)
        self.passed = [
            move(
                pick(total, lax.rem(self.chip + step, self.chips)).astype(BF),
                self.reps,
                self.chips,
                along_chips(step, self.chips),
            )
            for step in range(1, self.chips)
        ]

    def chip_sum(self):
        total = self.total
        for block in self.passed:
            total = total + block.astype(F32)
        return total.astype(BF)


def share_reps(place, total, reps, chips):
    others = [move(total, reps, chips, across_reps(other)) for other in range(1, reps)]
    return in_order(place[0], reps, total, others, 0).astype(F32), others


def exchange_reps(place, rows, reps, chips):
    rep = place[0]
    parts = rows.reshape(reps, -1, rows.shape[1])
    total = pick(parts, rep).astype(F32)
    arrived = [
        move(pick(parts, rep ^ other), reps, chips, across_reps(other))
        for other in range(1, reps)
    ]
    for block in arrived:
        total = total + block.astype(F32)
    return total.astype(BF), arrived


def per_device(
    tokens,
    exit_layer,
    qkv_weight,
    query_bias,
    value_bias,
    out_weight,
    out_bias,
    attn_gain,
    attn_shift,
    up_weight,
    up_bias,
    down_weight,
    down_bias,
    block_gain,
    block_shift,
    pool_weight,
    pool_bias,
    class_weight,
    class_bias,
    output_grad,
    logit_grad,
):
    reps = lax.axis_size("rep")
    shards = lax.axis_size("fsdp")
    mine = lax.axis_index("fsdp")
    rows, width = tokens.shape
    count = exit_layer.shape[0]
    length = rows // count
    classes = class_weight.shape[1]
    part = out_weight.shape[0]
    hidden = up_weight.shape[1]

    def gather(shard):
        return lax.all_gather(shard, "fsdp", axis=0, tiled=True)

    packed = pack_vectors(
        [
            query_bias,
            value_bias,
            out_bias,
            attn_gain,
            attn_shift,
            down_bias,
            block_gain,
            block_shift,
            pool_bias,
        ],
        up_bias,
        class_weight,
    )
    joint_own = jnp.concatenate([qkv_weight, out_weight], axis=1)
    deep = down_weight.shape[0]
    chips = shards // 2
    place = jnp.stack([lax.axis_index("rep"), mine // 2, mine % 2]).astype(jnp.int32)
    direct = (
        part % 16 == 0
        and reps & (reps - 1) == 0
        and reps * width == hidden
        and reps == 4
        and packed.shape[0] <= 16
    )
    if direct:
        lines = packed.shape[0]
        held = jnp.pad(packed, ((0, 16 - lines), (0, width - part)))
        own = jnp.concatenate([joint_own, jnp.tile(held, (1, reps))], axis=0)
        rep = place[0]

        def block_of(weights, at):
            return lax.dynamic_slice_in_dim(weights, at * width, width, axis=1)

        def second_of(at):
            return [
                block_of(up_weight, at),
                lax.dynamic_slice_in_dim(down_weight, at * part, part, axis=0),
            ]

        along = along_z(block_of(own, rep), reps, chips)
        chain = gather(after(jnp.concatenate(second_of(rep), axis=0), *along))
        chain = chain.reshape(chips, 2, 2 * part, width)
        twin = move(own, reps, chips, to_twin)
        stacked = jnp.concatenate([rows_[:part] for rows_ in along], axis=0)
        across = over_reps(stacked, reps, chips, range(1, reps))
        far_chain = gather(after(jnp.concatenate(second_of(rep ^ FAR), axis=0), *across))
        swapped = [move(rows_, reps, chips, to_twin) for rows_ in [stacked] + across]
        extra = move(
            jnp.concatenate([rows_[part:] for rows_ in along], axis=0), reps, chips, to_twin
        )
        up_twin = move(up_weight, reps, chips, to_twin)
        down_twin = move(down_weight, reps, chips, to_twin)
        joint, vec = lay(
            first_plan,
            place,
            [
                [own, twin],
                along,
                across,
                swapped,
                [extra],
            ],
            [((reps, width, width), BF), ((16, width), F32)],
            [(shards, 16, width)],
            2 * chips * (reps + 1),
            part,
            chips,
            reps,
        )
        mine_chain = lax.dynamic_index_in_dim(
            after(chain, joint), place[2], axis=1, keepdims=False
        )
        second_stacked = jnp.concatenate(
            [
                pick(mine_chain, lax.rem(place[1] + chips - step, chips))
                for step in range(1, chips)
            ],
            axis=0,
        )
        second_across = over_reps(after(second_stacked, *across), reps, chips, NEAR)
        up_row = (
            vec[VECTOR_ROWS:lines].reshape(-1, shards, part).transpose(1, 0, 2).reshape(1, hidden)
        )
        down_block = (width // deep, deep, width)
    else:
        small = gather(packed[None])
        vec = small[:, :VECTOR_ROWS].transpose(1, 0, 2).reshape(VECTOR_ROWS, width).astype(F32)
        vec = jnp.pad(vec, ((0, 16 - VECTOR_ROWS), (0, 0)))
        up_row = small[:, VECTOR_ROWS:].transpose(0, 1, 2).reshape(1, hidden).astype(F32)
        pool = gather(pool_weight)
        joint = jnp.stack(jnp.split(gather(joint_own), 4, axis=1))
        up = jnp.stack(jnp.split(gather(up_weight), hidden // width, axis=1))
        down = gather(down_weight).reshape(-1, width, width)
        down_block = (1, width, width)
    joined, probs, ctx = attend(tokens, joint, vec, length)
    if direct:
        pool = gather(after(pool_weight, ctx))
        far_chain = after(far_chain, ctx)
        second_swapped = [
            move(after(rows_, ctx), reps, chips, to_twin) for rows_ in second_across
        ]
        groups = [
            [up_weight, up_twin, down_weight, down_twin],
            [
                chain.reshape(shards, 2 * part, width),
                far_chain.reshape(shards, 2 * part, width),
            ],
            second_across,
            second_swapped,
        ]
        weights = [ref for group in groups for ref in group]
        load = functools.partial(load_second, [len(group) for group in groups], chips, reps, part)
        shapes = [(reps, width, width), (shards, deep, width)]
    else:
        weights, load, shapes = [up, down], None, None
    turned, act, slope, unit1, scale1, unit2, scale2, output, *laid = feed(
        place, exit_layer, tokens, ctx, joint, vec, up_row, weights, load, shapes, length
    )
    if direct:
        up, down = laid
    class_bias_row = jnp.pad(class_bias.astype(F32), (0, 8 - classes))[None]
    logit_grad_rows = jnp.pad(logit_grad, ((0, 0), (0, 8 - classes)))
    outer, branch, low_grad, exit_sums, class_grad, logits, stats = leave(
        exit_layer,
        output,
        unit2,
        scale2,
        output_grad,
        pool,
        vec,
        class_bias_row,
        logit_grad_rows,
        act,
        full((width, width)),
        shards,
        length,
        classes,
    )
    def scatter(grad):
        return lax.psum_scatter(grad, "fsdp", scatter_dimension=0, tiled=True)

    low_part = scatter(low_grad.reshape(-1, width))
    up_keep, up_send, up_sum, inner, attended, ctx_grad, feed_sums = feed_back(
        place, chips, branch, slope, turned, down, down_block, up, outer, unit1, scale1, joint, vec, ctx
    )
    if direct:
        up_red = Reduction(place, up_keep, up_send, reps, chips)
        up_red.over_reps()
        ctx_grad = after(ctx_grad, up_red.both)
    joined_grad, joined_sum = attend_back(joined, probs, ctx_grad, length)
    joined_seen = joined_grad
    if direct:
        inner = after(inner, joined_grad)
    sums = jnp.concatenate(
        [
            joined_sum.reshape(3, width)[::2],
            feed_sums,
            exit_sums,
            class_grad[:classes],
        ],
        axis=0,
    )
    lines = sums.shape[0]
    own_sums = sums.reshape(lines, shards, part).transpose(1, 0, 2).reshape(shards, lines * part)
    own_sums = jnp.concatenate([own_sums, up_sum.reshape(shards, deep)], axis=1)
    used = own_sums.shape[1]
    seqs_total = count * reps * shards
    figures = jnp.concatenate([stats[0, :1], stats[1, :classes]])
    slots = reps * shards * figures.shape[0] * 3
    direct = direct and used + slots <= part * LANES
    small_lines = 16
    if direct:
        high = figures.astype(BF).astype(F32)
        middle = (figures - high).astype(BF).astype(F32)
        lowest = figures - high - middle
        split = jnp.concatenate([high, middle, lowest])
        slot = lax.axis_index("rep") * shards + mine
        lone = jnp.where(
            jnp.arange(reps * shards)[:, None] == slot, split[None], 0.0
        ).reshape(1, slots)
        row = jnp.concatenate([own_sums, jnp.broadcast_to(lone, (shards, slots))], axis=1)
        small_lines = -(-row.shape[1] // (LANES * 16)) * 16
        row = jnp.pad(row, ((0, 0), (0, small_lines * LANES - row.shape[1])))
        row = row.reshape(shards, small_lines, LANES)
    else:
        row = jnp.zeros((shards, small_lines, LANES), F32)
    joint_grad = weight_grads(tokens, joined_seen, row, shards, LANES if direct else 0)
    input_grad = input_back(inner, joined_grad, joint)

    if direct:
        joint_grad = after(joint_grad, low_part)
    joint_part = scatter(joint_grad.reshape(width, -1))
    if direct:
        low_total, low_arrived = exchange_reps(
            place, after(low_part, joint_grad, *up_red.arrived), reps, chips
        )
        up_red.over_chips(*low_arrived)
        wide = (deep + part) * width // part
        up_total = up_red.chip_sum()
        columns = up_total.shape[1]
        pair, pair_others = share_reps(
            place,
            jnp.concatenate([up_total, low_total.reshape(-1, wide)], axis=1),
            reps,
            chips,
        )
        up_sum = pair[:, :columns]
        low_sum = pair[:, columns:].reshape(deep + part, width)
        joint_total, _ = exchange_reps(
            place, after(joint_part, *pair_others), reps, chips
        )
        joint_sum, _ = share_reps(place, joint_total, reps, chips)
        small_sum = joint_sum[:small_lines, 3 * width :].reshape(-1)
        total = small_sum[used : used + slots].reshape(-1, figures.shape[0]).sum(axis=0)
    else:
        first = mine % 2 == 0

        def whole_of(kept, sent):
            pair = jnp.stack([jnp.where(first, kept, sent), jnp.where(first, sent, kept)], axis=1)
            return pair.reshape(-1, kept.shape[2])

        joint_sum, low_sum, up_sum = lax.psum(
            (joint_part, low_part, scatter(whole_of(up_keep, up_send))), "rep"
        )
        joint_sum, low_sum, up_sum = (
            joint_sum.astype(F32),
            low_sum.astype(F32),
            up_sum.astype(F32),
        )
        own_sums, total = lax.psum((own_sums, figures), ("rep", "fsdp"))
        small_sum = pick(own_sums, mine)
    own = small_sum[: lines * part].reshape(lines, part)
    return (
        output,
        logits[:, :classes],
        total[0] / seqs_total,
        input_grad,
        joint_sum[:, : 3 * width],
        own[0],
        own[1],
        up_sum[:, hidden:],
        own[4],
        own[2],
        own[3],
        up_sum[:, :hidden],
        small_sum[lines * part : used],
        low_sum[:deep],
        own[7],
        own[5],
        own[6],
        low_sum[deep:],
        own[8],
        own[9 : 9 + classes].T,
        total[1:],
    )


def solution(mesh):
    return jax.shard_map(
        per_device,
        mesh=mesh,
        in_specs=(
            P(("rep", "fsdp"), None),
            P(("rep", "fsdp")),
            P("fsdp", None),
            P("fsdp"),
            P("fsdp"),
            P("fsdp", None),
            P("fsdp"),
            P("fsdp"),
            P("fsdp"),
            P("fsdp", None),
            P("fsdp"),
            P("fsdp", None),
            P("fsdp"),
            P("fsdp"),
            P("fsdp"),
            P("fsdp", None),
            P("fsdp"),
            P("fsdp", None),
            P(),
            P(("rep", "fsdp"), None),
            P(("rep", "fsdp"), None),
        ),
        out_specs=(
            P(("rep", "fsdp"), None),
            P(("rep", "fsdp"), None),
            P(),
            P(("rep", "fsdp"), None),
            P("fsdp", None),
            P("fsdp"),
            P("fsdp"),
            P("fsdp", None),
            P("fsdp"),
            P("fsdp"),
            P("fsdp"),
            P("fsdp", None),
            P("fsdp"),
            P("fsdp", None),
            P("fsdp"),
            P("fsdp"),
            P("fsdp"),
            P("fsdp", None),
            P("fsdp"),
            P("fsdp", None),
            P(),
        ),
        check_vma=False,
    )
```

```python
import functools
import math

import jax
import jax.numpy as jnp
from jax import lax
from jax.experimental import pallas as pl
from jax.experimental.pallas import tpu as pltpu
from jax.sharding import PartitionSpec as P

HD = 64
LAYER = 6
PAIR = 2 * HD
NEAR = (1, 2)
FAR = 3
LANES = 128
VMEM_BYTES = 58 * 2**20
BF = jnp.bfloat16
F32 = jnp.float32

QUERY_BIAS, VALUE_BIAS, OUT_BIAS, ATTN_GAIN, ATTN_SHIFT = 0, 1, 2, 3, 4
DOWN_BIAS, BLOCK_GAIN, BLOCK_SHIFT, CLASS_ROWS, POOL_BIAS = 5, 6, 7, 8, 11
VECTOR_ROWS = 12


def nn(left, right):
    return jnp.dot(left, right, preferred_element_type=F32)


def tn(left, right):
    return lax.dot_general(left, right, (((0,), (0,)), ((), ())), preferred_element_type=F32)


def nt(left, right):
    return lax.dot_general(left, right, (((1,), (1,)), ((), ())), preferred_element_type=F32)


def full(shape):
    return pl.BlockSpec(shape, lambda *at: (0,) * len(shape))


def params():
    return pltpu.CompilerParams(
        dimension_semantics=("arbitrary",), vmem_limit_bytes=VMEM_BYTES
    )


def cost(flops, moved, trans=0):
    return pl.CostEstimate(flops=flops, bytes_accessed=moved, transcendentals=trans)


def split_heads(pair):
    lane = lax.broadcasted_iota(jnp.int32, pair.shape, 1)
    zero = jnp.zeros_like(pair)
    return jnp.concatenate(
        [jnp.where(lane < HD, pair, zero), jnp.where(lane < HD, zero, pair)], axis=0
    )


def norm_stats(values):
    center = values - jnp.mean(values, axis=-1, keepdims=True)
    spread = jnp.mean(center * center, axis=-1, keepdims=True)
    scale = lax.rsqrt(spread + 1e-06)
    return center * scale, scale


def norm_back(grad, unit, scale, gain):
    inner = grad * gain
    first = jnp.mean(inner, axis=-1, keepdims=True)
    second = jnp.mean(inner * unit, axis=-1, keepdims=True)
    return scale * (inner - first - unit * second)


def gelu_parts(values):
    base = 1.0 + 0.23164189 * jnp.abs(values)
    t = pl.reciprocal(base, approx=True)
    t = t * (2.0 - base * t)
    bell = jnp.exp2((values * values) * -0.7213475204444817)
    poly = t * (
        0.127414796
        + t * (-0.142248368 + t * (0.7107068705 + t * (-0.7265760135 + t * 0.5307027145)))
    )
    tail = poly * bell
    below = jnp.where(values >= 0.0, 1.0 - tail, tail)
    return values * below, below + values * (bell * 0.3989422804014327)


def attend_kernel(length, tok_ref, w_ref, vec_ref, joined_ref, probs_ref, ctx_ref):
    rows, width = ctx_ref.shape
    pairs = width // PAIR
    for part in range(3):
        cols = slice(part * width, (part + 1) * width)
        value = nn(tok_ref[...], w_ref[part])
        if part == 0:
            value += vec_ref[QUERY_BIAS : QUERY_BIAS + 1]
        elif part == 2:
            value += vec_ref[VALUE_BIAS : VALUE_BIAS + 1]
        joined_ref[:, cols] = value.astype(BF)

    def one(seq, carry):
        at = pl.ds(pl.multiple_of(seq * length, length), length)
        scores = []
        for pair in range(pairs):
            query = joined_ref[at, pair * PAIR : (pair + 1) * PAIR] * jnp.asarray(0.125, BF)
            keys = split_heads(joined_ref[at, width + pair * PAIR : width + (pair + 1) * PAIR])
            scores.append(nt(keys, query))
        all_probs = []
        for pair in range(pairs):
            halves = []
            for head in range(2):
                part = scores[pair][head * length : (head + 1) * length]
                part = jnp.exp(part - jnp.max(part, axis=0, keepdims=True))
                part = part * (1.0 / jnp.sum(part, axis=0, keepdims=True))
                halves.append(part.astype(BF))
            probs = jnp.concatenate(halves, axis=0)
            probs_ref[seq, pair] = probs
            all_probs.append(probs)
        for pair in range(pairs):
            vals = split_heads(
                joined_ref[at, 2 * width + pair * PAIR : 2 * width + (pair + 1) * PAIR]
            )
            ctx_ref[at, pair * PAIR : (pair + 1) * PAIR] = tn(all_probs[pair], vals).astype(BF)
        return carry

    lax.fori_loop(0, rows // length, one, 0)


def attend(tokens, qkv, vec, length):
    rows, width = tokens.shape
    count = rows // length
    steps = 2
    block = rows // steps
    pairs = width // PAIR
    return pl.pallas_call(
        functools.partial(attend_kernel, length),
        grid=(steps,),
        in_specs=[
            pl.BlockSpec((block, width), lambda i: (i, 0)),
            full((3, width, width)),
            full(vec.shape),
        ],
        out_specs=[
            pl.BlockSpec((block, 3 * width), lambda i: (i, 0)),
            pl.BlockSpec((count // steps, pairs, 2 * length, length), lambda i: (i, 0, 0, 0)),
            pl.BlockSpec((block, width), lambda i: (i, 0)),
        ],
        out_shape=[
            jax.ShapeDtypeStruct((rows, 3 * width), BF),
            jax.ShapeDtypeStruct((count, pairs, 2 * length, length), BF),
            jax.ShapeDtypeStruct((rows, width), BF),
        ],
        compiler_params=params(),
        cost_estimate=cost(8 * rows * width * width, 20 * rows * width, rows * width),
        name="attend",
    )(tokens, qkv, vec)


def feed_kernel(
    length,
    load,
    inputs,
    place_ref,
    exit_ref,
    tok_ref,
    ctx_ref,
    out_w_ref,
    vec_ref,
    up_b_ref,
    *refs,
):
    weights, refs = refs[:inputs], refs[inputs:]
    (
        turned_ref,
        act_ref,
        slope_ref,
        unit1_ref,
        scale1_ref,
        unit2_ref,
        scale2_ref,
        output_ref,
        *more,
        acc_ref,
        low_ref,
        line_ref,
    ) = refs[: 11 + (2 if load else 0)]
    step = pl.program_id(0)
    last = pl.num_programs(0) - 1
    rows, width = tok_ref.shape
    sub = 256
    if load:
        up_all, down_all, sems, out_sems = refs[13:]
        each = down_all.shape[0] // up_all.shape[0]
        stores = [
            pltpu.make_async_copy(up_all, more[0], out_sems.at[0]),
            pltpu.make_async_copy(down_all, more[1], out_sems.at[1]),
        ]

        def up_part(cols):
            return up_all[step, :, cols]

        def down_part(cols):
            return down_all[pl.ds(step * each, each), :, cols].reshape(width, sub)

    else:

        def up_part(cols):
            return weights[0][0, :, cols]

        def down_part(cols):
            return weights[1][:, :, cols].reshape(width, sub)

    @pl.when(step == 0)
    def _():
        if load:
            copies = load(weights, up_all, down_all, place_ref, sems)
        for m in range(rows // sub):
            at = slice(m * sub, (m + 1) * sub)
            inner = tok_ref[at].astype(F32) + (
                nn(ctx_ref[at], out_w_ref[0]) + vec_ref[OUT_BIAS : OUT_BIAS + 1]
            )
            unit, scale = norm_stats(inner)
            first = unit * vec_ref[ATTN_GAIN : ATTN_GAIN + 1] + vec_ref[ATTN_SHIFT : ATTN_SHIFT + 1]
            unit1_ref[at] = unit.astype(BF)
            scale1_ref[at] = scale
            low = first.astype(BF)
            low_ref[at] = low
            turned_ref[:, at] = low.T
            acc_ref[at] = first + vec_ref[DOWN_BIAS : DOWN_BIAS + 1]
        if load:
            for copy in copies:
                copy.wait()
            for store in stores:
                store.start()

    tiles = [(m, n) for m in range(rows // sub) for n in range(width // sub)]

    def rows_of(m):
        return slice(m * sub, (m + 1) * sub)

    def first_product(tile):
        return nn(low_ref[rows_of(tile[0])], up_part(rows_of(tile[1])))

    def second_product(m, n):
        at, cols = rows_of(m), rows_of(n)
        acc_ref[at, cols] += nn(line_ref[m % 2], down_part(cols))

    ahead = first_product(tiles[0])
    for index, (m, n) in enumerate(tiles):
        at, cols = rows_of(m), rows_of(n)
        hidden = ahead + up_b_ref[:, cols]
        if index + 1 < len(tiles):
            ahead = first_product(tiles[index + 1])
        if m > 0:
            second_product(m - 1, n)
        act, slope = gelu_parts(hidden)
        act = act.astype(BF)
        line_ref[m % 2, :, cols] = act
        act_ref[cols, at] = act.T
        slope_ref[at, cols] = slope.astype(BF)
    for n in range(width // sub):
        second_product(rows // sub - 1, n)

    @pl.when(step == last)
    def _():
        for seq in range(rows // length):
            at = slice(seq * length, (seq + 1) * length)
            active = (exit_ref[seq] >= LAYER).astype(F32)
            unit, scale = norm_stats(acc_ref[at])
            unit2_ref[at] = unit.astype(BF)
            scale2_ref[at] = scale
            result = (
                unit * vec_ref[BLOCK_GAIN : BLOCK_GAIN + 1] + vec_ref[BLOCK_SHIFT : BLOCK_SHIFT + 1]
            ) * active
            output_ref[at] = result.astype(BF)
        if load:
            for store in stores:
                store.wait()


def feed(place, exit_layer, tokens, ctx, out_w, vec, up_bias, weights, load, shapes, length):
    rows, width = tokens.shape
    hidden = up_bias.shape[1]
    steps = hidden // width
    whole = full((rows, width))
    if load:
        weight_specs = [pl.BlockSpec(memory_space=pl.ANY)] * len(weights)
        more_specs = [pl.BlockSpec(memory_space=pl.ANY)] * 2
        more = [jax.ShapeDtypeStruct(shape, BF) for shape in shapes]
        copies = 2 * shapes[1][0] * shapes[0][0]
        scratch = [pltpu.VMEM(shape, BF) for shape in shapes] + [
            pltpu.SemaphoreType.DMA((copies,)),
            pltpu.SemaphoreType.DMA((2,)),
        ]
    else:
        weight_specs = [
            pl.BlockSpec((1, width, width), lambda i: (i, 0, 0)),
            pl.BlockSpec((1, width, width), lambda i: (i, 0, 0)),
        ]
        more_specs, more, scratch = [], [], []
    return pl.pallas_call(
        functools.partial(feed_kernel, length, load, len(weights)),
        grid=(steps,),
        in_specs=[
            pl.BlockSpec(memory_space=pltpu.SMEM),
            pl.BlockSpec(memory_space=pltpu.SMEM),
            whole,
            whole,
            pl.BlockSpec((1, width, width), lambda i: (3, 0, 0)),
            full(vec.shape),
            pl.BlockSpec((1, width), lambda i: (0, i)),
        ]
        + weight_specs,
        out_specs=[
            full((width, rows)),
            pl.BlockSpec((width, rows), lambda i: (i, 0)),
            pl.BlockSpec((rows, width), lambda i: (0, i)),
            whole,
            full((rows, 1)),
            whole,
            full((rows, 1)),
            whole,
        ]
        + more_specs,
        out_shape=[
            jax.ShapeDtypeStruct((width, rows), BF),
            jax.ShapeDtypeStruct((hidden, rows), BF),
            jax.ShapeDtypeStruct((rows, hidden), BF),
            jax.ShapeDtypeStruct((rows, width), BF),
            jax.ShapeDtypeStruct((rows, 1), F32),
            jax.ShapeDtypeStruct((rows, width), BF),
            jax.ShapeDtypeStruct((rows, 1), F32),
            jax.ShapeDtypeStruct((rows, width), BF),
        ]
        + more,
        scratch_shapes=[
            pltpu.VMEM((rows, width), F32),
            pltpu.VMEM((rows, width), BF),
            pltpu.VMEM((2, 256, width), BF),
        ]
        + scratch,
        compiler_params=params(),
        cost_estimate=cost(18 * rows * width * width, 40 * rows * width, 8 * rows * width),
        name="feed",
    )(place, exit_layer, tokens, ctx, out_w, vec, up_bias, *weights)


def load_second(counts, chips, reps, part, weights, up_all, down_all, place_ref, sems):
    at = 0
    groups = []
    for number in counts:
        groups.append(weights[at : at + number])
        at += number
    copies = []

    def start(source, target):
        copies.append(pltpu.make_async_copy(source, target, sems.at[len(copies)]))
        copies[-1].start()

    second_plan(
        start,
        groups,
        (up_all, down_all),
        place_ref[0],
        place_ref[1],
        place_ref[2],
        chips,
        reps,
        part,
    )
    return copies


def leave_kernel(
    length,
    classes,
    exit_ref,
    output_ref,
    unit2_ref,
    scale2_ref,
    grad_ref,
    pool_ref,
    vec_ref,
    class_bias_ref,
    logit_grad_ref,
    act_ref,
    outer_ref,
    branch_ref,
    joint_grad_ref,
    sums_ref,
    class_grad_ref,
    logits_ref,
    stats_ref,
    lead_ref,
    pool_grad_ref,
):
    step = pl.program_id(0)
    rows, width = output_ref.shape
    pool = pool_ref[...].reshape(width, width)
    count = rows // length

    @pl.when(step == 0)
    def _():
        place = lax.broadcasted_iota(jnp.int32, (count, 1), 0)
        active = jnp.zeros((count, 1), F32)
        for seq in range(count):
            on = (exit_ref[seq] >= LAYER).astype(F32)
            active = jnp.where(place == seq, on, active)
        leading = jnp.concatenate(
            [output_ref[seq * length : seq * length + 1].astype(F32) for seq in range(count)],
            axis=0,
        ).astype(BF)
        pooled = jnp.tanh(nn(leading, pool) + vec_ref[POOL_BIAS : POOL_BIAS + 1])
        pooled_low = pooled.astype(BF)
        used = lax.broadcasted_iota(jnp.int32, (8, width), 0) < classes
        class_rows = jnp.where(used, vec_ref[CLASS_ROWS : CLASS_ROWS + 8], 0.0).astype(BF)
        raw = nt(pooled_low, class_rows) + class_bias_ref[...]
        lane = lax.broadcasted_iota(jnp.int32, raw.shape, 1) < classes
        top = jnp.max(jnp.where(lane, raw, -jnp.inf), axis=-1, keepdims=True)
        spread = jnp.where(lane, jnp.exp(raw - top), 0.0)
        logprob = raw - top - jnp.log(jnp.sum(spread, axis=-1, keepdims=True))
        entropy = -jnp.sum(
            jnp.where(lane, jnp.exp(logprob) * logprob, 0.0), axis=-1, keepdims=True
        )
        logits_ref[...] = raw * active
        class_grad = (logit_grad_ref[...].astype(F32) * active).astype(BF)
        stats_ref[0:1] = jnp.broadcast_to(jnp.sum(entropy * active, axis=0, keepdims=True), (1, 8))
        stats_ref[1:2] = jnp.sum(class_grad.astype(F32), axis=0, keepdims=True)
        class_grad_ref[...] = tn(class_grad, pooled_low)
        pooled_grad = nn(class_grad, class_rows)
        pre_grad = (pooled_grad * (1.0 - pooled * pooled)).astype(BF)
        sums_ref[3:4] = jnp.sum(pre_grad.astype(F32), axis=0, keepdims=True)
        pool_grad_ref[...] = tn(leading, pre_grad).reshape(pool_grad_ref.shape).astype(BF)
        lead_ref[...] = nt(pre_grad, pool)
        head = lax.broadcasted_iota(jnp.int32, (length, 1), 0) == 0
        gain = vec_ref[BLOCK_GAIN : BLOCK_GAIN + 1]
        gain_sum = jnp.zeros((1, width), F32)
        shift_sum = jnp.zeros((1, width), F32)
        bias_sum = jnp.zeros((1, width), F32)
        for seq in range(count):
            at = slice(seq * length, (seq + 1) * length)
            on = (exit_ref[seq] >= LAYER).astype(F32)
            top_grad = (
                grad_ref[at].astype(F32) + jnp.where(head, lead_ref[seq : seq + 1], 0.0)
            ) * on
            unit = unit2_ref[at].astype(F32)
            outer = norm_back(top_grad, unit, scale2_ref[at], gain)
            branch = outer.astype(BF)
            outer_ref[at] = outer
            branch_ref[at] = branch
            gain_sum += jnp.sum(top_grad * unit, axis=0, keepdims=True)
            shift_sum += jnp.sum(top_grad, axis=0, keepdims=True)
            bias_sum += jnp.sum(branch.astype(F32), axis=0, keepdims=True)
        sums_ref[0:1] = gain_sum
        sums_ref[1:2] = shift_sum
        sums_ref[2:3] = bias_sum

    @pl.when(step > 0)
    def _():
        few, both, _ = joint_grad_ref.shape
        deep = width // few
        value = nn(act_ref[...], branch_ref[...])
        for at in range(few):
            joint_grad_ref[at, 0:deep] = value[at * deep : (at + 1) * deep].astype(BF)
            joint_grad_ref[at, deep:both] = pool_grad_ref[(step - 1) * few + at]


def leave(
    exit_layer, output, unit2, scale2, output_grad, pool, vec, class_bias, logit_grad, act,
    pool_spec, shards, length, classes,
):
    rows, width = output.shape
    count = rows // length
    hidden = act.shape[0]
    steps = hidden // width
    few = shards // steps
    both = (hidden + width) // shards
    whole = full((rows, width))
    return pl.pallas_call(
        functools.partial(leave_kernel, length, classes),
        grid=(steps + 1,),
        in_specs=[
            pl.BlockSpec(memory_space=pltpu.SMEM),
            whole,
            whole,
            full((rows, 1)),
            whole,
            pool_spec,
            full(vec.shape),
            full(class_bias.shape),
            full(logit_grad.shape),
            pl.BlockSpec((width, rows), lambda i: (jnp.maximum(i - 1, 0), 0)),
        ],
        out_specs=[
            whole,
            whole,
            pl.BlockSpec((few, both, width), lambda i: (jnp.maximum(i - 1, 0), 0, 0)),
            full((4, width)),
            full((8, width)),
            full((count, 8)),
            full((2, 8)),
        ],
        out_shape=[
            jax.ShapeDtypeStruct((rows, width), F32),
            jax.ShapeDtypeStruct((rows, width), BF),
            jax.ShapeDtypeStruct((shards, both, width), BF),
            jax.ShapeDtypeStruct((4, width), F32),
            jax.ShapeDtypeStruct((8, width), F32),
            jax.ShapeDtypeStruct((count, 8), F32),
            jax.ShapeDtypeStruct((2, 8), F32),
        ],
        scratch_shapes=[
            pltpu.VMEM((count, width), F32),
            pltpu.VMEM((shards, width // shards, width), BF),
        ],
        compiler_params=params(),
        cost_estimate=cost(8 * rows * width * width, 30 * rows * width),
        name="leave",
    )(
        exit_layer, output, unit2, scale2, output_grad, pool, vec, class_bias, logit_grad, act
    )


def split_cores(value, place_ref, keep_ref, send_ref):
    chips, part, _ = keep_ref.shape
    first = place_ref[2] == 0
    for chip in range(chips):
        even = value[2 * chip * part : (2 * chip + 1) * part]
        odd = value[(2 * chip + 1) * part : (2 * chip + 2) * part]
        keep_ref[chip] = jnp.where(first, even, odd).astype(BF)
        send_ref[chip] = jnp.where(first, odd, even).astype(BF)


def feed_back_kernel(
    place_ref,
    branch_ref,
    slope_ref,
    turned_ref,
    down_ref,
    up_ref,
    outer_ref,
    unit1_ref,
    scale1_ref,
    out_w_ref,
    vec_ref,
    ctx_ref,
    keep_ref,
    send_ref,
    up_sum_ref,
    inner_ref,
    attended_ref,
    ctx_grad_ref,
    sums_ref,
    acc_ref,
    hid_ref,
):
    step = pl.program_id(0)
    rows, width = branch_ref.shape
    sub = 512

    @pl.when(step == 0)
    def _():
        acc_ref[...] = outer_ref[...]

    last = pl.num_programs(0) - 1

    @pl.when(step < last)
    def _():
        total = jnp.zeros((1, width), F32)
        down = down_ref[...].reshape(up_ref.shape[1:])
        ahead = nt(branch_ref[0:sub], down)
        for m in range(rows // sub):
            at = slice(m * sub, (m + 1) * sub)
            hid = (ahead * slope_ref[at].astype(F32)).astype(BF)
            if (m + 1) * sub < rows:
                ahead = nt(branch_ref[(m + 1) * sub : (m + 2) * sub], down)
            hid_ref[at] = hid
            total += jnp.sum(hid.astype(F32), axis=0, keepdims=True)
            acc_ref[at] += nt(hid, up_ref[0])
        up_sum_ref[...] = total
        split_cores(nn(turned_ref[...], hid_ref[...]), place_ref, keep_ref, send_ref)

    @pl.when(step == last)
    def _():
        gain = vec_ref[ATTN_GAIN : ATTN_GAIN + 1]
        gain_sum = jnp.zeros((1, width), F32)
        shift_sum = jnp.zeros((1, width), F32)
        bias_sum = jnp.zeros((1, width), F32)
        for m in range(rows // sub):
            at = slice(m * sub, (m + 1) * sub)
            grad = acc_ref[at]
            unit = unit1_ref[at].astype(F32)
            inner = norm_back(grad, unit, scale1_ref[at], gain)
            attended = inner.astype(BF)
            inner_ref[at] = inner
            attended_ref[at] = attended
            ctx_grad_ref[at] = nt(attended, out_w_ref[0]).astype(BF)
            gain_sum += jnp.sum(grad * unit, axis=0, keepdims=True)
            shift_sum += jnp.sum(grad, axis=0, keepdims=True)
            bias_sum += jnp.sum(attended.astype(F32), axis=0, keepdims=True)
        sums_ref[0:1] = gain_sum
        sums_ref[1:2] = shift_sum
        sums_ref[2:3] = bias_sum
        split_cores(tn(ctx_ref[...], attended_ref[...]), place_ref, keep_ref, send_ref)


def feed_back(place, chips, branch, slope, low, down, down_block, up, outer, unit1, scale1, out_w, vec, ctx):
    rows, width = branch.shape
    hidden = slope.shape[1]
    steps = hidden // width
    whole = full((rows, width))
    end = steps - 1
    part = width // (2 * chips)
    return pl.pallas_call(
        feed_back_kernel,
        grid=(steps + 1,),
        in_specs=[
            pl.BlockSpec(memory_space=pltpu.SMEM),
            whole,
            pl.BlockSpec((rows, width), lambda i: (0, jnp.minimum(i, end))),
            full((width, rows)),
            pl.BlockSpec(down_block, lambda i: (jnp.minimum(i, end), 0, 0)),
            pl.BlockSpec((1, width, width), lambda i: (jnp.minimum(i, end), 0, 0)),
            whole,
            whole,
            full((rows, 1)),
            pl.BlockSpec((1, width, width), lambda i: (3, 0, 0)),
            full(vec.shape),
            whole,
        ],
        out_specs=[
            pl.BlockSpec((chips, part, width), lambda i: (0, 0, i)),
            pl.BlockSpec((chips, part, width), lambda i: (0, 0, i)),
            pl.BlockSpec((1, width), lambda i: (0, jnp.minimum(i, end))),
            whole,
            whole,
            whole,
            full((3, width)),
        ],
        out_shape=[
            jax.ShapeDtypeStruct((chips, part, hidden + width), BF),
            jax.ShapeDtypeStruct((chips, part, hidden + width), BF),
            jax.ShapeDtypeStruct((1, hidden), F32),
            jax.ShapeDtypeStruct((rows, width), F32),
            jax.ShapeDtypeStruct((rows, width), BF),
            jax.ShapeDtypeStruct((rows, width), BF),
            jax.ShapeDtypeStruct((3, width), F32),
        ],
        scratch_shapes=[pltpu.VMEM((rows, width), F32), pltpu.VMEM((rows, width), BF)],
        compiler_params=params(),
        cost_estimate=cost(28 * rows * width * width, 40 * rows * width),
        name="feed_back",
    )(place, branch, slope, low, down, up, outer, unit1, scale1, out_w, vec, ctx)


def attend_back_kernel(length, joined_ref, probs_ref, ctx_grad_ref, grad_ref, sum_ref):
    rows, width = ctx_grad_ref.shape
    pairs = width // PAIR

    def one(seq, carry):
        at = pl.ds(pl.multiple_of(seq * length, length), length)

        def columns(part, pair):
            return slice(part * width + pair * PAIR, part * width + (pair + 1) * PAIR)

        prob_grads = []
        for pair in range(pairs):
            vals = split_heads(joined_ref[at, columns(2, pair)])
            prob_grads.append(nt(vals, ctx_grad_ref[at, columns(0, pair)]))
        score_grads = []
        for pair in range(pairs):
            probs = probs_ref[seq, pair]
            halves = []
            for head in range(2):
                cut = slice(head * length, (head + 1) * length)
                held = probs[cut].astype(F32)
                part = prob_grads[pair][cut]
                base = jnp.sum(part * held, axis=0, keepdims=True)
                halves.append((held * (part - base)).astype(BF))
            score_grads.append(halves)
        for pair in range(pairs):
            probs = probs_ref[seq, pair]
            beside = jnp.concatenate([probs[:length], probs[length:]], axis=1)
            ctx_grads = split_heads(ctx_grad_ref[at, columns(0, pair)])
            grad_ref[at, columns(2, pair)] = nn(beside, ctx_grads).astype(BF)
        for pair in range(pairs):
            queries = split_heads(joined_ref[at, columns(0, pair)] * jnp.asarray(0.125, BF))
            beside = jnp.concatenate(score_grads[pair], axis=1)
            grad_ref[at, columns(1, pair)] = nn(beside, queries).astype(BF)
        for pair in range(pairs):
            keys = split_heads(joined_ref[at, columns(1, pair)])
            stacked = jnp.concatenate(score_grads[pair], axis=0)
            grad_ref[at, columns(0, pair)] = (tn(stacked, keys) * 0.125).astype(BF)
        return carry

    lax.fori_loop(0, rows // length, one, 0)
    total = jnp.zeros(sum_ref.shape, F32)
    for m in range(rows // length):
        total += jnp.sum(
            grad_ref[m * length : (m + 1) * length].astype(F32), axis=0, keepdims=True
        )

    @pl.when(pl.program_id(0) == 0)
    def _():
        sum_ref[...] = total

    @pl.when(pl.program_id(0) > 0)
    def _():
        sum_ref[...] += total


def attend_back(joined, probs, ctx_grad, length):
    rows, width = ctx_grad.shape
    count = rows // length
    steps = 2
    block = rows // steps
    pairs = width // PAIR
    return pl.pallas_call(
        functools.partial(attend_back_kernel, length),
        grid=(steps,),
        in_specs=[
            pl.BlockSpec((block, 3 * width), lambda i: (i, 0)),
            pl.BlockSpec((count // steps, pairs, 2 * length, length), lambda i: (i, 0, 0, 0)),
            pl.BlockSpec((block, width), lambda i: (i, 0)),
        ],
        out_specs=[
            pl.BlockSpec((block, 3 * width), lambda i: (i, 0)),
            full((1, 3 * width)),
        ],
        out_shape=[
            jax.ShapeDtypeStruct((rows, 3 * width), BF),
            jax.ShapeDtypeStruct((1, 3 * width), F32),
        ],
        compiler_params=params(),
        cost_estimate=cost(rows * width, rows * width),
        name="attend_back",
    )(joined, probs, ctx_grad)


def weight_grads_kernel(tok_ref, joined_ref, small_ref, out_ref, turned_ref):
    step = pl.program_id(0)
    last = pl.num_programs(0) - 1
    shards, part, width = out_ref.shape

    @pl.when(step == 0)
    def _():
        turned_ref[...] = tok_ref[...].T

    value = nn(turned_ref[...], joined_ref[...])
    cols = pl.ds(pl.multiple_of(step * joined_ref.shape[1], joined_ref.shape[1]), joined_ref.shape[1])
    out_ref[:, :, cols] = value.reshape(shards, part, joined_ref.shape[1]).astype(BF)
    tail = 3 * joined_ref.shape[1]
    if width > tail:

        @pl.when(step == last)
        def _():
            lines = small_ref.shape[1]
            out_ref[:, lines:part, tail:width] = jnp.zeros(
                (shards, part - lines, width - tail), BF
            )
            out_ref[:, 0:lines, tail:width] = small_ref[...].astype(BF)


def weight_grads(tokens, joined_grad, small, shards, extra):
    rows, width = tokens.shape
    shape = (shards, width // shards, 3 * width + extra)
    return pl.pallas_call(
        weight_grads_kernel,
        grid=(3,),
        in_specs=[
            full((rows, width)),
            pl.BlockSpec((rows, width), lambda i: (0, i)),
            full(small.shape),
        ],
        out_specs=full(shape),
        out_shape=jax.ShapeDtypeStruct(shape, BF),
        scratch_shapes=[pltpu.VMEM((width, rows), BF)],
        compiler_params=params(),
        cost_estimate=cost(rows * width, rows * width),
        name="weight_grads",
    )(tokens, joined_grad, small)


def input_kernel(inner_ref, joined_ref, w_ref, out_ref):
    width = inner_ref.shape[1]
    total = inner_ref[...]
    for part in range(3):
        total += nt(joined_ref[:, part * width : (part + 1) * width], w_ref[part])
    out_ref[...] = total.astype(BF)


def input_back(inner, joined_grad, qkv):
    rows, width = inner.shape
    steps = 4
    block = rows // steps
    return pl.pallas_call(
        input_kernel,
        grid=(steps,),
        in_specs=[
            pl.BlockSpec((block, width), lambda i: (i, 0)),
            pl.BlockSpec((block, 3 * width), lambda i: (i, 0)),
            full((3, width, width)),
        ],
        out_specs=pl.BlockSpec((block, width), lambda i: (i, 0)),
        out_shape=jax.ShapeDtypeStruct((rows, width), BF),
        compiler_params=params(),
        cost_estimate=cost(rows * width, rows * width),
        name="input_back",
    )(inner, joined_grad, qkv)


def lay_kernel(plan, chips, reps, part, counts, place_ref, *refs):
    at = 0
    groups = []
    for number in counts:
        groups.append(refs[at : at + number])
        at += number
    sems = refs[-1]
    rep, chip, core = place_ref[0], place_ref[1], place_ref[2]
    copies = []

    def start(source, target):
        copies.append(pltpu.make_async_copy(source, target, sems.at[len(copies)]))
        copies[-1].start()

    finish = plan(start, groups, refs[at:-1], rep, chip, core, chips, reps, part)
    for copy in copies:
        copy.wait()
    if finish is not None:
        finish()


def blocks_plan(
    put, own, twin, along, across, swapped, depth, first, rep, chip, core, chips, reps, part
):
    for block in range(reps):
        put(own(block), block, chip, core)
        put(twin(block), block, chip, 1 - core)
    for step in range(1, chips):
        source = lax.rem(chip + chips - step, chips)
        rows = pl.ds((step - 1) * depth + first, part)
        for other, block in along.items():
            put(block(step, source, 0), rep ^ other, source, core)
            put(block(step, source, 1), rep ^ other, source, 1 - core)
        for other in across:
            put(across[other].at[rows], rep ^ other, source, core)
            put(swapped[other].at[rows], rep ^ other, source, 1 - core)


def wide_put(start, out_ref, part):
    def put(source, block, at_chip, at_core):
        row = pl.multiple_of((at_chip * 2 + at_core) * part, part)
        start(source, out_ref.at[block, pl.ds(row, part)])

    return put


def wide_block(ref, width, part):
    return lambda block: ref.at[pl.ds(0, part), pl.ds(block * width, width)]


def first_plan(start, groups, outs, rep, chip, core, chips, reps, part):
    (own, twin), along, across, swapped, (extra,) = groups
    out_ref, vec_ref, more_ref = outs
    width = out_ref.shape[2]

    def near(step, source, side):
        if side == 0:
            return along[step - 1].at[pl.ds(0, part)]
        return swapped[0].at[pl.ds((step - 1) * part, part)]

    blocks_plan(
        wide_put(start, out_ref, part),
        wide_block(own, width, part),
        wide_block(twin, width, part),
        {0: near},
        {at + 1: ref for at, ref in enumerate(across)},
        {at + 1: ref for at, ref in enumerate(swapped[1:])},
        part,
        0,
        rep,
        chip,
        core,
        chips,
        reps,
        part,
    )
    tail = pl.ds(part, 16)
    cols = pl.ds(0, width)
    start(own.at[tail, cols], more_ref.at[chip * 2 + core])
    start(twin.at[tail, cols], more_ref.at[chip * 2 + 1 - core])
    for step in range(1, chips):
        source = lax.rem(chip + chips - step, chips)
        start(along[step - 1].at[tail], more_ref.at[source * 2 + core])
        start(extra.at[pl.ds((step - 1) * 16, 16)], more_ref.at[source * 2 + 1 - core])

    def finish():
        lane = lax.broadcasted_iota(jnp.int32, (LANES, width), 0)
        place = lax.broadcasted_iota(jnp.int32, (LANES, width), 1)
        total = jnp.zeros((16, width), F32)
        for shard in range(2 * chips):
            there = (place - shard * part == lane) & (lane < part)
            total += nn(more_ref[shard, :, 0:LANES], there.astype(F32).astype(BF))
        vec_ref[...] = total

    return finish


def second_plan(start, groups, outs, rep, chip, core, chips, reps, part):
    (up, up_twin, down, down_twin), (close, far), across, swapped = groups
    up_ref, down_ref = outs
    width = up_ref.shape[2]
    where = (rep, chip, core, chips, reps, part)

    def chained(chain, first):
        def block(step, source, side):
            shard = source * 2 + (core if side == 0 else 1 - core)
            return chain.at[shard, pl.ds(first, part)]

        return block

    across = dict(zip(NEAR, across))
    swapped = dict(zip(NEAR, swapped))
    blocks_plan(
        wide_put(start, up_ref, part),
        wide_block(up, width, part),
        wide_block(up_twin, width, part),
        {0: chained(close, 0), FAR: chained(far, 0)},
        across,
        swapped,
        2 * part,
        0,
        *where,
    )

    def put(source, block, at_chip, at_core):
        row = pl.multiple_of(block * part, part)
        start(source, down_ref.at[at_chip * 2 + at_core, pl.ds(row, part)])

    def tall(ref):
        return lambda block: ref.at[pl.ds(block * part, part)]

    blocks_plan(
        put,
        tall(down),
        tall(down_twin),
        {0: chained(close, part), FAR: chained(far, part)},
        across,
        swapped,
        2 * part,
        part,
        *where,
    )


def lay(plan, place, groups, shapes, scratch, copies, part, chips, reps):
    anywhere = pl.BlockSpec(memory_space=pl.ANY)
    inputs = [ref for group in groups for ref in group]
    return pl.pallas_call(
        functools.partial(
            lay_kernel, plan, chips, reps, part, [len(group) for group in groups]
        ),
        in_specs=[pl.BlockSpec(memory_space=pltpu.SMEM)] + [anywhere] * len(inputs),
        out_specs=[pl.BlockSpec(memory_space=pltpu.VMEM)] * len(shapes),
        out_shape=[jax.ShapeDtypeStruct(shape, kind) for shape, kind in shapes],
        scratch_shapes=[pltpu.VMEM(shape, BF) for shape in scratch]
        + [pltpu.SemaphoreType.DMA((copies,))],
        compiler_params=pltpu.CompilerParams(vmem_limit_bytes=VMEM_BYTES),
        cost_estimate=cost(0, 4 * sum(math.prod(shape) for shape, kind in shapes)),
        name="lay",
    )(place, *inputs)


def pack_vectors(rows, up_bias, class_weight):
    part = rows[0].shape[0]
    lines = [row[None] for row in rows[:8]] + [class_weight.T] + [row[None] for row in rows[8:]]
    pieces = up_bias.shape[0] // part
    lines += [up_bias[None, at * part : (at + 1) * part] for at in range(pieces)]
    return jnp.concatenate(lines, axis=0)


def move(values, reps, chips, target):
    pairs = []
    for rep in range(reps):
        for chip in range(chips):
            for core in range(2):
                to_rep, to_chip, to_core = target(rep, chip, core)
                pairs.append(
                    (
                        (rep * chips + chip) * 2 + core,
                        (to_rep * chips + to_chip) * 2 + to_core,
                    )
                )
    return lax.ppermute(values, ("rep", "fsdp"), pairs)


def along_chips(step, chips):
    return lambda rep, chip, core: (rep, (chip + step) % chips, core)


def across_reps(other):
    return lambda rep, chip, core: (rep ^ other, chip, core)


def to_twin(rep, chip, core):
    return rep, chip, 1 - core


def after(values, *gates):
    return lax.optimization_barrier((values, *gates))[0]


def along_z(mine, reps, chips):
    return [move(mine, reps, chips, along_chips(step, chips)) for step in range(1, chips)]


def over_reps(stacked, reps, chips, others):
    return [move(stacked, reps, chips, across_reps(other)) for other in others]


def pick(parts, at):
    return lax.dynamic_index_in_dim(parts, at, axis=0, keepdims=False)


def in_order(rep, reps, own, others, axis):
    blocks = jnp.stack([own] + others)
    return jnp.concatenate([pick(blocks, rep ^ at) for at in range(reps)], axis=axis)


class Reduction:
    def __init__(self, place, keep, send, reps, chips):
        self.rep, self.chip = place[0], place[1]
        self.reps, self.chips = reps, chips
        self.keep = keep
        self.got = move(send, reps, chips, to_twin)

    def at_rep(self, at):
        return lax.dynamic_index_in_dim(self.both, at, axis=1, keepdims=False)

    def over_reps(self):
        chips, rows, width = self.keep.shape
        both = (self.keep.astype(F32) + self.got.astype(F32)).astype(BF)
        self.both = lax.optimization_barrier(both).reshape(
            chips, self.reps, rows // self.reps, width
        )
        self.arrived = [self.over_rep(other) for other in NEAR]

    def over_rep(self, other, *gates):
        block = self.at_rep(self.rep ^ other)
        if gates:
            block = after(block, *gates)
        return move(block, self.reps, self.chips, across_reps(other))

    def over_far(self, *gates):
        self.arrived = self.arrived + [self.over_rep(FAR, *gates)]

    def over_chips(self, *gates):
        if gates:
            self.arrived = [after(block, *gates) for block in self.arrived]
        total = self.at_rep(self.rep).astype(F32)
        for block in self.arrived:
            total = total + block.astype(F32)
        self.total = pick(total, self.chip)
        self.passed = [
            move(
                pick(total, lax.rem(self.chip + step, self.chips)).astype(BF),
                self.reps,
                self.chips,
                along_chips(step, self.chips),
            )
            for step in range(1, self.chips)
        ]

    def chip_sum(self):
        total = self.total
        for block in self.passed:
            total = total + block.astype(F32)
        return total.astype(BF)


def share_reps(place, total, reps, chips):
    others = [move(total, reps, chips, across_reps(other)) for other in range(1, reps)]
    return in_order(place[0], reps, total, others, 0).astype(F32), others


def exchange_reps(place, rows, reps, chips):
    rep = place[0]
    parts = rows.reshape(reps, -1, rows.shape[1])
    total = pick(parts, rep).astype(F32)
    arrived = [
        move(pick(parts, rep ^ other), reps, chips, across_reps(other))
        for other in range(1, reps)
    ]
    for block in arrived:
        total = total + block.astype(F32)
    return total.astype(BF), arrived


def per_device(
    tokens,
    exit_layer,
    qkv_weight,
    query_bias,
    value_bias,
    out_weight,
    out_bias,
    attn_gain,
    attn_shift,
    up_weight,
    up_bias,
    down_weight,
    down_bias,
    block_gain,
    block_shift,
    pool_weight,
    pool_bias,
    class_weight,
    class_bias,
    output_grad,
    logit_grad,
):
    reps = lax.axis_size("rep")
    shards = lax.axis_size("fsdp")
    mine = lax.axis_index("fsdp")
    rows, width = tokens.shape
    count = exit_layer.shape[0]
    length = rows // count
    classes = class_weight.shape[1]
    part = out_weight.shape[0]
    hidden = up_weight.shape[1]

    def gather(shard):
        return lax.all_gather(shard, "fsdp", axis=0, tiled=True)

    packed = pack_vectors(
        [
            query_bias,
            value_bias,
            out_bias,
            attn_gain,
            attn_shift,
            down_bias,
            block_gain,
            block_shift,
            pool_bias,
        ],
        up_bias,
        class_weight,
    )
    joint_own = jnp.concatenate([qkv_weight, out_weight], axis=1)
    deep = down_weight.shape[0]
    chips = shards // 2
    place = jnp.stack([lax.axis_index("rep"), mine // 2, mine % 2]).astype(jnp.int32)
    direct = (
        part % 16 == 0
        and reps & (reps - 1) == 0
        and reps * width == hidden
        and reps == 4
        and packed.shape[0] <= 16
    )
    if direct:
        lines = packed.shape[0]
        held = jnp.pad(packed, ((0, 16 - lines), (0, width - part)))
        own = jnp.concatenate([joint_own, jnp.tile(held, (1, reps))], axis=0)
        rep = place[0]

        def block_of(weights, at):
            return lax.dynamic_slice_in_dim(weights, at * width, width, axis=1)

        def second_of(at):
            return [
                block_of(up_weight, at),
                lax.dynamic_slice_in_dim(down_weight, at * part, part, axis=0),
            ]

        along = along_z(block_of(own, rep), reps, chips)
        chain = gather(after(jnp.concatenate(second_of(rep), axis=0), *along))
        chain = chain.reshape(chips, 2, 2 * part, width)
        twin = move(own, reps, chips, to_twin)
        stacked = jnp.concatenate([rows_[:part] for rows_ in along], axis=0)
        across = over_reps(stacked, reps, chips, range(1, reps))
        far_chain = gather(after(jnp.concatenate(second_of(rep ^ FAR), axis=0), *across))
        swapped = [move(rows_, reps, chips, to_twin) for rows_ in [stacked] + across]
        extra = move(
            jnp.concatenate([rows_[part:] for rows_ in along], axis=0), reps, chips, to_twin
        )
        up_twin = move(up_weight, reps, chips, to_twin)
        down_twin = move(down_weight, reps, chips, to_twin)
        joint, vec = lay(
            first_plan,
            place,
            [
                [own, twin],
                along,
                across,
                swapped,
                [extra],
            ],
            [((reps, width, width), BF), ((16, width), F32)],
            [(shards, 16, width)],
            2 * chips * (reps + 1),
            part,
            chips,
            reps,
        )
        mine_chain = lax.dynamic_index_in_dim(
            after(chain, joint), place[2], axis=1, keepdims=False
        )
        second_stacked = jnp.concatenate(
            [
                pick(mine_chain, lax.rem(place[1] + chips - step, chips))
                for step in range(1, chips)
            ],
            axis=0,
        )
        second_across = over_reps(after(second_stacked, *across), reps, chips, NEAR)
        up_row = (
            vec[VECTOR_ROWS:lines].reshape(-1, shards, part).transpose(1, 0, 2).reshape(1, hidden)
        )
        down_block = (width // deep, deep, width)
    else:
        small = gather(packed[None])
        vec = small[:, :VECTOR_ROWS].transpose(1, 0, 2).reshape(VECTOR_ROWS, width).astype(F32)
        vec = jnp.pad(vec, ((0, 16 - VECTOR_ROWS), (0, 0)))
        up_row = small[:, VECTOR_ROWS:].transpose(0, 1, 2).reshape(1, hidden).astype(F32)
        pool = gather(pool_weight)
        joint = jnp.stack(jnp.split(gather(joint_own), 4, axis=1))
        up = jnp.stack(jnp.split(gather(up_weight), hidden // width, axis=1))
        down = gather(down_weight).reshape(-1, width, width)
        down_block = (1, width, width)
    joined, probs, ctx = attend(tokens, joint, vec, length)
    if direct:
        pool = gather(after(pool_weight, ctx))
        far_chain = after(far_chain, ctx)
        second_swapped = [
            move(after(rows_, ctx), reps, chips, to_twin) for rows_ in second_across
        ]
        groups = [
            [up_weight, up_twin, down_weight, down_twin],
            [
                chain.reshape(shards, 2 * part, width),
                far_chain.reshape(shards, 2 * part, width),
            ],
            second_across,
            second_swapped,
        ]
        weights = [ref for group in groups for ref in group]
        load = functools.partial(load_second, [len(group) for group in groups], chips, reps, part)
        shapes = [(reps, width, width), (shards, deep, width)]
    else:
        weights, load, shapes = [up, down], None, None
    turned, act, slope, unit1, scale1, unit2, scale2, output, *laid = feed(
        place, exit_layer, tokens, ctx, joint, vec, up_row, weights, load, shapes, length
    )
    if direct:
        up, down = laid
    class_bias_row = jnp.pad(class_bias.astype(F32), (0, 8 - classes))[None]
    logit_grad_rows = jnp.pad(logit_grad, ((0, 0), (0, 8 - classes)))
    outer, branch, low_grad, exit_sums, class_grad, logits, stats = leave(
        exit_layer,
        output,
        unit2,
        scale2,
        output_grad,
        pool,
        vec,
        class_bias_row,
        logit_grad_rows,
        act,
        full((width, width)),
        shards,
        length,
        classes,
    )
    def scatter(grad):
        return lax.psum_scatter(grad, "fsdp", scatter_dimension=0, tiled=True)

    low_part = scatter(low_grad.reshape(-1, width))
    up_keep, up_send, up_sum, inner, attended, ctx_grad, feed_sums = feed_back(
        place, chips, branch, slope, turned, down, down_block, up, outer, unit1, scale1, joint, vec, ctx
    )
    if direct:
        up_red = Reduction(place, up_keep, up_send, reps, chips)
        up_red.over_reps()
        ctx_grad = after(ctx_grad, up_red.both)
    joined_grad, joined_sum = attend_back(joined, probs, ctx_grad, length)
    joined_seen = joined_grad
    if direct:
        joined_seen = after(joined_grad, low_part, *up_red.arrived)
    sums = jnp.concatenate(
        [
            joined_sum.reshape(3, width)[::2],
            feed_sums,
            exit_sums,
            class_grad[:classes],
        ],
        axis=0,
    )
    lines = sums.shape[0]
    own_sums = sums.reshape(lines, shards, part).transpose(1, 0, 2).reshape(shards, lines * part)
    own_sums = jnp.concatenate([own_sums, up_sum.reshape(shards, deep)], axis=1)
    used = own_sums.shape[1]
    seqs_total = count * reps * shards
    figures = jnp.concatenate([stats[0, :1], stats[1, :classes]])
    slots = reps * shards * figures.shape[0] * 3
    direct = direct and used + slots <= part * LANES
    small_lines = 16
    if direct:
        high = figures.astype(BF).astype(F32)
        middle = (figures - high).astype(BF).astype(F32)
        lowest = figures - high - middle
        split = jnp.concatenate([high, middle, lowest])
        slot = lax.axis_index("rep") * shards + mine
        lone = jnp.where(
            jnp.arange(reps * shards)[:, None] == slot, split[None], 0.0
        ).reshape(1, slots)
        row = jnp.concatenate([own_sums, jnp.broadcast_to(lone, (shards, slots))], axis=1)
        small_lines = -(-row.shape[1] // (LANES * 16)) * 16
        row = jnp.pad(row, ((0, 0), (0, small_lines * LANES - row.shape[1])))
        row = row.reshape(shards, small_lines, LANES)
    else:
        row = jnp.zeros((shards, small_lines, LANES), F32)
    joint_grad = weight_grads(tokens, joined_seen, row, shards, LANES if direct else 0)
    input_grad = input_back(inner, joined_grad, joint)

    if direct:
        up_red.over_far(joint_grad)
        joint_grad = after(joint_grad, low_part)
    joint_part = scatter(joint_grad.reshape(width, -1))
    if direct:
        low_total, low_arrived = exchange_reps(
            place, after(low_part, joint_grad), reps, chips
        )
        up_red.over_chips(*low_arrived)
        wide = (deep + part) * width // part
        up_total = up_red.chip_sum()
        columns = up_total.shape[1]
        pair, pair_others = share_reps(
            place,
            jnp.concatenate([up_total, low_total.reshape(-1, wide)], axis=1),
            reps,
            chips,
        )
        up_sum = pair[:, :columns]
        low_sum = pair[:, columns:].reshape(deep + part, width)
        joint_total, _ = exchange_reps(
            place, after(joint_part, *pair_others), reps, chips
        )
        joint_sum, _ = share_reps(place, joint_total, reps, chips)
        small_sum = joint_sum[:small_lines, 3 * width :].reshape(-1)
        total = small_sum[used : used + slots].reshape(-1, figures.shape[0]).sum(axis=0)
    else:
        first = mine % 2 == 0

        def whole_of(kept, sent):
            pair = jnp.stack([jnp.where(first, kept, sent), jnp.where(first, sent, kept)], axis=1)
            return pair.reshape(-1, kept.shape[2])

        joint_sum, low_sum, up_sum = lax.psum(
            (joint_part, low_part, scatter(whole_of(up_keep, up_send))), "rep"
        )
        joint_sum, low_sum, up_sum = (
            joint_sum.astype(F32),
            low_sum.astype(F32),
            up_sum.astype(F32),
        )
        own_sums, total = lax.psum((own_sums, figures), ("rep", "fsdp"))
        small_sum = pick(own_sums, mine)
    own = small_sum[: lines * part].reshape(lines, part)
    return (
        output,
        logits[:, :classes],
        total[0] / seqs_total,
        input_grad,
        joint_sum[:, : 3 * width],
        own[0],
        own[1],
        up_sum[:, hidden:],
        own[4],
        own[2],
        own[3],
        up_sum[:, :hidden],
        small_sum[lines * part : used],
        low_sum[:deep],
        own[7],
        own[5],
        own[6],
        low_sum[deep:],
        own[8],
        own[9 : 9 + classes].T,
        total[1:],
    )


def solution(mesh):
    return jax.shard_map(
        per_device,
        mesh=mesh,
        in_specs=(
            P(("rep", "fsdp"), None),
            P(("rep", "fsdp")),
            P("fsdp", None),
            P("fsdp"),
            P("fsdp"),
            P("fsdp", None),
            P("fsdp"),
            P("fsdp"),
            P("fsdp"),
            P("fsdp", None),
            P("fsdp"),
            P("fsdp", None),
            P("fsdp"),
            P("fsdp"),
            P("fsdp"),
            P("fsdp", None),
            P("fsdp"),
            P("fsdp", None),
            P(),
            P(("rep", "fsdp"), None),
            P(("rep", "fsdp"), None),
        ),
        out_specs=(
            P(("rep", "fsdp"), None),
            P(("rep", "fsdp"), None),
            P(),
            P(("rep", "fsdp"), None),
            P("fsdp", None),
            P("fsdp"),
            P("fsdp"),
            P("fsdp", None),
            P("fsdp"),
            P("fsdp"),
            P("fsdp"),
            P("fsdp", None),
            P("fsdp"),
            P("fsdp", None),
            P("fsdp"),
            P("fsdp"),
            P("fsdp"),
            P("fsdp", None),
            P("fsdp"),
            P("fsdp", None),
            P(),
        ),
        check_vma=False,
    )
```

```python
import functools
import math

import jax
import jax.numpy as jnp
from jax import lax
from jax.experimental import pallas as pl
from jax.experimental.pallas import tpu as pltpu
from jax.sharding import PartitionSpec as P

HD = 64
LAYER = 6
PAIR = 2 * HD
NEAR = (1, 2)
FAR = 3
LANES = 128
VMEM_BYTES = 58 * 2**20
BF = jnp.bfloat16
F32 = jnp.float32

QUERY_BIAS, VALUE_BIAS, OUT_BIAS, ATTN_GAIN, ATTN_SHIFT = 0, 1, 2, 3, 4
DOWN_BIAS, BLOCK_GAIN, BLOCK_SHIFT, CLASS_ROWS, POOL_BIAS = 5, 6, 7, 8, 11
VECTOR_ROWS = 12


def nn(left, right):
    return jnp.dot(left, right, preferred_element_type=F32)


def tn(left, right):
    return lax.dot_general(left, right, (((0,), (0,)), ((), ())), preferred_element_type=F32)


def nt(left, right):
    return lax.dot_general(left, right, (((1,), (1,)), ((), ())), preferred_element_type=F32)


def full(shape):
    return pl.BlockSpec(shape, lambda *at: (0,) * len(shape))


def params():
    return pltpu.CompilerParams(
        dimension_semantics=("arbitrary",), vmem_limit_bytes=VMEM_BYTES
    )


def cost(flops, moved, trans=0):
    return pl.CostEstimate(flops=flops, bytes_accessed=moved, transcendentals=trans)


def split_heads(pair):
    lane = lax.broadcasted_iota(jnp.int32, pair.shape, 1)
    zero = jnp.zeros_like(pair)
    return jnp.concatenate(
        [jnp.where(lane < HD, pair, zero), jnp.where(lane < HD, zero, pair)], axis=0
    )


def norm_stats(values):
    center = values - jnp.mean(values, axis=-1, keepdims=True)
    spread = jnp.mean(center * center, axis=-1, keepdims=True)
    scale = lax.rsqrt(spread + 1e-06)
    return center * scale, scale


def norm_back(grad, unit, scale, gain):
    inner = grad * gain
    first = jnp.mean(inner, axis=-1, keepdims=True)
    second = jnp.mean(inner * unit, axis=-1, keepdims=True)
    return scale * (inner - first - unit * second)


def gelu_parts(values):
    base = 1.0 + 0.23164189 * jnp.abs(values)
    t = pl.reciprocal(base, approx=True)
    t = t * (2.0 - base * t)
    bell = jnp.exp2((values * values) * -0.7213475204444817)
    poly = t * (
        0.127414796
        + t * (-0.142248368 + t * (0.7107068705 + t * (-0.7265760135 + t * 0.5307027145)))
    )
    tail = poly * bell
    below = jnp.where(values >= 0.0, 1.0 - tail, tail)
    return values * below, below + values * (bell * 0.3989422804014327)


def attend_kernel(length, tok_ref, w_ref, vec_ref, joined_ref, probs_ref, ctx_ref):
    rows, width = ctx_ref.shape
    pairs = width // PAIR
    for part in range(3):
        cols = slice(part * width, (part + 1) * width)
        value = nn(tok_ref[...], w_ref[part])
        if part == 0:
            value += vec_ref[QUERY_BIAS : QUERY_BIAS + 1]
        elif part == 2:
            value += vec_ref[VALUE_BIAS : VALUE_BIAS + 1]
        joined_ref[:, cols] = value.astype(BF)

    def one(seq, carry):
        at = pl.ds(pl.multiple_of(seq * length, length), length)
        scores = []
        for pair in range(pairs):
            query = joined_ref[at, pair * PAIR : (pair + 1) * PAIR] * jnp.asarray(0.125, BF)
            keys = split_heads(joined_ref[at, width + pair * PAIR : width + (pair + 1) * PAIR])
            scores.append(nt(keys, query))
        all_probs = []
        for pair in range(pairs):
            halves = []
            for head in range(2):
                part = scores[pair][head * length : (head + 1) * length]
                part = jnp.exp(part - jnp.max(part, axis=0, keepdims=True))
                part = part * (1.0 / jnp.sum(part, axis=0, keepdims=True))
                halves.append(part.astype(BF))
            probs = jnp.concatenate(halves, axis=0)
            probs_ref[seq, pair] = probs
            all_probs.append(probs)
        for pair in range(pairs):
            vals = split_heads(
                joined_ref[at, 2 * width + pair * PAIR : 2 * width + (pair + 1) * PAIR]
            )
            ctx_ref[at, pair * PAIR : (pair + 1) * PAIR] = tn(all_probs[pair], vals).astype(BF)
        return carry

    lax.fori_loop(0, rows // length, one, 0)


def attend(tokens, qkv, vec, length):
    rows, width = tokens.shape
    count = rows // length
    steps = 2
    block = rows // steps
    pairs = width // PAIR
    return pl.pallas_call(
        functools.partial(attend_kernel, length),
        grid=(steps,),
        in_specs=[
            pl.BlockSpec((block, width), lambda i: (i, 0)),
            full((3, width, width)),
            full(vec.shape),
        ],
        out_specs=[
            pl.BlockSpec((block, 3 * width), lambda i: (i, 0)),
            pl.BlockSpec((count // steps, pairs, 2 * length, length), lambda i: (i, 0, 0, 0)),
            pl.BlockSpec((block, width), lambda i: (i, 0)),
        ],
        out_shape=[
            jax.ShapeDtypeStruct((rows, 3 * width), BF),
            jax.ShapeDtypeStruct((count, pairs, 2 * length, length), BF),
            jax.ShapeDtypeStruct((rows, width), BF),
        ],
        compiler_params=params(),
        cost_estimate=cost(8 * rows * width * width, 20 * rows * width, rows * width),
        name="attend",
    )(tokens, qkv, vec)


def feed_kernel(
    length,
    load,
    inputs,
    place_ref,
    exit_ref,
    tok_ref,
    ctx_ref,
    out_w_ref,
    vec_ref,
    up_b_ref,
    *refs,
):
    weights, refs = refs[:inputs], refs[inputs:]
    (
        turned_ref,
        act_ref,
        slope_ref,
        unit1_ref,
        scale1_ref,
        unit2_ref,
        scale2_ref,
        output_ref,
        *more,
        acc_ref,
        low_ref,
        line_ref,
    ) = refs[: 11 + (2 if load else 0)]
    step = pl.program_id(0)
    last = pl.num_programs(0) - 1
    rows, width = tok_ref.shape
    sub = 256
    if load:
        up_all, down_all, sems, out_sems = refs[13:]
        each = down_all.shape[0] // up_all.shape[0]
        stores = [
            pltpu.make_async_copy(up_all, more[0], out_sems.at[0]),
            pltpu.make_async_copy(down_all, more[1], out_sems.at[1]),
        ]

        def up_part(cols):
            return up_all[step, :, cols]

        def down_part(cols):
            return down_all[pl.ds(step * each, each), :, cols].reshape(width, sub)

    else:

        def up_part(cols):
            return weights[0][0, :, cols]

        def down_part(cols):
            return weights[1][:, :, cols].reshape(width, sub)

    @pl.when(step == 0)
    def _():
        if load:
            copies = load(weights, up_all, down_all, place_ref, sems)
        for m in range(rows // sub):
            at = slice(m * sub, (m + 1) * sub)
            inner = tok_ref[at].astype(F32) + (
                nn(ctx_ref[at], out_w_ref[0]) + vec_ref[OUT_BIAS : OUT_BIAS + 1]
            )
            unit, scale = norm_stats(inner)
            first = unit * vec_ref[ATTN_GAIN : ATTN_GAIN + 1] + vec_ref[ATTN_SHIFT : ATTN_SHIFT + 1]
            unit1_ref[at] = unit.astype(BF)
            scale1_ref[at] = scale
            low = first.astype(BF)
            low_ref[at] = low
            turned_ref[:, at] = low.T
            acc_ref[at] = first + vec_ref[DOWN_BIAS : DOWN_BIAS + 1]
        if load:
            for copy in copies:
                copy.wait()
            for store in stores:
                store.start()

    tiles = [(m, n) for m in range(rows // sub) for n in range(width // sub)]

    def rows_of(m):
        return slice(m * sub, (m + 1) * sub)

    def first_product(tile):
        return nn(low_ref[rows_of(tile[0])], up_part(rows_of(tile[1])))

    def second_product(m, n):
        at, cols = rows_of(m), rows_of(n)
        acc_ref[at, cols] += nn(line_ref[m % 2], down_part(cols))

    ahead = first_product(tiles[0])
    for index, (m, n) in enumerate(tiles):
        at, cols = rows_of(m), rows_of(n)
        hidden = ahead + up_b_ref[:, cols]
        if index + 1 < len(tiles):
            ahead = first_product(tiles[index + 1])
        if m > 0:
            second_product(m - 1, n)
        act, slope = gelu_parts(hidden)
        act = act.astype(BF)
        line_ref[m % 2, :, cols] = act
        act_ref[cols, at] = act.T
        slope_ref[at, cols] = slope.astype(BF)
    for n in range(width // sub):
        second_product(rows // sub - 1, n)

    @pl.when(step == last)
    def _():
        for seq in range(rows // length):
            at = slice(seq * length, (seq + 1) * length)
            active = (exit_ref[seq] >= LAYER).astype(F32)
            unit, scale = norm_stats(acc_ref[at])
            unit2_ref[at] = unit.astype(BF)
            scale2_ref[at] = scale
            result = (
                unit * vec_ref[BLOCK_GAIN : BLOCK_GAIN + 1] + vec_ref[BLOCK_SHIFT : BLOCK_SHIFT + 1]
            ) * active
            output_ref[at] = result.astype(BF)
        if load:
            for store in stores:
                store.wait()


def feed(place, exit_layer, tokens, ctx, out_w, vec, up_bias, weights, load, shapes, length):
    rows, width = tokens.shape
    hidden = up_bias.shape[1]
    steps = hidden // width
    whole = full((rows, width))
    if load:
        weight_specs = [pl.BlockSpec(memory_space=pl.ANY)] * len(weights)
        more_specs = [pl.BlockSpec(memory_space=pl.ANY)] * 2
        more = [jax.ShapeDtypeStruct(shape, BF) for shape in shapes]
        copies = 2 * shapes[1][0] * shapes[0][0]
        scratch = [pltpu.VMEM(shape, BF) for shape in shapes] + [
            pltpu.SemaphoreType.DMA((copies,)),
            pltpu.SemaphoreType.DMA((2,)),
        ]
    else:
        weight_specs = [
            pl.BlockSpec((1, width, width), lambda i: (i, 0, 0)),
            pl.BlockSpec((1, width, width), lambda i: (i, 0, 0)),
        ]
        more_specs, more, scratch = [], [], []
    return pl.pallas_call(
        functools.partial(feed_kernel, length, load, len(weights)),
        grid=(steps,),
        in_specs=[
            pl.BlockSpec(memory_space=pltpu.SMEM),
            pl.BlockSpec(memory_space=pltpu.SMEM),
            whole,
            whole,
            pl.BlockSpec((1, width, width), lambda i: (3, 0, 0)),
            full(vec.shape),
            pl.BlockSpec((1, width), lambda i: (0, i)),
        ]
        + weight_specs,
        out_specs=[
            full((width, rows)),
            pl.BlockSpec((width, rows), lambda i: (i, 0)),
            pl.BlockSpec((rows, width), lambda i: (0, i)),
            whole,
            full((rows, 1)),
            whole,
            full((rows, 1)),
            whole,
        ]
        + more_specs,
        out_shape=[
            jax.ShapeDtypeStruct((width, rows), BF),
            jax.ShapeDtypeStruct((hidden, rows), BF),
            jax.ShapeDtypeStruct((rows, hidden), BF),
            jax.ShapeDtypeStruct((rows, width), BF),
            jax.ShapeDtypeStruct((rows, 1), F32),
            jax.ShapeDtypeStruct((rows, width), BF),
            jax.ShapeDtypeStruct((rows, 1), F32),
            jax.ShapeDtypeStruct((rows, width), BF),
        ]
        + more,
        scratch_shapes=[
            pltpu.VMEM((rows, width), F32),
            pltpu.VMEM((rows, width), BF),
            pltpu.VMEM((2, 256, width), BF),
        ]
        + scratch,
        compiler_params=params(),
        cost_estimate=cost(18 * rows * width * width, 40 * rows * width, 8 * rows * width),
        name="feed",
    )(place, exit_layer, tokens, ctx, out_w, vec, up_bias, *weights)


def load_second(counts, chips, reps, part, weights, up_all, down_all, place_ref, sems):
    at = 0
    groups = []
    for number in counts:
        groups.append(weights[at : at + number])
        at += number
    copies = []

    def start(source, target):
        copies.append(pltpu.make_async_copy(source, target, sems.at[len(copies)]))
        copies[-1].start()

    second_plan(
        start,
        groups,
        (up_all, down_all),
        place_ref[0],
        place_ref[1],
        place_ref[2],
        chips,
        reps,
        part,
    )
    return copies


def leave_kernel(
    length,
    classes,
    exit_ref,
    output_ref,
    unit2_ref,
    scale2_ref,
    grad_ref,
    pool_ref,
    vec_ref,
    class_bias_ref,
    logit_grad_ref,
    act_ref,
    outer_ref,
    branch_ref,
    joint_grad_ref,
    sums_ref,
    class_grad_ref,
    logits_ref,
    stats_ref,
    lead_ref,
    pool_grad_ref,
):
    step = pl.program_id(0)
    rows, width = output_ref.shape
    pool = pool_ref[...].reshape(width, width)
    count = rows // length

    @pl.when(step == 0)
    def _():
        place = lax.broadcasted_iota(jnp.int32, (count, 1), 0)
        active = jnp.zeros((count, 1), F32)
        for seq in range(count):
            on = (exit_ref[seq] >= LAYER).astype(F32)
            active = jnp.where(place == seq, on, active)
        leading = jnp.concatenate(
            [output_ref[seq * length : seq * length + 1].astype(F32) for seq in range(count)],
            axis=0,
        ).astype(BF)
        pooled = jnp.tanh(nn(leading, pool) + vec_ref[POOL_BIAS : POOL_BIAS + 1])
        pooled_low = pooled.astype(BF)
        used = lax.broadcasted_iota(jnp.int32, (8, width), 0) < classes
        class_rows = jnp.where(used, vec_ref[CLASS_ROWS : CLASS_ROWS + 8], 0.0).astype(BF)
        raw = nt(pooled_low, class_rows) + class_bias_ref[...]
        lane = lax.broadcasted_iota(jnp.int32, raw.shape, 1) < classes
        top = jnp.max(jnp.where(lane, raw, -jnp.inf), axis=-1, keepdims=True)
        spread = jnp.where(lane, jnp.exp(raw - top), 0.0)
        logprob = raw - top - jnp.log(jnp.sum(spread, axis=-1, keepdims=True))
        entropy = -jnp.sum(
            jnp.where(lane, jnp.exp(logprob) * logprob, 0.0), axis=-1, keepdims=True
        )
        logits_ref[...] = raw * active
        class_grad = (logit_grad_ref[...].astype(F32) * active).astype(BF)
        stats_ref[0:1] = jnp.broadcast_to(jnp.sum(entropy * active, axis=0, keepdims=True), (1, 8))
        stats_ref[1:2] = jnp.sum(class_grad.astype(F32), axis=0, keepdims=True)
        class_grad_ref[...] = tn(class_grad, pooled_low)
        pooled_grad = nn(class_grad, class_rows)
        pre_grad = (pooled_grad * (1.0 - pooled * pooled)).astype(BF)
        sums_ref[3:4] = jnp.sum(pre_grad.astype(F32), axis=0, keepdims=True)
        pool_grad_ref[...] = tn(leading, pre_grad).reshape(pool_grad_ref.shape).astype(BF)
        lead_ref[...] = nt(pre_grad, pool)
        head = lax.broadcasted_iota(jnp.int32, (length, 1), 0) == 0
        gain = vec_ref[BLOCK_GAIN : BLOCK_GAIN + 1]
        gain_sum = jnp.zeros((1, width), F32)
        shift_sum = jnp.zeros((1, width), F32)
        bias_sum = jnp.zeros((1, width), F32)
        for seq in range(count):
            at = slice(seq * length, (seq + 1) * length)
            on = (exit_ref[seq] >= LAYER).astype(F32)
            top_grad = (
                grad_ref[at].astype(F32) + jnp.where(head, lead_ref[seq : seq + 1], 0.0)
            ) * on
            unit = unit2_ref[at].astype(F32)
            outer = norm_back(top_grad, unit, scale2_ref[at], gain)
            branch = outer.astype(BF)
            outer_ref[at] = outer
            branch_ref[at] = branch
            gain_sum += jnp.sum(top_grad * unit, axis=0, keepdims=True)
            shift_sum += jnp.sum(top_grad, axis=0, keepdims=True)
            bias_sum += jnp.sum(branch.astype(F32), axis=0, keepdims=True)
        sums_ref[0:1] = gain_sum
        sums_ref[1:2] = shift_sum
        sums_ref[2:3] = bias_sum

    @pl.when(step > 0)
    def _():
        few, both, _ = joint_grad_ref.shape
        deep = width // few
        value = nn(act_ref[...], branch_ref[...])
        for at in range(few):
            joint_grad_ref[at, 0:deep] = value[at * deep : (at + 1) * deep].astype(BF)
            joint_grad_ref[at, deep:both] = pool_grad_ref[(step - 1) * few + at]


def leave(
    exit_layer, output, unit2, scale2, output_grad, pool, vec, class_bias, logit_grad, act,
    pool_spec, shards, length, classes,
):
    rows, width = output.shape
    count = rows // length
    hidden = act.shape[0]
    steps = hidden // width
    few = shards // steps
    both = (hidden + width) // shards
    whole = full((rows, width))
    return pl.pallas_call(
        functools.partial(leave_kernel, length, classes),
        grid=(steps + 1,),
        in_specs=[
            pl.BlockSpec(memory_space=pltpu.SMEM),
            whole,
            whole,
            full((rows, 1)),
            whole,
            pool_spec,
            full(vec.shape),
            full(class_bias.shape),
            full(logit_grad.shape),
            pl.BlockSpec((width, rows), lambda i: (jnp.maximum(i - 1, 0), 0)),
        ],
        out_specs=[
            whole,
            whole,
            pl.BlockSpec((few, both, width), lambda i: (jnp.maximum(i - 1, 0), 0, 0)),
            full((4, width)),
            full((8, width)),
            full((count, 8)),
            full((2, 8)),
        ],
        out_shape=[
            jax.ShapeDtypeStruct((rows, width), F32),
            jax.ShapeDtypeStruct((rows, width), BF),
            jax.ShapeDtypeStruct((shards, both, width), BF),
            jax.ShapeDtypeStruct((4, width), F32),
            jax.ShapeDtypeStruct((8, width), F32),
            jax.ShapeDtypeStruct((count, 8), F32),
            jax.ShapeDtypeStruct((2, 8), F32),
        ],
        scratch_shapes=[
            pltpu.VMEM((count, width), F32),
            pltpu.VMEM((shards, width // shards, width), BF),
        ],
        compiler_params=params(),
        cost_estimate=cost(8 * rows * width * width, 30 * rows * width),
        name="leave",
    )(
        exit_layer, output, unit2, scale2, output_grad, pool, vec, class_bias, logit_grad, act
    )


def split_cores(value, place_ref, keep_ref, send_ref):
    chips, part, _ = keep_ref.shape
    first = place_ref[2] == 0
    for chip in range(chips):
        even = value[2 * chip * part : (2 * chip + 1) * part]
        odd = value[(2 * chip + 1) * part : (2 * chip + 2) * part]
        keep_ref[chip] = jnp.where(first, even, odd).astype(BF)
        send_ref[chip] = jnp.where(first, odd, even).astype(BF)


def feed_back_kernel(
    place_ref,
    branch_ref,
    slope_ref,
    turned_ref,
    down_ref,
    up_ref,
    outer_ref,
    unit1_ref,
    scale1_ref,
    out_w_ref,
    vec_ref,
    ctx_ref,
    keep_ref,
    send_ref,
    up_sum_ref,
    inner_ref,
    attended_ref,
    ctx_grad_ref,
    sums_ref,
    acc_ref,
    hid_ref,
):
    step = pl.program_id(0)
    rows, width = branch_ref.shape
    sub = 512

    @pl.when(step == 0)
    def _():
        acc_ref[...] = outer_ref[...]

    last = pl.num_programs(0) - 1

    @pl.when(step < last)
    def _():
        total = jnp.zeros((1, width), F32)
        down = down_ref[...].reshape(up_ref.shape[1:])
        ahead = nt(branch_ref[0:sub], down)
        for m in range(rows // sub):
            at = slice(m * sub, (m + 1) * sub)
            hid = (ahead * slope_ref[at].astype(F32)).astype(BF)
            if (m + 1) * sub < rows:
                ahead = nt(branch_ref[(m + 1) * sub : (m + 2) * sub], down)
            hid_ref[at] = hid
            total += jnp.sum(hid.astype(F32), axis=0, keepdims=True)
            acc_ref[at] += nt(hid, up_ref[0])
        up_sum_ref[...] = total
        split_cores(nn(turned_ref[...], hid_ref[...]), place_ref, keep_ref, send_ref)

    @pl.when(step == last)
    def _():
        gain = vec_ref[ATTN_GAIN : ATTN_GAIN + 1]
        gain_sum = jnp.zeros((1, width), F32)
        shift_sum = jnp.zeros((1, width), F32)
        bias_sum = jnp.zeros((1, width), F32)
        for m in range(rows // sub):
            at = slice(m * sub, (m + 1) * sub)
            grad = acc_ref[at]
            unit = unit1_ref[at].astype(F32)
            inner = norm_back(grad, unit, scale1_ref[at], gain)
            attended = inner.astype(BF)
            inner_ref[at] = inner
            attended_ref[at] = attended
            ctx_grad_ref[at] = nt(attended, out_w_ref[0]).astype(BF)
            gain_sum += jnp.sum(grad * unit, axis=0, keepdims=True)
            shift_sum += jnp.sum(grad, axis=0, keepdims=True)
            bias_sum += jnp.sum(attended.astype(F32), axis=0, keepdims=True)
        sums_ref[0:1] = gain_sum
        sums_ref[1:2] = shift_sum
        sums_ref[2:3] = bias_sum
        split_cores(tn(ctx_ref[...], attended_ref[...]), place_ref, keep_ref, send_ref)


def feed_back(place, chips, branch, slope, low, down, down_block, up, outer, unit1, scale1, out_w, vec, ctx):
    rows, width = branch.shape
    hidden = slope.shape[1]
    steps = hidden // width
    whole = full((rows, width))
    end = steps - 1
    part = width // (2 * chips)
    return pl.pallas_call(
        feed_back_kernel,
        grid=(steps + 1,),
        in_specs=[
            pl.BlockSpec(memory_space=pltpu.SMEM),
            whole,
            pl.BlockSpec((rows, width), lambda i: (0, jnp.minimum(i, end))),
            full((width, rows)),
            pl.BlockSpec(down_block, lambda i: (jnp.minimum(i, end), 0, 0)),
            pl.BlockSpec((1, width, width), lambda i: (jnp.minimum(i, end), 0, 0)),
            whole,
            whole,
            full((rows, 1)),
            pl.BlockSpec((1, width, width), lambda i: (3, 0, 0)),
            full(vec.shape),
            whole,
        ],
        out_specs=[
            pl.BlockSpec((chips, part, width), lambda i: (0, 0, i)),
            pl.BlockSpec((chips, part, width), lambda i: (0, 0, i)),
            pl.BlockSpec((1, width), lambda i: (0, jnp.minimum(i, end))),
            whole,
            whole,
            whole,
            full((3, width)),
        ],
        out_shape=[
            jax.ShapeDtypeStruct((chips, part, hidden + width), BF),
            jax.ShapeDtypeStruct((chips, part, hidden + width), BF),
            jax.ShapeDtypeStruct((1, hidden), F32),
            jax.ShapeDtypeStruct((rows, width), F32),
            jax.ShapeDtypeStruct((rows, width), BF),
            jax.ShapeDtypeStruct((rows, width), BF),
            jax.ShapeDtypeStruct((3, width), F32),
        ],
        scratch_shapes=[pltpu.VMEM((rows, width), F32), pltpu.VMEM((rows, width), BF)],
        compiler_params=params(),
        cost_estimate=cost(28 * rows * width * width, 40 * rows * width),
        name="feed_back",
    )(place, branch, slope, low, down, up, outer, unit1, scale1, out_w, vec, ctx)


def attend_back_kernel(length, joined_ref, probs_ref, ctx_grad_ref, grad_ref, sum_ref):
    rows, width = ctx_grad_ref.shape
    pairs = width // PAIR

    def one(seq, carry):
        at = pl.ds(pl.multiple_of(seq * length, length), length)

        def columns(part, pair):
            return slice(part * width + pair * PAIR, part * width + (pair + 1) * PAIR)

        prob_grads = []
        for pair in range(pairs):
            vals = split_heads(joined_ref[at, columns(2, pair)])
            prob_grads.append(nt(vals, ctx_grad_ref[at, columns(0, pair)]))
        score_grads = []
        for pair in range(pairs):
            probs = probs_ref[seq, pair]
            halves = []
            for head in range(2):
                cut = slice(head * length, (head + 1) * length)
                held = probs[cut].astype(F32)
                part = prob_grads[pair][cut]
                base = jnp.sum(part * held, axis=0, keepdims=True)
                halves.append((held * (part - base)).astype(BF))
            score_grads.append(halves)
        for pair in range(pairs):
            probs = probs_ref[seq, pair]
            beside = jnp.concatenate([probs[:length], probs[length:]], axis=1)
            ctx_grads = split_heads(ctx_grad_ref[at, columns(0, pair)])
            grad_ref[at, columns(2, pair)] = nn(beside, ctx_grads).astype(BF)
        for pair in range(pairs):
            queries = split_heads(joined_ref[at, columns(0, pair)] * jnp.asarray(0.125, BF))
            beside = jnp.concatenate(score_grads[pair], axis=1)
            grad_ref[at, columns(1, pair)] = nn(beside, queries).astype(BF)
        for pair in range(pairs):
            keys = split_heads(joined_ref[at, columns(1, pair)])
            stacked = jnp.concatenate(score_grads[pair], axis=0)
            grad_ref[at, columns(0, pair)] = (tn(stacked, keys) * 0.125).astype(BF)
        return carry

    lax.fori_loop(0, rows // length, one, 0)
    total = jnp.zeros(sum_ref.shape, F32)
    for m in range(rows // length):
        total += jnp.sum(
            grad_ref[m * length : (m + 1) * length].astype(F32), axis=0, keepdims=True
        )

    @pl.when(pl.program_id(0) == 0)
    def _():
        sum_ref[...] = total

    @pl.when(pl.program_id(0) > 0)
    def _():
        sum_ref[...] += total


def attend_back(joined, probs, ctx_grad, length):
    rows, width = ctx_grad.shape
    count = rows // length
    steps = 2
    block = rows // steps
    pairs = width // PAIR
    return pl.pallas_call(
        functools.partial(attend_back_kernel, length),
        grid=(steps,),
        in_specs=[
            pl.BlockSpec((block, 3 * width), lambda i: (i, 0)),
            pl.BlockSpec((count // steps, pairs, 2 * length, length), lambda i: (i, 0, 0, 0)),
            pl.BlockSpec((block, width), lambda i: (i, 0)),
        ],
        out_specs=[
            pl.BlockSpec((block, 3 * width), lambda i: (i, 0)),
            full((1, 3 * width)),
        ],
        out_shape=[
            jax.ShapeDtypeStruct((rows, 3 * width), BF),
            jax.ShapeDtypeStruct((1, 3 * width), F32),
        ],
        compiler_params=params(),
        cost_estimate=cost(rows * width, rows * width),
        name="attend_back",
    )(joined, probs, ctx_grad)


def weight_grads_kernel(
    place_ref, tok_ref, joined_ref, small_ref, keep_ref, send_ref, turned_ref
):
    chips, part, _ = keep_ref.shape
    step = pl.program_id(0)
    width = tok_ref.shape[1]
    first = place_ref[2] == 0

    @pl.when(step == 0)
    def _():
        turned_ref[...] = tok_ref[...].T

    value = nn(turned_ref[...], joined_ref[...])
    cols = pl.ds(pl.multiple_of(step * width, width), width)
    for chip in range(chips):
        even = value[2 * chip * part : (2 * chip + 1) * part]
        odd = value[(2 * chip + 1) * part : (2 * chip + 2) * part]
        keep_ref[chip, :, cols] = jnp.where(first, even, odd).astype(BF)
        send_ref[chip, :, cols] = jnp.where(first, odd, even).astype(BF)

    lines = small_ref.shape[1]
    if keep_ref.shape[2] > 3 * width:

        @pl.when(step == 0)
        def _():
            tail = slice(3 * width, keep_ref.shape[2])
            keep_ref[:, :, tail] = jnp.zeros((chips, part, keep_ref.shape[2] - 3 * width), BF)
            send_ref[:, :, tail] = jnp.zeros((chips, part, keep_ref.shape[2] - 3 * width), BF)
            for chip in range(chips):
                even, odd = small_ref[2 * chip], small_ref[2 * chip + 1]
                keep_ref[chip, 0:lines, tail] = jnp.where(first, even, odd).astype(BF)
                send_ref[chip, 0:lines, tail] = jnp.where(first, odd, even).astype(BF)


def weight_grads(place, tokens, joined_grad, small, chips, extra):
    rows, width = tokens.shape
    shape = (chips, width // (2 * chips), 3 * width + extra)
    return pl.pallas_call(
        weight_grads_kernel,
        grid=(3,),
        in_specs=[
            pl.BlockSpec(memory_space=pltpu.SMEM),
            full((rows, width)),
            pl.BlockSpec((rows, width), lambda i: (0, i)),
            full(small.shape),
        ],
        out_specs=[full(shape), full(shape)],
        out_shape=[jax.ShapeDtypeStruct(shape, BF)] * 2,
        scratch_shapes=[pltpu.VMEM((width, rows), BF)],
        compiler_params=params(),
        cost_estimate=cost(rows * width, rows * width),
        name="weight_grads",
    )(place, tokens, joined_grad, small)


def input_kernel(inner_ref, joined_ref, w_ref, out_ref):
    width = inner_ref.shape[1]
    total = inner_ref[...]
    for part in range(3):
        total += nt(joined_ref[:, part * width : (part + 1) * width], w_ref[part])
    out_ref[...] = total.astype(BF)


def input_back(inner, joined_grad, qkv):
    rows, width = inner.shape
    steps = 4
    block = rows // steps
    return pl.pallas_call(
        input_kernel,
        grid=(steps,),
        in_specs=[
            pl.BlockSpec((block, width), lambda i: (i, 0)),
            pl.BlockSpec((block, 3 * width), lambda i: (i, 0)),
            full((3, width, width)),
        ],
        out_specs=pl.BlockSpec((block, width), lambda i: (i, 0)),
        out_shape=jax.ShapeDtypeStruct((rows, width), BF),
        compiler_params=params(),
        cost_estimate=cost(rows * width, rows * width),
        name="input_back",
    )(inner, joined_grad, qkv)


def lay_kernel(plan, chips, reps, part, counts, place_ref, *refs):
    at = 0
    groups = []
    for number in counts:
        groups.append(refs[at : at + number])
        at += number
    sems = refs[-1]
    rep, chip, core = place_ref[0], place_ref[1], place_ref[2]
    copies = []

    def start(source, target):
        copies.append(pltpu.make_async_copy(source, target, sems.at[len(copies)]))
        copies[-1].start()

    finish = plan(start, groups, refs[at:-1], rep, chip, core, chips, reps, part)
    for copy in copies:
        copy.wait()
    if finish is not None:
        finish()


def blocks_plan(
    put, own, twin, along, across, swapped, depth, first, rep, chip, core, chips, reps, part
):
    for block in range(reps):
        put(own(block), block, chip, core)
        put(twin(block), block, chip, 1 - core)
    for step in range(1, chips):
        source = lax.rem(chip + chips - step, chips)
        rows = pl.ds((step - 1) * depth + first, part)
        for other, block in along.items():
            put(block(step, source, 0), rep ^ other, source, core)
            put(block(step, source, 1), rep ^ other, source, 1 - core)
        for other in across:
            put(across[other].at[rows], rep ^ other, source, core)
            put(swapped[other].at[rows], rep ^ other, source, 1 - core)


def wide_put(start, out_ref, part):
    def put(source, block, at_chip, at_core):
        row = pl.multiple_of((at_chip * 2 + at_core) * part, part)
        start(source, out_ref.at[block, pl.ds(row, part)])

    return put


def wide_block(ref, width, part):
    return lambda block: ref.at[pl.ds(0, part), pl.ds(block * width, width)]


def first_plan(start, groups, outs, rep, chip, core, chips, reps, part):
    (own, twin), along, across, swapped, (extra,) = groups
    out_ref, vec_ref, more_ref = outs
    width = out_ref.shape[2]

    def near(step, source, side):
        if side == 0:
            return along[step - 1].at[pl.ds(0, part)]
        return swapped[0].at[pl.ds((step - 1) * part, part)]

    blocks_plan(
        wide_put(start, out_ref, part),
        wide_block(own, width, part),
        wide_block(twin, width, part),
        {0: near},
        {at + 1: ref for at, ref in enumerate(across)},
        {at + 1: ref for at, ref in enumerate(swapped[1:])},
        part,
        0,
        rep,
        chip,
        core,
        chips,
        reps,
        part,
    )
    tail = pl.ds(part, 16)
    cols = pl.ds(0, width)
    start(own.at[tail, cols], more_ref.at[chip * 2 + core])
    start(twin.at[tail, cols], more_ref.at[chip * 2 + 1 - core])
    for step in range(1, chips):
        source = lax.rem(chip + chips - step, chips)
        start(along[step - 1].at[tail], more_ref.at[source * 2 + core])
        start(extra.at[pl.ds((step - 1) * 16, 16)], more_ref.at[source * 2 + 1 - core])

    def finish():
        lane = lax.broadcasted_iota(jnp.int32, (LANES, width), 0)
        place = lax.broadcasted_iota(jnp.int32, (LANES, width), 1)
        total = jnp.zeros((16, width), F32)
        for shard in range(2 * chips):
            there = (place - shard * part == lane) & (lane < part)
            total += nn(more_ref[shard, :, 0:LANES], there.astype(F32).astype(BF))
        vec_ref[...] = total

    return finish


def second_plan(start, groups, outs, rep, chip, core, chips, reps, part):
    (up, up_twin, down, down_twin), (close, far), across, swapped = groups
    up_ref, down_ref = outs
    width = up_ref.shape[2]
    where = (rep, chip, core, chips, reps, part)

    def chained(chain, first):
        def block(step, source, side):
            shard = source * 2 + (core if side == 0 else 1 - core)
            return chain.at[shard, pl.ds(first, part)]

        return block

    across = dict(zip(NEAR, across))
    swapped = dict(zip(NEAR, swapped))
    blocks_plan(
        wide_put(start, up_ref, part),
        wide_block(up, width, part),
        wide_block(up_twin, width, part),
        {0: chained(close, 0), FAR: chained(far, 0)},
        across,
        swapped,
        2 * part,
        0,
        *where,
    )

    def put(source, block, at_chip, at_core):
        row = pl.multiple_of(block * part, part)
        start(source, down_ref.at[at_chip * 2 + at_core, pl.ds(row, part)])

    def tall(ref):
        return lambda block: ref.at[pl.ds(block * part, part)]

    blocks_plan(
        put,
        tall(down),
        tall(down_twin),
        {0: chained(close, part), FAR: chained(far, part)},
        across,
        swapped,
        2 * part,
        part,
        *where,
    )


def lay(plan, place, groups, shapes, scratch, copies, part, chips, reps):
    anywhere = pl.BlockSpec(memory_space=pl.ANY)
    inputs = [ref for group in groups for ref in group]
    return pl.pallas_call(
        functools.partial(
            lay_kernel, plan, chips, reps, part, [len(group) for group in groups]
        ),
        in_specs=[pl.BlockSpec(memory_space=pltpu.SMEM)] + [anywhere] * len(inputs),
        out_specs=[pl.BlockSpec(memory_space=pltpu.VMEM)] * len(shapes),
        out_shape=[jax.ShapeDtypeStruct(shape, kind) for shape, kind in shapes],
        scratch_shapes=[pltpu.VMEM(shape, BF) for shape in scratch]
        + [pltpu.SemaphoreType.DMA((copies,))],
        compiler_params=pltpu.CompilerParams(vmem_limit_bytes=VMEM_BYTES),
        cost_estimate=cost(0, 4 * sum(math.prod(shape) for shape, kind in shapes)),
        name="lay",
    )(place, *inputs)


def pack_vectors(rows, up_bias, class_weight):
    part = rows[0].shape[0]
    lines = [row[None] for row in rows[:8]] + [class_weight.T] + [row[None] for row in rows[8:]]
    pieces = up_bias.shape[0] // part
    lines += [up_bias[None, at * part : (at + 1) * part] for at in range(pieces)]
    return jnp.concatenate(lines, axis=0)


def move(values, reps, chips, target):
    pairs = []
    for rep in range(reps):
        for chip in range(chips):
            for core in range(2):
                to_rep, to_chip, to_core = target(rep, chip, core)
                pairs.append(
                    (
                        (rep * chips + chip) * 2 + core,
                        (to_rep * chips + to_chip) * 2 + to_core,
                    )
                )
    return lax.ppermute(values, ("rep", "fsdp"), pairs)


def along_chips(step, chips):
    return lambda rep, chip, core: (rep, (chip + step) % chips, core)


def across_reps(other):
    return lambda rep, chip, core: (rep ^ other, chip, core)


def to_twin(rep, chip, core):
    return rep, chip, 1 - core


def after(values, *gates):
    return lax.optimization_barrier((values, *gates))[0]


def along_z(mine, reps, chips):
    return [move(mine, reps, chips, along_chips(step, chips)) for step in range(1, chips)]


def over_reps(stacked, reps, chips, others):
    return [move(stacked, reps, chips, across_reps(other)) for other in others]


def pick(parts, at):
    return lax.dynamic_index_in_dim(parts, at, axis=0, keepdims=False)


def in_order(rep, reps, own, others, axis):
    blocks = jnp.stack([own] + others)
    return jnp.concatenate([pick(blocks, rep ^ at) for at in range(reps)], axis=axis)


class Reduction:
    def __init__(self, place, keep, send, reps, chips):
        self.rep, self.chip = place[0], place[1]
        self.reps, self.chips = reps, chips
        self.keep = keep
        self.got = move(send, reps, chips, to_twin)

    def at_rep(self, at):
        return lax.dynamic_index_in_dim(self.both, at, axis=1, keepdims=False)

    def over_reps(self):
        chips, rows, width = self.keep.shape
        both = (self.keep.astype(F32) + self.got.astype(F32)).astype(BF)
        self.both = lax.optimization_barrier(both).reshape(
            chips, self.reps, rows // self.reps, width
        )
        self.arrived = [self.over_rep(other) for other in NEAR]

    def over_rep(self, other, *gates):
        block = self.at_rep(self.rep ^ other)
        if gates:
            block = after(block, *gates)
        return move(block, self.reps, self.chips, across_reps(other))

    def over_far(self, *gates):
        self.arrived = self.arrived + [self.over_rep(FAR, *gates)]

    def over_chips(self, *gates):
        if gates:
            self.arrived = [after(block, *gates) for block in self.arrived]
        total = self.at_rep(self.rep).astype(F32)
        for block in self.arrived:
            total = total + block.astype(F32)
        self.total = pick(total, self.chip)
        self.passed = [
            move(
                pick(total, lax.rem(self.chip + step, self.chips)).astype(BF),
                self.reps,
                self.chips,
                along_chips(step, self.chips),
            )
            for step in range(1, self.chips)
        ]

    def chip_sum(self):
        total = self.total
        for block in self.passed:
            total = total + block.astype(F32)
        return total.astype(BF)


def share_reps(place, total, reps, chips):
    others = [move(total, reps, chips, across_reps(other)) for other in range(1, reps)]
    return in_order(place[0], reps, total, others, 0).astype(F32), others


def exchange_reps(place, rows, reps, chips):
    rep = place[0]
    parts = rows.reshape(reps, -1, rows.shape[1])
    total = pick(parts, rep).astype(F32)
    arrived = [
        move(pick(parts, rep ^ other), reps, chips, across_reps(other))
        for other in range(1, reps)
    ]
    for block in arrived:
        total = total + block.astype(F32)
    return total.astype(BF), arrived


def per_device(
    tokens,
    exit_layer,
    qkv_weight,
    query_bias,
    value_bias,
    out_weight,
    out_bias,
    attn_gain,
    attn_shift,
    up_weight,
    up_bias,
    down_weight,
    down_bias,
    block_gain,
    block_shift,
    pool_weight,
    pool_bias,
    class_weight,
    class_bias,
    output_grad,
    logit_grad,
):
    reps = lax.axis_size("rep")
    shards = lax.axis_size("fsdp")
    mine = lax.axis_index("fsdp")
    rows, width = tokens.shape
    count = exit_layer.shape[0]
    length = rows // count
    classes = class_weight.shape[1]
    part = out_weight.shape[0]
    hidden = up_weight.shape[1]

    def gather(shard):
        return lax.all_gather(shard, "fsdp", axis=0, tiled=True)

    packed = pack_vectors(
        [
            query_bias,
            value_bias,
            out_bias,
            attn_gain,
            attn_shift,
            down_bias,
            block_gain,
            block_shift,
            pool_bias,
        ],
        up_bias,
        class_weight,
    )
    joint_own = jnp.concatenate([qkv_weight, out_weight], axis=1)
    deep = down_weight.shape[0]
    chips = shards // 2
    place = jnp.stack([lax.axis_index("rep"), mine // 2, mine % 2]).astype(jnp.int32)
    direct = (
        part % 16 == 0
        and reps & (reps - 1) == 0
        and reps * width == hidden
        and reps == 4
        and packed.shape[0] <= 16
    )
    if direct:
        lines = packed.shape[0]
        held = jnp.pad(packed, ((0, 16 - lines), (0, width - part)))
        own = jnp.concatenate([joint_own, jnp.tile(held, (1, reps))], axis=0)
        rep = place[0]

        def block_of(weights, at):
            return lax.dynamic_slice_in_dim(weights, at * width, width, axis=1)

        def second_of(at):
            return [
                block_of(up_weight, at),
                lax.dynamic_slice_in_dim(down_weight, at * part, part, axis=0),
            ]

        along = along_z(block_of(own, rep), reps, chips)
        chain = gather(after(jnp.concatenate(second_of(rep), axis=0), *along))
        chain = chain.reshape(chips, 2, 2 * part, width)
        twin = move(own, reps, chips, to_twin)
        stacked = jnp.concatenate([rows_[:part] for rows_ in along], axis=0)
        across = over_reps(stacked, reps, chips, range(1, reps))
        far_chain = gather(after(jnp.concatenate(second_of(rep ^ FAR), axis=0), *across))
        swapped = [move(rows_, reps, chips, to_twin) for rows_ in [stacked] + across]
        extra = move(
            jnp.concatenate([rows_[part:] for rows_ in along], axis=0), reps, chips, to_twin
        )
        up_twin = move(up_weight, reps, chips, to_twin)
        down_twin = move(down_weight, reps, chips, to_twin)
        joint, vec = lay(
            first_plan,
            place,
            [
                [own, twin],
                along,
                across,
                swapped,
                [extra],
            ],
            [((reps, width, width), BF), ((16, width), F32)],
            [(shards, 16, width)],
            2 * chips * (reps + 1),
            part,
            chips,
            reps,
        )
        mine_chain = lax.dynamic_index_in_dim(
            after(chain, joint), place[2], axis=1, keepdims=False
        )
        second_stacked = jnp.concatenate(
            [
                pick(mine_chain, lax.rem(place[1] + chips - step, chips))
                for step in range(1, chips)
            ],
            axis=0,
        )
        second_across = over_reps(after(second_stacked, *across), reps, chips, NEAR)
        up_row = (
            vec[VECTOR_ROWS:lines].reshape(-1, shards, part).transpose(1, 0, 2).reshape(1, hidden)
        )
        down_block = (width // deep, deep, width)
    else:
        small = gather(packed[None])
        vec = small[:, :VECTOR_ROWS].transpose(1, 0, 2).reshape(VECTOR_ROWS, width).astype(F32)
        vec = jnp.pad(vec, ((0, 16 - VECTOR_ROWS), (0, 0)))
        up_row = small[:, VECTOR_ROWS:].transpose(0, 1, 2).reshape(1, hidden).astype(F32)
        pool = gather(pool_weight)
        joint = jnp.stack(jnp.split(gather(joint_own), 4, axis=1))
        up = jnp.stack(jnp.split(gather(up_weight), hidden // width, axis=1))
        down = gather(down_weight).reshape(-1, width, width)
        down_block = (1, width, width)
    joined, probs, ctx = attend(tokens, joint, vec, length)
    if direct:
        pool = gather(after(pool_weight, ctx))
        far_chain = after(far_chain, ctx)
        second_swapped = [
            move(after(rows_, ctx), reps, chips, to_twin) for rows_ in second_across
        ]
        groups = [
            [up_weight, up_twin, down_weight, down_twin],
            [
                chain.reshape(shards, 2 * part, width),
                far_chain.reshape(shards, 2 * part, width),
            ],
            second_across,
            second_swapped,
        ]
        weights = [ref for group in groups for ref in group]
        load = functools.partial(load_second, [len(group) for group in groups], chips, reps, part)
        shapes = [(reps, width, width), (shards, deep, width)]
    else:
        weights, load, shapes = [up, down], None, None
    turned, act, slope, unit1, scale1, unit2, scale2, output, *laid = feed(
        place, exit_layer, tokens, ctx, joint, vec, up_row, weights, load, shapes, length
    )
    if direct:
        up, down = laid
    class_bias_row = jnp.pad(class_bias.astype(F32), (0, 8 - classes))[None]
    logit_grad_rows = jnp.pad(logit_grad, ((0, 0), (0, 8 - classes)))
    outer, branch, low_grad, exit_sums, class_grad, logits, stats = leave(
        exit_layer,
        output,
        unit2,
        scale2,
        output_grad,
        pool,
        vec,
        class_bias_row,
        logit_grad_rows,
        act,
        full((width, width)),
        shards,
        length,
        classes,
    )
    def scatter(grad):
        return lax.psum_scatter(grad, "fsdp", scatter_dimension=0, tiled=True)

    low_part = scatter(low_grad.reshape(-1, width))
    up_keep, up_send, up_sum, inner, attended, ctx_grad, feed_sums = feed_back(
        place, chips, branch, slope, turned, down, down_block, up, outer, unit1, scale1, joint, vec, ctx
    )
    if direct:
        up_red = Reduction(place, up_keep, up_send, reps, chips)
        up_red.over_reps()
        ctx_grad = after(ctx_grad, up_red.both)
    joined_grad, joined_sum = attend_back(joined, probs, ctx_grad, length)
    joined_seen = joined_grad
    if direct:
        joined_seen = after(joined_grad, low_part, *up_red.arrived)
    sums = jnp.concatenate(
        [
            joined_sum.reshape(3, width)[::2],
            feed_sums,
            exit_sums,
            class_grad[:classes],
        ],
        axis=0,
    )
    lines = sums.shape[0]
    own_sums = sums.reshape(lines, shards, part).transpose(1, 0, 2).reshape(shards, lines * part)
    own_sums = jnp.concatenate([own_sums, up_sum.reshape(shards, deep)], axis=1)
    used = own_sums.shape[1]
    seqs_total = count * reps * shards
    figures = jnp.concatenate([stats[0, :1], stats[1, :classes]])
    slots = reps * shards * figures.shape[0] * 3
    direct = direct and used + slots <= part * LANES
    small_lines = 16
    if direct:
        high = figures.astype(BF).astype(F32)
        middle = (figures - high).astype(BF).astype(F32)
        lowest = figures - high - middle
        split = jnp.concatenate([high, middle, lowest])
        slot = lax.axis_index("rep") * shards + mine
        lone = jnp.where(
            jnp.arange(reps * shards)[:, None] == slot, split[None], 0.0
        ).reshape(1, slots)
        row = jnp.concatenate([own_sums, jnp.broadcast_to(lone, (shards, slots))], axis=1)
        small_lines = -(-row.shape[1] // (LANES * 16)) * 16
        row = jnp.pad(row, ((0, 0), (0, small_lines * LANES - row.shape[1])))
        row = row.reshape(shards, small_lines, LANES)
    else:
        row = jnp.zeros((shards, small_lines, LANES), F32)
    keep, send = weight_grads(
        place, tokens, joined_seen, row, chips, LANES if direct else 0
    )
    input_grad = input_back(inner, joined_grad, joint)

    if direct:
        up_red.over_far(keep)
        joint_red = Reduction(place, keep, send, reps, chips)
        joint_red.over_reps()
        up_red.over_chips()
        joint_red.over_far()
        low_total, low_arrived = exchange_reps(
            place, after(low_part, *joint_red.arrived), reps, chips
        )
        joint_red.over_chips(*up_red.passed)
        wide = (deep + part) * width // part
        up_total = up_red.chip_sum()
        joint_total = joint_red.chip_sum()
        columns = up_total.shape[1]
        others = columns + joint_total.shape[1]
        total, _ = share_reps(
            place,
            jnp.concatenate([up_total, joint_total, low_total.reshape(-1, wide)], axis=1),
            reps,
            chips,
        )
        up_sum = total[:, :columns]
        joint_sum = total[:, columns:others]
        low_sum = total[:, others:].reshape(deep + part, width)
        small_sum = joint_sum[:small_lines, 3 * width :].reshape(-1)
        total = small_sum[used : used + slots].reshape(-1, figures.shape[0]).sum(axis=0)
    else:
        first = mine % 2 == 0

        def whole_of(kept, sent):
            pair = jnp.stack([jnp.where(first, kept, sent), jnp.where(first, sent, kept)], axis=1)
            return pair.reshape(-1, kept.shape[2])

        joint_sum, low_sum, up_sum = lax.psum(
            (scatter(whole_of(keep, send)), low_part, scatter(whole_of(up_keep, up_send))), "rep"
        )
        joint_sum, low_sum, up_sum = (
            joint_sum.astype(F32),
            low_sum.astype(F32),
            up_sum.astype(F32),
        )
        own_sums, total = lax.psum((own_sums, figures), ("rep", "fsdp"))
        small_sum = pick(own_sums, mine)
    own = small_sum[: lines * part].reshape(lines, part)
    return (
        output,
        logits[:, :classes],
        total[0] / seqs_total,
        input_grad,
        joint_sum[:, : 3 * width],
        own[0],
        own[1],
        up_sum[:, hidden:],
        own[4],
        own[2],
        own[3],
        up_sum[:, :hidden],
        small_sum[lines * part : used],
        low_sum[:deep],
        own[7],
        own[5],
        own[6],
        low_sum[deep:],
        own[8],
        own[9 : 9 + classes].T,
        total[1:],
    )


def solution(mesh):
    return jax.shard_map(
        per_device,
        mesh=mesh,
        in_specs=(
            P(("rep", "fsdp"), None),
            P(("rep", "fsdp")),
            P("fsdp", None),
            P("fsdp"),
            P("fsdp"),
            P("fsdp", None),
            P("fsdp"),
            P("fsdp"),
            P("fsdp"),
            P("fsdp", None),
            P("fsdp"),
            P("fsdp", None),
            P("fsdp"),
            P("fsdp"),
            P("fsdp"),
            P("fsdp", None),
            P("fsdp"),
            P("fsdp", None),
            P(),
            P(("rep", "fsdp"), None),
            P(("rep", "fsdp"), None),
        ),
        out_specs=(
            P(("rep", "fsdp"), None),
            P(("rep", "fsdp"), None),
            P(),
            P(("rep", "fsdp"), None),
            P("fsdp", None),
            P("fsdp"),
            P("fsdp"),
            P("fsdp", None),
            P("fsdp"),
            P("fsdp"),
            P("fsdp"),
            P("fsdp", None),
            P("fsdp"),
            P("fsdp", None),
            P("fsdp"),
            P("fsdp"),
            P("fsdp"),
            P("fsdp", None),
            P("fsdp"),
            P("fsdp", None),
            P(),
        ),
        check_vma=False,
    )
```

```python
import functools
import math

import jax
import jax.numpy as jnp
from jax import lax
from jax.experimental import pallas as pl
from jax.experimental.pallas import tpu as pltpu
from jax.sharding import PartitionSpec as P

HD = 64
LAYER = 6
PAIR = 2 * HD
NEAR = (1, 2)
FAR = 3
LANES = 128
VMEM_BYTES = 58 * 2**20
BF = jnp.bfloat16
F32 = jnp.float32

QUERY_BIAS, VALUE_BIAS, OUT_BIAS, ATTN_GAIN, ATTN_SHIFT = 0, 1, 2, 3, 4
DOWN_BIAS, BLOCK_GAIN, BLOCK_SHIFT, CLASS_ROWS, POOL_BIAS = 5, 6, 7, 8, 11
VECTOR_ROWS = 12


def nn(left, right):
    return jnp.dot(left, right, preferred_element_type=F32)


def tn(left, right):
    return lax.dot_general(left, right, (((0,), (0,)), ((), ())), preferred_element_type=F32)


def nt(left, right):
    return lax.dot_general(left, right, (((1,), (1,)), ((), ())), preferred_element_type=F32)


def full(shape):
    return pl.BlockSpec(shape, lambda *at: (0,) * len(shape))


def params():
    return pltpu.CompilerParams(
        dimension_semantics=("arbitrary",), vmem_limit_bytes=VMEM_BYTES
    )


def cost(flops, moved, trans=0):
    return pl.CostEstimate(flops=flops, bytes_accessed=moved, transcendentals=trans)


def split_heads(pair):
    lane = lax.broadcasted_iota(jnp.int32, pair.shape, 1)
    zero = jnp.zeros_like(pair)
    return jnp.concatenate(
        [jnp.where(lane < HD, pair, zero), jnp.where(lane < HD, zero, pair)], axis=0
    )


def norm_stats(values):
    center = values - jnp.mean(values, axis=-1, keepdims=True)
    spread = jnp.mean(center * center, axis=-1, keepdims=True)
    scale = lax.rsqrt(spread + 1e-06)
    return center * scale, scale


def norm_back(grad, unit, scale, gain):
    inner = grad * gain
    first = jnp.mean(inner, axis=-1, keepdims=True)
    second = jnp.mean(inner * unit, axis=-1, keepdims=True)
    return scale * (inner - first - unit * second)


def gelu_parts(values):
    base = 1.0 + 0.23164189 * jnp.abs(values)
    t = pl.reciprocal(base, approx=True)
    t = t * (2.0 - base * t)
    bell = jnp.exp2((values * values) * -0.7213475204444817)
    poly = t * (
        0.127414796
        + t * (-0.142248368 + t * (0.7107068705 + t * (-0.7265760135 + t * 0.5307027145)))
    )
    tail = poly * bell
    below = jnp.where(values >= 0.0, 1.0 - tail, tail)
    return values * below, below + values * (bell * 0.3989422804014327)


def attend_kernel(length, tok_ref, w_ref, vec_ref, joined_ref, probs_ref, ctx_ref):
    rows, width = ctx_ref.shape
    pairs = width // PAIR
    for part in range(3):
        cols = slice(part * width, (part + 1) * width)
        value = nn(tok_ref[...], w_ref[part])
        if part == 0:
            value += vec_ref[QUERY_BIAS : QUERY_BIAS + 1]
        elif part == 2:
            value += vec_ref[VALUE_BIAS : VALUE_BIAS + 1]
        joined_ref[:, cols] = value.astype(BF)

    def one(seq, carry):
        at = pl.ds(pl.multiple_of(seq * length, length), length)
        scores = []
        for pair in range(pairs):
            query = joined_ref[at, pair * PAIR : (pair + 1) * PAIR] * jnp.asarray(0.125, BF)
            keys = split_heads(joined_ref[at, width + pair * PAIR : width + (pair + 1) * PAIR])
            scores.append(nt(keys, query))
        all_probs = []
        for pair in range(pairs):
            halves = []
            for head in range(2):
                part = scores[pair][head * length : (head + 1) * length]
                part = jnp.exp(part - jnp.max(part, axis=0, keepdims=True))
                part = part * (1.0 / jnp.sum(part, axis=0, keepdims=True))
                halves.append(part.astype(BF))
            probs = jnp.concatenate(halves, axis=0)
            probs_ref[seq, pair] = probs
            all_probs.append(probs)
        for pair in range(pairs):
            vals = split_heads(
                joined_ref[at, 2 * width + pair * PAIR : 2 * width + (pair + 1) * PAIR]
            )
            ctx_ref[at, pair * PAIR : (pair + 1) * PAIR] = tn(all_probs[pair], vals).astype(BF)
        return carry

    lax.fori_loop(0, rows // length, one, 0)


def attend(tokens, qkv, vec, length):
    rows, width = tokens.shape
    count = rows // length
    steps = 2
    block = rows // steps
    pairs = width // PAIR
    return pl.pallas_call(
        functools.partial(attend_kernel, length),
        grid=(steps,),
        in_specs=[
            pl.BlockSpec((block, width), lambda i: (i, 0)),
            full((3, width, width)),
            full(vec.shape),
        ],
        out_specs=[
            pl.BlockSpec((block, 3 * width), lambda i: (i, 0)),
            pl.BlockSpec((count // steps, pairs, 2 * length, length), lambda i: (i, 0, 0, 0)),
            pl.BlockSpec((block, width), lambda i: (i, 0)),
        ],
        out_shape=[
            jax.ShapeDtypeStruct((rows, 3 * width), BF),
            jax.ShapeDtypeStruct((count, pairs, 2 * length, length), BF),
            jax.ShapeDtypeStruct((rows, width), BF),
        ],
        compiler_params=params(),
        cost_estimate=cost(8 * rows * width * width, 20 * rows * width, rows * width),
        name="attend",
    )(tokens, qkv, vec)


def feed_kernel(
    length,
    load,
    inputs,
    place_ref,
    exit_ref,
    tok_ref,
    ctx_ref,
    out_w_ref,
    vec_ref,
    up_b_ref,
    *refs,
):
    weights, refs = refs[:inputs], refs[inputs:]
    (
        turned_ref,
        act_ref,
        slope_ref,
        unit1_ref,
        scale1_ref,
        unit2_ref,
        scale2_ref,
        output_ref,
        *more,
        acc_ref,
        low_ref,
        line_ref,
    ) = refs[: 11 + (2 if load else 0)]
    step = pl.program_id(0)
    last = pl.num_programs(0) - 1
    rows, width = tok_ref.shape
    sub = 256
    if load:
        up_all, down_all, sems, out_sems = refs[13:]
        each = down_all.shape[0] // up_all.shape[0]
        stores = [
            pltpu.make_async_copy(up_all, more[0], out_sems.at[0]),
            pltpu.make_async_copy(down_all, more[1], out_sems.at[1]),
        ]

        def up_part(cols):
            return up_all[step, :, cols]

        def down_part(cols):
            return down_all[pl.ds(step * each, each), :, cols].reshape(width, sub)

    else:

        def up_part(cols):
            return weights[0][0, :, cols]

        def down_part(cols):
            return weights[1][:, :, cols].reshape(width, sub)

    @pl.when(step == 0)
    def _():
        if load:
            copies = load(weights, up_all, down_all, place_ref, sems)
        for m in range(rows // sub):
            at = slice(m * sub, (m + 1) * sub)
            inner = tok_ref[at].astype(F32) + (
                nn(ctx_ref[at], out_w_ref[0]) + vec_ref[OUT_BIAS : OUT_BIAS + 1]
            )
            unit, scale = norm_stats(inner)
            first = unit * vec_ref[ATTN_GAIN : ATTN_GAIN + 1] + vec_ref[ATTN_SHIFT : ATTN_SHIFT + 1]
            unit1_ref[at] = unit.astype(BF)
            scale1_ref[at] = scale
            low = first.astype(BF)
            low_ref[at] = low
            turned_ref[:, at] = low.T
            acc_ref[at] = first + vec_ref[DOWN_BIAS : DOWN_BIAS + 1]
        if load:
            for copy in copies:
                copy.wait()
            for store in stores:
                store.start()

    tiles = [(m, n) for m in range(rows // sub) for n in range(width // sub)]

    def rows_of(m):
        return slice(m * sub, (m + 1) * sub)

    def first_product(tile):
        return nn(low_ref[rows_of(tile[0])], up_part(rows_of(tile[1])))

    def second_product(m, n):
        at, cols = rows_of(m), rows_of(n)
        acc_ref[at, cols] += nn(line_ref[m % 2], down_part(cols))

    ahead = first_product(tiles[0])
    for index, (m, n) in enumerate(tiles):
        at, cols = rows_of(m), rows_of(n)
        hidden = ahead + up_b_ref[:, cols]
        if index + 1 < len(tiles):
            ahead = first_product(tiles[index + 1])
        if m > 0:
            second_product(m - 1, n)
        act, slope = gelu_parts(hidden)
        act = act.astype(BF)
        line_ref[m % 2, :, cols] = act
        act_ref[cols, at] = act.T
        slope_ref[at, cols] = slope.astype(BF)
    for n in range(width // sub):
        second_product(rows // sub - 1, n)

    @pl.when(step == last)
    def _():
        for seq in range(rows // length):
            at = slice(seq * length, (seq + 1) * length)
            active = (exit_ref[seq] >= LAYER).astype(F32)
            unit, scale = norm_stats(acc_ref[at])
            unit2_ref[at] = unit.astype(BF)
            scale2_ref[at] = scale
            result = (
                unit * vec_ref[BLOCK_GAIN : BLOCK_GAIN + 1] + vec_ref[BLOCK_SHIFT : BLOCK_SHIFT + 1]
            ) * active
            output_ref[at] = result.astype(BF)
        if load:
            for store in stores:
                store.wait()


def feed(place, exit_layer, tokens, ctx, out_w, vec, up_bias, weights, load, shapes, length):
    rows, width = tokens.shape
    hidden = up_bias.shape[1]
    steps = hidden // width
    whole = full((rows, width))
    if load:
        weight_specs = [pl.BlockSpec(memory_space=pl.ANY)] * len(weights)
        more_specs = [pl.BlockSpec(memory_space=pl.ANY)] * 2
        more = [jax.ShapeDtypeStruct(shape, BF) for shape in shapes]
        copies = 2 * shapes[1][0] * shapes[0][0]
        scratch = [pltpu.VMEM(shape, BF) for shape in shapes] + [
            pltpu.SemaphoreType.DMA((copies,)),
            pltpu.SemaphoreType.DMA((2,)),
        ]
    else:
        weight_specs = [
            pl.BlockSpec((1, width, width), lambda i: (i, 0, 0)),
            pl.BlockSpec((1, width, width), lambda i: (i, 0, 0)),
        ]
        more_specs, more, scratch = [], [], []
    return pl.pallas_call(
        functools.partial(feed_kernel, length, load, len(weights)),
        grid=(steps,),
        in_specs=[
            pl.BlockSpec(memory_space=pltpu.SMEM),
            pl.BlockSpec(memory_space=pltpu.SMEM),
            whole,
            whole,
            pl.BlockSpec((1, width, width), lambda i: (3, 0, 0)),
            full(vec.shape),
            pl.BlockSpec((1, width), lambda i: (0, i)),
        ]
        + weight_specs,
        out_specs=[
            full((width, rows)),
            pl.BlockSpec((width, rows), lambda i: (i, 0)),
            pl.BlockSpec((rows, width), lambda i: (0, i)),
            whole,
            full((rows, 1)),
            whole,
            full((rows, 1)),
            whole,
        ]
        + more_specs,
        out_shape=[
            jax.ShapeDtypeStruct((width, rows), BF),
            jax.ShapeDtypeStruct((hidden, rows), BF),
            jax.ShapeDtypeStruct((rows, hidden), BF),
            jax.ShapeDtypeStruct((rows, width), BF),
            jax.ShapeDtypeStruct((rows, 1), F32),
            jax.ShapeDtypeStruct((rows, width), BF),
            jax.ShapeDtypeStruct((rows, 1), F32),
            jax.ShapeDtypeStruct((rows, width), BF),
        ]
        + more,
        scratch_shapes=[
            pltpu.VMEM((rows, width), F32),
            pltpu.VMEM((rows, width), BF),
            pltpu.VMEM((2, 256, width), BF),
        ]
        + scratch,
        compiler_params=params(),
        cost_estimate=cost(18 * rows * width * width, 40 * rows * width, 8 * rows * width),
        name="feed",
    )(place, exit_layer, tokens, ctx, out_w, vec, up_bias, *weights)


def load_second(counts, chips, reps, part, weights, up_all, down_all, place_ref, sems):
    at = 0
    groups = []
    for number in counts:
        groups.append(weights[at : at + number])
        at += number
    copies = []

    def start(source, target):
        copies.append(pltpu.make_async_copy(source, target, sems.at[len(copies)]))
        copies[-1].start()

    second_plan(
        start,
        groups,
        (up_all, down_all),
        place_ref[0],
        place_ref[1],
        place_ref[2],
        chips,
        reps,
        part,
    )
    return copies


def leave_kernel(
    length,
    classes,
    exit_ref,
    output_ref,
    unit2_ref,
    scale2_ref,
    grad_ref,
    pool_ref,
    vec_ref,
    class_bias_ref,
    logit_grad_ref,
    act_ref,
    outer_ref,
    branch_ref,
    joint_grad_ref,
    sums_ref,
    class_grad_ref,
    logits_ref,
    stats_ref,
    lead_ref,
    pool_grad_ref,
):
    step = pl.program_id(0)
    rows, width = output_ref.shape
    pool = pool_ref[...].reshape(width, width)
    count = rows // length

    @pl.when(step == 0)
    def _():
        place = lax.broadcasted_iota(jnp.int32, (count, 1), 0)
        active = jnp.zeros((count, 1), F32)
        for seq in range(count):
            on = (exit_ref[seq] >= LAYER).astype(F32)
            active = jnp.where(place == seq, on, active)
        leading = jnp.concatenate(
            [output_ref[seq * length : seq * length + 1].astype(F32) for seq in range(count)],
            axis=0,
        ).astype(BF)
        pooled = jnp.tanh(nn(leading, pool) + vec_ref[POOL_BIAS : POOL_BIAS + 1])
        pooled_low = pooled.astype(BF)
        used = lax.broadcasted_iota(jnp.int32, (8, width), 0) < classes
        class_rows = jnp.where(used, vec_ref[CLASS_ROWS : CLASS_ROWS + 8], 0.0).astype(BF)
        raw = nt(pooled_low, class_rows) + class_bias_ref[...]
        lane = lax.broadcasted_iota(jnp.int32, raw.shape, 1) < classes
        top = jnp.max(jnp.where(lane, raw, -jnp.inf), axis=-1, keepdims=True)
        spread = jnp.where(lane, jnp.exp(raw - top), 0.0)
        logprob = raw - top - jnp.log(jnp.sum(spread, axis=-1, keepdims=True))
        entropy = -jnp.sum(
            jnp.where(lane, jnp.exp(logprob) * logprob, 0.0), axis=-1, keepdims=True
        )
        logits_ref[...] = raw * active
        class_grad = (logit_grad_ref[...].astype(F32) * active).astype(BF)
        stats_ref[0:1] = jnp.broadcast_to(jnp.sum(entropy * active, axis=0, keepdims=True), (1, 8))
        stats_ref[1:2] = jnp.sum(class_grad.astype(F32), axis=0, keepdims=True)
        class_grad_ref[...] = tn(class_grad, pooled_low)
        pooled_grad = nn(class_grad, class_rows)
        pre_grad = (pooled_grad * (1.0 - pooled * pooled)).astype(BF)
        sums_ref[3:4] = jnp.sum(pre_grad.astype(F32), axis=0, keepdims=True)
        pool_grad_ref[...] = tn(leading, pre_grad).reshape(pool_grad_ref.shape).astype(BF)
        lead_ref[...] = nt(pre_grad, pool)
        head = lax.broadcasted_iota(jnp.int32, (length, 1), 0) == 0
        gain = vec_ref[BLOCK_GAIN : BLOCK_GAIN + 1]
        gain_sum = jnp.zeros((1, width), F32)
        shift_sum = jnp.zeros((1, width), F32)
        bias_sum = jnp.zeros((1, width), F32)
        for seq in range(count):
            at = slice(seq * length, (seq + 1) * length)
            on = (exit_ref[seq] >= LAYER).astype(F32)
            top_grad = (
                grad_ref[at].astype(F32) + jnp.where(head, lead_ref[seq : seq + 1], 0.0)
            ) * on
            unit = unit2_ref[at].astype(F32)
            outer = norm_back(top_grad, unit, scale2_ref[at], gain)
            branch = outer.astype(BF)
            outer_ref[at] = outer
            branch_ref[at] = branch
            gain_sum += jnp.sum(top_grad * unit, axis=0, keepdims=True)
            shift_sum += jnp.sum(top_grad, axis=0, keepdims=True)
            bias_sum += jnp.sum(branch.astype(F32), axis=0, keepdims=True)
        sums_ref[0:1] = gain_sum
        sums_ref[1:2] = shift_sum
        sums_ref[2:3] = bias_sum

    @pl.when(step > 0)
    def _():
        few, both, _ = joint_grad_ref.shape
        deep = width // few
        value = nn(act_ref[...], branch_ref[...])
        for at in range(few):
            joint_grad_ref[at, 0:deep] = value[at * deep : (at + 1) * deep].astype(BF)
            joint_grad_ref[at, deep:both] = pool_grad_ref[(step - 1) * few + at]


def leave(
    exit_layer, output, unit2, scale2, output_grad, pool, vec, class_bias, logit_grad, act,
    pool_spec, shards, length, classes,
):
    rows, width = output.shape
    count = rows // length
    hidden = act.shape[0]
    steps = hidden // width
    few = shards // steps
    both = (hidden + width) // shards
    whole = full((rows, width))
    return pl.pallas_call(
        functools.partial(leave_kernel, length, classes),
        grid=(steps + 1,),
        in_specs=[
            pl.BlockSpec(memory_space=pltpu.SMEM),
            whole,
            whole,
            full((rows, 1)),
            whole,
            pool_spec,
            full(vec.shape),
            full(class_bias.shape),
            full(logit_grad.shape),
            pl.BlockSpec((width, rows), lambda i: (jnp.maximum(i - 1, 0), 0)),
        ],
        out_specs=[
            whole,
            whole,
            pl.BlockSpec((few, both, width), lambda i: (jnp.maximum(i - 1, 0), 0, 0)),
            full((4, width)),
            full((8, width)),
            full((count, 8)),
            full((2, 8)),
        ],
        out_shape=[
            jax.ShapeDtypeStruct((rows, width), F32),
            jax.ShapeDtypeStruct((rows, width), BF),
            jax.ShapeDtypeStruct((shards, both, width), BF),
            jax.ShapeDtypeStruct((4, width), F32),
            jax.ShapeDtypeStruct((8, width), F32),
            jax.ShapeDtypeStruct((count, 8), F32),
            jax.ShapeDtypeStruct((2, 8), F32),
        ],
        scratch_shapes=[
            pltpu.VMEM((count, width), F32),
            pltpu.VMEM((shards, width // shards, width), BF),
        ],
        compiler_params=params(),
        cost_estimate=cost(8 * rows * width * width, 30 * rows * width),
        name="leave",
    )(
        exit_layer, output, unit2, scale2, output_grad, pool, vec, class_bias, logit_grad, act
    )


def split_cores(value, place_ref, keep_ref, send_ref):
    chips, part, _ = keep_ref.shape
    first = place_ref[2] == 0
    for chip in range(chips):
        even = value[2 * chip * part : (2 * chip + 1) * part]
        odd = value[(2 * chip + 1) * part : (2 * chip + 2) * part]
        keep_ref[chip] = jnp.where(first, even, odd).astype(BF)
        send_ref[chip] = jnp.where(first, odd, even).astype(BF)


def feed_back_kernel(
    place_ref,
    branch_ref,
    slope_ref,
    turned_ref,
    down_ref,
    up_ref,
    outer_ref,
    unit1_ref,
    scale1_ref,
    out_w_ref,
    vec_ref,
    ctx_ref,
    keep_ref,
    send_ref,
    up_sum_ref,
    inner_ref,
    attended_ref,
    ctx_grad_ref,
    sums_ref,
    acc_ref,
    hid_ref,
):
    step = pl.program_id(0)
    rows, width = branch_ref.shape
    sub = 512

    @pl.when(step == 0)
    def _():
        acc_ref[...] = outer_ref[...]

    last = pl.num_programs(0) - 1

    @pl.when(step < last)
    def _():
        total = jnp.zeros((1, width), F32)
        down = down_ref[...].reshape(up_ref.shape[1:])
        ahead = nt(branch_ref[0:sub], down)
        for m in range(rows // sub):
            at = slice(m * sub, (m + 1) * sub)
            hid = (ahead * slope_ref[at].astype(F32)).astype(BF)
            if (m + 1) * sub < rows:
                ahead = nt(branch_ref[(m + 1) * sub : (m + 2) * sub], down)
            hid_ref[at] = hid
            total += jnp.sum(hid.astype(F32), axis=0, keepdims=True)
            acc_ref[at] += nt(hid, up_ref[0])
        up_sum_ref[...] = total
        split_cores(nn(turned_ref[...], hid_ref[...]), place_ref, keep_ref, send_ref)

    @pl.when(step == last)
    def _():
        gain = vec_ref[ATTN_GAIN : ATTN_GAIN + 1]
        gain_sum = jnp.zeros((1, width), F32)
        shift_sum = jnp.zeros((1, width), F32)
        bias_sum = jnp.zeros((1, width), F32)
        for m in range(rows // sub):
            at = slice(m * sub, (m + 1) * sub)
            grad = acc_ref[at]
            unit = unit1_ref[at].astype(F32)
            inner = norm_back(grad, unit, scale1_ref[at], gain)
            attended = inner.astype(BF)
            inner_ref[at] = inner
            attended_ref[at] = attended
            ctx_grad_ref[at] = nt(attended, out_w_ref[0]).astype(BF)
            gain_sum += jnp.sum(grad * unit, axis=0, keepdims=True)
            shift_sum += jnp.sum(grad, axis=0, keepdims=True)
            bias_sum += jnp.sum(attended.astype(F32), axis=0, keepdims=True)
        sums_ref[0:1] = gain_sum
        sums_ref[1:2] = shift_sum
        sums_ref[2:3] = bias_sum
        split_cores(tn(ctx_ref[...], attended_ref[...]), place_ref, keep_ref, send_ref)


def feed_back(place, chips, branch, slope, low, down, down_block, up, outer, unit1, scale1, out_w, vec, ctx):
    rows, width = branch.shape
    hidden = slope.shape[1]
    steps = hidden // width
    whole = full((rows, width))
    end = steps - 1
    part = width // (2 * chips)
    return pl.pallas_call(
        feed_back_kernel,
        grid=(steps + 1,),
        in_specs=[
            pl.BlockSpec(memory_space=pltpu.SMEM),
            whole,
            pl.BlockSpec((rows, width), lambda i: (0, jnp.minimum(i, end))),
            full((width, rows)),
            pl.BlockSpec(down_block, lambda i: (jnp.minimum(i, end), 0, 0)),
            pl.BlockSpec((1, width, width), lambda i: (jnp.minimum(i, end), 0, 0)),
            whole,
            whole,
            full((rows, 1)),
            pl.BlockSpec((1, width, width), lambda i: (3, 0, 0)),
            full(vec.shape),
            whole,
        ],
        out_specs=[
            pl.BlockSpec((chips, part, width), lambda i: (0, 0, i)),
            pl.BlockSpec((chips, part, width), lambda i: (0, 0, i)),
            pl.BlockSpec((1, width), lambda i: (0, jnp.minimum(i, end))),
            whole,
            whole,
            whole,
            full((3, width)),
        ],
        out_shape=[
            jax.ShapeDtypeStruct((chips, part, hidden + width), BF),
            jax.ShapeDtypeStruct((chips, part, hidden + width), BF),
            jax.ShapeDtypeStruct((1, hidden), F32),
            jax.ShapeDtypeStruct((rows, width), F32),
            jax.ShapeDtypeStruct((rows, width), BF),
            jax.ShapeDtypeStruct((rows, width), BF),
            jax.ShapeDtypeStruct((3, width), F32),
        ],
        scratch_shapes=[pltpu.VMEM((rows, width), F32), pltpu.VMEM((rows, width), BF)],
        compiler_params=params(),
        cost_estimate=cost(28 * rows * width * width, 40 * rows * width),
        name="feed_back",
    )(place, branch, slope, low, down, up, outer, unit1, scale1, out_w, vec, ctx)


def attend_back_kernel(length, joined_ref, probs_ref, ctx_grad_ref, grad_ref, sum_ref):
    rows, width = ctx_grad_ref.shape
    pairs = width // PAIR

    def one(seq, carry):
        at = pl.ds(pl.multiple_of(seq * length, length), length)

        def columns(part, pair):
            return slice(part * width + pair * PAIR, part * width + (pair + 1) * PAIR)

        prob_grads = []
        for pair in range(pairs):
            vals = split_heads(joined_ref[at, columns(2, pair)])
            prob_grads.append(nt(vals, ctx_grad_ref[at, columns(0, pair)]))
        score_grads = []
        for pair in range(pairs):
            probs = probs_ref[seq, pair]
            halves = []
            for head in range(2):
                cut = slice(head * length, (head + 1) * length)
                held = probs[cut].astype(F32)
                part = prob_grads[pair][cut]
                base = jnp.sum(part * held, axis=0, keepdims=True)
                halves.append((held * (part - base)).astype(BF))
            score_grads.append(halves)
        for pair in range(pairs):
            probs = probs_ref[seq, pair]
            beside = jnp.concatenate([probs[:length], probs[length:]], axis=1)
            ctx_grads = split_heads(ctx_grad_ref[at, columns(0, pair)])
            grad_ref[at, columns(2, pair)] = nn(beside, ctx_grads).astype(BF)
        for pair in range(pairs):
            queries = split_heads(joined_ref[at, columns(0, pair)] * jnp.asarray(0.125, BF))
            beside = jnp.concatenate(score_grads[pair], axis=1)
            grad_ref[at, columns(1, pair)] = nn(beside, queries).astype(BF)
        for pair in range(pairs):
            keys = split_heads(joined_ref[at, columns(1, pair)])
            stacked = jnp.concatenate(score_grads[pair], axis=0)
            grad_ref[at, columns(0, pair)] = (tn(stacked, keys) * 0.125).astype(BF)
        return carry

    lax.fori_loop(0, rows // length, one, 0)
    total = jnp.zeros(sum_ref.shape, F32)
    for m in range(rows // length):
        total += jnp.sum(
            grad_ref[m * length : (m + 1) * length].astype(F32), axis=0, keepdims=True
        )

    @pl.when(pl.program_id(0) == 0)
    def _():
        sum_ref[...] = total

    @pl.when(pl.program_id(0) > 0)
    def _():
        sum_ref[...] += total


def attend_back(joined, probs, ctx_grad, length):
    rows, width = ctx_grad.shape
    count = rows // length
    steps = 2
    block = rows // steps
    pairs = width // PAIR
    return pl.pallas_call(
        functools.partial(attend_back_kernel, length),
        grid=(steps,),
        in_specs=[
            pl.BlockSpec((block, 3 * width), lambda i: (i, 0)),
            pl.BlockSpec((count // steps, pairs, 2 * length, length), lambda i: (i, 0, 0, 0)),
            pl.BlockSpec((block, width), lambda i: (i, 0)),
        ],
        out_specs=[
            pl.BlockSpec((block, 3 * width), lambda i: (i, 0)),
            full((1, 3 * width)),
        ],
        out_shape=[
            jax.ShapeDtypeStruct((rows, 3 * width), BF),
            jax.ShapeDtypeStruct((1, 3 * width), F32),
        ],
        compiler_params=params(),
        cost_estimate=cost(rows * width, rows * width),
        name="attend_back",
    )(joined, probs, ctx_grad)


def weight_grads_kernel(
    place_ref, tok_ref, joined_ref, small_ref, keep_ref, send_ref, turned_ref
):
    chips, part, _ = keep_ref.shape
    step = pl.program_id(0)
    width = tok_ref.shape[1]
    first = place_ref[2] == 0

    @pl.when(step == 0)
    def _():
        turned_ref[...] = tok_ref[...].T

    value = nn(turned_ref[...], joined_ref[...])
    cols = pl.ds(pl.multiple_of(step * width, width), width)
    for chip in range(chips):
        even = value[2 * chip * part : (2 * chip + 1) * part]
        odd = value[(2 * chip + 1) * part : (2 * chip + 2) * part]
        keep_ref[chip, :, cols] = jnp.where(first, even, odd).astype(BF)
        send_ref[chip, :, cols] = jnp.where(first, odd, even).astype(BF)

    lines = small_ref.shape[1]
    if keep_ref.shape[2] > 3 * width:

        @pl.when(step == 0)
        def _():
            tail = slice(3 * width, keep_ref.shape[2])
            keep_ref[:, :, tail] = jnp.zeros((chips, part, keep_ref.shape[2] - 3 * width), BF)
            send_ref[:, :, tail] = jnp.zeros((chips, part, keep_ref.shape[2] - 3 * width), BF)
            for chip in range(chips):
                even, odd = small_ref[2 * chip], small_ref[2 * chip + 1]
                keep_ref[chip, 0:lines, tail] = jnp.where(first, even, odd).astype(BF)
                send_ref[chip, 0:lines, tail] = jnp.where(first, odd, even).astype(BF)


def weight_grads(place, tokens, joined_grad, small, chips, extra):
    rows, width = tokens.shape
    shape = (chips, width // (2 * chips), 3 * width + extra)
    return pl.pallas_call(
        weight_grads_kernel,
        grid=(3,),
        in_specs=[
            pl.BlockSpec(memory_space=pltpu.SMEM),
            full((rows, width)),
            pl.BlockSpec((rows, width), lambda i: (0, i)),
            full(small.shape),
        ],
        out_specs=[full(shape), full(shape)],
        out_shape=[jax.ShapeDtypeStruct(shape, BF)] * 2,
        scratch_shapes=[pltpu.VMEM((width, rows), BF)],
        compiler_params=params(),
        cost_estimate=cost(rows * width, rows * width),
        name="weight_grads",
    )(place, tokens, joined_grad, small)


def input_kernel(inner_ref, joined_ref, w_ref, out_ref):
    width = inner_ref.shape[1]
    total = inner_ref[...]
    for part in range(3):
        total += nt(joined_ref[:, part * width : (part + 1) * width], w_ref[part])
    out_ref[...] = total.astype(BF)


def input_back(inner, joined_grad, qkv):
    rows, width = inner.shape
    steps = 4
    block = rows // steps
    return pl.pallas_call(
        input_kernel,
        grid=(steps,),
        in_specs=[
            pl.BlockSpec((block, width), lambda i: (i, 0)),
            pl.BlockSpec((block, 3 * width), lambda i: (i, 0)),
            full((3, width, width)),
        ],
        out_specs=pl.BlockSpec((block, width), lambda i: (i, 0)),
        out_shape=jax.ShapeDtypeStruct((rows, width), BF),
        compiler_params=params(),
        cost_estimate=cost(rows * width, rows * width),
        name="input_back",
    )(inner, joined_grad, qkv)


def lay_kernel(plan, chips, reps, part, counts, place_ref, *refs):
    at = 0
    groups = []
    for number in counts:
        groups.append(refs[at : at + number])
        at += number
    sems = refs[-1]
    rep, chip, core = place_ref[0], place_ref[1], place_ref[2]
    copies = []

    def start(source, target):
        copies.append(pltpu.make_async_copy(source, target, sems.at[len(copies)]))
        copies[-1].start()

    finish = plan(start, groups, refs[at:-1], rep, chip, core, chips, reps, part)
    for copy in copies:
        copy.wait()
    if finish is not None:
        finish()


def blocks_plan(
    put, own, twin, along, across, swapped, depth, first, rep, chip, core, chips, reps, part
):
    for block in range(reps):
        put(own(block), block, chip, core)
        put(twin(block), block, chip, 1 - core)
    for step in range(1, chips):
        source = lax.rem(chip + chips - step, chips)
        rows = pl.ds((step - 1) * depth + first, part)
        for other, block in along.items():
            put(block(step, source, 0), rep ^ other, source, core)
            put(block(step, source, 1), rep ^ other, source, 1 - core)
        for other in across:
            put(across[other].at[rows], rep ^ other, source, core)
            put(swapped[other].at[rows], rep ^ other, source, 1 - core)


def wide_put(start, out_ref, part):
    def put(source, block, at_chip, at_core):
        row = pl.multiple_of((at_chip * 2 + at_core) * part, part)
        start(source, out_ref.at[block, pl.ds(row, part)])

    return put


def wide_block(ref, width, part):
    return lambda block: ref.at[pl.ds(0, part), pl.ds(block * width, width)]


def first_plan(start, groups, outs, rep, chip, core, chips, reps, part):
    (own, twin), along, across, swapped, (extra,) = groups
    out_ref, vec_ref, more_ref = outs
    width = out_ref.shape[2]

    def near(step, source, side):
        if side == 0:
            return along[step - 1].at[pl.ds(0, part)]
        return swapped[0].at[pl.ds((step - 1) * part, part)]

    blocks_plan(
        wide_put(start, out_ref, part),
        wide_block(own, width, part),
        wide_block(twin, width, part),
        {0: near},
        {at + 1: ref for at, ref in enumerate(across)},
        {at + 1: ref for at, ref in enumerate(swapped[1:])},
        part,
        0,
        rep,
        chip,
        core,
        chips,
        reps,
        part,
    )
    tail = pl.ds(part, 16)
    cols = pl.ds(0, width)
    start(own.at[tail, cols], more_ref.at[chip * 2 + core])
    start(twin.at[tail, cols], more_ref.at[chip * 2 + 1 - core])
    for step in range(1, chips):
        source = lax.rem(chip + chips - step, chips)
        start(along[step - 1].at[tail], more_ref.at[source * 2 + core])
        start(extra.at[pl.ds((step - 1) * 16, 16)], more_ref.at[source * 2 + 1 - core])

    def finish():
        lane = lax.broadcasted_iota(jnp.int32, (LANES, width), 0)
        place = lax.broadcasted_iota(jnp.int32, (LANES, width), 1)
        total = jnp.zeros((16, width), F32)
        for shard in range(2 * chips):
            there = (place - shard * part == lane) & (lane < part)
            total += nn(more_ref[shard, :, 0:LANES], there.astype(F32).astype(BF))
        vec_ref[...] = total

    return finish


def second_plan(start, groups, outs, rep, chip, core, chips, reps, part):
    (up, up_twin, down, down_twin), (close, far), across, swapped = groups
    up_ref, down_ref = outs
    width = up_ref.shape[2]
    where = (rep, chip, core, chips, reps, part)

    def chained(chain, first):
        def block(step, source, side):
            shard = source * 2 + (core if side == 0 else 1 - core)
            return chain.at[shard, pl.ds(first, part)]

        return block

    across = dict(zip(NEAR, across))
    swapped = dict(zip(NEAR, swapped))
    blocks_plan(
        wide_put(start, up_ref, part),
        wide_block(up, width, part),
        wide_block(up_twin, width, part),
        {0: chained(close, 0), FAR: chained(far, 0)},
        across,
        swapped,
        2 * part,
        0,
        *where,
    )

    def put(source, block, at_chip, at_core):
        row = pl.multiple_of(block * part, part)
        start(source, down_ref.at[at_chip * 2 + at_core, pl.ds(row, part)])

    def tall(ref):
        return lambda block: ref.at[pl.ds(block * part, part)]

    blocks_plan(
        put,
        tall(down),
        tall(down_twin),
        {0: chained(close, part), FAR: chained(far, part)},
        across,
        swapped,
        2 * part,
        part,
        *where,
    )


def lay(plan, place, groups, shapes, scratch, copies, part, chips, reps):
    anywhere = pl.BlockSpec(memory_space=pl.ANY)
    inputs = [ref for group in groups for ref in group]
    return pl.pallas_call(
        functools.partial(
            lay_kernel, plan, chips, reps, part, [len(group) for group in groups]
        ),
        in_specs=[pl.BlockSpec(memory_space=pltpu.SMEM)] + [anywhere] * len(inputs),
        out_specs=[pl.BlockSpec(memory_space=pltpu.VMEM)] * len(shapes),
        out_shape=[jax.ShapeDtypeStruct(shape, kind) for shape, kind in shapes],
        scratch_shapes=[pltpu.VMEM(shape, BF) for shape in scratch]
        + [pltpu.SemaphoreType.DMA((copies,))],
        compiler_params=pltpu.CompilerParams(vmem_limit_bytes=VMEM_BYTES),
        cost_estimate=cost(0, 4 * sum(math.prod(shape) for shape, kind in shapes)),
        name="lay",
    )(place, *inputs)


def pack_vectors(rows, up_bias, class_weight):
    part = rows[0].shape[0]
    lines = [row[None] for row in rows[:8]] + [class_weight.T] + [row[None] for row in rows[8:]]
    pieces = up_bias.shape[0] // part
    lines += [up_bias[None, at * part : (at + 1) * part] for at in range(pieces)]
    return jnp.concatenate(lines, axis=0)


def move(values, reps, chips, target):
    pairs = []
    for rep in range(reps):
        for chip in range(chips):
            for core in range(2):
                to_rep, to_chip, to_core = target(rep, chip, core)
                pairs.append(
                    (
                        (rep * chips + chip) * 2 + core,
                        (to_rep * chips + to_chip) * 2 + to_core,
                    )
                )
    return lax.ppermute(values, ("rep", "fsdp"), pairs)


def along_chips(step, chips):
    return lambda rep, chip, core: (rep, (chip + step) % chips, core)


def across_reps(other):
    return lambda rep, chip, core: (rep ^ other, chip, core)


def to_twin(rep, chip, core):
    return rep, chip, 1 - core


def after(values, *gates):
    return lax.optimization_barrier((values, *gates))[0]


def along_z(mine, reps, chips):
    return [move(mine, reps, chips, along_chips(step, chips)) for step in range(1, chips)]


def over_reps(stacked, reps, chips, others):
    return [move(stacked, reps, chips, across_reps(other)) for other in others]


def pick(parts, at):
    return lax.dynamic_index_in_dim(parts, at, axis=0, keepdims=False)


def in_order(rep, reps, own, others, axis):
    blocks = jnp.stack([own] + others)
    return jnp.concatenate([pick(blocks, rep ^ at) for at in range(reps)], axis=axis)


class Reduction:
    def __init__(self, place, keep, send, reps, chips):
        self.rep, self.chip = place[0], place[1]
        self.reps, self.chips = reps, chips
        self.keep = keep
        self.got = move(send, reps, chips, to_twin)

    def at_rep(self, at):
        return lax.dynamic_index_in_dim(self.both, at, axis=1, keepdims=False)

    def over_reps(self):
        chips, rows, width = self.keep.shape
        both = (self.keep.astype(F32) + self.got.astype(F32)).astype(BF)
        self.both = lax.optimization_barrier(both).reshape(
            chips, self.reps, rows // self.reps, width
        )
        self.arrived = [self.over_rep(other) for other in NEAR]

    def over_rep(self, other, *gates):
        block = self.at_rep(self.rep ^ other)
        if gates:
            block = after(block, *gates)
        return move(block, self.reps, self.chips, across_reps(other))

    def over_far(self, *gates):
        self.arrived = self.arrived + [self.over_rep(FAR, *gates)]

    def over_chips(self, *gates):
        if gates:
            self.arrived = [after(block, *gates) for block in self.arrived]
        total = self.at_rep(self.rep).astype(F32)
        for block in self.arrived:
            total = total + block.astype(F32)
        self.total = pick(total, self.chip)
        self.passed = [
            move(
                pick(total, lax.rem(self.chip + step, self.chips)).astype(BF),
                self.reps,
                self.chips,
                along_chips(step, self.chips),
            )
            for step in range(1, self.chips)
        ]

    def chip_sum(self):
        total = self.total
        for block in self.passed:
            total = total + block.astype(F32)
        return total.astype(BF)


def share_reps(place, total, reps, chips):
    others = [move(total, reps, chips, across_reps(other)) for other in range(1, reps)]
    return in_order(place[0], reps, total, others, 0).astype(F32), others


def exchange_reps(place, rows, reps, chips):
    rep = place[0]
    parts = rows.reshape(reps, -1, rows.shape[1])
    total = pick(parts, rep).astype(F32)
    arrived = [
        move(pick(parts, rep ^ other), reps, chips, across_reps(other))
        for other in range(1, reps)
    ]
    for block in arrived:
        total = total + block.astype(F32)
    return total.astype(BF), arrived


def per_device(
    tokens,
    exit_layer,
    qkv_weight,
    query_bias,
    value_bias,
    out_weight,
    out_bias,
    attn_gain,
    attn_shift,
    up_weight,
    up_bias,
    down_weight,
    down_bias,
    block_gain,
    block_shift,
    pool_weight,
    pool_bias,
    class_weight,
    class_bias,
    output_grad,
    logit_grad,
):
    reps = lax.axis_size("rep")
    shards = lax.axis_size("fsdp")
    mine = lax.axis_index("fsdp")
    rows, width = tokens.shape
    count = exit_layer.shape[0]
    length = rows // count
    classes = class_weight.shape[1]
    part = out_weight.shape[0]
    hidden = up_weight.shape[1]

    def gather(shard):
        return lax.all_gather(shard, "fsdp", axis=0, tiled=True)

    packed = pack_vectors(
        [
            query_bias,
            value_bias,
            out_bias,
            attn_gain,
            attn_shift,
            down_bias,
            block_gain,
            block_shift,
            pool_bias,
        ],
        up_bias,
        class_weight,
    )
    joint_own = jnp.concatenate([qkv_weight, out_weight], axis=1)
    deep = down_weight.shape[0]
    chips = shards // 2
    place = jnp.stack([lax.axis_index("rep"), mine // 2, mine % 2]).astype(jnp.int32)
    direct = (
        part % 16 == 0
        and reps & (reps - 1) == 0
        and reps * width == hidden
        and reps == 4
        and packed.shape[0] <= 16
    )
    if direct:
        lines = packed.shape[0]
        held = jnp.pad(packed, ((0, 16 - lines), (0, width - part)))
        own = jnp.concatenate([joint_own, jnp.tile(held, (1, reps))], axis=0)
        rep = place[0]

        def block_of(weights, at):
            return lax.dynamic_slice_in_dim(weights, at * width, width, axis=1)

        def second_of(at):
            return [
                block_of(up_weight, at),
                lax.dynamic_slice_in_dim(down_weight, at * part, part, axis=0),
            ]

        along = along_z(block_of(own, rep), reps, chips)
        chain = gather(after(jnp.concatenate(second_of(rep), axis=0), *along))
        chain = chain.reshape(chips, 2, 2 * part, width)
        twin = move(own, reps, chips, to_twin)
        stacked = jnp.concatenate([rows_[:part] for rows_ in along], axis=0)
        across = over_reps(stacked, reps, chips, range(1, reps))
        far_chain = gather(after(jnp.concatenate(second_of(rep ^ FAR), axis=0), *across))
        swapped = [move(rows_, reps, chips, to_twin) for rows_ in [stacked] + across]
        extra = move(
            jnp.concatenate([rows_[part:] for rows_ in along], axis=0), reps, chips, to_twin
        )
        up_twin = move(up_weight, reps, chips, to_twin)
        down_twin = move(down_weight, reps, chips, to_twin)
        joint, vec = lay(
            first_plan,
            place,
            [
                [own, twin],
                along,
                across,
                swapped,
                [extra],
            ],
            [((reps, width, width), BF), ((16, width), F32)],
            [(shards, 16, width)],
            2 * chips * (reps + 1),
            part,
            chips,
            reps,
        )
        mine_chain = lax.dynamic_index_in_dim(
            after(chain, joint), place[2], axis=1, keepdims=False
        )
        second_stacked = jnp.concatenate(
            [
                pick(mine_chain, lax.rem(place[1] + chips - step, chips))
                for step in range(1, chips)
            ],
            axis=0,
        )
        second_across = over_reps(after(second_stacked, *across), reps, chips, NEAR)
        up_row = (
            vec[VECTOR_ROWS:lines].reshape(-1, shards, part).transpose(1, 0, 2).reshape(1, hidden)
        )
        down_block = (width // deep, deep, width)
    else:
        small = gather(packed[None])
        vec = small[:, :VECTOR_ROWS].transpose(1, 0, 2).reshape(VECTOR_ROWS, width).astype(F32)
        vec = jnp.pad(vec, ((0, 16 - VECTOR_ROWS), (0, 0)))
        up_row = small[:, VECTOR_ROWS:].transpose(0, 1, 2).reshape(1, hidden).astype(F32)
        pool = gather(pool_weight)
        joint = jnp.stack(jnp.split(gather(joint_own), 4, axis=1))
        up = jnp.stack(jnp.split(gather(up_weight), hidden // width, axis=1))
        down = gather(down_weight).reshape(-1, width, width)
        down_block = (1, width, width)
    joined, probs, ctx = attend(tokens, joint, vec, length)
    if direct:
        pool = gather(after(pool_weight, ctx))
        far_chain = after(far_chain, ctx)
        second_swapped = [
            move(after(rows_, ctx), reps, chips, to_twin) for rows_ in second_across
        ]
        groups = [
            [up_weight, up_twin, down_weight, down_twin],
            [
                chain.reshape(shards, 2 * part, width),
                far_chain.reshape(shards, 2 * part, width),
            ],
            second_across,
            second_swapped,
        ]
        weights = [ref for group in groups for ref in group]
        load = functools.partial(load_second, [len(group) for group in groups], chips, reps, part)
        shapes = [(reps, width, width), (shards, deep, width)]
    else:
        weights, load, shapes = [up, down], None, None
    turned, act, slope, unit1, scale1, unit2, scale2, output, *laid = feed(
        place, exit_layer, tokens, ctx, joint, vec, up_row, weights, load, shapes, length
    )
    if direct:
        up, down = laid
    class_bias_row = jnp.pad(class_bias.astype(F32), (0, 8 - classes))[None]
    logit_grad_rows = jnp.pad(logit_grad, ((0, 0), (0, 8 - classes)))
    outer, branch, low_grad, exit_sums, class_grad, logits, stats = leave(
        exit_layer,
        output,
        unit2,
        scale2,
        output_grad,
        pool,
        vec,
        class_bias_row,
        logit_grad_rows,
        act,
        full((width, width)),
        shards,
        length,
        classes,
    )
    def scatter(grad):
        return lax.psum_scatter(grad, "fsdp", scatter_dimension=0, tiled=True)

    low_part = scatter(low_grad.reshape(-1, width))
    up_keep, up_send, up_sum, inner, attended, ctx_grad, feed_sums = feed_back(
        place, chips, branch, slope, turned, down, down_block, up, outer, unit1, scale1, joint, vec, ctx
    )
    if direct:
        up_red = Reduction(place, up_keep, up_send, reps, chips)
        up_red.over_reps()
        ctx_grad = after(ctx_grad, up_red.both)
    joined_grad, joined_sum = attend_back(joined, probs, ctx_grad, length)
    joined_seen = joined_grad
    if direct:
        joined_seen = after(joined_grad, low_part, *up_red.arrived)
    sums = jnp.concatenate(
        [
            joined_sum.reshape(3, width)[::2],
            feed_sums,
            exit_sums,
            class_grad[:classes],
        ],
        axis=0,
    )
    lines = sums.shape[0]
    own_sums = sums.reshape(lines, shards, part).transpose(1, 0, 2).reshape(shards, lines * part)
    own_sums = jnp.concatenate([own_sums, up_sum.reshape(shards, deep)], axis=1)
    used = own_sums.shape[1]
    seqs_total = count * reps * shards
    figures = jnp.concatenate([stats[0, :1], stats[1, :classes]])
    slots = reps * shards * figures.shape[0] * 3
    direct = direct and used + slots <= part * LANES
    small_lines = 16
    if direct:
        high = figures.astype(BF).astype(F32)
        middle = (figures - high).astype(BF).astype(F32)
        lowest = figures - high - middle
        split = jnp.concatenate([high, middle, lowest])
        slot = lax.axis_index("rep") * shards + mine
        lone = jnp.where(
            jnp.arange(reps * shards)[:, None] == slot, split[None], 0.0
        ).reshape(1, slots)
        row = jnp.concatenate([own_sums, jnp.broadcast_to(lone, (shards, slots))], axis=1)
        small_lines = -(-row.shape[1] // (LANES * 16)) * 16
        row = jnp.pad(row, ((0, 0), (0, small_lines * LANES - row.shape[1])))
        row = row.reshape(shards, small_lines, LANES)
    else:
        row = jnp.zeros((shards, small_lines, LANES), F32)
    keep, send = weight_grads(
        place, tokens, joined_seen, row, chips, LANES if direct else 0
    )
    input_grad = input_back(inner, joined_grad, joint)

    if direct:
        up_red.over_far(keep)
        joint_red = Reduction(place, keep, send, reps, chips)
        joint_red.over_reps()
        up_red.over_chips(joint_red.both)
        joint_red.over_far()
        low_total, low_arrived = exchange_reps(
            place, after(low_part, *joint_red.arrived), reps, chips
        )
        joint_red.over_chips(*up_red.passed)
        wide = (deep + part) * width // part
        up_total = up_red.chip_sum()
        joint_total = joint_red.chip_sum()
        columns = up_total.shape[1]
        others = columns + joint_total.shape[1]
        total, _ = share_reps(
            place,
            jnp.concatenate([up_total, joint_total, low_total.reshape(-1, wide)], axis=1),
            reps,
            chips,
        )
        up_sum = total[:, :columns]
        joint_sum = total[:, columns:others]
        low_sum = total[:, others:].reshape(deep + part, width)
        small_sum = joint_sum[:small_lines, 3 * width :].reshape(-1)
        total = small_sum[used : used + slots].reshape(-1, figures.shape[0]).sum(axis=0)
    else:
        first = mine % 2 == 0

        def whole_of(kept, sent):
            pair = jnp.stack([jnp.where(first, kept, sent), jnp.where(first, sent, kept)], axis=1)
            return pair.reshape(-1, kept.shape[2])

        joint_sum, low_sum, up_sum = lax.psum(
            (scatter(whole_of(keep, send)), low_part, scatter(whole_of(up_keep, up_send))), "rep"
        )
        joint_sum, low_sum, up_sum = (
            joint_sum.astype(F32),
            low_sum.astype(F32),
            up_sum.astype(F32),
        )
        own_sums, total = lax.psum((own_sums, figures), ("rep", "fsdp"))
        small_sum = pick(own_sums, mine)
    own = small_sum[: lines * part].reshape(lines, part)
    return (
        output,
        logits[:, :classes],
        total[0] / seqs_total,
        input_grad,
        joint_sum[:, : 3 * width],
        own[0],
        own[1],
        up_sum[:, hidden:],
        own[4],
        own[2],
        own[3],
        up_sum[:, :hidden],
        small_sum[lines * part : used],
        low_sum[:deep],
        own[7],
        own[5],
        own[6],
        low_sum[deep:],
        own[8],
        own[9 : 9 + classes].T,
        total[1:],
    )


def solution(mesh):
    return jax.shard_map(
        per_device,
        mesh=mesh,
        in_specs=(
            P(("rep", "fsdp"), None),
            P(("rep", "fsdp")),
            P("fsdp", None),
            P("fsdp"),
            P("fsdp"),
            P("fsdp", None),
            P("fsdp"),
            P("fsdp"),
            P("fsdp"),
            P("fsdp", None),
            P("fsdp"),
            P("fsdp", None),
            P("fsdp"),
            P("fsdp"),
            P("fsdp"),
            P("fsdp", None),
            P("fsdp"),
            P("fsdp", None),
            P(),
            P(("rep", "fsdp"), None),
            P(("rep", "fsdp"), None),
        ),
        out_specs=(
            P(("rep", "fsdp"), None),
            P(("rep", "fsdp"), None),
            P(),
            P(("rep", "fsdp"), None),
            P("fsdp", None),
            P("fsdp"),
            P("fsdp"),
            P("fsdp", None),
            P("fsdp"),
            P("fsdp"),
            P("fsdp"),
            P("fsdp", None),
            P("fsdp"),
            P("fsdp", None),
            P("fsdp"),
            P("fsdp"),
            P("fsdp"),
            P("fsdp", None),
            P("fsdp"),
            P("fsdp", None),
            P(),
        ),
        check_vma=False,
    )
```

```python
import functools
import math

import jax
import jax.numpy as jnp
from jax import lax
from jax.experimental import pallas as pl
from jax.experimental.pallas import tpu as pltpu
from jax.sharding import PartitionSpec as P

HD = 64
LAYER = 6
PAIR = 2 * HD
NEAR = (1, 2)
FAR = 3
LANES = 128
VMEM_BYTES = 58 * 2**20
BF = jnp.bfloat16
F32 = jnp.float32

QUERY_BIAS, VALUE_BIAS, OUT_BIAS, ATTN_GAIN, ATTN_SHIFT = 0, 1, 2, 3, 4
DOWN_BIAS, BLOCK_GAIN, BLOCK_SHIFT, CLASS_ROWS, POOL_BIAS = 5, 6, 7, 8, 11
VECTOR_ROWS = 12


def nn(left, right):
    return jnp.dot(left, right, preferred_element_type=F32)


def tn(left, right):
    return lax.dot_general(left, right, (((0,), (0,)), ((), ())), preferred_element_type=F32)


def nt(left, right):
    return lax.dot_general(left, right, (((1,), (1,)), ((), ())), preferred_element_type=F32)


def full(shape):
    return pl.BlockSpec(shape, lambda *at: (0,) * len(shape))


def params():
    return pltpu.CompilerParams(
        dimension_semantics=("arbitrary",), vmem_limit_bytes=VMEM_BYTES
    )


def cost(flops, moved, trans=0):
    return pl.CostEstimate(flops=flops, bytes_accessed=moved, transcendentals=trans)


def split_heads(pair):
    lane = lax.broadcasted_iota(jnp.int32, pair.shape, 1)
    zero = jnp.zeros_like(pair)
    return jnp.concatenate(
        [jnp.where(lane < HD, pair, zero), jnp.where(lane < HD, zero, pair)], axis=0
    )


def norm_stats(values):
    center = values - jnp.mean(values, axis=-1, keepdims=True)
    spread = jnp.mean(center * center, axis=-1, keepdims=True)
    scale = lax.rsqrt(spread + 1e-06)
    return center * scale, scale


def norm_back(grad, unit, scale, gain):
    inner = grad * gain
    first = jnp.mean(inner, axis=-1, keepdims=True)
    second = jnp.mean(inner * unit, axis=-1, keepdims=True)
    return scale * (inner - first - unit * second)


def gelu_parts(values):
    base = 1.0 + 0.23164189 * jnp.abs(values)
    t = pl.reciprocal(base, approx=True)
    t = t * (2.0 - base * t)
    bell = jnp.exp2((values * values) * -0.7213475204444817)
    poly = t * (
        0.127414796
        + t * (-0.142248368 + t * (0.7107068705 + t * (-0.7265760135 + t * 0.5307027145)))
    )
    tail = poly * bell
    below = jnp.where(values >= 0.0, 1.0 - tail, tail)
    return values * below, below + values * (bell * 0.3989422804014327)


def attend_kernel(length, tok_ref, w_ref, vec_ref, joined_ref, probs_ref, ctx_ref):
    rows, width = ctx_ref.shape
    pairs = width // PAIR
    for part in range(3):
        cols = slice(part * width, (part + 1) * width)
        value = nn(tok_ref[...], w_ref[part])
        if part == 0:
            value += vec_ref[QUERY_BIAS : QUERY_BIAS + 1]
        elif part == 2:
            value += vec_ref[VALUE_BIAS : VALUE_BIAS + 1]
        joined_ref[:, cols] = value.astype(BF)

    def one(seq, carry):
        at = pl.ds(pl.multiple_of(seq * length, length), length)
        scores = []
        for pair in range(pairs):
            query = joined_ref[at, pair * PAIR : (pair + 1) * PAIR] * jnp.asarray(0.125, BF)
            keys = split_heads(joined_ref[at, width + pair * PAIR : width + (pair + 1) * PAIR])
            scores.append(nt(keys, query))
        all_probs = []
        for pair in range(pairs):
            halves = []
            for head in range(2):
                part = scores[pair][head * length : (head + 1) * length]
                part = jnp.exp(part - jnp.max(part, axis=0, keepdims=True))
                part = part * (1.0 / jnp.sum(part, axis=0, keepdims=True))
                halves.append(part.astype(BF))
            probs = jnp.concatenate(halves, axis=0)
            probs_ref[seq, pair] = probs
            all_probs.append(probs)
        for pair in range(pairs):
            vals = split_heads(
                joined_ref[at, 2 * width + pair * PAIR : 2 * width + (pair + 1) * PAIR]
            )
            ctx_ref[at, pair * PAIR : (pair + 1) * PAIR] = tn(all_probs[pair], vals).astype(BF)
        return carry

    lax.fori_loop(0, rows // length, one, 0)


def attend(tokens, qkv, vec, length):
    rows, width = tokens.shape
    count = rows // length
    steps = 2
    block = rows // steps
    pairs = width // PAIR
    return pl.pallas_call(
        functools.partial(attend_kernel, length),
        grid=(steps,),
        in_specs=[
            pl.BlockSpec((block, width), lambda i: (i, 0)),
            full((3, width, width)),
            full(vec.shape),
        ],
        out_specs=[
            pl.BlockSpec((block, 3 * width), lambda i: (i, 0)),
            pl.BlockSpec((count // steps, pairs, 2 * length, length), lambda i: (i, 0, 0, 0)),
            pl.BlockSpec((block, width), lambda i: (i, 0)),
        ],
        out_shape=[
            jax.ShapeDtypeStruct((rows, 3 * width), BF),
            jax.ShapeDtypeStruct((count, pairs, 2 * length, length), BF),
            jax.ShapeDtypeStruct((rows, width), BF),
        ],
        compiler_params=params(),
        cost_estimate=cost(8 * rows * width * width, 20 * rows * width, rows * width),
        name="attend",
    )(tokens, qkv, vec)


def feed_kernel(
    length,
    load,
    inputs,
    place_ref,
    exit_ref,
    tok_ref,
    ctx_ref,
    out_w_ref,
    vec_ref,
    up_b_ref,
    *refs,
):
    weights, refs = refs[:inputs], refs[inputs:]
    (
        turned_ref,
        act_ref,
        slope_ref,
        unit1_ref,
        scale1_ref,
        unit2_ref,
        scale2_ref,
        output_ref,
        *more,
        acc_ref,
        low_ref,
        line_ref,
    ) = refs[: 11 + (2 if load else 0)]
    step = pl.program_id(0)
    last = pl.num_programs(0) - 1
    rows, width = tok_ref.shape
    sub = 256
    if load:
        up_all, down_all, sems, out_sems = refs[13:]
        each = down_all.shape[0] // up_all.shape[0]
        stores = [
            pltpu.make_async_copy(up_all, more[0], out_sems.at[0]),
            pltpu.make_async_copy(down_all, more[1], out_sems.at[1]),
        ]

        def up_part(cols):
            return up_all[step, :, cols]

        def down_part(cols):
            return down_all[pl.ds(step * each, each), :, cols].reshape(width, sub)

    else:

        def up_part(cols):
            return weights[0][0, :, cols]

        def down_part(cols):
            return weights[1][:, :, cols].reshape(width, sub)

    @pl.when(step == 0)
    def _():
        if load:
            copies = load(weights, up_all, down_all, place_ref, sems)
        for m in range(rows // sub):
            at = slice(m * sub, (m + 1) * sub)
            inner = tok_ref[at].astype(F32) + (
                nn(ctx_ref[at], out_w_ref[0]) + vec_ref[OUT_BIAS : OUT_BIAS + 1]
            )
            unit, scale = norm_stats(inner)
            first = unit * vec_ref[ATTN_GAIN : ATTN_GAIN + 1] + vec_ref[ATTN_SHIFT : ATTN_SHIFT + 1]
            unit1_ref[at] = unit.astype(BF)
            scale1_ref[at] = scale
            low = first.astype(BF)
            low_ref[at] = low
            turned_ref[:, at] = low.T
            acc_ref[at] = first + vec_ref[DOWN_BIAS : DOWN_BIAS + 1]
        if load:
            for copy in copies:
                copy.wait()
            for store in stores:
                store.start()

    tiles = [(m, n) for m in range(rows // sub) for n in range(width // sub)]

    def rows_of(m):
        return slice(m * sub, (m + 1) * sub)

    def first_product(tile):
        return nn(low_ref[rows_of(tile[0])], up_part(rows_of(tile[1])))

    def second_product(m, n):
        at, cols = rows_of(m), rows_of(n)
        acc_ref[at, cols] += nn(line_ref[m % 2], down_part(cols))

    ahead = first_product(tiles[0])
    for index, (m, n) in enumerate(tiles):
        at, cols = rows_of(m), rows_of(n)
        hidden = ahead + up_b_ref[:, cols]
        if index + 1 < len(tiles):
            ahead = first_product(tiles[index + 1])
        if m > 0:
            second_product(m - 1, n)
        act, slope = gelu_parts(hidden)
        act = act.astype(BF)
        line_ref[m % 2, :, cols] = act
        act_ref[cols, at] = act.T
        slope_ref[at, cols] = slope.astype(BF)
    for n in range(width // sub):
        second_product(rows // sub - 1, n)

    @pl.when(step == last)
    def _():
        for seq in range(rows // length):
            at = slice(seq * length, (seq + 1) * length)
            active = (exit_ref[seq] >= LAYER).astype(F32)
            unit, scale = norm_stats(acc_ref[at])
            unit2_ref[at] = unit.astype(BF)
            scale2_ref[at] = scale
            result = (
                unit * vec_ref[BLOCK_GAIN : BLOCK_GAIN + 1] + vec_ref[BLOCK_SHIFT : BLOCK_SHIFT + 1]
            ) * active
            output_ref[at] = result.astype(BF)
        if load:
            for store in stores:
                store.wait()


def feed(place, exit_layer, tokens, ctx, out_w, vec, up_bias, weights, load, shapes, length):
    rows, width = tokens.shape
    hidden = up_bias.shape[1]
    steps = hidden // width
    whole = full((rows, width))
    if load:
        weight_specs = [pl.BlockSpec(memory_space=pl.ANY)] * len(weights)
        more_specs = [pl.BlockSpec(memory_space=pl.ANY)] * 2
        more = [jax.ShapeDtypeStruct(shape, BF) for shape in shapes]
        copies = 2 * shapes[1][0] * shapes[0][0]
        scratch = [pltpu.VMEM(shape, BF) for shape in shapes] + [
            pltpu.SemaphoreType.DMA((copies,)),
            pltpu.SemaphoreType.DMA((2,)),
        ]
    else:
        weight_specs = [
            pl.BlockSpec((1, width, width), lambda i: (i, 0, 0)),
            pl.BlockSpec((1, width, width), lambda i: (i, 0, 0)),
        ]
        more_specs, more, scratch = [], [], []
    return pl.pallas_call(
        functools.partial(feed_kernel, length, load, len(weights)),
        grid=(steps,),
        in_specs=[
            pl.BlockSpec(memory_space=pltpu.SMEM),
            pl.BlockSpec(memory_space=pltpu.SMEM),
            whole,
            whole,
            pl.BlockSpec((1, width, width), lambda i: (3, 0, 0)),
            full(vec.shape),
            pl.BlockSpec((1, width), lambda i: (0, i)),
        ]
        + weight_specs,
        out_specs=[
            full((width, rows)),
            pl.BlockSpec((width, rows), lambda i: (i, 0)),
            pl.BlockSpec((rows, width), lambda i: (0, i)),
            whole,
            full((rows, 1)),
            whole,
            full((rows, 1)),
            whole,
        ]
        + more_specs,
        out_shape=[
            jax.ShapeDtypeStruct((width, rows), BF),
            jax.ShapeDtypeStruct((hidden, rows), BF),
            jax.ShapeDtypeStruct((rows, hidden), BF),
            jax.ShapeDtypeStruct((rows, width), BF),
            jax.ShapeDtypeStruct((rows, 1), F32),
            jax.ShapeDtypeStruct((rows, width), BF),
            jax.ShapeDtypeStruct((rows, 1), F32),
            jax.ShapeDtypeStruct((rows, width), BF),
        ]
        + more,
        scratch_shapes=[
            pltpu.VMEM((rows, width), F32),
            pltpu.VMEM((rows, width), BF),
            pltpu.VMEM((2, 256, width), BF),
        ]
        + scratch,
        compiler_params=params(),
        cost_estimate=cost(18 * rows * width * width, 40 * rows * width, 8 * rows * width),
        name="feed",
    )(place, exit_layer, tokens, ctx, out_w, vec, up_bias, *weights)


def load_second(counts, chips, reps, part, weights, up_all, down_all, place_ref, sems):
    at = 0
    groups = []
    for number in counts:
        groups.append(weights[at : at + number])
        at += number
    copies = []

    def start(source, target):
        copies.append(pltpu.make_async_copy(source, target, sems.at[len(copies)]))
        copies[-1].start()

    second_plan(
        start,
        groups,
        (up_all, down_all),
        place_ref[0],
        place_ref[1],
        place_ref[2],
        chips,
        reps,
        part,
    )
    return copies


def leave_kernel(
    length,
    classes,
    exit_ref,
    output_ref,
    unit2_ref,
    scale2_ref,
    grad_ref,
    pool_ref,
    vec_ref,
    class_bias_ref,
    logit_grad_ref,
    act_ref,
    outer_ref,
    branch_ref,
    joint_grad_ref,
    sums_ref,
    class_grad_ref,
    logits_ref,
    stats_ref,
    lead_ref,
    pool_grad_ref,
):
    step = pl.program_id(0)
    rows, width = output_ref.shape
    pool = pool_ref[...].reshape(width, width)
    count = rows // length

    @pl.when(step == 0)
    def _():
        place = lax.broadcasted_iota(jnp.int32, (count, 1), 0)
        active = jnp.zeros((count, 1), F32)
        for seq in range(count):
            on = (exit_ref[seq] >= LAYER).astype(F32)
            active = jnp.where(place == seq, on, active)
        leading = jnp.concatenate(
            [output_ref[seq * length : seq * length + 1].astype(F32) for seq in range(count)],
            axis=0,
        ).astype(BF)
        pooled = jnp.tanh(nn(leading, pool) + vec_ref[POOL_BIAS : POOL_BIAS + 1])
        pooled_low = pooled.astype(BF)
        used = lax.broadcasted_iota(jnp.int32, (8, width), 0) < classes
        class_rows = jnp.where(used, vec_ref[CLASS_ROWS : CLASS_ROWS + 8], 0.0).astype(BF)
        raw = nt(pooled_low, class_rows) + class_bias_ref[...]
        lane = lax.broadcasted_iota(jnp.int32, raw.shape, 1) < classes
        top = jnp.max(jnp.where(lane, raw, -jnp.inf), axis=-1, keepdims=True)
        spread = jnp.where(lane, jnp.exp(raw - top), 0.0)
        logprob = raw - top - jnp.log(jnp.sum(spread, axis=-1, keepdims=True))
        entropy = -jnp.sum(
            jnp.where(lane, jnp.exp(logprob) * logprob, 0.0), axis=-1, keepdims=True
        )
        logits_ref[...] = raw * active
        class_grad = (logit_grad_ref[...].astype(F32) * active).astype(BF)
        stats_ref[0:1] = jnp.broadcast_to(jnp.sum(entropy * active, axis=0, keepdims=True), (1, 8))
        stats_ref[1:2] = jnp.sum(class_grad.astype(F32), axis=0, keepdims=True)
        class_grad_ref[...] = tn(class_grad, pooled_low)
        pooled_grad = nn(class_grad, class_rows)
        pre_grad = (pooled_grad * (1.0 - pooled * pooled)).astype(BF)
        sums_ref[3:4] = jnp.sum(pre_grad.astype(F32), axis=0, keepdims=True)
        pool_grad_ref[...] = tn(leading, pre_grad).reshape(pool_grad_ref.shape).astype(BF)
        lead_ref[...] = nt(pre_grad, pool)
        head = lax.broadcasted_iota(jnp.int32, (length, 1), 0) == 0
        gain = vec_ref[BLOCK_GAIN : BLOCK_GAIN + 1]
        gain_sum = jnp.zeros((1, width), F32)
        shift_sum = jnp.zeros((1, width), F32)
        bias_sum = jnp.zeros((1, width), F32)
        for seq in range(count):
            at = slice(seq * length, (seq + 1) * length)
            on = (exit_ref[seq] >= LAYER).astype(F32)
            top_grad = (
                grad_ref[at].astype(F32) + jnp.where(head, lead_ref[seq : seq + 1], 0.0)
            ) * on
            unit = unit2_ref[at].astype(F32)
            outer = norm_back(top_grad, unit, scale2_ref[at], gain)
            branch = outer.astype(BF)
            outer_ref[at] = outer
            branch_ref[at] = branch
            gain_sum += jnp.sum(top_grad * unit, axis=0, keepdims=True)
            shift_sum += jnp.sum(top_grad, axis=0, keepdims=True)
            bias_sum += jnp.sum(branch.astype(F32), axis=0, keepdims=True)
        sums_ref[0:1] = gain_sum
        sums_ref[1:2] = shift_sum
        sums_ref[2:3] = bias_sum

    @pl.when(step > 0)
    def _():
        few, both, _ = joint_grad_ref.shape
        deep = width // few
        value = nn(act_ref[...], branch_ref[...])
        for at in range(few):
            joint_grad_ref[at, 0:deep] = value[at * deep : (at + 1) * deep].astype(BF)
            joint_grad_ref[at, deep:both] = pool_grad_ref[(step - 1) * few + at]


def leave(
    exit_layer, output, unit2, scale2, output_grad, pool, vec, class_bias, logit_grad, act,
    pool_spec, shards, length, classes,
):
    rows, width = output.shape
    count = rows // length
    hidden = act.shape[0]
    steps = hidden // width
    few = shards // steps
    both = (hidden + width) // shards
    whole = full((rows, width))
    return pl.pallas_call(
        functools.partial(leave_kernel, length, classes),
        grid=(steps + 1,),
        in_specs=[
            pl.BlockSpec(memory_space=pltpu.SMEM),
            whole,
            whole,
            full((rows, 1)),
            whole,
            pool_spec,
            full(vec.shape),
            full(class_bias.shape),
            full(logit_grad.shape),
            pl.BlockSpec((width, rows), lambda i: (jnp.maximum(i - 1, 0), 0)),
        ],
        out_specs=[
            whole,
            whole,
            pl.BlockSpec((few, both, width), lambda i: (jnp.maximum(i - 1, 0), 0, 0)),
            full((4, width)),
            full((8, width)),
            full((count, 8)),
            full((2, 8)),
        ],
        out_shape=[
            jax.ShapeDtypeStruct((rows, width), F32),
            jax.ShapeDtypeStruct((rows, width), BF),
            jax.ShapeDtypeStruct((shards, both, width), BF),
            jax.ShapeDtypeStruct((4, width), F32),
            jax.ShapeDtypeStruct((8, width), F32),
            jax.ShapeDtypeStruct((count, 8), F32),
            jax.ShapeDtypeStruct((2, 8), F32),
        ],
        scratch_shapes=[
            pltpu.VMEM((count, width), F32),
            pltpu.VMEM((shards, width // shards, width), BF),
        ],
        compiler_params=params(),
        cost_estimate=cost(8 * rows * width * width, 30 * rows * width),
        name="leave",
    )(
        exit_layer, output, unit2, scale2, output_grad, pool, vec, class_bias, logit_grad, act
    )


def split_cores(value, place_ref, keep_ref, send_ref):
    chips, part, _ = keep_ref.shape
    first = place_ref[2] == 0
    for chip in range(chips):
        even = value[2 * chip * part : (2 * chip + 1) * part]
        odd = value[(2 * chip + 1) * part : (2 * chip + 2) * part]
        keep_ref[chip] = jnp.where(first, even, odd).astype(BF)
        send_ref[chip] = jnp.where(first, odd, even).astype(BF)


def feed_back_kernel(
    place_ref,
    branch_ref,
    slope_ref,
    turned_ref,
    down_ref,
    up_ref,
    outer_ref,
    unit1_ref,
    scale1_ref,
    out_w_ref,
    vec_ref,
    ctx_ref,
    keep_ref,
    send_ref,
    up_sum_ref,
    inner_ref,
    attended_ref,
    ctx_grad_ref,
    sums_ref,
    acc_ref,
    hid_ref,
):
    step = pl.program_id(0)
    rows, width = branch_ref.shape
    sub = 512

    @pl.when(step == 0)
    def _():
        acc_ref[...] = outer_ref[...]

    last = pl.num_programs(0) - 1

    @pl.when(step < last)
    def _():
        total = jnp.zeros((1, width), F32)
        down = down_ref[...].reshape(up_ref.shape[1:])
        ahead = nt(branch_ref[0:sub], down)
        for m in range(rows // sub):
            at = slice(m * sub, (m + 1) * sub)
            hid = (ahead * slope_ref[at].astype(F32)).astype(BF)
            if (m + 1) * sub < rows:
                ahead = nt(branch_ref[(m + 1) * sub : (m + 2) * sub], down)
            hid_ref[at] = hid
            total += jnp.sum(hid.astype(F32), axis=0, keepdims=True)
            acc_ref[at] += nt(hid, up_ref[0])
        up_sum_ref[...] = total
        split_cores(nn(turned_ref[...], hid_ref[...]), place_ref, keep_ref, send_ref)

    @pl.when(step == last)
    def _():
        gain = vec_ref[ATTN_GAIN : ATTN_GAIN + 1]
        gain_sum = jnp.zeros((1, width), F32)
        shift_sum = jnp.zeros((1, width), F32)
        bias_sum = jnp.zeros((1, width), F32)
        for m in range(rows // sub):
            at = slice(m * sub, (m + 1) * sub)
            grad = acc_ref[at]
            unit = unit1_ref[at].astype(F32)
            inner = norm_back(grad, unit, scale1_ref[at], gain)
            attended = inner.astype(BF)
            inner_ref[at] = inner
            attended_ref[at] = attended
            ctx_grad_ref[at] = nt(attended, out_w_ref[0]).astype(BF)
            gain_sum += jnp.sum(grad * unit, axis=0, keepdims=True)
            shift_sum += jnp.sum(grad, axis=0, keepdims=True)
            bias_sum += jnp.sum(attended.astype(F32), axis=0, keepdims=True)
        sums_ref[0:1] = gain_sum
        sums_ref[1:2] = shift_sum
        sums_ref[2:3] = bias_sum
        split_cores(tn(ctx_ref[...], attended_ref[...]), place_ref, keep_ref, send_ref)


def feed_back(place, chips, branch, slope, low, down, down_block, up, outer, unit1, scale1, out_w, vec, ctx):
    rows, width = branch.shape
    hidden = slope.shape[1]
    steps = hidden // width
    whole = full((rows, width))
    end = steps - 1
    part = width // (2 * chips)
    return pl.pallas_call(
        feed_back_kernel,
        grid=(steps + 1,),
        in_specs=[
            pl.BlockSpec(memory_space=pltpu.SMEM),
            whole,
            pl.BlockSpec((rows, width), lambda i: (0, jnp.minimum(i, end))),
            full((width, rows)),
            pl.BlockSpec(down_block, lambda i: (jnp.minimum(i, end), 0, 0)),
            pl.BlockSpec((1, width, width), lambda i: (jnp.minimum(i, end), 0, 0)),
            whole,
            whole,
            full((rows, 1)),
            pl.BlockSpec((1, width, width), lambda i: (3, 0, 0)),
            full(vec.shape),
            whole,
        ],
        out_specs=[
            pl.BlockSpec((chips, part, width), lambda i: (0, 0, i)),
            pl.BlockSpec((chips, part, width), lambda i: (0, 0, i)),
            pl.BlockSpec((1, width), lambda i: (0, jnp.minimum(i, end))),
            whole,
            whole,
            whole,
            full((3, width)),
        ],
        out_shape=[
            jax.ShapeDtypeStruct((chips, part, hidden + width), BF),
            jax.ShapeDtypeStruct((chips, part, hidden + width), BF),
            jax.ShapeDtypeStruct((1, hidden), F32),
            jax.ShapeDtypeStruct((rows, width), F32),
            jax.ShapeDtypeStruct((rows, width), BF),
            jax.ShapeDtypeStruct((rows, width), BF),
            jax.ShapeDtypeStruct((3, width), F32),
        ],
        scratch_shapes=[pltpu.VMEM((rows, width), F32), pltpu.VMEM((rows, width), BF)],
        compiler_params=params(),
        cost_estimate=cost(28 * rows * width * width, 40 * rows * width),
        name="feed_back",
    )(place, branch, slope, low, down, up, outer, unit1, scale1, out_w, vec, ctx)


def attend_back_kernel(length, joined_ref, probs_ref, ctx_grad_ref, grad_ref, sum_ref):
    rows, width = ctx_grad_ref.shape
    pairs = width // PAIR

    def one(seq, carry):
        at = pl.ds(pl.multiple_of(seq * length, length), length)

        def columns(part, pair):
            return slice(part * width + pair * PAIR, part * width + (pair + 1) * PAIR)

        prob_grads = []
        for pair in range(pairs):
            vals = split_heads(joined_ref[at, columns(2, pair)])
            prob_grads.append(nt(vals, ctx_grad_ref[at, columns(0, pair)]))
        score_grads = []
        for pair in range(pairs):
            probs = probs_ref[seq, pair]
            halves = []
            for head in range(2):
                cut = slice(head * length, (head + 1) * length)
                held = probs[cut].astype(F32)
                part = prob_grads[pair][cut]
                base = jnp.sum(part * held, axis=0, keepdims=True)
                halves.append((held * (part - base)).astype(BF))
            score_grads.append(halves)
        for pair in range(pairs):
            probs = probs_ref[seq, pair]
            beside = jnp.concatenate([probs[:length], probs[length:]], axis=1)
            ctx_grads = split_heads(ctx_grad_ref[at, columns(0, pair)])
            grad_ref[at, columns(2, pair)] = nn(beside, ctx_grads).astype(BF)
        for pair in range(pairs):
            queries = split_heads(joined_ref[at, columns(0, pair)] * jnp.asarray(0.125, BF))
            beside = jnp.concatenate(score_grads[pair], axis=1)
            grad_ref[at, columns(1, pair)] = nn(beside, queries).astype(BF)
        for pair in range(pairs):
            keys = split_heads(joined_ref[at, columns(1, pair)])
            stacked = jnp.concatenate(score_grads[pair], axis=0)
            grad_ref[at, columns(0, pair)] = (tn(stacked, keys) * 0.125).astype(BF)
        return carry

    lax.fori_loop(0, rows // length, one, 0)
    total = jnp.zeros(sum_ref.shape, F32)
    for m in range(rows // length):
        total += jnp.sum(
            grad_ref[m * length : (m + 1) * length].astype(F32), axis=0, keepdims=True
        )

    @pl.when(pl.program_id(0) == 0)
    def _():
        sum_ref[...] = total

    @pl.when(pl.program_id(0) > 0)
    def _():
        sum_ref[...] += total


def attend_back(joined, probs, ctx_grad, length):
    rows, width = ctx_grad.shape
    count = rows // length
    steps = 2
    block = rows // steps
    pairs = width // PAIR
    return pl.pallas_call(
        functools.partial(attend_back_kernel, length),
        grid=(steps,),
        in_specs=[
            pl.BlockSpec((block, 3 * width), lambda i: (i, 0)),
            pl.BlockSpec((count // steps, pairs, 2 * length, length), lambda i: (i, 0, 0, 0)),
            pl.BlockSpec((block, width), lambda i: (i, 0)),
        ],
        out_specs=[
            pl.BlockSpec((block, 3 * width), lambda i: (i, 0)),
            full((1, 3 * width)),
        ],
        out_shape=[
            jax.ShapeDtypeStruct((rows, 3 * width), BF),
            jax.ShapeDtypeStruct((1, 3 * width), F32),
        ],
        compiler_params=params(),
        cost_estimate=cost(rows * width, rows * width),
        name="attend_back",
    )(joined, probs, ctx_grad)


def weight_grads_kernel(
    place_ref, tok_ref, joined_ref, small_ref, keep_ref, send_ref, turned_ref
):
    chips, part, _ = keep_ref.shape
    step = pl.program_id(0)
    width = tok_ref.shape[1]
    first = place_ref[2] == 0

    @pl.when(step == 0)
    def _():
        turned_ref[...] = tok_ref[...].T

    value = nn(turned_ref[...], joined_ref[...])
    cols = pl.ds(pl.multiple_of(step * width, width), width)
    for chip in range(chips):
        even = value[2 * chip * part : (2 * chip + 1) * part]
        odd = value[(2 * chip + 1) * part : (2 * chip + 2) * part]
        keep_ref[chip, :, cols] = jnp.where(first, even, odd).astype(BF)
        send_ref[chip, :, cols] = jnp.where(first, odd, even).astype(BF)

    lines = small_ref.shape[1]
    if keep_ref.shape[2] > 3 * width:

        @pl.when(step == 0)
        def _():
            tail = slice(3 * width, keep_ref.shape[2])
            keep_ref[:, :, tail] = jnp.zeros((chips, part, keep_ref.shape[2] - 3 * width), BF)
            send_ref[:, :, tail] = jnp.zeros((chips, part, keep_ref.shape[2] - 3 * width), BF)
            for chip in range(chips):
                even, odd = small_ref[2 * chip], small_ref[2 * chip + 1]
                keep_ref[chip, 0:lines, tail] = jnp.where(first, even, odd).astype(BF)
                send_ref[chip, 0:lines, tail] = jnp.where(first, odd, even).astype(BF)


def weight_grads(place, tokens, joined_grad, small, chips, extra):
    rows, width = tokens.shape
    shape = (chips, width // (2 * chips), 3 * width + extra)
    return pl.pallas_call(
        weight_grads_kernel,
        grid=(3,),
        in_specs=[
            pl.BlockSpec(memory_space=pltpu.SMEM),
            full((rows, width)),
            pl.BlockSpec((rows, width), lambda i: (0, i)),
            full(small.shape),
        ],
        out_specs=[full(shape), full(shape)],
        out_shape=[jax.ShapeDtypeStruct(shape, BF)] * 2,
        scratch_shapes=[pltpu.VMEM((width, rows), BF)],
        compiler_params=params(),
        cost_estimate=cost(rows * width, rows * width),
        name="weight_grads",
    )(place, tokens, joined_grad, small)


def input_kernel(inner_ref, joined_ref, w_ref, out_ref):
    width = inner_ref.shape[1]
    total = inner_ref[...]
    for part in range(3):
        total += nt(joined_ref[:, part * width : (part + 1) * width], w_ref[part])
    out_ref[...] = total.astype(BF)


def input_back(inner, joined_grad, qkv):
    rows, width = inner.shape
    steps = 4
    block = rows // steps
    return pl.pallas_call(
        input_kernel,
        grid=(steps,),
        in_specs=[
            pl.BlockSpec((block, width), lambda i: (i, 0)),
            pl.BlockSpec((block, 3 * width), lambda i: (i, 0)),
            full((3, width, width)),
        ],
        out_specs=pl.BlockSpec((block, width), lambda i: (i, 0)),
        out_shape=jax.ShapeDtypeStruct((rows, width), BF),
        compiler_params=params(),
        cost_estimate=cost(rows * width, rows * width),
        name="input_back",
    )(inner, joined_grad, qkv)


def lay_kernel(plan, chips, reps, part, counts, place_ref, *refs):
    at = 0
    groups = []
    for number in counts:
        groups.append(refs[at : at + number])
        at += number
    sems = refs[-1]
    rep, chip, core = place_ref[0], place_ref[1], place_ref[2]
    copies = []

    def start(source, target):
        copies.append(pltpu.make_async_copy(source, target, sems.at[len(copies)]))
        copies[-1].start()

    finish = plan(start, groups, refs[at:-1], rep, chip, core, chips, reps, part)
    for copy in copies:
        copy.wait()
    if finish is not None:
        finish()


def blocks_plan(
    put, own, twin, along, across, swapped, depth, first, rep, chip, core, chips, reps, part
):
    for block in range(reps):
        put(own(block), block, chip, core)
        put(twin(block), block, chip, 1 - core)
    for step in range(1, chips):
        source = lax.rem(chip + chips - step, chips)
        rows = pl.ds((step - 1) * depth + first, part)
        for other, block in along.items():
            put(block(step, source, 0), rep ^ other, source, core)
            put(block(step, source, 1), rep ^ other, source, 1 - core)
        for other in across:
            put(across[other].at[rows], rep ^ other, source, core)
            put(swapped[other].at[rows], rep ^ other, source, 1 - core)


def wide_put(start, out_ref, part):
    def put(source, block, at_chip, at_core):
        row = pl.multiple_of((at_chip * 2 + at_core) * part, part)
        start(source, out_ref.at[block, pl.ds(row, part)])

    return put


def wide_block(ref, width, part):
    return lambda block: ref.at[pl.ds(0, part), pl.ds(block * width, width)]


def first_plan(start, groups, outs, rep, chip, core, chips, reps, part):
    (own, twin), along, across, swapped, (extra,) = groups
    out_ref, vec_ref, more_ref = outs
    width = out_ref.shape[2]

    def near(step, source, side):
        if side == 0:
            return along[step - 1].at[pl.ds(0, part)]
        return swapped[0].at[pl.ds((step - 1) * part, part)]

    blocks_plan(
        wide_put(start, out_ref, part),
        wide_block(own, width, part),
        wide_block(twin, width, part),
        {0: near},
        {at + 1: ref for at, ref in enumerate(across)},
        {at + 1: ref for at, ref in enumerate(swapped[1:])},
        part,
        0,
        rep,
        chip,
        core,
        chips,
        reps,
        part,
    )
    tail = pl.ds(part, 16)
    cols = pl.ds(0, width)
    start(own.at[tail, cols], more_ref.at[chip * 2 + core])
    start(twin.at[tail, cols], more_ref.at[chip * 2 + 1 - core])
    for step in range(1, chips):
        source = lax.rem(chip + chips - step, chips)
        start(along[step - 1].at[tail], more_ref.at[source * 2 + core])
        start(extra.at[pl.ds((step - 1) * 16, 16)], more_ref.at[source * 2 + 1 - core])

    def finish():
        lane = lax.broadcasted_iota(jnp.int32, (LANES, width), 0)
        place = lax.broadcasted_iota(jnp.int32, (LANES, width), 1)
        total = jnp.zeros((16, width), F32)
        for shard in range(2 * chips):
            there = (place - shard * part == lane) & (lane < part)
            total += nn(more_ref[shard, :, 0:LANES], there.astype(F32).astype(BF))
        vec_ref[...] = total

    return finish


def second_plan(start, groups, outs, rep, chip, core, chips, reps, part):
    (up, up_twin, down, down_twin), (close, far), across, swapped = groups
    up_ref, down_ref = outs
    width = up_ref.shape[2]
    where = (rep, chip, core, chips, reps, part)

    def chained(chain, first):
        def block(step, source, side):
            shard = source * 2 + (core if side == 0 else 1 - core)
            return chain.at[shard, pl.ds(first, part)]

        return block

    across = dict(zip(NEAR, across))
    swapped = dict(zip(NEAR, swapped))
    blocks_plan(
        wide_put(start, up_ref, part),
        wide_block(up, width, part),
        wide_block(up_twin, width, part),
        {0: chained(close, 0), FAR: chained(far, 0)},
        across,
        swapped,
        2 * part,
        0,
        *where,
    )

    def put(source, block, at_chip, at_core):
        row = pl.multiple_of(block * part, part)
        start(source, down_ref.at[at_chip * 2 + at_core, pl.ds(row, part)])

    def tall(ref):
        return lambda block: ref.at[pl.ds(block * part, part)]

    blocks_plan(
        put,
        tall(down),
        tall(down_twin),
        {0: chained(close, part), FAR: chained(far, part)},
        across,
        swapped,
        2 * part,
        part,
        *where,
    )


def lay(plan, place, groups, shapes, scratch, copies, part, chips, reps):
    anywhere = pl.BlockSpec(memory_space=pl.ANY)
    inputs = [ref for group in groups for ref in group]
    return pl.pallas_call(
        functools.partial(
            lay_kernel, plan, chips, reps, part, [len(group) for group in groups]
        ),
        in_specs=[pl.BlockSpec(memory_space=pltpu.SMEM)] + [anywhere] * len(inputs),
        out_specs=[pl.BlockSpec(memory_space=pltpu.VMEM)] * len(shapes),
        out_shape=[jax.ShapeDtypeStruct(shape, kind) for shape, kind in shapes],
        scratch_shapes=[pltpu.VMEM(shape, BF) for shape in scratch]
        + [pltpu.SemaphoreType.DMA((copies,))],
        compiler_params=pltpu.CompilerParams(vmem_limit_bytes=VMEM_BYTES),
        cost_estimate=cost(0, 4 * sum(math.prod(shape) for shape, kind in shapes)),
        name="lay",
    )(place, *inputs)


def pack_vectors(rows, up_bias, class_weight):
    part = rows[0].shape[0]
    lines = [row[None] for row in rows[:8]] + [class_weight.T] + [row[None] for row in rows[8:]]
    pieces = up_bias.shape[0] // part
    lines += [up_bias[None, at * part : (at + 1) * part] for at in range(pieces)]
    return jnp.concatenate(lines, axis=0)


def move(values, reps, chips, target):
    pairs = []
    for rep in range(reps):
        for chip in range(chips):
            for core in range(2):
                to_rep, to_chip, to_core = target(rep, chip, core)
                pairs.append(
                    (
                        (rep * chips + chip) * 2 + core,
                        (to_rep * chips + to_chip) * 2 + to_core,
                    )
                )
    return lax.ppermute(values, ("rep", "fsdp"), pairs)


def along_chips(step, chips):
    return lambda rep, chip, core: (rep, (chip + step) % chips, core)


def across_reps(other):
    return lambda rep, chip, core: (rep ^ other, chip, core)


def to_twin(rep, chip, core):
    return rep, chip, 1 - core


def after(values, *gates):
    return lax.optimization_barrier((values, *gates))[0]


def along_z(mine, reps, chips):
    return [move(mine, reps, chips, along_chips(step, chips)) for step in range(1, chips)]


def over_reps(stacked, reps, chips, others):
    return [move(stacked, reps, chips, across_reps(other)) for other in others]


def pick(parts, at):
    return lax.dynamic_index_in_dim(parts, at, axis=0, keepdims=False)


def in_order(rep, reps, own, others, axis):
    blocks = jnp.stack([own] + others)
    return jnp.concatenate([pick(blocks, rep ^ at) for at in range(reps)], axis=axis)


class Reduction:
    def __init__(self, place, keep, send, reps, chips):
        self.rep, self.chip = place[0], place[1]
        self.reps, self.chips = reps, chips
        self.keep = keep
        self.got = move(send, reps, chips, to_twin)

    def at_rep(self, at):
        return lax.dynamic_index_in_dim(self.both, at, axis=1, keepdims=False)

    def over_reps(self):
        chips, rows, width = self.keep.shape
        both = (self.keep.astype(F32) + self.got.astype(F32)).astype(BF)
        self.both = lax.optimization_barrier(both).reshape(
            chips, self.reps, rows // self.reps, width
        )
        self.arrived = [self.over_rep(other) for other in NEAR]

    def over_rep(self, other, *gates):
        block = self.at_rep(self.rep ^ other)
        if gates:
            block = after(block, *gates)
        return move(block, self.reps, self.chips, across_reps(other))

    def over_far(self, *gates):
        self.arrived = self.arrived + [self.over_rep(FAR, *gates)]

    def over_chips(self, *gates):
        if gates:
            self.arrived = [after(block, *gates) for block in self.arrived]
        total = self.at_rep(self.rep).astype(F32)
        for block in self.arrived:
            total = total + block.astype(F32)
        self.total = pick(total, self.chip)
        self.passed = [
            move(
                pick(total, lax.rem(self.chip + step, self.chips)).astype(BF),
                self.reps,
                self.chips,
                along_chips(step, self.chips),
            )
            for step in range(1, self.chips)
        ]

    def chip_sum(self):
        total = self.total
        for block in self.passed:
            total = total + block.astype(F32)
        return total.astype(BF)


def share_reps(place, total, reps, chips):
    others = [move(total, reps, chips, across_reps(other)) for other in range(1, reps)]
    return in_order(place[0], reps, total, others, 0).astype(F32), others


def exchange_reps(place, rows, reps, chips):
    rep = place[0]
    parts = rows.reshape(reps, -1, rows.shape[1])
    total = pick(parts, rep).astype(F32)
    arrived = [
        move(pick(parts, rep ^ other), reps, chips, across_reps(other))
        for other in range(1, reps)
    ]
    for block in arrived:
        total = total + block.astype(F32)
    return total.astype(BF), arrived


def per_device(
    tokens,
    exit_layer,
    qkv_weight,
    query_bias,
    value_bias,
    out_weight,
    out_bias,
    attn_gain,
    attn_shift,
    up_weight,
    up_bias,
    down_weight,
    down_bias,
    block_gain,
    block_shift,
    pool_weight,
    pool_bias,
    class_weight,
    class_bias,
    output_grad,
    logit_grad,
):
    reps = lax.axis_size("rep")
    shards = lax.axis_size("fsdp")
    mine = lax.axis_index("fsdp")
    rows, width = tokens.shape
    count = exit_layer.shape[0]
    length = rows // count
    classes = class_weight.shape[1]
    part = out_weight.shape[0]
    hidden = up_weight.shape[1]

    def gather(shard):
        return lax.all_gather(shard, "fsdp", axis=0, tiled=True)

    packed = pack_vectors(
        [
            query_bias,
            value_bias,
            out_bias,
            attn_gain,
            attn_shift,
            down_bias,
            block_gain,
            block_shift,
            pool_bias,
        ],
        up_bias,
        class_weight,
    )
    joint_own = jnp.concatenate([qkv_weight, out_weight], axis=1)
    deep = down_weight.shape[0]
    chips = shards // 2
    place = jnp.stack([lax.axis_index("rep"), mine // 2, mine % 2]).astype(jnp.int32)
    direct = (
        part % 16 == 0
        and reps & (reps - 1) == 0
        and reps * width == hidden
        and reps == 4
        and packed.shape[0] <= 16
    )
    if direct:
        lines = packed.shape[0]
        held = jnp.pad(packed, ((0, 16 - lines), (0, width - part)))
        own = jnp.concatenate([joint_own, jnp.tile(held, (1, reps))], axis=0)
        rep = place[0]

        def block_of(weights, at):
            return lax.dynamic_slice_in_dim(weights, at * width, width, axis=1)

        def second_of(at):
            return [
                block_of(up_weight, at),
                lax.dynamic_slice_in_dim(down_weight, at * part, part, axis=0),
            ]

        along = along_z(block_of(own, rep), reps, chips)
        chain = gather(after(jnp.concatenate(second_of(rep), axis=0), *along))
        chain = chain.reshape(chips, 2, 2 * part, width)
        twin = move(own, reps, chips, to_twin)
        stacked = jnp.concatenate([rows_[:part] for rows_ in along], axis=0)
        across = over_reps(stacked, reps, chips, range(1, reps))
        far_chain = gather(after(jnp.concatenate(second_of(rep ^ FAR), axis=0), *across))
        swapped = [move(rows_, reps, chips, to_twin) for rows_ in [stacked] + across]
        extra = move(
            jnp.concatenate([rows_[part:] for rows_ in along], axis=0), reps, chips, to_twin
        )
        up_twin = move(up_weight, reps, chips, to_twin)
        down_twin = move(down_weight, reps, chips, to_twin)
        joint, vec = lay(
            first_plan,
            place,
            [
                [own, twin],
                along,
                across,
                swapped,
                [extra],
            ],
            [((reps, width, width), BF), ((16, width), F32)],
            [(shards, 16, width)],
            2 * chips * (reps + 1),
            part,
            chips,
            reps,
        )
        mine_chain = lax.dynamic_index_in_dim(
            after(chain, joint), place[2], axis=1, keepdims=False
        )
        second_stacked = jnp.concatenate(
            [
                pick(mine_chain, lax.rem(place[1] + chips - step, chips))
                for step in range(1, chips)
            ],
            axis=0,
        )
        second_across = over_reps(after(second_stacked, *across), reps, chips, NEAR)
        up_row = (
            vec[VECTOR_ROWS:lines].reshape(-1, shards, part).transpose(1, 0, 2).reshape(1, hidden)
        )
        down_block = (width // deep, deep, width)
    else:
        small = gather(packed[None])
        vec = small[:, :VECTOR_ROWS].transpose(1, 0, 2).reshape(VECTOR_ROWS, width).astype(F32)
        vec = jnp.pad(vec, ((0, 16 - VECTOR_ROWS), (0, 0)))
        up_row = small[:, VECTOR_ROWS:].transpose(0, 1, 2).reshape(1, hidden).astype(F32)
        pool = gather(pool_weight)
        joint = jnp.stack(jnp.split(gather(joint_own), 4, axis=1))
        up = jnp.stack(jnp.split(gather(up_weight), hidden // width, axis=1))
        down = gather(down_weight).reshape(-1, width, width)
        down_block = (1, width, width)
    joined, probs, ctx = attend(tokens, joint, vec, length)
    if direct:
        pool = gather(after(pool_weight, ctx))
        far_chain = after(far_chain, ctx)
        second_swapped = [
            move(after(rows_, ctx), reps, chips, to_twin) for rows_ in second_across
        ]
        groups = [
            [up_weight, up_twin, down_weight, down_twin],
            [
                chain.reshape(shards, 2 * part, width),
                far_chain.reshape(shards, 2 * part, width),
            ],
            second_across,
            second_swapped,
        ]
        weights = [ref for group in groups for ref in group]
        load = functools.partial(load_second, [len(group) for group in groups], chips, reps, part)
        shapes = [(reps, width, width), (shards, deep, width)]
    else:
        weights, load, shapes = [up, down], None, None
    turned, act, slope, unit1, scale1, unit2, scale2, output, *laid = feed(
        place, exit_layer, tokens, ctx, joint, vec, up_row, weights, load, shapes, length
    )
    if direct:
        up, down = laid
    class_bias_row = jnp.pad(class_bias.astype(F32), (0, 8 - classes))[None]
    logit_grad_rows = jnp.pad(logit_grad, ((0, 0), (0, 8 - classes)))
    outer, branch, low_grad, exit_sums, class_grad, logits, stats = leave(
        exit_layer,
        output,
        unit2,
        scale2,
        output_grad,
        pool,
        vec,
        class_bias_row,
        logit_grad_rows,
        act,
        full((width, width)),
        shards,
        length,
        classes,
    )
    def scatter(grad):
        return lax.psum_scatter(grad, "fsdp", scatter_dimension=0, tiled=True)

    low_part = scatter(low_grad.reshape(-1, width))
    up_keep, up_send, up_sum, inner, attended, ctx_grad, feed_sums = feed_back(
        place, chips, branch, slope, turned, down, down_block, up, outer, unit1, scale1, joint, vec, ctx
    )
    if direct:
        up_red = Reduction(place, up_keep, up_send, reps, chips)
        up_red.over_reps()
        ctx_grad = after(ctx_grad, up_red.both)
    joined_grad, joined_sum = attend_back(joined, probs, ctx_grad, length)
    joined_seen = joined_grad
    if direct:
        joined_seen = after(joined_grad, low_part, *up_red.arrived)
    sums = jnp.concatenate(
        [
            joined_sum.reshape(3, width)[::2],
            feed_sums,
            exit_sums,
            class_grad[:classes],
        ],
        axis=0,
    )
    lines = sums.shape[0]
    own_sums = sums.reshape(lines, shards, part).transpose(1, 0, 2).reshape(shards, lines * part)
    own_sums = jnp.concatenate([own_sums, up_sum.reshape(shards, deep)], axis=1)
    used = own_sums.shape[1]
    seqs_total = count * reps * shards
    figures = jnp.concatenate([stats[0, :1], stats[1, :classes]])
    slots = reps * shards * figures.shape[0] * 3
    direct = direct and used + slots <= part * LANES
    small_lines = 16
    if direct:
        high = figures.astype(BF).astype(F32)
        middle = (figures - high).astype(BF).astype(F32)
        lowest = figures - high - middle
        split = jnp.concatenate([high, middle, lowest])
        slot = lax.axis_index("rep") * shards + mine
        lone = jnp.where(
            jnp.arange(reps * shards)[:, None] == slot, split[None], 0.0
        ).reshape(1, slots)
        row = jnp.concatenate([own_sums, jnp.broadcast_to(lone, (shards, slots))], axis=1)
        small_lines = -(-row.shape[1] // (LANES * 16)) * 16
        row = jnp.pad(row, ((0, 0), (0, small_lines * LANES - row.shape[1])))
        row = row.reshape(shards, small_lines, LANES)
    else:
        row = jnp.zeros((shards, small_lines, LANES), F32)
    keep, send = weight_grads(
        place, tokens, joined_seen, row, chips, LANES if direct else 0
    )
    input_grad = input_back(inner, joined_grad, joint)

    if direct:
        up_red.over_far(joined_seen)
        joint_red = Reduction(place, keep, send, reps, chips)
        joint_red.over_reps()
        up_red.over_chips(joint_red.both)
        joint_red.over_far()
        low_total, low_arrived = exchange_reps(
            place, after(low_part, *joint_red.arrived), reps, chips
        )
        joint_red.over_chips(*up_red.passed)
        wide = (deep + part) * width // part
        up_total = up_red.chip_sum()
        joint_total = joint_red.chip_sum()
        columns = up_total.shape[1]
        others = columns + joint_total.shape[1]
        total, _ = share_reps(
            place,
            jnp.concatenate([up_total, joint_total, low_total.reshape(-1, wide)], axis=1),
            reps,
            chips,
        )
        up_sum = total[:, :columns]
        joint_sum = total[:, columns:others]
        low_sum = total[:, others:].reshape(deep + part, width)
        small_sum = joint_sum[:small_lines, 3 * width :].reshape(-1)
        total = small_sum[used : used + slots].reshape(-1, figures.shape[0]).sum(axis=0)
    else:
        first = mine % 2 == 0

        def whole_of(kept, sent):
            pair = jnp.stack([jnp.where(first, kept, sent), jnp.where(first, sent, kept)], axis=1)
            return pair.reshape(-1, kept.shape[2])

        joint_sum, low_sum, up_sum = lax.psum(
            (scatter(whole_of(keep, send)), low_part, scatter(whole_of(up_keep, up_send))), "rep"
        )
        joint_sum, low_sum, up_sum = (
            joint_sum.astype(F32),
            low_sum.astype(F32),
            up_sum.astype(F32),
        )
        own_sums, total = lax.psum((own_sums, figures), ("rep", "fsdp"))
        small_sum = pick(own_sums, mine)
    own = small_sum[: lines * part].reshape(lines, part)
    return (
        output,
        logits[:, :classes],
        total[0] / seqs_total,
        input_grad,
        joint_sum[:, : 3 * width],
        own[0],
        own[1],
        up_sum[:, hidden:],
        own[4],
        own[2],
        own[3],
        up_sum[:, :hidden],
        small_sum[lines * part : used],
        low_sum[:deep],
        own[7],
        own[5],
        own[6],
        low_sum[deep:],
        own[8],
        own[9 : 9 + classes].T,
        total[1:],
    )


def solution(mesh):
    return jax.shard_map(
        per_device,
        mesh=mesh,
        in_specs=(
            P(("rep", "fsdp"), None),
            P(("rep", "fsdp")),
            P("fsdp", None),
            P("fsdp"),
            P("fsdp"),
            P("fsdp", None),
            P("fsdp"),
            P("fsdp"),
            P("fsdp"),
            P("fsdp", None),
            P("fsdp"),
            P("fsdp", None),
            P("fsdp"),
            P("fsdp"),
            P("fsdp"),
            P("fsdp", None),
            P("fsdp"),
            P("fsdp", None),
            P(),
            P(("rep", "fsdp"), None),
            P(("rep", "fsdp"), None),
        ),
        out_specs=(
            P(("rep", "fsdp"), None),
            P(("rep", "fsdp"), None),
            P(),
            P(("rep", "fsdp"), None),
            P("fsdp", None),
            P("fsdp"),
            P("fsdp"),
            P("fsdp", None),
            P("fsdp"),
            P("fsdp"),
            P("fsdp"),
            P("fsdp", None),
            P("fsdp"),
            P("fsdp", None),
            P("fsdp"),
            P("fsdp"),
            P("fsdp"),
            P("fsdp", None),
            P("fsdp"),
            P("fsdp", None),
            P(),
        ),
        check_vma=False,
    )
```
